32 devices in a mesh: dp: 8 (over z, y), rep: 2 (over x), cores: 2 (over core).
Axes of the slice: x: 2, y: 2, z: 4, core: 2. Of those that a mesh axis runs over, the one named last changes fastest.
Arguments:
- tokens: bfloat16 [16384, 1024], P(('dp', 'rep', 'cores')), may hold values from -6 to 6
- norm_attn: bfloat16 [1024], P('dp'), may hold values from 0.5 to 1.5
- w_query: bfloat16 [1024, 1024], P('dp'), may hold values from -0.1875 to 0.1875
- w_key: bfloat16 [1024, 1024], P('dp'), may hold values from -0.1875 to 0.1875
- w_value: bfloat16 [1024, 1024], P('dp'), may hold values from -0.1875 to 0.1875
- w_out: bfloat16 [1024, 1024], P('dp'), may hold values from -0.75 to 0.75
- norm_ffn: bfloat16 [1024], P('dp'), may hold values from 0.5 to 1.5
- w_gate: bfloat16 [1024, 2816], P('dp'), may hold values from -0.1875 to 0.1875
- w_up: bfloat16 [1024, 2816], P('dp'), may hold values from -0.1875 to 0.1875
- w_down: bfloat16 [2816, 1024], P('dp'), may hold values from -0.109375 to 0.109375
- lengths: int32 [32, 1], P(('dp', 'rep', 'cores')), may hold values from 384 to 512, as said below
- cotangent: bfloat16 [16384, 1024], P(('dp', 'rep', 'cores')), may hold values from -6 to 6
Outputs:
- mixed: bfloat16 [16384, 1024], P(('dp', 'rep', 'cores'))
- input_grad: float32 [16384, 1024], P(('dp', 'rep', 'cores'))
- grad_norm_attn: float32 [1024], P('dp')
- grad_query: float32 [1024, 1024], P('dp')
- grad_key: float32 [1024, 1024], P('dp')
- grad_value: float32 [1024, 1024], P('dp')
- grad_out: float32 [1024, 1024], P('dp')
- grad_norm_ffn: float32 [1024], P('dp')
- grad_gate: float32 [1024, 2816], P('dp')
- grad_up: float32 [1024, 2816], P('dp')
- grad_down: float32 [2816, 1024], P('dp')
The draws below stay inside these ranges and needn't reach their ends.
Inputs may be any that keep to these rules, and one draw needn't show every extreme that they name: Block b holds one whole sequence of lengths[b] patches from its first slot; the remaining slots are padding. The sequence in block 0 fills all 512 slots.
All inputs are finite; a program needn't handle non-finite values.
Results may differ from the reference program's by a relative error of at most 0.017.
Values may be sent and summed in bfloat16 or wider, within the bound.
A program may use at most 192 MiB of HBM per device.

```python
import jax
import jax.numpy as jnp
from jax import lax

D = 1024
HEADS = 16
HEAD = 64
FF = 2816
TOK_DEV = 512
SEQS = 1
TOKENS = 16384


def draw_lengths(key, part):
    key = jax.random.fold_in(key, 7)
    blocks = TOKENS // TOK_DEV
    loads = jax.random.randint(key, (blocks,), 3 * TOK_DEV // 4, TOK_DEV + 1)
    loads = loads.at[0].set(TOK_DEV)
    result = jnp.zeros((blocks, SEQS), jnp.int32).at[:, 0].set(loads)
    return result.astype(jnp.int32)


def level_of(key, dims, cuts, low, top_value):
    def one(position, parts):
        heights = jax.random.uniform(jax.random.fold_in(jax.random.fold_in(key, 6), position), (parts,), jnp.float32, low / len(cuts), top_value / len(cuts))
        return jnp.repeat(jnp.exp(heights), dims[position] // parts).reshape((-1,) + (1,) * (len(dims) - position - 1))

    loudness = one(*cuts[0])
    for cut in cuts[1:]:
        loudness = loudness * one(*cut)
    return loudness


def normal_values(own_key, extent, deviation, most, cuts=(), kind=jnp.bfloat16):
    drawn = deviation * jax.random.normal(own_key, extent, jnp.float32)
    if cuts:
        drawn = drawn * level_of(own_key, extent, cuts, -0.22, 0.18)
    return jnp.clip(drawn, -most, most).astype(kind)


def setup_inputs(seed: int = 0) -> dict:
    arg_keys = jax.random.split(jax.random.key(seed), 13)
    return {
        "tokens": normal_values(arg_keys[0], (TOKENS, D), 1.0, 6.0, ((0, 32),)),
        "norm_attn": jnp.clip(1.0 + 0.1 * jax.random.normal(arg_keys[1], (D,), jnp.float32), 0.5, 1.5).astype(jnp.bfloat16),
        "w_query": normal_values(arg_keys[2], (D, D), D ** -0.5, 0.1875, ((0, 8),)),
        "w_key": normal_values(arg_keys[3], (D, D), D ** -0.5, 0.1875, ((0, 8),)),
        "w_value": normal_values(arg_keys[4], (D, D), D ** -0.5, 0.1875, ((0, 8),)),
        "w_out": normal_values(arg_keys[5], (D, D), (D // 16) ** -0.5, 0.75, ((0, 8),)),
        "norm_ffn": jnp.clip(1.0 + 0.1 * jax.random.normal(arg_keys[6], (D,), jnp.float32), 0.5, 1.5).astype(jnp.bfloat16),
        "w_gate": normal_values(arg_keys[7], (D, FF), D ** -0.5, 0.1875, ((0, 8),)),
        "w_up": normal_values(arg_keys[8], (D, FF), D ** -0.5, 0.1875, ((0, 8),)),
        "w_down": normal_values(arg_keys[9], (FF, D), FF ** -0.5, 0.109375, ((0, 8),)),
        "lengths": draw_lengths(jax.random.fold_in(arg_keys[12], 71), 0),
        "cotangent": normal_values(arg_keys[11], (TOKENS, D), 1.0, 6.0, ((0, 32),)),
    }


NORM_EPS = 1e-05
SCORE_SCALE = 0.125
NEGATIVE = -1e+30

@jax.custom_vjp
def low(v):
    return lax.optimization_barrier(v.astype(jnp.bfloat16)).astype(jnp.float32)

@jax.custom_vjp
def low_back(v):
    return v

def low_keep(v):
    return (low(v), None)

def low_pass(kept, grad):
    return (grad,)

def back_keep(v):
    return (v, None)

def back_low(kept, grad):
    return (low(grad),)
low.defvjp(low_keep, low_pass)
low_back.defvjp(back_keep, back_low)

def exact(left, right):
    return jnp.dot(left, right, precision=lax.Precision.HIGHEST, preferred_element_type=jnp.float32)

def masks(block_len):
    bounds = jnp.cumsum(block_len)
    place = jnp.arange(TOK_DEV, dtype=jnp.int32)
    segment = lax.optimization_barrier(jnp.sum((place[:, None] >= bounds[None, :]).astype(jnp.int32), axis=1))
    allowed = (segment[:, None] == segment[None, :]) & (place[None, :] <= place[:, None])
    valid = (segment < SEQS).astype(jnp.float32)
    return (allowed, valid)

def attention(query, keyed, valued, allowed):
    rows = query.shape[0]
    query3 = query.reshape(rows, HEADS, HEAD)
    keyed3 = keyed.reshape(rows, HEADS, HEAD)
    valued3 = valued.reshape(rows, HEADS, HEAD)
    raw = jnp.einsum('qhe,khe->hqk', query3, keyed3, precision=lax.Precision.HIGHEST) * SCORE_SCALE
    scores = jnp.where(allowed[None], low_back(raw), NEGATIVE)
    top = lax.optimization_barrier(jnp.max(scores, axis=-1, keepdims=True))
    expo = jnp.exp(scores - top)
    probs = expo / lax.optimization_barrier(jnp.sum(expo, axis=-1, keepdims=True))
    result = jnp.einsum('hqk,khe->qhe', low(probs), valued3, precision=lax.Precision.HIGHEST)
    return result.reshape(rows, HEADS * HEAD)
attention_saved = jax.checkpoint(attention)

def layer(inputs, params, allowed, valid):
    gain_attn, w_query, w_key, w_value, w_out, gain_ffn, w_gate, w_up, w_down = params
    normed = inputs * lax.rsqrt(lax.optimization_barrier(jnp.mean(inputs * inputs, axis=-1, keepdims=True)) + NORM_EPS)
    hidden = low(normed * gain_attn)
    query = low(low_back(exact(hidden, w_query)))
    keyed = low(low_back(exact(hidden, w_key)))
    valued = low(low_back(exact(hidden, w_value)))
    attended = low(low_back(attention_saved(query, keyed, valued, allowed)))
    residual = inputs + low_back(exact(attended, w_out))
    normed_two = residual * lax.rsqrt(lax.optimization_barrier(jnp.mean(residual * residual, axis=-1, keepdims=True)) + NORM_EPS)
    hidden_two = low(normed_two * gain_ffn)
    gate = low_back(exact(hidden_two, w_gate))
    upward = low_back(exact(hidden_two, w_up))
    middle = low(gate * jax.nn.sigmoid(gate) * upward)
    return valid[:, None] * (residual + low_back(exact(middle, w_down)))

def reference(tokens, norm_attn, w_query, w_key, w_value, w_out, norm_ffn, w_gate, w_up, w_down, lengths, cotangent):
    weights = tuple((w.astype(jnp.float32) for w in (norm_attn, w_query, w_key, w_value, w_out, norm_ffn, w_gate, w_up, w_down)))
    blocks = TOKENS // TOK_DEV
    inputs = tokens.reshape(blocks, TOK_DEV, D)
    seeds = cotangent.reshape(blocks, TOK_DEV, D)

    def step(totals, item):
        block_in, block_seed, block_len = item
        allowed, valid = masks(block_len)
        output, pullback = jax.vjp(lambda values, params: layer(values, params, allowed, valid), block_in.astype(jnp.float32), weights)
        grad_in, grad_params = pullback(block_seed.astype(jnp.float32))
        totals = tuple((a + b for a, b in zip(totals, grad_params)))
        return (totals, (output.astype(jnp.bfloat16), grad_in))
    start = tuple((jnp.zeros_like(w) for w in weights))
    totals, (outputs, input_grads) = lax.scan(step, start, (inputs, seeds, lengths))
    return (outputs.reshape(TOKENS, D), input_grads.reshape(TOKENS, D), totals[0], totals[1], totals[2], totals[3], totals[4], totals[5], totals[6], totals[7], totals[8])
```

```python
from functools import partial

import jax
import jax.numpy as jnp
from jax import lax
from jax.experimental import pallas as pl
from jax.experimental.pallas import tpu as pltpu
from jax.sharding import PartitionSpec as P

HEADS = 16
HEAD = 64


NORM_EPS = 1e-05
SCORE_SCALE = 0.125
NEGATIVE = -1e30
head_group = 4
MESH = pl.DeviceIdType.MESH
MIB = 1024 * 1024


def masks(block_len, rows):
    bounds = jnp.cumsum(block_len[0])
    place = jnp.arange(rows, dtype=jnp.int32)
    segment = jnp.sum((place[:, None] >= bounds[None, :]).astype(jnp.int32), axis=1)
    allowed = (segment[:, None] == segment[None, :]) & (place[None, :] <= place[:, None])
    valid = (segment < block_len.shape[1]).astype(jnp.float32)
    return (allowed, valid)


def normalize(values):
    factor = lax.rsqrt(jnp.mean(values * values, axis=-1, keepdims=True) + NORM_EPS)
    return (values * factor, factor)


def norm_back(grad_normed, normed, factor):
    return factor * (grad_normed - normed * jnp.mean(grad_normed * normed, axis=-1, keepdims=True))


def matmul(left, right):
    return jnp.dot(left, right, preferred_element_type=jnp.float32)


def matmul_tn(left, right):
    return lax.dot_general(
        left, right, (((0,), (0,)), ((), ())), preferred_element_type=jnp.float32
    )


def matmul_nt(left, right):
    return lax.dot_general(
        left, right, (((1,), (1,)), ((), ())), preferred_element_type=jnp.float32
    )


def to_groups(matrix):
    rows = matrix.shape[0]
    split = matrix.reshape(rows, HEADS // head_group, head_group, HEAD)
    return split.transpose(1, 2, 0, 3)


def from_groups(grouped):
    rows = grouped.shape[2]
    return grouped.transpose(2, 0, 1, 3).reshape(rows, HEADS * HEAD)


def group_scores(allowed, query_g, key_g):
    raw = (
        jnp.einsum("hqe,hke->hqk", query_g, key_g, preferred_element_type=jnp.float32) * SCORE_SCALE
    )
    return jnp.where(allowed[None], raw, NEGATIVE)


def attend(allowed, operands):
    query_g, key_g, value_g = operands
    scores = group_scores(allowed, query_g, key_g)
    top = jnp.max(scores, axis=-1, keepdims=True)
    expo = jnp.exp(scores - top)
    total = jnp.sum(expo, axis=-1, keepdims=True)
    probs_low = (expo / total).astype(jnp.bfloat16)
    result = jnp.einsum("hqk,hke->hqe", probs_low, value_g, preferred_element_type=jnp.float32)
    return (result.astype(jnp.bfloat16), top[..., 0] + jnp.log(total[..., 0]))


def attend_back(allowed, operands):
    query_g, key_g, value_g, grad_g, log_total = operands
    scores = group_scores(allowed, query_g, key_g)
    probs = jnp.exp(scores - log_total[..., None])
    grad_probs = jnp.einsum("hqe,hke->hqk", grad_g, value_g, preferred_element_type=jnp.float32)
    centre = jnp.sum(grad_probs * probs, axis=-1, keepdims=True)
    grad_scores = (probs * (grad_probs - centre)).astype(jnp.bfloat16)
    grad_query = (
        jnp.einsum("hqk,hke->hqe", grad_scores, key_g, preferred_element_type=jnp.float32)
        * SCORE_SCALE
    )
    grad_key = (
        jnp.einsum("hqk,hqe->hke", grad_scores, query_g, preferred_element_type=jnp.float32)
        * SCORE_SCALE
    )
    grad_value = jnp.einsum(
        "hqk,hqe->hke", probs.astype(jnp.bfloat16), grad_g, preferred_element_type=jnp.float32
    )
    return (
        grad_query.astype(jnp.bfloat16),
        grad_key.astype(jnp.bfloat16),
        grad_value.astype(jnp.bfloat16),
    )


class Item:
    def __init__(self, weight, tall, start, size, x_first):
        self.weight, self.tall, self.start, self.size = weight, tall, start, size
        self.x_first = x_first
        self.block = (size, 256) if tall else (32, size)

    def quarter(self, ref, lead, c, x):
        if self.tall:
            columns = pl.ds(pl.multiple_of(c * 512 + x * 256, 256), 256)
            return ref.at[(*lead, pl.ds(self.start, self.size), columns)]
        return ref.at[(*lead, c, x, slice(None), pl.ds(self.start, self.size))]

    def half(self, ref, lead, c):
        if self.tall:
            columns = pl.ds(pl.multiple_of(c * 512, 512), 512)
            return ref.at[(*lead, pl.ds(self.start, self.size), columns)]
        return ref.at[(*lead, c, slice(None), slice(None), pl.ds(self.start, self.size))]


def pieces(total, most):
    return [(start, min(most, total - start)) for start in range(0, total, most)]


def items_of(weights, wide, tall_rows, x_first):
    found = []
    for weight, columns in weights:
        cuts = pieces(352, tall_rows) if columns is None else pieces(columns, wide)
        for start, size in cuts:
            number = len(found)
            found.append(Item(weight, columns is None, start, size, number % 8 in x_first))
    return found


def place():
    d = lax.axis_index("dp")
    return lax.div(d, 2), lax.rem(d, 2), lax.axis_index("rep"), lax.axis_index("cores")


def device(z, y, x, c):
    return {"dp": 2 * z + y, "rep": x, "cores": c}


def greet():
    z, y, x, c = place()
    barrier = pltpu.get_barrier_semaphore()
    others = [device(lax.rem(z + k, 4), y, x, c) for k in (1, 2, 3)]
    others += [device(z, 1 - y, x, c), device(z, y, 1 - x, c), device(z, y, x, 1 - c)]
    for other in others:
        pl.semaphore_signal(barrier, inc=1, device_id=other, device_id_type=MESH)
    pl.semaphore_wait(barrier, len(others))


class Wires:
    def __init__(self, send_sems, recv_sems):
        self.send_sems, self.recv_sems, self.sent = send_sems, recv_sems, []

    def copy(self, slot, source, target, other):
        return pltpu.make_async_remote_copy(
            src_ref=source,
            dst_ref=target,
            send_sem=self.send_sems.at[slot],
            recv_sem=self.recv_sems.at[slot],
            device_id=other,
            device_id_type=MESH,
        )

    def send(self, slot, source, target, other):
        copy = self.copy(slot, source, target, other)
        copy.start()
        self.sent.append(copy)

    def arrived(self, slot, target):
        z, y, x, c = place()
        self.copy(slot, target, target, device(z, y, x, 1 - c)).wait_recv()

    def finish(self):
        for copy in self.sent:
            copy.wait_send()


GATHER_SLOTS = 12
ALL = slice(None)


def gather_kernel(items, n_weights, *refs):
    shares = refs[:n_weights]
    gains = refs[n_weights]
    full = refs[n_weights + 1 : 2 * n_weights + 1]
    full_gains = refs[2 * n_weights + 1]
    send_sems, recv_sems, own_sems = refs[2 * n_weights + 2 :]
    z, y, x, c = place()
    far = [lax.rem(z + k, 4) for k in range(4)]
    back = [lax.rem(z + 4 - k, 4) for k in range(4)]
    x_other, y_other, c_other = (
        device(z, y, 1 - x, c),
        device(z, 1 - y, x, c),
        device(z, y, x, 1 - c),
    )
    greet()
    wires = Wires(send_sems, recv_sems)
    own = [
        pltpu.make_async_copy(share, whole.at[z, y], own_sems.at[i])
        for i, (share, whole) in enumerate(zip(shares, full))
    ]
    own_gains = pltpu.make_async_copy(gains, full_gains.at[z, y], own_sems.at[n_weights])
    own_gains.start()
    gain_slot = GATHER_SLOTS * len(items)
    for k in (1, 2, 3):
        wires.send(gain_slot + k, gains, full_gains.at[z, y], device(far[k], y, x, c))
    for copy in own:
        copy.start()

    def slot(i, k):
        return GATHER_SLOTS * i + k

    def along_z(i):
        item = items[i]
        share, whole = shares[item.weight], full[item.weight]
        for k in (1, 2, 3):
            wires.send(
                slot(i, k),
                item.quarter(share, (), c, x),
                item.quarter(whole, (z, y), c, x),
                device(far[k], y, x, c),
            )

    own_done = set()

    def first_hop(i):
        item = items[i]
        whole = full[item.weight]
        if item.weight not in own_done:
            own[item.weight].wait()
            own_done.add(item.weight)
        for k in (1, 2, 3):
            block = item.quarter(whole, (back[k], y), c, x)
            wires.arrived(slot(i, k), block)
            wires.send(slot(i, 3 + k), block, block, x_other)
        if not item.x_first:
            block = item.quarter(whole, (ALL, y), c, x)
            wires.send(slot(i, 7), block, block, y_other)

    def second_hop(i):
        item = items[i]
        whole = full[item.weight]
        if not item.x_first:
            block = item.quarter(whole, (ALL, 1 - y), c, x)
            wires.arrived(slot(i, 7), block)
            wires.send(slot(i, 0), block, block, x_other)
        for k in (1, 2, 3):
            wires.arrived(slot(i, 3 + k), item.quarter(whole, (back[k], y), c, 1 - x))
        if item.x_first:
            block = item.half(whole, (ALL, y), c)
            wires.send(slot(i, 7), block, block, y_other)
        for k in (1, 2, 3):
            block = item.half(whole, (back[k], y), c)
            wires.send(slot(i, 7 + k), block, block, c_other)

    def last_hop(i):
        item = items[i]
        whole = full[item.weight]
        block = item.half(whole, (ALL, 1 - y), c)
        if item.x_first:
            wires.arrived(slot(i, 7), block)
        else:
            wires.arrived(slot(i, 0), item.quarter(whole, (ALL, 1 - y), c, 1 - x))
        wires.send(slot(i, 11), block, block, c_other)

    def complete(i):
        item = items[i]
        whole = full[item.weight]
        for k in (1, 2, 3):
            wires.arrived(slot(i, 7 + k), item.half(whole, (back[k], y), 1 - c))
        wires.arrived(slot(i, 11), item.half(whole, (ALL, 1 - y), 1 - c))

    ahead = 3
    for i in range(min(ahead, len(items))):
        along_z(i)
    own_gains.wait()
    for k in (1, 2, 3):
        wires.arrived(gain_slot + k, full_gains.at[back[k], y])
    wires.send(gain_slot, full_gains.at[:, y], full_gains.at[:, y], y_other)
    for step in range(len(items) + 3):
        if step >= 3:
            complete(step - 3)
        if 2 <= step < len(items) + 2:
            last_hop(step - 2)
        if 1 <= step < len(items) + 1:
            second_hop(step - 1)
        if step < len(items):
            first_hop(step)
        if step + ahead < len(items):
            along_z(step + ahead)
    wires.arrived(gain_slot, full_gains.at[:, 1 - y])
    wires.finish()


COLUMNS = (1024, 1024, 1024, 1024, 2816, 2816, None)


def share_view(share, columns):
    return share if columns is None else share.reshape(2, 2, 32, columns)


def whole_shape(columns):
    return (4, 2, 352, 1024) if columns is None else (4, 2, 2, 2, 32, columns)


def gather_weights(weights, gains):
    items = items_of(list(enumerate(COLUMNS)), 1024, 128, (0, 3, 6))
    shares = [share_view(w, n) for w, n in zip(weights, COLUMNS)]
    lines = jnp.zeros((16, 128), jnp.bfloat16)
    for i, gain in enumerate(gains):
        lines = lines.at[i].set(gain)
    shapes = [jax.ShapeDtypeStruct(whole_shape(n), jnp.bfloat16) for n in COLUMNS]
    shapes.append(jax.ShapeDtypeStruct((4, 2, 16, 128), jnp.bfloat16))
    count = GATHER_SLOTS * len(items) + 4
    anywhere = pl.BlockSpec(memory_space=pl.ANY)
    out = pl.pallas_call(
        partial(gather_kernel, items, len(shares)),
        out_shape=shapes,
        in_specs=[anywhere] * (len(shares) + 1),
        out_specs=[anywhere] * (len(shares) + 1),
        scratch_shapes=[
            pltpu.SemaphoreType.DMA((count,)),
            pltpu.SemaphoreType.DMA((count,)),
            pltpu.SemaphoreType.DMA((len(shares) + 1,)),
        ],
        compiler_params=pltpu.CompilerParams(collective_id=0, has_side_effects=True),
        name="gather_weights",
    )(*shares, lines)
    whole = [w.reshape(-1, w.shape[-1]) for w in out[:-1]]
    return whole, [out[-1][:, :, i].reshape(1024) for i in range(len(gains))]


SUM_SLOTS = 12


def plus(left, right):
    return (left.astype(jnp.float32) + right.astype(jnp.float32)).astype(left.dtype)


def sum_kernel(items, n_weights, *refs):
    refs = list(refs)

    def take(n):
        taken = refs[:n]
        del refs[:n]
        return taken

    grads = take(n_weights)
    (gain_grads,) = take(1)
    sums = take(n_weights)
    (gain_sums,) = take(1)
    mine, from_core = take(len(items)), take(len(items))
    from_first, from_second, from_z = take(len(items)), take(len(items)), take(len(items))
    gain_mine, gain_core, gain_x, gain_y, gain_z = take(5)
    send_sems, recv_sems, load_sems = refs
    z, y, x, c = place()
    far = [lax.rem(z + k, 4) for k in range(4)]
    back = [lax.rem(z + 4 - k, 4) for k in range(4)]
    x_other, y_other, c_other = (
        device(z, y, 1 - x, c),
        device(z, 1 - y, x, c),
        device(z, y, x, 1 - c),
    )
    greet()
    wires = Wires(send_sems, recv_sems)
    loads = {}

    def slot(i, k):
        return SUM_SLOTS * i + k

    def to_core(i):
        item = items[i]
        grad = grads[item.weight]
        if item.tall:
            for side in (0, 1):
                wires.send(
                    slot(i, side),
                    item.quarter(grad, (ALL, ALL), 1 - c, side),
                    from_core[i].at[:, :, side],
                    c_other,
                )
            loads[i] = [
                pltpu.make_async_copy(
                    item.quarter(grad, (ALL, ALL), c, side),
                    mine[i].at[:, :, side],
                    load_sems.at[2 * i + side],
                )
                for side in (0, 1)
            ]
        else:
            wires.send(
                slot(i, 0), item.half(grad, (ALL, ALL), 1 - c), from_core[i], c_other
            )
            loads[i] = [
                pltpu.make_async_copy(
                    item.half(grad, (ALL, ALL), c), mine[i], load_sems.at[2 * i]
                )
            ]
        for load in loads[i]:
            load.start()

    def first_hop(i):
        item, own, other = items[i], mine[i], from_core[i]
        for load in loads[i]:
            load.wait()
        if item.tall:
            for side in (0, 1):
                wires.arrived(slot(i, side), other.at[:, :, side])
        else:
            wires.arrived(slot(i, 0), other)

        def add(at, _):
            for yy in (0, 1):
                for xx in (0, 1):
                    own[at, yy, xx] = plus(own[at, yy, xx], other[at, yy, xx])
            return 0

        lax.fori_loop(0, 4, add, 0)
        if item.x_first:
            wires.send(slot(i, 2), own.at[:, :, 1 - x], from_first[i], x_other)
        else:
            wires.send(slot(i, 2), own.at[:, 1 - y], from_first[i], y_other)

    def second_hop(i):
        item, own, other = items[i], mine[i], from_first[i]
        wires.arrived(slot(i, 2), other)

        def add(at, _):
            for side in (0, 1):
                where = (at, side, x) if item.x_first else (at, y, side)
                own[where] = plus(own[where], other[at, side])
            return 0

        lax.fori_loop(0, 4, add, 0)
        if item.x_first:
            wires.send(slot(i, 3), own.at[:, 1 - y, x], from_second[i], y_other)
        else:
            wires.send(slot(i, 3), own.at[:, y, 1 - x], from_second[i], x_other)

    def along_z(i):
        own, other = mine[i], from_second[i]
        wires.arrived(slot(i, 3), other)

        def add(at, _):
            own[at, y, x] = plus(own[at, y, x], other[at])
            return 0

        lax.fori_loop(0, 4, add, 0)
        for k in (1, 2, 3):
            wires.send(
                slot(i, 3 + k),
                own.at[far[k], y, x],
                from_z[i].at[k - 1],
                device(far[k], y, x, c),
            )

    def to_x(i):
        item = items[i]
        total = mine[i][z, y, x].astype(jnp.float32)
        for k in (1, 2, 3):
            wires.arrived(slot(i, 3 + k), from_z[i].at[k - 1])
            total += from_z[i][k - 1].astype(jnp.float32)
        block = item.quarter(sums[item.weight], (), c, x)
        block[...] = total.astype(jnp.bfloat16)
        wires.send(slot(i, 7), block, block, x_other)

    def to_sibling(i):
        item = items[i]
        wires.arrived(slot(i, 7), item.quarter(sums[item.weight], (), c, 1 - x))
        block = item.half(sums[item.weight], (), c)
        wires.send(slot(i, 8), block, block, c_other)

    def complete(i):
        item = items[i]
        wires.arrived(slot(i, 8), item.half(sums[item.weight], (), 1 - c))

    base = SUM_SLOTS * len(items)
    wires.send(base, gain_grads, gain_core, c_other)
    ahead = 3
    for i in range(min(ahead, len(items))):
        to_core(i)
    wires.arrived(base, gain_core)
    gain_mine[...] = gain_grads[...] + gain_core[...]
    wires.send(base + 1, gain_mine, gain_x, x_other)
    stages = (complete, to_sibling, to_x, along_z, second_hop, first_hop)
    for step in range(len(items) + len(stages) - 1):
        for back_by, stage in zip(range(len(stages) - 1, -1, -1), stages):
            if 0 <= step - back_by < len(items):
                stage(step - back_by)
        if step + ahead < len(items):
            to_core(step + ahead)
        if step == 0:
            wires.arrived(base + 1, gain_x)
            gain_core[...] = gain_mine[...] + gain_x[...]
            wires.send(base + 2, gain_core.at[:, 1 - y], gain_y, y_other)
        if step == 1:
            wires.arrived(base + 2, gain_y)
            gain_y[...] = gain_core[:, y] + gain_y[...]
            for k in (1, 2, 3):
                wires.send(
                    base + 2 + k,
                    gain_y.at[far[k]],
                    gain_z.at[z],
                    device(far[k], y, x, c),
                )
            gain_z[z] = gain_y[z]
    for k in (1, 2, 3):
        wires.arrived(base + 2 + k, gain_z.at[back[k]])
    gain_sums[...] = (gain_z[0] + gain_z[1]) + (gain_z[2] + gain_z[3])
    wires.finish()


def sum_grads(grads, gain_grads):
    items = items_of([(6, None), (4, 2816), (5, 2816), (3, 1024), (0, 1024), (1, 1024), (2, 1024)], 1024, 128, (0, 3, 6))
    views = [g.reshape(whole_shape(n)) for g, n in zip(grads, COLUMNS)]
    lines = jnp.zeros((4, 2, 8, 128), jnp.float32)
    for i, grad in enumerate(gain_grads):
        lines = lines.at[:, :, i].set(grad.reshape(4, 2, 128))
    shapes = [
        jax.ShapeDtypeStruct((352, 1024) if n is None else (2, 2, 32, n), jnp.bfloat16)
        for n in COLUMNS
    ]
    shapes.append(jax.ShapeDtypeStruct((8, 128), jnp.float32))
    count = SUM_SLOTS * len(items) + 6
    in_vmem = pl.BlockSpec(memory_space=pltpu.VMEM)

    def buffers(*lead_of):
        return [pltpu.VMEM(lead + item.block, jnp.bfloat16) for item, lead in zip(items, lead_of)]

    gain_line = partial(pltpu.VMEM, dtype=jnp.float32)
    out = pl.pallas_call(
        partial(sum_kernel, items, len(views)),
        out_shape=shapes,
        in_specs=[pl.BlockSpec(memory_space=pl.ANY)] * len(views) + [in_vmem],
        out_specs=[in_vmem] * len(shapes),
        scratch_shapes=buffers(*[(4, 2, 2)] * len(items))
        + buffers(*[(4, 2, 2)] * len(items))
        + buffers(*[(4, 2)] * len(items))
        + buffers(*[(4,)] * len(items))
        + buffers(*[(3,)] * len(items))
        + [
            pltpu.VMEM((4, 2, 8, 128), jnp.float32),
            pltpu.VMEM((4, 2, 8, 128), jnp.float32),
            pltpu.VMEM((4, 2, 8, 128), jnp.float32),
            pltpu.VMEM((4, 8, 128), jnp.float32),
            pltpu.VMEM((4, 8, 128), jnp.float32),
            pltpu.SemaphoreType.DMA((count,)),
            pltpu.SemaphoreType.DMA((count,)),
            pltpu.SemaphoreType.DMA((2 * len(items),)),
        ],
        compiler_params=pltpu.CompilerParams(
            collective_id=1, has_side_effects=True, vmem_limit_bytes=60 * MIB
        ),
        name="sum_grads",
    )(*views, lines)
    shares = [s.reshape(-1, s.shape[-1]).astype(jnp.float32) for s in out[:-1]]
    return shares, [out[-1][i] for i in range(len(gain_grads))]


def gather_plain(weights, gains):
    everything = (*weights, *gains)
    whole = [lax.all_gather(v, "dp", axis=0, tiled=True) for v in everything]
    return whole[: len(weights)], whole[len(weights) :]


def sum_plain(grads, gain_grads):
    shares = [
        lax.psum_scatter(g.astype(jnp.float32), "dp", scatter_dimension=0, tiled=True)
        for g in (*grads, *gain_grads)
    ]
    sums = [lax.psum(s, ("rep", "cores")) for s in shares]
    return sums[: len(grads)], sums[len(grads) :]


def on_device(
    gather,
    add_up,
    tokens,
    norm_attn,
    w_query,
    w_key,
    w_value,
    w_out,
    norm_ffn,
    w_gate,
    w_up,
    w_down,
    lengths,
    cotangent,
):
    rows = tokens.shape[0]
    low = jnp.bfloat16
    allowed, valid = masks(lengths, rows)
    whole, gains = gather(
        (w_query, w_key, w_value, w_out, w_gate, w_up, w_down), (norm_attn, norm_ffn)
    )
    full_query, full_key, full_value, full_out, full_gate, full_up, full_down = whole
    gain_attn, gain_ffn = gains
    inputs = tokens.astype(jnp.float32)
    normed, factor = normalize(inputs)
    hidden = (normed * gain_attn.astype(jnp.float32)).astype(low)
    query = matmul(hidden, full_query).astype(low)
    keyed = matmul(hidden, full_key).astype(low)
    valued = matmul(hidden, full_value).astype(low)
    query_groups, key_groups, value_groups = (to_groups(query), to_groups(keyed), to_groups(valued))
    attended_groups, log_total = lax.map(
        partial(attend, allowed), (query_groups, key_groups, value_groups)
    )
    attended = from_groups(attended_groups)
    residual = inputs + matmul(attended, full_out)
    normed_two, factor_two = normalize(residual)
    hidden_two = (normed_two * gain_ffn.astype(jnp.float32)).astype(low)
    gate = matmul(hidden_two, full_gate)
    upward = matmul(hidden_two, full_up)
    sigma = jax.nn.sigmoid(gate)
    middle = (gate * sigma * upward).astype(low)
    mixed = (valid[:, None] * (residual + matmul(middle, full_down))).astype(low)
    grad_output = cotangent.astype(jnp.float32) * valid[:, None]
    grad_branch = grad_output.astype(low)
    grad_down = matmul_tn(middle, grad_branch)
    grad_middle = matmul_nt(grad_branch, full_down)
    grad_gate_rows = (grad_middle * upward * sigma * (1.0 + gate * (1.0 - sigma))).astype(low)
    grad_up_rows = (grad_middle * gate * sigma).astype(low)
    grad_gate = matmul_tn(hidden_two, grad_gate_rows)
    grad_up = matmul_tn(hidden_two, grad_up_rows)
    grad_hidden_two = matmul_nt(grad_gate_rows, full_gate) + matmul_nt(grad_up_rows, full_up)
    grad_gain_ffn = jnp.sum(grad_hidden_two * normed_two, axis=0)
    grad_residual = grad_output + norm_back(
        grad_hidden_two * gain_ffn.astype(jnp.float32), normed_two, factor_two
    )
    grad_proj = grad_residual.astype(low)
    grad_out = matmul_tn(attended, grad_proj)
    grad_attended = matmul_nt(grad_proj, full_out).astype(low)
    grad_query_g, grad_key_g, grad_value_g = lax.map(
        partial(attend_back, allowed),
        (query_groups, key_groups, value_groups, to_groups(grad_attended), log_total),
    )
    grad_query_rows = from_groups(grad_query_g)
    grad_key_rows = from_groups(grad_key_g)
    grad_value_rows = from_groups(grad_value_g)
    grad_query = matmul_tn(hidden, grad_query_rows)
    grad_key = matmul_tn(hidden, grad_key_rows)
    grad_value = matmul_tn(hidden, grad_value_rows)
    grad_hidden = (
        matmul_nt(grad_query_rows, full_query)
        + matmul_nt(grad_key_rows, full_key)
        + matmul_nt(grad_value_rows, full_value)
    )
    grad_gain_attn = jnp.sum(grad_hidden * normed, axis=0)
    input_grad = grad_residual + norm_back(
        grad_hidden * gain_attn.astype(jnp.float32), normed, factor
    )
    grads = (grad_query, grad_key, grad_value, grad_out, grad_gate, grad_up, grad_down)
    sums, gain_sums = add_up([g.astype(low) for g in grads], (grad_gain_attn, grad_gain_ffn))
    return (
        mixed,
        input_grad,
        gain_sums[0],
        sums[0],
        sums[1],
        sums[2],
        sums[3],
        gain_sums[1],
        sums[4],
        sums[5],
        sums[6],
    )


def solution(mesh):
    tuned = dict(mesh.shape) == {"dp": 8, "rep": 2, "cores": 2}
    gather, add_up = (gather_weights, sum_grads) if tuned else (gather_plain, sum_plain)
    tokens_placed = P(("dp", "rep", "cores"), None)
    share, gain = P("dp", None), P("dp")
    return jax.shard_map(
        partial(on_device, gather, add_up),
        mesh=mesh,
        in_specs=(
            tokens_placed,
            gain,
            share,
            share,
            share,
            share,
            gain,
            share,
            share,
            share,
            tokens_placed,
            tokens_placed,
        ),
        out_specs=(
            tokens_placed,
            tokens_placed,
            gain,
            share,
            share,
            share,
            share,
            gain,
            share,
            share,
            share,
        ),
        check_vma=False,
    )
```

```python
from functools import partial

import jax
import jax.numpy as jnp
from jax import lax
from jax.experimental import pallas as pl
from jax.experimental.pallas import tpu as pltpu
from jax.sharding import PartitionSpec as P

HEADS = 16
HEAD = 64


NORM_EPS = 1e-05
SCORE_SCALE = 0.125
NEGATIVE = -1e30
head_group = 4
MESH = pl.DeviceIdType.MESH
MIB = 1024 * 1024


def masks(block_len, rows):
    bounds = jnp.cumsum(block_len[0])
    place = jnp.arange(rows, dtype=jnp.int32)
    segment = jnp.sum((place[:, None] >= bounds[None, :]).astype(jnp.int32), axis=1)
    allowed = (segment[:, None] == segment[None, :]) & (place[None, :] <= place[:, None])
    valid = (segment < block_len.shape[1]).astype(jnp.float32)
    return (allowed, valid)


def normalize(values):
    factor = lax.rsqrt(jnp.mean(values * values, axis=-1, keepdims=True) + NORM_EPS)
    return (values * factor, factor)


def norm_back(grad_normed, normed, factor):
    return factor * (grad_normed - normed * jnp.mean(grad_normed * normed, axis=-1, keepdims=True))


def matmul(left, right):
    return jnp.dot(left, right, preferred_element_type=jnp.float32)


def matmul_tn(left, right):
    return lax.dot_general(
        left, right, (((0,), (0,)), ((), ())), preferred_element_type=jnp.float32
    )


def matmul_nt(left, right):
    return lax.dot_general(
        left, right, (((1,), (1,)), ((), ())), preferred_element_type=jnp.float32
    )


def to_groups(matrix):
    rows = matrix.shape[0]
    split = matrix.reshape(rows, HEADS // head_group, head_group, HEAD)
    return split.transpose(1, 2, 0, 3)


def from_groups(grouped):
    rows = grouped.shape[2]
    return grouped.transpose(2, 0, 1, 3).reshape(rows, HEADS * HEAD)


def group_scores(allowed, query_g, key_g):
    raw = (
        jnp.einsum("hqe,hke->hqk", query_g, key_g, preferred_element_type=jnp.float32) * SCORE_SCALE
    )
    return jnp.where(allowed[None], raw, NEGATIVE)


def attend(allowed, operands):
    query_g, key_g, value_g = operands
    scores = group_scores(allowed, query_g, key_g)
    top = jnp.max(scores, axis=-1, keepdims=True)
    expo = jnp.exp(scores - top)
    total = jnp.sum(expo, axis=-1, keepdims=True)
    probs_low = (expo / total).astype(jnp.bfloat16)
    result = jnp.einsum("hqk,hke->hqe", probs_low, value_g, preferred_element_type=jnp.float32)
    return (result.astype(jnp.bfloat16), top[..., 0] + jnp.log(total[..., 0]))


def attend_back(allowed, operands):
    query_g, key_g, value_g, grad_g, log_total = operands
    scores = group_scores(allowed, query_g, key_g)
    probs = jnp.exp(scores - log_total[..., None])
    grad_probs = jnp.einsum("hqe,hke->hqk", grad_g, value_g, preferred_element_type=jnp.float32)
    centre = jnp.sum(grad_probs * probs, axis=-1, keepdims=True)
    grad_scores = (probs * (grad_probs - centre)).astype(jnp.bfloat16)
    grad_query = (
        jnp.einsum("hqk,hke->hqe", grad_scores, key_g, preferred_element_type=jnp.float32)
        * SCORE_SCALE
    )
    grad_key = (
        jnp.einsum("hqk,hqe->hke", grad_scores, query_g, preferred_element_type=jnp.float32)
        * SCORE_SCALE
    )
    grad_value = jnp.einsum(
        "hqk,hqe->hke", probs.astype(jnp.bfloat16), grad_g, preferred_element_type=jnp.float32
    )
    return (
        grad_query.astype(jnp.bfloat16),
        grad_key.astype(jnp.bfloat16),
        grad_value.astype(jnp.bfloat16),
    )


class Item:
    def __init__(self, weight, tall, start, size, x_first):
        self.weight, self.tall, self.start, self.size = weight, tall, start, size
        self.x_first = x_first
        self.block = (size, 256) if tall else (32, size)

    def quarter(self, ref, lead, c, x):
        if self.tall:
            columns = pl.ds(pl.multiple_of(c * 512 + x * 256, 256), 256)
            return ref.at[(*lead, pl.ds(self.start, self.size), columns)]
        return ref.at[(*lead, c, x, slice(None), pl.ds(self.start, self.size))]

    def half(self, ref, lead, c):
        if self.tall:
            columns = pl.ds(pl.multiple_of(c * 512, 512), 512)
            return ref.at[(*lead, pl.ds(self.start, self.size), columns)]
        return ref.at[(*lead, c, slice(None), slice(None), pl.ds(self.start, self.size))]


def pieces(total, most):
    return [(start, min(most, total - start)) for start in range(0, total, most)]


def items_of(weights, wide, tall_rows, x_first):
    found = []
    for weight, columns in weights:
        cuts = pieces(352, tall_rows) if columns is None else pieces(columns, wide)
        for start, size in cuts:
            number = len(found)
            found.append(Item(weight, columns is None, start, size, number % 8 in x_first))
    return found


def place():
    d = lax.axis_index("dp")
    return lax.div(d, 2), lax.rem(d, 2), lax.axis_index("rep"), lax.axis_index("cores")


def device(z, y, x, c):
    return {"dp": 2 * z + y, "rep": x, "cores": c}


def greet():
    z, y, x, c = place()
    barrier = pltpu.get_barrier_semaphore()
    others = [device(lax.rem(z + k, 4), y, x, c) for k in (1, 2, 3)]
    others += [device(z, 1 - y, x, c), device(z, y, 1 - x, c), device(z, y, x, 1 - c)]
    for other in others:
        pl.semaphore_signal(barrier, inc=1, device_id=other, device_id_type=MESH)
    pl.semaphore_wait(barrier, len(others))


class Wires:
    def __init__(self, send_sems, recv_sems):
        self.send_sems, self.recv_sems, self.sent = send_sems, recv_sems, []

    def copy(self, slot, source, target, other):
        return pltpu.make_async_remote_copy(
            src_ref=source,
            dst_ref=target,
            send_sem=self.send_sems.at[slot],
            recv_sem=self.recv_sems.at[slot],
            device_id=other,
            device_id_type=MESH,
        )

    def send(self, slot, source, target, other):
        copy = self.copy(slot, source, target, other)
        copy.start()
        self.sent.append(copy)

    def arrived(self, slot, target):
        z, y, x, c = place()
        self.copy(slot, target, target, device(z, y, x, 1 - c)).wait_recv()

    def finish(self):
        for copy in self.sent:
            copy.wait_send()


GATHER_SLOTS = 12
ALL = slice(None)


def gather_kernel(items, n_weights, *refs):
    shares = refs[:n_weights]
    gains = refs[n_weights]
    full = refs[n_weights + 1 : 2 * n_weights + 1]
    full_gains = refs[2 * n_weights + 1]
    send_sems, recv_sems, own_sems = refs[2 * n_weights + 2 :]
    z, y, x, c = place()
    far = [lax.rem(z + k, 4) for k in range(4)]
    back = [lax.rem(z + 4 - k, 4) for k in range(4)]
    x_other, y_other, c_other = (
        device(z, y, 1 - x, c),
        device(z, 1 - y, x, c),
        device(z, y, x, 1 - c),
    )
    greet()
    wires = Wires(send_sems, recv_sems)
    own = [
        pltpu.make_async_copy(share, whole.at[z, y], own_sems.at[i])
        for i, (share, whole) in enumerate(zip(shares, full))
    ]
    own_gains = pltpu.make_async_copy(gains, full_gains.at[z, y], own_sems.at[n_weights])
    own_gains.start()
    gain_slot = GATHER_SLOTS * len(items)
    for k in (1, 2, 3):
        wires.send(gain_slot + k, gains, full_gains.at[z, y], device(far[k], y, x, c))
    for copy in own:
        copy.start()

    def slot(i, k):
        return GATHER_SLOTS * i + k

    def along_z(i):
        item = items[i]
        share, whole = shares[item.weight], full[item.weight]
        for k in (1, 2, 3):
            wires.send(
                slot(i, k),
                item.quarter(share, (), c, x),
                item.quarter(whole, (z, y), c, x),
                device(far[k], y, x, c),
            )

    own_done = set()

    def first_hop(i):
        item = items[i]
        whole = full[item.weight]
        if item.weight not in own_done:
            own[item.weight].wait()
            own_done.add(item.weight)
        for k in (1, 2, 3):
            block = item.quarter(whole, (back[k], y), c, x)
            wires.arrived(slot(i, k), block)
            wires.send(slot(i, 3 + k), block, block, x_other)
        if not item.x_first:
            block = item.quarter(whole, (ALL, y), c, x)
            wires.send(slot(i, 7), block, block, y_other)

    def second_hop(i):
        item = items[i]
        whole = full[item.weight]
        if not item.x_first:
            block = item.quarter(whole, (ALL, 1 - y), c, x)
            wires.arrived(slot(i, 7), block)
            wires.send(slot(i, 0), block, block, x_other)
        for k in (1, 2, 3):
            wires.arrived(slot(i, 3 + k), item.quarter(whole, (back[k], y), c, 1 - x))
        if item.x_first:
            block = item.half(whole, (ALL, y), c)
            wires.send(slot(i, 7), block, block, y_other)
        for k in (1, 2, 3):
            block = item.half(whole, (back[k], y), c)
            wires.send(slot(i, 7 + k), block, block, c_other)

    def last_hop(i):
        item = items[i]
        whole = full[item.weight]
        block = item.half(whole, (ALL, 1 - y), c)
        if item.x_first:
            wires.arrived(slot(i, 7), block)
        else:
            wires.arrived(slot(i, 0), item.quarter(whole, (ALL, 1 - y), c, 1 - x))
        wires.send(slot(i, 11), block, block, c_other)

    def complete(i):
        item = items[i]
        whole = full[item.weight]
        for k in (1, 2, 3):
            wires.arrived(slot(i, 7 + k), item.half(whole, (back[k], y), 1 - c))
        wires.arrived(slot(i, 11), item.half(whole, (ALL, 1 - y), 1 - c))

    ahead = 3
    for i in range(min(ahead, len(items))):
        along_z(i)
    own_gains.wait()
    for k in (1, 2, 3):
        wires.arrived(gain_slot + k, full_gains.at[back[k], y])
    wires.send(gain_slot, full_gains.at[:, y], full_gains.at[:, y], y_other)
    for step in range(len(items) + 2):
        if 2 <= step < len(items) + 2:
            last_hop(step - 2)
        if 1 <= step < len(items) + 1:
            second_hop(step - 1)
        if step < len(items):
            first_hop(step)
        if step + ahead < len(items):
            along_z(step + ahead)
    wires.arrived(gain_slot, full_gains.at[:, 1 - y])
    for i in range(len(items)):
        complete(i)
    wires.finish()


COLUMNS = (1024, 1024, 1024, 1024, 2816, 2816, None)


def share_view(share, columns):
    return share if columns is None else share.reshape(2, 2, 32, columns)


def whole_shape(columns):
    return (4, 2, 352, 1024) if columns is None else (4, 2, 2, 2, 32, columns)


def gather_weights(weights, gains):
    items = items_of(list(enumerate(COLUMNS)), 512, 64, (0, 3, 6))
    shares = [share_view(w, n) for w, n in zip(weights, COLUMNS)]
    lines = jnp.zeros((16, 128), jnp.bfloat16)
    for i, gain in enumerate(gains):
        lines = lines.at[i].set(gain)
    shapes = [jax.ShapeDtypeStruct(whole_shape(n), jnp.bfloat16) for n in COLUMNS]
    shapes.append(jax.ShapeDtypeStruct((4, 2, 16, 128), jnp.bfloat16))
    count = GATHER_SLOTS * len(items) + 4
    anywhere = pl.BlockSpec(memory_space=pl.ANY)
    out = pl.pallas_call(
        partial(gather_kernel, items, len(shares)),
        out_shape=shapes,
        in_specs=[anywhere] * (len(shares) + 1),
        out_specs=[anywhere] * (len(shares) + 1),
        scratch_shapes=[
            pltpu.SemaphoreType.DMA((count,)),
            pltpu.SemaphoreType.DMA((count,)),
            pltpu.SemaphoreType.DMA((len(shares) + 1,)),
        ],
        compiler_params=pltpu.CompilerParams(collective_id=0, has_side_effects=True),
        name="gather_weights",
    )(*shares, lines)
    whole = [w.reshape(-1, w.shape[-1]) for w in out[:-1]]
    return whole, [out[-1][:, :, i].reshape(1024) for i in range(len(gains))]


SUM_SLOTS = 12


def plus(left, right):
    return (left.astype(jnp.float32) + right.astype(jnp.float32)).astype(left.dtype)


def sum_kernel(items, n_weights, *refs):
    refs = list(refs)

    def take(n):
        taken = refs[:n]
        del refs[:n]
        return taken

    grads = take(n_weights)
    (gain_grads,) = take(1)
    sums = take(n_weights)
    (gain_sums,) = take(1)
    mine, from_core = take(len(items)), take(len(items))
    from_first, from_second, from_z = take(len(items)), take(len(items)), take(len(items))
    gain_mine, gain_core, gain_x, gain_y, gain_z = take(5)
    send_sems, recv_sems, load_sems = refs
    z, y, x, c = place()
    far = [lax.rem(z + k, 4) for k in range(4)]
    back = [lax.rem(z + 4 - k, 4) for k in range(4)]
    x_other, y_other, c_other = (
        device(z, y, 1 - x, c),
        device(z, 1 - y, x, c),
        device(z, y, x, 1 - c),
    )
    greet()
    wires = Wires(send_sems, recv_sems)
    loads = {}

    def slot(i, k):
        return SUM_SLOTS * i + k

    def to_core(i):
        item = items[i]
        grad = grads[item.weight]
        if item.tall:
            for side in (0, 1):
                wires.send(
                    slot(i, side),
                    item.quarter(grad, (ALL, ALL), 1 - c, side),
                    from_core[i].at[:, :, side],
                    c_other,
                )
            loads[i] = [
                pltpu.make_async_copy(
                    item.quarter(grad, (ALL, ALL), c, side),
                    mine[i].at[:, :, side],
                    load_sems.at[2 * i + side],
                )
                for side in (0, 1)
            ]
        else:
            wires.send(
                slot(i, 0), item.half(grad, (ALL, ALL), 1 - c), from_core[i], c_other
            )
            loads[i] = [
                pltpu.make_async_copy(
                    item.half(grad, (ALL, ALL), c), mine[i], load_sems.at[2 * i]
                )
            ]
        for load in loads[i]:
            load.start()

    def first_hop(i):
        item, own, other = items[i], mine[i], from_core[i]
        for load in loads[i]:
            load.wait()
        if item.tall:
            for side in (0, 1):
                wires.arrived(slot(i, side), other.at[:, :, side])
        else:
            wires.arrived(slot(i, 0), other)

        def add(at, _):
            for yy in (0, 1):
                for xx in (0, 1):
                    own[at, yy, xx] = plus(own[at, yy, xx], other[at, yy, xx])
            return 0

        lax.fori_loop(0, 4, add, 0)
        if item.x_first:
            wires.send(slot(i, 2), own.at[:, :, 1 - x], from_first[i], x_other)
        else:
            wires.send(slot(i, 2), own.at[:, 1 - y], from_first[i], y_other)

    def second_hop(i):
        item, own, other = items[i], mine[i], from_first[i]
        wires.arrived(slot(i, 2), other)

        def add(at, _):
            for side in (0, 1):
                where = (at, side, x) if item.x_first else (at, y, side)
                own[where] = plus(own[where], other[at, side])
            return 0

        lax.fori_loop(0, 4, add, 0)
        if item.x_first:
            wires.send(slot(i, 3), own.at[:, 1 - y, x], from_second[i], y_other)
        else:
            wires.send(slot(i, 3), own.at[:, y, 1 - x], from_second[i], x_other)

    def along_z(i):
        own, other = mine[i], from_second[i]
        wires.arrived(slot(i, 3), other)

        def add(at, _):
            own[at, y, x] = plus(own[at, y, x], other[at])
            return 0

        lax.fori_loop(0, 4, add, 0)
        for k in (1, 2, 3):
            wires.send(
                slot(i, 3 + k),
                own.at[far[k], y, x],
                from_z[i].at[k - 1],
                device(far[k], y, x, c),
            )

    def to_x(i):
        item = items[i]
        total = mine[i][z, y, x].astype(jnp.float32)
        for k in (1, 2, 3):
            wires.arrived(slot(i, 3 + k), from_z[i].at[k - 1])
            total += from_z[i][k - 1].astype(jnp.float32)
        block = item.quarter(sums[item.weight], (), c, x)
        block[...] = total.astype(jnp.bfloat16)
        wires.send(slot(i, 7), block, block, x_other)

    def to_sibling(i):
        item = items[i]
        wires.arrived(slot(i, 7), item.quarter(sums[item.weight], (), c, 1 - x))
        block = item.half(sums[item.weight], (), c)
        wires.send(slot(i, 8), block, block, c_other)

    def complete(i):
        item = items[i]
        wires.arrived(slot(i, 8), item.half(sums[item.weight], (), 1 - c))

    base = SUM_SLOTS * len(items)
    wires.send(base, gain_grads, gain_core, c_other)
    ahead = 3
    for i in range(min(ahead, len(items))):
        to_core(i)
    wires.arrived(base, gain_core)
    gain_mine[...] = gain_grads[...] + gain_core[...]
    wires.send(base + 1, gain_mine, gain_x, x_other)
    stages = (complete, to_sibling, to_x, along_z, second_hop, first_hop)
    for step in range(len(items) + len(stages) - 1):
        for back_by, stage in zip(range(len(stages) - 1, -1, -1), stages):
            if 0 <= step - back_by < len(items):
                stage(step - back_by)
        if step + ahead < len(items):
            to_core(step + ahead)
        if step == 0:
            wires.arrived(base + 1, gain_x)
            gain_core[...] = gain_mine[...] + gain_x[...]
            wires.send(base + 2, gain_core.at[:, 1 - y], gain_y, y_other)
        if step == 1:
            wires.arrived(base + 2, gain_y)
            gain_y[...] = gain_core[:, y] + gain_y[...]
            for k in (1, 2, 3):
                wires.send(
                    base + 2 + k,
                    gain_y.at[far[k]],
                    gain_z.at[z],
                    device(far[k], y, x, c),
                )
            gain_z[z] = gain_y[z]
    for k in (1, 2, 3):
        wires.arrived(base + 2 + k, gain_z.at[back[k]])
    gain_sums[...] = (gain_z[0] + gain_z[1]) + (gain_z[2] + gain_z[3])
    wires.finish()


def sum_grads(grads, gain_grads):
    items = items_of([(6, None), (4, 2816), (5, 2816), (3, 1024), (0, 1024), (1, 1024), (2, 1024)], 512, 64, (0, 3, 6))
    views = [g.reshape(whole_shape(n)) for g, n in zip(grads, COLUMNS)]
    lines = jnp.zeros((4, 2, 8, 128), jnp.float32)
    for i, grad in enumerate(gain_grads):
        lines = lines.at[:, :, i].set(grad.reshape(4, 2, 128))
    shapes = [
        jax.ShapeDtypeStruct((352, 1024) if n is None else (2, 2, 32, n), jnp.bfloat16)
        for n in COLUMNS
    ]
    shapes.append(jax.ShapeDtypeStruct((8, 128), jnp.float32))
    count = SUM_SLOTS * len(items) + 6
    in_vmem = pl.BlockSpec(memory_space=pltpu.VMEM)

    def buffers(*lead_of):
        return [pltpu.VMEM(lead + item.block, jnp.bfloat16) for item, lead in zip(items, lead_of)]

    gain_line = partial(pltpu.VMEM, dtype=jnp.float32)
    out = pl.pallas_call(
        partial(sum_kernel, items, len(views)),
        out_shape=shapes,
        in_specs=[pl.BlockSpec(memory_space=pl.ANY)] * len(views) + [in_vmem],
        out_specs=[in_vmem] * len(shapes),
        scratch_shapes=buffers(*[(4, 2, 2)] * len(items))
        + buffers(*[(4, 2, 2)] * len(items))
        + buffers(*[(4, 2)] * len(items))
        + buffers(*[(4,)] * len(items))
        + buffers(*[(3,)] * len(items))
        + [
            pltpu.VMEM((4, 2, 8, 128), jnp.float32),
            pltpu.VMEM((4, 2, 8, 128), jnp.float32),
            pltpu.VMEM((4, 2, 8, 128), jnp.float32),
            pltpu.VMEM((4, 8, 128), jnp.float32),
            pltpu.VMEM((4, 8, 128), jnp.float32),
            pltpu.SemaphoreType.DMA((count,)),
            pltpu.SemaphoreType.DMA((count,)),
            pltpu.SemaphoreType.DMA((2 * len(items),)),
        ],
        compiler_params=pltpu.CompilerParams(
            collective_id=1, has_side_effects=True, vmem_limit_bytes=60 * MIB
        ),
        name="sum_grads",
    )(*views, lines)
    shares = [s.reshape(-1, s.shape[-1]).astype(jnp.float32) for s in out[:-1]]
    return shares, [out[-1][i] for i in range(len(gain_grads))]


def gather_plain(weights, gains):
    everything = (*weights, *gains)
    whole = [lax.all_gather(v, "dp", axis=0, tiled=True) for v in everything]
    return whole[: len(weights)], whole[len(weights) :]


def sum_plain(grads, gain_grads):
    shares = [
        lax.psum_scatter(g.astype(jnp.float32), "dp", scatter_dimension=0, tiled=True)
        for g in (*grads, *gain_grads)
    ]
    sums = [lax.psum(s, ("rep", "cores")) for s in shares]
    return sums[: len(grads)], sums[len(grads) :]


def on_device(
    gather,
    add_up,
    tokens,
    norm_attn,
    w_query,
    w_key,
    w_value,
    w_out,
    norm_ffn,
    w_gate,
    w_up,
    w_down,
    lengths,
    cotangent,
):
    rows = tokens.shape[0]
    low = jnp.bfloat16
    allowed, valid = masks(lengths, rows)
    whole, gains = gather(
        (w_query, w_key, w_value, w_out, w_gate, w_up, w_down), (norm_attn, norm_ffn)
    )
    full_query, full_key, full_value, full_out, full_gate, full_up, full_down = whole
    gain_attn, gain_ffn = gains
    inputs = tokens.astype(jnp.float32)
    normed, factor = normalize(inputs)
    hidden = (normed * gain_attn.astype(jnp.float32)).astype(low)
    query = matmul(hidden, full_query).astype(low)
    keyed = matmul(hidden, full_key).astype(low)
    valued = matmul(hidden, full_value).astype(low)
    query_groups, key_groups, value_groups = (to_groups(query), to_groups(keyed), to_groups(valued))
    attended_groups, log_total = lax.map(
        partial(attend, allowed), (query_groups, key_groups, value_groups)
    )
    attended = from_groups(attended_groups)
    residual = inputs + matmul(attended, full_out)
    normed_two, factor_two = normalize(residual)
    hidden_two = (normed_two * gain_ffn.astype(jnp.float32)).astype(low)
    gate = matmul(hidden_two, full_gate)
    upward = matmul(hidden_two, full_up)
    sigma = jax.nn.sigmoid(gate)
    middle = (gate * sigma * upward).astype(low)
    mixed = (valid[:, None] * (residual + matmul(middle, full_down))).astype(low)
    grad_output = cotangent.astype(jnp.float32) * valid[:, None]
    grad_branch = grad_output.astype(low)
    grad_down = matmul_tn(middle, grad_branch)
    grad_middle = matmul_nt(grad_branch, full_down)
    grad_gate_rows = (grad_middle * upward * sigma * (1.0 + gate * (1.0 - sigma))).astype(low)
    grad_up_rows = (grad_middle * gate * sigma).astype(low)
    grad_gate = matmul_tn(hidden_two, grad_gate_rows)
    grad_up = matmul_tn(hidden_two, grad_up_rows)
    grad_hidden_two = matmul_nt(grad_gate_rows, full_gate) + matmul_nt(grad_up_rows, full_up)
    grad_gain_ffn = jnp.sum(grad_hidden_two * normed_two, axis=0)
    grad_residual = grad_output + norm_back(
        grad_hidden_two * gain_ffn.astype(jnp.float32), normed_two, factor_two
    )
    grad_proj = grad_residual.astype(low)
    grad_out = matmul_tn(attended, grad_proj)
    grad_attended = matmul_nt(grad_proj, full_out).astype(low)
    grad_query_g, grad_key_g, grad_value_g = lax.map(
        partial(attend_back, allowed),
        (query_groups, key_groups, value_groups, to_groups(grad_attended), log_total),
    )
    grad_query_rows = from_groups(grad_query_g)
    grad_key_rows = from_groups(grad_key_g)
    grad_value_rows = from_groups(grad_value_g)
    grad_query = matmul_tn(hidden, grad_query_rows)
    grad_key = matmul_tn(hidden, grad_key_rows)
    grad_value = matmul_tn(hidden, grad_value_rows)
    grad_hidden = (
        matmul_nt(grad_query_rows, full_query)
        + matmul_nt(grad_key_rows, full_key)
        + matmul_nt(grad_value_rows, full_value)
    )
    grad_gain_attn = jnp.sum(grad_hidden * normed, axis=0)
    input_grad = grad_residual + norm_back(
        grad_hidden * gain_attn.astype(jnp.float32), normed, factor
    )
    grads = (grad_query, grad_key, grad_value, grad_out, grad_gate, grad_up, grad_down)
    sums, gain_sums = add_up([g.astype(low) for g in grads], (grad_gain_attn, grad_gain_ffn))
    return (
        mixed,
        input_grad,
        gain_sums[0],
        sums[0],
        sums[1],
        sums[2],
        sums[3],
        gain_sums[1],
        sums[4],
        sums[5],
        sums[6],
    )


def solution(mesh):
    tuned = dict(mesh.shape) == {"dp": 8, "rep": 2, "cores": 2}
    gather, add_up = (gather_weights, sum_grads) if tuned else (gather_plain, sum_plain)
    tokens_placed = P(("dp", "rep", "cores"), None)
    share, gain = P("dp", None), P("dp")
    return jax.shard_map(
        partial(on_device, gather, add_up),
        mesh=mesh,
        in_specs=(
            tokens_placed,
            gain,
            share,
            share,
            share,
            share,
            gain,
            share,
            share,
            share,
            tokens_placed,
            tokens_placed,
        ),
        out_specs=(
            tokens_placed,
            tokens_placed,
            gain,
            share,
            share,
            share,
            share,
            gain,
            share,
            share,
            share,
        ),
        check_vma=False,
    )
```

```python
from functools import partial

import jax
import jax.numpy as jnp
from jax import lax
from jax.experimental import pallas as pl
from jax.experimental.pallas import tpu as pltpu
from jax.sharding import PartitionSpec as P

HEADS = 16
HEAD = 64


NORM_EPS = 1e-05
SCORE_SCALE = 0.125
NEGATIVE = -1e30
head_group = 4
MESH = pl.DeviceIdType.MESH
MIB = 1024 * 1024


def masks(block_len, rows):
    bounds = jnp.cumsum(block_len[0])
    place = jnp.arange(rows, dtype=jnp.int32)
    segment = jnp.sum((place[:, None] >= bounds[None, :]).astype(jnp.int32), axis=1)
    allowed = (segment[:, None] == segment[None, :]) & (place[None, :] <= place[:, None])
    valid = (segment < block_len.shape[1]).astype(jnp.float32)
    return (allowed, valid)


def normalize(values):
    factor = lax.rsqrt(jnp.mean(values * values, axis=-1, keepdims=True) + NORM_EPS)
    return (values * factor, factor)


def norm_back(grad_normed, normed, factor):
    return factor * (grad_normed - normed * jnp.mean(grad_normed * normed, axis=-1, keepdims=True))


def matmul(left, right):
    return jnp.dot(left, right, preferred_element_type=jnp.float32)


def matmul_tn(left, right):
    return lax.dot_general(
        left, right, (((0,), (0,)), ((), ())), preferred_element_type=jnp.float32
    )


def matmul_nt(left, right):
    return lax.dot_general(
        left, right, (((1,), (1,)), ((), ())), preferred_element_type=jnp.float32
    )


def to_groups(matrix):
    rows = matrix.shape[0]
    split = matrix.reshape(rows, HEADS // head_group, head_group, HEAD)
    return split.transpose(1, 2, 0, 3)


def from_groups(grouped):
    rows = grouped.shape[2]
    return grouped.transpose(2, 0, 1, 3).reshape(rows, HEADS * HEAD)


def group_scores(allowed, query_g, key_g):
    raw = (
        jnp.einsum("hqe,hke->hqk", query_g, key_g, preferred_element_type=jnp.float32) * SCORE_SCALE
    )
    return jnp.where(allowed[None], raw, NEGATIVE)


def attend(allowed, operands):
    query_g, key_g, value_g = operands
    scores = group_scores(allowed, query_g, key_g)
    top = jnp.max(scores, axis=-1, keepdims=True)
    expo = jnp.exp(scores - top)
    total = jnp.sum(expo, axis=-1, keepdims=True)
    probs_low = (expo / total).astype(jnp.bfloat16)
    result = jnp.einsum("hqk,hke->hqe", probs_low, value_g, preferred_element_type=jnp.float32)
    return (result.astype(jnp.bfloat16), top[..., 0] + jnp.log(total[..., 0]))


def attend_back(allowed, operands):
    query_g, key_g, value_g, grad_g, log_total = operands
    scores = group_scores(allowed, query_g, key_g)
    probs = jnp.exp(scores - log_total[..., None])
    grad_probs = jnp.einsum("hqe,hke->hqk", grad_g, value_g, preferred_element_type=jnp.float32)
    centre = jnp.sum(grad_probs * probs, axis=-1, keepdims=True)
    grad_scores = (probs * (grad_probs - centre)).astype(jnp.bfloat16)
    grad_query = (
        jnp.einsum("hqk,hke->hqe", grad_scores, key_g, preferred_element_type=jnp.float32)
        * SCORE_SCALE
    )
    grad_key = (
        jnp.einsum("hqk,hqe->hke", grad_scores, query_g, preferred_element_type=jnp.float32)
        * SCORE_SCALE
    )
    grad_value = jnp.einsum(
        "hqk,hqe->hke", probs.astype(jnp.bfloat16), grad_g, preferred_element_type=jnp.float32
    )
    return (
        grad_query.astype(jnp.bfloat16),
        grad_key.astype(jnp.bfloat16),
        grad_value.astype(jnp.bfloat16),
    )


class Item:
    def __init__(self, weight, tall, start, size, x_first):
        self.weight, self.tall, self.start, self.size = weight, tall, start, size
        self.x_first = x_first
        self.block = (size, 256) if tall else (32, size)

    def quarter(self, ref, lead, c, x):
        if self.tall:
            columns = pl.ds(pl.multiple_of(c * 512 + x * 256, 256), 256)
            return ref.at[(*lead, pl.ds(self.start, self.size), columns)]
        return ref.at[(*lead, c, x, slice(None), pl.ds(self.start, self.size))]

    def half(self, ref, lead, c):
        if self.tall:
            columns = pl.ds(pl.multiple_of(c * 512, 512), 512)
            return ref.at[(*lead, pl.ds(self.start, self.size), columns)]
        return ref.at[(*lead, c, slice(None), slice(None), pl.ds(self.start, self.size))]


def pieces(total, most):
    return [(start, min(most, total - start)) for start in range(0, total, most)]


def items_of(weights, wide, tall_rows, x_first):
    found = []
    for weight, columns in weights:
        cuts = pieces(352, tall_rows) if columns is None else pieces(columns, wide)
        for start, size in cuts:
            number = len(found)
            found.append(Item(weight, columns is None, start, size, number % 8 in x_first))
    return found


def place():
    d = lax.axis_index("dp")
    return lax.div(d, 2), lax.rem(d, 2), lax.axis_index("rep"), lax.axis_index("cores")


def device(z, y, x, c):
    return {"dp": 2 * z + y, "rep": x, "cores": c}


def greet():
    z, y, x, c = place()
    barrier = pltpu.get_barrier_semaphore()
    others = [device(lax.rem(z + k, 4), y, x, c) for k in (1, 2, 3)]
    others += [device(z, 1 - y, x, c), device(z, y, 1 - x, c), device(z, y, x, 1 - c)]
    for other in others:
        pl.semaphore_signal(barrier, inc=1, device_id=other, device_id_type=MESH)
    pl.semaphore_wait(barrier, len(others))


class Wires:
    def __init__(self, send_sems, recv_sems):
        self.send_sems, self.recv_sems, self.sent = send_sems, recv_sems, []

    def copy(self, slot, source, target, other):
        return pltpu.make_async_remote_copy(
            src_ref=source,
            dst_ref=target,
            send_sem=self.send_sems.at[slot],
            recv_sem=self.recv_sems.at[slot],
            device_id=other,
            device_id_type=MESH,
        )

    def send(self, slot, source, target, other):
        copy = self.copy(slot, source, target, other)
        copy.start()
        self.sent.append(copy)

    def arrived(self, slot, target):
        z, y, x, c = place()
        self.copy(slot, target, target, device(z, y, x, 1 - c)).wait_recv()

    def finish(self):
        for copy in self.sent:
            copy.wait_send()


GATHER_SLOTS = 12
LAG = 2
ALL = slice(None)


def gather_kernel(items, n_weights, *refs):
    shares = refs[:n_weights]
    gains = refs[n_weights]
    full = refs[n_weights + 1 : 2 * n_weights + 1]
    full_gains = refs[2 * n_weights + 1]
    send_sems, recv_sems, own_sems = refs[2 * n_weights + 2 :]
    z, y, x, c = place()
    far = [lax.rem(z + k, 4) for k in range(4)]
    back = [lax.rem(z + 4 - k, 4) for k in range(4)]
    x_other, y_other, c_other = (
        device(z, y, 1 - x, c),
        device(z, 1 - y, x, c),
        device(z, y, x, 1 - c),
    )
    greet()
    wires = Wires(send_sems, recv_sems)
    own = [
        pltpu.make_async_copy(share, whole.at[z, y], own_sems.at[i])
        for i, (share, whole) in enumerate(zip(shares, full))
    ]
    own_gains = pltpu.make_async_copy(gains, full_gains.at[z, y], own_sems.at[n_weights])
    own_gains.start()
    gain_slot = GATHER_SLOTS * len(items)
    for k in (1, 2, 3):
        wires.send(gain_slot + k, gains, full_gains.at[z, y], device(far[k], y, x, c))
    for copy in own:
        copy.start()

    def slot(i, k):
        return GATHER_SLOTS * i + k

    def along_z(i):
        item = items[i]
        share, whole = shares[item.weight], full[item.weight]
        for k in (1, 2, 3):
            wires.send(
                slot(i, k),
                item.quarter(share, (), c, x),
                item.quarter(whole, (z, y), c, x),
                device(far[k], y, x, c),
            )

    own_done = set()

    def first_hop(i):
        item = items[i]
        whole = full[item.weight]
        if item.weight not in own_done:
            own[item.weight].wait()
            own_done.add(item.weight)
        for k in (1, 2, 3):
            block = item.quarter(whole, (back[k], y), c, x)
            wires.arrived(slot(i, k), block)
            wires.send(slot(i, 3 + k), block, block, x_other)
        if not item.x_first:
            block = item.quarter(whole, (ALL, y), c, x)
            wires.send(slot(i, 7), block, block, y_other)

    def second_hop(i):
        item = items[i]
        whole = full[item.weight]
        if not item.x_first:
            block = item.quarter(whole, (ALL, 1 - y), c, x)
            wires.arrived(slot(i, 7), block)
            wires.send(slot(i, 0), block, block, x_other)
        for k in (1, 2, 3):
            wires.arrived(slot(i, 3 + k), item.quarter(whole, (back[k], y), c, 1 - x))
        if item.x_first:
            block = item.half(whole, (ALL, y), c)
            wires.send(slot(i, 7), block, block, y_other)
        for k in (1, 2, 3):
            block = item.half(whole, (back[k], y), c)
            wires.send(slot(i, 7 + k), block, block, c_other)

    def last_hop(i):
        item = items[i]
        whole = full[item.weight]
        block = item.half(whole, (ALL, 1 - y), c)
        if item.x_first:
            wires.arrived(slot(i, 7), block)
        else:
            wires.arrived(slot(i, 0), item.quarter(whole, (ALL, 1 - y), c, 1 - x))
        wires.send(slot(i, 11), block, block, c_other)

    def complete(i):
        item = items[i]
        whole = full[item.weight]
        for k in (1, 2, 3):
            wires.arrived(slot(i, 7 + k), item.half(whole, (back[k], y), 1 - c))
        wires.arrived(slot(i, 11), item.half(whole, (ALL, 1 - y), 1 - c))

    ahead = 3
    for i in range(min(ahead, len(items))):
        along_z(i)
    own_gains.wait()
    for k in (1, 2, 3):
        wires.arrived(gain_slot + k, full_gains.at[back[k], y])
    wires.send(gain_slot, full_gains.at[:, y], full_gains.at[:, y], y_other)
    stages = (last_hop, second_hop, first_hop)
    for step in range(len(items) + 2 * LAG):
        for late, stage in zip((2 * LAG, LAG, 0), stages):
            if 0 <= step - late < len(items):
                stage(step - late)
        if step + ahead < len(items):
            along_z(step + ahead)
    wires.arrived(gain_slot, full_gains.at[:, 1 - y])
    for i in range(len(items)):
        complete(i)
    wires.finish()


COLUMNS = (1024, 1024, 1024, 1024, 2816, 2816, None)


def share_view(share, columns):
    return share if columns is None else share.reshape(2, 2, 32, columns)


def whole_shape(columns):
    return (4, 2, 352, 1024) if columns is None else (4, 2, 2, 2, 32, columns)


def gather_weights(weights, gains):
    items = items_of(list(enumerate(COLUMNS)), 1024, 128, (0, 3, 6))
    shares = [share_view(w, n) for w, n in zip(weights, COLUMNS)]
    lines = jnp.zeros((16, 128), jnp.bfloat16)
    for i, gain in enumerate(gains):
        lines = lines.at[i].set(gain)
    shapes = [jax.ShapeDtypeStruct(whole_shape(n), jnp.bfloat16) for n in COLUMNS]
    shapes.append(jax.ShapeDtypeStruct((4, 2, 16, 128), jnp.bfloat16))
    count = GATHER_SLOTS * len(items) + 4
    anywhere = pl.BlockSpec(memory_space=pl.ANY)
    out = pl.pallas_call(
        partial(gather_kernel, items, len(shares)),
        out_shape=shapes,
        in_specs=[anywhere] * (len(shares) + 1),
        out_specs=[anywhere] * (len(shares) + 1),
        scratch_shapes=[
            pltpu.SemaphoreType.DMA((count,)),
            pltpu.SemaphoreType.DMA((count,)),
            pltpu.SemaphoreType.DMA((len(shares) + 1,)),
        ],
        compiler_params=pltpu.CompilerParams(collective_id=0, has_side_effects=True),
        name="gather_weights",
    )(*shares, lines)
    whole = [w.reshape(-1, w.shape[-1]) for w in out[:-1]]
    return whole, [out[-1][:, :, i].reshape(1024) for i in range(len(gains))]


SUM_SLOTS = 12


def plus(left, right):
    return (left.astype(jnp.float32) + right.astype(jnp.float32)).astype(left.dtype)


def sum_kernel(items, n_weights, *refs):
    refs = list(refs)

    def take(n):
        taken = refs[:n]
        del refs[:n]
        return taken

    grads = take(n_weights)
    (gain_grads,) = take(1)
    sums = take(n_weights)
    (gain_sums,) = take(1)
    mine, from_core = take(len(items)), take(len(items))
    from_first, from_second, from_z = take(len(items)), take(len(items)), take(len(items))
    gain_mine, gain_core, gain_x, gain_y, gain_z = take(5)
    send_sems, recv_sems, load_sems = refs
    z, y, x, c = place()
    far = [lax.rem(z + k, 4) for k in range(4)]
    back = [lax.rem(z + 4 - k, 4) for k in range(4)]
    x_other, y_other, c_other = (
        device(z, y, 1 - x, c),
        device(z, 1 - y, x, c),
        device(z, y, x, 1 - c),
    )
    greet()
    wires = Wires(send_sems, recv_sems)
    loads = {}

    def slot(i, k):
        return SUM_SLOTS * i + k

    def to_core(i):
        item = items[i]
        grad = grads[item.weight]
        if item.tall:
            for side in (0, 1):
                wires.send(
                    slot(i, side),
                    item.quarter(grad, (ALL, ALL), 1 - c, side),
                    from_core[i].at[:, :, side],
                    c_other,
                )
            loads[i] = [
                pltpu.make_async_copy(
                    item.quarter(grad, (ALL, ALL), c, side),
                    mine[i].at[:, :, side],
                    load_sems.at[2 * i + side],
                )
                for side in (0, 1)
            ]
        else:
            wires.send(
                slot(i, 0), item.half(grad, (ALL, ALL), 1 - c), from_core[i], c_other
            )
            loads[i] = [
                pltpu.make_async_copy(
                    item.half(grad, (ALL, ALL), c), mine[i], load_sems.at[2 * i]
                )
            ]
        for load in loads[i]:
            load.start()

    def first_hop(i):
        item, own, other = items[i], mine[i], from_core[i]
        for load in loads[i]:
            load.wait()
        if item.tall:
            for side in (0, 1):
                wires.arrived(slot(i, side), other.at[:, :, side])
        else:
            wires.arrived(slot(i, 0), other)

        def add(at, _):
            for yy in (0, 1):
                for xx in (0, 1):
                    own[at, yy, xx] = plus(own[at, yy, xx], other[at, yy, xx])
            return 0

        lax.fori_loop(0, 4, add, 0)
        if item.x_first:
            wires.send(slot(i, 2), own.at[:, :, 1 - x], from_first[i], x_other)
        else:
            wires.send(slot(i, 2), own.at[:, 1 - y], from_first[i], y_other)

    def second_hop(i):
        item, own, other = items[i], mine[i], from_first[i]
        wires.arrived(slot(i, 2), other)

        def add(at, _):
            for side in (0, 1):
                where = (at, side, x) if item.x_first else (at, y, side)
                own[where] = plus(own[where], other[at, side])
            return 0

        lax.fori_loop(0, 4, add, 0)
        if item.x_first:
            wires.send(slot(i, 3), own.at[:, 1 - y, x], from_second[i], y_other)
        else:
            wires.send(slot(i, 3), own.at[:, y, 1 - x], from_second[i], x_other)

    def along_z(i):
        own, other = mine[i], from_second[i]
        wires.arrived(slot(i, 3), other)

        def add(at, _):
            own[at, y, x] = plus(own[at, y, x], other[at])
            return 0

        lax.fori_loop(0, 4, add, 0)
        for k in (1, 2, 3):
            wires.send(
                slot(i, 3 + k),
                own.at[far[k], y, x],
                from_z[i].at[k - 1],
                device(far[k], y, x, c),
            )

    def to_x(i):
        item = items[i]
        total = mine[i][z, y, x].astype(jnp.float32)
        for k in (1, 2, 3):
            wires.arrived(slot(i, 3 + k), from_z[i].at[k - 1])
            total += from_z[i][k - 1].astype(jnp.float32)
        block = item.quarter(sums[item.weight], (), c, x)
        block[...] = total.astype(jnp.bfloat16)
        wires.send(slot(i, 7), block, block, x_other)

    def to_sibling(i):
        item = items[i]
        wires.arrived(slot(i, 7), item.quarter(sums[item.weight], (), c, 1 - x))
        block = item.half(sums[item.weight], (), c)
        wires.send(slot(i, 8), block, block, c_other)

    def complete(i):
        item = items[i]
        wires.arrived(slot(i, 8), item.half(sums[item.weight], (), 1 - c))

    base = SUM_SLOTS * len(items)
    wires.send(base, gain_grads, gain_core, c_other)
    ahead = 3
    for i in range(min(ahead, len(items))):
        to_core(i)
    wires.arrived(base, gain_core)
    gain_mine[...] = gain_grads[...] + gain_core[...]
    wires.send(base + 1, gain_mine, gain_x, x_other)
    stages = (complete, to_sibling, to_x, along_z, second_hop, first_hop)
    for step in range(len(items) + LAG * (len(stages) - 1)):
        for number, stage in enumerate(stages):
            late = LAG * (len(stages) - 1 - number)
            if 0 <= step - late < len(items):
                stage(step - late)
        if step + ahead < len(items):
            to_core(step + ahead)
        if step == 0:
            wires.arrived(base + 1, gain_x)
            gain_core[...] = gain_mine[...] + gain_x[...]
            wires.send(base + 2, gain_core.at[:, 1 - y], gain_y, y_other)
        if step == 1:
            wires.arrived(base + 2, gain_y)
            gain_y[...] = gain_core[:, y] + gain_y[...]
            for k in (1, 2, 3):
                wires.send(
                    base + 2 + k,
                    gain_y.at[far[k]],
                    gain_z.at[z],
                    device(far[k], y, x, c),
                )
            gain_z[z] = gain_y[z]
    for k in (1, 2, 3):
        wires.arrived(base + 2 + k, gain_z.at[back[k]])
    gain_sums[...] = (gain_z[0] + gain_z[1]) + (gain_z[2] + gain_z[3])
    wires.finish()


def sum_grads(grads, gain_grads):
    items = items_of([(6, None), (4, 2816), (5, 2816), (3, 1024), (0, 1024), (1, 1024), (2, 1024)], 1024, 128, (0, 3, 6))
    views = [g.reshape(whole_shape(n)) for g, n in zip(grads, COLUMNS)]
    lines = jnp.zeros((4, 2, 8, 128), jnp.float32)
    for i, grad in enumerate(gain_grads):
        lines = lines.at[:, :, i].set(grad.reshape(4, 2, 128))
    shapes = [
        jax.ShapeDtypeStruct((352, 1024) if n is None else (2, 2, 32, n), jnp.bfloat16)
        for n in COLUMNS
    ]
    shapes.append(jax.ShapeDtypeStruct((8, 128), jnp.float32))
    count = SUM_SLOTS * len(items) + 6
    in_vmem = pl.BlockSpec(memory_space=pltpu.VMEM)

    def buffers(*lead_of):
        return [pltpu.VMEM(lead + item.block, jnp.bfloat16) for item, lead in zip(items, lead_of)]

    gain_line = partial(pltpu.VMEM, dtype=jnp.float32)
    out = pl.pallas_call(
        partial(sum_kernel, items, len(views)),
        out_shape=shapes,
        in_specs=[pl.BlockSpec(memory_space=pl.ANY)] * len(views) + [in_vmem],
        out_specs=[in_vmem] * len(shapes),
        scratch_shapes=buffers(*[(4, 2, 2)] * len(items))
        + buffers(*[(4, 2, 2)] * len(items))
        + buffers(*[(4, 2)] * len(items))
        + buffers(*[(4,)] * len(items))
        + buffers(*[(3,)] * len(items))
        + [
            pltpu.VMEM((4, 2, 8, 128), jnp.float32),
            pltpu.VMEM((4, 2, 8, 128), jnp.float32),
            pltpu.VMEM((4, 2, 8, 128), jnp.float32),
            pltpu.VMEM((4, 8, 128), jnp.float32),
            pltpu.VMEM((4, 8, 128), jnp.float32),
            pltpu.SemaphoreType.DMA((count,)),
            pltpu.SemaphoreType.DMA((count,)),
            pltpu.SemaphoreType.DMA((2 * len(items),)),
        ],
        compiler_params=pltpu.CompilerParams(
            collective_id=1, has_side_effects=True, vmem_limit_bytes=60 * MIB
        ),
        name="sum_grads",
    )(*views, lines)
    shares = [s.reshape(-1, s.shape[-1]).astype(jnp.float32) for s in out[:-1]]
    return shares, [out[-1][i] for i in range(len(gain_grads))]


def gather_plain(weights, gains):
    everything = (*weights, *gains)
    whole = [lax.all_gather(v, "dp", axis=0, tiled=True) for v in everything]
    return whole[: len(weights)], whole[len(weights) :]


def sum_plain(grads, gain_grads):
    shares = [
        lax.psum_scatter(g.astype(jnp.float32), "dp", scatter_dimension=0, tiled=True)
        for g in (*grads, *gain_grads)
    ]
    sums = [lax.psum(s, ("rep", "cores")) for s in shares]
    return sums[: len(grads)], sums[len(grads) :]


def on_device(
    gather,
    add_up,
    tokens,
    norm_attn,
    w_query,
    w_key,
    w_value,
    w_out,
    norm_ffn,
    w_gate,
    w_up,
    w_down,
    lengths,
    cotangent,
):
    rows = tokens.shape[0]
    low = jnp.bfloat16
    allowed, valid = masks(lengths, rows)
    whole, gains = gather(
        (w_query, w_key, w_value, w_out, w_gate, w_up, w_down), (norm_attn, norm_ffn)
    )
    full_query, full_key, full_value, full_out, full_gate, full_up, full_down = whole
    gain_attn, gain_ffn = gains
    inputs = tokens.astype(jnp.float32)
    normed, factor = normalize(inputs)
    hidden = (normed * gain_attn.astype(jnp.float32)).astype(low)
    query = matmul(hidden, full_query).astype(low)
    keyed = matmul(hidden, full_key).astype(low)
    valued = matmul(hidden, full_value).astype(low)
    query_groups, key_groups, value_groups = (to_groups(query), to_groups(keyed), to_groups(valued))
    attended_groups, log_total = lax.map(
        partial(attend, allowed), (query_groups, key_groups, value_groups)
    )
    attended = from_groups(attended_groups)
    residual = inputs + matmul(attended, full_out)
    normed_two, factor_two = normalize(residual)
    hidden_two = (normed_two * gain_ffn.astype(jnp.float32)).astype(low)
    gate = matmul(hidden_two, full_gate)
    upward = matmul(hidden_two, full_up)
    sigma = jax.nn.sigmoid(gate)
    middle = (gate * sigma * upward).astype(low)
    mixed = (valid[:, None] * (residual + matmul(middle, full_down))).astype(low)
    grad_output = cotangent.astype(jnp.float32) * valid[:, None]
    grad_branch = grad_output.astype(low)
    grad_down = matmul_tn(middle, grad_branch)
    grad_middle = matmul_nt(grad_branch, full_down)
    grad_gate_rows = (grad_middle * upward * sigma * (1.0 + gate * (1.0 - sigma))).astype(low)
    grad_up_rows = (grad_middle * gate * sigma).astype(low)
    grad_gate = matmul_tn(hidden_two, grad_gate_rows)
    grad_up = matmul_tn(hidden_two, grad_up_rows)
    grad_hidden_two = matmul_nt(grad_gate_rows, full_gate) + matmul_nt(grad_up_rows, full_up)
    grad_gain_ffn = jnp.sum(grad_hidden_two * normed_two, axis=0)
    grad_residual = grad_output + norm_back(
        grad_hidden_two * gain_ffn.astype(jnp.float32), normed_two, factor_two
    )
    grad_proj = grad_residual.astype(low)
    grad_out = matmul_tn(attended, grad_proj)
    grad_attended = matmul_nt(grad_proj, full_out).astype(low)
    grad_query_g, grad_key_g, grad_value_g = lax.map(
        partial(attend_back, allowed),
        (query_groups, key_groups, value_groups, to_groups(grad_attended), log_total),
    )
    grad_query_rows = from_groups(grad_query_g)
    grad_key_rows = from_groups(grad_key_g)
    grad_value_rows = from_groups(grad_value_g)
    grad_query = matmul_tn(hidden, grad_query_rows)
    grad_key = matmul_tn(hidden, grad_key_rows)
    grad_value = matmul_tn(hidden, grad_value_rows)
    grad_hidden = (
        matmul_nt(grad_query_rows, full_query)
        + matmul_nt(grad_key_rows, full_key)
        + matmul_nt(grad_value_rows, full_value)
    )
    grad_gain_attn = jnp.sum(grad_hidden * normed, axis=0)
    input_grad = grad_residual + norm_back(
        grad_hidden * gain_attn.astype(jnp.float32), normed, factor
    )
    grads = (grad_query, grad_key, grad_value, grad_out, grad_gate, grad_up, grad_down)
    sums, gain_sums = add_up([g.astype(low) for g in grads], (grad_gain_attn, grad_gain_ffn))
    return (
        mixed,
        input_grad,
        gain_sums[0],
        sums[0],
        sums[1],
        sums[2],
        sums[3],
        gain_sums[1],
        sums[4],
        sums[5],
        sums[6],
    )


def solution(mesh):
    tuned = dict(mesh.shape) == {"dp": 8, "rep": 2, "cores": 2}
    gather, add_up = (gather_weights, sum_grads) if tuned else (gather_plain, sum_plain)
    tokens_placed = P(("dp", "rep", "cores"), None)
    share, gain = P("dp", None), P("dp")
    return jax.shard_map(
        partial(on_device, gather, add_up),
        mesh=mesh,
        in_specs=(
            tokens_placed,
            gain,
            share,
            share,
            share,
            share,
            gain,
            share,
            share,
            share,
            tokens_placed,
            tokens_placed,
        ),
        out_specs=(
            tokens_placed,
            tokens_placed,
            gain,
            share,
            share,
            share,
            share,
            gain,
            share,
            share,
            share,
        ),
        check_vma=False,
    )
```

```python
from functools import partial

import jax
import jax.numpy as jnp
from jax import lax
from jax.experimental import pallas as pl
from jax.experimental.pallas import tpu as pltpu
from jax.sharding import PartitionSpec as P

HEADS = 16
HEAD = 64


NORM_EPS = 1e-05
SCORE_SCALE = 0.125
NEGATIVE = -1e30
head_group = 4
MESH = pl.DeviceIdType.MESH
MIB = 1024 * 1024


def masks(block_len, rows):
    bounds = jnp.cumsum(block_len[0])
    place = jnp.arange(rows, dtype=jnp.int32)
    segment = jnp.sum((place[:, None] >= bounds[None, :]).astype(jnp.int32), axis=1)
    allowed = (segment[:, None] == segment[None, :]) & (place[None, :] <= place[:, None])
    valid = (segment < block_len.shape[1]).astype(jnp.float32)
    return (allowed, valid)


def normalize(values):
    factor = lax.rsqrt(jnp.mean(values * values, axis=-1, keepdims=True) + NORM_EPS)
    return (values * factor, factor)


def norm_back(grad_normed, normed, factor):
    return factor * (grad_normed - normed * jnp.mean(grad_normed * normed, axis=-1, keepdims=True))


def matmul(left, right):
    return jnp.dot(left, right, preferred_element_type=jnp.float32)


def matmul_tn(left, right):
    return lax.dot_general(
        left, right, (((0,), (0,)), ((), ())), preferred_element_type=jnp.float32
    )


def matmul_nt(left, right):
    return lax.dot_general(
        left, right, (((1,), (1,)), ((), ())), preferred_element_type=jnp.float32
    )


def to_groups(matrix):
    rows = matrix.shape[0]
    split = matrix.reshape(rows, HEADS // head_group, head_group, HEAD)
    return split.transpose(1, 2, 0, 3)


def from_groups(grouped):
    rows = grouped.shape[2]
    return grouped.transpose(2, 0, 1, 3).reshape(rows, HEADS * HEAD)


def group_scores(allowed, query_g, key_g):
    raw = (
        jnp.einsum("hqe,hke->hqk", query_g, key_g, preferred_element_type=jnp.float32) * SCORE_SCALE
    )
    return jnp.where(allowed[None], raw, NEGATIVE)


def attend(allowed, operands):
    query_g, key_g, value_g = operands
    scores = group_scores(allowed, query_g, key_g)
    top = jnp.max(scores, axis=-1, keepdims=True)
    expo = jnp.exp(scores - top)
    total = jnp.sum(expo, axis=-1, keepdims=True)
    probs_low = (expo / total).astype(jnp.bfloat16)
    result = jnp.einsum("hqk,hke->hqe", probs_low, value_g, preferred_element_type=jnp.float32)
    return (result.astype(jnp.bfloat16), top[..., 0] + jnp.log(total[..., 0]))


def attend_back(allowed, operands):
    query_g, key_g, value_g, grad_g, log_total = operands
    scores = group_scores(allowed, query_g, key_g)
    probs = jnp.exp(scores - log_total[..., None])
    grad_probs = jnp.einsum("hqe,hke->hqk", grad_g, value_g, preferred_element_type=jnp.float32)
    centre = jnp.sum(grad_probs * probs, axis=-1, keepdims=True)
    grad_scores = (probs * (grad_probs - centre)).astype(jnp.bfloat16)
    grad_query = (
        jnp.einsum("hqk,hke->hqe", grad_scores, key_g, preferred_element_type=jnp.float32)
        * SCORE_SCALE
    )
    grad_key = (
        jnp.einsum("hqk,hqe->hke", grad_scores, query_g, preferred_element_type=jnp.float32)
        * SCORE_SCALE
    )
    grad_value = jnp.einsum(
        "hqk,hqe->hke", probs.astype(jnp.bfloat16), grad_g, preferred_element_type=jnp.float32
    )
    return (
        grad_query.astype(jnp.bfloat16),
        grad_key.astype(jnp.bfloat16),
        grad_value.astype(jnp.bfloat16),
    )


class Item:
    def __init__(self, weight, tall, start, size, x_first):
        self.weight, self.tall, self.start, self.size = weight, tall, start, size
        self.x_first = x_first
        self.block = (size, 256) if tall else (32, size)

    def quarter(self, ref, lead, c, x):
        if self.tall:
            columns = pl.ds(pl.multiple_of(c * 512 + x * 256, 256), 256)
            return ref.at[(*lead, pl.ds(self.start, self.size), columns)]
        return ref.at[(*lead, c, x, slice(None), pl.ds(self.start, self.size))]

    def half(self, ref, lead, c):
        if self.tall:
            columns = pl.ds(pl.multiple_of(c * 512, 512), 512)
            return ref.at[(*lead, pl.ds(self.start, self.size), columns)]
        return ref.at[(*lead, c, slice(None), slice(None), pl.ds(self.start, self.size))]


def pieces(total, most):
    return [(start, min(most, total - start)) for start in range(0, total, most)]


def items_of(weights, wide, tall_rows, x_first):
    found = []
    for weight, columns in weights:
        cuts = pieces(352, tall_rows) if columns is None else pieces(columns, wide)
        for start, size in cuts:
            number = len(found)
            found.append(Item(weight, columns is None, start, size, number % 8 in x_first))
    return found


def place():
    d = lax.axis_index("dp")
    return lax.div(d, 2), lax.rem(d, 2), lax.axis_index("rep"), lax.axis_index("cores")


def device(z, y, x, c):
    return {"dp": 2 * z + y, "rep": x, "cores": c}


def greet():
    z, y, x, c = place()
    barrier = pltpu.get_barrier_semaphore()
    others = [device(lax.rem(z + k, 4), y, x, c) for k in (1, 2, 3)]
    others += [device(z, 1 - y, x, c), device(z, y, 1 - x, c), device(z, y, x, 1 - c)]
    for other in others:
        pl.semaphore_signal(barrier, inc=1, device_id=other, device_id_type=MESH)
    pl.semaphore_wait(barrier, len(others))


class Wires:
    def __init__(self, send_sems, recv_sems):
        self.send_sems, self.recv_sems, self.sent = send_sems, recv_sems, []

    def copy(self, slot, source, target, other):
        return pltpu.make_async_remote_copy(
            src_ref=source,
            dst_ref=target,
            send_sem=self.send_sems.at[slot],
            recv_sem=self.recv_sems.at[slot],
            device_id=other,
            device_id_type=MESH,
        )

    def send(self, slot, source, target, other):
        copy = self.copy(slot, source, target, other)
        copy.start()
        self.sent.append((slot, copy))

    def arrived(self, slot, target):
        z, y, x, c = place()
        self.copy(slot, target, target, device(z, y, x, 1 - c)).wait_recv()

    def finish(self, chosen=lambda slot: True):
        for slot, copy in self.sent:
            if chosen(slot):
                copy.wait_send()
        self.sent = [(slot, copy) for slot, copy in self.sent if not chosen(slot)]


GATHER_SLOTS = 12
LAG = 2
ALL = slice(None)
COLUMNS = (1024, 1024, 1024, 1024, 2816, 2816, None)
QUERY, KEY, VALUE, OUT, GATE, UP, DOWN = range(7)
TILE = 256
FF_TILE = 256


class Part(Item):
    def quarter(self, ref, lead, c, x):
        if self.tall:
            return Item.quarter(self, ref, lead, c, x)
        return ref.at[(*lead, x, slice(None), self.columns(c))]

    def half(self, ref, lead, c):
        if self.tall:
            return Item.half(self, ref, lead, c)
        return ref.at[(*lead, slice(None), slice(None), self.columns(c))]

    def columns(self, c):
        width = self.size // 2
        return pl.ds(pl.multiple_of(self.start + c * width, 128), width)


def gather_items():
    order = [(w, 0, 1024) for w in (QUERY, KEY, VALUE, OUT)]
    order += [(DOWN, start, size) for start, size in pieces(352, 128)]
    for start, size in pieces(2816, 1024):
        order += [(GATE, start, size), (UP, start, size)]
    return [Part(w, w == DOWN, start, size, i % 8 in (0, 3, 6)) for i, (w, start, size) in enumerate(order)]


def dot(left, right):
    return lax.dot_general(
        left, right, (((1,), (0,)), ((), ())), preferred_element_type=jnp.float32
    )


def dot_nt(left, right):
    return lax.dot_general(
        left, right, (((1,), (1,)), ((), ())), preferred_element_type=jnp.float32
    )


def tile(index, size):
    return pl.ds(pl.multiple_of(index * size, size), size)


def weight_columns(ref, at):
    return ref[:, :, :, :, at].reshape(1024, -1)


class Forward:
    def __init__(self, refs):
        self.__dict__.update(refs)

    def prepare(self):
        for s in range(8):
            self.gain_row[:, 128 * s : 128 * s + 128] = self.gains[s // 2, s % 2]
        length = self.length[0, 0]
        for block in range(4):
            rows = slice(128 * block, 128 * block + 128)
            place_q = lax.broadcasted_iota(jnp.int32, (128, 512), 0) + 128 * block
            place_k = lax.broadcasted_iota(jnp.int32, (128, 512), 1)
            same = (place_q >= length) == (place_k >= length)
            allowed = same & (place_k <= place_q)
            self.bias[rows, :] = jnp.where(allowed, 0.0, NEGATIVE)

        def normed(block, _):
            rows = tile(block, 64)
            values = self.tokens[rows, :].astype(jnp.float32)
            factor = lax.rsqrt(jnp.mean(values * values, axis=-1, keepdims=True) + NORM_EPS)
            gain = self.gain_row[0:1, :].astype(jnp.float32)
            self.hidden[rows, :] = (values * factor * gain).astype(jnp.bfloat16)
            place = lax.broadcasted_iota(jnp.int32, (64, 1024), 0) + 64 * block
            branch = jnp.where(place < length, self.cotangent[rows, :].astype(jnp.float32), 0.0)
            self.branch[rows, :] = branch.astype(jnp.bfloat16)
            return 0

        lax.fori_loop(0, 8, normed, 0)

    def project(self, weight, result):
        def columns(n, _):
            at = tile(n, TILE)
            result[:, at] = dot(self.hidden[...], weight_columns(weight, at)).astype(jnp.bfloat16)
            return 0

        lax.fori_loop(0, 1024 // TILE, columns, 0)

    def attend(self, first, last):
        def pair(p, _):
            at = tile(p, 128)
            left = lax.broadcasted_iota(jnp.int32, (256, 128), 1) < HEAD
            for block in (0, 1):
                rows, seen = slice(256 * block, 256 * block + 256), slice(0, 256 * block + 256)
                query = self.query[rows, at].astype(jnp.float32) * SCORE_SCALE
                outs, totals = [], []
                for side in (left, ~left):
                    own = jnp.where(side, query, 0.0).astype(jnp.bfloat16)
                    scores = dot_nt(own, self.key[seen, at]) + self.bias[rows, seen]
                    top = jnp.max(scores, axis=-1, keepdims=True)
                    expo = jnp.exp(scores - top)
                    total = jnp.sum(expo, axis=-1, keepdims=True)
                    probs = (expo * (1.0 / total)).astype(jnp.bfloat16)
                    outs.append(dot(probs, self.value[seen, at]))
                    totals.append(top + jnp.log(total))
                self.attended[rows, at] = jnp.where(left, outs[0], outs[1]).astype(jnp.bfloat16)
                self.log_total[p, rows, :] = jnp.where(left, totals[0], totals[1])
            return 0

        lax.fori_loop(first, last, pair, 0)

    def project_out(self):
        def columns(n, _):
            at = tile(n, TILE)
            self.residual[:, at] = self.tokens[:, at].astype(jnp.float32) + dot(
                self.attended[...], weight_columns(self.w_out, at)
            )
            return 0

        lax.fori_loop(0, 1024 // TILE, columns, 0)

        def normed(block, _):
            rows = tile(block, 64)
            values = self.residual[rows, :]
            factor = lax.rsqrt(jnp.mean(values * values, axis=-1, keepdims=True) + NORM_EPS)
            gain = self.gain_row[1:2, :].astype(jnp.float32)
            self.hidden_two[rows, :] = (values * factor * gain).astype(jnp.bfloat16)
            return 0

        lax.fori_loop(0, 8, normed, 0)

    def feed_forward(self, first, last):
        def columns(n, first_of_all):
            at = tile(n, FF_TILE)
            low = jnp.bfloat16
            gate_w = weight_columns(self.w_gate, at)
            up_w = weight_columns(self.w_up, at)
            down_w = self.w_down[at, :]
            gate = dot(self.hidden_two[...], gate_w)
            upward = dot(self.hidden_two[...], up_w)
            grad_middle = dot_nt(self.branch[...], down_w)
            sigma = 1.0 / (1.0 + jnp.exp(-gate))
            silu = gate * sigma
            middle = (silu * upward).astype(low)
            grad_up = (grad_middle * silu).astype(low)
            grad_gate = (grad_middle * upward * sigma * (1.0 + gate * (1.0 - sigma))).astype(low)
            self.middle[:, at] = middle
            self.grad_up[:, at] = grad_up
            self.grad_gate[:, at] = grad_gate
            for j in range(4):
                part = slice(256 * j, 256 * j + 256)
                mixed = dot(middle, down_w[:, part])
                grad = dot_nt(grad_gate, gate_w[part, :]) + dot_nt(grad_up, up_w[part, :])
                if first_of_all is True:
                    self.total[:, part] = mixed
                    self.grad_hidden_two[:, part] = grad
                else:
                    self.total[:, part] += mixed
                    self.grad_hidden_two[:, part] += grad
            return 0

        if first == 0:
            columns(0, True)
            first = 1
        lax.fori_loop(first, last, lambda n, _: columns(n, False), 0)

    def finish(self):
        length = self.length[0, 0]

        def rows_of(block, _):
            rows = tile(block, 64)
            place = lax.broadcasted_iota(jnp.int32, (64, 1024), 0) + 64 * block
            mixed = jnp.where(place < length, self.residual[rows, :] + self.total[rows, :], 0.0)
            self.mixed[rows, :] = mixed.astype(jnp.bfloat16)
            return 0

        lax.fori_loop(0, 8, rows_of, 0)


FORWARD_OUTS = (
    ("mixed", (512, 1024), jnp.bfloat16),
    ("hidden", (512, 1024), jnp.bfloat16),
    ("query", (512, 1024), jnp.bfloat16),
    ("key", (512, 1024), jnp.bfloat16),
    ("value", (512, 1024), jnp.bfloat16),
    ("attended", (512, 1024), jnp.bfloat16),
    ("log_total", (8, 512, 128), jnp.float32),
    ("residual", (512, 1024), jnp.float32),
    ("hidden_two", (512, 1024), jnp.bfloat16),
    ("branch", (512, 1024), jnp.bfloat16),
    ("middle", (512, 2816), jnp.bfloat16),
    ("grad_gate", (512, 2816), jnp.bfloat16),
    ("grad_up", (512, 2816), jnp.bfloat16),
    ("grad_hidden_two", (512, 1024), jnp.float32),
    ("gain_row", (16, 1024), jnp.bfloat16),
)
KEPT = (QUERY, KEY, VALUE, OUT)


def share_shape(columns):
    return (352, 1024) if columns is None else (2, 64, columns)


def forward_kernel(items, *refs):
    refs = list(refs)

    def take(n):
        taken = refs[:n]
        del refs[:n]
        return taken

    shares = take(7)
    gains, tokens, cotangent, length = take(4)
    kept = take(len(KEPT))
    outs = dict(zip([name for name, _, _ in FORWARD_OUTS], take(len(FORWARD_OUTS))))
    full = take(7)
    full_gains, bias, total = take(3)
    send_sems, recv_sems, own_sems, keep_sems = refs
    z, y, x, c = place()
    far = [lax.rem(z + k, 4) for k in range(4)]
    back = [lax.rem(z + 4 - k, 4) for k in range(4)]
    x_other, y_other, c_other = (
        device(z, y, 1 - x, c),
        device(z, 1 - y, x, c),
        device(z, y, x, 1 - c),
    )
    greet()
    wires = Wires(send_sems, recv_sems)
    own = [
        pltpu.make_async_copy(share, whole.at[z, y], own_sems.at[i])
        for i, (share, whole) in enumerate(zip(shares, full))
    ]
    own_gains = pltpu.make_async_copy(gains, full_gains.at[z, y], own_sems.at[7])
    keep = [
        pltpu.make_async_copy(full[w], kept[n], keep_sems.at[n]) for n, w in enumerate(KEPT)
    ]
    own_gains.start()
    gain_slot = GATHER_SLOTS * len(items)
    for k in (1, 2, 3):
        wires.send(gain_slot + k, gains, full_gains.at[z, y], device(far[k], y, x, c))
    for copy in own:
        copy.start()

    def slot(i, k):
        return GATHER_SLOTS * i + k

    def along_z(i):
        item = items[i]
        share, whole = shares[item.weight], full[item.weight]
        for k in (1, 2, 3):
            wires.send(
                slot(i, k),
                item.quarter(share, (), c, x),
                item.quarter(whole, (z, y), c, x),
                device(far[k], y, x, c),
            )

    own_done = set()

    def first_hop(i):
        item = items[i]
        whole = full[item.weight]
        if item.weight not in own_done:
            own[item.weight].wait()
            own_done.add(item.weight)
        for k in (1, 2, 3):
            block = item.quarter(whole, (back[k], y), c, x)
            wires.arrived(slot(i, k), block)
            wires.send(slot(i, 3 + k), block, block, x_other)
        if not item.x_first:
            block = item.quarter(whole, (ALL, y), c, x)
            wires.send(slot(i, 7), block, block, y_other)

    def second_hop(i):
        item = items[i]
        whole = full[item.weight]
        if not item.x_first:
            block = item.quarter(whole, (ALL, 1 - y), c, x)
            wires.arrived(slot(i, 7), block)
            wires.send(slot(i, 0), block, block, x_other)
        for k in (1, 2, 3):
            wires.arrived(slot(i, 3 + k), item.quarter(whole, (back[k], y), c, 1 - x))
        if item.x_first:
            block = item.half(whole, (ALL, y), c)
            wires.send(slot(i, 7), block, block, y_other)
        for k in (1, 2, 3):
            block = item.half(whole, (back[k], y), c)
            wires.send(slot(i, 7 + k), block, block, c_other)

    def last_hop(i):
        item = items[i]
        whole = full[item.weight]
        block = item.half(whole, (ALL, 1 - y), c)
        if item.x_first:
            wires.arrived(slot(i, 7), block)
        else:
            wires.arrived(slot(i, 0), item.quarter(whole, (ALL, 1 - y), c, 1 - x))
        wires.send(slot(i, 11), block, block, c_other)

    def complete(i):
        item = items[i]
        whole = full[item.weight]
        for k in (1, 2, 3):
            wires.arrived(slot(i, 7 + k), item.half(whole, (back[k], y), 1 - c))
        wires.arrived(slot(i, 11), item.half(whole, (ALL, 1 - y), 1 - c))

    def retire(i):
        wires.finish(lambda slot: slot // GATHER_SLOTS == i)

    step_of = Forward(
        dict(
            outs,
            tokens=tokens,
            cotangent=cotangent,
            length=length,
            gains=full_gains,
            bias=bias,
            total=total,
            w_out=full[OUT],
            w_gate=full[GATE],
            w_up=full[UP],
            w_down=full[DOWN].reshape(2816, 1024),
        )
    )
    tasks = [(-1, 3, step_of.prepare)]
    for n, name in enumerate(("query", "key", "value")):
        tasks.append((n, 2, partial(step_of.project, full[n], outs[name])))
    tasks += [(2, 3, partial(step_of.attend, p, p + 2)) for p in (0, 2, 4, 6)]
    tasks.append((3, 3, step_of.project_out))
    place_of = 7
    tiles = 0
    for _, size in pieces(2816, 1024):
        for n in range(tiles, tiles + size // FF_TILE):
            tasks.append((place_of + 1, 3, partial(step_of.feed_forward, n, n + 1)))
        tiles += size // FF_TILE
        place_of += 2

    ahead = 3
    for i in range(min(ahead, len(items))):
        along_z(i)
    own_gains.wait()
    for k in (1, 2, 3):
        wires.arrived(gain_slot + k, full_gains.at[back[k], y])
    wires.send(gain_slot, full_gains.at[:, y], full_gains.at[:, y], y_other)
    stages = (retire, complete, last_hop, second_hop, first_hop)
    lates = (3 * LAG, 3 * LAG - 1, 2 * LAG, LAG, 0)
    for step in range(len(items) + 3 * LAG):
        for late, stage in zip(lates, stages):
            if 0 <= step - late < len(items):
                stage(step - late)
        if step + ahead < len(items):
            along_z(step + ahead)
        if step == 0:
            wires.arrived(gain_slot, full_gains.at[:, 1 - y])
        there = step - lates[1]
        if 0 <= there < len(KEPT):
            keep[there].start()
        spent = 0
        while tasks and tasks[0][0] <= there and spent < 6:
            _, cost, task = tasks.pop(0)
            task()
            spent += cost
    for _, _, task in tasks:
        task()
    step_of.finish()
    for copy in keep:
        copy.wait()
    wires.finish()


def forward(tokens, cotangent, lengths, weights, gains):
    items = gather_items()
    shares = [w.reshape(share_shape(n)) for w, n in zip(weights, COLUMNS)]
    lines = jnp.zeros((16, 128), jnp.bfloat16)
    for i, gain in enumerate(gains):
        lines = lines.at[i].set(gain)
    wholes = [(4, 2) + share_shape(n) for n in COLUMNS]
    shapes = [jax.ShapeDtypeStruct(wholes[w], jnp.bfloat16) for w in KEPT]
    shapes += [jax.ShapeDtypeStruct(shape, dtype) for _, shape, dtype in FORWARD_OUTS]
    count = GATHER_SLOTS * len(items) + 4
    anywhere = pl.BlockSpec(memory_space=pl.ANY)
    in_vmem = pl.BlockSpec(memory_space=pltpu.VMEM)
    out = pl.pallas_call(
        partial(forward_kernel, items),
        out_shape=shapes,
        in_specs=[anywhere] * 8
        + [in_vmem] * 2
        + [pl.BlockSpec(memory_space=pltpu.SMEM)],
        out_specs=[anywhere] * len(KEPT) + [in_vmem] * len(FORWARD_OUTS),
        scratch_shapes=[pltpu.VMEM(shape, jnp.bfloat16) for shape in wholes]
        + [
            pltpu.VMEM((4, 2, 16, 128), jnp.bfloat16),
            pltpu.VMEM((512, 512), jnp.float32),
            pltpu.VMEM((512, 1024), jnp.float32),
            pltpu.SemaphoreType.DMA((count,)),
            pltpu.SemaphoreType.DMA((count,)),
            pltpu.SemaphoreType.DMA((8,)),
            pltpu.SemaphoreType.DMA((len(KEPT),)),
        ],
        compiler_params=pltpu.CompilerParams(
            collective_id=0, has_side_effects=True, vmem_limit_bytes=60 * MIB
        ),
        name="gather_forward",
    )(*shares, lines, tokens, cotangent, lengths)
    kept = [w.reshape(-1, w.shape[-1]) for w in out[: len(KEPT)]]
    return kept, dict(zip([name for name, _, _ in FORWARD_OUTS], out[len(KEPT) :]))


def whole_shape(columns):
    return (4, 2, 352, 1024) if columns is None else (4, 2, 2, 2, 32, columns)


SUM_SLOTS = 12


def plus(left, right):
    return (left.astype(jnp.float32) + right.astype(jnp.float32)).astype(left.dtype)


def sum_kernel(items, n_weights, *refs):
    refs = list(refs)

    def take(n):
        taken = refs[:n]
        del refs[:n]
        return taken

    grads = take(n_weights)
    (gain_grads,) = take(1)
    sums = take(n_weights)
    (gain_sums,) = take(1)
    mine, from_core = take(len(items)), take(len(items))
    from_first, from_second, from_z = take(len(items)), take(len(items)), take(len(items))
    gain_mine, gain_core, gain_x, gain_y, gain_z = take(5)
    send_sems, recv_sems, load_sems = refs
    z, y, x, c = place()
    far = [lax.rem(z + k, 4) for k in range(4)]
    back = [lax.rem(z + 4 - k, 4) for k in range(4)]
    x_other, y_other, c_other = (
        device(z, y, 1 - x, c),
        device(z, 1 - y, x, c),
        device(z, y, x, 1 - c),
    )
    greet()
    wires = Wires(send_sems, recv_sems)
    loads = {}

    def slot(i, k):
        return SUM_SLOTS * i + k

    def to_core(i):
        item = items[i]
        grad = grads[item.weight]
        if item.tall:
            for side in (0, 1):
                wires.send(
                    slot(i, side),
                    item.quarter(grad, (ALL, ALL), 1 - c, side),
                    from_core[i].at[:, :, side],
                    c_other,
                )
            loads[i] = [
                pltpu.make_async_copy(
                    item.quarter(grad, (ALL, ALL), c, side),
                    mine[i].at[:, :, side],
                    load_sems.at[2 * i + side],
                )
                for side in (0, 1)
            ]
        else:
            wires.send(
                slot(i, 0), item.half(grad, (ALL, ALL), 1 - c), from_core[i], c_other
            )
            loads[i] = [
                pltpu.make_async_copy(
                    item.half(grad, (ALL, ALL), c), mine[i], load_sems.at[2 * i]
                )
            ]
        for load in loads[i]:
            load.start()

    def first_hop(i):
        item, own, other = items[i], mine[i], from_core[i]
        for load in loads[i]:
            load.wait()
        if item.tall:
            for side in (0, 1):
                wires.arrived(slot(i, side), other.at[:, :, side])
        else:
            wires.arrived(slot(i, 0), other)

        def add(at, _):
            for yy in (0, 1):
                for xx in (0, 1):
                    own[at, yy, xx] = plus(own[at, yy, xx], other[at, yy, xx])
            return 0

        lax.fori_loop(0, 4, add, 0)
        if item.x_first:
            wires.send(slot(i, 2), own.at[:, :, 1 - x], from_first[i], x_other)
        else:
            wires.send(slot(i, 2), own.at[:, 1 - y], from_first[i], y_other)

    def second_hop(i):
        item, own, other = items[i], mine[i], from_first[i]
        wires.arrived(slot(i, 2), other)

        def add(at, _):
            for side in (0, 1):
                where = (at, side, x) if item.x_first else (at, y, side)
                own[where] = plus(own[where], other[at, side])
            return 0

        lax.fori_loop(0, 4, add, 0)
        if item.x_first:
            wires.send(slot(i, 3), own.at[:, 1 - y, x], from_second[i], y_other)
        else:
            wires.send(slot(i, 3), own.at[:, y, 1 - x], from_second[i], x_other)

    def along_z(i):
        own, other = mine[i], from_second[i]
        wires.arrived(slot(i, 3), other)

        def add(at, _):
            own[at, y, x] = plus(own[at, y, x], other[at])
            return 0

        lax.fori_loop(0, 4, add, 0)
        for k in (1, 2, 3):
            wires.send(
                slot(i, 3 + k),
                own.at[far[k], y, x],
                from_z[i].at[k - 1],
                device(far[k], y, x, c),
            )

    def to_x(i):
        item = items[i]
        total = mine[i][z, y, x].astype(jnp.float32)
        for k in (1, 2, 3):
            wires.arrived(slot(i, 3 + k), from_z[i].at[k - 1])
            total += from_z[i][k - 1].astype(jnp.float32)
        block = item.quarter(sums[item.weight], (), c, x)
        block[...] = total.astype(jnp.bfloat16)
        wires.send(slot(i, 7), block, block, x_other)

    def to_sibling(i):
        item = items[i]
        wires.arrived(slot(i, 7), item.quarter(sums[item.weight], (), c, 1 - x))
        block = item.half(sums[item.weight], (), c)
        wires.send(slot(i, 8), block, block, c_other)

    def complete(i):
        item = items[i]
        wires.arrived(slot(i, 8), item.half(sums[item.weight], (), 1 - c))

    base = SUM_SLOTS * len(items)
    wires.send(base, gain_grads, gain_core, c_other)
    ahead = 3
    for i in range(min(ahead, len(items))):
        to_core(i)
    wires.arrived(base, gain_core)
    gain_mine[...] = gain_grads[...] + gain_core[...]
    wires.send(base + 1, gain_mine, gain_x, x_other)
    stages = (complete, to_sibling, to_x, along_z, second_hop, first_hop)
    for step in range(len(items) + LAG * (len(stages) - 1)):
        for number, stage in enumerate(stages):
            late = LAG * (len(stages) - 1 - number)
            if 0 <= step - late < len(items):
                stage(step - late)
        if step + ahead < len(items):
            to_core(step + ahead)
        if step == 0:
            wires.arrived(base + 1, gain_x)
            gain_core[...] = gain_mine[...] + gain_x[...]
            wires.send(base + 2, gain_core.at[:, 1 - y], gain_y, y_other)
        if step == 1:
            wires.arrived(base + 2, gain_y)
            gain_y[...] = gain_core[:, y] + gain_y[...]
            for k in (1, 2, 3):
                wires.send(
                    base + 2 + k,
                    gain_y.at[far[k]],
                    gain_z.at[z],
                    device(far[k], y, x, c),
                )
            gain_z[z] = gain_y[z]
    for k in (1, 2, 3):
        wires.arrived(base + 2 + k, gain_z.at[back[k]])
    gain_sums[...] = (gain_z[0] + gain_z[1]) + (gain_z[2] + gain_z[3])
    wires.finish()


def sum_grads(grads, gain_grads):
    items = items_of([(6, None), (4, 2816), (5, 2816), (3, 1024), (0, 1024), (1, 1024), (2, 1024)], 1024, 128, (0, 3, 6))
    views = [g.reshape(whole_shape(n)) for g, n in zip(grads, COLUMNS)]
    lines = jnp.zeros((4, 2, 8, 128), jnp.float32)
    for i, grad in enumerate(gain_grads):
        lines = lines.at[:, :, i].set(grad.reshape(4, 2, 128))
    shapes = [
        jax.ShapeDtypeStruct((352, 1024) if n is None else (2, 2, 32, n), jnp.bfloat16)
        for n in COLUMNS
    ]
    shapes.append(jax.ShapeDtypeStruct((8, 128), jnp.float32))
    count = SUM_SLOTS * len(items) + 6
    in_vmem = pl.BlockSpec(memory_space=pltpu.VMEM)

    def buffers(*lead_of):
        return [pltpu.VMEM(lead + item.block, jnp.bfloat16) for item, lead in zip(items, lead_of)]

    gain_line = partial(pltpu.VMEM, dtype=jnp.float32)
    out = pl.pallas_call(
        partial(sum_kernel, items, len(views)),
        out_shape=shapes,
        in_specs=[pl.BlockSpec(memory_space=pl.ANY)] * len(views) + [in_vmem],
        out_specs=[in_vmem] * len(shapes),
        scratch_shapes=buffers(*[(4, 2, 2)] * len(items))
        + buffers(*[(4, 2, 2)] * len(items))
        + buffers(*[(4, 2)] * len(items))
        + buffers(*[(4,)] * len(items))
        + buffers(*[(3,)] * len(items))
        + [
            pltpu.VMEM((4, 2, 8, 128), jnp.float32),
            pltpu.VMEM((4, 2, 8, 128), jnp.float32),
            pltpu.VMEM((4, 2, 8, 128), jnp.float32),
            pltpu.VMEM((4, 8, 128), jnp.float32),
            pltpu.VMEM((4, 8, 128), jnp.float32),
            pltpu.SemaphoreType.DMA((count,)),
            pltpu.SemaphoreType.DMA((count,)),
            pltpu.SemaphoreType.DMA((2 * len(items),)),
        ],
        compiler_params=pltpu.CompilerParams(
            collective_id=1, has_side_effects=True, vmem_limit_bytes=60 * MIB
        ),
        name="sum_grads",
    )(*views, lines)
    shares = [s.reshape(-1, s.shape[-1]).astype(jnp.float32) for s in out[:-1]]
    return shares, [out[-1][i] for i in range(len(gain_grads))]


def gather_plain(weights, gains):
    everything = (*weights, *gains)
    whole = [lax.all_gather(v, "dp", axis=0, tiled=True) for v in everything]
    return whole[: len(weights)], whole[len(weights) :]


def sum_plain(grads, gain_grads):
    shares = [
        lax.psum_scatter(g.astype(jnp.float32), "dp", scatter_dimension=0, tiled=True)
        for g in (*grads, *gain_grads)
    ]
    sums = [lax.psum(s, ("rep", "cores")) for s in shares]
    return sums[: len(grads)], sums[len(grads) :]


def on_any_device(
    tokens,
    norm_attn,
    w_query,
    w_key,
    w_value,
    w_out,
    norm_ffn,
    w_gate,
    w_up,
    w_down,
    lengths,
    cotangent,
):
    rows = tokens.shape[0]
    low = jnp.bfloat16
    allowed, valid = masks(lengths, rows)
    whole, gains = gather_plain(
        (w_query, w_key, w_value, w_out, w_gate, w_up, w_down), (norm_attn, norm_ffn)
    )
    full_query, full_key, full_value, full_out, full_gate, full_up, full_down = whole
    gain_attn, gain_ffn = gains
    inputs = tokens.astype(jnp.float32)
    normed, factor = normalize(inputs)
    hidden = (normed * gain_attn.astype(jnp.float32)).astype(low)
    query = matmul(hidden, full_query).astype(low)
    keyed = matmul(hidden, full_key).astype(low)
    valued = matmul(hidden, full_value).astype(low)
    query_groups, key_groups, value_groups = (to_groups(query), to_groups(keyed), to_groups(valued))
    attended_groups, log_total = lax.map(
        partial(attend, allowed), (query_groups, key_groups, value_groups)
    )
    attended = from_groups(attended_groups)
    residual = inputs + matmul(attended, full_out)
    normed_two, factor_two = normalize(residual)
    hidden_two = (normed_two * gain_ffn.astype(jnp.float32)).astype(low)
    gate = matmul(hidden_two, full_gate)
    upward = matmul(hidden_two, full_up)
    sigma = jax.nn.sigmoid(gate)
    middle = (gate * sigma * upward).astype(low)
    mixed = (valid[:, None] * (residual + matmul(middle, full_down))).astype(low)
    grad_output = cotangent.astype(jnp.float32) * valid[:, None]
    grad_branch = grad_output.astype(low)
    grad_down = matmul_tn(middle, grad_branch)
    grad_middle = matmul_nt(grad_branch, full_down)
    grad_gate_rows = (grad_middle * upward * sigma * (1.0 + gate * (1.0 - sigma))).astype(low)
    grad_up_rows = (grad_middle * gate * sigma).astype(low)
    grad_gate = matmul_tn(hidden_two, grad_gate_rows)
    grad_up = matmul_tn(hidden_two, grad_up_rows)
    grad_hidden_two = matmul_nt(grad_gate_rows, full_gate) + matmul_nt(grad_up_rows, full_up)
    grad_gain_ffn = jnp.sum(grad_hidden_two * normed_two, axis=0)
    grad_residual = grad_output + norm_back(
        grad_hidden_two * gain_ffn.astype(jnp.float32), normed_two, factor_two
    )
    grad_proj = grad_residual.astype(low)
    grad_out = matmul_tn(attended, grad_proj)
    grad_attended = matmul_nt(grad_proj, full_out).astype(low)
    grad_query_g, grad_key_g, grad_value_g = lax.map(
        partial(attend_back, allowed),
        (query_groups, key_groups, value_groups, to_groups(grad_attended), log_total),
    )
    grad_query_rows = from_groups(grad_query_g)
    grad_key_rows = from_groups(grad_key_g)
    grad_value_rows = from_groups(grad_value_g)
    grad_query = matmul_tn(hidden, grad_query_rows)
    grad_key = matmul_tn(hidden, grad_key_rows)
    grad_value = matmul_tn(hidden, grad_value_rows)
    grad_hidden = (
        matmul_nt(grad_query_rows, full_query)
        + matmul_nt(grad_key_rows, full_key)
        + matmul_nt(grad_value_rows, full_value)
    )
    grad_gain_attn = jnp.sum(grad_hidden * normed, axis=0)
    input_grad = grad_residual + norm_back(
        grad_hidden * gain_attn.astype(jnp.float32), normed, factor
    )
    grads = (grad_query, grad_key, grad_value, grad_out, grad_gate, grad_up, grad_down)
    sums, gain_sums = sum_plain([g.astype(low) for g in grads], (grad_gain_attn, grad_gain_ffn))
    return (
        mixed,
        input_grad,
        gain_sums[0],
        sums[0],
        sums[1],
        sums[2],
        sums[3],
        gain_sums[1],
        sums[4],
        sums[5],
        sums[6],
    )


def backward_tuned(tokens, cotangent, kept, saved, lengths):
    rows = tokens.shape[0]
    low = jnp.bfloat16
    allowed, valid = masks(lengths, rows)
    full_query, full_key, full_value, full_out = kept
    gain_attn, gain_ffn = saved["gain_row"][0], saved["gain_row"][1]
    normed, factor = normalize(tokens.astype(jnp.float32))
    normed_two, factor_two = normalize(saved["residual"])
    hidden, hidden_two, attended = saved["hidden"], saved["hidden_two"], saved["attended"]
    grad_output = cotangent.astype(jnp.float32) * valid[:, None]
    grad_down = matmul_tn(saved["middle"], saved["branch"])
    grad_gate = matmul_tn(hidden_two, saved["grad_gate"])
    grad_up = matmul_tn(hidden_two, saved["grad_up"])
    grad_hidden_two = saved["grad_hidden_two"]
    grad_gain_ffn = jnp.sum(grad_hidden_two * normed_two, axis=0)
    grad_residual = grad_output + norm_back(
        grad_hidden_two * gain_ffn.astype(jnp.float32), normed_two, factor_two
    )
    grad_proj = grad_residual.astype(low)
    grad_out = matmul_tn(attended, grad_proj)
    grad_attended = matmul_nt(grad_proj, full_out).astype(low)
    log_total = saved["log_total"][:, :, ::HEAD].transpose(0, 2, 1).reshape(
        HEADS // head_group, head_group, rows
    )
    grad_query_g, grad_key_g, grad_value_g = lax.map(
        partial(attend_back, allowed),
        (
            to_groups(saved["query"]),
            to_groups(saved["key"]),
            to_groups(saved["value"]),
            to_groups(grad_attended),
            log_total,
        ),
    )
    grad_query_rows = from_groups(grad_query_g)
    grad_key_rows = from_groups(grad_key_g)
    grad_value_rows = from_groups(grad_value_g)
    grad_query = matmul_tn(hidden, grad_query_rows)
    grad_key = matmul_tn(hidden, grad_key_rows)
    grad_value = matmul_tn(hidden, grad_value_rows)
    grad_hidden = (
        matmul_nt(grad_query_rows, full_query)
        + matmul_nt(grad_key_rows, full_key)
        + matmul_nt(grad_value_rows, full_value)
    )
    grad_gain_attn = jnp.sum(grad_hidden * normed, axis=0)
    input_grad = grad_residual + norm_back(
        grad_hidden * gain_attn.astype(jnp.float32), normed, factor
    )
    grads = (grad_query, grad_key, grad_value, grad_out, grad_gate, grad_up, grad_down)
    sums, gain_sums = sum_grads([g.astype(low) for g in grads], (grad_gain_attn, grad_gain_ffn))
    return input_grad, sums, gain_sums


def on_tuned_device(
    tokens,
    norm_attn,
    w_query,
    w_key,
    w_value,
    w_out,
    norm_ffn,
    w_gate,
    w_up,
    w_down,
    lengths,
    cotangent,
):
    weights = (w_query, w_key, w_value, w_out, w_gate, w_up, w_down)
    kept, saved = forward(tokens, cotangent, lengths, weights, (norm_attn, norm_ffn))
    input_grad, sums, gain_sums = backward_tuned(tokens, cotangent, kept, saved, lengths)
    return (
        saved["mixed"],
        input_grad,
        gain_sums[0],
        *sums[:4],
        gain_sums[1],
        *sums[4:],
    )


def solution(mesh):
    tuned = dict(mesh.shape) == {"dp": 8, "rep": 2, "cores": 2}
    tokens_placed = P(("dp", "rep", "cores"), None)
    share, gain = P("dp", None), P("dp")
    return jax.shard_map(
        on_tuned_device if tuned else on_any_device,
        mesh=mesh,
        in_specs=(
            tokens_placed,
            gain,
            share,
            share,
            share,
            share,
            gain,
            share,
            share,
            share,
            tokens_placed,
            tokens_placed,
        ),
        out_specs=(
            tokens_placed,
            tokens_placed,
            gain,
            share,
            share,
            share,
            share,
            gain,
            share,
            share,
            share,
        ),
        check_vma=False,
    )
```

```python
from functools import partial

import jax
import jax.numpy as jnp
from jax import lax
from jax.experimental import pallas as pl
from jax.experimental.pallas import tpu as pltpu
from jax.sharding import PartitionSpec as P

HEADS = 16
HEAD = 64


NORM_EPS = 1e-05
SCORE_SCALE = 0.125
NEGATIVE = -1e30
head_group = 4
MESH = pl.DeviceIdType.MESH
MIB = 1024 * 1024


def masks(block_len, rows):
    bounds = jnp.cumsum(block_len[0])
    place = jnp.arange(rows, dtype=jnp.int32)
    segment = jnp.sum((place[:, None] >= bounds[None, :]).astype(jnp.int32), axis=1)
    allowed = (segment[:, None] == segment[None, :]) & (place[None, :] <= place[:, None])
    valid = (segment < block_len.shape[1]).astype(jnp.float32)
    return (allowed, valid)


def normalize(values):
    factor = lax.rsqrt(jnp.mean(values * values, axis=-1, keepdims=True) + NORM_EPS)
    return (values * factor, factor)


def norm_back(grad_normed, normed, factor):
    return factor * (grad_normed - normed * jnp.mean(grad_normed * normed, axis=-1, keepdims=True))


def matmul(left, right):
    return jnp.dot(left, right, preferred_element_type=jnp.float32)


def matmul_tn(left, right):
    return lax.dot_general(
        left, right, (((0,), (0,)), ((), ())), preferred_element_type=jnp.float32
    )


def matmul_nt(left, right):
    return lax.dot_general(
        left, right, (((1,), (1,)), ((), ())), preferred_element_type=jnp.float32
    )


def to_groups(matrix):
    rows = matrix.shape[0]
    split = matrix.reshape(rows, HEADS // head_group, head_group, HEAD)
    return split.transpose(1, 2, 0, 3)


def from_groups(grouped):
    rows = grouped.shape[2]
    return grouped.transpose(2, 0, 1, 3).reshape(rows, HEADS * HEAD)


def group_scores(allowed, query_g, key_g):
    raw = (
        jnp.einsum("hqe,hke->hqk", query_g, key_g, preferred_element_type=jnp.float32) * SCORE_SCALE
    )
    return jnp.where(allowed[None], raw, NEGATIVE)


def attend(allowed, operands):
    query_g, key_g, value_g = operands
    scores = group_scores(allowed, query_g, key_g)
    top = jnp.max(scores, axis=-1, keepdims=True)
    expo = jnp.exp(scores - top)
    total = jnp.sum(expo, axis=-1, keepdims=True)
    probs_low = (expo / total).astype(jnp.bfloat16)
    result = jnp.einsum("hqk,hke->hqe", probs_low, value_g, preferred_element_type=jnp.float32)
    return (result.astype(jnp.bfloat16), top[..., 0] + jnp.log(total[..., 0]))


def attend_back(allowed, operands):
    query_g, key_g, value_g, grad_g, log_total = operands
    scores = group_scores(allowed, query_g, key_g)
    probs = jnp.exp(scores - log_total[..., None])
    grad_probs = jnp.einsum("hqe,hke->hqk", grad_g, value_g, preferred_element_type=jnp.float32)
    centre = jnp.sum(grad_probs * probs, axis=-1, keepdims=True)
    grad_scores = (probs * (grad_probs - centre)).astype(jnp.bfloat16)
    grad_query = (
        jnp.einsum("hqk,hke->hqe", grad_scores, key_g, preferred_element_type=jnp.float32)
        * SCORE_SCALE
    )
    grad_key = (
        jnp.einsum("hqk,hqe->hke", grad_scores, query_g, preferred_element_type=jnp.float32)
        * SCORE_SCALE
    )
    grad_value = jnp.einsum(
        "hqk,hqe->hke", probs.astype(jnp.bfloat16), grad_g, preferred_element_type=jnp.float32
    )
    return (
        grad_query.astype(jnp.bfloat16),
        grad_key.astype(jnp.bfloat16),
        grad_value.astype(jnp.bfloat16),
    )


class Item:
    def __init__(self, weight, tall, start, size, x_first):
        self.weight, self.tall, self.start, self.size = weight, tall, start, size
        self.x_first = x_first
        self.block = (size, 256) if tall else (32, size)

    def quarter(self, ref, lead, c, x):
        if self.tall:
            columns = pl.ds(pl.multiple_of(c * 512 + x * 256, 256), 256)
            return ref.at[(*lead, pl.ds(self.start, self.size), columns)]
        return ref.at[(*lead, c, x, slice(None), pl.ds(self.start, self.size))]

    def half(self, ref, lead, c):
        if self.tall:
            columns = pl.ds(pl.multiple_of(c * 512, 512), 512)
            return ref.at[(*lead, pl.ds(self.start, self.size), columns)]
        return ref.at[(*lead, c, slice(None), slice(None), pl.ds(self.start, self.size))]


def pieces(total, most):
    return [(start, min(most, total - start)) for start in range(0, total, most)]


def items_of(weights, wide, tall_rows, x_first):
    found = []
    for weight, columns in weights:
        cuts = pieces(352, tall_rows) if columns is None else pieces(columns, wide)
        for start, size in cuts:
            number = len(found)
            found.append(Item(weight, columns is None, start, size, number % 8 in x_first))
    return found


def place():
    d = lax.axis_index("dp")
    return lax.div(d, 2), lax.rem(d, 2), lax.axis_index("rep"), lax.axis_index("cores")


def device(z, y, x, c):
    return {"dp": 2 * z + y, "rep": x, "cores": c}


def greet():
    z, y, x, c = place()
    barrier = pltpu.get_barrier_semaphore()
    others = [device(lax.rem(z + k, 4), y, x, c) for k in (1, 2, 3)]
    others += [device(z, 1 - y, x, c), device(z, y, 1 - x, c), device(z, y, x, 1 - c)]
    for other in others:
        pl.semaphore_signal(barrier, inc=1, device_id=other, device_id_type=MESH)
    pl.semaphore_wait(barrier, len(others))


class Wires:
    def __init__(self, send_sems, recv_sems):
        self.send_sems, self.recv_sems, self.sent = send_sems, recv_sems, []

    def copy(self, slot, source, target, other):
        return pltpu.make_async_remote_copy(
            src_ref=source,
            dst_ref=target,
            send_sem=self.send_sems.at[slot],
            recv_sem=self.recv_sems.at[slot],
            device_id=other,
            device_id_type=MESH,
        )

    def send(self, slot, source, target, other):
        copy = self.copy(slot, source, target, other)
        copy.start()
        self.sent.append((slot, copy))

    def arrived(self, slot, target):
        z, y, x, c = place()
        self.copy(slot, target, target, device(z, y, x, 1 - c)).wait_recv()

    def finish(self, chosen=lambda slot: True):
        for slot, copy in self.sent:
            if chosen(slot):
                copy.wait_send()
        self.sent = [(slot, copy) for slot, copy in self.sent if not chosen(slot)]


GATHER_SLOTS = 12
LAG = 2
ALL = slice(None)
COLUMNS = (1024, 1024, 1024, 1024, 2816, 2816, None)
QUERY, KEY, VALUE, OUT, GATE, UP, DOWN = range(7)
TILE = 256
FF_TILE = 256


class Part(Item):
    def quarter(self, ref, lead, c, x):
        if self.tall:
            return Item.quarter(self, ref, lead, c, x)
        return ref.at[(*lead, x, slice(None), self.columns(c))]

    def half(self, ref, lead, c):
        if self.tall:
            return Item.half(self, ref, lead, c)
        return ref.at[(*lead, slice(None), slice(None), self.columns(c))]

    def columns(self, c):
        width = self.size // 2
        return pl.ds(pl.multiple_of(self.start + c * width, 128), width)


def gather_items():
    order = [(w, 0, 1024) for w in (QUERY, KEY, VALUE, OUT)]
    order += [(DOWN, start, size) for start, size in pieces(352, 128)]
    for start, size in pieces(2816, 1024):
        order += [(GATE, start, size), (UP, start, size)]
    return [Part(w, w == DOWN, start, size, i % 8 in (0, 3, 6)) for i, (w, start, size) in enumerate(order)]


def dot(left, right):
    return lax.dot_general(
        left, right, (((1,), (0,)), ((), ())), preferred_element_type=jnp.float32
    )


def dot_nt(left, right):
    return lax.dot_general(
        left, right, (((1,), (1,)), ((), ())), preferred_element_type=jnp.float32
    )


def tile(index, size):
    return pl.ds(pl.multiple_of(index * size, size), size)


def weight_columns(ref, at):
    return ref[:, :, :, :, at].reshape(1024, -1)


class Forward:
    def __init__(self, refs):
        self.__dict__.update(refs)

    def prepare(self):
        for s in range(8):
            self.gain_row[:, 128 * s : 128 * s + 128] = self.gains[s // 2, s % 2]
        length = self.length[0, 0]
        for block in range(4):
            rows = slice(128 * block, 128 * block + 128)
            place_q = lax.broadcasted_iota(jnp.int32, (128, 512), 0) + 128 * block
            place_k = lax.broadcasted_iota(jnp.int32, (128, 512), 1)
            same = (place_q >= length) == (place_k >= length)
            allowed = same & (place_k <= place_q)
            self.bias[rows, :] = jnp.where(allowed, 0.0, NEGATIVE)

        def normed(block, _):
            rows = tile(block, 64)
            values = self.tokens[rows, :].astype(jnp.float32)
            factor = lax.rsqrt(jnp.mean(values * values, axis=-1, keepdims=True) + NORM_EPS)
            gain = self.gain_row[0:1, :].astype(jnp.float32)
            self.hidden[rows, :] = (values * factor * gain).astype(jnp.bfloat16)
            place = lax.broadcasted_iota(jnp.int32, (64, 1024), 0) + 64 * block
            branch = jnp.where(place < length, self.cotangent[rows, :].astype(jnp.float32), 0.0)
            self.branch[rows, :] = branch.astype(jnp.bfloat16)
            return 0

        lax.fori_loop(0, 8, normed, 0)
        self.turn(self.hidden, self.hidden_t)
        self.out("branch")

    def turn(self, matrix, turned):
        def columns(n, _):
            at = tile(n, 128)
            turned[at, :] = matrix[:, at].astype(jnp.float32).T.astype(jnp.bfloat16)
            return 0

        lax.fori_loop(0, 8, columns, 0)

    def project(self, weight, result):
        def columns(n, _):
            at = tile(n, TILE)
            result[:, at] = dot(self.hidden[...], weight_columns(weight, at)).astype(jnp.bfloat16)
            return 0

        lax.fori_loop(0, 1024 // TILE, columns, 0)

    def attend(self, first, last):
        def pair(p, _):
            at = tile(p, 128)
            left = lax.broadcasted_iota(jnp.int32, (256, 128), 1) < HEAD
            for block in (0, 1):
                rows, seen = slice(256 * block, 256 * block + 256), slice(0, 256 * block + 256)
                query = self.query[rows, at].astype(jnp.float32) * SCORE_SCALE
                outs, totals = [], []
                for side in (left, ~left):
                    own = jnp.where(side, query, 0.0).astype(jnp.bfloat16)
                    scores = dot_nt(own, self.key[seen, at]) + self.bias[rows, seen]
                    top = jnp.max(scores, axis=-1, keepdims=True)
                    expo = jnp.exp(scores - top)
                    total = jnp.sum(expo, axis=-1, keepdims=True)
                    probs = (expo * (1.0 / total)).astype(jnp.bfloat16)
                    outs.append(dot(probs, self.value[seen, at]))
                    totals.append(top + jnp.log(total))
                self.attended[rows, at] = jnp.where(left, outs[0], outs[1]).astype(jnp.bfloat16)
                turned = jnp.where(left, totals[0], totals[1]).T
                self.log_total[p, 0:1, rows] = turned[0:1]
                self.log_total[p, 1:2, rows] = turned[HEAD : HEAD + 1]
            return 0

        lax.fori_loop(first, last, pair, 0)

    def project_out(self):
        def columns(n, _):
            at = tile(n, TILE)
            self.residual[:, at] = self.tokens[:, at].astype(jnp.float32) + dot(
                self.attended[...], weight_columns(self.w_out, at)
            )
            return 0

        lax.fori_loop(0, 1024 // TILE, columns, 0)

        def normed(block, _):
            rows = tile(block, 64)
            values = self.residual[rows, :]
            factor = lax.rsqrt(jnp.mean(values * values, axis=-1, keepdims=True) + NORM_EPS)
            gain = self.gain_row[1:2, :].astype(jnp.float32)
            self.hidden_two[rows, :] = (values * factor * gain).astype(jnp.bfloat16)
            return 0

        lax.fori_loop(0, 8, normed, 0)
        self.turn(self.hidden_two, self.hidden_two_t)
        self.turn(self.attended, self.attended_t)
        for name in ("query", "key", "value", "log_total", "hidden_t", "hidden_two_t", "attended_t"):
            self.out(name)

    def feed_forward(self, first, last):
        def columns(n, first_of_all):
            at = tile(n, FF_TILE)
            low = jnp.bfloat16
            gate_w = weight_columns(self.w_gate, at)
            up_w = weight_columns(self.w_up, at)
            down_w = self.w_down[at, :]
            gate = dot(self.hidden_two[...], gate_w)
            upward = dot(self.hidden_two[...], up_w)
            grad_middle = dot_nt(self.branch[...], down_w)
            sigma = 1.0 / (1.0 + jnp.exp(-gate))
            silu = gate * sigma
            middle = (silu * upward).astype(low)
            grad_up = (grad_middle * silu).astype(low)
            grad_gate = (grad_middle * upward * sigma * (1.0 + gate * (1.0 - sigma))).astype(low)
            self.middle[:, at] = middle
            self.grad_up[:, at] = grad_up
            self.grad_gate[:, at] = grad_gate
            for j in range(4):
                part = slice(256 * j, 256 * j + 256)
                mixed = dot(middle, down_w[:, part])
                grad = dot_nt(grad_gate, gate_w[part, :]) + dot_nt(grad_up, up_w[part, :])
                if first_of_all is True:
                    self.total[:, part] = mixed
                    self.grad_hidden_two[:, part] = grad
                else:
                    self.total[:, part] += mixed
                    self.grad_hidden_two[:, part] += grad
            return 0

        if first == 0:
            columns(0, True)
            first = 1
        lax.fori_loop(first, last, lambda n, _: columns(n, False), 0)

    def flush(self, start, size):
        for name in ("middle", "grad_gate", "grad_up"):
            self.out(name, pl.ds(start, size))

    def finish(self):
        length = self.length[0, 0]
        self.gain_grad[...] = jnp.zeros_like(self.gain_grad)

        def rows_of(block, _):
            rows = tile(block, 64)
            place = lax.broadcasted_iota(jnp.int32, (64, 1024), 0) + 64 * block
            residual = self.residual[rows, :]
            mixed = jnp.where(place < length, residual + self.total[rows, :], 0.0)
            self.mixed[rows, :] = mixed.astype(jnp.bfloat16)
            factor = lax.rsqrt(jnp.mean(residual * residual, axis=-1, keepdims=True) + NORM_EPS)
            normed = residual * factor
            grad = self.grad_hidden_two[rows, :]
            self.gain_grad[...] += jnp.sum((grad * normed).reshape(8, 8, 1024), axis=0)
            grad_normed = grad * self.gain_row[1:2, :].astype(jnp.float32)
            grad_out = jnp.where(place < length, self.cotangent[rows, :].astype(jnp.float32), 0.0)
            mean = jnp.mean(grad_normed * normed, axis=-1, keepdims=True)
            grad_residual = grad_out + factor * (grad_normed - normed * mean)
            self.grad_residual[rows, :] = grad_residual
            self.grad_proj[rows, :] = grad_residual.astype(jnp.bfloat16)
            return 0

        lax.fori_loop(0, 8, rows_of, 0)
        for name in ("mixed", "grad_residual", "grad_proj", "gain_grad", "gain_row"):
            self.out(name)


FORWARD_OUTS = (
    ("mixed", (512, 1024), jnp.bfloat16),
    ("query", (512, 1024), jnp.bfloat16),
    ("key", (512, 1024), jnp.bfloat16),
    ("value", (512, 1024), jnp.bfloat16),
    ("log_total", (8, 8, 512), jnp.float32),
    ("hidden_t", (1024, 512), jnp.bfloat16),
    ("hidden_two_t", (1024, 512), jnp.bfloat16),
    ("attended_t", (1024, 512), jnp.bfloat16),
    ("branch", (512, 1024), jnp.bfloat16),
    ("middle", (512, 2816), jnp.bfloat16),
    ("grad_gate", (512, 2816), jnp.bfloat16),
    ("grad_up", (512, 2816), jnp.bfloat16),
    ("grad_residual", (512, 1024), jnp.float32),
    ("grad_proj", (512, 1024), jnp.bfloat16),
    ("gain_grad", (8, 1024), jnp.float32),
    ("gain_row", (16, 1024), jnp.bfloat16),
)
FORWARD_OWN = (
    ("hidden", (512, 1024), jnp.bfloat16),
    ("attended", (512, 1024), jnp.bfloat16),
    ("residual", (512, 1024), jnp.float32),
    ("hidden_two", (512, 1024), jnp.bfloat16),
    ("grad_hidden_two", (512, 1024), jnp.float32),
    ("bias", (512, 512), jnp.float32),
    ("total", (512, 1024), jnp.float32),
)
OUT_COPIES = len(FORWARD_OUTS) + 6
KEPT = (QUERY, KEY, VALUE, OUT)


def share_shape(columns):
    return (352, 1024) if columns is None else (2, 64, columns)


def forward_kernel(items, *refs):
    refs = list(refs)

    def take(n):
        taken = refs[:n]
        del refs[:n]
        return taken

    shares = take(7)
    gains, tokens, cotangent, length = take(4)
    kept = take(len(KEPT))
    names = [name for name, _, _ in FORWARD_OUTS]
    outs = dict(zip(names, take(len(names))))
    full = take(7)
    (full_gains,) = take(1)
    own_names = names + [name for name, _, _ in FORWARD_OWN]
    state = dict(zip(own_names, take(len(own_names))))
    send_sems, recv_sems, own_sems, keep_sems, out_sems = refs
    outgoing = []

    def put(name, columns=None):
        source, target = state[name], outs[name]
        if columns is not None:
            source, target = source.at[:, columns], target.at[:, columns]
        outgoing.append(pltpu.make_async_copy(source, target, out_sems.at[len(outgoing)]))
        outgoing[-1].start()

    z, y, x, c = place()
    far = [lax.rem(z + k, 4) for k in range(4)]
    back = [lax.rem(z + 4 - k, 4) for k in range(4)]
    x_other, y_other, c_other = (
        device(z, y, 1 - x, c),
        device(z, 1 - y, x, c),
        device(z, y, x, 1 - c),
    )
    greet()
    wires = Wires(send_sems, recv_sems)
    own = [
        pltpu.make_async_copy(share, whole.at[z, y], own_sems.at[i])
        for i, (share, whole) in enumerate(zip(shares, full))
    ]
    own_gains = pltpu.make_async_copy(gains, full_gains.at[z, y], own_sems.at[7])
    keep = [
        pltpu.make_async_copy(full[w], kept[n], keep_sems.at[n]) for n, w in enumerate(KEPT)
    ]
    own_gains.start()
    gain_slot = GATHER_SLOTS * len(items)
    for k in (1, 2, 3):
        wires.send(gain_slot + k, gains, full_gains.at[z, y], device(far[k], y, x, c))
    for copy in own:
        copy.start()

    def slot(i, k):
        return GATHER_SLOTS * i + k

    def along_z(i):
        item = items[i]
        share, whole = shares[item.weight], full[item.weight]
        for k in (1, 2, 3):
            wires.send(
                slot(i, k),
                item.quarter(share, (), c, x),
                item.quarter(whole, (z, y), c, x),
                device(far[k], y, x, c),
            )

    own_done = set()

    def first_hop(i):
        item = items[i]
        whole = full[item.weight]
        if item.weight not in own_done:
            own[item.weight].wait()
            own_done.add(item.weight)
        for k in (1, 2, 3):
            block = item.quarter(whole, (back[k], y), c, x)
            wires.arrived(slot(i, k), block)
            wires.send(slot(i, 3 + k), block, block, x_other)
        if not item.x_first:
            block = item.quarter(whole, (ALL, y), c, x)
            wires.send(slot(i, 7), block, block, y_other)

    def second_hop(i):
        item = items[i]
        whole = full[item.weight]
        if not item.x_first:
            block = item.quarter(whole, (ALL, 1 - y), c, x)
            wires.arrived(slot(i, 7), block)
            wires.send(slot(i, 0), block, block, x_other)
        for k in (1, 2, 3):
            wires.arrived(slot(i, 3 + k), item.quarter(whole, (back[k], y), c, 1 - x))
        if item.x_first:
            block = item.half(whole, (ALL, y), c)
            wires.send(slot(i, 7), block, block, y_other)
        for k in (1, 2, 3):
            block = item.half(whole, (back[k], y), c)
            wires.send(slot(i, 7 + k), block, block, c_other)

    def last_hop(i):
        item = items[i]
        whole = full[item.weight]
        block = item.half(whole, (ALL, 1 - y), c)
        if item.x_first:
            wires.arrived(slot(i, 7), block)
        else:
            wires.arrived(slot(i, 0), item.quarter(whole, (ALL, 1 - y), c, 1 - x))
        wires.send(slot(i, 11), block, block, c_other)

    def complete(i):
        item = items[i]
        whole = full[item.weight]
        for k in (1, 2, 3):
            wires.arrived(slot(i, 7 + k), item.half(whole, (back[k], y), 1 - c))
        wires.arrived(slot(i, 11), item.half(whole, (ALL, 1 - y), 1 - c))

    def retire(i):
        wires.finish(lambda slot: slot // GATHER_SLOTS == i)

    step_of = Forward(
        dict(
            state,
            out=put,
            tokens=tokens,
            cotangent=cotangent,
            length=length,
            gains=full_gains,
            w_out=full[OUT],
            w_gate=full[GATE],
            w_up=full[UP],
            w_down=full[DOWN].reshape(2816, 1024),
        )
    )
    tasks = [(-1, 3, step_of.prepare)]
    for n, name in enumerate(("query", "key", "value")):
        tasks.append((n, 2, partial(step_of.project, full[n], state[name])))
    tasks += [(2, 3, partial(step_of.attend, p, p + 2)) for p in (0, 2, 4, 6)]
    tasks.append((3, 3, step_of.project_out))
    place_of = 7
    tiles = 0
    for start, size in pieces(2816, 1024):
        for n in range(tiles, tiles + size // FF_TILE):
            tasks.append((place_of + 1, 3, partial(step_of.feed_forward, n, n + 1)))
        tasks.append((place_of + 1, 0, partial(step_of.flush, start, size)))
        tiles += size // FF_TILE
        place_of += 2

    ahead = 3
    for i in range(min(ahead, len(items))):
        along_z(i)
    own_gains.wait()
    for k in (1, 2, 3):
        wires.arrived(gain_slot + k, full_gains.at[back[k], y])
    wires.send(gain_slot, full_gains.at[:, y], full_gains.at[:, y], y_other)
    stages = (retire, complete, last_hop, second_hop, first_hop)
    lates = (3 * LAG, 3 * LAG - 1, 2 * LAG, LAG, 0)
    for step in range(len(items) + 3 * LAG):
        for late, stage in zip(lates, stages):
            if 0 <= step - late < len(items):
                stage(step - late)
        if step + ahead < len(items):
            along_z(step + ahead)
        if step == 0:
            wires.arrived(gain_slot, full_gains.at[:, 1 - y])
        there = step - lates[1]
        if 0 <= there < len(KEPT):
            keep[there].start()
        spent = 0
        while tasks and tasks[0][0] <= there and spent < 6:
            _, cost, task = tasks.pop(0)
            task()
            spent += cost
    for _, _, task in tasks:
        task()
    step_of.finish()
    for copy in keep + outgoing:
        copy.wait()
    wires.finish()


def forward(tokens, cotangent, lengths, weights, gains):
    items = gather_items()
    shares = [w.reshape(share_shape(n)) for w, n in zip(weights, COLUMNS)]
    lines = jnp.zeros((16, 128), jnp.bfloat16)
    for i, gain in enumerate(gains):
        lines = lines.at[i].set(gain)
    wholes = [(4, 2) + share_shape(n) for n in COLUMNS]
    shapes = [jax.ShapeDtypeStruct(wholes[w], jnp.bfloat16) for w in KEPT]
    shapes += [jax.ShapeDtypeStruct(shape, dtype) for _, shape, dtype in FORWARD_OUTS]
    count = GATHER_SLOTS * len(items) + 4
    anywhere = pl.BlockSpec(memory_space=pl.ANY)
    in_vmem = pl.BlockSpec(memory_space=pltpu.VMEM)
    out = pl.pallas_call(
        partial(forward_kernel, items),
        out_shape=shapes,
        in_specs=[anywhere] * 8
        + [in_vmem] * 2
        + [pl.BlockSpec(memory_space=pltpu.SMEM)],
        out_specs=[anywhere] * len(shapes),
        scratch_shapes=[pltpu.VMEM(shape, jnp.bfloat16) for shape in wholes]
        + [pltpu.VMEM((4, 2, 16, 128), jnp.bfloat16)]
        + [pltpu.VMEM(shape, dtype) for _, shape, dtype in FORWARD_OUTS + FORWARD_OWN]
        + [
            pltpu.SemaphoreType.DMA((count,)),
            pltpu.SemaphoreType.DMA((count,)),
            pltpu.SemaphoreType.DMA((8,)),
            pltpu.SemaphoreType.DMA((len(KEPT),)),
            pltpu.SemaphoreType.DMA((OUT_COPIES,)),
        ],
        compiler_params=pltpu.CompilerParams(
            collective_id=0, has_side_effects=True, vmem_limit_bytes=62 * MIB
        ),
        name="gather_forward",
    )(*shares, lines, tokens, cotangent, lengths)
    return out[: len(KEPT)], dict(zip([name for name, _, _ in FORWARD_OUTS], out[len(KEPT) :]))


SUM_SLOTS = 9
RING = 4


class Share:
    def __init__(self, weight, start, size, x_first):
        self.weight, self.start, self.size, self.x_first = weight, start, size, x_first
        self.tall = weight == DOWN
        self.width = 128 if self.tall else size // 2
        self.block = (352 if self.tall else 64, self.width)

    def columns(self, c, x):
        start = c * 512 + x * 256 + self.start if self.tall else self.start + c * self.width
        return pl.ds(pl.multiple_of(start, 128), self.width)

    def quarter(self, sums, c, x):
        if self.tall:
            return sums.at[c, x, self.start // 128]
        return sums.at[x, :, self.columns(c, x)]

    def half(self, sums, c):
        if self.tall:
            return sums.at[c, :, self.start // 128]
        return sums.at[:, :, self.columns(c, 0)]


def share_items():
    order = [(DOWN, 0, 128), (DOWN, 128, 128)]
    order += [(w, start, size) for w in (GATE, UP) for start, size in pieces(2816, 1024)]
    order += [(w, 0, 1024) for w in (OUT, QUERY, KEY, VALUE)]
    return [Share(w, start, size, i in (0, 3, 6, 9)) for i, (w, start, size) in enumerate(order)]


def plus(left, right):
    return (left.astype(jnp.float32) + right.astype(jnp.float32)).astype(left.dtype)


def dot_tn(left, right):
    return lax.dot_general(
        left, right, (((0,), (0,)), ((), ())), preferred_element_type=jnp.float32
    )


BACKWARD_IN = (
    "query",
    "key",
    "value",
    "log_total",
    "hidden_t",
    "hidden_two_t",
    "attended_t",
    "branch",
    "grad_residual",
    "grad_proj",
    "gain_grad",
    "gain_row",
)


class Backward:
    def __init__(self, refs):
        self.__dict__.update(refs)

    def prepare(self):
        length = self.length[0, 0]
        for block in range(4):
            rows = slice(128 * block, 128 * block + 128)
            place_k = lax.broadcasted_iota(jnp.int32, (128, 512), 0) + 128 * block
            place_q = lax.broadcasted_iota(jnp.int32, (128, 512), 1)
            same = (place_q >= length) == (place_k >= length)
            allowed = same & (place_k <= place_q)
            self.bias[rows, :] = jnp.where(allowed, 0.0, NEGATIVE)

    def multiply(self, left_t, right, item, target, core):
        columns = item.columns(core, 0)

        def rows(m, _):
            product = dot(left_t[tile(m, 256), :], right[:, columns]).astype(jnp.bfloat16)
            product = product.reshape(2, 2, 64, item.width)
            for xx in (0, 1):
                target[xx, m] = product[:, xx]
            return 0

        lax.fori_loop(0, 4, rows, 0)

    def multiply_tall(self, left, right, item, target, core):
        both = jnp.concatenate([right[:, item.columns(core, xx)] for xx in (0, 1)], axis=1)
        flat = target.reshape(2, 2816, 128)

        def rows(m, _):
            at = tile(m, 256)
            product = dot_tn(left[:, at], both).astype(jnp.bfloat16)
            for xx in (0, 1):
                flat[xx, at, :] = product[:, 128 * xx : 128 * xx + 128]
            return 0

        lax.fori_loop(0, 11, rows, 0)

    def attend_back(self, first, last):
        low = jnp.bfloat16

        def pair(p, _):
            at = tile(p, 128)
            out_rows = self.w_rows[p].reshape(128, 1024)
            grad = dot_nt(self.grad_proj[...], out_rows).astype(low)
            query = (self.query[:, at].astype(jnp.float32) * SCORE_SCALE).astype(low)
            key, value = self.key[:, at], self.value[:, at]
            left = lax.broadcasted_iota(jnp.int32, (512, 128), 1) < HEAD
            none = jnp.zeros((512, 128), low)
            sides = [
                [jnp.where(side, v, none) for v in (query, key, value, grad)]
                for side in (left, ~left)
            ]
            grad_key, grad_value = [None, None], [None, None]
            for block in (0, 1):
                rows, seen = slice(256 * block, 256 * block + 256), slice(0, 256 * block + 256)
                grad_query = None
                parts_key, parts_value = None, None
                for n, (own_query, own_key, own_value, own_grad) in enumerate(sides):
                    scores = dot_nt(own_key[seen], query[rows]) + self.bias[seen, rows]
                    probs = jnp.exp(scores - self.log_total[p, n : n + 1, rows])
                    grad_probs = dot_nt(own_value[seen], grad[rows])
                    centre = jnp.sum(grad_probs * probs, axis=0, keepdims=True)
                    grad_scores = (probs * (grad_probs - centre)).astype(low)
                    part_query = dot_tn(grad_scores, own_key[seen])
                    part_key = dot(grad_scores, own_query[rows])
                    part_value = dot(probs.astype(low), own_grad[rows])
                    if n == 0:
                        grad_query, parts_key, parts_value = part_query, part_key, part_value
                    else:
                        grad_query += part_query
                        parts_key += part_key
                        parts_value += part_value
                self.query[rows, at] = (grad_query * SCORE_SCALE).astype(low)
                if block == 0:
                    grad_key[0], grad_value[0] = parts_key, parts_value
                else:
                    grad_key = [grad_key[0] + parts_key[:256], parts_key[256:]]
                    grad_value = [grad_value[0] + parts_value[:256], parts_value[256:]]
            for block in (0, 1):
                rows = slice(256 * block, 256 * block + 256)
                self.key[rows, at] = grad_key[block].astype(low)
                self.value[rows, at] = grad_value[block].astype(low)
            return 0

        lax.fori_loop(first, last, pair, 0)

    def grad_hidden(self, t):
        at = pl.ds(256 * t, 256)
        total = None
        for n, grad in enumerate((self.query, self.key, self.value)):
            part = dot_nt(grad[...], self.w_rows[2 * n : 2 * n + 2].reshape(256, 1024))
            total = part if total is None else total + part
        self.input_grad[:, at] = total

    def finish(self):
        self.gain_total[...] = jnp.zeros_like(self.gain_total)

        def rows_of(block, _):
            rows = tile(block, 64)
            values = self.tokens[rows, :].astype(jnp.float32)
            factor = lax.rsqrt(jnp.mean(values * values, axis=-1, keepdims=True) + NORM_EPS)
            normed = values * factor
            grad = self.input_grad[rows, :]
            self.gain_total[...] += jnp.sum((grad * normed).reshape(8, 8, 1024), axis=0)
            grad_normed = grad * self.gain_row[0:1, :].astype(jnp.float32)
            mean = jnp.mean(grad_normed * normed, axis=-1, keepdims=True)
            self.input_grad[rows, :] = self.grad_residual[rows, :] + factor * (
                grad_normed - normed * mean
            )
            return 0

        lax.fori_loop(0, 8, rows_of, 0)
        self.gain_lines[...] = jnp.zeros_like(self.gain_lines)
        lines = [jnp.sum(v[...], axis=0, keepdims=True) for v in (self.gain_total, self.gain_grad)]
        for s in range(8):
            for n, line in enumerate(lines):
                self.gain_lines[s // 2, s % 2, n : n + 1] = line[:, 128 * s : 128 * s + 128]


def backward_kernel(items, *refs):
    refs = list(refs)

    def take(n):
        taken = refs[:n]
        del refs[:n]
        return taken

    kept = take(len(KEPT))
    middle_in, grad_gate_in, grad_up_in = take(3)
    saved_in = dict(zip(BACKWARD_IN, take(len(BACKWARD_IN))))
    tokens_in, length = take(2)
    sums = take(7)
    gain_sums, input_grad_out = take(2)
    saved = dict(zip(BACKWARD_IN, take(len(BACKWARD_IN))))
    tokens, input_grad, wide, w_rows, bias, gain_total, gain_lines = take(7)
    mine, from_first, from_second, from_z = (take(len(items)) for _ in range(4))
    ring, tall_ring = take(RING), take(2)
    outbox, tall_outbox = take(2), take(1)
    gain_core, gain_x, gain_y, gain_z = take(4)
    send_sems, recv_sems, load_sems, credit = refs
    z, y, x, c = place()
    far = [lax.rem(z + k, 4) for k in range(4)]
    back = [lax.rem(z + 4 - k, 4) for k in range(4)]
    x_other, y_other, c_other = (
        device(z, y, 1 - x, c),
        device(z, 1 - y, x, c),
        device(z, y, x, 1 - c),
    )
    loads = {}

    def load(name, source, target):
        loads[name] = pltpu.make_async_copy(source, target, load_sems.at[len(loads)])
        loads[name].start()

    waited = set()

    def loaded(*names):
        for name in names:
            if name not in waited:
                loads[name].wait()
                waited.add(name)

    load("middle", middle_in, wide.at[0])
    load("branch", saved_in["branch"], saved["branch"])
    load("hidden_two_t", saved_in["hidden_two_t"], saved["hidden_two_t"])
    load("grad_gate", grad_gate_in, wide.at[1])
    load("out_rows", kept[OUT].reshape(8, 2, 64, 1024), w_rows)
    for name in BACKWARD_IN:
        if name not in loads:
            load(name, saved_in[name], saved[name])
    load("tokens", tokens_in, tokens)
    greet()
    wires = Wires(send_sems, recv_sems)
    work = Backward(
        dict(
            saved,
            tokens=tokens,
            length=length,
            w_rows=w_rows,
            bias=bias,
            input_grad=input_grad,
            gain_total=gain_total,
            gain_lines=gain_lines,
        )
    )
    wide_items = [i for i, item in enumerate(items) if not item.tall]

    def slot(i, k):
        return SUM_SLOTS * i + k

    def from_core(i):
        if items[i].tall:
            return tall_ring[i]
        return ring[wide_items.index(i) % RING].at[..., : items[i].width]

    def produce(i):
        item = items[i]
        if item.tall:
            loaded("middle", "branch")
            if i > 0:
                wires.finish(lambda s: s == slot(i - 1, 0))
            box = tall_outbox[0]
            multiply = partial(work.multiply_tall, wide.at[0], saved["branch"], item)
        else:
            number = wide_items.index(i)
            if number >= 2:
                wires.finish(lambda s: s == slot(wide_items[number - 2], 0))
            box = outbox[number % 2].at[..., : item.width]
            left, right, names = {
                GATE: (saved["hidden_two_t"], wide.at[1], ("hidden_two_t", "grad_gate")),
                UP: (saved["hidden_two_t"], wide.at[0], ("grad_up",)),
                OUT: (saved["attended_t"], saved["grad_proj"], ("attended_t", "grad_proj")),
                QUERY: (saved["hidden_t"], saved["query"], ("hidden_t",)),
                KEY: (saved["hidden_t"], saved["key"], ()),
                VALUE: (saved["hidden_t"], saved["value"], ()),
            }[item.weight]
            loaded(*names)
            multiply = partial(work.multiply, left, right, item)
            if number >= RING:
                pl.semaphore_wait(credit, 1)
        multiply(box, 1 - c)
        wires.send(slot(i, 0), box, from_core(i), c_other)
        multiply(mine[i], c)
        if item.tall and not items[i + 1].tall:
            load("grad_up", grad_up_in, wide.at[0])

    def first_hop(i):
        item, own, other = items[i], mine[i], from_core(i)
        wires.arrived(slot(i, 0), other)

        def add(at, _):
            for xx in (0, 1):
                for yy in (0, 1):
                    own[xx, at, yy] = plus(own[xx, at, yy], other[xx, at, yy])
            return 0

        lax.fori_loop(0, 4, add, 0)
        if not item.tall and wide_items.index(i) + RING < len(wide_items):
            pl.semaphore_signal(credit, inc=1, device_id=c_other, device_id_type=MESH)
        if item.x_first:
            wires.send(slot(i, 1), own.at[1 - x], from_first[i], x_other)
        else:
            wires.send(slot(i, 1), own.at[:, :, 1 - y], from_first[i], y_other)

    def second_hop(i):
        item, own, other = items[i], mine[i], from_first[i]
        wires.arrived(slot(i, 1), other)

        def add(at, _):
            for side in (0, 1):
                if item.x_first:
                    own[x, at, side] = plus(own[x, at, side], other[at, side])
                else:
                    own[side, at, y] = plus(own[side, at, y], other[side, at])
            return 0

        lax.fori_loop(0, 4, add, 0)
        if item.x_first:
            wires.send(slot(i, 2), own.at[x, :, 1 - y], from_second[i], y_other)
        else:
            wires.send(slot(i, 2), own.at[1 - x, :, y], from_second[i], x_other)

    def along_z(i):
        own, other = mine[i], from_second[i]
        wires.arrived(slot(i, 2), other)

        def add(at, _):
            own[x, at, y] = plus(own[x, at, y], other[at])
            return 0

        lax.fori_loop(0, 4, add, 0)
        for k in (1, 2, 3):
            wires.send(
                slot(i, 2 + k),
                own.at[x, far[k], y],
                from_z[i].at[k - 1],
                device(far[k], y, x, c),
            )

    def to_x(i):
        item = items[i]
        total = mine[i][x, z, y].astype(jnp.float32)
        for k in (1, 2, 3):
            wires.arrived(slot(i, 2 + k), from_z[i].at[k - 1])
            total += from_z[i][k - 1].astype(jnp.float32)
        block = item.quarter(sums[item.weight], c, x)
        block[...] = total.astype(jnp.bfloat16)
        wires.send(slot(i, 6), block, block, x_other)

    def to_sibling(i):
        item = items[i]
        wires.arrived(slot(i, 6), item.quarter(sums[item.weight], c, 1 - x))
        block = item.half(sums[item.weight], c)
        wires.send(slot(i, 7), block, block, c_other)

    def complete(i):
        item = items[i]
        wires.arrived(slot(i, 7), item.half(sums[item.weight], 1 - c))
        wires.finish(lambda s: s // SUM_SLOTS == i)

    base = SUM_SLOTS * len(items)

    def gains_one():
        wires.send(base, gain_lines, gain_core, c_other)

    def gains_two():
        wires.arrived(base, gain_core)
        gain_core[...] = gain_lines[...] + gain_core[...]
        wires.send(base + 1, gain_core, gain_x, x_other)

    def gains_three():
        wires.arrived(base + 1, gain_x)
        gain_x[...] = gain_core[...] + gain_x[...]
        wires.send(base + 2, gain_x.at[:, 1 - y], gain_y, y_other)

    def gains_four():
        wires.arrived(base + 2, gain_y)
        gain_y[...] = gain_x[:, y] + gain_y[...]
        for k in (1, 2, 3):
            wires.send(base + 2 + k, gain_y.at[far[k]], gain_z.at[z], device(far[k], y, x, c))
        gain_z[z] = gain_y[z]

    def gains_five():
        for k in (1, 2, 3):
            wires.arrived(base + 2 + k, gain_z.at[back[k]])
        gain_sums[...] = (gain_z[0] + gain_z[1]) + (gain_z[2] + gain_z[3])

    def fetch_rows(t):
        for n in range(3):
            load(("rows", n, t), kept[n].at[t], w_rows.at[2 * n : 2 * n + 2])

    def attend_back(p):
        if p == 0:
            loaded("query", "key", "value", "log_total", "grad_proj", "out_rows")
        work.attend_back(p, p + 1)
        if p == 7:
            fetch_rows(0)

    def grad_hidden(t):
        loaded(*[("rows", n, t) for n in range(3)])
        work.grad_hidden(t)
        if t < 3:
            fetch_rows(t + 1)

    def finish():
        loaded("tokens", "grad_residual", "gain_grad", "gain_row")
        work.finish()
        load("input_grad", input_grad, input_grad_out)
        gains_one()

    beside = {0: [work.prepare]}
    for p in range(8):
        beside.setdefault(p, []).append(partial(attend_back, p))
    for t in range(4):
        beside.setdefault(9 + t // 2, []).append(partial(grad_hidden, t))
    beside.setdefault(11, []).append(finish)
    for n, task in enumerate((gains_two, gains_three, gains_four, gains_five)):
        beside.setdefault(13 + 2 * n, []).append(task)

    stages = (complete, to_sibling, to_x, along_z, second_hop, first_hop, produce)
    lates = (11, 9, 7, 5, 3, 1, 0)
    for step in range(len(items) + lates[0]):
        for late, stage in zip(lates, stages):
            if 0 <= step - late < len(items):
                stage(step - late)
        for task in beside.get(step, []):
            task()
    loaded("input_grad")
    wires.finish()


def backward(tokens, lengths, kept, saved):
    items = share_items()
    low, wide = jnp.bfloat16, jnp.float32
    dtypes = {name: (shape, dtype) for name, shape, dtype in FORWARD_OUTS}
    shapes = [
        jax.ShapeDtypeStruct((2, 2, 2, 352, 128) if n is None else (2, 64, n), low) for n in COLUMNS
    ]
    shapes += [jax.ShapeDtypeStruct((8, 128), wide), jax.ShapeDtypeStruct((512, 1024), wide)]
    count = SUM_SLOTS * len(items) + 6
    anywhere = pl.BlockSpec(memory_space=pl.ANY)
    in_vmem = pl.BlockSpec(memory_space=pltpu.VMEM)
    n_loads = 6 + len(BACKWARD_IN) + 12

    def buffers(lead_of):
        return [pltpu.VMEM(lead_of(item) + item.block, low) for item in items]

    out = pl.pallas_call(
        partial(backward_kernel, items),
        out_shape=shapes,
        in_specs=[anywhere] * (len(KEPT) + 3 + len(BACKWARD_IN) + 1)
        + [pl.BlockSpec(memory_space=pltpu.SMEM)],
        out_specs=[in_vmem] * 8 + [anywhere],
        scratch_shapes=[pltpu.VMEM(*dtypes[name]) for name in BACKWARD_IN]
        + [
            pltpu.VMEM((512, 1024), low),
            pltpu.VMEM((512, 1024), wide),
            pltpu.VMEM((2, 512, 2816), low),
            pltpu.VMEM((8, 2, 64, 1024), low),
            pltpu.VMEM((512, 512), wide),
            pltpu.VMEM((8, 1024), wide),
            pltpu.VMEM((4, 2, 8, 128), wide),
        ]
        + buffers(lambda item: (2, 4, 2))
        + buffers(lambda item: (4, 2) if item.x_first else (2, 4))
        + buffers(lambda item: (4,))
        + buffers(lambda item: (3,))
        + [pltpu.VMEM((2, 4, 2, 64, 512), low)] * RING
        + [pltpu.VMEM((2, 4, 2, 352, 128), low)] * 2
        + [pltpu.VMEM((2, 4, 2, 64, 512), low)] * 2
        + [pltpu.VMEM((2, 4, 2, 352, 128), low)]
        + [
            pltpu.VMEM((4, 2, 8, 128), wide),
            pltpu.VMEM((4, 2, 8, 128), wide),
            pltpu.VMEM((4, 8, 128), wide),
            pltpu.VMEM((4, 8, 128), wide),
            pltpu.SemaphoreType.DMA((count,)),
            pltpu.SemaphoreType.DMA((count,)),
            pltpu.SemaphoreType.DMA((n_loads,)),
            pltpu.SemaphoreType.REGULAR,
        ],
        compiler_params=pltpu.CompilerParams(
            collective_id=1, has_side_effects=True, vmem_limit_bytes=62 * MIB
        ),
        name="backward_sum",
    )(
        *kept,
        saved["middle"],
        saved["grad_gate"],
        saved["grad_up"],
        *[saved[name] for name in BACKWARD_IN],
        tokens,
        lengths,
    )
    return out[:7], out[7], out[8]


def unpack_kernel(*refs):
    blocks, (gain_sums, mixed, input_grad) = refs[:7], refs[7:10]
    sums, (gain_attn, gain_ffn, mixed_out, input_out) = refs[10:17], refs[17:21]
    sems = refs[21]
    copies = [
        pltpu.make_async_copy(mixed, mixed_out, sems.at[0]),
        pltpu.make_async_copy(input_grad, input_out, sems.at[1]),
    ]
    for copy in copies:
        copy.start()
    for block, total in zip(blocks[:6], sums[:6]):
        total[...] = block[...].astype(jnp.float32)
    for b in range(8):
        sums[6][:, 128 * b : 128 * b + 128] = blocks[6][b // 4, b // 2 % 2, b % 2].astype(
            jnp.float32
        )
    gain_attn[...] = gain_sums[0:1]
    gain_ffn[...] = gain_sums[1:2]
    for copy in copies:
        copy.wait()


def unpack(blocks, gain_sums, mixed, input_grad):
    wide = jnp.float32
    anywhere = pl.BlockSpec(memory_space=pl.ANY)
    in_vmem = pl.BlockSpec(memory_space=pltpu.VMEM)
    shapes = [
        jax.ShapeDtypeStruct((352, 1024) if n is None else (2, 64, n), wide) for n in COLUMNS
    ]
    shapes += [jax.ShapeDtypeStruct((1, 128), wide)] * 2
    shapes += [jax.ShapeDtypeStruct(v.shape, v.dtype) for v in (mixed, input_grad)]
    out = pl.pallas_call(
        unpack_kernel,
        out_shape=shapes,
        in_specs=[in_vmem] * 8 + [anywhere] * 2,
        out_specs=[in_vmem] * 9 + [anywhere] * 2,
        scratch_shapes=[pltpu.SemaphoreType.DMA((2,))],
        compiler_params=pltpu.CompilerParams(vmem_limit_bytes=32 * MIB),
        name="unpack",
    )(*blocks, gain_sums, mixed, input_grad)
    sums = [s.reshape(-1, s.shape[-1]) for s in out[:7]]
    return sums, [g.reshape(128) for g in out[7:9]], out[9], out[10]


def gather_plain(weights, gains):
    everything = (*weights, *gains)
    whole = [lax.all_gather(v, "dp", axis=0, tiled=True) for v in everything]
    return whole[: len(weights)], whole[len(weights) :]


def sum_plain(grads, gain_grads):
    shares = [
        lax.psum_scatter(g.astype(jnp.float32), "dp", scatter_dimension=0, tiled=True)
        for g in (*grads, *gain_grads)
    ]
    sums = [lax.psum(s, ("rep", "cores")) for s in shares]
    return sums[: len(grads)], sums[len(grads) :]


def on_any_device(
    tokens,
    norm_attn,
    w_query,
    w_key,
    w_value,
    w_out,
    norm_ffn,
    w_gate,
    w_up,
    w_down,
    lengths,
    cotangent,
):
    rows = tokens.shape[0]
    low = jnp.bfloat16
    allowed, valid = masks(lengths, rows)
    whole, gains = gather_plain(
        (w_query, w_key, w_value, w_out, w_gate, w_up, w_down), (norm_attn, norm_ffn)
    )
    full_query, full_key, full_value, full_out, full_gate, full_up, full_down = whole
    gain_attn, gain_ffn = gains
    inputs = tokens.astype(jnp.float32)
    normed, factor = normalize(inputs)
    hidden = (normed * gain_attn.astype(jnp.float32)).astype(low)
    query = matmul(hidden, full_query).astype(low)
    keyed = matmul(hidden, full_key).astype(low)
    valued = matmul(hidden, full_value).astype(low)
    query_groups, key_groups, value_groups = (to_groups(query), to_groups(keyed), to_groups(valued))
    attended_groups, log_total = lax.map(
        partial(attend, allowed), (query_groups, key_groups, value_groups)
    )
    attended = from_groups(attended_groups)
    residual = inputs + matmul(attended, full_out)
    normed_two, factor_two = normalize(residual)
    hidden_two = (normed_two * gain_ffn.astype(jnp.float32)).astype(low)
    gate = matmul(hidden_two, full_gate)
    upward = matmul(hidden_two, full_up)
    sigma = jax.nn.sigmoid(gate)
    middle = (gate * sigma * upward).astype(low)
    mixed = (valid[:, None] * (residual + matmul(middle, full_down))).astype(low)
    grad_output = cotangent.astype(jnp.float32) * valid[:, None]
    grad_branch = grad_output.astype(low)
    grad_down = matmul_tn(middle, grad_branch)
    grad_middle = matmul_nt(grad_branch, full_down)
    grad_gate_rows = (grad_middle * upward * sigma * (1.0 + gate * (1.0 - sigma))).astype(low)
    grad_up_rows = (grad_middle * gate * sigma).astype(low)
    grad_gate = matmul_tn(hidden_two, grad_gate_rows)
    grad_up = matmul_tn(hidden_two, grad_up_rows)
    grad_hidden_two = matmul_nt(grad_gate_rows, full_gate) + matmul_nt(grad_up_rows, full_up)
    grad_gain_ffn = jnp.sum(grad_hidden_two * normed_two, axis=0)
    grad_residual = grad_output + norm_back(
        grad_hidden_two * gain_ffn.astype(jnp.float32), normed_two, factor_two
    )
    grad_proj = grad_residual.astype(low)
    grad_out = matmul_tn(attended, grad_proj)
    grad_attended = matmul_nt(grad_proj, full_out).astype(low)
    grad_query_g, grad_key_g, grad_value_g = lax.map(
        partial(attend_back, allowed),
        (query_groups, key_groups, value_groups, to_groups(grad_attended), log_total),
    )
    grad_query_rows = from_groups(grad_query_g)
    grad_key_rows = from_groups(grad_key_g)
    grad_value_rows = from_groups(grad_value_g)
    grad_query = matmul_tn(hidden, grad_query_rows)
    grad_key = matmul_tn(hidden, grad_key_rows)
    grad_value = matmul_tn(hidden, grad_value_rows)
    grad_hidden = (
        matmul_nt(grad_query_rows, full_query)
        + matmul_nt(grad_key_rows, full_key)
        + matmul_nt(grad_value_rows, full_value)
    )
    grad_gain_attn = jnp.sum(grad_hidden * normed, axis=0)
    input_grad = grad_residual + norm_back(
        grad_hidden * gain_attn.astype(jnp.float32), normed, factor
    )
    grads = (grad_query, grad_key, grad_value, grad_out, grad_gate, grad_up, grad_down)
    sums, gain_sums = sum_plain([g.astype(low) for g in grads], (grad_gain_attn, grad_gain_ffn))
    return (
        mixed,
        input_grad,
        gain_sums[0],
        sums[0],
        sums[1],
        sums[2],
        sums[3],
        gain_sums[1],
        sums[4],
        sums[5],
        sums[6],
    )


def on_tuned_device(
    tokens,
    norm_attn,
    w_query,
    w_key,
    w_value,
    w_out,
    norm_ffn,
    w_gate,
    w_up,
    w_down,
    lengths,
    cotangent,
):
    weights = (w_query, w_key, w_value, w_out, w_gate, w_up, w_down)
    kept, saved = forward(tokens, cotangent, lengths, weights, (norm_attn, norm_ffn))
    blocks, gain_lines, input_grad = backward(tokens, lengths, kept, saved)
    sums, gain_sums, mixed, input_grad = unpack(blocks, gain_lines, saved["mixed"], input_grad)
    return (
        mixed,
        input_grad,
        gain_sums[0],
        *sums[:4],
        gain_sums[1],
        *sums[4:],
    )


def solution(mesh):
    tuned = dict(mesh.shape) == {"dp": 8, "rep": 2, "cores": 2}
    tokens_placed = P(("dp", "rep", "cores"), None)
    share, gain = P("dp", None), P("dp")
    return jax.shard_map(
        on_tuned_device if tuned else on_any_device,
        mesh=mesh,
        in_specs=(
            tokens_placed,
            gain,
            share,
            share,
            share,
            share,
            gain,
            share,
            share,
            share,
            tokens_placed,
            tokens_placed,
        ),
        out_specs=(
            tokens_placed,
            tokens_placed,
            gain,
            share,
            share,
            share,
            share,
            gain,
            share,
            share,
            share,
        ),
        check_vma=False,
    )
```

```python
from functools import partial

import jax
import jax.numpy as jnp
from jax import lax
from jax.experimental import pallas as pl
from jax.experimental.pallas import tpu as pltpu
from jax.sharding import PartitionSpec as P

HEADS = 16
HEAD = 64


NORM_EPS = 1e-05
SCORE_SCALE = 0.125
NEGATIVE = -1e30
head_group = 4
MESH = pl.DeviceIdType.MESH
MIB = 1024 * 1024


def masks(block_len, rows):
    bounds = jnp.cumsum(block_len[0])
    place = jnp.arange(rows, dtype=jnp.int32)
    segment = jnp.sum((place[:, None] >= bounds[None, :]).astype(jnp.int32), axis=1)
    allowed = (segment[:, None] == segment[None, :]) & (place[None, :] <= place[:, None])
    valid = (segment < block_len.shape[1]).astype(jnp.float32)
    return (allowed, valid)


def normalize(values):
    factor = lax.rsqrt(jnp.mean(values * values, axis=-1, keepdims=True) + NORM_EPS)
    return (values * factor, factor)


def norm_back(grad_normed, normed, factor):
    return factor * (grad_normed - normed * jnp.mean(grad_normed * normed, axis=-1, keepdims=True))


def matmul(left, right):
    return jnp.dot(left, right, preferred_element_type=jnp.float32)


def matmul_tn(left, right):
    return lax.dot_general(
        left, right, (((0,), (0,)), ((), ())), preferred_element_type=jnp.float32
    )


def matmul_nt(left, right):
    return lax.dot_general(
        left, right, (((1,), (1,)), ((), ())), preferred_element_type=jnp.float32
    )


def to_groups(matrix):
    rows = matrix.shape[0]
    split = matrix.reshape(rows, HEADS // head_group, head_group, HEAD)
    return split.transpose(1, 2, 0, 3)


def from_groups(grouped):
    rows = grouped.shape[2]
    return grouped.transpose(2, 0, 1, 3).reshape(rows, HEADS * HEAD)


def group_scores(allowed, query_g, key_g):
    raw = (
        jnp.einsum("hqe,hke->hqk", query_g, key_g, preferred_element_type=jnp.float32) * SCORE_SCALE
    )
    return jnp.where(allowed[None], raw, NEGATIVE)


def attend(allowed, operands):
    query_g, key_g, value_g = operands
    scores = group_scores(allowed, query_g, key_g)
    top = jnp.max(scores, axis=-1, keepdims=True)
    expo = jnp.exp(scores - top)
    total = jnp.sum(expo, axis=-1, keepdims=True)
    probs_low = (expo / total).astype(jnp.bfloat16)
    result = jnp.einsum("hqk,hke->hqe", probs_low, value_g, preferred_element_type=jnp.float32)
    return (result.astype(jnp.bfloat16), top[..., 0] + jnp.log(total[..., 0]))


def attend_back(allowed, operands):
    query_g, key_g, value_g, grad_g, log_total = operands
    scores = group_scores(allowed, query_g, key_g)
    probs = jnp.exp(scores - log_total[..., None])
    grad_probs = jnp.einsum("hqe,hke->hqk", grad_g, value_g, preferred_element_type=jnp.float32)
    centre = jnp.sum(grad_probs * probs, axis=-1, keepdims=True)
    grad_scores = (probs * (grad_probs - centre)).astype(jnp.bfloat16)
    grad_query = (
        jnp.einsum("hqk,hke->hqe", grad_scores, key_g, preferred_element_type=jnp.float32)
        * SCORE_SCALE
    )
    grad_key = (
        jnp.einsum("hqk,hqe->hke", grad_scores, query_g, preferred_element_type=jnp.float32)
        * SCORE_SCALE
    )
    grad_value = jnp.einsum(
        "hqk,hqe->hke", probs.astype(jnp.bfloat16), grad_g, preferred_element_type=jnp.float32
    )
    return (
        grad_query.astype(jnp.bfloat16),
        grad_key.astype(jnp.bfloat16),
        grad_value.astype(jnp.bfloat16),
    )


class Part:
    def __init__(self, weight, tall, start, size, no_x):
        self.weight, self.tall, self.start, self.size = weight, tall, start, size
        self.no_x = no_x

    def quarter(self, ref, lead, c, x):
        if self.tall:
            columns = pl.ds(pl.multiple_of(c * 512 + x * 256, 256), 256)
            return ref.at[(*lead, pl.ds(self.start, self.size), columns)]
        return ref.at[(*lead, x, slice(None), self.columns(c))]

    def half(self, ref, lead, c):
        if self.tall:
            columns = pl.ds(pl.multiple_of(c * 512, 512), 512)
            return ref.at[(*lead, pl.ds(self.start, self.size), columns)]
        return ref.at[(*lead, slice(None), slice(None), self.columns(c))]

    def columns(self, c):
        width = self.size // 2
        return pl.ds(pl.multiple_of(self.start + c * width, 128), width)


def pieces(total, most):
    return [(start, min(most, total - start)) for start in range(0, total, most)]


def place():
    d = lax.axis_index("dp")
    return lax.div(d, 2), lax.rem(d, 2), lax.axis_index("rep"), lax.axis_index("cores")


def device(z, y, x, c):
    return {"dp": 2 * z + y, "rep": x, "cores": c}


def greet():
    z, y, x, c = place()
    barrier = pltpu.get_barrier_semaphore()
    others = [device(lax.rem(z + k, 4), y, x, c) for k in (1, 2, 3)]
    others += [device(z, 1 - y, x, c), device(z, y, 1 - x, c), device(z, y, x, 1 - c)]
    for other in others:
        pl.semaphore_signal(barrier, inc=1, device_id=other, device_id_type=MESH)
    pl.semaphore_wait(barrier, len(others))


class Wires:
    def __init__(self, send_sems, recv_sems):
        self.send_sems, self.recv_sems, self.sent = send_sems, recv_sems, []

    def copy(self, slot, source, target, other):
        return pltpu.make_async_remote_copy(
            src_ref=source,
            dst_ref=target,
            send_sem=self.send_sems.at[slot],
            recv_sem=self.recv_sems.at[slot],
            device_id=other,
            device_id_type=MESH,
        )

    def send(self, slot, source, target, other):
        copy = self.copy(slot, source, target, other)
        copy.start()
        self.sent.append((slot, copy))

    def arrived(self, slot, target):
        z, y, x, c = place()
        self.copy(slot, target, target, device(z, y, x, 1 - c)).wait_recv()

    def finish(self, chosen=lambda slot: True):
        for slot, copy in self.sent:
            if chosen(slot):
                copy.wait_send()
        self.sent = [(slot, copy) for slot, copy in self.sent if not chosen(slot)]


GATHER_SLOTS = 12
LAG = 2
ALL = slice(None)
COLUMNS = (1024, 1024, 1024, 1024, 2816, 2816, None)
QUERY, KEY, VALUE, OUT, GATE, UP, DOWN = range(7)
TILE = 256
FF_TILE = 256


FF_CHUNKS = ((0, 1024), (1024, 1024), (2048, 512), (2560, 256))


def gather_items():
    order = [(QUERY, 0, 256, True), (QUERY, 256, 768, False), (KEY, 0, 1024, True)]
    order += [(VALUE, 0, 1024, False), (OUT, 0, 1024, False)]
    order += [(DOWN, 0, 128, False), (DOWN, 128, 128, True), (DOWN, 256, 96, False)]
    for n, (start, size) in enumerate(FF_CHUNKS):
        order += [(GATE, start, size, n == 3), (UP, start, size, n in (0, 3))]
    return [Part(w, w == DOWN, start, size, no_x) for w, start, size, no_x in order]


def dot(left, right):
    return lax.dot_general(
        left, right, (((1,), (0,)), ((), ())), preferred_element_type=jnp.float32
    )


def dot_nt(left, right):
    return lax.dot_general(
        left, right, (((1,), (1,)), ((), ())), preferred_element_type=jnp.float32
    )


def tile(index, size):
    return pl.ds(pl.multiple_of(index * size, size), size)


def weight_columns(ref, at):
    return ref[:, :, :, :, at].reshape(1024, -1)


class Forward:
    def __init__(self, refs):
        self.__dict__.update(refs)

    def prepare(self):
        for s in range(8):
            self.gain_row[:, 128 * s : 128 * s + 128] = self.gains[s // 2, s % 2]
        length = self.length[0, 0]
        for block in range(4):
            rows = slice(128 * block, 128 * block + 128)
            place_q = lax.broadcasted_iota(jnp.int32, (128, 512), 0) + 128 * block
            place_k = lax.broadcasted_iota(jnp.int32, (128, 512), 1)
            same = (place_q >= length) == (place_k >= length)
            allowed = same & (place_k <= place_q)
            self.bias[rows, :] = jnp.where(allowed, 0.0, NEGATIVE)

        def normed(block, _):
            rows = tile(block, 64)
            values = self.tokens[rows, :].astype(jnp.float32)
            factor = lax.rsqrt(jnp.mean(values * values, axis=-1, keepdims=True) + NORM_EPS)
            gain = self.gain_row[0:1, :].astype(jnp.float32)
            self.hidden[rows, :] = (values * factor * gain).astype(jnp.bfloat16)
            place = lax.broadcasted_iota(jnp.int32, (64, 1024), 0) + 64 * block
            branch = jnp.where(place < length, self.cotangent[rows, :].astype(jnp.float32), 0.0)
            self.branch[rows, :] = branch.astype(jnp.bfloat16)
            return 0

        lax.fori_loop(0, 8, normed, 0)
        self.turn(self.hidden, self.hidden_t)
        self.out("branch")

    def turn(self, matrix, turned):
        def columns(n, _):
            at = tile(n, 128)
            turned[at, :] = matrix[:, at].astype(jnp.float32).T.astype(jnp.bfloat16)
            return 0

        lax.fori_loop(0, 8, columns, 0)

    def project(self, weight, result):
        def columns(n, _):
            at = tile(n, TILE)
            result[:, at] = dot(self.hidden[...], weight_columns(weight, at)).astype(jnp.bfloat16)
            return 0

        lax.fori_loop(0, 1024 // TILE, columns, 0)

    def attend(self, first, last):
        def pair(p, _):
            at = tile(p, 128)
            left = lax.broadcasted_iota(jnp.int32, (256, 128), 1) < HEAD
            for block in (0, 1):
                rows, seen = slice(256 * block, 256 * block + 256), slice(0, 256 * block + 256)
                query = self.query[rows, at].astype(jnp.float32) * SCORE_SCALE
                outs, totals = [], []
                for side in (left, ~left):
                    own = jnp.where(side, query, 0.0).astype(jnp.bfloat16)
                    scores = dot_nt(own, self.key[seen, at]) + self.bias[rows, seen]
                    top = jnp.max(scores, axis=-1, keepdims=True)
                    expo = jnp.exp(scores - top)
                    total = jnp.sum(expo, axis=-1, keepdims=True)
                    probs = (expo * (1.0 / total)).astype(jnp.bfloat16)
                    outs.append(dot(probs, self.value[seen, at]))
                    totals.append(top + jnp.log(total))
                self.attended[rows, at] = jnp.where(left, outs[0], outs[1]).astype(jnp.bfloat16)
                turned = jnp.where(left, totals[0], totals[1]).T
                self.log_total[p, 0:1, rows] = turned[0:1]
                self.log_total[p, 1:2, rows] = turned[HEAD : HEAD + 1]
            return 0

        lax.fori_loop(first, last, pair, 0)

    def project_out(self):
        def columns(n, _):
            at = tile(n, TILE)
            self.residual[:, at] = self.tokens[:, at].astype(jnp.float32) + dot(
                self.attended[...], weight_columns(self.w_out, at)
            )
            return 0

        lax.fori_loop(0, 1024 // TILE, columns, 0)

        def normed(block, _):
            rows = tile(block, 64)
            values = self.residual[rows, :]
            factor = lax.rsqrt(jnp.mean(values * values, axis=-1, keepdims=True) + NORM_EPS)
            gain = self.gain_row[8:9, :].astype(jnp.float32)
            self.hidden_two[rows, :] = (values * factor * gain).astype(jnp.bfloat16)
            return 0

        lax.fori_loop(0, 8, normed, 0)
        self.turn(self.hidden_two, self.hidden_two_t)
        self.turn(self.attended, self.attended_t)
        for name in ("query", "key", "value", "log_total", "hidden_t", "hidden_two_t", "attended_t"):
            self.out(name)

    def feed_forward(self, first, last):
        def columns(n, first_of_all):
            at = tile(n, FF_TILE)
            low = jnp.bfloat16
            gate_w = weight_columns(self.w_gate, at)
            up_w = weight_columns(self.w_up, at)
            down_w = self.w_down[at, :]
            gate = dot(self.hidden_two[...], gate_w)
            upward = dot(self.hidden_two[...], up_w)
            grad_middle = dot_nt(self.branch[...], down_w)
            sigma = 1.0 / (1.0 + jnp.exp(-gate))
            silu = gate * sigma
            middle = (silu * upward).astype(low)
            grad_up = (grad_middle * silu).astype(low)
            grad_gate = (grad_middle * upward * sigma * (1.0 + gate * (1.0 - sigma))).astype(low)
            self.middle[:, at] = middle
            self.grad_up[:, at] = grad_up
            self.grad_gate[:, at] = grad_gate
            for j in range(4):
                part = slice(256 * j, 256 * j + 256)
                mixed = dot(middle, down_w[:, part])
                grad = dot_nt(grad_gate, gate_w[part, :]) + dot_nt(grad_up, up_w[part, :])
                if first_of_all is True:
                    self.total[:, part] = mixed
                    self.grad_hidden_two[:, part] = grad
                else:
                    self.total[:, part] += mixed
                    self.grad_hidden_two[:, part] += grad
            return 0

        if first == 0:
            columns(0, True)
            first = 1
        lax.fori_loop(first, last, lambda n, _: columns(n, False), 0)

    def flush(self, start, size):
        for name in ("middle", "grad_gate", "grad_up"):
            self.out(name, pl.ds(start, size))

    def finish(self):
        length = self.length[0, 0]
        self.gain_grad[...] = jnp.zeros_like(self.gain_grad)

        def rows_of(block, _):
            rows = tile(block, 64)
            place = lax.broadcasted_iota(jnp.int32, (64, 1024), 0) + 64 * block
            residual = self.residual[rows, :]
            mixed = jnp.where(place < length, residual + self.total[rows, :], 0.0)
            self.mixed[rows, :] = mixed.astype(jnp.bfloat16)
            factor = lax.rsqrt(jnp.mean(residual * residual, axis=-1, keepdims=True) + NORM_EPS)
            normed = residual * factor
            grad = self.grad_hidden_two[rows, :]
            self.gain_grad[...] += jnp.sum((grad * normed).reshape(8, 8, 1024), axis=0)
            grad_normed = grad * self.gain_row[8:9, :].astype(jnp.float32)
            grad_out = jnp.where(place < length, self.cotangent[rows, :].astype(jnp.float32), 0.0)
            mean = jnp.mean(grad_normed * normed, axis=-1, keepdims=True)
            grad_residual = grad_out + factor * (grad_normed - normed * mean)
            self.grad_residual[rows, :] = grad_residual
            self.grad_proj[rows, :] = grad_residual.astype(jnp.bfloat16)
            return 0

        lax.fori_loop(0, 8, rows_of, 0)
        for name in ("mixed", "grad_residual", "grad_proj", "gain_grad", "gain_row"):
            self.out(name)


FORWARD_OUTS = (
    ("mixed", (512, 1024), jnp.bfloat16),
    ("query", (512, 1024), jnp.bfloat16),
    ("key", (512, 1024), jnp.bfloat16),
    ("value", (512, 1024), jnp.bfloat16),
    ("log_total", (8, 8, 512), jnp.float32),
    ("hidden_t", (1024, 512), jnp.bfloat16),
    ("hidden_two_t", (1024, 512), jnp.bfloat16),
    ("attended_t", (1024, 512), jnp.bfloat16),
    ("branch", (512, 1024), jnp.bfloat16),
    ("middle", (512, 2816), jnp.bfloat16),
    ("grad_gate", (512, 2816), jnp.bfloat16),
    ("grad_up", (512, 2816), jnp.bfloat16),
    ("grad_residual", (512, 1024), jnp.float32),
    ("grad_proj", (512, 1024), jnp.bfloat16),
    ("gain_grad", (8, 1024), jnp.float32),
    ("gain_row", (16, 1024), jnp.bfloat16),
)
FORWARD_OWN = (
    ("hidden", (512, 1024), jnp.bfloat16),
    ("attended", (512, 1024), jnp.bfloat16),
    ("residual", (512, 1024), jnp.float32),
    ("hidden_two", (512, 1024), jnp.bfloat16),
    ("grad_hidden_two", (512, 1024), jnp.float32),
    ("bias", (512, 512), jnp.float32),
    ("total", (512, 1024), jnp.float32),
)
OUT_COPIES = len(FORWARD_OUTS) - 3 + 3 * len(FF_CHUNKS)
KEPT = (QUERY, KEY, VALUE, OUT)


def share_shape(columns):
    return (352, 1024) if columns is None else (2, 64, columns)


def forward_kernel(items, *refs):
    refs = list(refs)

    def take(n):
        taken = refs[:n]
        del refs[:n]
        return taken

    shares = take(7)
    gain_attn, gain_ffn, tokens, cotangent, length = take(5)
    kept = take(len(KEPT))
    names = [name for name, _, _ in FORWARD_OUTS]
    outs = dict(zip(names, take(len(names))))
    full = take(7)
    full_gains, gains = take(2)
    own_names = names + [name for name, _, _ in FORWARD_OWN]
    state = dict(zip(own_names, take(len(own_names))))
    send_sems, recv_sems, own_sems, keep_sems, out_sems = refs
    outgoing = []

    def put(name, columns=None):
        source, target = state[name], outs[name]
        if columns is not None:
            source, target = source.at[:, columns], target.at[:, columns]
        outgoing.append(pltpu.make_async_copy(source, target, out_sems.at[len(outgoing)]))
        outgoing[-1].start()

    z, y, x, c = place()
    far = [lax.rem(z + k, 4) for k in range(4)]
    back = [lax.rem(z + 4 - k, 4) for k in range(4)]
    x_other, y_other, c_other = (
        device(z, y, 1 - x, c),
        device(z, 1 - y, x, c),
        device(z, y, x, 1 - c),
    )
    greet()
    wires = Wires(send_sems, recv_sems)
    own = [
        pltpu.make_async_copy(share, whole.at[z, y], own_sems.at[i])
        for i, (share, whole) in enumerate(zip(shares, full))
    ]
    own_gains = pltpu.make_async_copy(gains, full_gains.at[z, y], own_sems.at[7])
    keep = [
        pltpu.make_async_copy(full[w], kept[n], keep_sems.at[n]) for n, w in enumerate(KEPT)
    ]
    gains[...] = jnp.where(
        lax.broadcasted_iota(jnp.int32, (16, 128), 0) < 8,
        jnp.broadcast_to(gain_attn[...].astype(jnp.float32), (16, 128)),
        jnp.broadcast_to(gain_ffn[...].astype(jnp.float32), (16, 128)),
    ).astype(jnp.bfloat16)
    own_gains.start()
    gain_slot = GATHER_SLOTS * len(items)
    for k in (1, 2, 3):
        wires.send(gain_slot + k, gains, full_gains.at[z, y], device(far[k], y, x, c))
    for copy in own:
        copy.start()

    def slot(i, k):
        return GATHER_SLOTS * i + k

    def along_z(i):
        item = items[i]
        share, whole = shares[item.weight], full[item.weight]
        for k in (1, 2, 3):
            if item.no_x:
                source, target = item.half(share, (), c), item.half(whole, (z, y), c)
            else:
                source, target = item.quarter(share, (), c, x), item.quarter(whole, (z, y), c, x)
            wires.send(slot(i, k), source, target, device(far[k], y, x, c))

    own_done = set()

    def first_hop(i):
        item = items[i]
        whole = full[item.weight]
        if item.weight not in own_done:
            own[item.weight].wait()
            own_done.add(item.weight)
        for k in (1, 2, 3):
            if item.no_x:
                block = item.half(whole, (back[k], y), c)
                wires.arrived(slot(i, k), block)
                wires.send(slot(i, 7 + k), block, block, c_other)
            else:
                block = item.quarter(whole, (back[k], y), c, x)
                wires.arrived(slot(i, k), block)
                wires.send(slot(i, 3 + k), block, block, x_other)
        if item.no_x:
            block = item.half(whole, (ALL, y), c)
        else:
            block = item.quarter(whole, (ALL, y), c, x)
        wires.send(slot(i, 7), block, block, y_other)

    def second_hop(i):
        item = items[i]
        whole = full[item.weight]
        if item.no_x:
            block = item.half(whole, (ALL, 1 - y), c)
            wires.arrived(slot(i, 7), block)
            wires.send(slot(i, 11), block, block, c_other)
            return
        block = item.quarter(whole, (ALL, 1 - y), c, x)
        wires.arrived(slot(i, 7), block)
        wires.send(slot(i, 0), block, block, x_other)
        for k in (1, 2, 3):
            wires.arrived(slot(i, 3 + k), item.quarter(whole, (back[k], y), c, 1 - x))
        for k in (1, 2, 3):
            block = item.half(whole, (back[k], y), c)
            wires.send(slot(i, 7 + k), block, block, c_other)

    def last_hop(i):
        item = items[i]
        whole = full[item.weight]
        if not item.no_x:
            block = item.half(whole, (ALL, 1 - y), c)
            wires.arrived(slot(i, 0), item.quarter(whole, (ALL, 1 - y), c, 1 - x))
            wires.send(slot(i, 11), block, block, c_other)

    def complete(i):
        item = items[i]
        whole = full[item.weight]
        for k in (1, 2, 3):
            wires.arrived(slot(i, 7 + k), item.half(whole, (back[k], y), 1 - c))
        wires.arrived(slot(i, 11), item.half(whole, (ALL, 1 - y), 1 - c))

    def retire(i):
        wires.finish(lambda slot: slot // GATHER_SLOTS == i)

    step_of = Forward(
        dict(
            state,
            out=put,
            tokens=tokens,
            cotangent=cotangent,
            length=length,
            gains=full_gains,
            w_out=full[OUT],
            w_gate=full[GATE],
            w_up=full[UP],
            w_down=full[DOWN].reshape(2816, 1024),
        )
    )
    last_of = {item.weight: i for i, item in enumerate(items)}
    tasks = [(-1, 3, step_of.prepare)]
    for n, name in enumerate(("query", "key", "value")):
        tasks.append((last_of[n], 2, partial(step_of.project, full[n], state[name])))
    tasks += [(last_of[VALUE], 3, partial(step_of.attend, p, p + 2)) for p in (0, 2, 4, 6)]
    tasks.append((last_of[OUT], 3, step_of.project_out))
    for start, size in FF_CHUNKS:
        there = max(
            i for i, item in enumerate(items) if item.weight == UP and item.start == start
        )
        for n in range(start // FF_TILE, (start + size) // FF_TILE):
            tasks.append((there, 3, partial(step_of.feed_forward, n, n + 1)))
        tasks.append((there, 0, partial(step_of.flush, start, size)))

    ahead = 3
    for i in range(min(ahead, len(items))):
        along_z(i)
    own_gains.wait()
    for k in (1, 2, 3):
        wires.arrived(gain_slot + k, full_gains.at[back[k], y])
    wires.send(gain_slot, full_gains.at[:, y], full_gains.at[:, y], y_other)
    stages = (retire, complete, last_hop, second_hop, first_hop)
    lates = (3 * LAG, 3 * LAG - 1, 2 * LAG, LAG, 0)
    for step in range(len(items) + 3 * LAG):
        for late, stage in zip(lates, stages):
            if 0 <= step - late < len(items):
                stage(step - late)
        if step + ahead < len(items):
            along_z(step + ahead)
        if step == 0:
            wires.arrived(gain_slot, full_gains.at[:, 1 - y])
        there = step - lates[1]
        for n, w in enumerate(KEPT):
            if there == last_of[w]:
                keep[n].start()
        spent = 0
        while tasks and tasks[0][0] <= there and spent < 6:
            _, cost, task = tasks.pop(0)
            task()
            spent += cost
    for _, _, task in tasks:
        task()
    step_of.finish()
    for copy in keep + outgoing:
        copy.wait()
    wires.finish()


def forward(tokens, cotangent, lengths, weights, gains):
    items = gather_items()
    shares = [w.reshape(share_shape(n)) for w, n in zip(weights, COLUMNS)]
    wholes = [(4, 2) + share_shape(n) for n in COLUMNS]
    shapes = [jax.ShapeDtypeStruct(wholes[w], jnp.bfloat16) for w in KEPT]
    shapes += [jax.ShapeDtypeStruct(shape, dtype) for _, shape, dtype in FORWARD_OUTS]
    count = GATHER_SLOTS * len(items) + 4
    anywhere = pl.BlockSpec(memory_space=pl.ANY)
    in_vmem = pl.BlockSpec(memory_space=pltpu.VMEM)
    out = pl.pallas_call(
        partial(forward_kernel, items),
        out_shape=shapes,
        in_specs=[anywhere] * 7
        + [in_vmem] * 4
        + [pl.BlockSpec(memory_space=pltpu.SMEM)],
        out_specs=[anywhere] * len(shapes),
        scratch_shapes=[pltpu.VMEM(shape, jnp.bfloat16) for shape in wholes]
        + [pltpu.VMEM((4, 2, 16, 128), jnp.bfloat16), pltpu.VMEM((16, 128), jnp.bfloat16)]
        + [pltpu.VMEM(shape, dtype) for _, shape, dtype in FORWARD_OUTS + FORWARD_OWN]
        + [
            pltpu.SemaphoreType.DMA((count,)),
            pltpu.SemaphoreType.DMA((count,)),
            pltpu.SemaphoreType.DMA((8,)),
            pltpu.SemaphoreType.DMA((len(KEPT),)),
            pltpu.SemaphoreType.DMA((OUT_COPIES,)),
        ],
        compiler_params=pltpu.CompilerParams(
            collective_id=0, has_side_effects=True, vmem_limit_bytes=62 * MIB
        ),
        name="gather_forward",
    )(*shares, *[g.reshape(1, 128) for g in gains], tokens, cotangent, lengths)
    return out[: len(KEPT)], dict(zip([name for name, _, _ in FORWARD_OUTS], out[len(KEPT) :]))


SUM_SLOTS = 9
RING = 4


class Share:
    def __init__(self, weight, start, size, x_first):
        self.weight, self.start, self.size, self.x_first = weight, start, size, x_first
        self.tall = weight == DOWN
        self.width = 128 if self.tall else size // 2
        self.block = (352 if self.tall else 64, self.width)

    def columns(self, c, x):
        start = c * 512 + x * 256 + self.start if self.tall else self.start + c * self.width
        return pl.ds(pl.multiple_of(start, 128), self.width)

    def quarter(self, sums, c, x):
        if self.tall:
            return sums.at[c, x, self.start // 128]
        return sums.at[x, :, self.columns(c, x)]

    def half(self, sums, c):
        if self.tall:
            return sums.at[c, :, self.start // 128]
        return sums.at[:, :, self.columns(c, 0)]


def share_items():
    order = [(GATE, 2048, 768, True), (DOWN, 0, 128, False), (DOWN, 128, 128, True)]
    order += [(GATE, 0, 1024, False), (GATE, 1024, 1024, True)]
    order += [(UP, 0, 1024, True), (UP, 1024, 1024, False), (UP, 2048, 768, False)]
    order += [(OUT, 0, 1024, True), (QUERY, 0, 1024, False), (KEY, 0, 1024, True)]
    order += [(VALUE, 0, 768, True), (VALUE, 768, 256, False)]
    return [Share(*item) for item in order]


def plus(left, right):
    return (left.astype(jnp.float32) + right.astype(jnp.float32)).astype(left.dtype)


def dot_tn(left, right):
    return lax.dot_general(
        left, right, (((0,), (0,)), ((), ())), preferred_element_type=jnp.float32
    )


BACKWARD_IN = (
    "query",
    "key",
    "value",
    "log_total",
    "hidden_t",
    "hidden_two_t",
    "attended_t",
    "branch",
    "grad_residual",
    "grad_proj",
    "gain_grad",
    "gain_row",
)


class Backward:
    def __init__(self, refs):
        self.__dict__.update(refs)

    def prepare(self):
        length = self.length[0, 0]
        for block in range(4):
            rows = slice(128 * block, 128 * block + 128)
            place_k = lax.broadcasted_iota(jnp.int32, (128, 512), 0) + 128 * block
            place_q = lax.broadcasted_iota(jnp.int32, (128, 512), 1)
            same = (place_q >= length) == (place_k >= length)
            allowed = same & (place_k <= place_q)
            self.bias[rows, :] = jnp.where(allowed, 0.0, NEGATIVE)

    def multiply(self, left_t, right, item, target, core):
        columns = item.columns(core, 0)

        def rows(m, _):
            product = dot(left_t[tile(m, 256), :], right[:, columns]).astype(jnp.bfloat16)
            product = product.reshape(2, 2, 64, item.width)
            for xx in (0, 1):
                target[xx, m] = product[:, xx]
            return 0

        lax.fori_loop(0, 4, rows, 0)

    def multiply_tall(self, left, right, item, target, core):
        both = jnp.concatenate([right[:, item.columns(core, xx)] for xx in (0, 1)], axis=1)
        flat = target.reshape(2, 2816, 128)

        def rows(m, _):
            at = tile(m, 256)
            product = dot_tn(left[:, at], both).astype(jnp.bfloat16)
            for xx in (0, 1):
                flat[xx, at, :] = product[:, 128 * xx : 128 * xx + 128]
            return 0

        lax.fori_loop(0, 11, rows, 0)

    def attend_back(self, first, last):
        low = jnp.bfloat16

        def pair(p, _):
            at = tile(p, 128)
            out_rows = self.w_rows[p].reshape(128, 1024)
            grad = dot_nt(self.grad_proj[...], out_rows).astype(low)
            query = (self.query[:, at].astype(jnp.float32) * SCORE_SCALE).astype(low)
            key, value = self.key[:, at], self.value[:, at]
            left = lax.broadcasted_iota(jnp.int32, (512, 128), 1) < HEAD
            none = jnp.zeros((512, 128), low)
            sides = [
                [jnp.where(side, v, none) for v in (query, key, value, grad)]
                for side in (left, ~left)
            ]
            grad_key, grad_value = [None, None], [None, None]
            for block in (0, 1):
                rows, seen = slice(256 * block, 256 * block + 256), slice(0, 256 * block + 256)
                grad_query = None
                parts_key, parts_value = None, None
                for n, (own_query, own_key, own_value, own_grad) in enumerate(sides):
                    scores = dot_nt(own_key[seen], query[rows]) + self.bias[seen, rows]
                    probs = jnp.exp(scores - self.log_total[p, n : n + 1, rows])
                    grad_probs = dot_nt(own_value[seen], grad[rows])
                    centre = jnp.sum(grad_probs * probs, axis=0, keepdims=True)
                    grad_scores = (probs * (grad_probs - centre)).astype(low)
                    part_query = dot_tn(grad_scores, own_key[seen])
                    part_key = dot(grad_scores, own_query[rows])
                    part_value = dot(probs.astype(low), own_grad[rows])
                    if n == 0:
                        grad_query, parts_key, parts_value = part_query, part_key, part_value
                    else:
                        grad_query += part_query
                        parts_key += part_key
                        parts_value += part_value
                self.query[rows, at] = (grad_query * SCORE_SCALE).astype(low)
                if block == 0:
                    grad_key[0], grad_value[0] = parts_key, parts_value
                else:
                    grad_key = [grad_key[0] + parts_key[:256], parts_key[256:]]
                    grad_value = [grad_value[0] + parts_value[:256], parts_value[256:]]
            for block in (0, 1):
                rows = slice(256 * block, 256 * block + 256)
                self.key[rows, at] = grad_key[block].astype(low)
                self.value[rows, at] = grad_value[block].astype(low)
            return 0

        lax.fori_loop(first, last, pair, 0)

    def grad_hidden(self, t):
        at = pl.ds(256 * t, 256)
        total = None
        for n, grad in enumerate((self.query, self.key, self.value)):
            part = dot_nt(grad[...], self.w_rows[2 * n : 2 * n + 2].reshape(256, 1024))
            total = part if total is None else total + part
        self.input_grad[:, at] = total

    def finish(self):
        self.gain_total[...] = jnp.zeros_like(self.gain_total)

        def rows_of(block, _):
            rows = tile(block, 64)
            values = self.tokens[rows, :].astype(jnp.float32)
            factor = lax.rsqrt(jnp.mean(values * values, axis=-1, keepdims=True) + NORM_EPS)
            normed = values * factor
            grad = self.input_grad[rows, :]
            self.gain_total[...] += jnp.sum((grad * normed).reshape(8, 8, 1024), axis=0)
            grad_normed = grad * self.gain_row[0:1, :].astype(jnp.float32)
            mean = jnp.mean(grad_normed * normed, axis=-1, keepdims=True)
            self.input_grad[rows, :] = self.grad_residual[rows, :] + factor * (
                grad_normed - normed * mean
            )
            return 0

        lax.fori_loop(0, 8, rows_of, 0)
        self.gain_lines[...] = jnp.zeros_like(self.gain_lines)
        lines = [jnp.sum(v[...], axis=0, keepdims=True) for v in (self.gain_total, self.gain_grad)]
        for s in range(8):
            for n, line in enumerate(lines):
                self.gain_lines[s // 2, s % 2, n : n + 1] = line[:, 128 * s : 128 * s + 128]


def backward_kernel(items, *refs):
    refs = list(refs)

    def take(n):
        taken = refs[:n]
        del refs[:n]
        return taken

    kept = take(len(KEPT))
    middle_in, grad_gate_in, grad_up_in = take(3)
    saved_in = dict(zip(BACKWARD_IN, take(len(BACKWARD_IN))))
    tokens_in, length = take(2)
    sums = take(7)
    gain_sums, input_grad_out = take(2)
    saved = dict(zip(BACKWARD_IN, take(len(BACKWARD_IN))))
    tokens, input_grad, wide, w_rows, bias, gain_total, gain_lines = take(7)
    mine, from_first, from_second, from_z = (take(len(items)) for _ in range(4))
    ring, tall_ring = take(RING), take(2)
    outbox, tall_outbox = take(2), take(1)
    gain_core, gain_x, gain_y, gain_z = take(4)
    send_sems, recv_sems, load_sems, credit = refs
    z, y, x, c = place()
    far = [lax.rem(z + k, 4) for k in range(4)]
    back = [lax.rem(z + 4 - k, 4) for k in range(4)]
    x_other, y_other, c_other = (
        device(z, y, 1 - x, c),
        device(z, 1 - y, x, c),
        device(z, y, x, 1 - c),
    )
    loads = {}

    def load(name, source, target):
        loads[name] = pltpu.make_async_copy(source, target, load_sems.at[len(loads)])
        loads[name].start()

    waited = set()

    def loaded(*names):
        for name in names:
            if name not in waited:
                loads[name].wait()
                waited.add(name)

    load("grad_gate", grad_gate_in, wide.at[1])
    load("hidden_two_t", saved_in["hidden_two_t"], saved["hidden_two_t"])
    load("middle", middle_in, wide.at[0])
    load("branch", saved_in["branch"], saved["branch"])
    load("out_rows", kept[OUT].reshape(8, 2, 64, 1024), w_rows)
    for name in BACKWARD_IN:
        if name not in loads:
            load(name, saved_in[name], saved[name])
    load("tokens", tokens_in, tokens)
    greet()
    wires = Wires(send_sems, recv_sems)
    work = Backward(
        dict(
            saved,
            tokens=tokens,
            length=length,
            w_rows=w_rows,
            bias=bias,
            input_grad=input_grad,
            gain_total=gain_total,
            gain_lines=gain_lines,
        )
    )
    tall_items = [i for i, item in enumerate(items) if item.tall]
    wide_items = [i for i, item in enumerate(items) if not item.tall]

    def slot(i, k):
        return SUM_SLOTS * i + k

    def from_core(i):
        if items[i].tall:
            return tall_ring[tall_items.index(i)]
        return ring[wide_items.index(i) % RING].at[..., : items[i].width]

    def produce(i):
        item = items[i]
        if item.tall:
            loaded("middle", "branch")
            before = tall_items.index(i) - 1
            if before >= 0:
                wires.finish(lambda s: s == slot(tall_items[before], 0))
            box = tall_outbox[0]
            multiply = partial(work.multiply_tall, wide.at[0], saved["branch"], item)
        else:
            number = wide_items.index(i)
            if number >= 2:
                wires.finish(lambda s: s == slot(wide_items[number - 2], 0))
            box = outbox[number % 2].at[..., : item.width]
            left, right, names = {
                GATE: (saved["hidden_two_t"], wide.at[1], ("hidden_two_t", "grad_gate")),
                UP: (saved["hidden_two_t"], wide.at[0], ("grad_up",)),
                OUT: (saved["attended_t"], saved["grad_proj"], ("attended_t", "grad_proj")),
                QUERY: (saved["hidden_t"], saved["query"], ("hidden_t",)),
                KEY: (saved["hidden_t"], saved["key"], ()),
                VALUE: (saved["hidden_t"], saved["value"], ()),
            }[item.weight]
            loaded(*names)
            multiply = partial(work.multiply, left, right, item)
            if number >= RING:
                pl.semaphore_wait(credit, 1)
        multiply(box, 1 - c)
        wires.send(slot(i, 0), box, from_core(i), c_other)
        multiply(mine[i], c)
        if i == tall_items[-1]:
            load("grad_up", grad_up_in, wide.at[0])

    def first_hop(i):
        item, own, other = items[i], mine[i], from_core(i)
        wires.arrived(slot(i, 0), other)

        def add(at, _):
            for xx in (0, 1):
                for yy in (0, 1):
                    own[xx, at, yy] = plus(own[xx, at, yy], other[xx, at, yy])
            return 0

        lax.fori_loop(0, 4, add, 0)
        if not item.tall and wide_items.index(i) + RING < len(wide_items):
            pl.semaphore_signal(credit, inc=1, device_id=c_other, device_id_type=MESH)
        if item.x_first:
            wires.send(slot(i, 1), own.at[1 - x], from_first[i], x_other)
        else:
            wires.send(slot(i, 1), own.at[:, :, 1 - y], from_first[i], y_other)

    def second_hop(i):
        item, own, other = items[i], mine[i], from_first[i]
        wires.arrived(slot(i, 1), other)

        def add(at, _):
            for side in (0, 1):
                if item.x_first:
                    own[x, at, side] = plus(own[x, at, side], other[at, side])
                else:
                    own[side, at, y] = plus(own[side, at, y], other[side, at])
            return 0

        lax.fori_loop(0, 4, add, 0)
        if item.x_first:
            wires.send(slot(i, 2), own.at[x, :, 1 - y], from_second[i], y_other)
        else:
            to_z(i, lambda k: own.at[:, far[k], y])

    def to_z(i, block):
        for k in (1, 2, 3):
            wires.send(slot(i, 2 + k), block(k), from_z[i].at[k - 1], device(far[k], y, x, c))

    def z_total(i, own_part):
        total = own_part.astype(jnp.float32)
        for k in (1, 2, 3):
            wires.arrived(slot(i, 2 + k), from_z[i].at[k - 1])
            total += from_z[i][k - 1].astype(jnp.float32)
        return total.astype(jnp.bfloat16)

    def third_hop(i):
        item, own, other = items[i], mine[i], from_second[i]
        if not item.x_first:
            own[:, z, y] = z_total(i, own[:, z, y])
            wires.send(slot(i, 2), own.at[:, z, y], other, x_other)
            return
        wires.arrived(slot(i, 2), other)

        def add(at, _):
            own[x, at, y] = plus(own[x, at, y], other[at])
            return 0

        lax.fori_loop(0, 4, add, 0)
        to_z(i, lambda k: own.at[x, far[k], y])

    def fourth_hop(i):
        item, own = items[i], mine[i]
        if not item.x_first:
            wires.arrived(slot(i, 2), from_second[i])
            block = item.half(sums[item.weight], c)
            block[...] = plus(own[:, z, y], from_second[i][...])
            wires.send(slot(i, 7), block, block, c_other)
            return
        block = item.quarter(sums[item.weight], c, x)
        block[...] = z_total(i, own[x, z, y])
        wires.send(slot(i, 6), block, block, x_other)

    def to_sibling(i):
        item = items[i]
        if item.x_first:
            wires.arrived(slot(i, 6), item.quarter(sums[item.weight], c, 1 - x))
            block = item.half(sums[item.weight], c)
            wires.send(slot(i, 7), block, block, c_other)

    def complete(i):
        item = items[i]
        wires.arrived(slot(i, 7), item.half(sums[item.weight], 1 - c))
        wires.finish(lambda s: s // SUM_SLOTS == i)

    base = SUM_SLOTS * len(items)

    def gains_one():
        wires.send(base, gain_lines, gain_core, c_other)

    def gains_two():
        wires.arrived(base, gain_core)
        gain_core[...] = gain_lines[...] + gain_core[...]
        wires.send(base + 1, gain_core, gain_x, x_other)

    def gains_three():
        wires.arrived(base + 1, gain_x)
        gain_x[...] = gain_core[...] + gain_x[...]
        wires.send(base + 2, gain_x.at[:, 1 - y], gain_y, y_other)

    def gains_four():
        wires.arrived(base + 2, gain_y)
        gain_y[...] = gain_x[:, y] + gain_y[...]
        for k in (1, 2, 3):
            wires.send(base + 2 + k, gain_y.at[far[k]], gain_z.at[z], device(far[k], y, x, c))
        gain_z[z] = gain_y[z]

    def gains_five():
        for k in (1, 2, 3):
            wires.arrived(base + 2 + k, gain_z.at[back[k]])
        gain_sums[...] = (gain_z[0] + gain_z[1]) + (gain_z[2] + gain_z[3])

    def fetch_rows(t):
        for n in range(3):
            load(("rows", n, t), kept[n].at[t], w_rows.at[2 * n : 2 * n + 2])

    def attend_back(p):
        if p == 0:
            loaded("query", "key", "value", "log_total", "grad_proj", "out_rows")
        work.attend_back(p, p + 1)
        if p == 7:
            fetch_rows(0)

    def grad_hidden(t):
        loaded(*[("rows", n, t) for n in range(3)])
        work.grad_hidden(t)
        if t < 3:
            fetch_rows(t + 1)

    def finish():
        loaded("tokens", "grad_residual", "gain_grad", "gain_row")
        work.finish()
        load("input_grad", input_grad, input_grad_out)
        gains_one()

    beside = {1: [work.prepare]}
    for p in range(8):
        beside.setdefault(1 + p, []).append(partial(attend_back, p))
    for t in range(4):
        beside.setdefault(9 + t // 2, []).append(partial(grad_hidden, t))
    beside.setdefault(11, []).append(finish)
    for n, task in enumerate((gains_two, gains_three, gains_four, gains_five)):
        beside.setdefault(13 + 2 * n, []).append(task)

    stages = (complete, to_sibling, fourth_hop, third_hop, second_hop, first_hop, produce)
    lates = (11, 9, 7, 5, 3, 1, 0)
    for step in range(len(items) + lates[0]):
        for late, stage in zip(lates, stages):
            if 0 <= step - late < len(items):
                stage(step - late)
        for task in beside.get(step, []):
            task()
    loaded("input_grad")
    wires.finish()


def backward(tokens, lengths, kept, saved):
    items = share_items()
    low, wide = jnp.bfloat16, jnp.float32
    dtypes = {name: (shape, dtype) for name, shape, dtype in FORWARD_OUTS}
    shapes = [
        jax.ShapeDtypeStruct((2, 2, 2, 352, 128) if n is None else (2, 64, n), low) for n in COLUMNS
    ]
    shapes += [jax.ShapeDtypeStruct((8, 128), wide), jax.ShapeDtypeStruct((512, 1024), wide)]
    count = SUM_SLOTS * len(items) + 6
    anywhere = pl.BlockSpec(memory_space=pl.ANY)
    in_vmem = pl.BlockSpec(memory_space=pltpu.VMEM)
    n_loads = 6 + len(BACKWARD_IN) + 12

    def buffers(lead_of):
        return [pltpu.VMEM(lead_of(item) + item.block, low) for item in items]

    out = pl.pallas_call(
        partial(backward_kernel, items),
        out_shape=shapes,
        in_specs=[anywhere] * (len(KEPT) + 3 + len(BACKWARD_IN) + 1)
        + [pl.BlockSpec(memory_space=pltpu.SMEM)],
        out_specs=[in_vmem] * 8 + [anywhere],
        scratch_shapes=[pltpu.VMEM(*dtypes[name]) for name in BACKWARD_IN]
        + [
            pltpu.VMEM((512, 1024), low),
            pltpu.VMEM((512, 1024), wide),
            pltpu.VMEM((2, 512, 2816), low),
            pltpu.VMEM((8, 2, 64, 1024), low),
            pltpu.VMEM((512, 512), wide),
            pltpu.VMEM((8, 1024), wide),
            pltpu.VMEM((4, 2, 8, 128), wide),
        ]
        + buffers(lambda item: (2, 4, 2))
        + buffers(lambda item: (4, 2) if item.x_first else (2, 4))
        + buffers(lambda item: (4,) if item.x_first else (2,))
        + buffers(lambda item: (3,) if item.x_first else (3, 2))
        + [pltpu.VMEM((2, 4, 2, 64, 512), low)] * RING
        + [pltpu.VMEM((2, 4, 2, 352, 128), low)] * 2
        + [pltpu.VMEM((2, 4, 2, 64, 512), low)] * 2
        + [pltpu.VMEM((2, 4, 2, 352, 128), low)]
        + [
            pltpu.VMEM((4, 2, 8, 128), wide),
            pltpu.VMEM((4, 2, 8, 128), wide),
            pltpu.VMEM((4, 8, 128), wide),
            pltpu.VMEM((4, 8, 128), wide),
            pltpu.SemaphoreType.DMA((count,)),
            pltpu.SemaphoreType.DMA((count,)),
            pltpu.SemaphoreType.DMA((n_loads,)),
            pltpu.SemaphoreType.REGULAR,
        ],
        compiler_params=pltpu.CompilerParams(
            collective_id=1, has_side_effects=True, vmem_limit_bytes=62 * MIB
        ),
        name="backward_sum",
    )(
        *kept,
        saved["middle"],
        saved["grad_gate"],
        saved["grad_up"],
        *[saved[name] for name in BACKWARD_IN],
        tokens,
        lengths,
    )
    return out[:7], out[7], out[8]


def unpack_kernel(*refs):
    blocks, (gain_sums, mixed, input_grad) = refs[:7], refs[7:10]
    sums, (gain_attn, gain_ffn, mixed_out, input_out) = refs[10:17], refs[17:21]
    sems = refs[21]
    copies = [
        pltpu.make_async_copy(mixed, mixed_out, sems.at[0]),
        pltpu.make_async_copy(input_grad, input_out, sems.at[1]),
    ]
    for copy in copies:
        copy.start()
    for block, total in zip(blocks[:6], sums[:6]):
        total[...] = block[...].astype(jnp.float32)
    for b in range(8):
        sums[6][:, 128 * b : 128 * b + 128] = blocks[6][b // 4, b // 2 % 2, b % 2].astype(
            jnp.float32
        )
    gain_attn[...] = gain_sums[0:1]
    gain_ffn[...] = gain_sums[1:2]
    for copy in copies:
        copy.wait()


def unpack(blocks, gain_sums, mixed, input_grad):
    wide = jnp.float32
    anywhere = pl.BlockSpec(memory_space=pl.ANY)
    in_vmem = pl.BlockSpec(memory_space=pltpu.VMEM)
    shapes = [
        jax.ShapeDtypeStruct((352, 1024) if n is None else (2, 64, n), wide) for n in COLUMNS
    ]
    shapes += [jax.ShapeDtypeStruct((1, 128), wide)] * 2
    shapes += [jax.ShapeDtypeStruct(v.shape, v.dtype) for v in (mixed, input_grad)]
    out = pl.pallas_call(
        unpack_kernel,
        out_shape=shapes,
        in_specs=[in_vmem] * 8 + [anywhere] * 2,
        out_specs=[in_vmem] * 9 + [anywhere] * 2,
        scratch_shapes=[pltpu.SemaphoreType.DMA((2,))],
        compiler_params=pltpu.CompilerParams(vmem_limit_bytes=62 * MIB),
        name="unpack",
    )(*blocks, gain_sums, mixed, input_grad)
    sums = [s.reshape(-1, s.shape[-1]) for s in out[:7]]
    return sums, [g.reshape(128) for g in out[7:9]], out[9], out[10]


def gather_plain(weights, gains):
    everything = (*weights, *gains)
    whole = [lax.all_gather(v, "dp", axis=0, tiled=True) for v in everything]
    return whole[: len(weights)], whole[len(weights) :]


def sum_plain(grads, gain_grads):
    shares = [
        lax.psum_scatter(g.astype(jnp.float32), "dp", scatter_dimension=0, tiled=True)
        for g in (*grads, *gain_grads)
    ]
    sums = [lax.psum(s, ("rep", "cores")) for s in shares]
    return sums[: len(grads)], sums[len(grads) :]


def on_any_device(
    tokens,
    norm_attn,
    w_query,
    w_key,
    w_value,
    w_out,
    norm_ffn,
    w_gate,
    w_up,
    w_down,
    lengths,
    cotangent,
):
    rows = tokens.shape[0]
    low = jnp.bfloat16
    allowed, valid = masks(lengths, rows)
    whole, gains = gather_plain(
        (w_query, w_key, w_value, w_out, w_gate, w_up, w_down), (norm_attn, norm_ffn)
    )
    full_query, full_key, full_value, full_out, full_gate, full_up, full_down = whole
    gain_attn, gain_ffn = gains
    inputs = tokens.astype(jnp.float32)
    normed, factor = normalize(inputs)
    hidden = (normed * gain_attn.astype(jnp.float32)).astype(low)
    query = matmul(hidden, full_query).astype(low)
    keyed = matmul(hidden, full_key).astype(low)
    valued = matmul(hidden, full_value).astype(low)
    query_groups, key_groups, value_groups = (to_groups(query), to_groups(keyed), to_groups(valued))
    attended_groups, log_total = lax.map(
        partial(attend, allowed), (query_groups, key_groups, value_groups)
    )
    attended = from_groups(attended_groups)
    residual = inputs + matmul(attended, full_out)
    normed_two, factor_two = normalize(residual)
    hidden_two = (normed_two * gain_ffn.astype(jnp.float32)).astype(low)
    gate = matmul(hidden_two, full_gate)
    upward = matmul(hidden_two, full_up)
    sigma = jax.nn.sigmoid(gate)
    middle = (gate * sigma * upward).astype(low)
    mixed = (valid[:, None] * (residual + matmul(middle, full_down))).astype(low)
    grad_output = cotangent.astype(jnp.float32) * valid[:, None]
    grad_branch = grad_output.astype(low)
    grad_down = matmul_tn(middle, grad_branch)
    grad_middle = matmul_nt(grad_branch, full_down)
    grad_gate_rows = (grad_middle * upward * sigma * (1.0 + gate * (1.0 - sigma))).astype(low)
    grad_up_rows = (grad_middle * gate * sigma).astype(low)
    grad_gate = matmul_tn(hidden_two, grad_gate_rows)
    grad_up = matmul_tn(hidden_two, grad_up_rows)
    grad_hidden_two = matmul_nt(grad_gate_rows, full_gate) + matmul_nt(grad_up_rows, full_up)
    grad_gain_ffn = jnp.sum(grad_hidden_two * normed_two, axis=0)
    grad_residual = grad_output + norm_back(
        grad_hidden_two * gain_ffn.astype(jnp.float32), normed_two, factor_two
    )
    grad_proj = grad_residual.astype(low)
    grad_out = matmul_tn(attended, grad_proj)
    grad_attended = matmul_nt(grad_proj, full_out).astype(low)
    grad_query_g, grad_key_g, grad_value_g = lax.map(
        partial(attend_back, allowed),
        (query_groups, key_groups, value_groups, to_groups(grad_attended), log_total),
    )
    grad_query_rows = from_groups(grad_query_g)
    grad_key_rows = from_groups(grad_key_g)
    grad_value_rows = from_groups(grad_value_g)
    grad_query = matmul_tn(hidden, grad_query_rows)
    grad_key = matmul_tn(hidden, grad_key_rows)
    grad_value = matmul_tn(hidden, grad_value_rows)
    grad_hidden = (
        matmul_nt(grad_query_rows, full_query)
        + matmul_nt(grad_key_rows, full_key)
        + matmul_nt(grad_value_rows, full_value)
    )
    grad_gain_attn = jnp.sum(grad_hidden * normed, axis=0)
    input_grad = grad_residual + norm_back(
        grad_hidden * gain_attn.astype(jnp.float32), normed, factor
    )
    grads = (grad_query, grad_key, grad_value, grad_out, grad_gate, grad_up, grad_down)
    sums, gain_sums = sum_plain([g.astype(low) for g in grads], (grad_gain_attn, grad_gain_ffn))
    return (
        mixed,
        input_grad,
        gain_sums[0],
        sums[0],
        sums[1],
        sums[2],
        sums[3],
        gain_sums[1],
        sums[4],
        sums[5],
        sums[6],
    )


def on_tuned_device(
    tokens,
    norm_attn,
    w_query,
    w_key,
    w_value,
    w_out,
    norm_ffn,
    w_gate,
    w_up,
    w_down,
    lengths,
    cotangent,
):
    weights = (w_query, w_key, w_value, w_out, w_gate, w_up, w_down)
    kept, saved = forward(tokens, cotangent, lengths, weights, (norm_attn, norm_ffn))
    blocks, gain_lines, input_grad = backward(tokens, lengths, kept, saved)
    sums, gain_sums, mixed, input_grad = unpack(blocks, gain_lines, saved["mixed"], input_grad)
    return (
        mixed,
        input_grad,
        gain_sums[0],
        *sums[:4],
        gain_sums[1],
        *sums[4:],
    )


def solution(mesh):
    tuned = dict(mesh.shape) == {"dp": 8, "rep": 2, "cores": 2}
    tokens_placed = P(("dp", "rep", "cores"), None)
    share, gain = P("dp", None), P("dp")
    return jax.shard_map(
        on_tuned_device if tuned else on_any_device,
        mesh=mesh,
        in_specs=(
            tokens_placed,
            gain,
            share,
            share,
            share,
            share,
            gain,
            share,
            share,
            share,
            tokens_placed,
            tokens_placed,
        ),
        out_specs=(
            tokens_placed,
            tokens_placed,
            gain,
            share,
            share,
            share,
            share,
            gain,
            share,
            share,
            share,
        ),
        check_vma=False,
    )
```

```python
from functools import partial

import jax
import jax.numpy as jnp
from jax import lax
from jax.experimental import pallas as pl
from jax.experimental.pallas import tpu as pltpu
from jax.sharding import PartitionSpec as P

HEADS = 16
HEAD = 64


NORM_EPS = 1e-05
SCORE_SCALE = 0.125
NEGATIVE = -1e30
head_group = 4
MESH = pl.DeviceIdType.MESH
MIB = 1024 * 1024


def masks(block_len, rows):
    bounds = jnp.cumsum(block_len[0])
    place = jnp.arange(rows, dtype=jnp.int32)
    segment = jnp.sum((place[:, None] >= bounds[None, :]).astype(jnp.int32), axis=1)
    allowed = (segment[:, None] == segment[None, :]) & (place[None, :] <= place[:, None])
    valid = (segment < block_len.shape[1]).astype(jnp.float32)
    return (allowed, valid)


def normalize(values):
    factor = lax.rsqrt(jnp.mean(values * values, axis=-1, keepdims=True) + NORM_EPS)
    return (values * factor, factor)


def norm_back(grad_normed, normed, factor):
    return factor * (grad_normed - normed * jnp.mean(grad_normed * normed, axis=-1, keepdims=True))


def matmul(left, right):
    return jnp.dot(left, right, preferred_element_type=jnp.float32)


def matmul_tn(left, right):
    return lax.dot_general(
        left, right, (((0,), (0,)), ((), ())), preferred_element_type=jnp.float32
    )


def matmul_nt(left, right):
    return lax.dot_general(
        left, right, (((1,), (1,)), ((), ())), preferred_element_type=jnp.float32
    )


def to_groups(matrix):
    rows = matrix.shape[0]
    split = matrix.reshape(rows, HEADS // head_group, head_group, HEAD)
    return split.transpose(1, 2, 0, 3)


def from_groups(grouped):
    rows = grouped.shape[2]
    return grouped.transpose(2, 0, 1, 3).reshape(rows, HEADS * HEAD)


def group_scores(allowed, query_g, key_g):
    raw = (
        jnp.einsum("hqe,hke->hqk", query_g, key_g, preferred_element_type=jnp.float32) * SCORE_SCALE
    )
    return jnp.where(allowed[None], raw, NEGATIVE)


def attend(allowed, operands):
    query_g, key_g, value_g = operands
    scores = group_scores(allowed, query_g, key_g)
    top = jnp.max(scores, axis=-1, keepdims=True)
    expo = jnp.exp(scores - top)
    total = jnp.sum(expo, axis=-1, keepdims=True)
    probs_low = (expo / total).astype(jnp.bfloat16)
    result = jnp.einsum("hqk,hke->hqe", probs_low, value_g, preferred_element_type=jnp.float32)
    return (result.astype(jnp.bfloat16), top[..., 0] + jnp.log(total[..., 0]))


def attend_back(allowed, operands):
    query_g, key_g, value_g, grad_g, log_total = operands
    scores = group_scores(allowed, query_g, key_g)
    probs = jnp.exp(scores - log_total[..., None])
    grad_probs = jnp.einsum("hqe,hke->hqk", grad_g, value_g, preferred_element_type=jnp.float32)
    centre = jnp.sum(grad_probs * probs, axis=-1, keepdims=True)
    grad_scores = (probs * (grad_probs - centre)).astype(jnp.bfloat16)
    grad_query = (
        jnp.einsum("hqk,hke->hqe", grad_scores, key_g, preferred_element_type=jnp.float32)
        * SCORE_SCALE
    )
    grad_key = (
        jnp.einsum("hqk,hqe->hke", grad_scores, query_g, preferred_element_type=jnp.float32)
        * SCORE_SCALE
    )
    grad_value = jnp.einsum(
        "hqk,hqe->hke", probs.astype(jnp.bfloat16), grad_g, preferred_element_type=jnp.float32
    )
    return (
        grad_query.astype(jnp.bfloat16),
        grad_key.astype(jnp.bfloat16),
        grad_value.astype(jnp.bfloat16),
    )


class Part:
    def __init__(self, weight, tall, start, size, no_x):
        self.weight, self.tall, self.start, self.size = weight, tall, start, size
        self.no_x = no_x

    def quarter(self, ref, lead, c, x):
        if self.tall:
            columns = pl.ds(pl.multiple_of(c * 512 + x * 256, 256), 256)
            return ref.at[(*lead, pl.ds(self.start, self.size), columns)]
        return ref.at[(*lead, x, slice(None), self.columns(c))]

    def half(self, ref, lead, c):
        if self.tall:
            columns = pl.ds(pl.multiple_of(c * 512, 512), 512)
            return ref.at[(*lead, pl.ds(self.start, self.size), columns)]
        return ref.at[(*lead, slice(None), slice(None), self.columns(c))]

    def columns(self, c):
        width = self.size // 2
        return pl.ds(pl.multiple_of(self.start + c * width, 128), width)


def pieces(total, most):
    return [(start, min(most, total - start)) for start in range(0, total, most)]


def place():
    d = lax.axis_index("dp")
    return lax.div(d, 2), lax.rem(d, 2), lax.axis_index("rep"), lax.axis_index("cores")


def device(z, y, x, c):
    return {"dp": 2 * z + y, "rep": x, "cores": c}


def greet():
    z, y, x, c = place()
    barrier = pltpu.get_barrier_semaphore()
    others = [device(lax.rem(z + k, 4), y, x, c) for k in (1, 2, 3)]
    others += [device(z, 1 - y, x, c), device(z, y, 1 - x, c), device(z, y, x, 1 - c)]
    for other in others:
        pl.semaphore_signal(barrier, inc=1, device_id=other, device_id_type=MESH)
    pl.semaphore_wait(barrier, len(others))


class Wires:
    def __init__(self, send_sems, recv_sems):
        self.send_sems, self.recv_sems, self.sent = send_sems, recv_sems, []

    def copy(self, slot, source, target, other):
        return pltpu.make_async_remote_copy(
            src_ref=source,
            dst_ref=target,
            send_sem=self.send_sems.at[slot],
            recv_sem=self.recv_sems.at[slot],
            device_id=other,
            device_id_type=MESH,
        )

    def send(self, slot, source, target, other):
        copy = self.copy(slot, source, target, other)
        copy.start()
        self.sent.append((slot, copy))

    def arrived(self, slot, target):
        z, y, x, c = place()
        self.copy(slot, target, target, device(z, y, x, 1 - c)).wait_recv()

    def finish(self, chosen=lambda slot: True):
        for slot, copy in self.sent:
            if chosen(slot):
                copy.wait_send()
        self.sent = [(slot, copy) for slot, copy in self.sent if not chosen(slot)]


GATHER_SLOTS = 12
LAG = 2
ALL = slice(None)
COLUMNS = (1024, 1024, 1024, 1024, 2816, 2816, None)
QUERY, KEY, VALUE, OUT, GATE, UP, DOWN = range(7)
TILE = 256
FF_TILE = 256


FF_CHUNKS = ((0, 512), (512, 768), (1280, 768), (2048, 512), (2560, 256))


def gather_items():
    order = [(QUERY, 0, 256, True), (QUERY, 256, 768, False), (KEY, 0, 1024, True)]
    order += [(VALUE, 0, 1024, False), (OUT, 0, 1024, False)]
    order += [(DOWN, 0, 128, False), (DOWN, 128, 128, True), (DOWN, 256, 96, False)]
    for n, (start, size) in enumerate(FF_CHUNKS):
        order += [(GATE, start, size, n == 4), (UP, start, size, n in (1, 4))]
    return [Part(w, w == DOWN, start, size, no_x) for w, start, size, no_x in order]


def dot(left, right):
    return lax.dot_general(
        left, right, (((1,), (0,)), ((), ())), preferred_element_type=jnp.float32
    )


def dot_nt(left, right):
    return lax.dot_general(
        left, right, (((1,), (1,)), ((), ())), preferred_element_type=jnp.float32
    )


def tile(index, size):
    return pl.ds(pl.multiple_of(index * size, size), size)


def weight_columns(ref, at):
    return ref[:, :, :, :, at].reshape(1024, -1)


class Forward:
    def __init__(self, refs):
        self.__dict__.update(refs)

    def prepare(self):
        for s in range(8):
            self.gain_row[:, 128 * s : 128 * s + 128] = self.gains[s // 2, s % 2]
        length = self.length[0, 0]
        for block in range(4):
            rows = slice(128 * block, 128 * block + 128)
            place_q = lax.broadcasted_iota(jnp.int32, (128, 512), 0) + 128 * block
            place_k = lax.broadcasted_iota(jnp.int32, (128, 512), 1)
            same = (place_q >= length) == (place_k >= length)
            allowed = same & (place_k <= place_q)
            self.bias[rows, :] = jnp.where(allowed, 0.0, NEGATIVE)

        def normed(block, _):
            rows = tile(block, 64)
            values = self.tokens[rows, :].astype(jnp.float32)
            factor = lax.rsqrt(jnp.mean(values * values, axis=-1, keepdims=True) + NORM_EPS)
            gain = self.gain_row[0:1, :].astype(jnp.float32)
            self.hidden[rows, :] = (values * factor * gain).astype(jnp.bfloat16)
            place = lax.broadcasted_iota(jnp.int32, (64, 1024), 0) + 64 * block
            branch = jnp.where(place < length, self.cotangent[rows, :].astype(jnp.float32), 0.0)
            self.branch[rows, :] = branch.astype(jnp.bfloat16)
            return 0

        lax.fori_loop(0, 8, normed, 0)
        self.turn(self.hidden, self.hidden_t)
        self.out("branch")

    def turn(self, matrix, turned):
        def columns(n, _):
            at = tile(n, 128)
            turned[at, :] = matrix[:, at].astype(jnp.float32).T.astype(jnp.bfloat16)
            return 0

        lax.fori_loop(0, 8, columns, 0)

    def project(self, weight, result):
        def columns(n, _):
            at = tile(n, TILE)
            result[:, at] = dot(self.hidden[...], weight_columns(weight, at)).astype(jnp.bfloat16)
            return 0

        lax.fori_loop(0, 1024 // TILE, columns, 0)

    def attend(self, first, last):
        def pair(p, _):
            at = tile(p, 128)
            left = lax.broadcasted_iota(jnp.int32, (256, 128), 1) < HEAD
            for block in (0, 1):
                rows, seen = slice(256 * block, 256 * block + 256), slice(0, 256 * block + 256)
                query = self.query[rows, at].astype(jnp.float32) * SCORE_SCALE
                outs, totals = [], []
                for side in (left, ~left):
                    own = jnp.where(side, query, 0.0).astype(jnp.bfloat16)
                    scores = dot_nt(own, self.key[seen, at]) + self.bias[rows, seen]
                    top = jnp.max(scores, axis=-1, keepdims=True)
                    expo = jnp.exp(scores - top)
                    total = jnp.sum(expo, axis=-1, keepdims=True)
                    probs = (expo * (1.0 / total)).astype(jnp.bfloat16)
                    outs.append(dot(probs, self.value[seen, at]))
                    totals.append(top + jnp.log(total))
                self.attended[rows, at] = jnp.where(left, outs[0], outs[1]).astype(jnp.bfloat16)
                turned = jnp.where(left, totals[0], totals[1]).T
                self.log_total[p, 0:1, rows] = turned[0:1]
                self.log_total[p, 1:2, rows] = turned[HEAD : HEAD + 1]
            return 0

        lax.fori_loop(first, last, pair, 0)

    def project_out(self):
        def columns(n, _):
            at = tile(n, TILE)
            self.residual[:, at] = self.tokens[:, at].astype(jnp.float32) + dot(
                self.attended[...], weight_columns(self.w_out, at)
            )
            return 0

        lax.fori_loop(0, 1024 // TILE, columns, 0)

        def normed(block, _):
            rows = tile(block, 64)
            values = self.residual[rows, :]
            factor = lax.rsqrt(jnp.mean(values * values, axis=-1, keepdims=True) + NORM_EPS)
            gain = self.gain_row[8:9, :].astype(jnp.float32)
            self.hidden_two[rows, :] = (values * factor * gain).astype(jnp.bfloat16)
            return 0

        lax.fori_loop(0, 8, normed, 0)
        self.turn(self.hidden_two, self.hidden_two_t)
        self.turn(self.attended, self.attended_t)
        for name in ("query", "key", "value", "log_total", "hidden_t", "hidden_two_t", "attended_t"):
            self.out(name)

    def grad_of_middle(self, first, last):
        def columns(n, _):
            at = tile(n, FF_TILE)
            grad = dot_nt(self.branch[...], self.w_down[at, :])
            self.grad_up[:, at] = grad.astype(jnp.bfloat16)
            return 0

        lax.fori_loop(first, last, columns, 0)

    def feed_forward(self, first, last):
        def columns(n, first_of_all):
            at = tile(n, FF_TILE)
            low = jnp.bfloat16
            gate_w = weight_columns(self.w_gate, at)
            up_w = weight_columns(self.w_up, at)
            down_w = self.w_down[at, :]
            gate = dot(self.hidden_two[...], gate_w)
            upward = dot(self.hidden_two[...], up_w)
            grad_middle = self.grad_up[:, at].astype(jnp.float32)
            sigma = 1.0 / (1.0 + jnp.exp(-gate))
            silu = gate * sigma
            middle = (silu * upward).astype(low)
            grad_up = (grad_middle * silu).astype(low)
            grad_gate = (grad_middle * upward * sigma * (1.0 + gate * (1.0 - sigma))).astype(low)
            self.middle[:, at] = middle
            self.grad_up[:, at] = grad_up
            self.grad_gate[:, at] = grad_gate
            for j in range(4):
                part = slice(256 * j, 256 * j + 256)
                mixed = dot(middle, down_w[:, part])
                grad = dot_nt(grad_gate, gate_w[part, :]) + dot_nt(grad_up, up_w[part, :])
                if first_of_all is True:
                    self.total[:, part] = mixed
                    self.grad_hidden_two[:, part] = grad
                else:
                    self.total[:, part] += mixed
                    self.grad_hidden_two[:, part] += grad
            return 0

        if first == 0:
            columns(0, True)
            first = 1
        lax.fori_loop(first, last, lambda n, _: columns(n, False), 0)

    def flush(self, start, size):
        for name in ("middle", "grad_gate", "grad_up"):
            self.out(name, pl.ds(start, size))

    def finish(self):
        length = self.length[0, 0]
        self.gain_grad[...] = jnp.zeros_like(self.gain_grad)

        def rows_of(block, _):
            rows = tile(block, 64)
            place = lax.broadcasted_iota(jnp.int32, (64, 1024), 0) + 64 * block
            residual = self.residual[rows, :]
            mixed = jnp.where(place < length, residual + self.total[rows, :], 0.0)
            self.mixed[rows, :] = mixed.astype(jnp.bfloat16)
            factor = lax.rsqrt(jnp.mean(residual * residual, axis=-1, keepdims=True) + NORM_EPS)
            normed = residual * factor
            grad = self.grad_hidden_two[rows, :]
            self.gain_grad[...] += jnp.sum((grad * normed).reshape(8, 8, 1024), axis=0)
            grad_normed = grad * self.gain_row[8:9, :].astype(jnp.float32)
            grad_out = jnp.where(place < length, self.cotangent[rows, :].astype(jnp.float32), 0.0)
            mean = jnp.mean(grad_normed * normed, axis=-1, keepdims=True)
            grad_residual = grad_out + factor * (grad_normed - normed * mean)
            self.grad_residual[rows, :] = grad_residual
            self.grad_proj[rows, :] = grad_residual.astype(jnp.bfloat16)
            return 0

        lax.fori_loop(0, 8, rows_of, 0)
        for name in ("mixed", "grad_residual", "grad_proj", "gain_grad", "gain_row"):
            self.out(name)


FORWARD_OUTS = (
    ("mixed", (512, 1024), jnp.bfloat16),
    ("query", (512, 1024), jnp.bfloat16),
    ("key", (512, 1024), jnp.bfloat16),
    ("value", (512, 1024), jnp.bfloat16),
    ("log_total", (8, 8, 512), jnp.float32),
    ("hidden_t", (1024, 512), jnp.bfloat16),
    ("hidden_two_t", (1024, 512), jnp.bfloat16),
    ("attended_t", (1024, 512), jnp.bfloat16),
    ("branch", (512, 1024), jnp.bfloat16),
    ("middle", (512, 2816), jnp.bfloat16),
    ("grad_gate", (512, 2816), jnp.bfloat16),
    ("grad_up", (512, 2816), jnp.bfloat16),
    ("grad_residual", (512, 1024), jnp.float32),
    ("grad_proj", (512, 1024), jnp.bfloat16),
    ("gain_grad", (8, 1024), jnp.float32),
    ("gain_row", (16, 1024), jnp.bfloat16),
)
FORWARD_OWN = (
    ("hidden", (512, 1024), jnp.bfloat16),
    ("attended", (512, 1024), jnp.bfloat16),
    ("residual", (512, 1024), jnp.float32),
    ("hidden_two", (512, 1024), jnp.bfloat16),
    ("grad_hidden_two", (512, 1024), jnp.float32),
    ("bias", (512, 512), jnp.float32),
    ("total", (512, 1024), jnp.float32),
)
OUT_COPIES = len(FORWARD_OUTS) - 3 + 3 * len(FF_CHUNKS)
KEPT = (QUERY, KEY, VALUE, OUT)


def share_shape(columns):
    return (352, 1024) if columns is None else (2, 64, columns)


def forward_kernel(items, *refs):
    refs = list(refs)

    def take(n):
        taken = refs[:n]
        del refs[:n]
        return taken

    shares = take(7)
    gain_attn, gain_ffn, tokens, cotangent, length = take(5)
    kept = take(len(KEPT))
    names = [name for name, _, _ in FORWARD_OUTS]
    outs = dict(zip(names, take(len(names))))
    full = take(7)
    full_gains, gains = take(2)
    own_names = names + [name for name, _, _ in FORWARD_OWN]
    state = dict(zip(own_names, take(len(own_names))))
    send_sems, recv_sems, own_sems, keep_sems, out_sems = refs
    outgoing = []

    def put(name, columns=None):
        source, target = state[name], outs[name]
        if columns is not None:
            source, target = source.at[:, columns], target.at[:, columns]
        outgoing.append(pltpu.make_async_copy(source, target, out_sems.at[len(outgoing)]))
        outgoing[-1].start()

    z, y, x, c = place()
    far = [lax.rem(z + k, 4) for k in range(4)]
    back = [lax.rem(z + 4 - k, 4) for k in range(4)]
    x_other, y_other, c_other = (
        device(z, y, 1 - x, c),
        device(z, 1 - y, x, c),
        device(z, y, x, 1 - c),
    )
    greet()
    wires = Wires(send_sems, recv_sems)
    own = [
        pltpu.make_async_copy(share, whole.at[z, y], own_sems.at[i])
        for i, (share, whole) in enumerate(zip(shares, full))
    ]
    own_gains = pltpu.make_async_copy(gains, full_gains.at[z, y], own_sems.at[7])
    keep = [
        pltpu.make_async_copy(full[w], kept[n], keep_sems.at[n]) for n, w in enumerate(KEPT)
    ]
    gains[...] = jnp.where(
        lax.broadcasted_iota(jnp.int32, (16, 128), 0) < 8,
        jnp.broadcast_to(gain_attn[...].astype(jnp.float32), (16, 128)),
        jnp.broadcast_to(gain_ffn[...].astype(jnp.float32), (16, 128)),
    ).astype(jnp.bfloat16)
    own_gains.start()
    gain_slot = GATHER_SLOTS * len(items)
    for k in (1, 2, 3):
        wires.send(gain_slot + k, gains, full_gains.at[z, y], device(far[k], y, x, c))
    for copy in own:
        copy.start()

    def slot(i, k):
        return GATHER_SLOTS * i + k

    def along_z(i):
        item = items[i]
        share, whole = shares[item.weight], full[item.weight]
        for k in (1, 2, 3):
            if item.no_x:
                source, target = item.half(share, (), c), item.half(whole, (z, y), c)
            else:
                source, target = item.quarter(share, (), c, x), item.quarter(whole, (z, y), c, x)
            wires.send(slot(i, k), source, target, device(far[k], y, x, c))

    own_done = set()

    def first_hop(i):
        item = items[i]
        whole = full[item.weight]
        if item.weight not in own_done:
            own[item.weight].wait()
            own_done.add(item.weight)
        for k in (1, 2, 3):
            if item.no_x:
                block = item.half(whole, (back[k], y), c)
                wires.arrived(slot(i, k), block)
                wires.send(slot(i, 7 + k), block, block, c_other)
            else:
                block = item.quarter(whole, (back[k], y), c, x)
                wires.arrived(slot(i, k), block)
                wires.send(slot(i, 3 + k), block, block, x_other)
        if item.no_x:
            block = item.half(whole, (ALL, y), c)
        else:
            block = item.quarter(whole, (ALL, y), c, x)
        wires.send(slot(i, 7), block, block, y_other)

    def second_hop(i):
        item = items[i]
        whole = full[item.weight]
        if item.no_x:
            block = item.half(whole, (ALL, 1 - y), c)
            wires.arrived(slot(i, 7), block)
            wires.send(slot(i, 11), block, block, c_other)
            return
        block = item.quarter(whole, (ALL, 1 - y), c, x)
        wires.arrived(slot(i, 7), block)
        wires.send(slot(i, 0), block, block, x_other)
        for k in (1, 2, 3):
            wires.arrived(slot(i, 3 + k), item.quarter(whole, (back[k], y), c, 1 - x))
        for k in (1, 2, 3):
            block = item.half(whole, (back[k], y), c)
            wires.send(slot(i, 7 + k), block, block, c_other)

    def last_hop(i):
        item = items[i]
        whole = full[item.weight]
        if not item.no_x:
            block = item.half(whole, (ALL, 1 - y), c)
            wires.arrived(slot(i, 0), item.quarter(whole, (ALL, 1 - y), c, 1 - x))
            wires.send(slot(i, 11), block, block, c_other)

    def complete(i):
        item = items[i]
        whole = full[item.weight]
        for k in (1, 2, 3):
            wires.arrived(slot(i, 7 + k), item.half(whole, (back[k], y), 1 - c))
        wires.arrived(slot(i, 11), item.half(whole, (ALL, 1 - y), 1 - c))

    def retire(i):
        wires.finish(lambda slot: slot // GATHER_SLOTS == i)

    step_of = Forward(
        dict(
            state,
            out=put,
            tokens=tokens,
            cotangent=cotangent,
            length=length,
            gains=full_gains,
            w_out=full[OUT],
            w_gate=full[GATE],
            w_up=full[UP],
            w_down=full[DOWN].reshape(2816, 1024),
        )
    )
    last_of = {item.weight: i for i, item in enumerate(items)}
    tasks = [(-1, 3, step_of.prepare)]
    for n, name in enumerate(("query", "key", "value")):
        tasks.append((last_of[n], 2, partial(step_of.project, full[n], state[name])))
    tasks += [(last_of[VALUE], 3, partial(step_of.attend, p, p + 2)) for p in (0, 2, 4, 6)]
    tasks.append((last_of[OUT], 3, step_of.project_out))
    for n in range(0, 11, 4):
        tasks.append((last_of[DOWN], 3, partial(step_of.grad_of_middle, n, min(n + 4, 11))))
    for start, size in FF_CHUNKS:
        there = max(
            i for i, item in enumerate(items) if item.weight == UP and item.start == start
        )
        for n in range(start // FF_TILE, (start + size) // FF_TILE):
            tasks.append((there, 3, partial(step_of.feed_forward, n, n + 1)))
        tasks.append((there, 0, partial(step_of.flush, start, size)))

    ahead = 3
    for i in range(min(ahead, len(items))):
        along_z(i)
    own_gains.wait()
    for k in (1, 2, 3):
        wires.arrived(gain_slot + k, full_gains.at[back[k], y])
    wires.send(gain_slot, full_gains.at[:, y], full_gains.at[:, y], y_other)
    stages = (retire, complete, last_hop, second_hop, first_hop)
    lates = (3 * LAG, 3 * LAG - 1, 2 * LAG, LAG, 0)
    for step in range(len(items) + 3 * LAG):
        for late, stage in zip(lates, stages):
            if 0 <= step - late < len(items):
                stage(step - late)
        if step + ahead < len(items):
            along_z(step + ahead)
        if step == 0:
            wires.arrived(gain_slot, full_gains.at[:, 1 - y])
        there = step - lates[1]
        for n, w in enumerate(KEPT):
            if there == last_of[w]:
                keep[n].start()
        spent = 0
        while tasks and tasks[0][0] <= there and spent < 6:
            _, cost, task = tasks.pop(0)
            task()
            spent += cost
    for _, _, task in tasks:
        task()
    step_of.finish()
    for copy in keep + outgoing:
        copy.wait()
    wires.finish()


def forward(tokens, cotangent, lengths, weights, gains):
    items = gather_items()
    shares = [w.reshape(share_shape(n)) for w, n in zip(weights, COLUMNS)]
    wholes = [(4, 2) + share_shape(n) for n in COLUMNS]
    shapes = [jax.ShapeDtypeStruct(wholes[w], jnp.bfloat16) for w in KEPT]
    shapes += [jax.ShapeDtypeStruct(shape, dtype) for _, shape, dtype in FORWARD_OUTS]
    count = GATHER_SLOTS * len(items) + 4
    anywhere = pl.BlockSpec(memory_space=pl.ANY)
    in_vmem = pl.BlockSpec(memory_space=pltpu.VMEM)
    out = pl.pallas_call(
        partial(forward_kernel, items),
        out_shape=shapes,
        in_specs=[anywhere] * 7
        + [in_vmem] * 4
        + [pl.BlockSpec(memory_space=pltpu.SMEM)],
        out_specs=[anywhere] * len(shapes),
        scratch_shapes=[pltpu.VMEM(shape, jnp.bfloat16) for shape in wholes]
        + [pltpu.VMEM((4, 2, 16, 128), jnp.bfloat16), pltpu.VMEM((16, 128), jnp.bfloat16)]
        + [pltpu.VMEM(shape, dtype) for _, shape, dtype in FORWARD_OUTS + FORWARD_OWN]
        + [
            pltpu.SemaphoreType.DMA((count,)),
            pltpu.SemaphoreType.DMA((count,)),
            pltpu.SemaphoreType.DMA((8,)),
            pltpu.SemaphoreType.DMA((len(KEPT),)),
            pltpu.SemaphoreType.DMA((OUT_COPIES,)),
        ],
        compiler_params=pltpu.CompilerParams(
            collective_id=0, has_side_effects=True, vmem_limit_bytes=62 * MIB
        ),
        name="gather_forward",
    )(*shares, *[g.reshape(1, 128) for g in gains], tokens, cotangent, lengths)
    return out[: len(KEPT)], dict(zip([name for name, _, _ in FORWARD_OUTS], out[len(KEPT) :]))


SUM_SLOTS = 10
RING = 4


class Share:
    def __init__(self, weight, start, size, x_first):
        self.weight, self.start, self.size, self.x_first = weight, start, size, x_first
        self.tall = weight == DOWN
        self.width = 128 if self.tall else size // 2
        self.block = (352 if self.tall else 64, self.width)

    def columns(self, c, x):
        start = c * 512 + x * 256 + self.start if self.tall else self.start + c * self.width
        return pl.ds(pl.multiple_of(start, 128), self.width)

    def quarter(self, sums, c, x):
        if self.tall:
            return sums.at[c, x, self.start // 128]
        return sums.at[x, :, self.columns(c, x)]

    def half(self, sums, c):
        if self.tall:
            return sums.at[c, :, self.start // 128]
        return sums.at[:, :, self.columns(c, 0)]


def share_items():
    order = [(GATE, 2048, 768, True), (DOWN, 0, 128, False), (DOWN, 128, 128, True)]
    order += [(GATE, 0, 1024, False), (GATE, 1024, 1024, True)]
    order += [(UP, 0, 1024, True), (UP, 1024, 1024, False), (UP, 2048, 768, False)]
    order += [(OUT, 0, 1024, True), (QUERY, 0, 1024, False), (KEY, 0, 1024, True)]
    order += [(VALUE, 0, 768, True), (VALUE, 768, 256, False)]
    return [Share(*item) for item in order]


def plus(left, right):
    return (left.astype(jnp.float32) + right.astype(jnp.float32)).astype(left.dtype)


def dot_tn(left, right):
    return lax.dot_general(
        left, right, (((0,), (0,)), ((), ())), preferred_element_type=jnp.float32
    )


BACKWARD_IN = (
    "query",
    "key",
    "value",
    "log_total",
    "hidden_t",
    "hidden_two_t",
    "attended_t",
    "branch",
    "grad_residual",
    "grad_proj",
    "gain_grad",
    "gain_row",
)


class Backward:
    def __init__(self, refs):
        self.__dict__.update(refs)

    def prepare(self):
        length = self.length[0, 0]
        for block in range(4):
            rows = slice(128 * block, 128 * block + 128)
            place_k = lax.broadcasted_iota(jnp.int32, (128, 512), 0) + 128 * block
            place_q = lax.broadcasted_iota(jnp.int32, (128, 512), 1)
            same = (place_q >= length) == (place_k >= length)
            allowed = same & (place_k <= place_q)
            self.bias[rows, :] = jnp.where(allowed, 0.0, NEGATIVE)

    def multiply(self, left_t, right, item, target, core):
        columns = item.columns(core, 0)

        def rows(m, _):
            product = dot(left_t[tile(m, 256), :], right[:, columns]).astype(jnp.bfloat16)
            product = product.reshape(2, 2, 64, item.width)
            for xx in (0, 1):
                target[xx, m] = product[:, xx]
            return 0

        lax.fori_loop(0, 4, rows, 0)

    def multiply_tall(self, left, right, item, target, core):
        both = jnp.concatenate([right[:, item.columns(core, xx)] for xx in (0, 1)], axis=1)
        flat = target.reshape(2, 2816, 128)

        def rows(m, _):
            at = tile(m, 256)
            product = dot_tn(left[:, at], both).astype(jnp.bfloat16)
            for xx in (0, 1):
                flat[xx, at, :] = product[:, 128 * xx : 128 * xx + 128]
            return 0

        lax.fori_loop(0, 11, rows, 0)

    def attend_back(self, first, last):
        low = jnp.bfloat16

        def pair(p, _):
            at = tile(p, 128)
            out_rows = self.w_rows[p].reshape(128, 1024)
            grad = dot_nt(self.grad_proj[...], out_rows).astype(low)
            query = (self.query[:, at].astype(jnp.float32) * SCORE_SCALE).astype(low)
            key, value = self.key[:, at], self.value[:, at]
            left = lax.broadcasted_iota(jnp.int32, (512, 128), 1) < HEAD
            none = jnp.zeros((512, 128), low)
            sides = [
                [jnp.where(side, v, none) for v in (query, key, value, grad)]
                for side in (left, ~left)
            ]
            grad_key, grad_value = [None, None], [None, None]
            for block in (0, 1):
                rows, seen = slice(256 * block, 256 * block + 256), slice(0, 256 * block + 256)
                grad_query = None
                parts_key, parts_value = None, None
                for n, (own_query, own_key, own_value, own_grad) in enumerate(sides):
                    scores = dot_nt(own_key[seen], query[rows]) + self.bias[seen, rows]
                    probs = jnp.exp(scores - self.log_total[p, n : n + 1, rows])
                    grad_probs = dot_nt(own_value[seen], grad[rows])
                    centre = jnp.sum(grad_probs * probs, axis=0, keepdims=True)
                    grad_scores = (probs * (grad_probs - centre)).astype(low)
                    part_query = dot_tn(grad_scores, own_key[seen])
                    part_key = dot(grad_scores, own_query[rows])
                    part_value = dot(probs.astype(low), own_grad[rows])
                    if n == 0:
                        grad_query, parts_key, parts_value = part_query, part_key, part_value
                    else:
                        grad_query += part_query
                        parts_key += part_key
                        parts_value += part_value
                self.query[rows, at] = (grad_query * SCORE_SCALE).astype(low)
                if block == 0:
                    grad_key[0], grad_value[0] = parts_key, parts_value
                else:
                    grad_key = [grad_key[0] + parts_key[:256], parts_key[256:]]
                    grad_value = [grad_value[0] + parts_value[:256], parts_value[256:]]
            for block in (0, 1):
                rows = slice(256 * block, 256 * block + 256)
                self.key[rows, at] = grad_key[block].astype(low)
                self.value[rows, at] = grad_value[block].astype(low)
            return 0

        lax.fori_loop(first, last, pair, 0)

    def grad_hidden(self, t):
        at = pl.ds(256 * t, 256)
        total = None
        for n, grad in enumerate((self.query, self.key, self.value)):
            part = dot_nt(grad[...], self.w_rows[2 * n : 2 * n + 2].reshape(256, 1024))
            total = part if total is None else total + part
        self.input_grad[:, at] = total

    def finish(self):
        self.gain_total[...] = jnp.zeros_like(self.gain_total)

        def rows_of(block, _):
            rows = tile(block, 64)
            values = self.tokens[rows, :].astype(jnp.float32)
            factor = lax.rsqrt(jnp.mean(values * values, axis=-1, keepdims=True) + NORM_EPS)
            normed = values * factor
            grad = self.input_grad[rows, :]
            self.gain_total[...] += jnp.sum((grad * normed).reshape(8, 8, 1024), axis=0)
            grad_normed = grad * self.gain_row[0:1, :].astype(jnp.float32)
            mean = jnp.mean(grad_normed * normed, axis=-1, keepdims=True)
            self.input_grad[rows, :] = self.grad_residual[rows, :] + factor * (
                grad_normed - normed * mean
            )
            return 0

        lax.fori_loop(0, 8, rows_of, 0)
        self.gain_lines[...] = jnp.zeros_like(self.gain_lines)
        lines = [jnp.sum(v[...], axis=0, keepdims=True) for v in (self.gain_total, self.gain_grad)]
        for s in range(8):
            for n, line in enumerate(lines):
                self.gain_lines[s // 2, s % 2, n : n + 1] = line[:, 128 * s : 128 * s + 128]


def backward_kernel(items, *refs):
    refs = list(refs)

    def take(n):
        taken = refs[:n]
        del refs[:n]
        return taken

    kept = take(len(KEPT))
    middle_in, grad_gate_in, grad_up_in = take(3)
    saved_in = dict(zip(BACKWARD_IN, take(len(BACKWARD_IN))))
    tokens_in, length = take(2)
    sums = take(7)
    gain_sums, input_grad_out = take(2)
    saved = dict(zip(BACKWARD_IN, take(len(BACKWARD_IN))))
    tokens, input_grad, wide, w_rows, bias, gain_total, gain_lines = take(7)
    mine, from_first, from_second, from_z = (take(len(items)) for _ in range(4))
    ring, tall_ring = take(RING), take(2)
    outbox, tall_outbox = take(2), take(1)
    gain_core, gain_x, gain_y, gain_z = take(4)
    send_sems, recv_sems, load_sems, credit = refs
    z, y, x, c = place()
    far = [lax.rem(z + k, 4) for k in range(4)]
    back = [lax.rem(z + 4 - k, 4) for k in range(4)]
    x_other, y_other, c_other = (
        device(z, y, 1 - x, c),
        device(z, 1 - y, x, c),
        device(z, y, x, 1 - c),
    )
    loads = {}

    def load(name, source, target):
        loads[name] = pltpu.make_async_copy(source, target, load_sems.at[len(loads)])
        loads[name].start()

    waited = set()

    def loaded(*names):
        for name in names:
            if name not in waited:
                loads[name].wait()
                waited.add(name)

    load("grad_gate", grad_gate_in, wide.at[1])
    load("hidden_two_t", saved_in["hidden_two_t"], saved["hidden_two_t"])
    load("middle", middle_in, wide.at[0])
    load("branch", saved_in["branch"], saved["branch"])
    load("out_rows", kept[OUT].reshape(8, 2, 64, 1024), w_rows)
    for name in BACKWARD_IN:
        if name not in loads:
            load(name, saved_in[name], saved[name])
    load("tokens", tokens_in, tokens)
    greet()
    wires = Wires(send_sems, recv_sems)
    work = Backward(
        dict(
            saved,
            tokens=tokens,
            length=length,
            w_rows=w_rows,
            bias=bias,
            input_grad=input_grad,
            gain_total=gain_total,
            gain_lines=gain_lines,
        )
    )
    tall_items = [i for i, item in enumerate(items) if item.tall]
    wide_items = [i for i, item in enumerate(items) if not item.tall]

    def slot(i, k):
        return SUM_SLOTS * i + k

    def core_slots(i):
        return (slot(i, 0), slot(i, 8))

    def from_core(i):
        if items[i].tall:
            return tall_ring[tall_items.index(i)]
        return ring[wide_items.index(i) % RING].at[..., : items[i].width]

    def produce(i):
        item = items[i]
        if item.tall:
            loaded("middle", "branch")
            before = tall_items.index(i) - 1
            if before >= 0:
                wires.finish(lambda s: s in core_slots(tall_items[before]))
            box = tall_outbox[0]
            multiply = partial(work.multiply_tall, wide.at[0], saved["branch"], item)
        else:
            number = wide_items.index(i)
            if number >= 2:
                wires.finish(lambda s: s in core_slots(wide_items[number - 2]))
            box = outbox[number % 2].at[..., : item.width]
            left, right, names = {
                GATE: (saved["hidden_two_t"], wide.at[1], ("hidden_two_t", "grad_gate")),
                UP: (saved["hidden_two_t"], wide.at[0], ("grad_up",)),
                OUT: (saved["attended_t"], saved["grad_proj"], ("attended_t", "grad_proj")),
                QUERY: (saved["hidden_t"], saved["query"], ("hidden_t",)),
                KEY: (saved["hidden_t"], saved["key"], ()),
                VALUE: (saved["hidden_t"], saved["value"], ()),
            }[item.weight]
            loaded(*names)
            multiply = partial(work.multiply, left, right, item)
            if number >= RING:
                pl.semaphore_wait(credit, 1)
        multiply(box, 1 - c)
        for xx in (0, 1):
            wires.send(core_slots(i)[xx], box.at[xx], from_core(i).at[xx], c_other)
        multiply(mine[i], c)
        if i == tall_items[-1]:
            load("grad_up", grad_up_in, wide.at[0])

    def first_hop(i):
        item, own, other = items[i], mine[i], from_core(i)
        for xx in (0, 1):
            wires.arrived(core_slots(i)[xx], other.at[xx])

        def add(at, _):
            for xx in (0, 1):
                for yy in (0, 1):
                    own[xx, at, yy] = plus(own[xx, at, yy], other[xx, at, yy])
            return 0

        lax.fori_loop(0, 4, add, 0)
        if not item.tall and wide_items.index(i) + RING < len(wide_items):
            pl.semaphore_signal(credit, inc=1, device_id=c_other, device_id_type=MESH)
        if item.x_first:
            wires.send(slot(i, 1), own.at[1 - x], from_first[i], x_other)
        else:
            wires.send(slot(i, 1), own.at[:, :, 1 - y], from_first[i], y_other)

    def second_hop(i):
        item, own, other = items[i], mine[i], from_first[i]
        wires.arrived(slot(i, 1), other)

        def add(at, _):
            for side in (0, 1):
                if item.x_first:
                    own[x, at, side] = plus(own[x, at, side], other[at, side])
                else:
                    own[side, at, y] = plus(own[side, at, y], other[side, at])
            return 0

        lax.fori_loop(0, 4, add, 0)
        if item.x_first:
            wires.send(slot(i, 2), own.at[x, :, 1 - y], from_second[i], y_other)
        else:
            to_z(i, lambda k: own.at[:, far[k], y])

    def to_z(i, block):
        for k in (1, 2, 3):
            wires.send(slot(i, 2 + k), block(k), from_z[i].at[k - 1], device(far[k], y, x, c))

    def z_total(i, own_part):
        total = own_part.astype(jnp.float32)
        for k in (1, 2, 3):
            wires.arrived(slot(i, 2 + k), from_z[i].at[k - 1])
            total += from_z[i][k - 1].astype(jnp.float32)
        return total.astype(jnp.bfloat16)

    def third_hop(i):
        item, own, other = items[i], mine[i], from_second[i]
        if not item.x_first:
            own[:, z, y] = z_total(i, own[:, z, y])
            wires.send(slot(i, 2), own.at[:, z, y], other, x_other)
            return
        wires.arrived(slot(i, 2), other)

        def add(at, _):
            own[x, at, y] = plus(own[x, at, y], other[at])
            return 0

        lax.fori_loop(0, 4, add, 0)
        to_z(i, lambda k: own.at[x, far[k], y])

    def fourth_hop(i):
        item, own = items[i], mine[i]
        if not item.x_first:
            wires.arrived(slot(i, 2), from_second[i])
            block = item.half(sums[item.weight], c)
            block[...] = plus(own[:, z, y], from_second[i][...])
            wires.send(slot(i, 7), block, block, c_other)
            return
        block = item.quarter(sums[item.weight], c, x)
        block[...] = z_total(i, own[x, z, y])
        wires.send(slot(i, 6), block, block, x_other)

    def to_sibling(i):
        item = items[i]
        if item.x_first:
            wires.arrived(slot(i, 6), item.quarter(sums[item.weight], c, 1 - x))
            block = item.half(sums[item.weight], c)
            wires.send(slot(i, 7), block, block, c_other)

    def complete(i):
        item = items[i]
        wires.arrived(slot(i, 7), item.half(sums[item.weight], 1 - c))
        wires.finish(lambda s: s // SUM_SLOTS == i)

    base = SUM_SLOTS * len(items)

    def gains_one():
        wires.send(base, gain_lines, gain_core, c_other)

    def gains_two():
        wires.arrived(base, gain_core)
        gain_core[...] = gain_lines[...] + gain_core[...]
        wires.send(base + 1, gain_core, gain_x, x_other)

    def gains_three():
        wires.arrived(base + 1, gain_x)
        gain_x[...] = gain_core[...] + gain_x[...]
        wires.send(base + 2, gain_x.at[:, 1 - y], gain_y, y_other)

    def gains_four():
        wires.arrived(base + 2, gain_y)
        gain_y[...] = gain_x[:, y] + gain_y[...]
        for k in (1, 2, 3):
            wires.send(base + 2 + k, gain_y.at[far[k]], gain_z.at[z], device(far[k], y, x, c))
        gain_z[z] = gain_y[z]

    def gains_five():
        for k in (1, 2, 3):
            wires.arrived(base + 2 + k, gain_z.at[back[k]])
        gain_sums[...] = (gain_z[0] + gain_z[1]) + (gain_z[2] + gain_z[3])

    def fetch_rows(t):
        for n in range(3):
            load(("rows", n, t), kept[n].at[t], w_rows.at[2 * n : 2 * n + 2])

    def attend_back(p):
        if p == 0:
            loaded("query", "key", "value", "log_total", "grad_proj", "out_rows")
        work.attend_back(p, p + 1)
        if p == 7:
            fetch_rows(0)

    def grad_hidden(t):
        loaded(*[("rows", n, t) for n in range(3)])
        work.grad_hidden(t)
        if t < 3:
            fetch_rows(t + 1)

    def finish():
        loaded("tokens", "grad_residual", "gain_grad", "gain_row")
        work.finish()
        load("input_grad", input_grad, input_grad_out)
        gains_one()

    beside = {1: [work.prepare]}
    for p in range(8):
        beside.setdefault(1 + p, []).append(partial(attend_back, p))
    for t in range(4):
        beside.setdefault(9 + t // 2, []).append(partial(grad_hidden, t))
    beside.setdefault(11, []).append(finish)
    for n, task in enumerate((gains_two, gains_three, gains_four, gains_five)):
        beside.setdefault(13 + 2 * n, []).append(task)

    stages = (complete, to_sibling, fourth_hop, third_hop, second_hop, first_hop, produce)
    lates = (12, 10, 8, 6, 4, 2, 0)
    for step in range(len(items) + lates[0]):
        for late, stage in zip(lates, stages):
            if 0 <= step - late < len(items):
                stage(step - late)
        for task in beside.get(step, []):
            task()
    loaded("input_grad")
    wires.finish()


def backward(tokens, lengths, kept, saved):
    items = share_items()
    low, wide = jnp.bfloat16, jnp.float32
    dtypes = {name: (shape, dtype) for name, shape, dtype in FORWARD_OUTS}
    shapes = [
        jax.ShapeDtypeStruct((2, 2, 2, 352, 128) if n is None else (2, 64, n), low) for n in COLUMNS
    ]
    shapes += [jax.ShapeDtypeStruct((8, 128), wide), jax.ShapeDtypeStruct((512, 1024), wide)]
    count = SUM_SLOTS * len(items) + 6
    anywhere = pl.BlockSpec(memory_space=pl.ANY)
    in_vmem = pl.BlockSpec(memory_space=pltpu.VMEM)
    n_loads = 6 + len(BACKWARD_IN) + 12

    def buffers(lead_of):
        return [pltpu.VMEM(lead_of(item) + item.block, low) for item in items]

    out = pl.pallas_call(
        partial(backward_kernel, items),
        out_shape=shapes,
        in_specs=[anywhere] * (len(KEPT) + 3 + len(BACKWARD_IN) + 1)
        + [pl.BlockSpec(memory_space=pltpu.SMEM)],
        out_specs=[in_vmem] * 8 + [anywhere],
        scratch_shapes=[pltpu.VMEM(*dtypes[name]) for name in BACKWARD_IN]
        + [
            pltpu.VMEM((512, 1024), low),
            pltpu.VMEM((512, 1024), wide),
            pltpu.VMEM((2, 512, 2816), low),
            pltpu.VMEM((8, 2, 64, 1024), low),
            pltpu.VMEM((512, 512), wide),
            pltpu.VMEM((8, 1024), wide),
            pltpu.VMEM((4, 2, 8, 128), wide),
        ]
        + buffers(lambda item: (2, 4, 2))
        + buffers(lambda item: (4, 2) if item.x_first else (2, 4))
        + buffers(lambda item: (4,) if item.x_first else (2,))
        + buffers(lambda item: (3,) if item.x_first else (3, 2))
        + [pltpu.VMEM((2, 4, 2, 64, 512), low)] * RING
        + [pltpu.VMEM((2, 4, 2, 352, 128), low)] * 2
        + [pltpu.VMEM((2, 4, 2, 64, 512), low)] * 2
        + [pltpu.VMEM((2, 4, 2, 352, 128), low)]
        + [
            pltpu.VMEM((4, 2, 8, 128), wide),
            pltpu.VMEM((4, 2, 8, 128), wide),
            pltpu.VMEM((4, 8, 128), wide),
            pltpu.VMEM((4, 8, 128), wide),
            pltpu.SemaphoreType.DMA((count,)),
            pltpu.SemaphoreType.DMA((count,)),
            pltpu.SemaphoreType.DMA((n_loads,)),
            pltpu.SemaphoreType.REGULAR,
        ],
        compiler_params=pltpu.CompilerParams(
            collective_id=1, has_side_effects=True, vmem_limit_bytes=62 * MIB
        ),
        name="backward_sum",
    )(
        *kept,
        saved["middle"],
        saved["grad_gate"],
        saved["grad_up"],
        *[saved[name] for name in BACKWARD_IN],
        tokens,
        lengths,
    )
    return out[:7], out[7], out[8]


def unpack_kernel(*refs):
    blocks, (gain_sums, mixed, input_grad) = refs[:7], refs[7:10]
    sums, (gain_attn, gain_ffn, mixed_out, input_out) = refs[10:17], refs[17:21]
    mixed_held, input_held, sems = refs[21:]
    routes = ((mixed, mixed_held, mixed_out), (input_grad, input_held, input_out))
    ins = [pltpu.make_async_copy(a, b, sems.at[n]) for n, (a, b, _) in enumerate(routes)]
    outs = [pltpu.make_async_copy(b, a, sems.at[2 + n]) for n, (_, b, a) in enumerate(routes)]
    for copy in ins:
        copy.start()
    for copy_in, copy_out in zip(ins, outs):
        copy_in.wait()
        copy_out.start()
    for block, total in zip(blocks[:6], sums[:6]):
        total[...] = block[...].astype(jnp.float32)
    for b in range(8):
        sums[6][:, 128 * b : 128 * b + 128] = blocks[6][b // 4, b // 2 % 2, b % 2].astype(
            jnp.float32
        )
    gain_attn[...] = gain_sums[0:1]
    gain_ffn[...] = gain_sums[1:2]
    for copy in outs:
        copy.wait()


def unpack(blocks, gain_sums, mixed, input_grad):
    wide = jnp.float32
    anywhere = pl.BlockSpec(memory_space=pl.ANY)
    in_vmem = pl.BlockSpec(memory_space=pltpu.VMEM)
    shapes = [
        jax.ShapeDtypeStruct((352, 1024) if n is None else (2, 64, n), wide) for n in COLUMNS
    ]
    shapes += [jax.ShapeDtypeStruct((1, 128), wide)] * 2
    shapes += [jax.ShapeDtypeStruct(v.shape, v.dtype) for v in (mixed, input_grad)]
    out = pl.pallas_call(
        unpack_kernel,
        out_shape=shapes,
        in_specs=[in_vmem] * 8 + [anywhere] * 2,
        out_specs=[in_vmem] * 9 + [anywhere] * 2,
        scratch_shapes=[
            pltpu.VMEM(mixed.shape, mixed.dtype),
            pltpu.VMEM(input_grad.shape, input_grad.dtype),
            pltpu.SemaphoreType.DMA((4,)),
        ],
        compiler_params=pltpu.CompilerParams(vmem_limit_bytes=62 * MIB),
        name="unpack",
    )(*blocks, gain_sums, mixed, input_grad)
    sums = [s.reshape(-1, s.shape[-1]) for s in out[:7]]
    return sums, [g.reshape(128) for g in out[7:9]], out[9], out[10]


def gather_plain(weights, gains):
    everything = (*weights, *gains)
    whole = [lax.all_gather(v, "dp", axis=0, tiled=True) for v in everything]
    return whole[: len(weights)], whole[len(weights) :]


def sum_plain(grads, gain_grads):
    shares = [
        lax.psum_scatter(g.astype(jnp.float32), "dp", scatter_dimension=0, tiled=True)
        for g in (*grads, *gain_grads)
    ]
    sums = [lax.psum(s, ("rep", "cores")) for s in shares]
    return sums[: len(grads)], sums[len(grads) :]


def on_any_device(
    tokens,
    norm_attn,
    w_query,
    w_key,
    w_value,
    w_out,
    norm_ffn,
    w_gate,
    w_up,
    w_down,
    lengths,
    cotangent,
):
    rows = tokens.shape[0]
    low = jnp.bfloat16
    allowed, valid = masks(lengths, rows)
    whole, gains = gather_plain(
        (w_query, w_key, w_value, w_out, w_gate, w_up, w_down), (norm_attn, norm_ffn)
    )
    full_query, full_key, full_value, full_out, full_gate, full_up, full_down = whole
    gain_attn, gain_ffn = gains
    inputs = tokens.astype(jnp.float32)
    normed, factor = normalize(inputs)
    hidden = (normed * gain_attn.astype(jnp.float32)).astype(low)
    query = matmul(hidden, full_query).astype(low)
    keyed = matmul(hidden, full_key).astype(low)
    valued = matmul(hidden, full_value).astype(low)
    query_groups, key_groups, value_groups = (to_groups(query), to_groups(keyed), to_groups(valued))
    attended_groups, log_total = lax.map(
        partial(attend, allowed), (query_groups, key_groups, value_groups)
    )
    attended = from_groups(attended_groups)
    residual = inputs + matmul(attended, full_out)
    normed_two, factor_two = normalize(residual)
    hidden_two = (normed_two * gain_ffn.astype(jnp.float32)).astype(low)
    gate = matmul(hidden_two, full_gate)
    upward = matmul(hidden_two, full_up)
    sigma = jax.nn.sigmoid(gate)
    middle = (gate * sigma * upward).astype(low)
    mixed = (valid[:, None] * (residual + matmul(middle, full_down))).astype(low)
    grad_output = cotangent.astype(jnp.float32) * valid[:, None]
    grad_branch = grad_output.astype(low)
    grad_down = matmul_tn(middle, grad_branch)
    grad_middle = matmul_nt(grad_branch, full_down)
    grad_gate_rows = (grad_middle * upward * sigma * (1.0 + gate * (1.0 - sigma))).astype(low)
    grad_up_rows = (grad_middle * gate * sigma).astype(low)
    grad_gate = matmul_tn(hidden_two, grad_gate_rows)
    grad_up = matmul_tn(hidden_two, grad_up_rows)
    grad_hidden_two = matmul_nt(grad_gate_rows, full_gate) + matmul_nt(grad_up_rows, full_up)
    grad_gain_ffn = jnp.sum(grad_hidden_two * normed_two, axis=0)
    grad_residual = grad_output + norm_back(
        grad_hidden_two * gain_ffn.astype(jnp.float32), normed_two, factor_two
    )
    grad_proj = grad_residual.astype(low)
    grad_out = matmul_tn(attended, grad_proj)
    grad_attended = matmul_nt(grad_proj, full_out).astype(low)
    grad_query_g, grad_key_g, grad_value_g = lax.map(
        partial(attend_back, allowed),
        (query_groups, key_groups, value_groups, to_groups(grad_attended), log_total),
    )
    grad_query_rows = from_groups(grad_query_g)
    grad_key_rows = from_groups(grad_key_g)
    grad_value_rows = from_groups(grad_value_g)
    grad_query = matmul_tn(hidden, grad_query_rows)
    grad_key = matmul_tn(hidden, grad_key_rows)
    grad_value = matmul_tn(hidden, grad_value_rows)
    grad_hidden = (
        matmul_nt(grad_query_rows, full_query)
        + matmul_nt(grad_key_rows, full_key)
        + matmul_nt(grad_value_rows, full_value)
    )
    grad_gain_attn = jnp.sum(grad_hidden * normed, axis=0)
    input_grad = grad_residual + norm_back(
        grad_hidden * gain_attn.astype(jnp.float32), normed, factor
    )
    grads = (grad_query, grad_key, grad_value, grad_out, grad_gate, grad_up, grad_down)
    sums, gain_sums = sum_plain([g.astype(low) for g in grads], (grad_gain_attn, grad_gain_ffn))
    return (
        mixed,
        input_grad,
        gain_sums[0],
        sums[0],
        sums[1],
        sums[2],
        sums[3],
        gain_sums[1],
        sums[4],
        sums[5],
        sums[6],
    )


def on_tuned_device(
    tokens,
    norm_attn,
    w_query,
    w_key,
    w_value,
    w_out,
    norm_ffn,
    w_gate,
    w_up,
    w_down,
    lengths,
    cotangent,
):
    weights = (w_query, w_key, w_value, w_out, w_gate, w_up, w_down)
    kept, saved = forward(tokens, cotangent, lengths, weights, (norm_attn, norm_ffn))
    blocks, gain_lines, input_grad = backward(tokens, lengths, kept, saved)
    sums, gain_sums, mixed, input_grad = unpack(blocks, gain_lines, saved["mixed"], input_grad)
    return (
        mixed,
        input_grad,
        gain_sums[0],
        *sums[:4],
        gain_sums[1],
        *sums[4:],
    )


def solution(mesh):
    tuned = dict(mesh.shape) == {"dp": 8, "rep": 2, "cores": 2}
    tokens_placed = P(("dp", "rep", "cores"), None)
    share, gain = P("dp", None), P("dp")
    return jax.shard_map(
        on_tuned_device if tuned else on_any_device,
        mesh=mesh,
        in_specs=(
            tokens_placed,
            gain,
            share,
            share,
            share,
            share,
            gain,
            share,
            share,
            share,
            tokens_placed,
            tokens_placed,
        ),
        out_specs=(
            tokens_placed,
            tokens_placed,
            gain,
            share,
            share,
            share,
            share,
            gain,
            share,
            share,
            share,
        ),
        check_vma=False,
    )
```

```python
from functools import partial

import jax
import jax.numpy as jnp
from jax import lax
from jax.experimental import pallas as pl
from jax.experimental.pallas import tpu as pltpu
from jax.sharding import PartitionSpec as P

HEADS = 16
HEAD = 64


NORM_EPS = 1e-05
SCORE_SCALE = 0.125
NEGATIVE = -1e30
head_group = 4
MESH = pl.DeviceIdType.MESH
MIB = 1024 * 1024


def masks(block_len, rows):
    bounds = jnp.cumsum(block_len[0])
    place = jnp.arange(rows, dtype=jnp.int32)
    segment = jnp.sum((place[:, None] >= bounds[None, :]).astype(jnp.int32), axis=1)
    allowed = (segment[:, None] == segment[None, :]) & (place[None, :] <= place[:, None])
    valid = (segment < block_len.shape[1]).astype(jnp.float32)
    return (allowed, valid)


def normalize(values):
    factor = lax.rsqrt(jnp.mean(values * values, axis=-1, keepdims=True) + NORM_EPS)
    return (values * factor, factor)


def norm_back(grad_normed, normed, factor):
    return factor * (grad_normed - normed * jnp.mean(grad_normed * normed, axis=-1, keepdims=True))


def matmul(left, right):
    return jnp.dot(left, right, preferred_element_type=jnp.float32)


def matmul_tn(left, right):
    return lax.dot_general(
        left, right, (((0,), (0,)), ((), ())), preferred_element_type=jnp.float32
    )


def matmul_nt(left, right):
    return lax.dot_general(
        left, right, (((1,), (1,)), ((), ())), preferred_element_type=jnp.float32
    )


def to_groups(matrix):
    rows = matrix.shape[0]
    split = matrix.reshape(rows, HEADS // head_group, head_group, HEAD)
    return split.transpose(1, 2, 0, 3)


def from_groups(grouped):
    rows = grouped.shape[2]
    return grouped.transpose(2, 0, 1, 3).reshape(rows, HEADS * HEAD)


def group_scores(allowed, query_g, key_g):
    raw = (
        jnp.einsum("hqe,hke->hqk", query_g, key_g, preferred_element_type=jnp.float32) * SCORE_SCALE
    )
    return jnp.where(allowed[None], raw, NEGATIVE)


def attend(allowed, operands):
    query_g, key_g, value_g = operands
    scores = group_scores(allowed, query_g, key_g)
    top = jnp.max(scores, axis=-1, keepdims=True)
    expo = jnp.exp(scores - top)
    total = jnp.sum(expo, axis=-1, keepdims=True)
    probs_low = (expo / total).astype(jnp.bfloat16)
    result = jnp.einsum("hqk,hke->hqe", probs_low, value_g, preferred_element_type=jnp.float32)
    return (result.astype(jnp.bfloat16), top[..., 0] + jnp.log(total[..., 0]))


def attend_back(allowed, operands):
    query_g, key_g, value_g, grad_g, log_total = operands
    scores = group_scores(allowed, query_g, key_g)
    probs = jnp.exp(scores - log_total[..., None])
    grad_probs = jnp.einsum("hqe,hke->hqk", grad_g, value_g, preferred_element_type=jnp.float32)
    centre = jnp.sum(grad_probs * probs, axis=-1, keepdims=True)
    grad_scores = (probs * (grad_probs - centre)).astype(jnp.bfloat16)
    grad_query = (
        jnp.einsum("hqk,hke->hqe", grad_scores, key_g, preferred_element_type=jnp.float32)
        * SCORE_SCALE
    )
    grad_key = (
        jnp.einsum("hqk,hqe->hke", grad_scores, query_g, preferred_element_type=jnp.float32)
        * SCORE_SCALE
    )
    grad_value = jnp.einsum(
        "hqk,hqe->hke", probs.astype(jnp.bfloat16), grad_g, preferred_element_type=jnp.float32
    )
    return (
        grad_query.astype(jnp.bfloat16),
        grad_key.astype(jnp.bfloat16),
        grad_value.astype(jnp.bfloat16),
    )


class Part:
    def __init__(self, weight, tall, start, size, no_x):
        self.weight, self.tall, self.start, self.size = weight, tall, start, size
        self.no_x = no_x

    def quarter(self, ref, lead, c, x):
        if self.tall:
            columns = pl.ds(pl.multiple_of(c * 512 + x * 256, 256), 256)
            return ref.at[(*lead, pl.ds(self.start, self.size), columns)]
        return ref.at[(*lead, x, slice(None), self.columns(c))]

    def half(self, ref, lead, c):
        if self.tall:
            columns = pl.ds(pl.multiple_of(c * 512, 512), 512)
            return ref.at[(*lead, pl.ds(self.start, self.size), columns)]
        return ref.at[(*lead, slice(None), slice(None), self.columns(c))]

    def columns(self, c):
        width = self.size // 2
        return pl.ds(pl.multiple_of(self.start + c * width, 128), width)


def pieces(total, most):
    return [(start, min(most, total - start)) for start in range(0, total, most)]


def place():
    d = lax.axis_index("dp")
    return lax.div(d, 2), lax.rem(d, 2), lax.axis_index("rep"), lax.axis_index("cores")


def device(z, y, x, c):
    return {"dp": 2 * z + y, "rep": x, "cores": c}


def greet():
    z, y, x, c = place()
    barrier = pltpu.get_barrier_semaphore()
    others = [device(lax.rem(z + k, 4), y, x, c) for k in (1, 2, 3)]
    others += [device(z, 1 - y, x, c), device(z, y, 1 - x, c), device(z, y, x, 1 - c)]
    for other in others:
        pl.semaphore_signal(barrier, inc=1, device_id=other, device_id_type=MESH)
    pl.semaphore_wait(barrier, len(others))


class Wires:
    def __init__(self, send_sems, recv_sems):
        self.send_sems, self.recv_sems, self.sent = send_sems, recv_sems, []

    def copy(self, slot, source, target, other):
        return pltpu.make_async_remote_copy(
            src_ref=source,
            dst_ref=target,
            send_sem=self.send_sems.at[slot],
            recv_sem=self.recv_sems.at[slot],
            device_id=other,
            device_id_type=MESH,
        )

    def send(self, slot, source, target, other):
        copy = self.copy(slot, source, target, other)
        copy.start()
        self.sent.append((slot, copy))

    def arrived(self, slot, target):
        z, y, x, c = place()
        self.copy(slot, target, target, device(z, y, x, 1 - c)).wait_recv()

    def finish(self, chosen=lambda slot: True):
        for slot, copy in self.sent:
            if chosen(slot):
                copy.wait_send()
        self.sent = [(slot, copy) for slot, copy in self.sent if not chosen(slot)]


GATHER_SLOTS = 12
LAG = 2
ALL = slice(None)
COLUMNS = (1024, 1024, 1024, 1024, 2816, 2816, None)
QUERY, KEY, VALUE, OUT, GATE, UP, DOWN = range(7)
TILE = 256
FF_TILE = 256


FF_CHUNKS = ((0, 512), (512, 768), (1280, 768), (2048, 512), (2560, 256))


def gather_items():
    order = [(QUERY, 0, 256, True), (QUERY, 256, 768, False), (KEY, 0, 1024, True)]
    order += [(VALUE, 0, 1024, False), (OUT, 0, 1024, False)]
    order += [(DOWN, 0, 128, False), (DOWN, 128, 128, True), (DOWN, 256, 96, False)]
    for n, (start, size) in enumerate(FF_CHUNKS):
        order += [(GATE, start, size, n == 4), (UP, start, size, n in (1, 4))]
    return [Part(w, w == DOWN, start, size, no_x) for w, start, size, no_x in order]


def dot(left, right):
    return lax.dot_general(
        left, right, (((1,), (0,)), ((), ())), preferred_element_type=jnp.float32
    )


def dot_nt(left, right):
    return lax.dot_general(
        left, right, (((1,), (1,)), ((), ())), preferred_element_type=jnp.float32
    )


def tile(index, size):
    return pl.ds(pl.multiple_of(index * size, size), size)


def weight_columns(ref, at):
    return ref[:, :, :, :, at].reshape(1024, -1)


class Forward:
    def __init__(self, refs):
        self.__dict__.update(refs)

    def prepare(self):
        for s in range(8):
            self.gain_row[:, 128 * s : 128 * s + 128] = self.gains[s // 2, s % 2]
        length = self.length[0, 0]
        for block in range(4):
            rows = slice(128 * block, 128 * block + 128)
            place_q = lax.broadcasted_iota(jnp.int32, (128, 512), 0) + 128 * block
            place_k = lax.broadcasted_iota(jnp.int32, (128, 512), 1)
            same = (place_q >= length) == (place_k >= length)
            allowed = same & (place_k <= place_q)
            self.bias[rows, :] = jnp.where(allowed, 0.0, NEGATIVE)

        def normed(block, _):
            rows = tile(block, 64)
            values = self.tokens[rows, :].astype(jnp.float32)
            factor = lax.rsqrt(jnp.mean(values * values, axis=-1, keepdims=True) + NORM_EPS)
            gain = self.gain_row[0:1, :].astype(jnp.float32)
            self.hidden[rows, :] = (values * factor * gain).astype(jnp.bfloat16)
            place = lax.broadcasted_iota(jnp.int32, (64, 1024), 0) + 64 * block
            branch = jnp.where(place < length, self.cotangent[rows, :].astype(jnp.float32), 0.0)
            self.branch[rows, :] = branch.astype(jnp.bfloat16)
            return 0

        lax.fori_loop(0, 8, normed, 0)
        self.turn(self.hidden, self.hidden_t)
        self.out("branch")

    def turn(self, matrix, turned):
        def columns(n, _):
            at = tile(n, 128)
            turned[at, :] = matrix[:, at].astype(jnp.float32).T.astype(jnp.bfloat16)
            return 0

        lax.fori_loop(0, 8, columns, 0)

    def project(self, weight, result):
        def columns(n, _):
            at = tile(n, TILE)
            result[:, at] = dot(self.hidden[...], weight_columns(weight, at)).astype(jnp.bfloat16)
            return 0

        lax.fori_loop(0, 1024 // TILE, columns, 0)

    def attend(self, first, last):
        def pair(p, _):
            at = tile(p, 128)
            left = lax.broadcasted_iota(jnp.int32, (256, 128), 1) < HEAD
            for block in (0, 1):
                rows, seen = slice(256 * block, 256 * block + 256), slice(0, 256 * block + 256)
                query = self.query[rows, at].astype(jnp.float32) * SCORE_SCALE
                outs = []
                for n, side in enumerate((left, ~left)):
                    own = jnp.where(side, query, 0.0).astype(jnp.bfloat16)
                    self.scores[:, seen] = dot_nt(own, self.key[seen, at])
                    self.softmax(block, n, seen)
                    outs.append(dot(self.probs[:, seen], self.value[seen, at]))
                self.attended[rows, at] = jnp.where(left, outs[0], outs[1]).astype(jnp.bfloat16)
                turned = self.totals[...].T
                self.log_total[p, 0:1, rows] = turned[0:1]
                self.log_total[p, 1:2, rows] = turned[HEAD : HEAD + 1]
            return 0

        lax.fori_loop(first, last, pair, 0)

    def softmax(self, block, n, seen):
        def rows_of(r, _):
            rows = tile(r, 32)
            biased = pl.ds(pl.multiple_of(256 * block + 32 * r, 32), 32)
            scores = self.scores[rows, seen] + self.bias[biased, seen]
            top = jnp.max(scores, axis=-1, keepdims=True)
            expo = jnp.exp(scores - top)
            total = jnp.sum(expo, axis=-1, keepdims=True)
            self.probs[rows, seen] = (expo * (1.0 / total)).astype(jnp.bfloat16)
            lanes = slice(HEAD * n, HEAD * n + HEAD)
            self.totals[rows, lanes] = jnp.broadcast_to(top + jnp.log(total), (32, HEAD))
            return 0

        lax.fori_loop(0, 8, rows_of, 0, unroll=2)

    def project_out(self):
        def columns(n, _):
            at = tile(n, TILE)
            self.residual[:, at] = self.tokens[:, at].astype(jnp.float32) + dot(
                self.attended[...], weight_columns(self.w_out, at)
            )
            return 0

        lax.fori_loop(0, 1024 // TILE, columns, 0)

        def normed(block, _):
            rows = tile(block, 64)
            values = self.residual[rows, :]
            factor = lax.rsqrt(jnp.mean(values * values, axis=-1, keepdims=True) + NORM_EPS)
            gain = self.gain_row[8:9, :].astype(jnp.float32)
            self.hidden_two[rows, :] = (values * factor * gain).astype(jnp.bfloat16)
            return 0

        lax.fori_loop(0, 8, normed, 0)
        self.turn(self.hidden_two, self.hidden_two_t)
        self.turn(self.attended, self.attended_t)
        for name in ("query", "key", "value", "log_total", "hidden_t", "hidden_two_t", "attended_t"):
            self.out(name)

    def grad_of_middle(self, first, last):
        def columns(n, _):
            at = tile(n, FF_TILE)
            grad = dot_nt(self.branch[...], self.w_down[at, :])
            self.grad_up[:, at] = grad.astype(jnp.bfloat16)
            return 0

        lax.fori_loop(first, last, columns, 0)

    def feed_forward(self, first, last):
        def columns(n, first_of_all):
            at = tile(n, FF_TILE)
            low = jnp.bfloat16
            gate_w = weight_columns(self.w_gate, at)
            up_w = weight_columns(self.w_up, at)
            down_w = self.w_down[at, :]
            self.gate[...] = dot(self.hidden_two[...], gate_w)
            self.upward[...] = dot(self.hidden_two[...], up_w)

            def rows_of(r, _):
                rows = tile(r, 32)
                gate, upward = self.gate[rows, :], self.upward[rows, :]
                grad_middle = self.grad_up[rows, at].astype(jnp.float32)
                sigma = 1.0 / (1.0 + jnp.exp(-gate))
                silu = gate * sigma
                self.middle[rows, at] = (silu * upward).astype(low)
                self.grad_up[rows, at] = (grad_middle * silu).astype(low)
                self.grad_gate[rows, at] = (
                    grad_middle * upward * sigma * (1.0 + gate * (1.0 - sigma))
                ).astype(low)
                return 0

            lax.fori_loop(0, 16, rows_of, 0, unroll=2)
            middle = self.middle[:, at]
            grad_gate, grad_up = self.grad_gate[:, at], self.grad_up[:, at]
            for j in range(4):
                part = slice(256 * j, 256 * j + 256)
                mixed = dot(middle, down_w[:, part])
                grad = dot_nt(grad_gate, gate_w[part, :]) + dot_nt(grad_up, up_w[part, :])
                if first_of_all is True:
                    self.total[:, part] = mixed
                    self.grad_hidden_two[:, part] = grad
                else:
                    self.total[:, part] += mixed
                    self.grad_hidden_two[:, part] += grad
            return 0

        if first == 0:
            columns(0, True)
            first = 1
        lax.fori_loop(first, last, lambda n, _: columns(n, False), 0)

    def flush(self, start, size):
        for name in ("middle", "grad_gate", "grad_up"):
            self.out(name, pl.ds(start, size))

    def finish(self):
        length = self.length[0, 0]
        self.gain_grad[...] = jnp.zeros_like(self.gain_grad)

        def rows_of(block, _):
            rows = tile(block, 64)
            place = lax.broadcasted_iota(jnp.int32, (64, 1024), 0) + 64 * block
            residual = self.residual[rows, :]
            mixed = jnp.where(place < length, residual + self.total[rows, :], 0.0)
            self.mixed[rows, :] = mixed.astype(jnp.bfloat16)
            factor = lax.rsqrt(jnp.mean(residual * residual, axis=-1, keepdims=True) + NORM_EPS)
            normed = residual * factor
            grad = self.grad_hidden_two[rows, :]
            self.gain_grad[...] += jnp.sum((grad * normed).reshape(8, 8, 1024), axis=0)
            grad_normed = grad * self.gain_row[8:9, :].astype(jnp.float32)
            grad_out = jnp.where(place < length, self.cotangent[rows, :].astype(jnp.float32), 0.0)
            mean = jnp.mean(grad_normed * normed, axis=-1, keepdims=True)
            grad_residual = grad_out + factor * (grad_normed - normed * mean)
            self.grad_residual[rows, :] = grad_residual
            self.grad_proj[rows, :] = grad_residual.astype(jnp.bfloat16)
            return 0

        lax.fori_loop(0, 8, rows_of, 0)
        for name in ("mixed", "grad_residual", "grad_proj", "gain_grad", "gain_row"):
            self.out(name)


FORWARD_OUTS = (
    ("mixed", (512, 1024), jnp.bfloat16),
    ("query", (512, 1024), jnp.bfloat16),
    ("key", (512, 1024), jnp.bfloat16),
    ("value", (512, 1024), jnp.bfloat16),
    ("log_total", (8, 8, 512), jnp.float32),
    ("hidden_t", (1024, 512), jnp.bfloat16),
    ("hidden_two_t", (1024, 512), jnp.bfloat16),
    ("attended_t", (1024, 512), jnp.bfloat16),
    ("branch", (512, 1024), jnp.bfloat16),
    ("middle", (512, 2816), jnp.bfloat16),
    ("grad_gate", (512, 2816), jnp.bfloat16),
    ("grad_up", (512, 2816), jnp.bfloat16),
    ("grad_residual", (512, 1024), jnp.float32),
    ("grad_proj", (512, 1024), jnp.bfloat16),
    ("gain_grad", (8, 1024), jnp.float32),
    ("gain_row", (16, 1024), jnp.bfloat16),
)
FORWARD_OWN = (
    ("hidden", (512, 1024), jnp.bfloat16),
    ("attended", (512, 1024), jnp.bfloat16),
    ("residual", (512, 1024), jnp.float32),
    ("hidden_two", (512, 1024), jnp.bfloat16),
    ("grad_hidden_two", (512, 1024), jnp.float32),
    ("bias", (512, 512), jnp.float32),
    ("total", (512, 1024), jnp.float32),
    ("scores", (256, 512), jnp.float32),
    ("probs", (256, 512), jnp.bfloat16),
    ("totals", (256, 128), jnp.float32),
    ("gate", (512, 256), jnp.float32),
    ("upward", (512, 256), jnp.float32),
)
OUT_COPIES = len(FORWARD_OUTS) - 3 + 3 * len(FF_CHUNKS)
KEPT = (QUERY, KEY, VALUE, OUT)


def share_shape(columns):
    return (352, 1024) if columns is None else (2, 64, columns)


def forward_kernel(items, *refs):
    refs = list(refs)

    def take(n):
        taken = refs[:n]
        del refs[:n]
        return taken

    shares = take(7)
    gain_attn, gain_ffn, tokens, cotangent, length = take(5)
    kept = take(len(KEPT))
    names = [name for name, _, _ in FORWARD_OUTS]
    outs = dict(zip(names, take(len(names))))
    full = take(7)
    full_gains, gains = take(2)
    own_names = names + [name for name, _, _ in FORWARD_OWN]
    state = dict(zip(own_names, take(len(own_names))))
    send_sems, recv_sems, own_sems, keep_sems, out_sems = refs
    outgoing = []

    def put(name, columns=None):
        source, target = state[name], outs[name]
        if columns is not None:
            source, target = source.at[:, columns], target.at[:, columns]
        outgoing.append(pltpu.make_async_copy(source, target, out_sems.at[len(outgoing)]))
        outgoing[-1].start()

    z, y, x, c = place()
    far = [lax.rem(z + k, 4) for k in range(4)]
    back = [lax.rem(z + 4 - k, 4) for k in range(4)]
    x_other, y_other, c_other = (
        device(z, y, 1 - x, c),
        device(z, 1 - y, x, c),
        device(z, y, x, 1 - c),
    )
    greet()
    wires = Wires(send_sems, recv_sems)
    own = [
        pltpu.make_async_copy(share, whole.at[z, y], own_sems.at[i])
        for i, (share, whole) in enumerate(zip(shares, full))
    ]
    own_gains = pltpu.make_async_copy(gains, full_gains.at[z, y], own_sems.at[7])
    keep = [
        pltpu.make_async_copy(full[w], kept[n], keep_sems.at[n]) for n, w in enumerate(KEPT)
    ]
    gains[...] = jnp.where(
        lax.broadcasted_iota(jnp.int32, (16, 128), 0) < 8,
        jnp.broadcast_to(gain_attn[...].astype(jnp.float32), (16, 128)),
        jnp.broadcast_to(gain_ffn[...].astype(jnp.float32), (16, 128)),
    ).astype(jnp.bfloat16)
    own_gains.start()
    gain_slot = GATHER_SLOTS * len(items)
    for k in (1, 2, 3):
        wires.send(gain_slot + k, gains, full_gains.at[z, y], device(far[k], y, x, c))
    for copy in own:
        copy.start()

    def slot(i, k):
        return GATHER_SLOTS * i + k

    def along_z(i):
        item = items[i]
        share, whole = shares[item.weight], full[item.weight]
        for k in (1, 2, 3):
            if item.no_x:
                source, target = item.half(share, (), c), item.half(whole, (z, y), c)
            else:
                source, target = item.quarter(share, (), c, x), item.quarter(whole, (z, y), c, x)
            wires.send(slot(i, k), source, target, device(far[k], y, x, c))

    own_done = set()

    def first_hop(i):
        item = items[i]
        whole = full[item.weight]
        if item.weight not in own_done:
            own[item.weight].wait()
            own_done.add(item.weight)
        for k in (1, 2, 3):
            if item.no_x:
                block = item.half(whole, (back[k], y), c)
                wires.arrived(slot(i, k), block)
                wires.send(slot(i, 7 + k), block, block, c_other)
            else:
                block = item.quarter(whole, (back[k], y), c, x)
                wires.arrived(slot(i, k), block)
                wires.send(slot(i, 3 + k), block, block, x_other)
        if item.no_x:
            block = item.half(whole, (ALL, y), c)
        else:
            block = item.quarter(whole, (ALL, y), c, x)
        wires.send(slot(i, 7), block, block, y_other)

    def second_hop(i):
        item = items[i]
        whole = full[item.weight]
        if item.no_x:
            block = item.half(whole, (ALL, 1 - y), c)
            wires.arrived(slot(i, 7), block)
            wires.send(slot(i, 11), block, block, c_other)
            return
        block = item.quarter(whole, (ALL, 1 - y), c, x)
        wires.arrived(slot(i, 7), block)
        wires.send(slot(i, 0), block, block, x_other)
        for k in (1, 2, 3):
            wires.arrived(slot(i, 3 + k), item.quarter(whole, (back[k], y), c, 1 - x))
        for k in (1, 2, 3):
            block = item.half(whole, (back[k], y), c)
            wires.send(slot(i, 7 + k), block, block, c_other)

    def last_hop(i):
        item = items[i]
        whole = full[item.weight]
        if not item.no_x:
            block = item.half(whole, (ALL, 1 - y), c)
            wires.arrived(slot(i, 0), item.quarter(whole, (ALL, 1 - y), c, 1 - x))
            wires.send(slot(i, 11), block, block, c_other)

    def complete(i):
        item = items[i]
        whole = full[item.weight]
        for k in (1, 2, 3):
            wires.arrived(slot(i, 7 + k), item.half(whole, (back[k], y), 1 - c))
        wires.arrived(slot(i, 11), item.half(whole, (ALL, 1 - y), 1 - c))

    def retire(i):
        wires.finish(lambda slot: slot // GATHER_SLOTS == i)

    step_of = Forward(
        dict(
            state,
            out=put,
            tokens=tokens,
            cotangent=cotangent,
            length=length,
            gains=full_gains,
            w_out=full[OUT],
            w_gate=full[GATE],
            w_up=full[UP],
            w_down=full[DOWN].reshape(2816, 1024),
        )
    )
    last_of = {item.weight: i for i, item in enumerate(items)}
    tasks = [(-1, 3, step_of.prepare)]
    for n, name in enumerate(("query", "key", "value")):
        tasks.append((last_of[n], 2, partial(step_of.project, full[n], state[name])))
    tasks += [(last_of[VALUE], 3, partial(step_of.attend, p, p + 2)) for p in (0, 2, 4, 6)]
    tasks.append((last_of[OUT], 3, step_of.project_out))
    for n in range(0, 11, 4):
        tasks.append((last_of[DOWN], 3, partial(step_of.grad_of_middle, n, min(n + 4, 11))))
    for start, size in FF_CHUNKS:
        there = max(
            i for i, item in enumerate(items) if item.weight == UP and item.start == start
        )
        for n in range(start // FF_TILE, (start + size) // FF_TILE):
            tasks.append((there, 3, partial(step_of.feed_forward, n, n + 1)))
        tasks.append((there, 0, partial(step_of.flush, start, size)))

    ahead = 3
    for i in range(min(ahead, len(items))):
        along_z(i)
    own_gains.wait()
    for k in (1, 2, 3):
        wires.arrived(gain_slot + k, full_gains.at[back[k], y])
    wires.send(gain_slot, full_gains.at[:, y], full_gains.at[:, y], y_other)
    stages = (retire, complete, last_hop, second_hop, first_hop)
    lates = (3 * LAG, 3 * LAG - 1, 2 * LAG, LAG, 0)
    for step in range(len(items) + 3 * LAG):
        for late, stage in zip(lates, stages):
            if 0 <= step - late < len(items):
                stage(step - late)
        if step + ahead < len(items):
            along_z(step + ahead)
        if step == 0:
            wires.arrived(gain_slot, full_gains.at[:, 1 - y])
        there = step - lates[1]
        for n, w in enumerate(KEPT):
            if there == last_of[w]:
                keep[n].start()
        spent = 0
        while tasks and tasks[0][0] <= there and spent < 6:
            _, cost, task = tasks.pop(0)
            task()
            spent += cost
    for _, _, task in tasks:
        task()
    step_of.finish()
    for copy in keep + outgoing:
        copy.wait()
    wires.finish()


def forward(tokens, cotangent, lengths, weights, gains):
    items = gather_items()
    shares = [w.reshape(share_shape(n)) for w, n in zip(weights, COLUMNS)]
    wholes = [(4, 2) + share_shape(n) for n in COLUMNS]
    shapes = [jax.ShapeDtypeStruct(wholes[w], jnp.bfloat16) for w in KEPT]
    shapes += [jax.ShapeDtypeStruct(shape, dtype) for _, shape, dtype in FORWARD_OUTS]
    count = GATHER_SLOTS * len(items) + 4
    anywhere = pl.BlockSpec(memory_space=pl.ANY)
    in_vmem = pl.BlockSpec(memory_space=pltpu.VMEM)
    out = pl.pallas_call(
        partial(forward_kernel, items),
        out_shape=shapes,
        in_specs=[anywhere] * 7
        + [in_vmem] * 4
        + [pl.BlockSpec(memory_space=pltpu.SMEM)],
        out_specs=[anywhere] * len(shapes),
        scratch_shapes=[pltpu.VMEM(shape, jnp.bfloat16) for shape in wholes]
        + [pltpu.VMEM((4, 2, 16, 128), jnp.bfloat16), pltpu.VMEM((16, 128), jnp.bfloat16)]
        + [pltpu.VMEM(shape, dtype) for _, shape, dtype in FORWARD_OUTS + FORWARD_OWN]
        + [
            pltpu.SemaphoreType.DMA((count,)),
            pltpu.SemaphoreType.DMA((count,)),
            pltpu.SemaphoreType.DMA((8,)),
            pltpu.SemaphoreType.DMA((len(KEPT),)),
            pltpu.SemaphoreType.DMA((OUT_COPIES,)),
        ],
        compiler_params=pltpu.CompilerParams(
            collective_id=0, has_side_effects=True, vmem_limit_bytes=62 * MIB
        ),
        name="gather_forward",
    )(*shares, *[g.reshape(1, 128) for g in gains], tokens, cotangent, lengths)
    return out[: len(KEPT)], dict(zip([name for name, _, _ in FORWARD_OUTS], out[len(KEPT) :]))


SUM_SLOTS = 10
RING = 4


class Share:
    def __init__(self, weight, start, size, x_first):
        self.weight, self.start, self.size, self.x_first = weight, start, size, x_first
        self.tall = weight == DOWN
        self.width = 128 if self.tall else size // 2
        self.block = (352 if self.tall else 64, self.width)

    def columns(self, c, x):
        start = c * 512 + x * 256 + self.start if self.tall else self.start + c * self.width
        return pl.ds(pl.multiple_of(start, 128), self.width)

    def quarter(self, sums, c, x):
        if self.tall:
            return sums.at[c, x, self.start // 128]
        return sums.at[x, :, self.columns(c, x)]

    def half(self, sums, c):
        if self.tall:
            return sums.at[c, :, self.start // 128]
        return sums.at[:, :, self.columns(c, 0)]


def share_items():
    order = [(GATE, 2048, 768, True), (DOWN, 0, 128, False), (DOWN, 128, 128, True)]
    order += [(GATE, 0, 1024, False), (GATE, 1024, 1024, True)]
    order += [(UP, 0, 1024, True), (UP, 1024, 1024, False), (UP, 2048, 768, False)]
    order += [(OUT, 0, 1024, True), (QUERY, 0, 1024, False), (KEY, 0, 1024, True)]
    order += [(VALUE, 0, 768, True), (VALUE, 768, 256, False)]
    return [Share(*item) for item in order]


def plus(left, right):
    return left + right


def dot_tn(left, right):
    return lax.dot_general(
        left, right, (((0,), (0,)), ((), ())), preferred_element_type=jnp.float32
    )


BACKWARD_IN = (
    "query",
    "key",
    "value",
    "log_total",
    "hidden_t",
    "hidden_two_t",
    "attended_t",
    "branch",
    "grad_residual",
    "grad_proj",
    "gain_grad",
    "gain_row",
)


class Backward:
    def __init__(self, refs):
        self.__dict__.update(refs)

    def prepare(self):
        length = self.length[0, 0]
        for block in range(4):
            rows = slice(128 * block, 128 * block + 128)
            place_k = lax.broadcasted_iota(jnp.int32, (128, 512), 0) + 128 * block
            place_q = lax.broadcasted_iota(jnp.int32, (128, 512), 1)
            same = (place_q >= length) == (place_k >= length)
            allowed = same & (place_k <= place_q)
            self.bias[rows, :] = jnp.where(allowed, 0.0, NEGATIVE)

    def multiply(self, left_t, right, item, target, core):
        columns = item.columns(core, 0)

        def rows(m, _):
            product = dot(left_t[tile(m, 256), :], right[:, columns]).astype(jnp.bfloat16)
            product = product.reshape(2, 2, 64, item.width)
            for xx in (0, 1):
                target[xx, m] = product[:, xx]
            return 0

        lax.fori_loop(0, 4, rows, 0)

    def multiply_tall(self, left, right, groups):
        def rows(m, _):
            at = tile(m, 256)
            turned = left[:, at].T
            for columns, targets in groups:
                product = dot(turned, right[:, columns]).astype(jnp.bfloat16)
                for n, (target, xx) in enumerate(targets):
                    target.reshape(2, 2816, 128)[xx, at, :] = product[:, 128 * n : 128 * n + 128]
            return 0

        lax.fori_loop(0, 11, rows, 0)

    def attend_back(self, first, last):
        low = jnp.bfloat16

        def pair(p, _):
            at = tile(p, 128)
            out_rows = self.w_rows[p].reshape(128, 1024)
            grad = dot_nt(self.grad_proj[...], out_rows).astype(low)
            query = (self.query[:, at].astype(jnp.float32) * SCORE_SCALE).astype(low)
            key, value = self.key[:, at], self.value[:, at]
            left = lax.broadcasted_iota(jnp.int32, (512, 128), 1) < HEAD
            none = jnp.zeros((512, 128), low)
            sides = [
                [jnp.where(side, v, none) for v in (query, key, value, grad)]
                for side in (left, ~left)
            ]
            grad_key, grad_value = [None, None], [None, None]
            for block in (0, 1):
                rows, seen = slice(256 * block, 256 * block + 256), slice(0, 256 * block + 256)
                grad_query = None
                parts_key, parts_value = None, None
                for n, (own_query, own_key, own_value, own_grad) in enumerate(sides):
                    self.input_grad[seen, 0:256] = dot_nt(own_key[seen], query[rows])
                    self.input_grad[seen, 256:512] = dot_nt(own_value[seen], grad[rows])
                    self.back_rows(p, n, rows, 256 * block + 256)
                    grad_scores, probs = self.grad_scores[seen, :], self.probs[seen, :]
                    part_query = dot_tn(grad_scores, own_key[seen])
                    part_key = dot(grad_scores, own_query[rows])
                    part_value = dot(probs, own_grad[rows])
                    if n == 0:
                        grad_query, parts_key, parts_value = part_query, part_key, part_value
                    else:
                        grad_query += part_query
                        parts_key += part_key
                        parts_value += part_value
                self.query[rows, at] = (grad_query * SCORE_SCALE).astype(low)
                if block == 0:
                    grad_key[0], grad_value[0] = parts_key, parts_value
                else:
                    grad_key = [grad_key[0] + parts_key[:256], parts_key[256:]]
                    grad_value = [grad_value[0] + parts_value[:256], parts_value[256:]]
            for block in (0, 1):
                rows = slice(256 * block, 256 * block + 256)
                self.key[rows, at] = grad_key[block].astype(low)
                self.value[rows, at] = grad_value[block].astype(low)
            return 0

        lax.fori_loop(first, last, pair, 0)

    def back_rows(self, p, n, rows, count):
        low = jnp.bfloat16
        held = self.input_grad
        log_total = self.log_total[p, n : n + 1, rows]

        def first_pass(r, centre):
            keys = tile(r, 64)
            probs = jnp.exp(held[keys, 0:256] + self.bias[keys, rows] - log_total)
            held[keys, 0:256] = probs
            self.probs[keys, :] = probs.astype(low)
            return centre + jnp.sum((held[keys, 256:512] * probs).reshape(8, 8, 256), axis=0)

        centre = lax.fori_loop(0, count // 64, first_pass, jnp.zeros((8, 256), jnp.float32), unroll=2)
        centre = jnp.sum(centre, axis=0, keepdims=True)

        def second_pass(r, _):
            keys = tile(r, 64)
            grad = held[keys, 0:256] * (held[keys, 256:512] - centre)
            self.grad_scores[keys, :] = grad.astype(low)
            return 0

        lax.fori_loop(0, count // 64, second_pass, 0, unroll=2)

    def grad_hidden(self, t):
        at = pl.ds(256 * t, 256)
        total = None
        for n, grad in enumerate((self.query, self.key, self.value)):
            part = dot_nt(grad[...], self.w_rows[2 * n : 2 * n + 2].reshape(256, 1024))
            total = part if total is None else total + part
        self.input_grad[:, at] = total

    def finish(self):
        self.gain_total[...] = jnp.zeros_like(self.gain_total)

        def rows_of(block, _):
            rows = tile(block, 64)
            values = self.tokens[rows, :].astype(jnp.float32)
            factor = lax.rsqrt(jnp.mean(values * values, axis=-1, keepdims=True) + NORM_EPS)
            normed = values * factor
            grad = self.input_grad[rows, :]
            self.gain_total[...] += jnp.sum((grad * normed).reshape(8, 8, 1024), axis=0)
            grad_normed = grad * self.gain_row[0:1, :].astype(jnp.float32)
            mean = jnp.mean(grad_normed * normed, axis=-1, keepdims=True)
            self.input_grad[rows, :] = self.grad_residual[rows, :] + factor * (
                grad_normed - normed * mean
            )
            return 0

        lax.fori_loop(0, 8, rows_of, 0)
        self.gain_lines[...] = jnp.zeros_like(self.gain_lines)
        lines = [jnp.sum(v[...], axis=0, keepdims=True) for v in (self.gain_total, self.gain_grad)]
        for s in range(8):
            for n, line in enumerate(lines):
                self.gain_lines[s // 2, s % 2, n : n + 1] = line[:, 128 * s : 128 * s + 128]


def backward_kernel(items, *refs):
    refs = list(refs)

    def take(n):
        taken = refs[:n]
        del refs[:n]
        return taken

    kept = take(len(KEPT))
    middle_in, grad_gate_in, grad_up_in = take(3)
    saved_in = dict(zip(BACKWARD_IN, take(len(BACKWARD_IN))))
    tokens_in, length = take(2)
    sums = take(7)
    gain_sums, input_grad_out = take(2)
    saved = dict(zip(BACKWARD_IN, take(len(BACKWARD_IN))))
    input_grad, wide, w_rows, bias, probs, grad_scores, gain_total, gain_lines = take(8)
    mine, from_first, from_second, from_z = (take(len(items)) for _ in range(4))
    ring, tall_ring = take(RING), take(2)
    outbox, tall_outbox = take(2), take(2)
    gain_core, gain_x, gain_y, gain_z = take(4)
    send_sems, recv_sems, load_sems, credit = refs
    z, y, x, c = place()
    far = [lax.rem(z + k, 4) for k in range(4)]
    back = [lax.rem(z + 4 - k, 4) for k in range(4)]
    x_other, y_other, c_other = (
        device(z, y, 1 - x, c),
        device(z, 1 - y, x, c),
        device(z, y, x, 1 - c),
    )
    loads = {}

    def load(name, source, target):
        loads[name] = pltpu.make_async_copy(source, target, load_sems.at[len(loads)])
        loads[name].start()

    waited = set()

    def loaded(*names):
        for name in names:
            if name not in waited:
                loads[name].wait()
                waited.add(name)

    load("grad_gate", grad_gate_in, wide.at[1])
    load("hidden_two_t", saved_in["hidden_two_t"], saved["hidden_two_t"])
    load("middle", middle_in, wide.at[0])
    load("branch", saved_in["branch"], saved["branch"])
    load("out_rows", kept[OUT].reshape(8, 2, 64, 1024), w_rows)
    for name in BACKWARD_IN:
        if name not in loads:
            load(name, saved_in[name], saved[name])
    greet()
    wires = Wires(send_sems, recv_sems)
    work = Backward(
        dict(
            saved,
            tokens=saved["branch"],
            length=length,
            w_rows=w_rows,
            probs=probs,
            grad_scores=grad_scores,
            bias=bias,
            input_grad=input_grad,
            gain_total=gain_total,
            gain_lines=gain_lines,
        )
    )
    tall_items = [i for i, item in enumerate(items) if item.tall]
    wide_items = [i for i, item in enumerate(items) if not item.tall]

    def slot(i, k):
        return SUM_SLOTS * i + k

    def core_slots(i):
        return (slot(i, 0), slot(i, 8))

    def from_core(i):
        if items[i].tall:
            return tall_ring[tall_items.index(i)]
        return ring[wide_items.index(i) % RING].at[..., : items[i].width]

    def produce(i):
        item = items[i]
        if item.tall:
            number = tall_items.index(i)
            if number == 0:
                loaded("middle", "branch")
                groups = []
                for core, boxes in ((1 - c, tall_outbox), (c, [mine[j] for j in tall_items])):
                    columns = pl.ds(pl.multiple_of(512 * core, 512), 512)
                    groups.append((columns, [(boxes[j], xx) for xx in (0, 1) for j in (0, 1)]))
                work.multiply_tall(wide.at[0], saved["branch"], groups)
                load("grad_up", grad_up_in, wide.at[0])
                load("tokens", tokens_in, saved["branch"])
            box = tall_outbox[number]
        else:
            number = wide_items.index(i)
            if number >= 2:
                wires.finish(lambda s: s in core_slots(wide_items[number - 2]))
            box = outbox[number % 2].at[..., : item.width]
            left, right, names = {
                GATE: (saved["hidden_two_t"], wide.at[1], ("hidden_two_t", "grad_gate")),
                UP: (saved["hidden_two_t"], wide.at[0], ("grad_up",)),
                OUT: (saved["attended_t"], saved["grad_proj"], ("attended_t", "grad_proj")),
                QUERY: (saved["hidden_t"], saved["query"], ("hidden_t",)),
                KEY: (saved["hidden_t"], saved["key"], ()),
                VALUE: (saved["hidden_t"], saved["value"], ()),
            }[item.weight]
            loaded(*names)
            multiply = partial(work.multiply, left, right, item)
            if number >= RING:
                pl.semaphore_wait(credit, 1)
            multiply(box, 1 - c)
        for xx in (0, 1):
            wires.send(core_slots(i)[xx], box.at[xx], from_core(i).at[xx], c_other)
        if not item.tall:
            multiply(mine[i], c)

    def first_hop(i):
        item, own, other = items[i], mine[i], from_core(i)
        for xx in (0, 1):
            wires.arrived(core_slots(i)[xx], other.at[xx])

        def add(at, _):
            for xx in (0, 1):
                for yy in (0, 1):
                    own[xx, at, yy] = plus(own[xx, at, yy], other[xx, at, yy])
            return 0

        lax.fori_loop(0, 4, add, 0)
        if not item.tall and wide_items.index(i) + RING < len(wide_items):
            pl.semaphore_signal(credit, inc=1, device_id=c_other, device_id_type=MESH)
        if item.x_first:
            wires.send(slot(i, 1), own.at[1 - x], from_first[i], x_other)
        else:
            wires.send(slot(i, 1), own.at[:, :, 1 - y], from_first[i], y_other)

    def second_hop(i):
        item, own, other = items[i], mine[i], from_first[i]
        wires.arrived(slot(i, 1), other)

        def add(at, _):
            for side in (0, 1):
                if item.x_first:
                    own[x, at, side] = plus(own[x, at, side], other[at, side])
                else:
                    own[side, at, y] = plus(own[side, at, y], other[side, at])
            return 0

        lax.fori_loop(0, 4, add, 0)
        if item.x_first:
            wires.send(slot(i, 2), own.at[x, :, 1 - y], from_second[i], y_other)
        else:
            to_z(i, lambda k: own.at[:, far[k], y])

    def to_z(i, block):
        for k in (1, 2, 3):
            wires.send(slot(i, 2 + k), block(k), from_z[i].at[k - 1], device(far[k], y, x, c))

    def z_total(i, own_part):
        total = own_part.astype(jnp.float32)
        for k in (1, 2, 3):
            wires.arrived(slot(i, 2 + k), from_z[i].at[k - 1])
            total += from_z[i][k - 1].astype(jnp.float32)
        return total.astype(jnp.bfloat16)

    def third_hop(i):
        item, own, other = items[i], mine[i], from_second[i]
        if not item.x_first:
            own[:, z, y] = z_total(i, own[:, z, y])
            wires.send(slot(i, 2), own.at[:, z, y], other, x_other)
            return
        wires.arrived(slot(i, 2), other)

        def add(at, _):
            own[x, at, y] = plus(own[x, at, y], other[at])
            return 0

        lax.fori_loop(0, 4, add, 0)
        to_z(i, lambda k: own.at[x, far[k], y])

    def fourth_hop(i):
        item, own = items[i], mine[i]
        if not item.x_first:
            wires.arrived(slot(i, 2), from_second[i])
            block = item.half(sums[item.weight], c)
            block[...] = plus(own[:, z, y], from_second[i][...])
            wires.send(slot(i, 7), block, block, c_other)
            return
        block = item.quarter(sums[item.weight], c, x)
        block[...] = z_total(i, own[x, z, y])
        wires.send(slot(i, 6), block, block, x_other)

    def to_sibling(i):
        item = items[i]
        if item.x_first:
            wires.arrived(slot(i, 6), item.quarter(sums[item.weight], c, 1 - x))
            block = item.half(sums[item.weight], c)
            wires.send(slot(i, 7), block, block, c_other)

    def complete(i):
        item = items[i]
        wires.arrived(slot(i, 7), item.half(sums[item.weight], 1 - c))
        wires.finish(lambda s: s // SUM_SLOTS == i)

    base = SUM_SLOTS * len(items)

    def gains_one():
        wires.send(base, gain_lines, gain_core, c_other)

    def gains_two():
        wires.arrived(base, gain_core)
        gain_core[...] = gain_lines[...] + gain_core[...]
        wires.send(base + 1, gain_core, gain_x, x_other)

    def gains_three():
        wires.arrived(base + 1, gain_x)
        gain_x[...] = gain_core[...] + gain_x[...]
        wires.send(base + 2, gain_x.at[:, 1 - y], gain_y, y_other)

    def gains_four():
        wires.arrived(base + 2, gain_y)
        gain_y[...] = gain_x[:, y] + gain_y[...]
        for k in (1, 2, 3):
            wires.send(base + 2 + k, gain_y.at[far[k]], gain_z.at[z], device(far[k], y, x, c))
        gain_z[z] = gain_y[z]

    def gains_five():
        for k in (1, 2, 3):
            wires.arrived(base + 2 + k, gain_z.at[back[k]])
        gain_sums[...] = (gain_z[0] + gain_z[1]) + (gain_z[2] + gain_z[3])

    def fetch_rows(t):
        for n in range(3):
            load(("rows", n, t), kept[n].at[t], w_rows.at[2 * n : 2 * n + 2])

    def attend_back(p):
        if p == 0:
            loaded("query", "key", "value", "log_total", "grad_proj", "out_rows")
        work.attend_back(p, p + 1)
        if p == 7:
            fetch_rows(0)

    def grad_hidden(t):
        loaded(*[("rows", n, t) for n in range(3)])
        work.grad_hidden(t)
        if t < 3:
            fetch_rows(t + 1)

    def finish():
        loaded("tokens", "grad_residual", "gain_grad", "gain_row")
        work.finish()
        load("input_grad", input_grad, input_grad_out)
        gains_one()

    beside = {1: [work.prepare]}
    for p in range(8):
        beside.setdefault(1 + p, []).append(partial(attend_back, p))
    for t in range(4):
        beside.setdefault(9 + t // 2, []).append(partial(grad_hidden, t))
    beside.setdefault(11, []).append(finish)
    for n, task in enumerate((gains_two, gains_three, gains_four, gains_five)):
        beside.setdefault(13 + 2 * n, []).append(task)

    stages = (complete, to_sibling, fourth_hop, third_hop, second_hop, first_hop, produce)
    lates = (12, 10, 8, 6, 4, 2, 0)
    for step in range(len(items) + lates[0]):
        for late, stage in zip(lates, stages):
            if 0 <= step - late < len(items):
                stage(step - late)
        for task in beside.get(step, []):
            task()
    loaded("input_grad")
    wires.finish()


def backward(tokens, lengths, kept, saved):
    items = share_items()
    low, wide = jnp.bfloat16, jnp.float32
    dtypes = {name: (shape, dtype) for name, shape, dtype in FORWARD_OUTS}
    shapes = [
        jax.ShapeDtypeStruct((2, 2, 2, 352, 128) if n is None else (2, 64, n), low) for n in COLUMNS
    ]
    shapes += [jax.ShapeDtypeStruct((8, 128), wide), jax.ShapeDtypeStruct((512, 1024), wide)]
    count = SUM_SLOTS * len(items) + 6
    anywhere = pl.BlockSpec(memory_space=pl.ANY)
    in_vmem = pl.BlockSpec(memory_space=pltpu.VMEM)
    n_loads = 6 + len(BACKWARD_IN) + 12

    def buffers(lead_of):
        return [pltpu.VMEM(lead_of(item) + item.block, low) for item in items]

    out = pl.pallas_call(
        partial(backward_kernel, items),
        out_shape=shapes,
        in_specs=[anywhere] * (len(KEPT) + 3 + len(BACKWARD_IN) + 1)
        + [pl.BlockSpec(memory_space=pltpu.SMEM)],
        out_specs=[in_vmem] * 8 + [anywhere],
        scratch_shapes=[pltpu.VMEM(*dtypes[name]) for name in BACKWARD_IN]
        + [
            pltpu.VMEM((512, 1024), wide),
            pltpu.VMEM((2, 512, 2816), low),
            pltpu.VMEM((8, 2, 64, 1024), low),
            pltpu.VMEM((512, 512), wide),
            pltpu.VMEM((512, 256), low),
            pltpu.VMEM((512, 256), low),
            pltpu.VMEM((8, 1024), wide),
            pltpu.VMEM((4, 2, 8, 128), wide),
        ]
        + buffers(lambda item: (2, 4, 2))
        + buffers(lambda item: (4, 2) if item.x_first else (2, 4))
        + buffers(lambda item: (4,) if item.x_first else (2,))
        + buffers(lambda item: (3,) if item.x_first else (3, 2))
        + [pltpu.VMEM((2, 4, 2, 64, 512), low)] * RING
        + [pltpu.VMEM((2, 4, 2, 352, 128), low)] * 2
        + [pltpu.VMEM((2, 4, 2, 64, 512), low)] * 2
        + [pltpu.VMEM((2, 4, 2, 352, 128), low)] * 2
        + [
            pltpu.VMEM((4, 2, 8, 128), wide),
            pltpu.VMEM((4, 2, 8, 128), wide),
            pltpu.VMEM((4, 8, 128), wide),
            pltpu.VMEM((4, 8, 128), wide),
            pltpu.SemaphoreType.DMA((count,)),
            pltpu.SemaphoreType.DMA((count,)),
            pltpu.SemaphoreType.DMA((n_loads,)),
            pltpu.SemaphoreType.REGULAR,
        ],
        compiler_params=pltpu.CompilerParams(
            collective_id=1, has_side_effects=True, vmem_limit_bytes=63 * MIB
        ),
        name="backward_sum",
    )(
        *kept,
        saved["middle"],
        saved["grad_gate"],
        saved["grad_up"],
        *[saved[name] for name in BACKWARD_IN],
        tokens,
        lengths,
    )
    return out[:7], out[7], out[8]


def unpack_kernel(*refs):
    blocks, (gain_sums, mixed, input_grad) = refs[:7], refs[7:10]
    sums, (gain_attn, gain_ffn, mixed_out, input_out) = refs[10:17], refs[17:21]
    mixed_held, input_held, sems = refs[21:]
    routes = ((mixed, mixed_held, mixed_out), (input_grad, input_held, input_out))
    ins = [pltpu.make_async_copy(a, b, sems.at[n]) for n, (a, b, _) in enumerate(routes)]
    outs = [pltpu.make_async_copy(b, a, sems.at[2 + n]) for n, (_, b, a) in enumerate(routes)]
    for copy in ins:
        copy.start()
    for copy_in, copy_out in zip(ins, outs):
        copy_in.wait()
        copy_out.start()
    for block, total in zip(blocks[:6], sums[:6]):
        total[...] = block[...].astype(jnp.float32)
    for b in range(8):
        sums[6][:, 128 * b : 128 * b + 128] = blocks[6][b // 4, b // 2 % 2, b % 2].astype(
            jnp.float32
        )
    gain_attn[...] = gain_sums[0:1]
    gain_ffn[...] = gain_sums[1:2]
    for copy in outs:
        copy.wait()


def unpack(blocks, gain_sums, mixed, input_grad):
    wide = jnp.float32
    anywhere = pl.BlockSpec(memory_space=pl.ANY)
    in_vmem = pl.BlockSpec(memory_space=pltpu.VMEM)
    shapes = [
        jax.ShapeDtypeStruct((352, 1024) if n is None else (2, 64, n), wide) for n in COLUMNS
    ]
    shapes += [jax.ShapeDtypeStruct((1, 128), wide)] * 2
    shapes += [jax.ShapeDtypeStruct(v.shape, v.dtype) for v in (mixed, input_grad)]
    out = pl.pallas_call(
        unpack_kernel,
        out_shape=shapes,
        in_specs=[in_vmem] * 8 + [anywhere] * 2,
        out_specs=[in_vmem] * 9 + [anywhere] * 2,
        scratch_shapes=[
            pltpu.VMEM(mixed.shape, mixed.dtype),
            pltpu.VMEM(input_grad.shape, input_grad.dtype),
            pltpu.SemaphoreType.DMA((4,)),
        ],
        compiler_params=pltpu.CompilerParams(vmem_limit_bytes=62 * MIB),
        name="unpack",
    )(*blocks, gain_sums, mixed, input_grad)
    sums = [s.reshape(-1, s.shape[-1]) for s in out[:7]]
    return sums, [g.reshape(128) for g in out[7:9]], out[9], out[10]


def gather_plain(weights, gains):
    everything = (*weights, *gains)
    whole = [lax.all_gather(v, "dp", axis=0, tiled=True) for v in everything]
    return whole[: len(weights)], whole[len(weights) :]


def sum_plain(grads, gain_grads):
    shares = [
        lax.psum_scatter(g.astype(jnp.float32), "dp", scatter_dimension=0, tiled=True)
        for g in (*grads, *gain_grads)
    ]
    sums = [lax.psum(s, ("rep", "cores")) for s in shares]
    return sums[: len(grads)], sums[len(grads) :]


def on_any_device(
    tokens,
    norm_attn,
    w_query,
    w_key,
    w_value,
    w_out,
    norm_ffn,
    w_gate,
    w_up,
    w_down,
    lengths,
    cotangent,
):
    rows = tokens.shape[0]
    low = jnp.bfloat16
    allowed, valid = masks(lengths, rows)
    whole, gains = gather_plain(
        (w_query, w_key, w_value, w_out, w_gate, w_up, w_down), (norm_attn, norm_ffn)
    )
    full_query, full_key, full_value, full_out, full_gate, full_up, full_down = whole
    gain_attn, gain_ffn = gains
    inputs = tokens.astype(jnp.float32)
    normed, factor = normalize(inputs)
    hidden = (normed * gain_attn.astype(jnp.float32)).astype(low)
    query = matmul(hidden, full_query).astype(low)
    keyed = matmul(hidden, full_key).astype(low)
    valued = matmul(hidden, full_value).astype(low)
    query_groups, key_groups, value_groups = (to_groups(query), to_groups(keyed), to_groups(valued))
    attended_groups, log_total = lax.map(
        partial(attend, allowed), (query_groups, key_groups, value_groups)
    )
    attended = from_groups(attended_groups)
    residual = inputs + matmul(attended, full_out)
    normed_two, factor_two = normalize(residual)
    hidden_two = (normed_two * gain_ffn.astype(jnp.float32)).astype(low)
    gate = matmul(hidden_two, full_gate)
    upward = matmul(hidden_two, full_up)
    sigma = jax.nn.sigmoid(gate)
    middle = (gate * sigma * upward).astype(low)
    mixed = (valid[:, None] * (residual + matmul(middle, full_down))).astype(low)
    grad_output = cotangent.astype(jnp.float32) * valid[:, None]
    grad_branch = grad_output.astype(low)
    grad_down = matmul_tn(middle, grad_branch)
    grad_middle = matmul_nt(grad_branch, full_down)
    grad_gate_rows = (grad_middle * upward * sigma * (1.0 + gate * (1.0 - sigma))).astype(low)
    grad_up_rows = (grad_middle * gate * sigma).astype(low)
    grad_gate = matmul_tn(hidden_two, grad_gate_rows)
    grad_up = matmul_tn(hidden_two, grad_up_rows)
    grad_hidden_two = matmul_nt(grad_gate_rows, full_gate) + matmul_nt(grad_up_rows, full_up)
    grad_gain_ffn = jnp.sum(grad_hidden_two * normed_two, axis=0)
    grad_residual = grad_output + norm_back(
        grad_hidden_two * gain_ffn.astype(jnp.float32), normed_two, factor_two
    )
    grad_proj = grad_residual.astype(low)
    grad_out = matmul_tn(attended, grad_proj)
    grad_attended = matmul_nt(grad_proj, full_out).astype(low)
    grad_query_g, grad_key_g, grad_value_g = lax.map(
        partial(attend_back, allowed),
        (query_groups, key_groups, value_groups, to_groups(grad_attended), log_total),
    )
    grad_query_rows = from_groups(grad_query_g)
    grad_key_rows = from_groups(grad_key_g)
    grad_value_rows = from_groups(grad_value_g)
    grad_query = matmul_tn(hidden, grad_query_rows)
    grad_key = matmul_tn(hidden, grad_key_rows)
    grad_value = matmul_tn(hidden, grad_value_rows)
    grad_hidden = (
        matmul_nt(grad_query_rows, full_query)
        + matmul_nt(grad_key_rows, full_key)
        + matmul_nt(grad_value_rows, full_value)
    )
    grad_gain_attn = jnp.sum(grad_hidden * normed, axis=0)
    input_grad = grad_residual + norm_back(
        grad_hidden * gain_attn.astype(jnp.float32), normed, factor
    )
    grads = (grad_query, grad_key, grad_value, grad_out, grad_gate, grad_up, grad_down)
    sums, gain_sums = sum_plain([g.astype(low) for g in grads], (grad_gain_attn, grad_gain_ffn))
    return (
        mixed,
        input_grad,
        gain_sums[0],
        sums[0],
        sums[1],
        sums[2],
        sums[3],
        gain_sums[1],
        sums[4],
        sums[5],
        sums[6],
    )


def on_tuned_device(
    tokens,
    norm_attn,
    w_query,
    w_key,
    w_value,
    w_out,
    norm_ffn,
    w_gate,
    w_up,
    w_down,
    lengths,
    cotangent,
):
    weights = (w_query, w_key, w_value, w_out, w_gate, w_up, w_down)
    kept, saved = forward(tokens, cotangent, lengths, weights, (norm_attn, norm_ffn))
    blocks, gain_lines, input_grad = backward(tokens, lengths, kept, saved)
    sums, gain_sums, mixed, input_grad = unpack(blocks, gain_lines, saved["mixed"], input_grad)
    return (
        mixed,
        input_grad,
        gain_sums[0],
        *sums[:4],
        gain_sums[1],
        *sums[4:],
    )


def solution(mesh):
    tuned = dict(mesh.shape) == {"dp": 8, "rep": 2, "cores": 2}
    tokens_placed = P(("dp", "rep", "cores"), None)
    share, gain = P("dp", None), P("dp")
    return jax.shard_map(
        on_tuned_device if tuned else on_any_device,
        mesh=mesh,
        in_specs=(
            tokens_placed,
            gain,
            share,
            share,
            share,
            share,
            gain,
            share,
            share,
            share,
            tokens_placed,
            tokens_placed,
        ),
        out_specs=(
            tokens_placed,
            tokens_placed,
            gain,
            share,
            share,
            share,
            share,
            gain,
            share,
            share,
            share,
        ),
        check_vma=False,
    )
```

```python
from functools import partial

import jax
import jax.numpy as jnp
from jax import lax
from jax.experimental import pallas as pl
from jax.experimental.pallas import tpu as pltpu
from jax.sharding import PartitionSpec as P

HEADS = 16
HEAD = 64


NORM_EPS = 1e-05
SCORE_SCALE = 0.125
NEGATIVE = -1e30
head_group = 4
MESH = pl.DeviceIdType.MESH
MIB = 1024 * 1024


def masks(block_len, rows):
    bounds = jnp.cumsum(block_len[0])
    place = jnp.arange(rows, dtype=jnp.int32)
    segment = jnp.sum((place[:, None] >= bounds[None, :]).astype(jnp.int32), axis=1)
    allowed = (segment[:, None] == segment[None, :]) & (place[None, :] <= place[:, None])
    valid = (segment < block_len.shape[1]).astype(jnp.float32)
    return (allowed, valid)


def normalize(values):
    factor = lax.rsqrt(jnp.mean(values * values, axis=-1, keepdims=True) + NORM_EPS)
    return (values * factor, factor)


def norm_back(grad_normed, normed, factor):
    return factor * (grad_normed - normed * jnp.mean(grad_normed * normed, axis=-1, keepdims=True))


def matmul(left, right):
    return jnp.dot(left, right, preferred_element_type=jnp.float32)


def matmul_tn(left, right):
    return lax.dot_general(
        left, right, (((0,), (0,)), ((), ())), preferred_element_type=jnp.float32
    )


def matmul_nt(left, right):
    return lax.dot_general(
        left, right, (((1,), (1,)), ((), ())), preferred_element_type=jnp.float32
    )


def to_groups(matrix):
    rows = matrix.shape[0]
    split = matrix.reshape(rows, HEADS // head_group, head_group, HEAD)
    return split.transpose(1, 2, 0, 3)


def from_groups(grouped):
    rows = grouped.shape[2]
    return grouped.transpose(2, 0, 1, 3).reshape(rows, HEADS * HEAD)


def group_scores(allowed, query_g, key_g):
    raw = (
        jnp.einsum("hqe,hke->hqk", query_g, key_g, preferred_element_type=jnp.float32) * SCORE_SCALE
    )
    return jnp.where(allowed[None], raw, NEGATIVE)


def attend(allowed, operands):
    query_g, key_g, value_g = operands
    scores = group_scores(allowed, query_g, key_g)
    top = jnp.max(scores, axis=-1, keepdims=True)
    expo = jnp.exp(scores - top)
    total = jnp.sum(expo, axis=-1, keepdims=True)
    probs_low = (expo / total).astype(jnp.bfloat16)
    result = jnp.einsum("hqk,hke->hqe", probs_low, value_g, preferred_element_type=jnp.float32)
    return (result.astype(jnp.bfloat16), top[..., 0] + jnp.log(total[..., 0]))


def attend_back(allowed, operands):
    query_g, key_g, value_g, grad_g, log_total = operands
    scores = group_scores(allowed, query_g, key_g)
    probs = jnp.exp(scores - log_total[..., None])
    grad_probs = jnp.einsum("hqe,hke->hqk", grad_g, value_g, preferred_element_type=jnp.float32)
    centre = jnp.sum(grad_probs * probs, axis=-1, keepdims=True)
    grad_scores = (probs * (grad_probs - centre)).astype(jnp.bfloat16)
    grad_query = (
        jnp.einsum("hqk,hke->hqe", grad_scores, key_g, preferred_element_type=jnp.float32)
        * SCORE_SCALE
    )
    grad_key = (
        jnp.einsum("hqk,hqe->hke", grad_scores, query_g, preferred_element_type=jnp.float32)
        * SCORE_SCALE
    )
    grad_value = jnp.einsum(
        "hqk,hqe->hke", probs.astype(jnp.bfloat16), grad_g, preferred_element_type=jnp.float32
    )
    return (
        grad_query.astype(jnp.bfloat16),
        grad_key.astype(jnp.bfloat16),
        grad_value.astype(jnp.bfloat16),
    )


class Part:
    def __init__(self, weight, tall, start, size, no_x):
        self.weight, self.tall, self.start, self.size = weight, tall, start, size
        self.no_x = no_x

    def quarter(self, ref, lead, c, x):
        if self.tall:
            columns = pl.ds(pl.multiple_of(c * 512 + x * 256, 256), 256)
            return ref.at[(*lead, pl.ds(self.start, self.size), columns)]
        return ref.at[(*lead, x, slice(None), self.columns(c))]

    def half(self, ref, lead, c):
        if self.tall:
            columns = pl.ds(pl.multiple_of(c * 512, 512), 512)
            return ref.at[(*lead, pl.ds(self.start, self.size), columns)]
        return ref.at[(*lead, slice(None), slice(None), self.columns(c))]

    def columns(self, c):
        width = self.size // 2
        return pl.ds(pl.multiple_of(self.start + c * width, 128), width)


def pieces(total, most):
    return [(start, min(most, total - start)) for start in range(0, total, most)]


def place():
    d = lax.axis_index("dp")
    return lax.div(d, 2), lax.rem(d, 2), lax.axis_index("rep"), lax.axis_index("cores")


def device(z, y, x, c):
    return {"dp": 2 * z + y, "rep": x, "cores": c}


def greet():
    z, y, x, c = place()
    barrier = pltpu.get_barrier_semaphore()
    others = [device(lax.rem(z + k, 4), y, x, c) for k in (1, 2, 3)]
    others += [device(z, 1 - y, x, c), device(z, y, 1 - x, c), device(z, y, x, 1 - c)]
    for other in others:
        pl.semaphore_signal(barrier, inc=1, device_id=other, device_id_type=MESH)
    pl.semaphore_wait(barrier, len(others))


class Wires:
    def __init__(self, send_sems, recv_sems):
        self.send_sems, self.recv_sems, self.sent = send_sems, recv_sems, []

    def copy(self, slot, source, target, other):
        return pltpu.make_async_remote_copy(
            src_ref=source,
            dst_ref=target,
            send_sem=self.send_sems.at[slot],
            recv_sem=self.recv_sems.at[slot],
            device_id=other,
            device_id_type=MESH,
        )

    def send(self, slot, source, target, other):
        copy = self.copy(slot, source, target, other)
        copy.start()
        self.sent.append((slot, copy))

    def arrived(self, slot, target):
        z, y, x, c = place()
        self.copy(slot, target, target, device(z, y, x, 1 - c)).wait_recv()

    def finish(self, chosen=lambda slot: True):
        for slot, copy in self.sent:
            if chosen(slot):
                copy.wait_send()
        self.sent = [(slot, copy) for slot, copy in self.sent if not chosen(slot)]


GATHER_SLOTS = 12
LAG = 2
ALL = slice(None)
COLUMNS = (1024, 1024, 1024, 1024, 2816, 2816, None)
QUERY, KEY, VALUE, OUT, GATE, UP, DOWN = range(7)
TILE = 512


FF_CHUNKS = ((0, 1024), (1024, 512), (1536, 512), (2048, 512), (2560, 256))


def gather_items():
    order = [(QUERY, 0, 256, True), (QUERY, 256, 768, False), (KEY, 0, 1024, True)]
    order += [(VALUE, 0, 1024, False), (OUT, 0, 1024, False)]
    order += [(DOWN, 0, 128, False), (DOWN, 128, 128, True), (DOWN, 256, 96, False)]
    for n, (start, size) in enumerate(FF_CHUNKS):
        order += [(GATE, start, size, n == 4), (UP, start, size, n in (1, 4))]
    return [Part(w, w == DOWN, start, size, no_x) for w, start, size, no_x in order]


def dot(left, right):
    return lax.dot_general(
        left, right, (((1,), (0,)), ((), ())), preferred_element_type=jnp.float32
    )


def dot_nt(left, right):
    return lax.dot_general(
        left, right, (((1,), (1,)), ((), ())), preferred_element_type=jnp.float32
    )


def tile(index, size):
    return pl.ds(pl.multiple_of(index * size, size), size)


def weight_columns(ref, at):
    return ref[:, :, :, :, at].reshape(1024, -1)


class Forward:
    def __init__(self, refs):
        self.__dict__.update(refs)

    def prepare(self):
        for s in range(8):
            self.gain_row[:, 128 * s : 128 * s + 128] = self.gains[s // 2, s % 2]
        length = self.length[0, 0]
        for block in range(4):
            rows = slice(128 * block, 128 * block + 128)
            place_q = lax.broadcasted_iota(jnp.int32, (128, 512), 0) + 128 * block
            place_k = lax.broadcasted_iota(jnp.int32, (128, 512), 1)
            same = (place_q >= length) == (place_k >= length)
            allowed = same & (place_k <= place_q)
            self.bias[rows, :] = jnp.where(allowed, 0.0, NEGATIVE)

        def normed(block, _):
            rows = tile(block, 64)
            values = self.tokens[rows, :].astype(jnp.float32)
            factor = lax.rsqrt(jnp.mean(values * values, axis=-1, keepdims=True) + NORM_EPS)
            gain = self.gain_row[0:1, :].astype(jnp.float32)
            self.hidden[rows, :] = (values * factor * gain).astype(jnp.bfloat16)
            place = lax.broadcasted_iota(jnp.int32, (64, 1024), 0) + 64 * block
            branch = jnp.where(place < length, self.cotangent[rows, :].astype(jnp.float32), 0.0)
            self.branch[rows, :] = branch.astype(jnp.bfloat16)
            return 0

        lax.fori_loop(0, 8, normed, 0)
        self.turn(self.hidden, self.hidden_t)
        self.out("branch")

    def turn(self, matrix, turned):
        def columns(n, _):
            at = tile(n, 128)
            turned[at, :] = matrix[:, at].astype(jnp.float32).T.astype(jnp.bfloat16)
            return 0

        lax.fori_loop(0, 8, columns, 0)

    def project(self, weight, result):
        def columns(n, _):
            at = tile(n, TILE)
            result[:, at] = dot(self.hidden[...], weight_columns(weight, at)).astype(jnp.bfloat16)
            return 0

        lax.fori_loop(0, 1024 // TILE, columns, 0)

    def attend(self, first, last):
        def pair(p, _):
            at = tile(p, 128)
            left = lax.broadcasted_iota(jnp.int32, (256, 128), 1) < HEAD
            for block in (0, 1):
                rows, seen = slice(256 * block, 256 * block + 256), slice(0, 256 * block + 256)
                query = self.query[rows, at].astype(jnp.float32) * SCORE_SCALE
                both = jnp.concatenate(
                    [jnp.where(left, query, 0.0), jnp.where(left, 0.0, query)], axis=0
                ).astype(jnp.bfloat16)
                bias = self.bias[rows, seen]
                scores = dot_nt(both, self.key[seen, at]) + jnp.concatenate([bias, bias], axis=0)
                top = jnp.max(scores, axis=-1, keepdims=True)
                expo = jnp.exp(scores - top)
                total = jnp.sum(expo, axis=-1, keepdims=True)
                probs = (expo * (1.0 / total)).astype(jnp.bfloat16)
                result = dot(probs, self.value[seen, at])
                self.attended[rows, at] = jnp.where(left, result[:256], result[256:]).astype(
                    jnp.bfloat16
                )
                log_total = top + jnp.log(total)
                turned = jnp.where(left, log_total[:256], log_total[256:]).T
                self.log_total[p, 0:1, rows] = turned[0:1]
                self.log_total[p, 1:2, rows] = turned[HEAD : HEAD + 1]
            return 0

        lax.fori_loop(first, last, pair, 0)

    def project_out(self):
        def columns(n, _):
            at = tile(n, TILE)
            self.residual[:, at] = self.tokens[:, at].astype(jnp.float32) + dot(
                self.attended[...], weight_columns(self.w_out, at)
            )
            return 0

        lax.fori_loop(0, 1024 // TILE, columns, 0)

        def normed(block, _):
            rows = tile(block, 64)
            values = self.residual[rows, :]
            factor = lax.rsqrt(jnp.mean(values * values, axis=-1, keepdims=True) + NORM_EPS)
            gain = self.gain_row[8:9, :].astype(jnp.float32)
            self.hidden_two[rows, :] = (values * factor * gain).astype(jnp.bfloat16)
            return 0

        lax.fori_loop(0, 8, normed, 0)
        self.turn(self.hidden_two, self.hidden_two_t)
        self.turn(self.attended, self.attended_t)
        for name in ("query", "key", "value", "log_total", "hidden_t", "hidden_two_t", "attended_t"):
            self.out(name)

    def grad_of_middle(self, start, size):
        at = pl.ds(start, size)
        self.grad_up[:, at] = dot_nt(self.branch[...], self.w_down[at, :]).astype(jnp.bfloat16)

    def feed_forward(self, start, size):
        at = pl.ds(start, size)
        low = jnp.bfloat16
        gate_w = weight_columns(self.w_gate, at)
        up_w = weight_columns(self.w_up, at)
        down_w = self.w_down[at, :]
        gate = dot(self.hidden_two[...], gate_w)
        upward = dot(self.hidden_two[...], up_w)
        grad_middle = self.grad_up[:, at].astype(jnp.float32)
        sigma = 1.0 / (1.0 + jnp.exp(-gate))
        silu = gate * sigma
        middle = (silu * upward).astype(low)
        grad_up = (grad_middle * silu).astype(low)
        grad_gate = (grad_middle * upward * sigma * (1.0 + gate * (1.0 - sigma))).astype(low)
        self.middle[:, at] = middle
        self.grad_up[:, at] = grad_up
        self.grad_gate[:, at] = grad_gate
        for j in range(1024 // TILE):
            part = slice(TILE * j, TILE * j + TILE)
            mixed = dot(middle, down_w[:, part])
            grad = dot_nt(grad_gate, gate_w[part, :]) + dot_nt(grad_up, up_w[part, :])
            if start == 0:
                self.total[:, part] = mixed
                self.grad_hidden_two[:, part] = grad
            else:
                self.total[:, part] += mixed
                self.grad_hidden_two[:, part] += grad

    def flush(self, start, size):
        for name in ("middle", "grad_gate", "grad_up"):
            self.out(name, pl.ds(start, size))

    def finish(self):
        length = self.length[0, 0]
        self.gain_grad[...] = jnp.zeros_like(self.gain_grad)

        def rows_of(block, _):
            rows = tile(block, 64)
            place = lax.broadcasted_iota(jnp.int32, (64, 1024), 0) + 64 * block
            residual = self.residual[rows, :]
            mixed = jnp.where(place < length, residual + self.total[rows, :], 0.0)
            self.mixed[rows, :] = mixed.astype(jnp.bfloat16)
            factor = lax.rsqrt(jnp.mean(residual * residual, axis=-1, keepdims=True) + NORM_EPS)
            normed = residual * factor
            grad = self.grad_hidden_two[rows, :]
            self.gain_grad[...] += jnp.sum((grad * normed).reshape(8, 8, 1024), axis=0)
            grad_normed = grad * self.gain_row[8:9, :].astype(jnp.float32)
            grad_out = jnp.where(place < length, self.cotangent[rows, :].astype(jnp.float32), 0.0)
            mean = jnp.mean(grad_normed * normed, axis=-1, keepdims=True)
            grad_residual = grad_out + factor * (grad_normed - normed * mean)
            self.grad_residual[rows, :] = grad_residual
            self.grad_proj[rows, :] = grad_residual.astype(jnp.bfloat16)
            return 0

        lax.fori_loop(0, 8, rows_of, 0)
        for name in ("mixed", "grad_residual", "grad_proj", "gain_grad", "gain_row"):
            self.out(name)


FORWARD_OUTS = (
    ("mixed", (512, 1024), jnp.bfloat16),
    ("query", (512, 1024), jnp.bfloat16),
    ("key", (512, 1024), jnp.bfloat16),
    ("value", (512, 1024), jnp.bfloat16),
    ("log_total", (8, 8, 512), jnp.float32),
    ("hidden_t", (1024, 512), jnp.bfloat16),
    ("hidden_two_t", (1024, 512), jnp.bfloat16),
    ("attended_t", (1024, 512), jnp.bfloat16),
    ("branch", (512, 1024), jnp.bfloat16),
    ("middle", (512, 2816), jnp.bfloat16),
    ("grad_gate", (512, 2816), jnp.bfloat16),
    ("grad_up", (512, 2816), jnp.bfloat16),
    ("grad_residual", (512, 1024), jnp.float32),
    ("grad_proj", (512, 1024), jnp.bfloat16),
    ("gain_grad", (8, 1024), jnp.float32),
    ("gain_row", (16, 1024), jnp.bfloat16),
)
FORWARD_OWN = (
    ("hidden", (512, 1024), jnp.bfloat16),
    ("attended", (512, 1024), jnp.bfloat16),
    ("residual", (512, 1024), jnp.float32),
    ("hidden_two", (512, 1024), jnp.bfloat16),
    ("grad_hidden_two", (512, 1024), jnp.float32),
    ("bias", (512, 512), jnp.float32),
    ("total", (512, 1024), jnp.float32),
)
OUT_COPIES = len(FORWARD_OUTS) - 3 + 3 * len(FF_CHUNKS)
KEPT = (QUERY, KEY, VALUE, OUT)


def share_shape(columns):
    return (352, 1024) if columns is None else (2, 64, columns)


def forward_kernel(items, *refs):
    refs = list(refs)

    def take(n):
        taken = refs[:n]
        del refs[:n]
        return taken

    shares = take(7)
    gain_attn, gain_ffn, tokens, cotangent, length = take(5)
    kept = take(len(KEPT))
    names = [name for name, _, _ in FORWARD_OUTS]
    outs = dict(zip(names, take(len(names))))
    full = take(7)
    full_gains, gains = take(2)
    own_names = names + [name for name, _, _ in FORWARD_OWN]
    state = dict(zip(own_names, take(len(own_names))))
    send_sems, recv_sems, own_sems, keep_sems, out_sems = refs
    outgoing = []

    def put(name, columns=None):
        source, target = state[name], outs[name]
        if columns is not None:
            source, target = source.at[:, columns], target.at[:, columns]
        outgoing.append(pltpu.make_async_copy(source, target, out_sems.at[len(outgoing)]))
        outgoing[-1].start()

    z, y, x, c = place()
    far = [lax.rem(z + k, 4) for k in range(4)]
    back = [lax.rem(z + 4 - k, 4) for k in range(4)]
    x_other, y_other, c_other = (
        device(z, y, 1 - x, c),
        device(z, 1 - y, x, c),
        device(z, y, x, 1 - c),
    )
    greet()
    wires = Wires(send_sems, recv_sems)
    own = [
        pltpu.make_async_copy(share, whole.at[z, y], own_sems.at[i])
        for i, (share, whole) in enumerate(zip(shares, full))
    ]
    own_gains = pltpu.make_async_copy(gains, full_gains.at[z, y], own_sems.at[7])
    keep = [
        pltpu.make_async_copy(full[w], kept[n], keep_sems.at[n]) for n, w in enumerate(KEPT)
    ]
    gains[...] = jnp.where(
        lax.broadcasted_iota(jnp.int32, (16, 128), 0) < 8,
        jnp.broadcast_to(gain_attn[...].astype(jnp.float32), (16, 128)),
        jnp.broadcast_to(gain_ffn[...].astype(jnp.float32), (16, 128)),
    ).astype(jnp.bfloat16)
    own_gains.start()
    gain_slot = GATHER_SLOTS * len(items)
    for k in (1, 2, 3):
        wires.send(gain_slot + k, gains, full_gains.at[z, y], device(far[k], y, x, c))
    for copy in own:
        copy.start()

    def slot(i, k):
        return GATHER_SLOTS * i + k

    def along_z(i):
        item = items[i]
        share, whole = shares[item.weight], full[item.weight]
        for k in (1, 2, 3):
            if item.no_x:
                source, target = item.half(share, (), c), item.half(whole, (z, y), c)
            else:
                source, target = item.quarter(share, (), c, x), item.quarter(whole, (z, y), c, x)
            wires.send(slot(i, k), source, target, device(far[k], y, x, c))

    own_done = set()

    def first_hop(i):
        item = items[i]
        whole = full[item.weight]
        if item.weight not in own_done:
            own[item.weight].wait()
            own_done.add(item.weight)
        for k in (1, 2, 3):
            if item.no_x:
                block = item.half(whole, (back[k], y), c)
                wires.arrived(slot(i, k), block)
                wires.send(slot(i, 7 + k), block, block, c_other)
            else:
                block = item.quarter(whole, (back[k], y), c, x)
                wires.arrived(slot(i, k), block)
                wires.send(slot(i, 3 + k), block, block, x_other)
        if item.no_x:
            block = item.half(whole, (ALL, y), c)
        else:
            block = item.quarter(whole, (ALL, y), c, x)
        wires.send(slot(i, 7), block, block, y_other)

    def second_hop(i):
        item = items[i]
        whole = full[item.weight]
        if item.no_x:
            block = item.half(whole, (ALL, 1 - y), c)
            wires.arrived(slot(i, 7), block)
            wires.send(slot(i, 11), block, block, c_other)
            return
        block = item.quarter(whole, (ALL, 1 - y), c, x)
        wires.arrived(slot(i, 7), block)
        wires.send(slot(i, 0), block, block, x_other)
        for k in (1, 2, 3):
            wires.arrived(slot(i, 3 + k), item.quarter(whole, (back[k], y), c, 1 - x))
        for k in (1, 2, 3):
            block = item.half(whole, (back[k], y), c)
            wires.send(slot(i, 7 + k), block, block, c_other)

    def last_hop(i):
        item = items[i]
        whole = full[item.weight]
        if not item.no_x:
            block = item.half(whole, (ALL, 1 - y), c)
            wires.arrived(slot(i, 0), item.quarter(whole, (ALL, 1 - y), c, 1 - x))
            wires.send(slot(i, 11), block, block, c_other)

    def complete(i):
        item = items[i]
        whole = full[item.weight]
        for k in (1, 2, 3):
            wires.arrived(slot(i, 7 + k), item.half(whole, (back[k], y), 1 - c))
        wires.arrived(slot(i, 11), item.half(whole, (ALL, 1 - y), 1 - c))

    def retire(i):
        wires.finish(lambda slot: slot // GATHER_SLOTS == i)

    step_of = Forward(
        dict(
            state,
            out=put,
            tokens=tokens,
            cotangent=cotangent,
            length=length,
            gains=full_gains,
            w_out=full[OUT],
            w_gate=full[GATE],
            w_up=full[UP],
            w_down=full[DOWN].reshape(2816, 1024),
        )
    )
    last_of = {item.weight: i for i, item in enumerate(items)}
    tasks = [(-1, 3, step_of.prepare)]
    for n, name in enumerate(("query", "key", "value")):
        tasks.append((last_of[n], 2, partial(step_of.project, full[n], state[name])))
    tasks += [(last_of[VALUE], 3, partial(step_of.attend, p, p + 2)) for p in (0, 2, 4, 6)]
    tasks.append((last_of[OUT], 3, step_of.project_out))
    for tile_of in pieces(2816, TILE):
        tasks.append((last_of[DOWN], 1, partial(step_of.grad_of_middle, *tile_of)))
    for start, size in FF_CHUNKS:
        there = max(
            i for i, item in enumerate(items) if item.weight == UP and item.start == start
        )
        for at, width in pieces(size, TILE):
            tasks.append((there, 5, partial(step_of.feed_forward, start + at, width)))
        tasks.append((there, 0, partial(step_of.flush, start, size)))

    ahead = 3
    for i in range(min(ahead, len(items))):
        along_z(i)
    own_gains.wait()
    for k in (1, 2, 3):
        wires.arrived(gain_slot + k, full_gains.at[back[k], y])
    wires.send(gain_slot, full_gains.at[:, y], full_gains.at[:, y], y_other)
    stages = (retire, complete, last_hop, second_hop, first_hop)
    lates = (3 * LAG, 3 * LAG - 1, 2 * LAG, LAG, 0)
    for step in range(len(items) + 3 * LAG):
        for late, stage in zip(lates, stages):
            if 0 <= step - late < len(items):
                stage(step - late)
        if step + ahead < len(items):
            along_z(step + ahead)
        if step == 0:
            wires.arrived(gain_slot, full_gains.at[:, 1 - y])
        there = step - lates[1]
        for n, w in enumerate(KEPT):
            if there == last_of[w]:
                keep[n].start()
        spent = 0
        while tasks and tasks[0][0] <= there and spent < 6:
            _, cost, task = tasks.pop(0)
            task()
            spent += cost
    for _, _, task in tasks:
        task()
    step_of.finish()
    for copy in keep + outgoing:
        copy.wait()
    wires.finish()


def forward(tokens, cotangent, lengths, weights, gains):
    items = gather_items()
    shares = [w.reshape(share_shape(n)) for w, n in zip(weights, COLUMNS)]
    wholes = [(4, 2) + share_shape(n) for n in COLUMNS]
    shapes = [jax.ShapeDtypeStruct(wholes[w], jnp.bfloat16) for w in KEPT]
    shapes += [jax.ShapeDtypeStruct(shape, dtype) for _, shape, dtype in FORWARD_OUTS]
    count = GATHER_SLOTS * len(items) + 4
    anywhere = pl.BlockSpec(memory_space=pl.ANY)
    in_vmem = pl.BlockSpec(memory_space=pltpu.VMEM)
    out = pl.pallas_call(
        partial(forward_kernel, items),
        out_shape=shapes,
        in_specs=[anywhere] * 7
        + [in_vmem] * 4
        + [pl.BlockSpec(memory_space=pltpu.SMEM)],
        out_specs=[anywhere] * len(shapes),
        scratch_shapes=[pltpu.VMEM(shape, jnp.bfloat16) for shape in wholes]
        + [pltpu.VMEM((4, 2, 16, 128), jnp.bfloat16), pltpu.VMEM((16, 128), jnp.bfloat16)]
        + [pltpu.VMEM(shape, dtype) for _, shape, dtype in FORWARD_OUTS + FORWARD_OWN]
        + [
            pltpu.SemaphoreType.DMA((count,)),
            pltpu.SemaphoreType.DMA((count,)),
            pltpu.SemaphoreType.DMA((8,)),
            pltpu.SemaphoreType.DMA((len(KEPT),)),
            pltpu.SemaphoreType.DMA((OUT_COPIES,)),
        ],
        compiler_params=pltpu.CompilerParams(
            collective_id=0, has_side_effects=True, vmem_limit_bytes=63 * MIB
        ),
        name="gather_forward",
    )(*shares, *[g.reshape(1, 128) for g in gains], tokens, cotangent, lengths)
    return out[: len(KEPT)], dict(zip([name for name, _, _ in FORWARD_OUTS], out[len(KEPT) :]))


SUM_SLOTS = 10
RING = 3


class Share:
    def __init__(self, weight, start, size, x_first):
        self.weight, self.start, self.size, self.x_first = weight, start, size, x_first
        self.tall = weight == DOWN
        self.width = 128 if self.tall else size // 2
        self.block = (352 if self.tall else 64, self.width)

    def columns(self, c, x):
        start = c * 512 + x * 256 + self.start if self.tall else self.start + c * self.width
        return pl.ds(pl.multiple_of(start, 128), self.width)

    def quarter(self, sums, c, x):
        if self.tall:
            return sums.at[c, x, self.start // 128]
        return sums.at[x, :, self.columns(c, x)]

    def half(self, sums, c):
        if self.tall:
            return sums.at[c, :, self.start // 128]
        return sums.at[:, :, self.columns(c, 0)]


def share_items():
    order = [(GATE, 2048, 768, True), (DOWN, 0, 128, False), (DOWN, 128, 128, True)]
    order += [(GATE, 0, 1024, False), (GATE, 1024, 1024, True)]
    order += [(UP, 0, 1024, True), (UP, 1024, 1024, False), (UP, 2048, 768, False)]
    order += [(OUT, 0, 1024, True), (QUERY, 0, 1024, False), (KEY, 0, 1024, True)]
    order += [(VALUE, 0, 768, True), (VALUE, 768, 256, False)]
    return [Share(*item) for item in order]


def plus(left, right):
    return left + right


def dot_tn(left, right):
    return lax.dot_general(
        left, right, (((0,), (0,)), ((), ())), preferred_element_type=jnp.float32
    )


BACKWARD_IN = (
    "query",
    "key",
    "value",
    "log_total",
    "hidden_t",
    "hidden_two_t",
    "attended_t",
    "branch",
    "grad_residual",
    "grad_proj",
    "gain_grad",
    "gain_row",
)


def held_names():
    return [name for name in BACKWARD_IN if name != "hidden_t"]


class Backward:
    def __init__(self, refs):
        self.__dict__.update(refs)

    def prepare(self):
        length = self.length[0, 0]
        for block in range(4):
            rows = slice(128 * block, 128 * block + 128)
            place_k = lax.broadcasted_iota(jnp.int32, (128, 512), 0) + 128 * block
            place_q = lax.broadcasted_iota(jnp.int32, (128, 512), 1)
            same = (place_q >= length) == (place_k >= length)
            allowed = same & (place_k <= place_q)
            self.bias[rows, :] = jnp.where(allowed, 0.0, NEGATIVE)

    def multiply(self, left_t, right, item, target, core):
        columns = item.columns(core, 0)

        def rows(m, _):
            product = dot(left_t[tile(m, 256), :], right[:, columns]).astype(jnp.bfloat16)
            product = product.reshape(2, 2, 64, item.width)
            for xx in (0, 1):
                target[xx, m] = product[:, xx]
            return 0

        lax.fori_loop(0, 4, rows, 0)

    def multiply_tall(self, left, right, groups):
        def rows(m, _):
            at = tile(m, 256)
            turned = left[:, at].T
            for columns, targets in groups:
                product = dot(turned, right[:, columns]).astype(jnp.bfloat16)
                for n, (target, xx) in enumerate(targets):
                    target.reshape(2, 2816, 128)[xx, at, :] = product[:, 128 * n : 128 * n + 128]
            return 0

        lax.fori_loop(0, 11, rows, 0)

    def grad_of_attended(self, j):
        part = slice(TILE * j, TILE * j + TILE)
        rows = self.w_rows[...].reshape(TILE, 1024)
        self.grad_attended[:, part] = dot_nt(self.grad_proj[...], rows).astype(jnp.bfloat16)

    def attend_back(self, first, last):
        low = jnp.bfloat16

        def pair(p, _):
            at = tile(p, 128)
            grad = self.grad_attended[:, at]
            query = (self.query[:, at].astype(jnp.float32) * SCORE_SCALE).astype(low)
            left = lax.broadcasted_iota(jnp.int32, (256, 128), 1) < HEAD
            none = jnp.zeros((256, 128), low)

            def heads(ref, count):
                parts = [ref[256 * n : 256 * n + 256, at] for n in range(count)]
                above = [jnp.where(left, part, none) for part in parts]
                below = [jnp.where(left, none, part) for part in parts]
                return jnp.concatenate(above + below, axis=0)

            def lanes(stacked, count):
                return [
                    jnp.where(
                        left,
                        stacked[256 * n : 256 * n + 256],
                        stacked[256 * (count + n) : 256 * (count + n) + 256],
                    )
                    for n in range(count)
                ]

            grad_queries, grad_keys, grad_values = [], [], []
            for block in (0, 1):
                count = block + 1
                rows, seen = slice(256 * block, 256 * block + 256), slice(0, 256 * count)
                keys, values = heads(self.key, count), heads(self.value, count)
                size = 256 * count
                held = [self.input_grad.at[seen, pl.ds(256 * n, 256)] for n in (0, 1)]
                scores = dot_nt(keys, query[rows])
                for n in (0, 1):
                    offset = self.bias[seen, rows] - self.log_total[p, n : n + 1, rows]
                    held[n][...] = jnp.exp(scores[size * n : size * n + size] + offset)
                grad_probs = dot_nt(values, grad[rows])
                grad_scores, probs = [], []
                for n in (0, 1):
                    own, grad_own = held[n][...], grad_probs[size * n : size * n + size]
                    product = grad_own * own
                    centre = jnp.sum(product, axis=0, keepdims=True)
                    grad_scores.append((product - own * centre).astype(low))
                    probs.append(own.astype(low))
                grad_scores = jnp.concatenate(grad_scores, axis=0)
                probs = jnp.concatenate(probs, axis=0)
                grad_queries.append(dot_tn(grad_scores, keys))
                grad_keys.append(lanes(dot(grad_scores, query[rows]), count))
                grad_values.append(lanes(dot(probs, grad[rows]), count))
            for block in (0, 1):
                rows = slice(256 * block, 256 * block + 256)
                self.query[rows, at] = (grad_queries[block] * SCORE_SCALE).astype(low)
                for ref, grads in ((self.key, grad_keys), (self.value, grad_values)):
                    total = grads[1][block] + grads[0][0] if block == 0 else grads[1][1]
                    ref[rows, at] = total.astype(low)
            return 0

        lax.fori_loop(first, last, pair, 0)

    def grad_hidden(self, n, j, grad):
        part = slice(TILE * j, TILE * j + TILE)
        total = dot_nt(grad[...], self.w_rows[...].reshape(TILE, 1024))
        if n == 0:
            self.input_grad[:, part] = total
        else:
            self.input_grad[:, part] += total

    def finish(self, half):
        if half == 0:
            self.gain_total[...] = jnp.zeros_like(self.gain_total)

        def rows_of(block, _):
            held = tile(block, 64)
            rows = pl.ds(pl.multiple_of(256 * half + 64 * block, 64), 64)
            values = self.tokens[rows, :].astype(jnp.float32)
            factor = lax.rsqrt(jnp.mean(values * values, axis=-1, keepdims=True) + NORM_EPS)
            normed = values * factor
            grad = self.input_grad[rows, :]
            self.gain_total[...] += jnp.sum((grad * normed).reshape(8, 8, 1024), axis=0)
            grad_normed = grad * self.gain_row[0:1, :].astype(jnp.float32)
            mean = jnp.mean(grad_normed * normed, axis=-1, keepdims=True)
            self.input_grad[rows, :] = self.grad_residual[held, :] + factor * (
                grad_normed - normed * mean
            )
            return 0

        lax.fori_loop(0, 4, rows_of, 0)
        if half == 0:
            return
        self.gain_lines[...] = jnp.zeros_like(self.gain_lines)
        lines = [jnp.sum(v[...], axis=0, keepdims=True) for v in (self.gain_total, self.gain_grad)]
        for s in range(8):
            for n, line in enumerate(lines):
                self.gain_lines[s // 2, s % 2, n : n + 1] = line[:, 128 * s : 128 * s + 128]


def backward_kernel(items, *refs):
    refs = list(refs)

    def take(n):
        taken = refs[:n]
        del refs[:n]
        return taken

    kept = take(len(KEPT))
    middle_in, grad_gate_in, grad_up_in = take(3)
    saved_in = dict(zip(BACKWARD_IN, take(len(BACKWARD_IN))))
    tokens_in, length = take(2)
    sums = take(7)
    gain_sums, input_grad_out = take(2)
    saved = dict(zip(held_names(), take(len(held_names()))))
    input_grad, wide, w_rows, bias, grad_attended, gain_total, gain_lines = take(7)
    mine, from_first, from_second, from_z = (take(len(items)) for _ in range(4))
    ring, tall_ring = take(RING), take(2)
    outbox, tall_outbox = take(2), take(2)
    gain_core, gain_x, gain_y, gain_z = take(4)
    send_sems, recv_sems, load_sems, credit = refs
    z, y, x, c = place()
    far = [lax.rem(z + k, 4) for k in range(4)]
    back = [lax.rem(z + 4 - k, 4) for k in range(4)]
    x_other, y_other, c_other = (
        device(z, y, 1 - x, c),
        device(z, 1 - y, x, c),
        device(z, y, x, 1 - c),
    )
    loads = {}

    def load(name, source, target):
        loads[name] = pltpu.make_async_copy(source, target, load_sems.at[len(loads)])
        loads[name].start()

    waited = set()

    def loaded(*names):
        for name in names:
            if name not in waited:
                loads[name].wait()
                waited.add(name)

    load("grad_gate", grad_gate_in, wide.at[1])
    load("hidden_two_t", saved_in["hidden_two_t"], saved["hidden_two_t"])
    load("middle", middle_in, wide.at[0])
    load("branch", saved_in["branch"], saved["branch"])

    def fetch(weight, j):
        load((weight, j), kept[KEPT.index(weight)].reshape(2, 4, 2, 64, 1024).at[j], w_rows)

    fetch(OUT, 0)
    for name in BACKWARD_IN:
        if name == "grad_residual":
            load(name, saved_in[name].at[0:256], saved[name])
        elif name not in loads and name != "hidden_t":
            load(name, saved_in[name], saved[name])
    greet()
    wires = Wires(send_sems, recv_sems)
    work = Backward(
        dict(
            saved,
            tokens=saved["branch"],
            length=length,
            w_rows=w_rows,
            grad_attended=grad_attended,
            bias=bias,
            input_grad=input_grad,
            gain_total=gain_total,
            gain_lines=gain_lines,
        )
    )
    tall_items = [i for i, item in enumerate(items) if item.tall]
    wide_items = [i for i, item in enumerate(items) if not item.tall]

    def slot(i, k):
        return SUM_SLOTS * i + k

    def core_slots(i):
        return (slot(i, 0), slot(i, 8))

    def from_core(i):
        if items[i].tall:
            return tall_ring[tall_items.index(i)]
        return ring[wide_items.index(i) % RING].at[..., : items[i].width]

    def produce(i):
        item = items[i]
        if item.tall:
            number = tall_items.index(i)
            if number == 0:
                loaded("middle", "branch")
                groups = []
                for core, boxes in ((1 - c, tall_outbox), (c, [mine[j] for j in tall_items])):
                    columns = pl.ds(pl.multiple_of(512 * core, 512), 512)
                    groups.append((columns, [(boxes[j], xx) for xx in (0, 1) for j in (0, 1)]))
                work.multiply_tall(wide.at[0], saved["branch"], groups)
                load("grad_up", grad_up_in, wide.at[0])
                load("tokens", tokens_in, saved["branch"])
            box = tall_outbox[number]
        else:
            number = wide_items.index(i)
            if number >= 2:
                wires.finish(lambda s: s in core_slots(wide_items[number - 2]))
            box = outbox[number % 2].at[..., : item.width]
            left, right, names = {
                GATE: (saved["hidden_two_t"], wide.at[1], ("hidden_two_t", "grad_gate")),
                UP: (saved["hidden_two_t"], wide.at[0], ("grad_up",)),
                OUT: (saved["attended_t"], saved["grad_proj"], ("attended_t", "grad_proj")),
                QUERY: (saved["hidden_two_t"], saved["query"], ("hidden_t",)),
                KEY: (saved["hidden_two_t"], saved["key"], ()),
                VALUE: (saved["hidden_two_t"], saved["value"], ()),
            }[item.weight]
            loaded(*names)
            multiply = partial(work.multiply, left, right, item)
            if number >= RING:
                pl.semaphore_wait(credit, 1)
            multiply(box, 1 - c)
        for xx in (0, 1):
            wires.send(core_slots(i)[xx], box.at[xx], from_core(i).at[xx], c_other)
        if not item.tall:
            multiply(mine[i], c)
        if i == max(j for j, other in enumerate(items) if other.weight == UP):
            load("hidden_t", saved_in["hidden_t"], saved["hidden_two_t"])

    def first_hop(i):
        item, own, other = items[i], mine[i], from_core(i)
        for xx in (0, 1):
            wires.arrived(core_slots(i)[xx], other.at[xx])

        def add(at, _):
            for xx in (0, 1):
                for yy in (0, 1):
                    own[xx, at, yy] = plus(own[xx, at, yy], other[xx, at, yy])
            return 0

        lax.fori_loop(0, 4, add, 0)
        if not item.tall and wide_items.index(i) + RING < len(wide_items):
            pl.semaphore_signal(credit, inc=1, device_id=c_other, device_id_type=MESH)
        if item.x_first:
            wires.send(slot(i, 1), own.at[1 - x], from_first[i], x_other)
        else:
            wires.send(slot(i, 1), own.at[:, :, 1 - y], from_first[i], y_other)

    def second_hop(i):
        item, own, other = items[i], mine[i], from_first[i]
        wires.arrived(slot(i, 1), other)

        def add(at, _):
            for side in (0, 1):
                if item.x_first:
                    own[x, at, side] = plus(own[x, at, side], other[at, side])
                else:
                    own[side, at, y] = plus(own[side, at, y], other[side, at])
            return 0

        lax.fori_loop(0, 4, add, 0)
        if item.x_first:
            wires.send(slot(i, 2), own.at[x, :, 1 - y], from_second[i], y_other)
        else:
            to_z(i, lambda k: own.at[:, far[k], y])

    def to_z(i, block):
        for k in (1, 2, 3):
            wires.send(slot(i, 2 + k), block(k), from_z[i].at[k - 1], device(far[k], y, x, c))

    def z_total(i, own_part):
        total = own_part.astype(jnp.float32)
        for k in (1, 2, 3):
            wires.arrived(slot(i, 2 + k), from_z[i].at[k - 1])
            total += from_z[i][k - 1].astype(jnp.float32)
        return total.astype(jnp.bfloat16)

    def third_hop(i):
        item, own, other = items[i], mine[i], from_second[i]
        if not item.x_first:
            own[:, z, y] = z_total(i, own[:, z, y])
            wires.send(slot(i, 2), own.at[:, z, y], other, x_other)
            return
        wires.arrived(slot(i, 2), other)

        def add(at, _):
            own[x, at, y] = plus(own[x, at, y], other[at])
            return 0

        lax.fori_loop(0, 4, add, 0)
        to_z(i, lambda k: own.at[x, far[k], y])

    def fourth_hop(i):
        item, own = items[i], mine[i]
        if not item.x_first:
            wires.arrived(slot(i, 2), from_second[i])
            block = item.half(sums[item.weight], c)
            block[...] = plus(own[:, z, y], from_second[i][...])
            wires.send(slot(i, 7), block, block, c_other)
            return
        block = item.quarter(sums[item.weight], c, x)
        block[...] = z_total(i, own[x, z, y])
        wires.send(slot(i, 6), block, block, x_other)

    def to_sibling(i):
        item = items[i]
        if item.x_first:
            wires.arrived(slot(i, 6), item.quarter(sums[item.weight], c, 1 - x))
            block = item.half(sums[item.weight], c)
            wires.send(slot(i, 7), block, block, c_other)

    def complete(i):
        item = items[i]
        wires.arrived(slot(i, 7), item.half(sums[item.weight], 1 - c))
        wires.finish(lambda s: s // SUM_SLOTS == i)

    base = SUM_SLOTS * len(items)

    def gains_one():
        wires.send(base, gain_lines, gain_core, c_other)

    def gains_two():
        wires.arrived(base, gain_core)
        gain_core[...] = gain_lines[...] + gain_core[...]
        wires.send(base + 1, gain_core, gain_x, x_other)

    def gains_three():
        wires.arrived(base + 1, gain_x)
        gain_x[...] = gain_core[...] + gain_x[...]
        wires.send(base + 2, gain_x.at[:, 1 - y], gain_y, y_other)

    def gains_four():
        wires.arrived(base + 2, gain_y)
        gain_y[...] = gain_x[:, y] + gain_y[...]
        for k in (1, 2, 3):
            wires.send(base + 2 + k, gain_y.at[far[k]], gain_z.at[z], device(far[k], y, x, c))
        gain_z[z] = gain_y[z]

    def gains_five():
        for k in (1, 2, 3):
            wires.arrived(base + 2 + k, gain_z.at[back[k]])
        gain_sums[...] = (gain_z[0] + gain_z[1]) + (gain_z[2] + gain_z[3])

    def prepare():
        work.prepare()
        loaded("query", "key", "value", "log_total", "grad_proj")

    turns = [(w, j) for w in (OUT, QUERY, KEY, VALUE) for j in (0, 1)]

    def use_rows(turn):
        weight, j = turns[turn]
        loaded((weight, j))
        if weight == OUT:
            work.grad_of_attended(j)
        else:
            grad = saved[("query", "key", "value")[KEPT.index(weight)]]
            work.grad_hidden(KEPT.index(weight), j, grad)
        if turn + 1 < len(turns):
            fetch(*turns[turn + 1])

    def attend_back(p):
        work.attend_back(p, p + 1)

    def finish(half):
        if half == 0:
            loaded("tokens", "grad_residual", "gain_grad", "gain_row")
        else:
            loaded("grad_residual_too")
        work.finish(half)
        if half == 0:
            load("grad_residual_too", saved_in["grad_residual"].at[256:512], saved["grad_residual"])
        else:
            load("input_grad", input_grad, input_grad_out)
            gains_one()

    beside = {1: [prepare, partial(use_rows, 0)], 3: [partial(use_rows, 1)]}
    for p in range(8):
        beside.setdefault(1 + p, []).append(partial(attend_back, p))
    for turn in range(2, len(turns)):
        beside.setdefault(8 + turn // 2, []).append(partial(use_rows, turn))
    for half in (0, 1):
        beside.setdefault(12 + half, []).append(partial(finish, half))
    for n, task in enumerate((gains_two, gains_three, gains_four, gains_five)):
        beside.setdefault(15 + 2 * n, []).append(task)

    stages = (complete, to_sibling, fourth_hop, third_hop, second_hop, first_hop, produce)
    lates = (12, 10, 8, 6, 4, 2, 0)
    for step in range(len(items) + lates[0]):
        for late, stage in zip(lates, stages):
            if 0 <= step - late < len(items):
                stage(step - late)
        for task in beside.get(step, []):
            task()
    loaded("input_grad")
    wires.finish()


def backward(tokens, lengths, kept, saved):
    items = share_items()
    low, wide = jnp.bfloat16, jnp.float32
    dtypes = {name: (shape, dtype) for name, shape, dtype in FORWARD_OUTS}
    dtypes["grad_residual"] = ((256, 1024), wide)
    shapes = [
        jax.ShapeDtypeStruct((2, 2, 2, 352, 128) if n is None else (2, 64, n), low) for n in COLUMNS
    ]
    shapes += [jax.ShapeDtypeStruct((8, 128), wide), jax.ShapeDtypeStruct((512, 1024), wide)]
    count = SUM_SLOTS * len(items) + 6
    anywhere = pl.BlockSpec(memory_space=pl.ANY)
    in_vmem = pl.BlockSpec(memory_space=pltpu.VMEM)
    n_loads = 6 + len(BACKWARD_IN) + 8

    def buffers(lead_of):
        return [pltpu.VMEM(lead_of(item) + item.block, low) for item in items]

    out = pl.pallas_call(
        partial(backward_kernel, items),
        out_shape=shapes,
        in_specs=[anywhere] * (len(KEPT) + 3 + len(BACKWARD_IN) + 1)
        + [pl.BlockSpec(memory_space=pltpu.SMEM)],
        out_specs=[in_vmem] * 8 + [anywhere],
        scratch_shapes=[pltpu.VMEM(*dtypes[name]) for name in held_names()]
        + [
            pltpu.VMEM((512, 1024), wide),
            pltpu.VMEM((2, 512, 2816), low),
            pltpu.VMEM((4, 2, 64, 1024), low),
            pltpu.VMEM((512, 512), wide),
            pltpu.VMEM((512, 1024), low),
            pltpu.VMEM((8, 1024), wide),
            pltpu.VMEM((4, 2, 8, 128), wide),
        ]
        + buffers(lambda item: (2, 4, 2))
        + buffers(lambda item: (4, 2) if item.x_first else (2, 4))
        + buffers(lambda item: (4,) if item.x_first else (2,))
        + buffers(lambda item: (3,) if item.x_first else (3, 2))
        + [pltpu.VMEM((2, 4, 2, 64, 512), low)] * RING
        + [pltpu.VMEM((2, 4, 2, 352, 128), low)] * 2
        + [pltpu.VMEM((2, 4, 2, 64, 512), low)] * 2
        + [pltpu.VMEM((2, 4, 2, 352, 128), low)] * 2
        + [
            pltpu.VMEM((4, 2, 8, 128), wide),
            pltpu.VMEM((4, 2, 8, 128), wide),
            pltpu.VMEM((4, 8, 128), wide),
            pltpu.VMEM((4, 8, 128), wide),
            pltpu.SemaphoreType.DMA((count,)),
            pltpu.SemaphoreType.DMA((count,)),
            pltpu.SemaphoreType.DMA((n_loads,)),
            pltpu.SemaphoreType.REGULAR,
        ],
        compiler_params=pltpu.CompilerParams(
            collective_id=1, has_side_effects=True, vmem_limit_bytes=63 * MIB
        ),
        name="backward_sum",
    )(
        *kept,
        saved["middle"],
        saved["grad_gate"],
        saved["grad_up"],
        *[saved[name] for name in BACKWARD_IN],
        tokens,
        lengths,
    )
    return out[:7], out[7], out[8]


def unpack_kernel(*refs):
    blocks, (gain_sums, mixed, input_grad) = refs[:7], refs[7:10]
    sums, (gain_attn, gain_ffn, mixed_out, input_out) = refs[10:17], refs[17:21]
    mixed_held, input_held, sems = refs[21:]
    routes = ((mixed, mixed_held, mixed_out), (input_grad, input_held, input_out))
    ins = [pltpu.make_async_copy(a, b, sems.at[n]) for n, (a, b, _) in enumerate(routes)]
    outs = [pltpu.make_async_copy(b, a, sems.at[2 + n]) for n, (_, b, a) in enumerate(routes)]
    for copy in ins:
        copy.start()
    for copy_in, copy_out in zip(ins, outs):
        copy_in.wait()
        copy_out.start()
    for block, total in zip(blocks[:6], sums[:6]):
        total[...] = block[...].astype(jnp.float32)
    for b in range(8):
        sums[6][:, 128 * b : 128 * b + 128] = blocks[6][b // 4, b // 2 % 2, b % 2].astype(
            jnp.float32
        )
    gain_attn[...] = gain_sums[0:1]
    gain_ffn[...] = gain_sums[1:2]
    for copy in outs:
        copy.wait()


def unpack(blocks, gain_sums, mixed, input_grad):
    wide = jnp.float32
    anywhere = pl.BlockSpec(memory_space=pl.ANY)
    in_vmem = pl.BlockSpec(memory_space=pltpu.VMEM)
    shapes = [
        jax.ShapeDtypeStruct((352, 1024) if n is None else (2, 64, n), wide) for n in COLUMNS
    ]
    shapes += [jax.ShapeDtypeStruct((1, 128), wide)] * 2
    shapes += [jax.ShapeDtypeStruct(v.shape, v.dtype) for v in (mixed, input_grad)]
    out = pl.pallas_call(
        unpack_kernel,
        out_shape=shapes,
        in_specs=[in_vmem] * 8 + [anywhere] * 2,
        out_specs=[in_vmem] * 9 + [anywhere] * 2,
        scratch_shapes=[
            pltpu.VMEM(mixed.shape, mixed.dtype),
            pltpu.VMEM(input_grad.shape, input_grad.dtype),
            pltpu.SemaphoreType.DMA((4,)),
        ],
        compiler_params=pltpu.CompilerParams(vmem_limit_bytes=63 * MIB),
        name="unpack",
    )(*blocks, gain_sums, mixed, input_grad)
    sums = [s.reshape(-1, s.shape[-1]) for s in out[:7]]
    return sums, [g.reshape(128) for g in out[7:9]], out[9], out[10]


def gather_plain(weights, gains):
    everything = (*weights, *gains)
    whole = [lax.all_gather(v, "dp", axis=0, tiled=True) for v in everything]
    return whole[: len(weights)], whole[len(weights) :]


def sum_plain(grads, gain_grads):
    shares = [
        lax.psum_scatter(g.astype(jnp.float32), "dp", scatter_dimension=0, tiled=True)
        for g in (*grads, *gain_grads)
    ]
    sums = [lax.psum(s, ("rep", "cores")) for s in shares]
    return sums[: len(grads)], sums[len(grads) :]


def on_any_device(
    tokens,
    norm_attn,
    w_query,
    w_key,
    w_value,
    w_out,
    norm_ffn,
    w_gate,
    w_up,
    w_down,
    lengths,
    cotangent,
):
    rows = tokens.shape[0]
    low = jnp.bfloat16
    allowed, valid = masks(lengths, rows)
    whole, gains = gather_plain(
        (w_query, w_key, w_value, w_out, w_gate, w_up, w_down), (norm_attn, norm_ffn)
    )
    full_query, full_key, full_value, full_out, full_gate, full_up, full_down = whole
    gain_attn, gain_ffn = gains
    inputs = tokens.astype(jnp.float32)
    normed, factor = normalize(inputs)
    hidden = (normed * gain_attn.astype(jnp.float32)).astype(low)
    query = matmul(hidden, full_query).astype(low)
    keyed = matmul(hidden, full_key).astype(low)
    valued = matmul(hidden, full_value).astype(low)
    query_groups, key_groups, value_groups = (to_groups(query), to_groups(keyed), to_groups(valued))
    attended_groups, log_total = lax.map(
        partial(attend, allowed), (query_groups, key_groups, value_groups)
    )
    attended = from_groups(attended_groups)
    residual = inputs + matmul(attended, full_out)
    normed_two, factor_two = normalize(residual)
    hidden_two = (normed_two * gain_ffn.astype(jnp.float32)).astype(low)
    gate = matmul(hidden_two, full_gate)
    upward = matmul(hidden_two, full_up)
    sigma = jax.nn.sigmoid(gate)
    middle = (gate * sigma * upward).astype(low)
    mixed = (valid[:, None] * (residual + matmul(middle, full_down))).astype(low)
    grad_output = cotangent.astype(jnp.float32) * valid[:, None]
    grad_branch = grad_output.astype(low)
    grad_down = matmul_tn(middle, grad_branch)
    grad_middle = matmul_nt(grad_branch, full_down)
    grad_gate_rows = (grad_middle * upward * sigma * (1.0 + gate * (1.0 - sigma))).astype(low)
    grad_up_rows = (grad_middle * gate * sigma).astype(low)
    grad_gate = matmul_tn(hidden_two, grad_gate_rows)
    grad_up = matmul_tn(hidden_two, grad_up_rows)
    grad_hidden_two = matmul_nt(grad_gate_rows, full_gate) + matmul_nt(grad_up_rows, full_up)
    grad_gain_ffn = jnp.sum(grad_hidden_two * normed_two, axis=0)
    grad_residual = grad_output + norm_back(
        grad_hidden_two * gain_ffn.astype(jnp.float32), normed_two, factor_two
    )
    grad_proj = grad_residual.astype(low)
    grad_out = matmul_tn(attended, grad_proj)
    grad_attended = matmul_nt(grad_proj, full_out).astype(low)
    grad_query_g, grad_key_g, grad_value_g = lax.map(
        partial(attend_back, allowed),
        (query_groups, key_groups, value_groups, to_groups(grad_attended), log_total),
    )
    grad_query_rows = from_groups(grad_query_g)
    grad_key_rows = from_groups(grad_key_g)
    grad_value_rows = from_groups(grad_value_g)
    grad_query = matmul_tn(hidden, grad_query_rows)
    grad_key = matmul_tn(hidden, grad_key_rows)
    grad_value = matmul_tn(hidden, grad_value_rows)
    grad_hidden = (
        matmul_nt(grad_query_rows, full_query)
        + matmul_nt(grad_key_rows, full_key)
        + matmul_nt(grad_value_rows, full_value)
    )
    grad_gain_attn = jnp.sum(grad_hidden * normed, axis=0)
    input_grad = grad_residual + norm_back(
        grad_hidden * gain_attn.astype(jnp.float32), normed, factor
    )
    grads = (grad_query, grad_key, grad_value, grad_out, grad_gate, grad_up, grad_down)
    sums, gain_sums = sum_plain([g.astype(low) for g in grads], (grad_gain_attn, grad_gain_ffn))
    return (
        mixed,
        input_grad,
        gain_sums[0],
        sums[0],
        sums[1],
        sums[2],
        sums[3],
        gain_sums[1],
        sums[4],
        sums[5],
        sums[6],
    )


def on_tuned_device(
    tokens,
    norm_attn,
    w_query,
    w_key,
    w_value,
    w_out,
    norm_ffn,
    w_gate,
    w_up,
    w_down,
    lengths,
    cotangent,
):
    weights = (w_query, w_key, w_value, w_out, w_gate, w_up, w_down)
    kept, saved = forward(tokens, cotangent, lengths, weights, (norm_attn, norm_ffn))
    blocks, gain_lines, input_grad = backward(tokens, lengths, kept, saved)
    sums, gain_sums, mixed, input_grad = unpack(blocks, gain_lines, saved["mixed"], input_grad)
    return (
        mixed,
        input_grad,
        gain_sums[0],
        *sums[:4],
        gain_sums[1],
        *sums[4:],
    )


def solution(mesh):
    tuned = dict(mesh.shape) == {"dp": 8, "rep": 2, "cores": 2}
    tokens_placed = P(("dp", "rep", "cores"), None)
    share, gain = P("dp", None), P("dp")
    return jax.shard_map(
        on_tuned_device if tuned else on_any_device,
        mesh=mesh,
        in_specs=(
            tokens_placed,
            gain,
            share,
            share,
            share,
            share,
            gain,
            share,
            share,
            share,
            tokens_placed,
            tokens_placed,
        ),
        out_specs=(
            tokens_placed,
            tokens_placed,
            gain,
            share,
            share,
            share,
            share,
            gain,
            share,
            share,
            share,
        ),
        check_vma=False,
    )
```

```python
from functools import partial

import jax
import jax.numpy as jnp
from jax import lax
from jax.experimental import pallas as pl
from jax.experimental.pallas import tpu as pltpu
from jax.sharding import PartitionSpec as P

HEADS = 16
HEAD = 64


NORM_EPS = 1e-05
SCORE_SCALE = 0.125
NEGATIVE = -1e30
head_group = 4
MESH = pl.DeviceIdType.MESH
MIB = 1024 * 1024


def masks(block_len, rows):
    bounds = jnp.cumsum(block_len[0])
    place = jnp.arange(rows, dtype=jnp.int32)
    segment = jnp.sum((place[:, None] >= bounds[None, :]).astype(jnp.int32), axis=1)
    allowed = (segment[:, None] == segment[None, :]) & (place[None, :] <= place[:, None])
    valid = (segment < block_len.shape[1]).astype(jnp.float32)
    return (allowed, valid)


def normalize(values):
    factor = lax.rsqrt(jnp.mean(values * values, axis=-1, keepdims=True) + NORM_EPS)
    return (values * factor, factor)


def norm_back(grad_normed, normed, factor):
    return factor * (grad_normed - normed * jnp.mean(grad_normed * normed, axis=-1, keepdims=True))


def matmul(left, right):
    return jnp.dot(left, right, preferred_element_type=jnp.float32)


def matmul_tn(left, right):
    return lax.dot_general(
        left, right, (((0,), (0,)), ((), ())), preferred_element_type=jnp.float32
    )


def matmul_nt(left, right):
    return lax.dot_general(
        left, right, (((1,), (1,)), ((), ())), preferred_element_type=jnp.float32
    )


def to_groups(matrix):
    rows = matrix.shape[0]
    split = matrix.reshape(rows, HEADS // head_group, head_group, HEAD)
    return split.transpose(1, 2, 0, 3)


def from_groups(grouped):
    rows = grouped.shape[2]
    return grouped.transpose(2, 0, 1, 3).reshape(rows, HEADS * HEAD)


def group_scores(allowed, query_g, key_g):
    raw = (
        jnp.einsum("hqe,hke->hqk", query_g, key_g, preferred_element_type=jnp.float32) * SCORE_SCALE
    )
    return jnp.where(allowed[None], raw, NEGATIVE)


def attend(allowed, operands):
    query_g, key_g, value_g = operands
    scores = group_scores(allowed, query_g, key_g)
    top = jnp.max(scores, axis=-1, keepdims=True)
    expo = jnp.exp(scores - top)
    total = jnp.sum(expo, axis=-1, keepdims=True)
    probs_low = (expo / total).astype(jnp.bfloat16)
    result = jnp.einsum("hqk,hke->hqe", probs_low, value_g, preferred_element_type=jnp.float32)
    return (result.astype(jnp.bfloat16), top[..., 0] + jnp.log(total[..., 0]))


def attend_back(allowed, operands):
    query_g, key_g, value_g, grad_g, lse = operands
    scores = group_scores(allowed, query_g, key_g)
    probs = jnp.exp(scores - lse[..., None])
    grad_probs = jnp.einsum("hqe,hke->hqk", grad_g, value_g, preferred_element_type=jnp.float32)
    centre = jnp.sum(grad_probs * probs, axis=-1, keepdims=True)
    grad_scores = (probs * (grad_probs - centre)).astype(jnp.bfloat16)
    grad_query = (
        jnp.einsum("hqk,hke->hqe", grad_scores, key_g, preferred_element_type=jnp.float32)
        * SCORE_SCALE
    )
    grad_key = (
        jnp.einsum("hqk,hqe->hke", grad_scores, query_g, preferred_element_type=jnp.float32)
        * SCORE_SCALE
    )
    grad_value = jnp.einsum(
        "hqk,hqe->hke", probs.astype(jnp.bfloat16), grad_g, preferred_element_type=jnp.float32
    )
    return (
        grad_query.astype(jnp.bfloat16),
        grad_key.astype(jnp.bfloat16),
        grad_value.astype(jnp.bfloat16),
    )


class Part:
    def __init__(self, weight, tall, start, size, no_x):
        self.weight, self.tall, self.start, self.size = weight, tall, start, size
        self.no_x = no_x

    def quarter(self, ref, lead, c, x):
        if self.tall:
            columns = pl.ds(pl.multiple_of(c * 512 + x * 256, 256), 256)
            return ref.at[(*lead, pl.ds(self.start, self.size), columns)]
        return ref.at[(*lead, x, slice(None), self.columns(c))]

    def half(self, ref, lead, c):
        if self.tall:
            columns = pl.ds(pl.multiple_of(c * 512, 512), 512)
            return ref.at[(*lead, pl.ds(self.start, self.size), columns)]
        return ref.at[(*lead, slice(None), slice(None), self.columns(c))]

    def columns(self, c):
        width = self.size // 2
        return pl.ds(pl.multiple_of(self.start + c * width, 128), width)


def pieces(total, most):
    return [(start, min(most, total - start)) for start in range(0, total, most)]


def place():
    d = lax.axis_index("dp")
    return lax.div(d, 2), lax.rem(d, 2), lax.axis_index("rep"), lax.axis_index("cores")


def device(z, y, x, c):
    return {"dp": 2 * z + y, "rep": x, "cores": c}


def greet():
    z, y, x, c = place()
    barrier = pltpu.get_barrier_semaphore()
    others = [device(lax.rem(z + k, 4), y, x, c) for k in (1, 2, 3)]
    others += [device(z, 1 - y, x, c), device(z, y, 1 - x, c), device(z, y, x, 1 - c)]
    for other in others:
        pl.semaphore_signal(barrier, inc=1, device_id=other, device_id_type=MESH)
    pl.semaphore_wait(barrier, len(others))


class Wires:
    def __init__(self, send_sems, recv_sems):
        self.send_sems, self.recv_sems = send_sems, recv_sems

    def copy(self, send_slot, recv_slot, source, target, other):
        return pltpu.make_async_remote_copy(
            src_ref=source,
            dst_ref=target,
            send_sem=self.send_sems.at[send_slot],
            recv_sem=self.recv_sems.at[recv_slot],
            device_id=other,
            device_id_type=MESH,
        )

    def send(self, send_slot, recv_slot, source, target, other):
        self.copy(send_slot, recv_slot, source, target, other).start()

    def waiter(self, slot, like):
        z, y, x, c = place()
        return self.copy(slot, slot, like, like, device(z, y, x, 1 - c))

    def arrived(self, slot, like):
        self.waiter(slot, like).wait_recv()

    def left(self, slot, like):
        self.waiter(slot, like).wait_send()


GATHER_SLOTS = 4
LAG = 2
ALL = slice(None)
COLUMNS = (1024, 1024, 1024, 1024, 2816, 2816, None)
QUERY, KEY, VALUE, OUT, GATE, UP, DOWN = range(7)
TILE = 512


FF_CHUNKS = ((0, 1024), (1024, 512), (1536, 512), (2048, 512), (2560, 256))


def gather_items():
    order = [(QUERY, 0, 256, True), (QUERY, 256, 768, False), (KEY, 0, 1024, True)]
    order += [(VALUE, 0, 1024, False), (OUT, 0, 1024, False)]
    order += [(DOWN, 0, 128, True), (DOWN, 128, 128, False), (DOWN, 256, 96, False)]
    for n, (start, size) in enumerate(FF_CHUNKS):
        order += [(GATE, start, size, n in (0, 4)), (UP, start, size, n in (2, 4))]
    return [Part(w, w == DOWN, start, size, no_x) for w, start, size, no_x in order]


def dot(left, right):
    return lax.dot_general(
        left, right, (((1,), (0,)), ((), ())), preferred_element_type=jnp.float32
    )


def dot_nt(left, right):
    return lax.dot_general(
        left, right, (((1,), (1,)), ((), ())), preferred_element_type=jnp.float32
    )


def tile(index, size):
    return pl.ds(pl.multiple_of(index * size, size), size)


def weight_columns(ref, at):
    return ref[:, :, :, :, at].reshape(1024, -1)


class Forward:
    def __init__(self, refs):
        self.__dict__.update(refs)

    def prepare(self):
        for s in range(8):
            self.gain[:, 128 * s : 128 * s + 128] = self.gains[s // 2, s % 2]
        length = self.length[0, 0]
        for block in range(4):
            rows = slice(128 * block, 128 * block + 128)
            place_q = lax.broadcasted_iota(jnp.int32, (128, 512), 0) + 128 * block
            place_k = lax.broadcasted_iota(jnp.int32, (128, 512), 1)
            same = (place_q >= length) == (place_k >= length)
            allowed = same & (place_k <= place_q)
            self.bias[rows, :] = jnp.where(allowed, 0.0, NEGATIVE)

        def normed(block, _):
            rows = tile(block, 64)
            values = self.tokens[rows, :].astype(jnp.float32)
            factor = lax.rsqrt(jnp.mean(values * values, axis=-1, keepdims=True) + NORM_EPS)
            gain = self.gain[0:1, :].astype(jnp.float32)
            self.hidden[rows, :] = (values * factor * gain).astype(jnp.bfloat16)
            place = lax.broadcasted_iota(jnp.int32, (64, 1024), 0) + 64 * block
            d_b = jnp.where(place < length, self.cotangent[rows, :].astype(jnp.float32), 0.0)
            self.d_b[rows, :] = d_b.astype(jnp.bfloat16)
            return 0

        lax.fori_loop(0, 8, normed, 0)
        self.turn(self.hidden, self.h_t)
        self.out("d_b")

    def turn(self, matrix, turned):
        def columns(n, _):
            at = tile(n, 128)
            turned[at, :] = matrix[:, at].astype(jnp.float32).T.astype(jnp.bfloat16)
            return 0

        lax.fori_loop(0, 8, columns, 0)

    def project(self, weight, result):
        def columns(n, _):
            at = tile(n, TILE)
            result[:, at] = dot(self.hidden[...], weight_columns(weight, at)).astype(jnp.bfloat16)
            return 0

        lax.fori_loop(0, 1024 // TILE, columns, 0)

    def attend(self, first, last):
        def pair(p, _):
            at = tile(p, 128)
            left = lax.broadcasted_iota(jnp.int32, (256, 128), 1) < HEAD
            for block in (0, 1):
                rows, seen = slice(256 * block, 256 * block + 256), slice(0, 256 * block + 256)
                query = self.query[rows, at].astype(jnp.float32) * SCORE_SCALE
                both = jnp.concatenate(
                    [jnp.where(left, query, 0.0), jnp.where(left, 0.0, query)], axis=0
                ).astype(jnp.bfloat16)
                bias = self.bias[rows, seen]
                scores = dot_nt(both, self.key[seen, at]) + jnp.concatenate([bias, bias], axis=0)
                top = jnp.max(scores, axis=-1, keepdims=True)
                expo = jnp.exp(scores - top)
                total = jnp.sum(expo, axis=-1, keepdims=True)
                probs = (expo * (1.0 / total)).astype(jnp.bfloat16)
                result = dot(probs, self.value[seen, at])
                self.attended[rows, at] = jnp.where(left, result[:256], result[256:]).astype(
                    jnp.bfloat16
                )
                lse = top + jnp.log(total)
                turned = jnp.where(left, lse[:256], lse[256:]).T
                self.lse[p, 0:1, rows] = turned[0:1]
                self.lse[p, 1:2, rows] = turned[HEAD : HEAD + 1]
            return 0

        lax.fori_loop(first, last, pair, 0)

    def project_out(self):
        def columns(n, _):
            at = tile(n, TILE)
            self.residual[:, at] = self.tokens[:, at].astype(jnp.float32) + dot(
                self.attended[...], weight_columns(self.w_out, at)
            )
            return 0

        lax.fori_loop(0, 1024 // TILE, columns, 0)

        def normed(block, _):
            rows = tile(block, 64)
            values = self.residual[rows, :]
            factor = lax.rsqrt(jnp.mean(values * values, axis=-1, keepdims=True) + NORM_EPS)
            gain = self.gain[8:9, :].astype(jnp.float32)
            self.h2[rows, :] = (values * factor * gain).astype(jnp.bfloat16)
            return 0

        lax.fori_loop(0, 8, normed, 0)
        self.turn(self.h2, self.h2_t)
        self.turn(self.attended, self.att_t)
        for name in ("query", "key", "value", "lse", "h_t", "h2_t", "att_t"):
            self.out(name)

    def grad_of_middle(self, start, size):
        at = pl.ds(start, size)
        self.d_up[:, at] = dot_nt(self.d_b[...], self.w_down[at, :]).astype(jnp.bfloat16)

    def feed_forward(self, start, size):
        at = pl.ds(start, size)
        low = jnp.bfloat16
        gate_w = weight_columns(self.w_gate, at)
        up_w = weight_columns(self.w_up, at)
        down_w = self.w_down[at, :]
        gate = dot(self.h2[...], gate_w)
        upward = dot(self.h2[...], up_w)
        grad_middle = self.d_up[:, at].astype(jnp.float32)
        sigma = 1.0 / (1.0 + jnp.exp(-gate))
        silu = gate * sigma
        mid = (silu * upward).astype(low)
        d_up = (grad_middle * silu).astype(low)
        d_gate = (grad_middle * upward * sigma * (1.0 + gate * (1.0 - sigma))).astype(low)
        self.mid[:, at] = mid
        self.d_up[:, at] = d_up
        self.d_gate[:, at] = d_gate
        for j in range(1024 // TILE):
            part = slice(TILE * j, TILE * j + TILE)
            mixed = dot(mid, down_w[:, part])
            grad = dot_nt(d_gate, gate_w[part, :]) + dot_nt(d_up, up_w[part, :])
            if start == 0:
                self.total[:, part] = mixed
                self.d_h2[:, part] = grad
            else:
                self.total[:, part] += mixed
                self.d_h2[:, part] += grad

    def flush(self, start, size):
        for name in ("mid", "d_gate", "d_up"):
            self.out(name, pl.ds(start, size))

    def finish(self):
        length = self.length[0, 0]
        self.g_ffn[...] = jnp.zeros_like(self.g_ffn)

        def rows_of(block, _):
            rows = tile(block, 64)
            place = lax.broadcasted_iota(jnp.int32, (64, 1024), 0) + 64 * block
            residual = self.residual[rows, :]
            mixed = jnp.where(place < length, residual + self.total[rows, :], 0.0)
            self.mixed[rows, :] = mixed.astype(jnp.bfloat16)
            factor = lax.rsqrt(jnp.mean(residual * residual, axis=-1, keepdims=True) + NORM_EPS)
            normed = residual * factor
            grad = self.d_h2[rows, :]
            self.g_ffn[...] += jnp.sum((grad * normed).reshape(8, 8, 1024), axis=0)
            grad_normed = grad * self.gain[8:9, :].astype(jnp.float32)
            grad_out = jnp.where(place < length, self.cotangent[rows, :].astype(jnp.float32), 0.0)
            mean = jnp.mean(grad_normed * normed, axis=-1, keepdims=True)
            d_res = grad_out + factor * (grad_normed - normed * mean)
            self.d_res[rows, :] = d_res
            self.d_proj[rows, :] = d_res.astype(jnp.bfloat16)
            return 0

        lax.fori_loop(0, 8, rows_of, 0)
        for name in ("mixed", "d_res", "d_proj", "g_ffn", "gain"):
            self.out(name)


FORWARD_OUTS = (
    ("mixed", (512, 1024), jnp.bfloat16),
    ("query", (512, 1024), jnp.bfloat16),
    ("key", (512, 1024), jnp.bfloat16),
    ("value", (512, 1024), jnp.bfloat16),
    ("lse", (8, 8, 512), jnp.float32),
    ("h_t", (1024, 512), jnp.bfloat16),
    ("h2_t", (1024, 512), jnp.bfloat16),
    ("att_t", (1024, 512), jnp.bfloat16),
    ("d_b", (512, 1024), jnp.bfloat16),
    ("mid", (512, 2816), jnp.bfloat16),
    ("d_gate", (512, 2816), jnp.bfloat16),
    ("d_up", (512, 2816), jnp.bfloat16),
    ("d_res", (512, 1024), jnp.float32),
    ("d_proj", (512, 1024), jnp.bfloat16),
    ("g_ffn", (8, 1024), jnp.float32),
    ("gain", (16, 1024), jnp.bfloat16),
)
FORWARD_OWN = (
    ("hidden", (512, 1024), jnp.bfloat16),
    ("attended", (512, 1024), jnp.bfloat16),
    ("residual", (512, 1024), jnp.float32),
    ("h2", (512, 1024), jnp.bfloat16),
    ("d_h2", (512, 1024), jnp.float32),
    ("bias", (512, 512), jnp.float32),
    ("total", (512, 1024), jnp.float32),
)
OUT_COPIES = len(FORWARD_OUTS) - 3 + 3 * len(FF_CHUNKS)
KEPT = (QUERY, KEY, VALUE, OUT)


def share_shape(columns):
    return (352, 1024) if columns is None else (2, 64, columns)


def forward_kernel(items, *refs):
    refs = list(refs)

    def take(n):
        taken = refs[:n]
        del refs[:n]
        return taken

    shares = take(7)
    gain_attn, gain_ffn, tokens, cotangent, length = take(5)
    kept = take(len(KEPT))
    names = [name for name, _, _ in FORWARD_OUTS]
    outs = dict(zip(names, take(len(names))))
    full = take(7)
    full_gains, gains = take(2)
    own_names = names + [name for name, _, _ in FORWARD_OWN]
    state = dict(zip(own_names, take(len(own_names))))
    send_sems, recv_sems, own_sems, keep_sems, out_sems = refs
    outgoing = []

    def put(name, columns=None):
        source, target = state[name], outs[name]
        if columns is not None:
            source, target = source.at[:, columns], target.at[:, columns]
        outgoing.append(pltpu.make_async_copy(source, target, out_sems.at[len(outgoing)]))
        outgoing[-1].start()

    z, y, x, c = place()
    far = [lax.rem(z + k, 4) for k in range(4)]
    x_other, y_other, c_other = (
        device(z, y, 1 - x, c),
        device(z, 1 - y, x, c),
        device(z, y, x, 1 - c),
    )
    greet()
    wires = Wires(send_sems, recv_sems)
    keep = [
        pltpu.make_async_copy(full[w], kept[n], keep_sems.at[n]) for n, w in enumerate(KEPT)
    ]
    gains[...] = jnp.where(
        lax.broadcasted_iota(jnp.int32, (16, 128), 0) < 8,
        jnp.broadcast_to(gain_attn[...].astype(jnp.float32), (16, 128)),
        jnp.broadcast_to(gain_ffn[...].astype(jnp.float32), (16, 128)),
    ).astype(jnp.bfloat16)
    own_gains = pltpu.make_async_copy(gains, full_gains.at[z, y], own_sems.at[len(items)])
    own_gains.start()
    gain_slot = GATHER_SLOTS * len(items)
    for k in (1, 2, 3):
        wires.send(gain_slot, gain_slot, gains, full_gains.at[z, y], device(far[k], y, x, c))

    Z, Y, X, C = range(4)

    def slot(i, k):
        return GATHER_SLOTS * i + k

    def carried(item, ref, lead):
        return item.half(ref, lead, c) if item.no_x else item.quarter(ref, lead, c, x)

    own = {}

    def along_z(i):
        item = items[i]
        source = carried(item, shares[item.weight], ())
        target = carried(item, full[item.weight], (z, y))
        for k in (1, 2, 3):
            wires.send(slot(i, Z), slot(i, Z), source, target, device(far[k], y, x, c))
        own[i] = pltpu.make_async_copy(source, target, own_sems.at[i])
        own[i].start()

    def first_hop(i):
        item = items[i]
        whole = full[item.weight]
        own[i].wait()
        wires.arrived(slot(i, Z), carried(item, whole, (pl.ds(0, 3), y)))
        block = carried(item, whole, (ALL, y))
        wires.send(slot(i, Y), slot(i, Y), block, block, y_other)

    def second_hop(i):
        item = items[i]
        whole = full[item.weight]
        wires.arrived(slot(i, Y), carried(item, whole, (ALL, 1 - y)))
        if item.no_x:
            to_core(i)
        else:
            block = carried(item, whole, (ALL, ALL))
            wires.send(slot(i, Y), slot(i, X), block, block, x_other)

    def to_core(i):
        block = items[i].half(full[items[i].weight], (ALL, ALL), c)
        wires.send(slot(i, C), slot(i, C), block, block, c_other)

    def last_hop(i):
        item = items[i]
        if not item.no_x:
            wires.arrived(
                slot(i, X), item.quarter(full[item.weight], (ALL, ALL), c, 1 - x)
            )
            to_core(i)

    def complete(i):
        wires.arrived(slot(i, C), items[i].half(full[items[i].weight], (ALL, ALL), 1 - c))

    def retire(i):
        item = items[i]
        whole = full[item.weight]
        wires.left(slot(i, Z), carried(item, whole, (pl.ds(0, 3), y)))
        block = carried(item, whole, (ALL, y)) if item.no_x else item.half(whole, (pl.ds(0, 3), ALL), c)
        wires.left(slot(i, Y), block)
        wires.left(slot(i, C), item.half(whole, (ALL, ALL), c))

    step_of = Forward(
        dict(
            state,
            out=put,
            tokens=tokens,
            cotangent=cotangent,
            length=length,
            gains=full_gains,
            w_out=full[OUT],
            w_gate=full[GATE],
            w_up=full[UP],
            w_down=full[DOWN].reshape(2816, 1024),
        )
    )
    last_of = {item.weight: i for i, item in enumerate(items)}
    tasks = [(-1, 3, step_of.prepare)]
    for n, name in enumerate(("query", "key", "value")):
        tasks.append((last_of[n], 2, partial(step_of.project, full[n], state[name])))
    tasks += [(last_of[VALUE], 3, partial(step_of.attend, p, p + 2)) for p in (0, 2, 4, 6)]
    tasks.append((last_of[OUT], 3, step_of.project_out))
    for tile_of in pieces(2816, TILE):
        tasks.append((last_of[DOWN], 1, partial(step_of.grad_of_middle, *tile_of)))
    for start, size in FF_CHUNKS:
        there = max(
            i for i, item in enumerate(items) if item.weight == UP and item.start == start
        )
        for at, width in pieces(size, TILE):
            tasks.append((there, 5, partial(step_of.feed_forward, start + at, width)))
        tasks.append((there, 0, partial(step_of.flush, start, size)))

    ahead = 3
    for i in range(min(ahead, len(items))):
        along_z(i)
    own_gains.wait()
    wires.arrived(gain_slot, full_gains.at[0:3, y])
    wires.send(gain_slot + 1, gain_slot + 1, full_gains.at[:, y], full_gains.at[:, y], y_other)
    stages = (retire, complete, last_hop, second_hop, first_hop)
    lates = (3 * LAG, 3 * LAG - 1, 2 * LAG, LAG, 0)
    for step in range(len(items) + 3 * LAG):
        for late, stage in zip(lates, stages):
            if 0 <= step - late < len(items):
                stage(step - late)
        if step + ahead < len(items):
            along_z(step + ahead)
        if step == 0:
            wires.arrived(gain_slot + 1, full_gains.at[:, 1 - y])
        there = step - lates[1]
        for n, w in enumerate(KEPT):
            if there == last_of[w]:
                keep[n].start()
        spent = 0
        while tasks and tasks[0][0] <= there and spent < 6:
            _, cost, task = tasks.pop(0)
            task()
            spent += cost
    for _, _, task in tasks:
        task()
    step_of.finish()
    for copy in keep + outgoing:
        copy.wait()
    wires.left(gain_slot, full_gains.at[0:3, y])
    wires.left(gain_slot + 1, full_gains.at[:, y])


def forward(tokens, cotangent, lengths, weights, gains):
    items = gather_items()
    shares = [w.reshape(share_shape(n)) for w, n in zip(weights, COLUMNS)]
    wholes = [(4, 2) + share_shape(n) for n in COLUMNS]
    shapes = [jax.ShapeDtypeStruct(wholes[w], jnp.bfloat16) for w in KEPT]
    shapes += [jax.ShapeDtypeStruct(shape, dtype) for _, shape, dtype in FORWARD_OUTS]
    count = GATHER_SLOTS * len(items) + 2
    anywhere = pl.BlockSpec(memory_space=pl.ANY)
    in_vmem = pl.BlockSpec(memory_space=pltpu.VMEM)
    out = pl.pallas_call(
        partial(forward_kernel, items),
        out_shape=shapes,
        in_specs=[anywhere] * 7
        + [in_vmem] * 4
        + [pl.BlockSpec(memory_space=pltpu.SMEM)],
        out_specs=[anywhere] * len(shapes),
        scratch_shapes=[pltpu.VMEM(shape, jnp.bfloat16) for shape in wholes]
        + [pltpu.VMEM((4, 2, 16, 128), jnp.bfloat16), pltpu.VMEM((16, 128), jnp.bfloat16)]
        + [pltpu.VMEM(shape, dtype) for _, shape, dtype in FORWARD_OUTS + FORWARD_OWN]
        + [
            pltpu.SemaphoreType.DMA((count,)),
            pltpu.SemaphoreType.DMA((count,)),
            pltpu.SemaphoreType.DMA((len(items) + 1,)),
            pltpu.SemaphoreType.DMA((len(KEPT),)),
            pltpu.SemaphoreType.DMA((OUT_COPIES,)),
        ],
        compiler_params=pltpu.CompilerParams(
            collective_id=0, has_side_effects=True, vmem_limit_bytes=63 * MIB
        ),
        name="gather_forward",
    )(*shares, *[g.reshape(1, 128) for g in gains], tokens, cotangent, lengths)
    return out[: len(KEPT)], dict(zip([name for name, _, _ in FORWARD_OUTS], out[len(KEPT) :]))


SUM_SLOTS = 6
RING = 4


class Share:
    def __init__(self, weight, start, size, x_first):
        self.weight, self.start, self.size, self.x_first = weight, start, size, x_first
        self.tall = weight == DOWN
        self.width = 128 if self.tall else size // 2
        self.block = (352 if self.tall else 64, self.width)

    def columns(self, c, x):
        start = c * 512 + x * 256 + self.start if self.tall else self.start + c * self.width
        return pl.ds(pl.multiple_of(start, 128), self.width)

    def quarter(self, sums, c, x):
        if self.tall:
            return sums.at[c, x, self.start // 128]
        return sums.at[x, :, self.columns(c, x)]

    def half(self, sums, c):
        if self.tall:
            return sums.at[c, :, self.start // 128]
        return sums.at[:, :, self.columns(c, 0)]


def share_items():
    order = [(GATE, 2048, 768, True), (DOWN, 0, 128, False), (DOWN, 128, 128, True)]
    order += [(GATE, 0, 1024, False), (GATE, 1024, 1024, True)]
    order += [(UP, 0, 1024, True), (UP, 1024, 1024, False), (UP, 2048, 768, False)]
    order += [(OUT, 0, 1024, True), (QUERY, 0, 1024, False), (KEY, 0, 1024, True)]
    order += [(VALUE, 0, 768, True), (VALUE, 768, 256, False)]
    return [Share(*item) for item in order]


def plus(left, right):
    return left + right


def dot_tn(left, right):
    return lax.dot_general(
        left, right, (((0,), (0,)), ((), ())), preferred_element_type=jnp.float32
    )


BACKWARD_IN = (
    "query",
    "key",
    "value",
    "lse",
    "h_t",
    "h2_t",
    "att_t",
    "d_b",
    "d_res",
    "d_proj",
    "g_ffn",
    "gain",
)


class Backward:
    def __init__(self, refs):
        self.__dict__.update(refs)

    def prepare(self):
        length = self.length[0, 0]
        for block in range(4):
            rows = slice(128 * block, 128 * block + 128)
            place_k = lax.broadcasted_iota(jnp.int32, (128, 512), 0) + 128 * block
            place_q = lax.broadcasted_iota(jnp.int32, (128, 512), 1)
            same = (place_q >= length) == (place_k >= length)
            allowed = same & (place_k <= place_q)
            self.bias[rows, :] = jnp.where(allowed, 0.0, NEGATIVE)

    def multiply(self, left_t, right, item, target, core):
        columns = item.columns(core, 0)

        def rows(m, _):
            product = dot(left_t[tile(m, 256), :], right[:, columns]).astype(jnp.bfloat16)
            product = product.reshape(2, 2, 64, item.width)
            for xx in (0, 1):
                target[xx, m] = product[:, xx]
            return 0

        lax.fori_loop(0, 4, rows, 0)

    def multiply_tall(self, left, right, groups):
        def rows(m, _):
            at = tile(m, 256)
            turned = left[:, at].T
            for columns, targets in groups:
                product = dot(turned, right[:, columns]).astype(jnp.bfloat16)
                for n, (target, xx) in enumerate(targets):
                    target.reshape(2, 2816, 128)[xx, at, :] = product[:, 128 * n : 128 * n + 128]
            return 0

        lax.fori_loop(0, 11, rows, 0)

    def attend_back(self, first, last):
        low = jnp.bfloat16

        def pair(p, _):
            at = tile(p, 128)
            w_rows = self.w_rows[p].reshape(128, 1024)
            grad = dot_nt(self.d_proj[...], w_rows).astype(low)
            query = (self.query[:, at].astype(jnp.float32) * SCORE_SCALE).astype(low)
            key, value = self.key[:, at], self.value[:, at]
            left = lax.broadcasted_iota(jnp.int32, (512, 128), 1) < HEAD
            none = jnp.zeros((512, 128), low)
            sides = [
                [jnp.where(side, v, none) for v in (query, key, value, grad)]
                for side in (left, ~left)
            ]
            grad_key, grad_value = [None, None], [None, None]
            for block in (0, 1):
                rows, seen = slice(256 * block, 256 * block + 256), slice(0, 256 * block + 256)
                grad_query = None
                parts_key, parts_value = None, None
                for n, (own_query, own_key, own_value, own_grad) in enumerate(sides):
                    self.d_in[seen, 0:256] = dot_nt(own_key[seen], query[rows])
                    self.d_in[seen, 256:512] = dot_nt(own_value[seen], grad[rows])
                    self.back_rows(p, n, rows, 256 * block + 256)
                    grad_scores, probs = self.grad_scores[seen, :], self.probs[seen, :]
                    part_query = dot_tn(grad_scores, own_key[seen])
                    part_key = dot(grad_scores, own_query[rows])
                    part_value = dot(probs, own_grad[rows])
                    if n == 0:
                        grad_query, parts_key, parts_value = part_query, part_key, part_value
                    else:
                        grad_query += part_query
                        parts_key += part_key
                        parts_value += part_value
                self.query[rows, at] = (grad_query * SCORE_SCALE).astype(low)
                if block == 0:
                    grad_key[0], grad_value[0] = parts_key, parts_value
                else:
                    grad_key = [grad_key[0] + parts_key[:256], parts_key[256:]]
                    grad_value = [grad_value[0] + parts_value[:256], parts_value[256:]]
            for block in (0, 1):
                rows = slice(256 * block, 256 * block + 256)
                self.key[rows, at] = grad_key[block].astype(low)
                self.value[rows, at] = grad_value[block].astype(low)
            return 0

        lax.fori_loop(first, last, pair, 0)

    def back_rows(self, p, n, rows, count):
        low = jnp.bfloat16
        held = self.d_in
        lse = self.lse[p, n : n + 1, rows]

        def first_pass(r, centre):
            keys = tile(r, 64)
            probs = jnp.exp(held[keys, 0:256] + self.bias[keys, rows] - lse)
            held[keys, 0:256] = probs
            self.probs[keys, :] = probs.astype(low)
            return centre + jnp.sum((held[keys, 256:512] * probs).reshape(8, 8, 256), axis=0)

        centre = lax.fori_loop(0, count // 64, first_pass, jnp.zeros((8, 256), jnp.float32), unroll=2)
        centre = jnp.sum(centre, axis=0, keepdims=True)

        def second_pass(r, _):
            keys = tile(r, 64)
            grad = held[keys, 0:256] * (held[keys, 256:512] - centre)
            self.grad_scores[keys, :] = grad.astype(low)
            return 0

        lax.fori_loop(0, count // 64, second_pass, 0, unroll=2)

    def grad_hidden(self, t):
        at = pl.ds(256 * t, 256)
        total = None
        for n, grad in enumerate((self.query, self.key, self.value)):
            part = dot_nt(grad[...], self.w_rows[2 * n : 2 * n + 2].reshape(256, 1024))
            total = part if total is None else total + part
        self.d_in[:, at] = total

    def finish(self):
        self.gain_total[...] = jnp.zeros_like(self.gain_total)

        def rows_of(block, _):
            rows = tile(block, 64)
            values = self.tokens[rows, :].astype(jnp.float32)
            factor = lax.rsqrt(jnp.mean(values * values, axis=-1, keepdims=True) + NORM_EPS)
            normed = values * factor
            grad = self.d_in[rows, :]
            self.gain_total[...] += jnp.sum((grad * normed).reshape(8, 8, 1024), axis=0)
            grad_normed = grad * self.gain[0:1, :].astype(jnp.float32)
            mean = jnp.mean(grad_normed * normed, axis=-1, keepdims=True)
            self.d_in[rows, :] = self.d_res[rows, :] + factor * (
                grad_normed - normed * mean
            )
            return 0

        lax.fori_loop(0, 8, rows_of, 0)
        self.gain_lines[...] = jnp.zeros_like(self.gain_lines)
        lines = [jnp.sum(v[...], axis=0, keepdims=True) for v in (self.gain_total, self.g_ffn)]
        for s in range(8):
            for n, line in enumerate(lines):
                self.gain_lines[s // 2, s % 2, n : n + 1] = line[:, 128 * s : 128 * s + 128]


def backward_kernel(items, *refs):
    refs = list(refs)

    def take(n):
        taken = refs[:n]
        del refs[:n]
        return taken

    kept = take(len(KEPT))
    middle_in, grad_gate_in, grad_up_in = take(3)
    saved_in = dict(zip(BACKWARD_IN, take(len(BACKWARD_IN))))
    tokens_in, length = take(2)
    sums = take(7)
    gain_sums, input_grad_out = take(2)
    saved = dict(zip(BACKWARD_IN, take(len(BACKWARD_IN))))
    d_in, wide, w_rows, bias, probs, grad_scores, gain_total, gain_lines = take(8)
    mine, from_first, from_second, from_z = (take(len(items)) for _ in range(4))
    ring, tall_ring = take(RING), take(2)
    outbox, tall_outbox = take(2), take(2)
    gain_core, gain_x, gain_y, gain_z = take(4)
    send_sems, recv_sems, load_sems, credit = refs
    z, y, x, c = place()
    far = [lax.rem(z + k, 4) for k in range(4)]
    x_other, y_other, c_other = (
        device(z, y, 1 - x, c),
        device(z, 1 - y, x, c),
        device(z, y, x, 1 - c),
    )
    loads = {}

    def load(name, source, target):
        loads[name] = pltpu.make_async_copy(source, target, load_sems.at[len(loads)])
        loads[name].start()

    waited = set()

    def loaded(*names):
        for name in names:
            if name not in waited:
                loads[name].wait()
                waited.add(name)

    load("d_gate", grad_gate_in, wide.at[1])
    load("h2_t", saved_in["h2_t"], saved["h2_t"])
    load("mid", middle_in, wide.at[0])
    load("d_b", saved_in["d_b"], saved["d_b"])
    load("w_rows", kept[OUT].reshape(8, 2, 64, 1024), w_rows)
    for name in BACKWARD_IN:
        if name not in loads:
            load(name, saved_in[name], saved[name])
    greet()
    wires = Wires(send_sems, recv_sems)
    work = Backward(
        dict(
            saved,
            tokens=saved["d_b"],
            length=length,
            w_rows=w_rows,
            probs=probs,
            grad_scores=grad_scores,
            bias=bias,
            d_in=d_in,
            gain_total=gain_total,
            gain_lines=gain_lines,
        )
    )
    tall_items = [i for i, item in enumerate(items) if item.tall]
    wide_items = [i for i, item in enumerate(items) if not item.tall]

    def slot(i, k):
        return SUM_SLOTS * i + k

    CORE, FIRST, SECOND, ALONG_Z, ALONG_X, LAST = range(6)
    MANY, LAST_SEND = FIRST, SECOND

    def from_core(i):
        if items[i].tall:
            return tall_ring[tall_items.index(i)]
        return ring[wide_items.index(i) % RING].at[..., : items[i].width]

    def produce(i):
        item = items[i]
        if item.tall:
            number = tall_items.index(i)
            if number == 0:
                loaded("mid", "d_b")
                groups = []
                for core, boxes in ((1 - c, tall_outbox), (c, [mine[j] for j in tall_items])):
                    columns = pl.ds(pl.multiple_of(512 * core, 512), 512)
                    groups.append((columns, [(boxes[j], xx) for xx in (0, 1) for j in (0, 1)]))
                work.multiply_tall(wide.at[0], saved["d_b"], groups)
                load("d_up", grad_up_in, wide.at[0])
                load("tokens", tokens_in, saved["d_b"])
            box = tall_outbox[number]
        else:
            number = wide_items.index(i)
            if number >= 2:
                before = wide_items[number - 2]
                wires.left(slot(before, CORE), from_core(before))
            box = outbox[number % 2].at[..., : item.width]
            left, right, names = {
                GATE: (saved["h2_t"], wide.at[1], ("h2_t", "d_gate")),
                UP: (saved["h2_t"], wide.at[0], ("d_up",)),
                OUT: (saved["att_t"], saved["d_proj"], ("att_t", "d_proj")),
                QUERY: (saved["h_t"], saved["query"], ("h_t",)),
                KEY: (saved["h_t"], saved["key"], ()),
                VALUE: (saved["h_t"], saved["value"], ()),
            }[item.weight]
            loaded(*names)
            multiply = partial(work.multiply, left, right, item)
            if number >= RING:
                pl.semaphore_wait(credit, 1)
            multiply(box, 1 - c)
        wires.send(slot(i, CORE), slot(i, CORE), box, from_core(i), c_other)
        if not item.tall:
            multiply(mine[i], c)

    def first_hop(i):
        item, own, other = items[i], mine[i], from_core(i)
        wires.arrived(slot(i, CORE), other)

        def add(at, _):
            for xx in (0, 1):
                for yy in (0, 1):
                    own[xx, at, yy] = plus(own[xx, at, yy], other[xx, at, yy])
            return 0

        lax.fori_loop(0, 4, add, 0)
        if not item.tall and wide_items.index(i) + RING < len(wide_items):
            pl.semaphore_signal(credit, inc=1, device_id=c_other, device_id_type=MESH)
        if item.x_first:
            block, other = own.at[1 - x], x_other
        else:
            block, other = own.at[:, :, 1 - y], y_other
        wires.send(slot(i, MANY), slot(i, FIRST), block, from_first[i], other)

    def second_hop(i):
        item, own, other = items[i], mine[i], from_first[i]
        wires.arrived(slot(i, FIRST), other)

        def add(at, _):
            for side in (0, 1):
                if item.x_first:
                    own[x, at, side] = plus(own[x, at, side], other[at, side])
                else:
                    own[side, at, y] = plus(own[side, at, y], other[side, at])
            return 0

        lax.fori_loop(0, 4, add, 0)
        if item.x_first:
            block = own.at[x, :, 1 - y]
            wires.send(slot(i, MANY), slot(i, SECOND), block, from_second[i], y_other)
        else:
            to_z(i, lambda k: own.at[:, far[k], y])

    def to_z(i, block):
        for k in (1, 2, 3):
            target = from_z[i].at[k - 1]
            wires.send(slot(i, MANY), slot(i, ALONG_Z), block(k), target, device(far[k], y, x, c))

    def z_total(i, own_part):
        total = own_part.astype(jnp.float32)
        wires.arrived(slot(i, ALONG_Z), from_z[i])
        for k in (1, 2, 3):
            total += from_z[i][k - 1].astype(jnp.float32)
        return total.astype(jnp.bfloat16)

    def third_hop(i):
        item, own, other = items[i], mine[i], from_second[i]
        if not item.x_first:
            own[:, z, y] = z_total(i, own[:, z, y])
            wires.send(slot(i, MANY), slot(i, SECOND), own.at[:, z, y], other, x_other)
            return
        wires.arrived(slot(i, SECOND), other)

        def add(at, _):
            own[x, at, y] = plus(own[x, at, y], other[at])
            return 0

        lax.fori_loop(0, 4, add, 0)
        to_z(i, lambda k: own.at[x, far[k], y])

    def fourth_hop(i):
        item, own = items[i], mine[i]
        if not item.x_first:
            wires.arrived(slot(i, SECOND), from_second[i])
            block = item.half(sums[item.weight], c)
            block[...] = plus(own[:, z, y], from_second[i][...])
            wires.send(slot(i, LAST_SEND), slot(i, LAST), block, block, c_other)
            return
        block = item.quarter(sums[item.weight], c, x)
        block[...] = z_total(i, own[x, z, y])
        wires.send(slot(i, MANY), slot(i, ALONG_X), block, block, x_other)

    def to_sibling(i):
        item = items[i]
        if item.x_first:
            wires.arrived(slot(i, ALONG_X), item.quarter(sums[item.weight], c, 1 - x))
            block = item.half(sums[item.weight], c)
            wires.send(slot(i, LAST_SEND), slot(i, LAST), block, block, c_other)

    def complete(i):
        item = items[i]
        wires.arrived(slot(i, LAST), item.half(sums[item.weight], 1 - c))
        wires.left(slot(i, MANY), mine[i])
        wires.left(slot(i, LAST_SEND), item.half(sums[item.weight], c))
        if item.tall or i in wide_items[-2:]:
            wires.left(slot(i, CORE), from_core(i))

    base = SUM_SLOTS * len(items)

    def gains_one():
        wires.send(base, base, gain_lines, gain_core, c_other)

    def gains_two():
        wires.arrived(base, gain_core)
        gain_core[...] = gain_lines[...] + gain_core[...]
        wires.send(base + 1, base + 1, gain_core, gain_x, x_other)

    def gains_three():
        wires.arrived(base + 1, gain_x)
        gain_x[...] = gain_core[...] + gain_x[...]
        wires.send(base + 2, base + 2, gain_x.at[:, 1 - y], gain_y, y_other)

    def gains_four():
        wires.arrived(base + 2, gain_y)
        gain_y[...] = gain_x[:, y] + gain_y[...]
        for k in (1, 2, 3):
            other = device(far[k], y, x, c)
            wires.send(base + 3, base + 3, gain_y.at[far[k]], gain_z.at[z], other)
        gain_z[z] = gain_y[z]

    def gains_five():
        wires.arrived(base + 3, gain_z.at[0:3])
        gain_sums[...] = (gain_z[0] + gain_z[1]) + (gain_z[2] + gain_z[3])

    def fetch_rows(t):
        for n in range(3):
            load(("rows", n, t), kept[n].at[t], w_rows.at[2 * n : 2 * n + 2])

    def attend_back(p):
        if p == 0:
            loaded("query", "key", "value", "lse", "d_proj", "w_rows")
        work.attend_back(p, p + 1)
        if p == 7:
            fetch_rows(0)

    def grad_hidden(t):
        loaded(*[("rows", n, t) for n in range(3)])
        work.grad_hidden(t)
        if t < 3:
            fetch_rows(t + 1)

    def finish():
        loaded("tokens", "d_res", "g_ffn", "gain")
        work.finish()
        load("d_in", d_in, input_grad_out)
        gains_one()

    beside = {1: [work.prepare]}
    for p in range(8):
        beside.setdefault(1 + p, []).append(partial(attend_back, p))
    for t in range(4):
        beside.setdefault(9 + t // 2, []).append(partial(grad_hidden, t))
    beside.setdefault(11, []).append(finish)
    for n, task in enumerate((gains_two, gains_three, gains_four, gains_five)):
        beside.setdefault(13 + 2 * n, []).append(task)

    stages = (complete, to_sibling, fourth_hop, third_hop, second_hop, first_hop, produce)
    lates = (12, 10, 8, 6, 4, 2, 0)
    for step in range(len(items) + lates[0]):
        for late, stage in zip(lates, stages):
            if 0 <= step - late < len(items):
                stage(step - late)
        for task in beside.get(step, []):
            task()
    loaded("d_in")
    for n, like in enumerate((gain_lines, gain_core, gain_x.at[:, 1 - y], gain_z.at[0:3])):
        wires.left(base + n, like)


def backward(tokens, lengths, kept, saved):
    items = share_items()
    low, wide = jnp.bfloat16, jnp.float32
    dtypes = {name: (shape, dtype) for name, shape, dtype in FORWARD_OUTS}
    shapes = [
        jax.ShapeDtypeStruct((2, 2, 2, 352, 128) if n is None else (2, 64, n), low) for n in COLUMNS
    ]
    shapes += [jax.ShapeDtypeStruct((8, 128), wide), jax.ShapeDtypeStruct((512, 1024), wide)]
    count = SUM_SLOTS * len(items) + 4
    anywhere = pl.BlockSpec(memory_space=pl.ANY)
    in_vmem = pl.BlockSpec(memory_space=pltpu.VMEM)
    n_loads = 6 + len(BACKWARD_IN) + 12

    def buffers(lead_of):
        return [pltpu.VMEM(lead_of(item) + item.block, low) for item in items]

    out = pl.pallas_call(
        partial(backward_kernel, items),
        out_shape=shapes,
        in_specs=[anywhere] * (len(KEPT) + 3 + len(BACKWARD_IN) + 1)
        + [pl.BlockSpec(memory_space=pltpu.SMEM)],
        out_specs=[in_vmem] * 8 + [anywhere],
        scratch_shapes=[pltpu.VMEM(*dtypes[name]) for name in BACKWARD_IN]
        + [
            pltpu.VMEM((512, 1024), wide),
            pltpu.VMEM((2, 512, 2816), low),
            pltpu.VMEM((8, 2, 64, 1024), low),
            pltpu.VMEM((512, 512), wide),
            pltpu.VMEM((512, 256), low),
            pltpu.VMEM((512, 256), low),
            pltpu.VMEM((8, 1024), wide),
            pltpu.VMEM((4, 2, 8, 128), wide),
        ]
        + buffers(lambda item: (2, 4, 2))
        + buffers(lambda item: (4, 2) if item.x_first else (2, 4))
        + buffers(lambda item: (4,) if item.x_first else (2,))
        + buffers(lambda item: (3,) if item.x_first else (3, 2))
        + [pltpu.VMEM((2, 4, 2, 64, 512), low)] * RING
        + [pltpu.VMEM((2, 4, 2, 352, 128), low)] * 2
        + [pltpu.VMEM((2, 4, 2, 64, 512), low)] * 2
        + [pltpu.VMEM((2, 4, 2, 352, 128), low)] * 2
        + [
            pltpu.VMEM((4, 2, 8, 128), wide),
            pltpu.VMEM((4, 2, 8, 128), wide),
            pltpu.VMEM((4, 8, 128), wide),
            pltpu.VMEM((4, 8, 128), wide),
            pltpu.SemaphoreType.DMA((count,)),
            pltpu.SemaphoreType.DMA((count,)),
            pltpu.SemaphoreType.DMA((n_loads,)),
            pltpu.SemaphoreType.REGULAR,
        ],
        compiler_params=pltpu.CompilerParams(
            collective_id=1, has_side_effects=True, vmem_limit_bytes=63 * MIB
        ),
        name="backward_sum",
    )(
        *kept,
        saved["mid"],
        saved["d_gate"],
        saved["d_up"],
        *[saved[name] for name in BACKWARD_IN],
        tokens,
        lengths,
    )
    return out[:7], out[7], out[8]


def unpack_kernel(*refs):
    blocks, (gain_sums, mixed, d_in) = refs[:7], refs[7:10]
    sums, (gain_attn, gain_ffn, mixed_out, input_out) = refs[10:17], refs[17:21]
    held, wide = refs[21:28], refs[28:35]
    mixed_held, input_held, in_sems, out_sems = refs[35:]
    sources = (d_in, mixed, *blocks)
    places = (input_held, mixed_held, *held)
    results = (input_held, mixed_held, *wide)
    targets = (input_out, mixed_out, *sums)
    ins = [pltpu.make_async_copy(a, b, in_sems.at[n]) for n, (a, b) in enumerate(zip(sources, places))]
    outs = [pltpu.make_async_copy(a, b, out_sems.at[n]) for n, (a, b) in enumerate(zip(results, targets))]
    order = (6, 7, 8, 2, 3, 4, 5, 0, 1)
    for n in order:
        ins[n].start()
    for n in order:
        ins[n].wait()
        if n == 8:
            for b in range(8):
                wide[6][:, 128 * b : 128 * b + 128] = held[6][b // 4, b // 2 % 2, b % 2].astype(
                    jnp.float32
                )
        elif n >= 2:
            wide[n - 2][...] = held[n - 2][...].astype(jnp.float32)
        outs[n].start()
    gain_attn[...] = gain_sums[0:1]
    gain_ffn[...] = gain_sums[1:2]
    for n in order:
        outs[n].wait()


def unpack(blocks, gain_sums, mixed, d_in):
    wide = jnp.float32
    anywhere = pl.BlockSpec(memory_space=pl.ANY)
    in_vmem = pl.BlockSpec(memory_space=pltpu.VMEM)
    shapes = [
        jax.ShapeDtypeStruct((352, 1024) if n is None else (2, 64, n), wide) for n in COLUMNS
    ]
    held = [pltpu.VMEM(b.shape, b.dtype) for b in blocks]
    held += [pltpu.VMEM(v.shape, wide) for v in shapes]
    held += [pltpu.VMEM(v.shape, v.dtype) for v in (mixed, d_in)]
    shapes += [jax.ShapeDtypeStruct((1, 128), wide)] * 2
    shapes += [jax.ShapeDtypeStruct(v.shape, v.dtype) for v in (mixed, d_in)]
    out = pl.pallas_call(
        unpack_kernel,
        out_shape=shapes,
        in_specs=[anywhere] * 7 + [in_vmem] + [anywhere] * 2,
        out_specs=[anywhere] * 7 + [in_vmem] * 2 + [anywhere] * 2,
        scratch_shapes=held + [pltpu.SemaphoreType.DMA((9,)), pltpu.SemaphoreType.DMA((9,))],
        compiler_params=pltpu.CompilerParams(vmem_limit_bytes=62 * MIB),
        name="unpack",
    )(*blocks, gain_sums, mixed, d_in)
    sums = [s.reshape(-1, s.shape[-1]) for s in out[:7]]
    return sums, [g.reshape(128) for g in out[7:9]], out[9], out[10]


def gather_plain(weights, gains):
    everything = (*weights, *gains)
    whole = [lax.all_gather(v, "dp", axis=0, tiled=True) for v in everything]
    return whole[: len(weights)], whole[len(weights) :]


def sum_plain(grads, gain_grads):
    shares = [
        lax.psum_scatter(g.astype(jnp.float32), "dp", scatter_dimension=0, tiled=True)
        for g in (*grads, *gain_grads)
    ]
    sums = [lax.psum(s, ("rep", "cores")) for s in shares]
    return sums[: len(grads)], sums[len(grads) :]


def on_any_device(
    tokens,
    norm_attn,
    w_query,
    w_key,
    w_value,
    w_out,
    norm_ffn,
    w_gate,
    w_up,
    w_down,
    lengths,
    cotangent,
):
    rows = tokens.shape[0]
    low = jnp.bfloat16
    allowed, valid = masks(lengths, rows)
    whole, gains = gather_plain(
        (w_query, w_key, w_value, w_out, w_gate, w_up, w_down), (norm_attn, norm_ffn)
    )
    full_query, full_key, full_value, full_out, full_gate, full_up, full_down = whole
    gain_attn, gain_ffn = gains
    inputs = tokens.astype(jnp.float32)
    normed, factor = normalize(inputs)
    hidden = (normed * gain_attn.astype(jnp.float32)).astype(low)
    query = matmul(hidden, full_query).astype(low)
    keyed = matmul(hidden, full_key).astype(low)
    valued = matmul(hidden, full_value).astype(low)
    query_groups, key_groups, value_groups = (to_groups(query), to_groups(keyed), to_groups(valued))
    attended_groups, log_total = lax.map(
        partial(attend, allowed), (query_groups, key_groups, value_groups)
    )
    attended = from_groups(attended_groups)
    residual = inputs + matmul(attended, full_out)
    normed_two, factor_two = normalize(residual)
    hidden_two = (normed_two * gain_ffn.astype(jnp.float32)).astype(low)
    gate = matmul(hidden_two, full_gate)
    upward = matmul(hidden_two, full_up)
    sigma = jax.nn.sigmoid(gate)
    middle = (gate * sigma * upward).astype(low)
    mixed = (valid[:, None] * (residual + matmul(middle, full_down))).astype(low)
    grad_output = cotangent.astype(jnp.float32) * valid[:, None]
    grad_branch = grad_output.astype(low)
    grad_down = matmul_tn(middle, grad_branch)
    grad_middle = matmul_nt(grad_branch, full_down)
    grad_gate_rows = (grad_middle * upward * sigma * (1.0 + gate * (1.0 - sigma))).astype(low)
    grad_up_rows = (grad_middle * gate * sigma).astype(low)
    grad_gate = matmul_tn(hidden_two, grad_gate_rows)
    grad_up = matmul_tn(hidden_two, grad_up_rows)
    grad_hidden_two = matmul_nt(grad_gate_rows, full_gate) + matmul_nt(grad_up_rows, full_up)
    grad_gain_ffn = jnp.sum(grad_hidden_two * normed_two, axis=0)
    grad_residual = grad_output + norm_back(
        grad_hidden_two * gain_ffn.astype(jnp.float32), normed_two, factor_two
    )
    grad_proj = grad_residual.astype(low)
    grad_out = matmul_tn(attended, grad_proj)
    grad_attended = matmul_nt(grad_proj, full_out).astype(low)
    grad_query_g, grad_key_g, grad_value_g = lax.map(
        partial(attend_back, allowed),
        (query_groups, key_groups, value_groups, to_groups(grad_attended), log_total),
    )
    grad_query_rows = from_groups(grad_query_g)
    grad_key_rows = from_groups(grad_key_g)
    grad_value_rows = from_groups(grad_value_g)
    grad_query = matmul_tn(hidden, grad_query_rows)
    grad_key = matmul_tn(hidden, grad_key_rows)
    grad_value = matmul_tn(hidden, grad_value_rows)
    grad_hidden = (
        matmul_nt(grad_query_rows, full_query)
        + matmul_nt(grad_key_rows, full_key)
        + matmul_nt(grad_value_rows, full_value)
    )
    grad_gain_attn = jnp.sum(grad_hidden * normed, axis=0)
    input_grad = grad_residual + norm_back(
        grad_hidden * gain_attn.astype(jnp.float32), normed, factor
    )
    grads = (grad_query, grad_key, grad_value, grad_out, grad_gate, grad_up, grad_down)
    sums, gain_sums = sum_plain([g.astype(low) for g in grads], (grad_gain_attn, grad_gain_ffn))
    return (
        mixed,
        input_grad,
        gain_sums[0],
        sums[0],
        sums[1],
        sums[2],
        sums[3],
        gain_sums[1],
        sums[4],
        sums[5],
        sums[6],
    )


def on_tuned_device(
    tokens,
    norm_attn,
    w_query,
    w_key,
    w_value,
    w_out,
    norm_ffn,
    w_gate,
    w_up,
    w_down,
    lengths,
    cotangent,
):
    weights = (w_query, w_key, w_value, w_out, w_gate, w_up, w_down)
    kept, saved = forward(tokens, cotangent, lengths, weights, (norm_attn, norm_ffn))
    blocks, gain_lines, d_in = backward(tokens, lengths, kept, saved)
    sums, gain_sums, mixed, d_in = unpack(blocks, gain_lines, saved["mixed"], d_in)
    return (
        mixed,
        d_in,
        gain_sums[0],
        *sums[:4],
        gain_sums[1],
        *sums[4:],
    )


def solution(mesh):
    tuned = dict(mesh.shape) == {"dp": 8, "rep": 2, "cores": 2}
    tokens_placed = P(("dp", "rep", "cores"), None)
    share, gain = P("dp", None), P("dp")
    return jax.shard_map(
        on_tuned_device if tuned else on_any_device,
        mesh=mesh,
        in_specs=(
            tokens_placed,
            gain,
            share,
            share,
            share,
            share,
            gain,
            share,
            share,
            share,
            tokens_placed,
            tokens_placed,
        ),
        out_specs=(
            tokens_placed,
            tokens_placed,
            gain,
            share,
            share,
            share,
            share,
            gain,
            share,
            share,
            share,
        ),
        check_vma=False,
    )
```

```python
from functools import partial

import jax
import jax.numpy as jnp
from jax import lax
from jax.experimental import pallas as pl
from jax.experimental.pallas import tpu as pltpu
from jax.sharding import PartitionSpec as P

HEADS = 16
HEAD = 64


NORM_EPS = 1e-05
SCORE_SCALE = 0.125
NEGATIVE = -1e30
head_group = 4
MESH = pl.DeviceIdType.MESH
MIB = 1024 * 1024


def masks(block_len, rows):
    bounds = jnp.cumsum(block_len[0])
    place = jnp.arange(rows, dtype=jnp.int32)
    segment = jnp.sum((place[:, None] >= bounds[None, :]).astype(jnp.int32), axis=1)
    allowed = (segment[:, None] == segment[None, :]) & (place[None, :] <= place[:, None])
    valid = (segment < block_len.shape[1]).astype(jnp.float32)
    return (allowed, valid)


def normalize(values):
    factor = lax.rsqrt(jnp.mean(values * values, axis=-1, keepdims=True) + NORM_EPS)
    return (values * factor, factor)


def norm_back(grad_normed, normed, factor):
    return factor * (grad_normed - normed * jnp.mean(grad_normed * normed, axis=-1, keepdims=True))


def matmul(left, right):
    return jnp.dot(left, right, preferred_element_type=jnp.float32)


def matmul_tn(left, right):
    return lax.dot_general(
        left, right, (((0,), (0,)), ((), ())), preferred_element_type=jnp.float32
    )


def matmul_nt(left, right):
    return lax.dot_general(
        left, right, (((1,), (1,)), ((), ())), preferred_element_type=jnp.float32
    )


def to_groups(matrix):
    rows = matrix.shape[0]
    split = matrix.reshape(rows, HEADS // head_group, head_group, HEAD)
    return split.transpose(1, 2, 0, 3)


def from_groups(grouped):
    rows = grouped.shape[2]
    return grouped.transpose(2, 0, 1, 3).reshape(rows, HEADS * HEAD)


def group_scores(allowed, query_g, key_g):
    raw = (
        jnp.einsum("hqe,hke->hqk", query_g, key_g, preferred_element_type=jnp.float32) * SCORE_SCALE
    )
    return jnp.where(allowed[None], raw, NEGATIVE)


def attend(allowed, operands):
    query_g, key_g, value_g = operands
    scores = group_scores(allowed, query_g, key_g)
    top = jnp.max(scores, axis=-1, keepdims=True)
    expo = jnp.exp(scores - top)
    total = jnp.sum(expo, axis=-1, keepdims=True)
    probs_low = (expo / total).astype(jnp.bfloat16)
    result = jnp.einsum("hqk,hke->hqe", probs_low, value_g, preferred_element_type=jnp.float32)
    return (result.astype(jnp.bfloat16), top[..., 0] + jnp.log(total[..., 0]))


def attend_back(allowed, operands):
    query_g, key_g, value_g, grad_g, lse = operands
    scores = group_scores(allowed, query_g, key_g)
    probs = jnp.exp(scores - lse[..., None])
    grad_probs = jnp.einsum("hqe,hke->hqk", grad_g, value_g, preferred_element_type=jnp.float32)
    centre = jnp.sum(grad_probs * probs, axis=-1, keepdims=True)
    grad_scores = (probs * (grad_probs - centre)).astype(jnp.bfloat16)
    grad_query = (
        jnp.einsum("hqk,hke->hqe", grad_scores, key_g, preferred_element_type=jnp.float32)
        * SCORE_SCALE
    )
    grad_key = (
        jnp.einsum("hqk,hqe->hke", grad_scores, query_g, preferred_element_type=jnp.float32)
        * SCORE_SCALE
    )
    grad_value = jnp.einsum(
        "hqk,hqe->hke", probs.astype(jnp.bfloat16), grad_g, preferred_element_type=jnp.float32
    )
    return (
        grad_query.astype(jnp.bfloat16),
        grad_key.astype(jnp.bfloat16),
        grad_value.astype(jnp.bfloat16),
    )


class Part:
    def __init__(self, weight, tall, start, size, no_x):
        self.weight, self.tall, self.start, self.size = weight, tall, start, size
        self.no_x = no_x

    def quarter(self, ref, lead, c, x):
        if self.tall:
            columns = pl.ds(pl.multiple_of(c * 512 + x * 256, 256), 256)
            return ref.at[(*lead, pl.ds(self.start, self.size), columns)]
        return ref.at[(*lead, x, slice(None), self.columns(c))]

    def half(self, ref, lead, c):
        if self.tall:
            columns = pl.ds(pl.multiple_of(c * 512, 512), 512)
            return ref.at[(*lead, pl.ds(self.start, self.size), columns)]
        return ref.at[(*lead, slice(None), slice(None), self.columns(c))]

    def columns(self, c):
        width = self.size // 2
        return pl.ds(pl.multiple_of(self.start + c * width, 128), width)


def pieces(total, most):
    return [(start, min(most, total - start)) for start in range(0, total, most)]


def place():
    d = lax.axis_index("dp")
    return lax.div(d, 2), lax.rem(d, 2), lax.axis_index("rep"), lax.axis_index("cores")


def device(z, y, x, c):
    return {"dp": 2 * z + y, "rep": x, "cores": c}


def greet():
    z, y, x, c = place()
    barrier = pltpu.get_barrier_semaphore()
    others = [device(lax.rem(z + k, 4), y, x, c) for k in (1, 2, 3)]
    others += [device(z, 1 - y, x, c), device(z, y, 1 - x, c), device(z, y, x, 1 - c)]
    for other in others:
        pl.semaphore_signal(barrier, inc=1, device_id=other, device_id_type=MESH)
    pl.semaphore_wait(barrier, len(others))


class Wires:
    def __init__(self, send_sems, recv_sems):
        self.send_sems, self.recv_sems = send_sems, recv_sems

    def copy(self, send_slot, recv_slot, source, target, other):
        return pltpu.make_async_remote_copy(
            src_ref=source,
            dst_ref=target,
            send_sem=self.send_sems.at[send_slot],
            recv_sem=self.recv_sems.at[recv_slot],
            device_id=other,
            device_id_type=MESH,
        )

    def send(self, send_slot, recv_slot, source, target, other):
        self.copy(send_slot, recv_slot, source, target, other).start()

    def waiter(self, slot, like):
        z, y, x, c = place()
        return self.copy(slot, slot, like, like, device(z, y, x, 1 - c))

    def arrived(self, slot, like):
        self.waiter(slot, like).wait_recv()

    def left(self, slot, like):
        self.waiter(slot, like).wait_send()


GATHER_SLOTS = 4
LAG = 2
ALL = slice(None)
COLUMNS = (1024, 1024, 1024, 1024, 2816, 2816, None)
QUERY, KEY, VALUE, OUT, GATE, UP, DOWN = range(7)
TILE = 512


FF_CHUNKS = ((0, 1024), (1024, 512), (1536, 512), (2048, 512), (2560, 256))


def gather_items():
    order = [(QUERY, 0, 256, True), (QUERY, 256, 768, False), (KEY, 0, 1024, True)]
    order += [(VALUE, 0, 1024, False), (OUT, 0, 1024, False)]
    order += [(DOWN, 0, 128, True), (DOWN, 128, 128, False), (DOWN, 256, 96, False)]
    for n, (start, size) in enumerate(FF_CHUNKS):
        order += [(GATE, start, size, n in (0, 4)), (UP, start, size, n in (2, 4))]
    return [Part(w, w == DOWN, start, size, no_x) for w, start, size, no_x in order]


def dot(left, right):
    return lax.dot_general(
        left, right, (((1,), (0,)), ((), ())), preferred_element_type=jnp.float32
    )


def dot_nt(left, right):
    return lax.dot_general(
        left, right, (((1,), (1,)), ((), ())), preferred_element_type=jnp.float32
    )


def tile(index, size):
    return pl.ds(pl.multiple_of(index * size, size), size)


def weight_columns(ref, at):
    return ref[:, :, :, :, at].reshape(1024, -1)


class Forward:
    def __init__(self, refs):
        self.__dict__.update(refs)

    def prepare(self):
        for s in range(8):
            self.gain[:, 128 * s : 128 * s + 128] = self.gains[s // 2, s % 2]
        length = self.length[0, 0]
        for block in range(4):
            rows = slice(128 * block, 128 * block + 128)
            place_q = lax.broadcasted_iota(jnp.int32, (128, 512), 0) + 128 * block
            place_k = lax.broadcasted_iota(jnp.int32, (128, 512), 1)
            same = (place_q >= length) == (place_k >= length)
            allowed = same & (place_k <= place_q)
            self.bias[rows, :] = jnp.where(allowed, 0.0, NEGATIVE)

        def normed(block, _):
            rows = tile(block, 64)
            values = self.tokens[rows, :].astype(jnp.float32)
            factor = lax.rsqrt(jnp.mean(values * values, axis=-1, keepdims=True) + NORM_EPS)
            gain = self.gain[0:1, :].astype(jnp.float32)
            self.hidden[rows, :] = (values * factor * gain).astype(jnp.bfloat16)
            place = lax.broadcasted_iota(jnp.int32, (64, 1024), 0) + 64 * block
            d_b = jnp.where(place < length, self.cotangent[rows, :].astype(jnp.float32), 0.0)
            self.d_b[rows, :] = d_b.astype(jnp.bfloat16)
            return 0

        lax.fori_loop(0, 8, normed, 0)
        self.turn(self.hidden, self.h_t)
        self.out("d_b")

    def turn(self, matrix, turned):
        def columns(n, _):
            at = tile(n, 128)
            turned[at, :] = matrix[:, at].astype(jnp.float32).T.astype(jnp.bfloat16)
            return 0

        lax.fori_loop(0, 8, columns, 0)

    def project(self, weight, result):
        def columns(n, _):
            at = tile(n, TILE)
            result[:, at] = dot(self.hidden[...], weight_columns(weight, at)).astype(jnp.bfloat16)
            return 0

        lax.fori_loop(0, 1024 // TILE, columns, 0)

    def attend(self, first, last):
        def pair(p, _):
            at = tile(p, 128)
            left = lax.broadcasted_iota(jnp.int32, (256, 128), 1) < HEAD
            for block in (0, 1):
                rows, seen = slice(256 * block, 256 * block + 256), slice(0, 256 * block + 256)
                query = self.query[rows, at].astype(jnp.float32) * SCORE_SCALE
                both = jnp.concatenate(
                    [jnp.where(left, query, 0.0), jnp.where(left, 0.0, query)], axis=0
                ).astype(jnp.bfloat16)
                bias = self.bias[rows, seen]
                scores = dot_nt(both, self.key[seen, at]) + jnp.concatenate([bias, bias], axis=0)
                top = jnp.max(scores, axis=-1, keepdims=True)
                expo = jnp.exp(scores - top)
                total = jnp.sum(expo, axis=-1, keepdims=True)
                probs = (expo * (1.0 / total)).astype(jnp.bfloat16)
                result = dot(probs, self.value[seen, at])
                self.attended[rows, at] = jnp.where(left, result[:256], result[256:]).astype(
                    jnp.bfloat16
                )
                lse = top + jnp.log(total)
                turned = jnp.where(left, lse[:256], lse[256:]).T
                self.lse[p, 0:1, rows] = turned[0:1]
                self.lse[p, 1:2, rows] = turned[HEAD : HEAD + 1]
            return 0

        lax.fori_loop(first, last, pair, 0)

    def project_out(self):
        def columns(n, _):
            at = tile(n, TILE)
            self.residual[:, at] = self.tokens[:, at].astype(jnp.float32) + dot(
                self.attended[...], weight_columns(self.w_out, at)
            )
            return 0

        lax.fori_loop(0, 1024 // TILE, columns, 0)

        def normed(block, _):
            rows = tile(block, 64)
            values = self.residual[rows, :]
            factor = lax.rsqrt(jnp.mean(values * values, axis=-1, keepdims=True) + NORM_EPS)
            gain = self.gain[8:9, :].astype(jnp.float32)
            self.h2[rows, :] = (values * factor * gain).astype(jnp.bfloat16)
            return 0

        lax.fori_loop(0, 8, normed, 0)
        self.turn(self.h2, self.h2_t)
        self.turn(self.attended, self.att_t)
        for name in ("query", "key", "value", "lse", "h_t", "h2_t", "att_t"):
            self.out(name)

    def grad_of_middle(self, start, size):
        at = pl.ds(start, size)
        self.d_up[:, at] = dot_nt(self.d_b[...], self.w_down[at, :]).astype(jnp.bfloat16)

    def feed_forward(self, start, size):
        at = pl.ds(start, size)
        low = jnp.bfloat16
        gate_w = weight_columns(self.w_gate, at)
        up_w = weight_columns(self.w_up, at)
        down_w = self.w_down[at, :]
        gate = dot(self.h2[...], gate_w)
        upward = dot(self.h2[...], up_w)
        grad_middle = self.d_up[:, at].astype(jnp.float32)
        sigma = 1.0 / (1.0 + jnp.exp(-gate))
        silu = gate * sigma
        mid = (silu * upward).astype(low)
        d_up = (grad_middle * silu).astype(low)
        d_gate = (grad_middle * upward * sigma * (1.0 + gate * (1.0 - sigma))).astype(low)
        self.mid[:, at] = mid
        self.d_up[:, at] = d_up
        self.d_gate[:, at] = d_gate
        for j in range(1024 // TILE):
            part = slice(TILE * j, TILE * j + TILE)
            mixed = dot(mid, down_w[:, part])
            grad = dot_nt(d_gate, gate_w[part, :]) + dot_nt(d_up, up_w[part, :])
            if start == 0:
                self.total[:, part] = mixed
                self.d_h2[:, part] = grad
            else:
                self.total[:, part] += mixed
                self.d_h2[:, part] += grad

    def flush(self, start, size):
        for name in ("mid", "d_gate", "d_up"):
            self.out(name, pl.ds(start, size))

    def finish(self):
        length = self.length[0, 0]
        self.g_ffn[...] = jnp.zeros_like(self.g_ffn)

        def rows_of(block, _):
            rows = tile(block, 64)
            place = lax.broadcasted_iota(jnp.int32, (64, 1024), 0) + 64 * block
            residual = self.residual[rows, :]
            mixed = jnp.where(place < length, residual + self.total[rows, :], 0.0)
            self.mixed[rows, :] = mixed.astype(jnp.bfloat16)
            factor = lax.rsqrt(jnp.mean(residual * residual, axis=-1, keepdims=True) + NORM_EPS)
            normed = residual * factor
            grad = self.d_h2[rows, :]
            self.g_ffn[...] += jnp.sum((grad * normed).reshape(8, 8, 1024), axis=0)
            grad_normed = grad * self.gain[8:9, :].astype(jnp.float32)
            grad_out = jnp.where(place < length, self.cotangent[rows, :].astype(jnp.float32), 0.0)
            mean = jnp.mean(grad_normed * normed, axis=-1, keepdims=True)
            d_res = grad_out + factor * (grad_normed - normed * mean)
            self.d_res[rows, :] = d_res
            self.d_proj[rows, :] = d_res.astype(jnp.bfloat16)
            return 0

        lax.fori_loop(0, 8, rows_of, 0)
        for name in ("mixed", "d_res", "d_proj", "g_ffn", "gain"):
            self.out(name)


FORWARD_OUTS = (
    ("mixed", (512, 1024), jnp.bfloat16),
    ("query", (512, 1024), jnp.bfloat16),
    ("key", (512, 1024), jnp.bfloat16),
    ("value", (512, 1024), jnp.bfloat16),
    ("lse", (8, 8, 512), jnp.float32),
    ("h_t", (1024, 512), jnp.bfloat16),
    ("h2_t", (1024, 512), jnp.bfloat16),
    ("att_t", (1024, 512), jnp.bfloat16),
    ("d_b", (512, 1024), jnp.bfloat16),
    ("mid", (512, 2816), jnp.bfloat16),
    ("d_gate", (512, 2816), jnp.bfloat16),
    ("d_up", (512, 2816), jnp.bfloat16),
    ("d_res", (512, 1024), jnp.float32),
    ("d_proj", (512, 1024), jnp.bfloat16),
    ("g_ffn", (8, 1024), jnp.float32),
    ("gain", (16, 1024), jnp.bfloat16),
)
FORWARD_OWN = (
    ("hidden", (512, 1024), jnp.bfloat16),
    ("attended", (512, 1024), jnp.bfloat16),
    ("residual", (512, 1024), jnp.float32),
    ("h2", (512, 1024), jnp.bfloat16),
    ("d_h2", (512, 1024), jnp.float32),
    ("bias", (512, 512), jnp.float32),
    ("total", (512, 1024), jnp.float32),
)
OUT_COPIES = len(FORWARD_OUTS) - 3 + 3 * len(FF_CHUNKS)
KEPT = (QUERY, KEY, VALUE, OUT)


def share_shape(columns):
    return (352, 1024) if columns is None else (2, 64, columns)


def forward_kernel(items, *refs):
    refs = list(refs)

    def take(n):
        taken = refs[:n]
        del refs[:n]
        return taken

    shares = take(7)
    gain_attn, gain_ffn, tokens, cotangent, length = take(5)
    kept = take(len(KEPT))
    names = [name for name, _, _ in FORWARD_OUTS]
    outs = dict(zip(names, take(len(names))))
    full = take(7)
    full_gains, gains = take(2)
    own_names = names + [name for name, _, _ in FORWARD_OWN]
    state = dict(zip(own_names, take(len(own_names))))
    send_sems, recv_sems, own_sems, keep_sems, out_sems = refs
    outgoing = []

    def put(name, columns=None):
        source, target = state[name], outs[name]
        if columns is not None:
            source, target = source.at[:, columns], target.at[:, columns]
        outgoing.append(pltpu.make_async_copy(source, target, out_sems.at[len(outgoing)]))
        outgoing[-1].start()

    z, y, x, c = place()
    far = [lax.rem(z + k, 4) for k in range(4)]
    x_other, y_other, c_other = (
        device(z, y, 1 - x, c),
        device(z, 1 - y, x, c),
        device(z, y, x, 1 - c),
    )
    greet()
    wires = Wires(send_sems, recv_sems)
    keep = [
        pltpu.make_async_copy(full[w], kept[n], keep_sems.at[n]) for n, w in enumerate(KEPT)
    ]
    gains[...] = jnp.where(
        lax.broadcasted_iota(jnp.int32, (16, 128), 0) < 8,
        jnp.broadcast_to(gain_attn[...].astype(jnp.float32), (16, 128)),
        jnp.broadcast_to(gain_ffn[...].astype(jnp.float32), (16, 128)),
    ).astype(jnp.bfloat16)
    own_gains = pltpu.make_async_copy(gains, full_gains.at[z, y], own_sems.at[len(items)])
    own_gains.start()
    gain_slot = GATHER_SLOTS * len(items)
    for k in (1, 2, 3):
        wires.send(gain_slot, gain_slot, gains, full_gains.at[z, y], device(far[k], y, x, c))

    Z, Y, X, C = range(4)

    def slot(i, k):
        return GATHER_SLOTS * i + k

    def carried(item, ref, lead):
        return item.half(ref, lead, c) if item.no_x else item.quarter(ref, lead, c, x)

    own = {}

    def along_z(i):
        item = items[i]
        source = carried(item, shares[item.weight], ())
        target = carried(item, full[item.weight], (z, y))
        for k in (1, 2, 3):
            wires.send(slot(i, Z), slot(i, Z), source, target, device(far[k], y, x, c))
        own[i] = pltpu.make_async_copy(source, target, own_sems.at[i])
        own[i].start()

    def first_hop(i):
        item = items[i]
        whole = full[item.weight]
        own[i].wait()
        wires.arrived(slot(i, Z), carried(item, whole, (pl.ds(0, 3), y)))
        for zz in range(4):
            block = carried(item, whole, (zz, y))
            wires.send(slot(i, Y), slot(i, Y), block, block, y_other)

    def second_hop(i):
        item = items[i]
        whole = full[item.weight]
        wires.arrived(slot(i, Y), carried(item, whole, (ALL, 1 - y)))
        if item.no_x:
            to_core(i)
        else:
            for zz in range(4):
                block = carried(item, whole, (zz, ALL))
                wires.send(slot(i, Y), slot(i, X), block, block, x_other)

    def to_core(i):
        for zz in range(4):
            block = items[i].half(full[items[i].weight], (zz, ALL), c)
            wires.send(slot(i, C), slot(i, C), block, block, c_other)

    def last_hop(i):
        item = items[i]
        if not item.no_x:
            wires.arrived(
                slot(i, X), item.quarter(full[item.weight], (ALL, ALL), c, 1 - x)
            )
            to_core(i)

    def complete(i):
        wires.arrived(slot(i, C), items[i].half(full[items[i].weight], (ALL, ALL), 1 - c))

    def retire(i):
        item = items[i]
        whole = full[item.weight]
        wires.left(slot(i, Z), carried(item, whole, (pl.ds(0, 3), y)))
        block = carried(item, whole, (ALL, y)) if item.no_x else item.half(whole, (pl.ds(0, 3), ALL), c)
        wires.left(slot(i, Y), block)
        wires.left(slot(i, C), item.half(whole, (ALL, ALL), c))

    step_of = Forward(
        dict(
            state,
            out=put,
            tokens=tokens,
            cotangent=cotangent,
            length=length,
            gains=full_gains,
            w_out=full[OUT],
            w_gate=full[GATE],
            w_up=full[UP],
            w_down=full[DOWN].reshape(2816, 1024),
        )
    )
    last_of = {item.weight: i for i, item in enumerate(items)}
    tasks = [(-1, 3, step_of.prepare)]
    for n, name in enumerate(("query", "key", "value")):
        tasks.append((last_of[n], 2, partial(step_of.project, full[n], state[name])))
    tasks += [(last_of[VALUE], 3, partial(step_of.attend, p, p + 2)) for p in (0, 2, 4, 6)]
    tasks.append((last_of[OUT], 3, step_of.project_out))
    for tile_of in pieces(2816, TILE):
        tasks.append((last_of[DOWN], 1, partial(step_of.grad_of_middle, *tile_of)))
    for start, size in FF_CHUNKS:
        there = max(
            i for i, item in enumerate(items) if item.weight == UP and item.start == start
        )
        for at, width in pieces(size, TILE):
            tasks.append((there, 5, partial(step_of.feed_forward, start + at, width)))
        tasks.append((there, 0, partial(step_of.flush, start, size)))

    ahead = 3
    for i in range(min(ahead, len(items))):
        along_z(i)
    own_gains.wait()
    wires.arrived(gain_slot, full_gains.at[0:3, y])
    wires.send(gain_slot + 1, gain_slot + 1, full_gains.at[:, y], full_gains.at[:, y], y_other)
    stages = (retire, complete, last_hop, second_hop, first_hop)
    lates = (3 * LAG, 3 * LAG - 1, 2 * LAG, LAG, 0)
    for step in range(len(items) + 3 * LAG):
        for late, stage in zip(lates, stages):
            if 0 <= step - late < len(items):
                stage(step - late)
        if step + ahead < len(items):
            along_z(step + ahead)
        if step == 0:
            wires.arrived(gain_slot + 1, full_gains.at[:, 1 - y])
        there = step - lates[1]
        for n, w in enumerate(KEPT):
            if there == last_of[w]:
                keep[n].start()
        spent = 0
        while tasks and tasks[0][0] <= there and spent < 6:
            _, cost, task = tasks.pop(0)
            task()
            spent += cost
    for _, _, task in tasks:
        task()
    step_of.finish()
    for copy in keep + outgoing:
        copy.wait()
    wires.left(gain_slot, full_gains.at[0:3, y])
    wires.left(gain_slot + 1, full_gains.at[:, y])


def forward(tokens, cotangent, lengths, weights, gains):
    items = gather_items()
    shares = [w.reshape(share_shape(n)) for w, n in zip(weights, COLUMNS)]
    wholes = [(4, 2) + share_shape(n) for n in COLUMNS]
    shapes = [jax.ShapeDtypeStruct(wholes[w], jnp.bfloat16) for w in KEPT]
    shapes += [jax.ShapeDtypeStruct(shape, dtype) for _, shape, dtype in FORWARD_OUTS]
    count = GATHER_SLOTS * len(items) + 2
    anywhere = pl.BlockSpec(memory_space=pl.ANY)
    in_vmem = pl.BlockSpec(memory_space=pltpu.VMEM)
    out = pl.pallas_call(
        partial(forward_kernel, items),
        out_shape=shapes,
        in_specs=[anywhere] * 7
        + [in_vmem] * 4
        + [pl.BlockSpec(memory_space=pltpu.SMEM)],
        out_specs=[anywhere] * len(shapes),
        scratch_shapes=[pltpu.VMEM(shape, jnp.bfloat16) for shape in wholes]
        + [pltpu.VMEM((4, 2, 16, 128), jnp.bfloat16), pltpu.VMEM((16, 128), jnp.bfloat16)]
        + [pltpu.VMEM(shape, dtype) for _, shape, dtype in FORWARD_OUTS + FORWARD_OWN]
        + [
            pltpu.SemaphoreType.DMA((count,)),
            pltpu.SemaphoreType.DMA((count,)),
            pltpu.SemaphoreType.DMA((len(items) + 1,)),
            pltpu.SemaphoreType.DMA((len(KEPT),)),
            pltpu.SemaphoreType.DMA((OUT_COPIES,)),
        ],
        compiler_params=pltpu.CompilerParams(
            collective_id=0, has_side_effects=True, vmem_limit_bytes=63 * MIB
        ),
        name="gather_forward",
    )(*shares, *[g.reshape(1, 128) for g in gains], tokens, cotangent, lengths)
    return out[: len(KEPT)], dict(zip([name for name, _, _ in FORWARD_OUTS], out[len(KEPT) :]))


SUM_SLOTS = 6
RING = 4


class Share:
    def __init__(self, weight, start, size, x_first):
        self.weight, self.start, self.size, self.x_first = weight, start, size, x_first
        self.tall = weight == DOWN
        self.width = 128 if self.tall else size // 2
        self.block = (352 if self.tall else 64, self.width)

    def columns(self, c, x):
        start = c * 512 + x * 256 + self.start if self.tall else self.start + c * self.width
        return pl.ds(pl.multiple_of(start, 128), self.width)

    def quarter(self, sums, c, x):
        if self.tall:
            return sums.at[c, x, self.start // 128]
        return sums.at[x, :, self.columns(c, x)]

    def half(self, sums, c):
        if self.tall:
            return sums.at[c, :, self.start // 128]
        return sums.at[:, :, self.columns(c, 0)]


def share_items():
    order = [(GATE, 2048, 768, True), (DOWN, 0, 128, False), (DOWN, 128, 128, True)]
    order += [(GATE, 0, 1024, False), (GATE, 1024, 1024, True)]
    order += [(UP, 0, 1024, True), (UP, 1024, 1024, False), (UP, 2048, 768, False)]
    order += [(OUT, 0, 1024, True), (QUERY, 0, 1024, False), (KEY, 0, 1024, True)]
    order += [(VALUE, 0, 768, True), (VALUE, 768, 256, False)]
    return [Share(*item) for item in order]


def plus(left, right):
    return left + right


def dot_tn(left, right):
    return lax.dot_general(
        left, right, (((0,), (0,)), ((), ())), preferred_element_type=jnp.float32
    )


BACKWARD_IN = (
    "query",
    "key",
    "value",
    "lse",
    "h_t",
    "h2_t",
    "att_t",
    "d_b",
    "d_res",
    "d_proj",
    "g_ffn",
    "gain",
)


class Backward:
    def __init__(self, refs):
        self.__dict__.update(refs)

    def prepare(self):
        length = self.length[0, 0]
        for block in range(4):
            rows = slice(128 * block, 128 * block + 128)
            place_k = lax.broadcasted_iota(jnp.int32, (128, 512), 0) + 128 * block
            place_q = lax.broadcasted_iota(jnp.int32, (128, 512), 1)
            same = (place_q >= length) == (place_k >= length)
            allowed = same & (place_k <= place_q)
            self.bias[rows, :] = jnp.where(allowed, 0.0, NEGATIVE)

    def multiply(self, left_t, right, item, target, core):
        columns = item.columns(core, 0)

        def rows(m, _):
            product = dot(left_t[tile(m, 256), :], right[:, columns]).astype(jnp.bfloat16)
            product = product.reshape(2, 2, 64, item.width)
            for xx in (0, 1):
                target[xx, m] = product[:, xx]
            return 0

        lax.fori_loop(0, 4, rows, 0)

    def multiply_tall(self, left, right, groups):
        def rows(m, _):
            at = tile(m, 256)
            turned = left[:, at].T
            for columns, targets in groups:
                product = dot(turned, right[:, columns]).astype(jnp.bfloat16)
                for n, (target, xx) in enumerate(targets):
                    target.reshape(2, 2816, 128)[xx, at, :] = product[:, 128 * n : 128 * n + 128]
            return 0

        lax.fori_loop(0, 11, rows, 0)

    def attend_back(self, first, last):
        low = jnp.bfloat16

        def pair(p, _):
            at = tile(p, 128)
            w_rows = self.w_rows[p].reshape(128, 1024)
            grad = dot_nt(self.d_proj[...], w_rows).astype(low)
            query = (self.query[:, at].astype(jnp.float32) * SCORE_SCALE).astype(low)
            key, value = self.key[:, at], self.value[:, at]
            left = lax.broadcasted_iota(jnp.int32, (512, 128), 1) < HEAD
            none = jnp.zeros((512, 128), low)
            sides = [
                [jnp.where(side, v, none) for v in (query, key, value, grad)]
                for side in (left, ~left)
            ]
            grad_key, grad_value = [None, None], [None, None]
            for block in (0, 1):
                rows, seen = slice(256 * block, 256 * block + 256), slice(0, 256 * block + 256)
                grad_query = None
                parts_key, parts_value = None, None
                for n, (own_query, own_key, own_value, own_grad) in enumerate(sides):
                    self.d_in[seen, 0:256] = dot_nt(own_key[seen], query[rows])
                    self.d_in[seen, 256:512] = dot_nt(own_value[seen], grad[rows])
                    self.back_rows(p, n, rows, 256 * block + 256)
                    grad_scores, probs = self.grad_scores[seen, :], self.probs[seen, :]
                    part_query = dot_tn(grad_scores, own_key[seen])
                    part_key = dot(grad_scores, own_query[rows])
                    part_value = dot(probs, own_grad[rows])
                    if n == 0:
                        grad_query, parts_key, parts_value = part_query, part_key, part_value
                    else:
                        grad_query += part_query
                        parts_key += part_key
                        parts_value += part_value
                self.query[rows, at] = (grad_query * SCORE_SCALE).astype(low)
                if block == 0:
                    grad_key[0], grad_value[0] = parts_key, parts_value
                else:
                    grad_key = [grad_key[0] + parts_key[:256], parts_key[256:]]
                    grad_value = [grad_value[0] + parts_value[:256], parts_value[256:]]
            for block in (0, 1):
                rows = slice(256 * block, 256 * block + 256)
                self.key[rows, at] = grad_key[block].astype(low)
                self.value[rows, at] = grad_value[block].astype(low)
            return 0

        lax.fori_loop(first, last, pair, 0)

    def back_rows(self, p, n, rows, count):
        low = jnp.bfloat16
        held = self.d_in
        lse = self.lse[p, n : n + 1, rows]

        def first_pass(r, centre):
            keys = tile(r, 64)
            probs = jnp.exp(held[keys, 0:256] + self.bias[keys, rows] - lse)
            held[keys, 0:256] = probs
            self.probs[keys, :] = probs.astype(low)
            return centre + jnp.sum((held[keys, 256:512] * probs).reshape(8, 8, 256), axis=0)

        centre = lax.fori_loop(0, count // 64, first_pass, jnp.zeros((8, 256), jnp.float32), unroll=2)
        centre = jnp.sum(centre, axis=0, keepdims=True)

        def second_pass(r, _):
            keys = tile(r, 64)
            grad = held[keys, 0:256] * (held[keys, 256:512] - centre)
            self.grad_scores[keys, :] = grad.astype(low)
            return 0

        lax.fori_loop(0, count // 64, second_pass, 0, unroll=2)

    def grad_hidden(self, t):
        at = pl.ds(256 * t, 256)
        total = None
        for n, grad in enumerate((self.query, self.key, self.value)):
            part = dot_nt(grad[...], self.w_rows[2 * n : 2 * n + 2].reshape(256, 1024))
            total = part if total is None else total + part
        self.d_in[:, at] = total

    def finish(self):
        self.gain_total[...] = jnp.zeros_like(self.gain_total)

        def rows_of(block, _):
            rows = tile(block, 64)
            values = self.tokens[rows, :].astype(jnp.float32)
            factor = lax.rsqrt(jnp.mean(values * values, axis=-1, keepdims=True) + NORM_EPS)
            normed = values * factor
            grad = self.d_in[rows, :]
            self.gain_total[...] += jnp.sum((grad * normed).reshape(8, 8, 1024), axis=0)
            grad_normed = grad * self.gain[0:1, :].astype(jnp.float32)
            mean = jnp.mean(grad_normed * normed, axis=-1, keepdims=True)
            self.d_in[rows, :] = self.d_res[rows, :] + factor * (
                grad_normed - normed * mean
            )
            return 0

        lax.fori_loop(0, 8, rows_of, 0)
        self.gain_lines[...] = jnp.zeros_like(self.gain_lines)
        lines = [jnp.sum(v[...], axis=0, keepdims=True) for v in (self.gain_total, self.g_ffn)]
        for s in range(8):
            for n, line in enumerate(lines):
                self.gain_lines[s // 2, s % 2, n : n + 1] = line[:, 128 * s : 128 * s + 128]


def backward_kernel(items, *refs):
    refs = list(refs)

    def take(n):
        taken = refs[:n]
        del refs[:n]
        return taken

    kept = take(len(KEPT))
    middle_in, grad_gate_in, grad_up_in = take(3)
    saved_in = dict(zip(BACKWARD_IN, take(len(BACKWARD_IN))))
    tokens_in, length = take(2)
    sums = take(7)
    gain_sums, input_grad_out = take(2)
    saved = dict(zip(BACKWARD_IN, take(len(BACKWARD_IN))))
    d_in, wide, w_rows, bias, probs, grad_scores, gain_total, gain_lines = take(8)
    mine, from_first, from_second, from_z = (take(len(items)) for _ in range(4))
    ring, tall_ring = take(RING), take(2)
    outbox, tall_outbox = take(2), take(2)
    gain_core, gain_x, gain_y, gain_z = take(4)
    send_sems, recv_sems, load_sems, credit = refs
    z, y, x, c = place()
    far = [lax.rem(z + k, 4) for k in range(4)]
    x_other, y_other, c_other = (
        device(z, y, 1 - x, c),
        device(z, 1 - y, x, c),
        device(z, y, x, 1 - c),
    )
    loads = {}

    def load(name, source, target):
        loads[name] = pltpu.make_async_copy(source, target, load_sems.at[len(loads)])
        loads[name].start()

    waited = set()

    def loaded(*names):
        for name in names:
            if name not in waited:
                loads[name].wait()
                waited.add(name)

    load("d_gate", grad_gate_in, wide.at[1])
    load("h2_t", saved_in["h2_t"], saved["h2_t"])
    load("mid", middle_in, wide.at[0])
    load("d_b", saved_in["d_b"], saved["d_b"])
    load("w_rows", kept[OUT].reshape(8, 2, 64, 1024), w_rows)
    for name in BACKWARD_IN:
        if name not in loads:
            load(name, saved_in[name], saved[name])
    greet()
    wires = Wires(send_sems, recv_sems)
    work = Backward(
        dict(
            saved,
            tokens=saved["d_b"],
            length=length,
            w_rows=w_rows,
            probs=probs,
            grad_scores=grad_scores,
            bias=bias,
            d_in=d_in,
            gain_total=gain_total,
            gain_lines=gain_lines,
        )
    )
    tall_items = [i for i, item in enumerate(items) if item.tall]
    wide_items = [i for i, item in enumerate(items) if not item.tall]

    def slot(i, k):
        return SUM_SLOTS * i + k

    CORE, FIRST, SECOND, ALONG_Z, ALONG_X, LAST = range(6)
    MANY, LAST_SEND = FIRST, SECOND

    def from_core(i):
        if items[i].tall:
            return tall_ring[tall_items.index(i)]
        return ring[wide_items.index(i) % RING].at[..., : items[i].width]

    def produce(i):
        item = items[i]
        if item.tall:
            number = tall_items.index(i)
            if number == 0:
                loaded("mid", "d_b")
                groups = []
                for core, boxes in ((1 - c, tall_outbox), (c, [mine[j] for j in tall_items])):
                    columns = pl.ds(pl.multiple_of(512 * core, 512), 512)
                    groups.append((columns, [(boxes[j], xx) for xx in (0, 1) for j in (0, 1)]))
                work.multiply_tall(wide.at[0], saved["d_b"], groups)
                load("d_up", grad_up_in, wide.at[0])
                load("tokens", tokens_in, saved["d_b"])
            box = tall_outbox[number]
        else:
            number = wide_items.index(i)
            if number >= 2:
                before = wide_items[number - 2]
                wires.left(slot(before, CORE), from_core(before))
            box = outbox[number % 2].at[..., : item.width]
            left, right, names = {
                GATE: (saved["h2_t"], wide.at[1], ("h2_t", "d_gate")),
                UP: (saved["h2_t"], wide.at[0], ("d_up",)),
                OUT: (saved["att_t"], saved["d_proj"], ("att_t", "d_proj")),
                QUERY: (saved["h_t"], saved["query"], ("h_t",)),
                KEY: (saved["h_t"], saved["key"], ()),
                VALUE: (saved["h_t"], saved["value"], ()),
            }[item.weight]
            loaded(*names)
            multiply = partial(work.multiply, left, right, item)
            if number >= RING:
                pl.semaphore_wait(credit, 1)
            multiply(box, 1 - c)
        for xx in (0, 1):
            for half in (0, 1):
                part = (xx, pl.ds(2 * half, 2))
                wires.send(
                    slot(i, CORE), slot(i, CORE), box.at[part], from_core(i).at[part], c_other
                )
        if not item.tall:
            multiply(mine[i], c)

    def first_hop(i):
        item, own, other = items[i], mine[i], from_core(i)
        wires.arrived(slot(i, CORE), other)

        def add(at, _):
            for xx in (0, 1):
                for yy in (0, 1):
                    own[xx, at, yy] = plus(own[xx, at, yy], other[xx, at, yy])
            return 0

        lax.fori_loop(0, 4, add, 0)
        if not item.tall and wide_items.index(i) + RING < len(wide_items):
            pl.semaphore_signal(credit, inc=1, device_id=c_other, device_id_type=MESH)
        if item.x_first:
            for zz in range(4):
                block, target = own.at[1 - x, zz], from_first[i].at[zz]
                wires.send(slot(i, MANY), slot(i, FIRST), block, target, x_other)
        else:
            for xx in (0, 1):
                for half in (0, 1):
                    part = pl.ds(2 * half, 2)
                    block, target = own.at[xx, part, 1 - y], from_first[i].at[xx, part]
                    wires.send(slot(i, MANY), slot(i, FIRST), block, target, y_other)

    def second_hop(i):
        item, own, other = items[i], mine[i], from_first[i]
        wires.arrived(slot(i, FIRST), other)

        def add(at, _):
            for side in (0, 1):
                if item.x_first:
                    own[x, at, side] = plus(own[x, at, side], other[at, side])
                else:
                    own[side, at, y] = plus(own[side, at, y], other[side, at])
            return 0

        lax.fori_loop(0, 4, add, 0)
        if item.x_first:
            for half in (0, 1):
                part = pl.ds(2 * half, 2)
                block, target = own.at[x, part, 1 - y], from_second[i].at[part]
                wires.send(slot(i, MANY), slot(i, SECOND), block, target, y_other)
        else:
            to_z(i, lambda k: own.at[:, far[k], y])

    def to_z(i, block):
        for k in (1, 2, 3):
            target = from_z[i].at[k - 1]
            wires.send(slot(i, MANY), slot(i, ALONG_Z), block(k), target, device(far[k], y, x, c))

    def z_total(i, own_part):
        total = own_part.astype(jnp.float32)
        wires.arrived(slot(i, ALONG_Z), from_z[i])
        for k in (1, 2, 3):
            total += from_z[i][k - 1].astype(jnp.float32)
        return total.astype(jnp.bfloat16)

    def third_hop(i):
        item, own, other = items[i], mine[i], from_second[i]
        if not item.x_first:
            own[:, z, y] = z_total(i, own[:, z, y])
            for xx in (0, 1):
                block, target = own.at[xx, z, y], other.at[xx]
                wires.send(slot(i, MANY), slot(i, SECOND), block, target, x_other)
            return
        wires.arrived(slot(i, SECOND), other)

        def add(at, _):
            own[x, at, y] = plus(own[x, at, y], other[at])
            return 0

        lax.fori_loop(0, 4, add, 0)
        to_z(i, lambda k: own.at[x, far[k], y])

    def fourth_hop(i):
        item, own = items[i], mine[i]
        if not item.x_first:
            wires.arrived(slot(i, SECOND), from_second[i])
            block = item.half(sums[item.weight], c)
            block[...] = plus(own[:, z, y], from_second[i][...])
            wires.send(slot(i, LAST_SEND), slot(i, LAST), block, block, c_other)
            return
        block = item.quarter(sums[item.weight], c, x)
        block[...] = z_total(i, own[x, z, y])
        wires.send(slot(i, MANY), slot(i, ALONG_X), block, block, x_other)

    def to_sibling(i):
        item = items[i]
        if item.x_first:
            wires.arrived(slot(i, ALONG_X), item.quarter(sums[item.weight], c, 1 - x))
            block = item.half(sums[item.weight], c)
            wires.send(slot(i, LAST_SEND), slot(i, LAST), block, block, c_other)

    def complete(i):
        item = items[i]
        wires.arrived(slot(i, LAST), item.half(sums[item.weight], 1 - c))
        wires.left(slot(i, MANY), mine[i])
        wires.left(slot(i, LAST_SEND), item.half(sums[item.weight], c))
        if item.tall or i in wide_items[-2:]:
            wires.left(slot(i, CORE), from_core(i))

    base = SUM_SLOTS * len(items)

    def gains_one():
        wires.send(base, base, gain_lines, gain_core, c_other)

    def gains_two():
        wires.arrived(base, gain_core)
        gain_core[...] = gain_lines[...] + gain_core[...]
        wires.send(base + 1, base + 1, gain_core, gain_x, x_other)

    def gains_three():
        wires.arrived(base + 1, gain_x)
        gain_x[...] = gain_core[...] + gain_x[...]
        wires.send(base + 2, base + 2, gain_x.at[:, 1 - y], gain_y, y_other)

    def gains_four():
        wires.arrived(base + 2, gain_y)
        gain_y[...] = gain_x[:, y] + gain_y[...]
        for k in (1, 2, 3):
            other = device(far[k], y, x, c)
            wires.send(base + 3, base + 3, gain_y.at[far[k]], gain_z.at[z], other)
        gain_z[z] = gain_y[z]

    def gains_five():
        wires.arrived(base + 3, gain_z.at[0:3])
        gain_sums[...] = (gain_z[0] + gain_z[1]) + (gain_z[2] + gain_z[3])

    def fetch_rows(t):
        for n in range(3):
            load(("rows", n, t), kept[n].at[t], w_rows.at[2 * n : 2 * n + 2])

    def attend_back(p):
        if p == 0:
            loaded("query", "key", "value", "lse", "d_proj", "w_rows")
        work.attend_back(p, p + 1)
        if p == 7:
            fetch_rows(0)

    def grad_hidden(t):
        loaded(*[("rows", n, t) for n in range(3)])
        work.grad_hidden(t)
        if t < 3:
            fetch_rows(t + 1)

    def finish():
        loaded("tokens", "d_res", "g_ffn", "gain")
        work.finish()
        load("d_in", d_in, input_grad_out)
        gains_one()

    beside = {1: [work.prepare]}
    for p in range(8):
        beside.setdefault(1 + p, []).append(partial(attend_back, p))
    for t in range(4):
        beside.setdefault(9 + t // 2, []).append(partial(grad_hidden, t))
    beside.setdefault(11, []).append(finish)
    for n, task in enumerate((gains_two, gains_three, gains_four, gains_five)):
        beside.setdefault(13 + 2 * n, []).append(task)

    stages = (complete, to_sibling, fourth_hop, third_hop, second_hop, first_hop, produce)
    lates = (12, 10, 8, 6, 4, 2, 0)
    for step in range(len(items) + lates[0]):
        for late, stage in zip(lates, stages):
            if 0 <= step - late < len(items):
                stage(step - late)
        for task in beside.get(step, []):
            task()
    loaded("d_in")
    for n, like in enumerate((gain_lines, gain_core, gain_x.at[:, 1 - y], gain_z.at[0:3])):
        wires.left(base + n, like)


def backward(tokens, lengths, kept, saved):
    items = share_items()
    low, wide = jnp.bfloat16, jnp.float32
    dtypes = {name: (shape, dtype) for name, shape, dtype in FORWARD_OUTS}
    shapes = [
        jax.ShapeDtypeStruct((2, 2, 2, 352, 128) if n is None else (2, 64, n), low) for n in COLUMNS
    ]
    shapes += [jax.ShapeDtypeStruct((8, 128), wide), jax.ShapeDtypeStruct((512, 1024), wide)]
    count = SUM_SLOTS * len(items) + 4
    anywhere = pl.BlockSpec(memory_space=pl.ANY)
    in_vmem = pl.BlockSpec(memory_space=pltpu.VMEM)
    n_loads = 6 + len(BACKWARD_IN) + 12

    def buffers(lead_of):
        return [pltpu.VMEM(lead_of(item) + item.block, low) for item in items]

    out = pl.pallas_call(
        partial(backward_kernel, items),
        out_shape=shapes,
        in_specs=[anywhere] * (len(KEPT) + 3 + len(BACKWARD_IN) + 1)
        + [pl.BlockSpec(memory_space=pltpu.SMEM)],
        out_specs=[in_vmem] * 8 + [anywhere],
        scratch_shapes=[pltpu.VMEM(*dtypes[name]) for name in BACKWARD_IN]
        + [
            pltpu.VMEM((512, 1024), wide),
            pltpu.VMEM((2, 512, 2816), low),
            pltpu.VMEM((8, 2, 64, 1024), low),
            pltpu.VMEM((512, 512), wide),
            pltpu.VMEM((512, 256), low),
            pltpu.VMEM((512, 256), low),
            pltpu.VMEM((8, 1024), wide),
            pltpu.VMEM((4, 2, 8, 128), wide),
        ]
        + buffers(lambda item: (2, 4, 2))
        + buffers(lambda item: (4, 2) if item.x_first else (2, 4))
        + buffers(lambda item: (4,) if item.x_first else (2,))
        + buffers(lambda item: (3,) if item.x_first else (3, 2))
        + [pltpu.VMEM((2, 4, 2, 64, 512), low)] * RING
        + [pltpu.VMEM((2, 4, 2, 352, 128), low)] * 2
        + [pltpu.VMEM((2, 4, 2, 64, 512), low)] * 2
        + [pltpu.VMEM((2, 4, 2, 352, 128), low)] * 2
        + [
            pltpu.VMEM((4, 2, 8, 128), wide),
            pltpu.VMEM((4, 2, 8, 128), wide),
            pltpu.VMEM((4, 8, 128), wide),
            pltpu.VMEM((4, 8, 128), wide),
            pltpu.SemaphoreType.DMA((count,)),
            pltpu.SemaphoreType.DMA((count,)),
            pltpu.SemaphoreType.DMA((n_loads,)),
            pltpu.SemaphoreType.REGULAR,
        ],
        compiler_params=pltpu.CompilerParams(
            collective_id=1, has_side_effects=True, vmem_limit_bytes=63 * MIB
        ),
        name="backward_sum",
    )(
        *kept,
        saved["mid"],
        saved["d_gate"],
        saved["d_up"],
        *[saved[name] for name in BACKWARD_IN],
        tokens,
        lengths,
    )
    return out[:7], out[7], out[8]


def unpack_kernel(*refs):
    blocks, (gain_sums, mixed, d_in) = refs[:7], refs[7:10]
    sums, (gain_attn, gain_ffn, mixed_out, input_out) = refs[10:17], refs[17:21]
    held, wide = refs[21:28], refs[28:35]
    mixed_held, input_held, in_sems, out_sems = refs[35:]
    sources = (d_in, mixed, *blocks)
    places = (input_held, mixed_held, *held)
    results = (input_held, mixed_held, *wide)
    targets = (input_out, mixed_out, *sums)
    ins = [pltpu.make_async_copy(a, b, in_sems.at[n]) for n, (a, b) in enumerate(zip(sources, places))]
    outs = [pltpu.make_async_copy(a, b, out_sems.at[n]) for n, (a, b) in enumerate(zip(results, targets))]
    order = (6, 7, 8, 2, 3, 4, 5, 0, 1)
    for n in order:
        ins[n].start()
    for n in order:
        ins[n].wait()
        if n == 8:
            for b in range(8):
                wide[6][:, 128 * b : 128 * b + 128] = held[6][b // 4, b // 2 % 2, b % 2].astype(
                    jnp.float32
                )
        elif n >= 2:
            wide[n - 2][...] = held[n - 2][...].astype(jnp.float32)
        outs[n].start()
    gain_attn[...] = gain_sums[0:1]
    gain_ffn[...] = gain_sums[1:2]
    for n in order:
        outs[n].wait()


def unpack(blocks, gain_sums, mixed, d_in):
    wide = jnp.float32
    anywhere = pl.BlockSpec(memory_space=pl.ANY)
    in_vmem = pl.BlockSpec(memory_space=pltpu.VMEM)
    shapes = [
        jax.ShapeDtypeStruct((352, 1024) if n is None else (2, 64, n), wide) for n in COLUMNS
    ]
    held = [pltpu.VMEM(b.shape, b.dtype) for b in blocks]
    held += [pltpu.VMEM(v.shape, wide) for v in shapes]
    held += [pltpu.VMEM(v.shape, v.dtype) for v in (mixed, d_in)]
    shapes += [jax.ShapeDtypeStruct((1, 128), wide)] * 2
    shapes += [jax.ShapeDtypeStruct(v.shape, v.dtype) for v in (mixed, d_in)]
    out = pl.pallas_call(
        unpack_kernel,
        out_shape=shapes,
        in_specs=[anywhere] * 7 + [in_vmem] + [anywhere] * 2,
        out_specs=[anywhere] * 7 + [in_vmem] * 2 + [anywhere] * 2,
        scratch_shapes=held + [pltpu.SemaphoreType.DMA((9,)), pltpu.SemaphoreType.DMA((9,))],
        compiler_params=pltpu.CompilerParams(vmem_limit_bytes=62 * MIB),
        name="unpack",
    )(*blocks, gain_sums, mixed, d_in)
    sums = [s.reshape(-1, s.shape[-1]) for s in out[:7]]
    return sums, [g.reshape(128) for g in out[7:9]], out[9], out[10]


def gather_plain(weights, gains):
    everything = (*weights, *gains)
    whole = [lax.all_gather(v, "dp", axis=0, tiled=True) for v in everything]
    return whole[: len(weights)], whole[len(weights) :]


def sum_plain(grads, gain_grads):
    shares = [
        lax.psum_scatter(g.astype(jnp.float32), "dp", scatter_dimension=0, tiled=True)
        for g in (*grads, *gain_grads)
    ]
    sums = [lax.psum(s, ("rep", "cores")) for s in shares]
    return sums[: len(grads)], sums[len(grads) :]


def on_any_device(
    tokens,
    norm_attn,
    w_query,
    w_key,
    w_value,
    w_out,
    norm_ffn,
    w_gate,
    w_up,
    w_down,
    lengths,
    cotangent,
):
    rows = tokens.shape[0]
    low = jnp.bfloat16
    allowed, valid = masks(lengths, rows)
    whole, gains = gather_plain(
        (w_query, w_key, w_value, w_out, w_gate, w_up, w_down), (norm_attn, norm_ffn)
    )
    full_query, full_key, full_value, full_out, full_gate, full_up, full_down = whole
    gain_attn, gain_ffn = gains
    inputs = tokens.astype(jnp.float32)
    normed, factor = normalize(inputs)
    hidden = (normed * gain_attn.astype(jnp.float32)).astype(low)
    query = matmul(hidden, full_query).astype(low)
    keyed = matmul(hidden, full_key).astype(low)
    valued = matmul(hidden, full_value).astype(low)
    query_groups, key_groups, value_groups = (to_groups(query), to_groups(keyed), to_groups(valued))
    attended_groups, log_total = lax.map(
        partial(attend, allowed), (query_groups, key_groups, value_groups)
    )
    attended = from_groups(attended_groups)
    residual = inputs + matmul(attended, full_out)
    normed_two, factor_two = normalize(residual)
    hidden_two = (normed_two * gain_ffn.astype(jnp.float32)).astype(low)
    gate = matmul(hidden_two, full_gate)
    upward = matmul(hidden_two, full_up)
    sigma = jax.nn.sigmoid(gate)
    middle = (gate * sigma * upward).astype(low)
    mixed = (valid[:, None] * (residual + matmul(middle, full_down))).astype(low)
    grad_output = cotangent.astype(jnp.float32) * valid[:, None]
    grad_branch = grad_output.astype(low)
    grad_down = matmul_tn(middle, grad_branch)
    grad_middle = matmul_nt(grad_branch, full_down)
    grad_gate_rows = (grad_middle * upward * sigma * (1.0 + gate * (1.0 - sigma))).astype(low)
    grad_up_rows = (grad_middle * gate * sigma).astype(low)
    grad_gate = matmul_tn(hidden_two, grad_gate_rows)
    grad_up = matmul_tn(hidden_two, grad_up_rows)
    grad_hidden_two = matmul_nt(grad_gate_rows, full_gate) + matmul_nt(grad_up_rows, full_up)
    grad_gain_ffn = jnp.sum(grad_hidden_two * normed_two, axis=0)
    grad_residual = grad_output + norm_back(
        grad_hidden_two * gain_ffn.astype(jnp.float32), normed_two, factor_two
    )
    grad_proj = grad_residual.astype(low)
    grad_out = matmul_tn(attended, grad_proj)
    grad_attended = matmul_nt(grad_proj, full_out).astype(low)
    grad_query_g, grad_key_g, grad_value_g = lax.map(
        partial(attend_back, allowed),
        (query_groups, key_groups, value_groups, to_groups(grad_attended), log_total),
    )
    grad_query_rows = from_groups(grad_query_g)
    grad_key_rows = from_groups(grad_key_g)
    grad_value_rows = from_groups(grad_value_g)
    grad_query = matmul_tn(hidden, grad_query_rows)
    grad_key = matmul_tn(hidden, grad_key_rows)
    grad_value = matmul_tn(hidden, grad_value_rows)
    grad_hidden = (
        matmul_nt(grad_query_rows, full_query)
        + matmul_nt(grad_key_rows, full_key)
        + matmul_nt(grad_value_rows, full_value)
    )
    grad_gain_attn = jnp.sum(grad_hidden * normed, axis=0)
    input_grad = grad_residual + norm_back(
        grad_hidden * gain_attn.astype(jnp.float32), normed, factor
    )
    grads = (grad_query, grad_key, grad_value, grad_out, grad_gate, grad_up, grad_down)
    sums, gain_sums = sum_plain([g.astype(low) for g in grads], (grad_gain_attn, grad_gain_ffn))
    return (
        mixed,
        input_grad,
        gain_sums[0],
        sums[0],
        sums[1],
        sums[2],
        sums[3],
        gain_sums[1],
        sums[4],
        sums[5],
        sums[6],
    )


def on_tuned_device(
    tokens,
    norm_attn,
    w_query,
    w_key,
    w_value,
    w_out,
    norm_ffn,
    w_gate,
    w_up,
    w_down,
    lengths,
    cotangent,
):
    weights = (w_query, w_key, w_value, w_out, w_gate, w_up, w_down)
    kept, saved = forward(tokens, cotangent, lengths, weights, (norm_attn, norm_ffn))
    blocks, gain_lines, d_in = backward(tokens, lengths, kept, saved)
    sums, gain_sums, mixed, d_in = unpack(blocks, gain_lines, saved["mixed"], d_in)
    return (
        mixed,
        d_in,
        gain_sums[0],
        *sums[:4],
        gain_sums[1],
        *sums[4:],
    )


def solution(mesh):
    tuned = dict(mesh.shape) == {"dp": 8, "rep": 2, "cores": 2}
    tokens_placed = P(("dp", "rep", "cores"), None)
    share, gain = P("dp", None), P("dp")
    return jax.shard_map(
        on_tuned_device if tuned else on_any_device,
        mesh=mesh,
        in_specs=(
            tokens_placed,
            gain,
            share,
            share,
            share,
            share,
            gain,
            share,
            share,
            share,
            tokens_placed,
            tokens_placed,
        ),
        out_specs=(
            tokens_placed,
            tokens_placed,
            gain,
            share,
            share,
            share,
            share,
            gain,
            share,
            share,
            share,
        ),
        check_vma=False,
    )
```

```python
from functools import partial

import jax
import jax.numpy as jnp
from jax import lax
from jax.experimental import pallas as pl
from jax.experimental.pallas import tpu as pltpu
from jax.sharding import PartitionSpec as P

HEADS = 16
HEAD = 64


NORM_EPS = 1e-05
SCORE_SCALE = 0.125
NEGATIVE = -1e30
head_group = 4
MESH = pl.DeviceIdType.MESH
MIB = 1024 * 1024


def masks(block_len, rows):
    bounds = jnp.cumsum(block_len[0])
    place = jnp.arange(rows, dtype=jnp.int32)
    segment = jnp.sum((place[:, None] >= bounds[None, :]).astype(jnp.int32), axis=1)
    allowed = (segment[:, None] == segment[None, :]) & (place[None, :] <= place[:, None])
    valid = (segment < block_len.shape[1]).astype(jnp.float32)
    return (allowed, valid)


def normalize(values):
    factor = lax.rsqrt(jnp.mean(values * values, axis=-1, keepdims=True) + NORM_EPS)
    return (values * factor, factor)


def norm_back(grad_normed, normed, factor):
    return factor * (grad_normed - normed * jnp.mean(grad_normed * normed, axis=-1, keepdims=True))


def matmul(left, right):
    return jnp.dot(left, right, preferred_element_type=jnp.float32)


def matmul_tn(left, right):
    return lax.dot_general(
        left, right, (((0,), (0,)), ((), ())), preferred_element_type=jnp.float32
    )


def matmul_nt(left, right):
    return lax.dot_general(
        left, right, (((1,), (1,)), ((), ())), preferred_element_type=jnp.float32
    )


def to_groups(matrix):
    rows = matrix.shape[0]
    split = matrix.reshape(rows, HEADS // head_group, head_group, HEAD)
    return split.transpose(1, 2, 0, 3)


def from_groups(grouped):
    rows = grouped.shape[2]
    return grouped.transpose(2, 0, 1, 3).reshape(rows, HEADS * HEAD)


def group_scores(allowed, query_g, key_g):
    raw = (
        jnp.einsum("hqe,hke->hqk", query_g, key_g, preferred_element_type=jnp.float32) * SCORE_SCALE
    )
    return jnp.where(allowed[None], raw, NEGATIVE)


def attend(allowed, operands):
    query_g, key_g, value_g = operands
    scores = group_scores(allowed, query_g, key_g)
    top = jnp.max(scores, axis=-1, keepdims=True)
    expo = jnp.exp(scores - top)
    total = jnp.sum(expo, axis=-1, keepdims=True)
    probs_low = (expo / total).astype(jnp.bfloat16)
    result = jnp.einsum("hqk,hke->hqe", probs_low, value_g, preferred_element_type=jnp.float32)
    return (result.astype(jnp.bfloat16), top[..., 0] + jnp.log(total[..., 0]))


def attend_back(allowed, operands):
    query_g, key_g, value_g, grad_g, lse = operands
    scores = group_scores(allowed, query_g, key_g)
    probs = jnp.exp(scores - lse[..., None])
    grad_probs = jnp.einsum("hqe,hke->hqk", grad_g, value_g, preferred_element_type=jnp.float32)
    centre = jnp.sum(grad_probs * probs, axis=-1, keepdims=True)
    grad_scores = (probs * (grad_probs - centre)).astype(jnp.bfloat16)
    grad_query = (
        jnp.einsum("hqk,hke->hqe", grad_scores, key_g, preferred_element_type=jnp.float32)
        * SCORE_SCALE
    )
    grad_key = (
        jnp.einsum("hqk,hqe->hke", grad_scores, query_g, preferred_element_type=jnp.float32)
        * SCORE_SCALE
    )
    grad_value = jnp.einsum(
        "hqk,hqe->hke", probs.astype(jnp.bfloat16), grad_g, preferred_element_type=jnp.float32
    )
    return (
        grad_query.astype(jnp.bfloat16),
        grad_key.astype(jnp.bfloat16),
        grad_value.astype(jnp.bfloat16),
    )


class Part:
    def __init__(self, weight, tall, start, size, no_x):
        self.weight, self.tall, self.start, self.size = weight, tall, start, size
        self.no_x = no_x

    def quarter(self, ref, lead, c, x):
        if self.tall:
            columns = pl.ds(pl.multiple_of(c * 512 + x * 256, 256), 256)
            return ref.at[(*lead, pl.ds(self.start, self.size), columns)]
        return ref.at[(*lead, x, slice(None), self.columns(c))]

    def half(self, ref, lead, c):
        if self.tall:
            columns = pl.ds(pl.multiple_of(c * 512, 512), 512)
            return ref.at[(*lead, pl.ds(self.start, self.size), columns)]
        return ref.at[(*lead, slice(None), slice(None), self.columns(c))]

    def columns(self, c):
        width = self.size // 2
        return pl.ds(pl.multiple_of(self.start + c * width, 128), width)


def pieces(total, most):
    return [(start, min(most, total - start)) for start in range(0, total, most)]


def place():
    d = lax.axis_index("dp")
    return lax.div(d, 2), lax.rem(d, 2), lax.axis_index("rep"), lax.axis_index("cores")


def device(z, y, x, c):
    return {"dp": 2 * z + y, "rep": x, "cores": c}


def greet():
    z, y, x, c = place()
    barrier = pltpu.get_barrier_semaphore()
    others = [device(lax.rem(z + k, 4), y, x, c) for k in (1, 2, 3)]
    others += [device(z, 1 - y, x, c), device(z, y, 1 - x, c), device(z, y, x, 1 - c)]
    for other in others:
        pl.semaphore_signal(barrier, inc=1, device_id=other, device_id_type=MESH)
    pl.semaphore_wait(barrier, len(others))


class Wires:
    def __init__(self, send_sems, recv_sems):
        self.send_sems, self.recv_sems, self.sent = send_sems, recv_sems, []

    def copy(self, slot, source, target, other):
        return pltpu.make_async_remote_copy(
            src_ref=source,
            dst_ref=target,
            send_sem=self.send_sems.at[slot],
            recv_sem=self.recv_sems.at[slot],
            device_id=other,
            device_id_type=MESH,
        )

    def send(self, slot, source, target, other):
        copy = self.copy(slot, source, target, other)
        copy.start()
        self.sent.append((slot, copy))

    def arrived(self, slot, target):
        z, y, x, c = place()
        self.copy(slot, target, target, device(z, y, x, 1 - c)).wait_recv()

    def finish(self, chosen=lambda slot: True):
        for slot, copy in self.sent:
            if chosen(slot):
                copy.wait_send()
        self.sent = [(slot, copy) for slot, copy in self.sent if not chosen(slot)]


GATHER_SLOTS = 12
LAG = 2
ALL = slice(None)
COLUMNS = (1024, 1024, 1024, 1024, 2816, 2816, None)
QUERY, KEY, VALUE, OUT, GATE, UP, DOWN = range(7)
TILE = 512


FF_CHUNKS = tuple(pieces(2816, 512))


def gather_items():
    order = [(QUERY, 0, 256, True), (QUERY, 256, 768, False), (KEY, 0, 1024, True)]
    order += [(VALUE, 0, 1024, False), (OUT, 0, 1024, False)]
    order += [(DOWN, 0, 128, False), (DOWN, 128, 128, True), (DOWN, 256, 96, False)]
    for n, (start, size) in enumerate(FF_CHUNKS):
        order += [(GATE, start, size, n == 5), (UP, start, size, n in (0, 3, 5))]
    return [Part(w, w == DOWN, start, size, no_x) for w, start, size, no_x in order]


def dot(left, right):
    return lax.dot_general(
        left, right, (((1,), (0,)), ((), ())), preferred_element_type=jnp.float32
    )


def dot_nt(left, right):
    return lax.dot_general(
        left, right, (((1,), (1,)), ((), ())), preferred_element_type=jnp.float32
    )


def tile(index, size):
    return pl.ds(pl.multiple_of(index * size, size), size)


def weight_columns(ref, at):
    return ref[:, :, :, :, at].reshape(1024, -1)


class Forward:
    def __init__(self, refs):
        self.__dict__.update(refs)

    def prepare(self):
        for s in range(8):
            self.gain[:, 128 * s : 128 * s + 128] = self.gains[s // 2, s % 2]
        length = self.length[0, 0]
        for block in range(4):
            rows = slice(128 * block, 128 * block + 128)
            place_q = lax.broadcasted_iota(jnp.int32, (128, 512), 0) + 128 * block
            place_k = lax.broadcasted_iota(jnp.int32, (128, 512), 1)
            same = (place_q >= length) == (place_k >= length)
            allowed = same & (place_k <= place_q)
            self.bias[rows, :] = jnp.where(allowed, 0.0, NEGATIVE)

        def normed(block, _):
            rows = tile(block, 64)
            values = self.tokens[rows, :].astype(jnp.float32)
            factor = lax.rsqrt(jnp.mean(values * values, axis=-1, keepdims=True) + NORM_EPS)
            gain = self.gain[0:1, :].astype(jnp.float32)
            self.hidden[rows, :] = (values * factor * gain).astype(jnp.bfloat16)
            place = lax.broadcasted_iota(jnp.int32, (64, 1024), 0) + 64 * block
            d_b = jnp.where(place < length, self.cotangent[rows, :].astype(jnp.float32), 0.0)
            self.d_b[rows, :] = d_b.astype(jnp.bfloat16)
            return 0

        lax.fori_loop(0, 8, normed, 0)
        self.turn(self.hidden, self.h_t)
        self.out("d_b")

    def turn(self, matrix, turned):
        def columns(n, _):
            at = tile(n, 128)
            turned[at, :] = matrix[:, at].astype(jnp.float32).T.astype(jnp.bfloat16)
            return 0

        lax.fori_loop(0, 8, columns, 0)

    def project(self, weight, result):
        def columns(n, _):
            at = tile(n, TILE)
            result[:, at] = dot(self.hidden[...], weight_columns(weight, at)).astype(jnp.bfloat16)
            return 0

        lax.fori_loop(0, 1024 // TILE, columns, 0)

    def attend(self, first, last):
        def pair(p, _):
            at = tile(p, 128)
            left = lax.broadcasted_iota(jnp.int32, (256, 128), 1) < HEAD
            for block in (0, 1):
                rows, seen = slice(256 * block, 256 * block + 256), slice(0, 256 * block + 256)
                query = self.query[rows, at].astype(jnp.float32) * SCORE_SCALE
                both = jnp.concatenate(
                    [jnp.where(left, query, 0.0), jnp.where(left, 0.0, query)], axis=0
                ).astype(jnp.bfloat16)
                bias = self.bias[rows, seen]
                scores = dot_nt(both, self.key[seen, at]) + jnp.concatenate([bias, bias], axis=0)
                top = jnp.max(scores, axis=-1, keepdims=True)
                expo = jnp.exp(scores - top)
                total = jnp.sum(expo, axis=-1, keepdims=True)
                probs = (expo * (1.0 / total)).astype(jnp.bfloat16)
                result = dot(probs, self.value[seen, at])
                self.attended[rows, at] = jnp.where(left, result[:256], result[256:]).astype(
                    jnp.bfloat16
                )
                lse = top + jnp.log(total)
                turned = jnp.where(left, lse[:256], lse[256:]).T
                self.lse[p, 0:1, rows] = turned[0:1]
                self.lse[p, 1:2, rows] = turned[HEAD : HEAD + 1]
            return 0

        lax.fori_loop(first, last, pair, 0)

    def project_out(self):
        def columns(n, _):
            at = tile(n, TILE)
            self.residual[:, at] = self.tokens[:, at].astype(jnp.float32) + dot(
                self.attended[...], weight_columns(self.w_out, at)
            )
            return 0

        lax.fori_loop(0, 1024 // TILE, columns, 0)

        def normed(block, _):
            rows = tile(block, 64)
            values = self.residual[rows, :]
            factor = lax.rsqrt(jnp.mean(values * values, axis=-1, keepdims=True) + NORM_EPS)
            gain = self.gain[8:9, :].astype(jnp.float32)
            self.h2[rows, :] = (values * factor * gain).astype(jnp.bfloat16)
            return 0

        lax.fori_loop(0, 8, normed, 0)
        self.turn(self.h2, self.h2_t)
        self.turn(self.attended, self.att_t)
        for name in ("query", "key", "value", "lse", "h_t", "h2_t", "att_t"):
            self.out(name)

    def grad_of_middle(self, start, size):
        at = pl.ds(start, size)
        self.d_up[:, at] = dot_nt(self.d_b[...], self.w_down[at, :]).astype(jnp.bfloat16)

    def feed_forward(self, start, size):
        at = pl.ds(start, size)
        low = jnp.bfloat16
        gate_w = weight_columns(self.w_gate, at)
        up_w = weight_columns(self.w_up, at)
        down_w = self.w_down[at, :]
        gate = dot(self.h2[...], gate_w)
        upward = dot(self.h2[...], up_w)
        grad_middle = self.d_up[:, at].astype(jnp.float32)
        sigma = 0.5 * jnp.tanh(0.5 * gate) + 0.5
        silu = gate * sigma
        mid = (silu * upward).astype(low)
        d_up = (grad_middle * silu).astype(low)
        d_gate = (grad_middle * upward * (sigma + silu - silu * sigma)).astype(low)
        self.mid[:, at] = mid
        self.d_up[:, at] = d_up
        self.d_gate[:, at] = d_gate
        for j in range(1024 // TILE):
            part = slice(TILE * j, TILE * j + TILE)
            mixed = dot(mid, down_w[:, part])
            grad = dot_nt(d_gate, gate_w[part, :]) + dot_nt(d_up, up_w[part, :])
            if start == 0:
                self.total[:, part] = mixed
                self.d_h2[:, part] = grad
            else:
                self.total[:, part] += mixed
                self.d_h2[:, part] += grad

    def flush(self, start, size):
        for name in ("mid", "d_gate", "d_up"):
            self.out(name, pl.ds(start, size))

    def finish(self):
        length = self.length[0, 0]
        self.g_ffn[...] = jnp.zeros_like(self.g_ffn)

        def rows_of(block, _):
            rows = tile(block, 64)
            place = lax.broadcasted_iota(jnp.int32, (64, 1024), 0) + 64 * block
            residual = self.residual[rows, :]
            mixed = jnp.where(place < length, residual + self.total[rows, :], 0.0)
            self.mixed[rows, :] = mixed.astype(jnp.bfloat16)
            factor = lax.rsqrt(jnp.mean(residual * residual, axis=-1, keepdims=True) + NORM_EPS)
            normed = residual * factor
            grad = self.d_h2[rows, :]
            self.g_ffn[...] += jnp.sum((grad * normed).reshape(8, 8, 1024), axis=0)
            grad_normed = grad * self.gain[8:9, :].astype(jnp.float32)
            grad_out = jnp.where(place < length, self.cotangent[rows, :].astype(jnp.float32), 0.0)
            mean = jnp.mean(grad_normed * normed, axis=-1, keepdims=True)
            d_res = grad_out + factor * (grad_normed - normed * mean)
            self.d_res[rows, :] = d_res
            self.d_proj[rows, :] = d_res.astype(jnp.bfloat16)
            return 0

        lax.fori_loop(0, 8, rows_of, 0)
        for name in ("mixed", "d_res", "d_proj", "g_ffn", "gain"):
            self.out(name)


FORWARD_OUTS = (
    ("mixed", (512, 1024), jnp.bfloat16),
    ("query", (512, 1024), jnp.bfloat16),
    ("key", (512, 1024), jnp.bfloat16),
    ("value", (512, 1024), jnp.bfloat16),
    ("lse", (8, 8, 512), jnp.float32),
    ("h_t", (1024, 512), jnp.bfloat16),
    ("h2_t", (1024, 512), jnp.bfloat16),
    ("att_t", (1024, 512), jnp.bfloat16),
    ("d_b", (512, 1024), jnp.bfloat16),
    ("mid", (512, 2816), jnp.bfloat16),
    ("d_gate", (512, 2816), jnp.bfloat16),
    ("d_up", (512, 2816), jnp.bfloat16),
    ("d_res", (512, 1024), jnp.float32),
    ("d_proj", (512, 1024), jnp.bfloat16),
    ("g_ffn", (8, 1024), jnp.float32),
    ("gain", (16, 1024), jnp.bfloat16),
)
FORWARD_OWN = (
    ("hidden", (512, 1024), jnp.bfloat16),
    ("attended", (512, 1024), jnp.bfloat16),
    ("residual", (512, 1024), jnp.float32),
    ("h2", (512, 1024), jnp.bfloat16),
    ("d_h2", (512, 1024), jnp.float32),
    ("bias", (512, 512), jnp.float32),
    ("total", (512, 1024), jnp.float32),
)
OUT_COPIES = len(FORWARD_OUTS) - 3 + 3 * len(FF_CHUNKS)
KEPT = (QUERY, KEY, VALUE, OUT)


def share_shape(columns):
    return (352, 1024) if columns is None else (2, 64, columns)


def forward_kernel(items, *refs):
    refs = list(refs)

    def take(n):
        taken = refs[:n]
        del refs[:n]
        return taken

    shares = take(7)
    gain_attn, gain_ffn, tokens, cotangent, length = take(5)
    kept = take(len(KEPT))
    names = [name for name, _, _ in FORWARD_OUTS]
    outs = dict(zip(names, take(len(names))))
    full = take(7)
    full_gains, gains = take(2)
    own_names = names + [name for name, _, _ in FORWARD_OWN]
    state = dict(zip(own_names, take(len(own_names))))
    send_sems, recv_sems, own_sems, keep_sems, out_sems = refs
    outgoing = []

    def put(name, columns=None):
        source, target = state[name], outs[name]
        if columns is not None:
            source, target = source.at[:, columns], target.at[:, columns]
        outgoing.append(pltpu.make_async_copy(source, target, out_sems.at[len(outgoing)]))
        outgoing[-1].start()

    z, y, x, c = place()
    far = [lax.rem(z + k, 4) for k in range(4)]
    back = [lax.rem(z + 4 - k, 4) for k in range(4)]
    x_other, y_other, c_other = (
        device(z, y, 1 - x, c),
        device(z, 1 - y, x, c),
        device(z, y, x, 1 - c),
    )
    greet()
    wires = Wires(send_sems, recv_sems)
    own = [
        pltpu.make_async_copy(share, whole.at[z, y], own_sems.at[i])
        for i, (share, whole) in enumerate(zip(shares, full))
    ]
    own_gains = pltpu.make_async_copy(gains, full_gains.at[z, y], own_sems.at[7])
    keep = [
        pltpu.make_async_copy(full[w], kept[n], keep_sems.at[n]) for n, w in enumerate(KEPT)
    ]
    gains[...] = jnp.where(
        lax.broadcasted_iota(jnp.int32, (16, 128), 0) < 8,
        jnp.broadcast_to(gain_attn[...].astype(jnp.float32), (16, 128)),
        jnp.broadcast_to(gain_ffn[...].astype(jnp.float32), (16, 128)),
    ).astype(jnp.bfloat16)
    own_gains.start()
    gain_slot = GATHER_SLOTS * len(items)
    for k in (1, 2, 3):
        wires.send(gain_slot + k, gains, full_gains.at[z, y], device(far[k], y, x, c))
    for copy in own:
        copy.start()

    def slot(i, k):
        return GATHER_SLOTS * i + k

    def along_z(i):
        item = items[i]
        share, whole = shares[item.weight], full[item.weight]
        for k in (1, 2, 3):
            if item.no_x:
                source, target = item.half(share, (), c), item.half(whole, (z, y), c)
            else:
                source, target = item.quarter(share, (), c, x), item.quarter(whole, (z, y), c, x)
            wires.send(slot(i, k), source, target, device(far[k], y, x, c))

    own_done = set()

    def first_hop(i):
        item = items[i]
        whole = full[item.weight]
        if item.weight not in own_done:
            own[item.weight].wait()
            own_done.add(item.weight)
        for k in (1, 2, 3):
            if item.no_x:
                block = item.half(whole, (back[k], y), c)
                wires.arrived(slot(i, k), block)
                wires.send(slot(i, 7 + k), block, block, c_other)
            else:
                block = item.quarter(whole, (back[k], y), c, x)
                wires.arrived(slot(i, k), block)
                wires.send(slot(i, 3 + k), block, block, x_other)
        if item.no_x:
            block = item.half(whole, (ALL, y), c)
        else:
            block = item.quarter(whole, (ALL, y), c, x)
        wires.send(slot(i, 7), block, block, y_other)

    def second_hop(i):
        item = items[i]
        whole = full[item.weight]
        if item.no_x:
            block = item.half(whole, (ALL, 1 - y), c)
            wires.arrived(slot(i, 7), block)
            wires.send(slot(i, 11), block, block, c_other)
            return
        block = item.quarter(whole, (ALL, 1 - y), c, x)
        wires.arrived(slot(i, 7), block)
        wires.send(slot(i, 0), block, block, x_other)
        for k in (1, 2, 3):
            wires.arrived(slot(i, 3 + k), item.quarter(whole, (back[k], y), c, 1 - x))
        for k in (1, 2, 3):
            block = item.half(whole, (back[k], y), c)
            wires.send(slot(i, 7 + k), block, block, c_other)

    def last_hop(i):
        item = items[i]
        whole = full[item.weight]
        if not item.no_x:
            block = item.half(whole, (ALL, 1 - y), c)
            wires.arrived(slot(i, 0), item.quarter(whole, (ALL, 1 - y), c, 1 - x))
            wires.send(slot(i, 11), block, block, c_other)

    def complete(i):
        item = items[i]
        whole = full[item.weight]
        for k in (1, 2, 3):
            wires.arrived(slot(i, 7 + k), item.half(whole, (back[k], y), 1 - c))
        wires.arrived(slot(i, 11), item.half(whole, (ALL, 1 - y), 1 - c))

    def retire(i):
        wires.finish(lambda slot: slot // GATHER_SLOTS == i)

    step_of = Forward(
        dict(
            state,
            out=put,
            tokens=tokens,
            cotangent=cotangent,
            length=length,
            gains=full_gains,
            w_out=full[OUT],
            w_gate=full[GATE],
            w_up=full[UP],
            w_down=full[DOWN].reshape(2816, 1024),
        )
    )
    last_of = {item.weight: i for i, item in enumerate(items)}
    tasks = [(-1, 3, step_of.prepare)]
    for n, name in enumerate(("query", "key", "value")):
        tasks.append((last_of[n], 2, partial(step_of.project, full[n], state[name])))
    tasks += [(last_of[VALUE], 3, partial(step_of.attend, p, p + 2)) for p in (0, 2, 4, 6)]
    tasks.append((last_of[OUT], 3, step_of.project_out))
    for tile_of in pieces(2816, TILE):
        tasks.append((last_of[DOWN], 1, partial(step_of.grad_of_middle, *tile_of)))
    for start, size in FF_CHUNKS:
        there = max(
            i for i, item in enumerate(items) if item.weight == UP and item.start == start
        )
        for at, width in pieces(size, TILE):
            tasks.append((there, 5, partial(step_of.feed_forward, start + at, width)))
        tasks.append((there, 0, partial(step_of.flush, start, size)))

    ahead = 3
    for i in range(min(ahead, len(items))):
        along_z(i)
    own_gains.wait()
    for k in (1, 2, 3):
        wires.arrived(gain_slot + k, full_gains.at[back[k], y])
    wires.send(gain_slot, full_gains.at[:, y], full_gains.at[:, y], y_other)
    stages = (retire, complete, last_hop, second_hop, first_hop)
    lates = (3 * LAG, 3 * LAG - 1, 2 * LAG, LAG, 0)
    for step in range(len(items) + 3 * LAG):
        for late, stage in zip(lates, stages):
            if 0 <= step - late < len(items):
                stage(step - late)
        if step + ahead < len(items):
            along_z(step + ahead)
        if step == 0:
            wires.arrived(gain_slot, full_gains.at[:, 1 - y])
        there = step - lates[1]
        for n, w in enumerate(KEPT):
            if there == last_of[w]:
                keep[n].start()
        spent = 0
        while tasks and tasks[0][0] <= there and spent < 6:
            _, cost, task = tasks.pop(0)
            task()
            spent += cost
    for _, _, task in tasks:
        task()
    step_of.finish()
    for copy in keep + outgoing:
        copy.wait()
    wires.finish()


def forward(tokens, cotangent, lengths, weights, gains):
    items = gather_items()
    shares = [w.reshape(share_shape(n)) for w, n in zip(weights, COLUMNS)]
    wholes = [(4, 2) + share_shape(n) for n in COLUMNS]
    shapes = [jax.ShapeDtypeStruct(wholes[w], jnp.bfloat16) for w in KEPT]
    shapes += [jax.ShapeDtypeStruct(shape, dtype) for _, shape, dtype in FORWARD_OUTS]
    count = GATHER_SLOTS * len(items) + 4
    anywhere = pl.BlockSpec(memory_space=pl.ANY)
    in_vmem = pl.BlockSpec(memory_space=pltpu.VMEM)
    out = pl.pallas_call(
        partial(forward_kernel, items),
        out_shape=shapes,
        in_specs=[anywhere] * 7
        + [in_vmem] * 4
        + [pl.BlockSpec(memory_space=pltpu.SMEM)],
        out_specs=[anywhere] * len(shapes),
        scratch_shapes=[pltpu.VMEM(shape, jnp.bfloat16) for shape in wholes]
        + [pltpu.VMEM((4, 2, 16, 128), jnp.bfloat16), pltpu.VMEM((16, 128), jnp.bfloat16)]
        + [pltpu.VMEM(shape, dtype) for _, shape, dtype in FORWARD_OUTS + FORWARD_OWN]
        + [
            pltpu.SemaphoreType.DMA((count,)),
            pltpu.SemaphoreType.DMA((count,)),
            pltpu.SemaphoreType.DMA((8,)),
            pltpu.SemaphoreType.DMA((len(KEPT),)),
            pltpu.SemaphoreType.DMA((OUT_COPIES,)),
        ],
        compiler_params=pltpu.CompilerParams(
            collective_id=0, has_side_effects=True, vmem_limit_bytes=63 * MIB
        ),
        name="gather_forward",
    )(*shares, *[g.reshape(1, 128) for g in gains], tokens, cotangent, lengths)
    return out[: len(KEPT)], dict(zip([name for name, _, _ in FORWARD_OUTS], out[len(KEPT) :]))


SUM_SLOTS = 10
RING = 4


class Share:
    def __init__(self, weight, start, size, x_first):
        self.weight, self.start, self.size, self.x_first = weight, start, size, x_first
        self.tall = weight == DOWN
        self.width = 128 if self.tall else size // 2
        self.block = (352 if self.tall else 64, self.width)

    def columns(self, c, x):
        start = c * 512 + x * 256 + self.start if self.tall else self.start + c * self.width
        return pl.ds(pl.multiple_of(start, 128), self.width)

    def quarter(self, sums, c, x):
        if self.tall:
            return sums.at[c, x, self.start // 128]
        return sums.at[x, :, self.columns(c, x)]

    def half(self, sums, c):
        if self.tall:
            return sums.at[c, :, self.start // 128]
        return sums.at[:, :, self.columns(c, 0)]


def share_items():
    order = [(GATE, 2048, 768, True), (DOWN, 0, 128, False), (DOWN, 128, 128, True)]
    order += [(GATE, 0, 1024, False), (GATE, 1024, 1024, True)]
    order += [(UP, 0, 1024, True), (UP, 1024, 1024, False), (UP, 2048, 768, False)]
    order += [(OUT, 0, 1024, True), (QUERY, 0, 1024, False), (KEY, 0, 1024, True)]
    order += [(VALUE, 0, 768, True), (VALUE, 768, 256, False)]
    return [Share(*item) for item in order]


def plus(left, right):
    return left + right


def dot_tn(left, right):
    return lax.dot_general(
        left, right, (((0,), (0,)), ((), ())), preferred_element_type=jnp.float32
    )


BACKWARD_IN = (
    "query",
    "key",
    "value",
    "lse",
    "h_t",
    "h2_t",
    "att_t",
    "d_b",
    "d_res",
    "d_proj",
    "g_ffn",
    "gain",
)


class Backward:
    def __init__(self, refs):
        self.__dict__.update(refs)

    def prepare(self):
        length = self.length[0, 0]
        for block in range(4):
            rows = slice(128 * block, 128 * block + 128)
            place_k = lax.broadcasted_iota(jnp.int32, (128, 512), 0) + 128 * block
            place_q = lax.broadcasted_iota(jnp.int32, (128, 512), 1)
            same = (place_q >= length) == (place_k >= length)
            allowed = same & (place_k <= place_q)
            self.bias[rows, :] = jnp.where(allowed, 0.0, NEGATIVE)

    def multiply(self, left_t, right, item, target, core):
        columns = item.columns(core, 0)

        def rows(m, _):
            product = dot(left_t[tile(m, 256), :], right[:, columns]).astype(jnp.bfloat16)
            product = product.reshape(2, 2, 64, item.width)
            for xx in (0, 1):
                target[xx, m] = product[:, xx]
            return 0

        lax.fori_loop(0, 4, rows, 0)

    def multiply_tall(self, left, right, groups):
        def rows(m, _):
            at = tile(m, 256)
            turned = left[:, at].T
            for columns, targets in groups:
                product = dot(turned, right[:, columns]).astype(jnp.bfloat16)
                for n, (target, xx) in enumerate(targets):
                    target.reshape(2, 2816, 128)[xx, at, :] = product[:, 128 * n : 128 * n + 128]
            return 0

        lax.fori_loop(0, 11, rows, 0)

    def attend_back(self, first, last):
        low = jnp.bfloat16

        def pair(p, _):
            at = tile(p, 128)
            wo_rows = self.w_rows[p].reshape(128, 1024)
            grad = dot_nt(self.d_proj[...], wo_rows).astype(low)
            query = (self.query[:, at].astype(jnp.float32) * SCORE_SCALE).astype(low)
            key, value = self.key[:, at], self.value[:, at]
            left = lax.broadcasted_iota(jnp.int32, (512, 128), 1) < HEAD
            none = jnp.zeros((512, 128), low)
            sides = [
                [jnp.where(side, v, none) for v in (query, key, value, grad)]
                for side in (left, ~left)
            ]
            grad_key, grad_value = [None, None], [None, None]
            for block in (0, 1):
                rows, seen = slice(256 * block, 256 * block + 256), slice(0, 256 * block + 256)
                grad_query = None
                parts_key, parts_value = None, None
                for n, (own_query, own_key, own_value, own_grad) in enumerate(sides):
                    self.d_in[seen, 0:256] = dot_nt(own_key[seen], query[rows])
                    self.d_in[seen, 256:512] = dot_nt(own_value[seen], grad[rows])
                    self.back_rows(p, n, rows, 256 * block + 256)
                    grad_scores, probs = self.grad_scores[seen, :], self.probs[seen, :]
                    part_query = dot_tn(grad_scores, own_key[seen])
                    part_key = dot(grad_scores, own_query[rows])
                    part_value = dot(probs, own_grad[rows])
                    if n == 0:
                        grad_query, parts_key, parts_value = part_query, part_key, part_value
                    else:
                        grad_query += part_query
                        parts_key += part_key
                        parts_value += part_value
                self.query[rows, at] = (grad_query * SCORE_SCALE).astype(low)
                if block == 0:
                    grad_key[0], grad_value[0] = parts_key, parts_value
                else:
                    grad_key = [grad_key[0] + parts_key[:256], parts_key[256:]]
                    grad_value = [grad_value[0] + parts_value[:256], parts_value[256:]]
            for block in (0, 1):
                rows = slice(256 * block, 256 * block + 256)
                self.key[rows, at] = grad_key[block].astype(low)
                self.value[rows, at] = grad_value[block].astype(low)
            return 0

        lax.fori_loop(first, last, pair, 0)

    def back_rows(self, p, n, rows, count):
        low = jnp.bfloat16
        held = self.d_in
        lse = self.lse[p, n : n + 1, rows]

        def first_pass(r, centre):
            keys = tile(r, 64)
            probs = jnp.exp(held[keys, 0:256] + self.bias[keys, rows] - lse)
            held[keys, 0:256] = probs
            self.probs[keys, :] = probs.astype(low)
            return centre + jnp.sum((held[keys, 256:512] * probs).reshape(8, 8, 256), axis=0)

        centre = lax.fori_loop(0, count // 64, first_pass, jnp.zeros((8, 256), jnp.float32), unroll=2)
        centre = jnp.sum(centre, axis=0, keepdims=True)

        def second_pass(r, _):
            keys = tile(r, 64)
            grad = held[keys, 0:256] * (held[keys, 256:512] - centre)
            self.grad_scores[keys, :] = grad.astype(low)
            return 0

        lax.fori_loop(0, count // 64, second_pass, 0, unroll=2)

    def grad_hidden(self, t):
        at = pl.ds(256 * t, 256)
        total = None
        for n, grad in enumerate((self.query, self.key, self.value)):
            part = dot_nt(grad[...], self.w_rows[2 * n : 2 * n + 2].reshape(256, 1024))
            total = part if total is None else total + part
        self.d_in[:, at] = total

    def finish(self):
        self.gain_total[...] = jnp.zeros_like(self.gain_total)

        def rows_of(block, _):
            rows = tile(block, 64)
            values = self.tokens[rows, :].astype(jnp.float32)
            factor = lax.rsqrt(jnp.mean(values * values, axis=-1, keepdims=True) + NORM_EPS)
            normed = values * factor
            grad = self.d_in[rows, :]
            self.gain_total[...] += jnp.sum((grad * normed).reshape(8, 8, 1024), axis=0)
            grad_normed = grad * self.gain[0:1, :].astype(jnp.float32)
            mean = jnp.mean(grad_normed * normed, axis=-1, keepdims=True)
            self.d_in[rows, :] = self.d_res[rows, :] + factor * (
                grad_normed - normed * mean
            )
            return 0

        lax.fori_loop(0, 8, rows_of, 0)
        self.gain_lines[...] = jnp.zeros_like(self.gain_lines)
        lines = [jnp.sum(v[...], axis=0, keepdims=True) for v in (self.gain_total, self.g_ffn)]
        for s in range(8):
            for n, line in enumerate(lines):
                self.gain_lines[s // 2, s % 2, n : n + 1] = line[:, 128 * s : 128 * s + 128]


def backward_kernel(items, *refs):
    refs = list(refs)

    def take(n):
        taken = refs[:n]
        del refs[:n]
        return taken

    kept = take(len(KEPT))
    middle_in, grad_gate_in, grad_up_in = take(3)
    saved_in = dict(zip(BACKWARD_IN, take(len(BACKWARD_IN))))
    tokens_in, length = take(2)
    sums = take(7)
    gain_sums, input_grad_out = take(2)
    saved = dict(zip(BACKWARD_IN, take(len(BACKWARD_IN))))
    d_in, wide, w_rows, bias, probs, grad_scores, gain_total, gain_lines = take(8)
    mine, from_first, from_second, from_z = (take(len(items)) for _ in range(4))
    ring, tall_ring = take(RING), take(2)
    outbox, tall_outbox = take(2), take(2)
    gain_core, gain_x, gain_y, gain_z = take(4)
    send_sems, recv_sems, load_sems, credit = refs
    z, y, x, c = place()
    far = [lax.rem(z + k, 4) for k in range(4)]
    back = [lax.rem(z + 4 - k, 4) for k in range(4)]
    x_other, y_other, c_other = (
        device(z, y, 1 - x, c),
        device(z, 1 - y, x, c),
        device(z, y, x, 1 - c),
    )
    loads = {}

    def load(name, source, target):
        loads[name] = pltpu.make_async_copy(source, target, load_sems.at[len(loads)])
        loads[name].start()

    waited = set()

    def loaded(*names):
        for name in names:
            if name not in waited:
                loads[name].wait()
                waited.add(name)

    load("d_gate", grad_gate_in, wide.at[1])
    load("h2_t", saved_in["h2_t"], saved["h2_t"])
    load("mid", middle_in, wide.at[0])
    load("d_b", saved_in["d_b"], saved["d_b"])
    load("wo_rows", kept[OUT].reshape(8, 2, 64, 1024), w_rows)
    for name in BACKWARD_IN:
        if name not in loads:
            load(name, saved_in[name], saved[name])
    greet()
    wires = Wires(send_sems, recv_sems)
    work = Backward(
        dict(
            saved,
            tokens=saved["d_b"],
            length=length,
            w_rows=w_rows,
            probs=probs,
            grad_scores=grad_scores,
            bias=bias,
            d_in=d_in,
            gain_total=gain_total,
            gain_lines=gain_lines,
        )
    )
    tall_items = [i for i, item in enumerate(items) if item.tall]
    wide_items = [i for i, item in enumerate(items) if not item.tall]

    def slot(i, k):
        return SUM_SLOTS * i + k

    def core_slots(i):
        return (slot(i, 0), slot(i, 8))

    def from_core(i):
        if items[i].tall:
            return tall_ring[tall_items.index(i)]
        return ring[wide_items.index(i) % RING].at[..., : items[i].width]

    def produce(i):
        item = items[i]
        if item.tall:
            number = tall_items.index(i)
            if number == 0:
                loaded("mid", "d_b")
                groups = []
                for core, boxes in ((1 - c, tall_outbox), (c, [mine[j] for j in tall_items])):
                    columns = pl.ds(pl.multiple_of(512 * core, 512), 512)
                    groups.append((columns, [(boxes[j], xx) for xx in (0, 1) for j in (0, 1)]))
                work.multiply_tall(wide.at[0], saved["d_b"], groups)
                load("d_up", grad_up_in, wide.at[0])
                load("tokens", tokens_in, saved["d_b"])
            box = tall_outbox[number]
        else:
            number = wide_items.index(i)
            if number >= 2:
                wires.finish(lambda s: s in core_slots(wide_items[number - 2]))
            box = outbox[number % 2].at[..., : item.width]
            left, right, names = {
                GATE: (saved["h2_t"], wide.at[1], ("h2_t", "d_gate")),
                UP: (saved["h2_t"], wide.at[0], ("d_up",)),
                OUT: (saved["att_t"], saved["d_proj"], ("att_t", "d_proj")),
                QUERY: (saved["h_t"], saved["query"], ("h_t",)),
                KEY: (saved["h_t"], saved["key"], ()),
                VALUE: (saved["h_t"], saved["value"], ()),
            }[item.weight]
            loaded(*names)
            multiply = partial(work.multiply, left, right, item)
            if number >= RING:
                pl.semaphore_wait(credit, 1)
            multiply(box, 1 - c)
        for xx in (0, 1):
            wires.send(core_slots(i)[xx], box.at[xx], from_core(i).at[xx], c_other)
        if not item.tall:
            multiply(mine[i], c)

    def first_hop(i):
        item, own, other = items[i], mine[i], from_core(i)
        for xx in (0, 1):
            wires.arrived(core_slots(i)[xx], other.at[xx])

        def add(at, _):
            for xx in (0, 1):
                for yy in (0, 1):
                    own[xx, at, yy] = plus(own[xx, at, yy], other[xx, at, yy])
            return 0

        lax.fori_loop(0, 4, add, 0)
        if not item.tall and wide_items.index(i) + RING < len(wide_items):
            pl.semaphore_signal(credit, inc=1, device_id=c_other, device_id_type=MESH)
        if item.x_first:
            wires.send(slot(i, 1), own.at[1 - x], from_first[i], x_other)
        else:
            wires.send(slot(i, 1), own.at[:, :, 1 - y], from_first[i], y_other)

    def second_hop(i):
        item, own, other = items[i], mine[i], from_first[i]
        wires.arrived(slot(i, 1), other)

        def add(at, _):
            for side in (0, 1):
                if item.x_first:
                    own[x, at, side] = plus(own[x, at, side], other[at, side])
                else:
                    own[side, at, y] = plus(own[side, at, y], other[side, at])
            return 0

        lax.fori_loop(0, 4, add, 0)
        if item.x_first:
            wires.send(slot(i, 2), own.at[x, :, 1 - y], from_second[i], y_other)
        else:
            to_z(i, lambda k: own.at[:, far[k], y])

    def to_z(i, block):
        for k in (1, 2, 3):
            wires.send(slot(i, 2 + k), block(k), from_z[i].at[k - 1], device(far[k], y, x, c))

    def z_total(i, own_part):
        total = own_part.astype(jnp.float32)
        for k in (1, 2, 3):
            wires.arrived(slot(i, 2 + k), from_z[i].at[k - 1])
            total += from_z[i][k - 1].astype(jnp.float32)
        return total.astype(jnp.bfloat16)

    def third_hop(i):
        item, own, other = items[i], mine[i], from_second[i]
        if not item.x_first:
            own[:, z, y] = z_total(i, own[:, z, y])
            wires.send(slot(i, 2), own.at[:, z, y], other, x_other)
            return
        wires.arrived(slot(i, 2), other)

        def add(at, _):
            own[x, at, y] = plus(own[x, at, y], other[at])
            return 0

        lax.fori_loop(0, 4, add, 0)
        to_z(i, lambda k: own.at[x, far[k], y])

    def fourth_hop(i):
        item, own = items[i], mine[i]
        if not item.x_first:
            wires.arrived(slot(i, 2), from_second[i])
            block = item.half(sums[item.weight], c)
            block[...] = plus(own[:, z, y], from_second[i][...])
            wires.send(slot(i, 7), block, block, c_other)
            return
        block = item.quarter(sums[item.weight], c, x)
        block[...] = z_total(i, own[x, z, y])
        wires.send(slot(i, 6), block, block, x_other)

    def to_sibling(i):
        item = items[i]
        if item.x_first:
            wires.arrived(slot(i, 6), item.quarter(sums[item.weight], c, 1 - x))
            block = item.half(sums[item.weight], c)
            wires.send(slot(i, 7), block, block, c_other)

    def complete(i):
        item = items[i]
        wires.arrived(slot(i, 7), item.half(sums[item.weight], 1 - c))
        wires.finish(lambda s: s // SUM_SLOTS == i)

    base = SUM_SLOTS * len(items)

    def gains_one():
        wires.send(base, gain_lines, gain_core, c_other)

    def gains_two():
        wires.arrived(base, gain_core)
        gain_core[...] = gain_lines[...] + gain_core[...]
        wires.send(base + 1, gain_core, gain_x, x_other)

    def gains_three():
        wires.arrived(base + 1, gain_x)
        gain_x[...] = gain_core[...] + gain_x[...]
        wires.send(base + 2, gain_x.at[:, 1 - y], gain_y, y_other)

    def gains_four():
        wires.arrived(base + 2, gain_y)
        gain_y[...] = gain_x[:, y] + gain_y[...]
        for k in (1, 2, 3):
            wires.send(base + 2 + k, gain_y.at[far[k]], gain_z.at[z], device(far[k], y, x, c))
        gain_z[z] = gain_y[z]

    def gains_five():
        for k in (1, 2, 3):
            wires.arrived(base + 2 + k, gain_z.at[back[k]])
        gain_sums[...] = (gain_z[0] + gain_z[1]) + (gain_z[2] + gain_z[3])

    def fetch_rows(t):
        for n in range(3):
            load(("rows", n, t), kept[n].at[t], w_rows.at[2 * n : 2 * n + 2])

    def attend_back(p):
        if p == 0:
            loaded("query", "key", "value", "lse", "d_proj", "wo_rows")
        work.attend_back(p, p + 1)
        if p == 7:
            fetch_rows(0)

    def grad_hidden(t):
        loaded(*[("rows", n, t) for n in range(3)])
        work.grad_hidden(t)
        if t < 3:
            fetch_rows(t + 1)

    def finish():
        loaded("tokens", "d_res", "g_ffn", "gain")
        work.finish()
        load("d_in", d_in, input_grad_out)
        gains_one()

    beside = {1: [work.prepare]}
    for p in range(8):
        beside.setdefault(1 + p, []).append(partial(attend_back, p))
    for t in range(4):
        beside.setdefault(9 + t // 2, []).append(partial(grad_hidden, t))
    beside.setdefault(11, []).append(finish)
    for n, task in enumerate((gains_two, gains_three, gains_four, gains_five)):
        beside.setdefault(13 + 2 * n, []).append(task)

    stages = (complete, to_sibling, fourth_hop, third_hop, second_hop, first_hop, produce)
    lates = (12, 10, 8, 6, 4, 2, 0)
    for step in range(len(items) + lates[0]):
        for late, stage in zip(lates, stages):
            if 0 <= step - late < len(items):
                stage(step - late)
        for task in beside.get(step, []):
            task()
    loaded("d_in")
    wires.finish()


def backward(tokens, lengths, kept, saved):
    items = share_items()
    low, wide = jnp.bfloat16, jnp.float32
    dtypes = {name: (shape, dtype) for name, shape, dtype in FORWARD_OUTS}
    shapes = [
        jax.ShapeDtypeStruct((2, 2, 2, 352, 128) if n is None else (2, 64, n), low) for n in COLUMNS
    ]
    shapes += [jax.ShapeDtypeStruct((8, 128), wide), jax.ShapeDtypeStruct((512, 1024), wide)]
    count = SUM_SLOTS * len(items) + 6
    anywhere = pl.BlockSpec(memory_space=pl.ANY)
    in_vmem = pl.BlockSpec(memory_space=pltpu.VMEM)
    n_loads = 6 + len(BACKWARD_IN) + 12

    def buffers(lead_of):
        return [pltpu.VMEM(lead_of(item) + item.block, low) for item in items]

    out = pl.pallas_call(
        partial(backward_kernel, items),
        out_shape=shapes,
        in_specs=[anywhere] * (len(KEPT) + 3 + len(BACKWARD_IN) + 1)
        + [pl.BlockSpec(memory_space=pltpu.SMEM)],
        out_specs=[in_vmem] * 8 + [anywhere],
        scratch_shapes=[pltpu.VMEM(*dtypes[name]) for name in BACKWARD_IN]
        + [
            pltpu.VMEM((512, 1024), wide),
            pltpu.VMEM((2, 512, 2816), low),
            pltpu.VMEM((8, 2, 64, 1024), low),
            pltpu.VMEM((512, 512), wide),
            pltpu.VMEM((512, 256), low),
            pltpu.VMEM((512, 256), low),
            pltpu.VMEM((8, 1024), wide),
            pltpu.VMEM((4, 2, 8, 128), wide),
        ]
        + buffers(lambda item: (2, 4, 2))
        + buffers(lambda item: (4, 2) if item.x_first else (2, 4))
        + buffers(lambda item: (4,) if item.x_first else (2,))
        + buffers(lambda item: (3,) if item.x_first else (3, 2))
        + [pltpu.VMEM((2, 4, 2, 64, 512), low)] * RING
        + [pltpu.VMEM((2, 4, 2, 352, 128), low)] * 2
        + [pltpu.VMEM((2, 4, 2, 64, 512), low)] * 2
        + [pltpu.VMEM((2, 4, 2, 352, 128), low)] * 2
        + [
            pltpu.VMEM((4, 2, 8, 128), wide),
            pltpu.VMEM((4, 2, 8, 128), wide),
            pltpu.VMEM((4, 8, 128), wide),
            pltpu.VMEM((4, 8, 128), wide),
            pltpu.SemaphoreType.DMA((count,)),
            pltpu.SemaphoreType.DMA((count,)),
            pltpu.SemaphoreType.DMA((n_loads,)),
            pltpu.SemaphoreType.REGULAR,
        ],
        compiler_params=pltpu.CompilerParams(
            collective_id=1, has_side_effects=True, vmem_limit_bytes=63 * MIB
        ),
        name="backward_sum",
    )(
        *kept,
        saved["mid"],
        saved["d_gate"],
        saved["d_up"],
        *[saved[name] for name in BACKWARD_IN],
        tokens,
        lengths,
    )
    return out[:7], out[7], out[8]


def unpack_kernel(*refs):
    blocks, (gain_sums, mixed, d_in) = refs[:7], refs[7:10]
    sums, (gain_attn, gain_ffn, mixed_out, input_out) = refs[10:17], refs[17:21]
    held, wide = refs[21:28], refs[28:35]
    mixed_held, input_held, in_sems, out_sems = refs[35:]
    sources = (d_in, mixed, *blocks)
    places = (input_held, mixed_held, *held)
    results = (input_held, mixed_held, *wide)
    targets = (input_out, mixed_out, *sums)
    ins = [pltpu.make_async_copy(a, b, in_sems.at[n]) for n, (a, b) in enumerate(zip(sources, places))]
    outs = [pltpu.make_async_copy(a, b, out_sems.at[n]) for n, (a, b) in enumerate(zip(results, targets))]
    order = (6, 7, 8, 2, 3, 4, 5, 0, 1)
    for n in order:
        ins[n].start()
    for n in order:
        ins[n].wait()
        if n == 8:
            for b in range(8):
                wide[6][:, 128 * b : 128 * b + 128] = held[6][b // 4, b // 2 % 2, b % 2].astype(
                    jnp.float32
                )
        elif n >= 2:
            wide[n - 2][...] = held[n - 2][...].astype(jnp.float32)
        outs[n].start()
    gain_attn[...] = gain_sums[0:1]
    gain_ffn[...] = gain_sums[1:2]
    for n in order:
        outs[n].wait()


def unpack(blocks, gain_sums, mixed, d_in):
    wide = jnp.float32
    anywhere = pl.BlockSpec(memory_space=pl.ANY)
    in_vmem = pl.BlockSpec(memory_space=pltpu.VMEM)
    shapes = [
        jax.ShapeDtypeStruct((352, 1024) if n is None else (2, 64, n), wide) for n in COLUMNS
    ]
    held = [pltpu.VMEM(b.shape, b.dtype) for b in blocks]
    held += [pltpu.VMEM(v.shape, wide) for v in shapes]
    held += [pltpu.VMEM(v.shape, v.dtype) for v in (mixed, d_in)]
    shapes += [jax.ShapeDtypeStruct((1, 128), wide)] * 2
    shapes += [jax.ShapeDtypeStruct(v.shape, v.dtype) for v in (mixed, d_in)]
    out = pl.pallas_call(
        unpack_kernel,
        out_shape=shapes,
        in_specs=[anywhere] * 7 + [in_vmem] + [anywhere] * 2,
        out_specs=[anywhere] * 7 + [in_vmem] * 2 + [anywhere] * 2,
        scratch_shapes=held + [pltpu.SemaphoreType.DMA((9,)), pltpu.SemaphoreType.DMA((9,))],
        compiler_params=pltpu.CompilerParams(vmem_limit_bytes=62 * MIB),
        name="unpack",
    )(*blocks, gain_sums, mixed, d_in)
    sums = [s.reshape(-1, s.shape[-1]) for s in out[:7]]
    return sums, [g.reshape(128) for g in out[7:9]], out[9], out[10]


def gather_plain(weights, gains):
    everything = (*weights, *gains)
    whole = [lax.all_gather(v, "dp", axis=0, tiled=True) for v in everything]
    return whole[: len(weights)], whole[len(weights) :]


def sum_plain(grads, gain_grads):
    shares = [
        lax.psum_scatter(g.astype(jnp.float32), "dp", scatter_dimension=0, tiled=True)
        for g in (*grads, *gain_grads)
    ]
    sums = [lax.psum(s, ("rep", "cores")) for s in shares]
    return sums[: len(grads)], sums[len(grads) :]


def on_any_device(
    tokens,
    norm_attn,
    w_query,
    w_key,
    w_value,
    w_out,
    norm_ffn,
    w_gate,
    w_up,
    w_down,
    lengths,
    cotangent,
):
    rows = tokens.shape[0]
    low = jnp.bfloat16
    allowed, valid = masks(lengths, rows)
    whole, gains = gather_plain(
        (w_query, w_key, w_value, w_out, w_gate, w_up, w_down), (norm_attn, norm_ffn)
    )
    full_query, full_key, full_value, full_out, full_gate, full_up, full_down = whole
    gain_attn, gain_ffn = gains
    inputs = tokens.astype(jnp.float32)
    normed, factor = normalize(inputs)
    hidden = (normed * gain_attn.astype(jnp.float32)).astype(low)
    query = matmul(hidden, full_query).astype(low)
    keyed = matmul(hidden, full_key).astype(low)
    valued = matmul(hidden, full_value).astype(low)
    query_groups, key_groups, value_groups = (to_groups(query), to_groups(keyed), to_groups(valued))
    attended_groups, log_total = lax.map(
        partial(attend, allowed), (query_groups, key_groups, value_groups)
    )
    attended = from_groups(attended_groups)
    residual = inputs + matmul(attended, full_out)
    normed_two, factor_two = normalize(residual)
    hidden_two = (normed_two * gain_ffn.astype(jnp.float32)).astype(low)
    gate = matmul(hidden_two, full_gate)
    upward = matmul(hidden_two, full_up)
    sigma = jax.nn.sigmoid(gate)
    middle = (gate * sigma * upward).astype(low)
    mixed = (valid[:, None] * (residual + matmul(middle, full_down))).astype(low)
    grad_output = cotangent.astype(jnp.float32) * valid[:, None]
    grad_branch = grad_output.astype(low)
    grad_down = matmul_tn(middle, grad_branch)
    grad_middle = matmul_nt(grad_branch, full_down)
    grad_gate_rows = (grad_middle * upward * sigma * (1.0 + gate * (1.0 - sigma))).astype(low)
    grad_up_rows = (grad_middle * gate * sigma).astype(low)
    grad_gate = matmul_tn(hidden_two, grad_gate_rows)
    grad_up = matmul_tn(hidden_two, grad_up_rows)
    grad_hidden_two = matmul_nt(grad_gate_rows, full_gate) + matmul_nt(grad_up_rows, full_up)
    grad_gain_ffn = jnp.sum(grad_hidden_two * normed_two, axis=0)
    grad_residual = grad_output + norm_back(
        grad_hidden_two * gain_ffn.astype(jnp.float32), normed_two, factor_two
    )
    grad_proj = grad_residual.astype(low)
    grad_out = matmul_tn(attended, grad_proj)
    grad_attended = matmul_nt(grad_proj, full_out).astype(low)
    grad_query_g, grad_key_g, grad_value_g = lax.map(
        partial(attend_back, allowed),
        (query_groups, key_groups, value_groups, to_groups(grad_attended), log_total),
    )
    grad_query_rows = from_groups(grad_query_g)
    grad_key_rows = from_groups(grad_key_g)
    grad_value_rows = from_groups(grad_value_g)
    grad_query = matmul_tn(hidden, grad_query_rows)
    grad_key = matmul_tn(hidden, grad_key_rows)
    grad_value = matmul_tn(hidden, grad_value_rows)
    grad_hidden = (
        matmul_nt(grad_query_rows, full_query)
        + matmul_nt(grad_key_rows, full_key)
        + matmul_nt(grad_value_rows, full_value)
    )
    grad_gain_attn = jnp.sum(grad_hidden * normed, axis=0)
    input_grad = grad_residual + norm_back(
        grad_hidden * gain_attn.astype(jnp.float32), normed, factor
    )
    grads = (grad_query, grad_key, grad_value, grad_out, grad_gate, grad_up, grad_down)
    sums, gain_sums = sum_plain([g.astype(low) for g in grads], (grad_gain_attn, grad_gain_ffn))
    return (
        mixed,
        input_grad,
        gain_sums[0],
        sums[0],
        sums[1],
        sums[2],
        sums[3],
        gain_sums[1],
        sums[4],
        sums[5],
        sums[6],
    )


def on_tuned_device(
    tokens,
    norm_attn,
    w_query,
    w_key,
    w_value,
    w_out,
    norm_ffn,
    w_gate,
    w_up,
    w_down,
    lengths,
    cotangent,
):
    weights = (w_query, w_key, w_value, w_out, w_gate, w_up, w_down)
    kept, saved = forward(tokens, cotangent, lengths, weights, (norm_attn, norm_ffn))
    blocks, gain_lines, d_in = backward(tokens, lengths, kept, saved)
    sums, gain_sums, mixed, d_in = unpack(blocks, gain_lines, saved["mixed"], d_in)
    return (
        mixed,
        d_in,
        gain_sums[0],
        *sums[:4],
        gain_sums[1],
        *sums[4:],
    )


def solution(mesh):
    tuned = dict(mesh.shape) == {"dp": 8, "rep": 2, "cores": 2}
    tokens_placed = P(("dp", "rep", "cores"), None)
    share, gain = P("dp", None), P("dp")
    return jax.shard_map(
        on_tuned_device if tuned else on_any_device,
        mesh=mesh,
        in_specs=(
            tokens_placed,
            gain,
            share,
            share,
            share,
            share,
            gain,
            share,
            share,
            share,
            tokens_placed,
            tokens_placed,
        ),
        out_specs=(
            tokens_placed,
            tokens_placed,
            gain,
            share,
            share,
            share,
            share,
            gain,
            share,
            share,
            share,
        ),
        check_vma=False,
    )
```

```python
from functools import partial

import jax
import jax.numpy as jnp
from jax import lax
from jax.experimental import pallas as pl
from jax.experimental.pallas import tpu as pltpu
from jax.sharding import PartitionSpec as P

HEADS = 16
HEAD = 64


NORM_EPS = 1e-05
SCORE_SCALE = 0.125
NEGATIVE = -1e30
head_group = 4
MESH = pl.DeviceIdType.MESH
MIB = 1024 * 1024


def masks(block_len, rows):
    bounds = jnp.cumsum(block_len[0])
    place = jnp.arange(rows, dtype=jnp.int32)
    segment = jnp.sum((place[:, None] >= bounds[None, :]).astype(jnp.int32), axis=1)
    allowed = (segment[:, None] == segment[None, :]) & (place[None, :] <= place[:, None])
    valid = (segment < block_len.shape[1]).astype(jnp.float32)
    return (allowed, valid)


def normalize(values):
    factor = lax.rsqrt(jnp.mean(values * values, axis=-1, keepdims=True) + NORM_EPS)
    return (values * factor, factor)


def norm_back(grad_normed, normed, factor):
    return factor * (grad_normed - normed * jnp.mean(grad_normed * normed, axis=-1, keepdims=True))


def matmul(left, right):
    return jnp.dot(left, right, preferred_element_type=jnp.float32)


def matmul_tn(left, right):
    return lax.dot_general(
        left, right, (((0,), (0,)), ((), ())), preferred_element_type=jnp.float32
    )


def matmul_nt(left, right):
    return lax.dot_general(
        left, right, (((1,), (1,)), ((), ())), preferred_element_type=jnp.float32
    )


def to_groups(matrix):
    rows = matrix.shape[0]
    split = matrix.reshape(rows, HEADS // head_group, head_group, HEAD)
    return split.transpose(1, 2, 0, 3)


def from_groups(grouped):
    rows = grouped.shape[2]
    return grouped.transpose(2, 0, 1, 3).reshape(rows, HEADS * HEAD)


def group_scores(allowed, query_g, key_g):
    raw = (
        jnp.einsum("hqe,hke->hqk", query_g, key_g, preferred_element_type=jnp.float32) * SCORE_SCALE
    )
    return jnp.where(allowed[None], raw, NEGATIVE)


def attend(allowed, operands):
    query_g, key_g, value_g = operands
    scores = group_scores(allowed, query_g, key_g)
    top = jnp.max(scores, axis=-1, keepdims=True)
    expo = jnp.exp(scores - top)
    total = jnp.sum(expo, axis=-1, keepdims=True)
    probs_low = (expo / total).astype(jnp.bfloat16)
    result = jnp.einsum("hqk,hke->hqe", probs_low, value_g, preferred_element_type=jnp.float32)
    return (result.astype(jnp.bfloat16), top[..., 0] + jnp.log(total[..., 0]))


def attend_back(allowed, operands):
    query_g, key_g, value_g, grad_g, lse = operands
    scores = group_scores(allowed, query_g, key_g)
    probs = jnp.exp(scores - lse[..., None])
    grad_probs = jnp.einsum("hqe,hke->hqk", grad_g, value_g, preferred_element_type=jnp.float32)
    centre = jnp.sum(grad_probs * probs, axis=-1, keepdims=True)
    grad_scores = (probs * (grad_probs - centre)).astype(jnp.bfloat16)
    grad_query = (
        jnp.einsum("hqk,hke->hqe", grad_scores, key_g, preferred_element_type=jnp.float32)
        * SCORE_SCALE
    )
    grad_key = (
        jnp.einsum("hqk,hqe->hke", grad_scores, query_g, preferred_element_type=jnp.float32)
        * SCORE_SCALE
    )
    grad_value = jnp.einsum(
        "hqk,hqe->hke", probs.astype(jnp.bfloat16), grad_g, preferred_element_type=jnp.float32
    )
    return (
        grad_query.astype(jnp.bfloat16),
        grad_key.astype(jnp.bfloat16),
        grad_value.astype(jnp.bfloat16),
    )


class Part:
    def __init__(self, weight, tall, start, size, no_x):
        self.weight, self.tall, self.start, self.size = weight, tall, start, size
        self.no_x = no_x

    def quarter(self, ref, lead, c, x):
        if self.tall:
            columns = pl.ds(pl.multiple_of(c * 512 + x * 256, 256), 256)
            return ref.at[(*lead, pl.ds(self.start, self.size), columns)]
        return ref.at[(*lead, x, slice(None), self.columns(c))]

    def half(self, ref, lead, c):
        if self.tall:
            columns = pl.ds(pl.multiple_of(c * 512, 512), 512)
            return ref.at[(*lead, pl.ds(self.start, self.size), columns)]
        return ref.at[(*lead, slice(None), slice(None), self.columns(c))]

    def columns(self, c):
        width = self.size // 2
        return pl.ds(pl.multiple_of(self.start + c * width, 128), width)


def pieces(total, most):
    return [(start, min(most, total - start)) for start in range(0, total, most)]


def place():
    d = lax.axis_index("dp")
    return lax.div(d, 2), lax.rem(d, 2), lax.axis_index("rep"), lax.axis_index("cores")


def device(z, y, x, c):
    return {"dp": 2 * z + y, "rep": x, "cores": c}


def greet():
    z, y, x, c = place()
    barrier = pltpu.get_barrier_semaphore()
    others = [device(lax.rem(z + k, 4), y, x, c) for k in (1, 2, 3)]
    others += [device(z, 1 - y, x, c), device(z, y, 1 - x, c), device(z, y, x, 1 - c)]
    for other in others:
        pl.semaphore_signal(barrier, inc=1, device_id=other, device_id_type=MESH)
    pl.semaphore_wait(barrier, len(others))


class Wires:
    def __init__(self, send_sems, recv_sems):
        self.send_sems, self.recv_sems, self.sent = send_sems, recv_sems, []

    def copy(self, slot, source, target, other):
        return pltpu.make_async_remote_copy(
            src_ref=source,
            dst_ref=target,
            send_sem=self.send_sems.at[slot],
            recv_sem=self.recv_sems.at[slot],
            device_id=other,
            device_id_type=MESH,
        )

    def send(self, slot, source, target, other):
        copy = self.copy(slot, source, target, other)
        copy.start()
        self.sent.append((slot, copy))

    def arrived(self, slot, target):
        z, y, x, c = place()
        self.copy(slot, target, target, device(z, y, x, 1 - c)).wait_recv()

    def finish(self, chosen=lambda slot: True):
        for slot, copy in self.sent:
            if chosen(slot):
                copy.wait_send()
        self.sent = [(slot, copy) for slot, copy in self.sent if not chosen(slot)]


GATHER_SLOTS = 12
LAG = 2
ALL = slice(None)
COLUMNS = (1024, 1024, 1024, 1024, 2816, 2816, None)
QUERY, KEY, VALUE, OUT, GATE, UP, DOWN = range(7)
TILE = 512


FF_CHUNKS = tuple(pieces(2816, 512))


def gather_items():
    order = [(QUERY, 0, 256, True), (QUERY, 256, 768, False), (KEY, 0, 1024, True)]
    order += [(VALUE, 0, 1024, False), (OUT, 0, 1024, False)]
    order += [(DOWN, 0, 128, False), (DOWN, 128, 128, True), (DOWN, 256, 96, False)]
    for n, (start, size) in enumerate(FF_CHUNKS):
        order += [(GATE, start, size, n == 5), (UP, start, size, n in (0, 3, 5))]
    return [Part(w, w == DOWN, start, size, no_x) for w, start, size, no_x in order]


def dot(left, right):
    return lax.dot_general(
        left, right, (((1,), (0,)), ((), ())), preferred_element_type=jnp.float32
    )


def dot_nt(left, right):
    return lax.dot_general(
        left, right, (((1,), (1,)), ((), ())), preferred_element_type=jnp.float32
    )


def tile(index, size):
    return pl.ds(pl.multiple_of(index * size, size), size)


def weight_columns(ref, at):
    return ref[:, :, :, :, at].reshape(1024, -1)


class Forward:
    def __init__(self, refs):
        self.__dict__.update(refs)

    def prepare(self):
        for s in range(8):
            self.gain[:, 128 * s : 128 * s + 128] = self.gains[s // 2, s % 2]
        length = self.length[0, 0]
        for block in range(4):
            rows = slice(128 * block, 128 * block + 128)
            place_q = lax.broadcasted_iota(jnp.int32, (128, 512), 0) + 128 * block
            place_k = lax.broadcasted_iota(jnp.int32, (128, 512), 1)
            same = (place_q >= length) == (place_k >= length)
            allowed = same & (place_k <= place_q)
            self.bias[rows, :] = jnp.where(allowed, 0.0, NEGATIVE)

        def normed(block, _):
            rows = tile(block, 64)
            values = self.tokens[rows, :].astype(jnp.float32)
            factor = lax.rsqrt(jnp.mean(values * values, axis=-1, keepdims=True) + NORM_EPS)
            gain = self.gain[0:1, :].astype(jnp.float32)
            self.hidden[rows, :] = (values * factor * gain).astype(jnp.bfloat16)
            place = lax.broadcasted_iota(jnp.int32, (64, 1024), 0) + 64 * block
            d_b = jnp.where(place < length, self.cotangent[rows, :].astype(jnp.float32), 0.0)
            self.d_b[rows, :] = d_b.astype(jnp.bfloat16)
            return 0

        lax.fori_loop(0, 8, normed, 0)
        self.turn(self.hidden, self.h_t)
        self.out("d_b")

    def turn(self, matrix, turned):
        def columns(n, _):
            at = tile(n, 128)
            turned[at, :] = matrix[:, at].astype(jnp.float32).T.astype(jnp.bfloat16)
            return 0

        lax.fori_loop(0, 8, columns, 0)

    def project(self, weight, result):
        def columns(n, _):
            at = tile(n, TILE)
            result[:, at] = dot(self.hidden[...], weight_columns(weight, at)).astype(jnp.bfloat16)
            return 0

        lax.fori_loop(0, 1024 // TILE, columns, 0)

    def attend(self, first, last):
        def pair(p, _):
            at = tile(p, 128)
            left = lax.broadcasted_iota(jnp.int32, (256, 128), 1) < HEAD
            for block in (0, 1):
                rows, seen = slice(256 * block, 256 * block + 256), slice(0, 256 * block + 256)
                query = self.query[rows, at].astype(jnp.float32) * SCORE_SCALE
                both = jnp.concatenate(
                    [jnp.where(left, query, 0.0), jnp.where(left, 0.0, query)], axis=0
                ).astype(jnp.bfloat16)
                bias = self.bias[rows, seen]
                scores = dot_nt(both, self.key[seen, at]) + jnp.concatenate([bias, bias], axis=0)
                top = jnp.max(scores, axis=-1, keepdims=True)
                expo = jnp.exp(scores - top)
                total = jnp.sum(expo, axis=-1, keepdims=True)
                probs = (expo * (1.0 / total)).astype(jnp.bfloat16)
                result = dot(probs, self.value[seen, at])
                self.attended[rows, at] = jnp.where(left, result[:256], result[256:]).astype(
                    jnp.bfloat16
                )
                lse = top + jnp.log(total)
                turned = jnp.where(left, lse[:256], lse[256:]).T
                self.lse[p, 0:1, rows] = turned[0:1]
                self.lse[p, 1:2, rows] = turned[HEAD : HEAD + 1]
            return 0

        lax.fori_loop(first, last, pair, 0)

    def project_out(self):
        def columns(n, _):
            at = tile(n, TILE)
            self.residual[:, at] = self.tokens[:, at].astype(jnp.float32) + dot(
                self.attended[...], weight_columns(self.w_out, at)
            )
            return 0

        lax.fori_loop(0, 1024 // TILE, columns, 0)

        def normed(block, _):
            rows = tile(block, 64)
            values = self.residual[rows, :]
            factor = lax.rsqrt(jnp.mean(values * values, axis=-1, keepdims=True) + NORM_EPS)
            gain = self.gain[8:9, :].astype(jnp.float32)
            self.h2[rows, :] = (values * factor * gain).astype(jnp.bfloat16)
            return 0

        lax.fori_loop(0, 8, normed, 0)
        self.turn(self.h2, self.h2_t)
        self.turn(self.attended, self.att_t)
        for name in ("residual", "query", "key", "value", "lse", "h_t", "h2_t", "att_t"):
            self.out(name)

    def grad_of_middle(self, start, size):
        at = pl.ds(start, size)
        self.d_up[:, at] = dot_nt(self.d_b[...], self.w_down[at, :]).astype(jnp.bfloat16)

    def feed_forward(self, start, size):
        at = pl.ds(start, size)
        low = jnp.bfloat16
        gate = dot(self.h2[...], weight_columns(self.w_gate, at))
        upward = dot(self.h2[...], weight_columns(self.w_up, at))
        grad_middle = self.d_up[:, at].astype(jnp.float32)
        sigma = 0.5 * jnp.tanh(0.5 * gate) + 0.5
        silu = gate * sigma
        self.mid[:, at] = (silu * upward).astype(low)
        self.d_up[:, at] = (grad_middle * silu).astype(low)
        self.d_gate[:, at] = (grad_middle * upward * (sigma + silu - silu * sigma)).astype(low)

    def feed_forward_back(self, start, size):
        at = pl.ds(start, size)
        gate_w, up_w = weight_columns(self.w_gate, at), weight_columns(self.w_up, at)
        d_gate, d_up = self.d_gate[:, at], self.d_up[:, at]
        for j in range(1024 // TILE):
            part = slice(TILE * j, TILE * j + TILE)
            grad = dot_nt(d_gate, gate_w[part, :]) + dot_nt(d_up, up_w[part, :])
            if start == 0:
                self.d_h2[:, part] = grad
            else:
                self.d_h2[:, part] += grad

    def flush(self, start, size):
        for name in ("mid", "d_gate", "d_up"):
            self.out(name, pl.ds(start, size))

    def finish(self):
        length = self.length[0, 0]
        self.g_ffn[...] = jnp.zeros_like(self.g_ffn)

        def rows_of(block, _):
            rows = tile(block, 64)
            place = lax.broadcasted_iota(jnp.int32, (64, 1024), 0) + 64 * block
            residual = self.residual[rows, :]
            factor = lax.rsqrt(jnp.mean(residual * residual, axis=-1, keepdims=True) + NORM_EPS)
            normed = residual * factor
            grad = self.d_h2[rows, :]
            self.g_ffn[...] += jnp.sum((grad * normed).reshape(8, 8, 1024), axis=0)
            grad_normed = grad * self.gain[8:9, :].astype(jnp.float32)
            grad_out = jnp.where(place < length, self.cotangent[rows, :].astype(jnp.float32), 0.0)
            mean = jnp.mean(grad_normed * normed, axis=-1, keepdims=True)
            d_res = grad_out + factor * (grad_normed - normed * mean)
            self.d_res[rows, :] = d_res
            self.d_proj[rows, :] = d_res.astype(jnp.bfloat16)
            return 0

        lax.fori_loop(0, 8, rows_of, 0)
        for name in ("d_res", "d_proj", "g_ffn", "gain"):
            self.out(name)


FORWARD_OUTS = (
    ("residual", (512, 1024), jnp.float32),
    ("query", (512, 1024), jnp.bfloat16),
    ("key", (512, 1024), jnp.bfloat16),
    ("value", (512, 1024), jnp.bfloat16),
    ("lse", (8, 8, 512), jnp.float32),
    ("h_t", (1024, 512), jnp.bfloat16),
    ("h2_t", (1024, 512), jnp.bfloat16),
    ("att_t", (1024, 512), jnp.bfloat16),
    ("d_b", (512, 1024), jnp.bfloat16),
    ("mid", (512, 2816), jnp.bfloat16),
    ("d_gate", (512, 2816), jnp.bfloat16),
    ("d_up", (512, 2816), jnp.bfloat16),
    ("d_res", (512, 1024), jnp.float32),
    ("d_proj", (512, 1024), jnp.bfloat16),
    ("g_ffn", (8, 1024), jnp.float32),
    ("gain", (16, 1024), jnp.bfloat16),
)
FORWARD_OWN = (
    ("hidden", (512, 1024), jnp.bfloat16),
    ("attended", (512, 1024), jnp.bfloat16),
    ("h2", (512, 1024), jnp.bfloat16),
    ("d_h2", (512, 1024), jnp.float32),
    ("bias", (512, 512), jnp.float32),
)
OUT_COPIES = len(FORWARD_OUTS) - 3 + 3 * len(FF_CHUNKS)
KEPT = (QUERY, KEY, VALUE, OUT, DOWN)


def share_shape(columns):
    return (352, 1024) if columns is None else (2, 64, columns)


def forward_kernel(items, *refs):
    refs = list(refs)

    def take(n):
        taken = refs[:n]
        del refs[:n]
        return taken

    shares = take(7)
    gain_attn, gain_ffn, tokens, cotangent, length = take(5)
    kept = take(len(KEPT))
    names = [name for name, _, _ in FORWARD_OUTS]
    outs = dict(zip(names, take(len(names))))
    full = take(7)
    full_gains, gains = take(2)
    own_names = names + [name for name, _, _ in FORWARD_OWN]
    state = dict(zip(own_names, take(len(own_names))))
    send_sems, recv_sems, own_sems, keep_sems, out_sems = refs
    outgoing = []

    def put(name, columns=None):
        source, target = state[name], outs[name]
        if columns is not None:
            source, target = source.at[:, columns], target.at[:, columns]
        outgoing.append(pltpu.make_async_copy(source, target, out_sems.at[len(outgoing)]))
        outgoing[-1].start()

    z, y, x, c = place()
    far = [lax.rem(z + k, 4) for k in range(4)]
    back = [lax.rem(z + 4 - k, 4) for k in range(4)]
    x_other, y_other, c_other = (
        device(z, y, 1 - x, c),
        device(z, 1 - y, x, c),
        device(z, y, x, 1 - c),
    )
    greet()
    wires = Wires(send_sems, recv_sems)
    own = [
        pltpu.make_async_copy(share, whole.at[z, y], own_sems.at[i])
        for i, (share, whole) in enumerate(zip(shares, full))
    ]
    own_gains = pltpu.make_async_copy(gains, full_gains.at[z, y], own_sems.at[7])
    keep = [
        pltpu.make_async_copy(full[w], kept[n], keep_sems.at[n]) for n, w in enumerate(KEPT)
    ]
    gains[...] = jnp.where(
        lax.broadcasted_iota(jnp.int32, (16, 128), 0) < 8,
        jnp.broadcast_to(gain_attn[...].astype(jnp.float32), (16, 128)),
        jnp.broadcast_to(gain_ffn[...].astype(jnp.float32), (16, 128)),
    ).astype(jnp.bfloat16)
    own_gains.start()
    gain_slot = GATHER_SLOTS * len(items)
    for k in (1, 2, 3):
        wires.send(gain_slot + k, gains, full_gains.at[z, y], device(far[k], y, x, c))
    for copy in own:
        copy.start()

    def slot(i, k):
        return GATHER_SLOTS * i + k

    def along_z(i):
        item = items[i]
        share, whole = shares[item.weight], full[item.weight]
        for k in (1, 2, 3):
            if item.no_x:
                source, target = item.half(share, (), c), item.half(whole, (z, y), c)
            else:
                source, target = item.quarter(share, (), c, x), item.quarter(whole, (z, y), c, x)
            wires.send(slot(i, k), source, target, device(far[k], y, x, c))

    own_done = set()

    def first_hop(i):
        item = items[i]
        whole = full[item.weight]
        if item.weight not in own_done:
            own[item.weight].wait()
            own_done.add(item.weight)
        for k in (1, 2, 3):
            if item.no_x:
                block = item.half(whole, (back[k], y), c)
                wires.arrived(slot(i, k), block)
                wires.send(slot(i, 7 + k), block, block, c_other)
            else:
                block = item.quarter(whole, (back[k], y), c, x)
                wires.arrived(slot(i, k), block)
                wires.send(slot(i, 3 + k), block, block, x_other)
        if item.no_x:
            block = item.half(whole, (ALL, y), c)
        else:
            block = item.quarter(whole, (ALL, y), c, x)
        wires.send(slot(i, 7), block, block, y_other)

    def second_hop(i):
        item = items[i]
        whole = full[item.weight]
        if item.no_x:
            block = item.half(whole, (ALL, 1 - y), c)
            wires.arrived(slot(i, 7), block)
            wires.send(slot(i, 11), block, block, c_other)
            return
        block = item.quarter(whole, (ALL, 1 - y), c, x)
        wires.arrived(slot(i, 7), block)
        wires.send(slot(i, 0), block, block, x_other)
        for k in (1, 2, 3):
            wires.arrived(slot(i, 3 + k), item.quarter(whole, (back[k], y), c, 1 - x))
        for k in (1, 2, 3):
            block = item.half(whole, (back[k], y), c)
            wires.send(slot(i, 7 + k), block, block, c_other)

    def last_hop(i):
        item = items[i]
        whole = full[item.weight]
        if not item.no_x:
            block = item.half(whole, (ALL, 1 - y), c)
            wires.arrived(slot(i, 0), item.quarter(whole, (ALL, 1 - y), c, 1 - x))
            wires.send(slot(i, 11), block, block, c_other)

    def complete(i):
        item = items[i]
        whole = full[item.weight]
        for k in (1, 2, 3):
            wires.arrived(slot(i, 7 + k), item.half(whole, (back[k], y), 1 - c))
        wires.arrived(slot(i, 11), item.half(whole, (ALL, 1 - y), 1 - c))

    def retire(i):
        wires.finish(lambda slot: slot // GATHER_SLOTS == i)

    step_of = Forward(
        dict(
            state,
            out=put,
            tokens=tokens,
            cotangent=cotangent,
            length=length,
            gains=full_gains,
            w_out=full[OUT],
            w_gate=full[GATE],
            w_up=full[UP],
            w_down=full[DOWN].reshape(2816, 1024),
        )
    )
    last_of = {item.weight: i for i, item in enumerate(items)}
    tasks = [(-1, 3, step_of.prepare)]
    for n, name in enumerate(("query", "key", "value")):
        tasks.append((last_of[n], 2, partial(step_of.project, full[n], state[name])))
    tasks += [(last_of[VALUE], 3, partial(step_of.attend, p, p + 2)) for p in (0, 2, 4, 6)]
    tasks.append((last_of[OUT], 3, step_of.project_out))
    for tile_of in pieces(2816, TILE):
        tasks.append((last_of[DOWN], 2, partial(step_of.grad_of_middle, *tile_of)))
    for start, size in FF_CHUNKS:
        there = max(
            i for i, item in enumerate(items) if item.weight == UP and item.start == start
        )
        for at, width in pieces(size, TILE):
            tasks.append((there, 6, partial(step_of.feed_forward, start + at, width)))
            tasks.append((there, 6, partial(step_of.feed_forward_back, start + at, width)))
        tasks.append((there, 0, partial(step_of.flush, start, size)))

    ahead = 3
    for i in range(min(ahead, len(items))):
        along_z(i)
    own_gains.wait()
    for k in (1, 2, 3):
        wires.arrived(gain_slot + k, full_gains.at[back[k], y])
    wires.send(gain_slot, full_gains.at[:, y], full_gains.at[:, y], y_other)
    stages = (retire, complete, last_hop, second_hop, first_hop)
    lates = (3 * LAG, 3 * LAG - 1, 2 * LAG, LAG, 0)
    for step in range(len(items) + 3 * LAG):
        for late, stage in zip(lates, stages):
            if 0 <= step - late < len(items):
                stage(step - late)
        if step + ahead < len(items):
            along_z(step + ahead)
        if step == 0:
            wires.arrived(gain_slot, full_gains.at[:, 1 - y])
        there = step - lates[1]
        for n, w in enumerate(KEPT):
            if there == last_of[w]:
                keep[n].start()
        spent = 0
        while tasks and tasks[0][0] <= there and spent < 6:
            _, cost, task = tasks.pop(0)
            task()
            spent += cost
    for _, _, task in tasks:
        task()
    step_of.finish()
    for copy in keep + outgoing:
        copy.wait()
    wires.finish()


def forward(tokens, cotangent, lengths, weights, gains):
    items = gather_items()
    shares = [w.reshape(share_shape(n)) for w, n in zip(weights, COLUMNS)]
    wholes = [(4, 2) + share_shape(n) for n in COLUMNS]
    shapes = [jax.ShapeDtypeStruct(wholes[w], jnp.bfloat16) for w in KEPT]
    shapes += [jax.ShapeDtypeStruct(shape, dtype) for _, shape, dtype in FORWARD_OUTS]
    count = GATHER_SLOTS * len(items) + 4
    anywhere = pl.BlockSpec(memory_space=pl.ANY)
    in_vmem = pl.BlockSpec(memory_space=pltpu.VMEM)
    out = pl.pallas_call(
        partial(forward_kernel, items),
        out_shape=shapes,
        in_specs=[anywhere] * 7
        + [in_vmem] * 4
        + [pl.BlockSpec(memory_space=pltpu.SMEM)],
        out_specs=[anywhere] * len(shapes),
        scratch_shapes=[pltpu.VMEM(shape, jnp.bfloat16) for shape in wholes]
        + [pltpu.VMEM((4, 2, 16, 128), jnp.bfloat16), pltpu.VMEM((16, 128), jnp.bfloat16)]
        + [pltpu.VMEM(shape, dtype) for _, shape, dtype in FORWARD_OUTS + FORWARD_OWN]
        + [
            pltpu.SemaphoreType.DMA((count,)),
            pltpu.SemaphoreType.DMA((count,)),
            pltpu.SemaphoreType.DMA((8,)),
            pltpu.SemaphoreType.DMA((len(KEPT),)),
            pltpu.SemaphoreType.DMA((OUT_COPIES,)),
        ],
        compiler_params=pltpu.CompilerParams(
            collective_id=0, has_side_effects=True, vmem_limit_bytes=63 * MIB
        ),
        name="gather_forward",
    )(*shares, *[g.reshape(1, 128) for g in gains], tokens, cotangent, lengths)
    return out[: len(KEPT)], dict(zip([name for name, _, _ in FORWARD_OUTS], out[len(KEPT) :]))


SUM_SLOTS = 10
RING = 4


class Share:
    def __init__(self, weight, start, size, x_first):
        self.weight, self.start, self.size, self.x_first = weight, start, size, x_first
        self.tall = weight == DOWN
        self.width = 128 if self.tall else size // 2
        self.block = (352 if self.tall else 64, self.width)

    def columns(self, c, x):
        start = c * 512 + x * 256 + self.start if self.tall else self.start + c * self.width
        return pl.ds(pl.multiple_of(start, 128), self.width)

    def quarter(self, sums, c, x):
        if self.tall:
            return sums.at[c, x, self.start // 128]
        return sums.at[x, :, self.columns(c, x)]

    def half(self, sums, c):
        if self.tall:
            return sums.at[c, :, self.start // 128]
        return sums.at[:, :, self.columns(c, 0)]


def share_items():
    order = [(GATE, 2048, 768, True), (DOWN, 0, 128, False), (DOWN, 128, 128, True)]
    order += [(GATE, 0, 1024, False), (GATE, 1024, 1024, True)]
    order += [(UP, 0, 1024, True), (UP, 1024, 1024, False), (UP, 2048, 768, False)]
    order += [(OUT, 0, 1024, True), (QUERY, 0, 1024, False), (KEY, 0, 1024, True)]
    order += [(VALUE, 0, 512, True), (VALUE, 512, 256, False), (VALUE, 768, 256, False)]
    return [Share(*item) for item in order]


def plus(left, right):
    return left + right


def dot_tn(left, right):
    return lax.dot_general(
        left, right, (((0,), (0,)), ((), ())), preferred_element_type=jnp.float32
    )


BACKWARD_IN = (
    "query",
    "key",
    "value",
    "lse",
    "h_t",
    "h2_t",
    "att_t",
    "d_b",
    "d_res",
    "d_proj",
    "g_ffn",
    "gain",
)


class Backward:
    def __init__(self, refs):
        self.__dict__.update(refs)

    def prepare(self):
        length = self.length[0, 0]
        for block in range(4):
            rows = slice(128 * block, 128 * block + 128)
            place_k = lax.broadcasted_iota(jnp.int32, (128, 512), 0) + 128 * block
            place_q = lax.broadcasted_iota(jnp.int32, (128, 512), 1)
            same = (place_q >= length) == (place_k >= length)
            allowed = same & (place_k <= place_q)
            self.bias[rows, :] = jnp.where(allowed, 0.0, NEGATIVE)

    def multiply(self, left_t, right, item, target, core):
        columns = item.columns(core, 0)

        def rows(m, _):
            product = dot(left_t[tile(m, 256), :], right[:, columns]).astype(jnp.bfloat16)
            product = product.reshape(2, 2, 64, item.width)
            for xx in (0, 1):
                target[xx, m] = product[:, xx]
            return 0

        lax.fori_loop(0, 4, rows, 0)

    def multiply_tall(self, left, right, groups):
        def rows(m, _):
            at = tile(m, 256)
            turned = left[:, at].T
            for columns, targets in groups:
                product = dot(turned, right[:, columns]).astype(jnp.bfloat16)
                for n, (target, xx) in enumerate(targets):
                    target.reshape(2, 2816, 128)[xx, at, :] = product[:, 128 * n : 128 * n + 128]
            return 0

        lax.fori_loop(0, 11, rows, 0)

    def attend_back(self, first, last):
        low = jnp.bfloat16

        def pair(p, _):
            at = tile(p, 128)
            wo_rows = self.w_rows[p].reshape(128, 1024)
            grad = dot_nt(self.d_proj[...], wo_rows).astype(low)
            query = (self.query[:, at].astype(jnp.float32) * SCORE_SCALE).astype(low)
            key, value = self.key[:, at], self.value[:, at]
            left = lax.broadcasted_iota(jnp.int32, (512, 128), 1) < HEAD
            none = jnp.zeros((512, 128), low)
            sides = [
                [jnp.where(side, v, none) for v in (query, key, value, grad)]
                for side in (left, ~left)
            ]
            grad_key, grad_value = [None, None], [None, None]
            for block in (0, 1):
                rows, seen = slice(256 * block, 256 * block + 256), slice(0, 256 * block + 256)
                grad_query = None
                parts_key, parts_value = None, None
                for n, (own_query, own_key, own_value, own_grad) in enumerate(sides):
                    self.d_in[seen, 0:256] = dot_nt(own_key[seen], query[rows])
                    self.d_in[seen, 256:512] = dot_nt(own_value[seen], grad[rows])
                    self.back_rows(p, n, rows, 256 * block + 256)
                    grad_scores, probs = self.grad_scores[seen, :], self.probs[seen, :]
                    part_query = dot_tn(grad_scores, own_key[seen])
                    part_key = dot(grad_scores, own_query[rows])
                    part_value = dot(probs, own_grad[rows])
                    if n == 0:
                        grad_query, parts_key, parts_value = part_query, part_key, part_value
                    else:
                        grad_query += part_query
                        parts_key += part_key
                        parts_value += part_value
                self.query[rows, at] = (grad_query * SCORE_SCALE).astype(low)
                if block == 0:
                    grad_key[0], grad_value[0] = parts_key, parts_value
                else:
                    grad_key = [grad_key[0] + parts_key[:256], parts_key[256:]]
                    grad_value = [grad_value[0] + parts_value[:256], parts_value[256:]]
            for block in (0, 1):
                rows = slice(256 * block, 256 * block + 256)
                self.key[rows, at] = grad_key[block].astype(low)
                self.value[rows, at] = grad_value[block].astype(low)
            return 0

        lax.fori_loop(first, last, pair, 0)

    def back_rows(self, p, n, rows, count):
        low = jnp.bfloat16
        held = self.d_in
        lse = self.lse[p, n : n + 1, rows]

        def first_pass(r, centre):
            keys = tile(r, 64)
            probs = jnp.exp(held[keys, 0:256] + self.bias[keys, rows] - lse)
            held[keys, 0:256] = probs
            self.probs[keys, :] = probs.astype(low)
            return centre + jnp.sum((held[keys, 256:512] * probs).reshape(8, 8, 256), axis=0)

        centre = lax.fori_loop(0, count // 64, first_pass, jnp.zeros((8, 256), jnp.float32), unroll=2)
        centre = jnp.sum(centre, axis=0, keepdims=True)

        def second_pass(r, _):
            keys = tile(r, 64)
            grad = held[keys, 0:256] * (held[keys, 256:512] - centre)
            self.grad_scores[keys, :] = grad.astype(low)
            return 0

        lax.fori_loop(0, count // 64, second_pass, 0, unroll=2)

    def grad_hidden(self, t):
        at = pl.ds(256 * t, 256)
        total = None
        for n, grad in enumerate((self.query, self.key, self.value)):
            part = dot_nt(grad[...], self.w_rows[2 * n : 2 * n + 2].reshape(256, 1024))
            total = part if total is None else total + part
        self.d_in[:, at] = total

    def add_mixed(self, mid, start, size):
        rows = self.w_rows[0 : size // 128].reshape(size, 1024)
        for j in range(1024 // TILE):
            part = slice(TILE * j, TILE * j + TILE)
            self.d_in[:, part] += dot(mid[:, start : start + size], rows[:, part])

    def mix(self, mixed):
        length = self.length[0, 0]

        def rows_of(block, _):
            rows = tile(block, 64)
            place = lax.broadcasted_iota(jnp.int32, (64, 1024), 0) + 64 * block
            mixed[rows, :] = jnp.where(place < length, self.d_in[rows, :], 0.0).astype(jnp.bfloat16)
            return 0

        lax.fori_loop(0, 8, rows_of, 0)

    def finish(self):
        self.gain_total[...] = jnp.zeros_like(self.gain_total)

        def rows_of(block, _):
            rows = tile(block, 64)
            values = self.tokens[rows, :].astype(jnp.float32)
            factor = lax.rsqrt(jnp.mean(values * values, axis=-1, keepdims=True) + NORM_EPS)
            normed = values * factor
            grad = self.d_in[rows, :]
            self.gain_total[...] += jnp.sum((grad * normed).reshape(8, 8, 1024), axis=0)
            grad_normed = grad * self.gain[0:1, :].astype(jnp.float32)
            mean = jnp.mean(grad_normed * normed, axis=-1, keepdims=True)
            self.d_in[rows, :] = self.d_res[rows, :] + factor * (
                grad_normed - normed * mean
            )
            return 0

        lax.fori_loop(0, 8, rows_of, 0)
        self.gain_lines[...] = jnp.zeros_like(self.gain_lines)
        lines = [jnp.sum(v[...], axis=0, keepdims=True) for v in (self.gain_total, self.g_ffn)]
        for s in range(8):
            for n, line in enumerate(lines):
                self.gain_lines[s // 2, s % 2, n : n + 1] = line[:, 128 * s : 128 * s + 128]


def backward_kernel(items, *refs):
    refs = list(refs)

    def take(n):
        taken = refs[:n]
        del refs[:n]
        return taken

    kept = take(len(KEPT))
    middle_in, grad_gate_in, grad_up_in, residual_in = take(4)
    saved_in = dict(zip(BACKWARD_IN, take(len(BACKWARD_IN))))
    tokens_in, length = take(2)
    sums = take(7)
    gain_sums, input_grad_out, mixed_out = take(3)
    saved = dict(zip(BACKWARD_IN, take(len(BACKWARD_IN))))
    d_in, wide, w_rows, bias, probs, grad_scores, gain_total, gain_lines = take(8)
    mine, from_first, from_second, from_z = (take(len(items)) for _ in range(4))
    ring, tall_ring = take(RING), take(2)
    outbox, tall_outbox = take(2), take(2)
    gain_core, gain_x, gain_y, gain_z = take(4)
    send_sems, recv_sems, load_sems, credit = refs
    z, y, x, c = place()
    far = [lax.rem(z + k, 4) for k in range(4)]
    back = [lax.rem(z + 4 - k, 4) for k in range(4)]
    x_other, y_other, c_other = (
        device(z, y, 1 - x, c),
        device(z, 1 - y, x, c),
        device(z, y, x, 1 - c),
    )
    loads = {}

    def load(name, source, target):
        loads[name] = pltpu.make_async_copy(source, target, load_sems.at[len(loads)])
        loads[name].start()

    waited = set()

    def loaded(*names):
        for name in names:
            if name not in waited:
                loads[name].wait()
                waited.add(name)

    load("d_gate", grad_gate_in, wide.at[1])
    load("h2_t", saved_in["h2_t"], saved["h2_t"])
    load("mid", middle_in, wide.at[0])
    load("d_b", saved_in["d_b"], saved["d_b"])
    load("wo_rows", kept[OUT].reshape(8, 2, 64, 1024), w_rows)
    for name in BACKWARD_IN:
        if name not in loads:
            load(name, saved_in[name], saved[name])
    greet()
    wires = Wires(send_sems, recv_sems)
    work = Backward(
        dict(
            saved,
            tokens=saved["d_b"],
            length=length,
            w_rows=w_rows,
            probs=probs,
            grad_scores=grad_scores,
            bias=bias,
            d_in=d_in,
            gain_total=gain_total,
            gain_lines=gain_lines,
        )
    )
    tall_items = [i for i, item in enumerate(items) if item.tall]
    wide_items = [i for i, item in enumerate(items) if not item.tall]

    def slot(i, k):
        return SUM_SLOTS * i + k

    def core_slots(i):
        return (slot(i, 0), slot(i, 8))

    def from_core(i):
        if items[i].tall:
            return tall_ring[tall_items.index(i)]
        return ring[wide_items.index(i) % RING].at[..., : items[i].width]

    def produce(i):
        item = items[i]
        if item.tall:
            number = tall_items.index(i)
            if number == 0:
                loaded("mid", "d_b")
                groups = []
                for core, boxes in ((1 - c, tall_outbox), (c, [mine[j] for j in tall_items])):
                    columns = pl.ds(pl.multiple_of(512 * core, 512), 512)
                    groups.append((columns, [(boxes[j], xx) for xx in (0, 1) for j in (0, 1)]))
                work.multiply_tall(wide.at[0], saved["d_b"], groups)
                load("d_up", grad_up_in, wide.at[0])
                load("tokens", tokens_in, saved["d_b"])
            box = tall_outbox[number]
        else:
            number = wide_items.index(i)
            if number >= 2:
                wires.finish(lambda s: s in core_slots(wide_items[number - 2]))
            box = outbox[number % 2].at[..., : item.width]
            left, right, names = {
                GATE: (saved["h2_t"], wide.at[1], ("h2_t", "d_gate")),
                UP: (saved["h2_t"], wide.at[0], ("d_up",)),
                OUT: (saved["att_t"], saved["d_proj"], ("att_t", "d_proj")),
                QUERY: (saved["h_t"], saved["query"], ("h_t",)),
                KEY: (saved["h_t"], saved["key"], ()),
                VALUE: (saved["h_t"], saved["value"], ()),
            }[item.weight]
            loaded(*names)
            multiply = partial(work.multiply, left, right, item)
            if number >= RING:
                pl.semaphore_wait(credit, 1)
            multiply(box, 1 - c)
        for xx in (0, 1):
            wires.send(core_slots(i)[xx], box.at[xx], from_core(i).at[xx], c_other)
        if not item.tall:
            multiply(mine[i], c)

    def first_hop(i):
        item, own, other = items[i], mine[i], from_core(i)
        for xx in (0, 1):
            wires.arrived(core_slots(i)[xx], other.at[xx])

        def add(at, _):
            for xx in (0, 1):
                for yy in (0, 1):
                    own[xx, at, yy] = plus(own[xx, at, yy], other[xx, at, yy])
            return 0

        lax.fori_loop(0, 4, add, 0)
        if not item.tall and wide_items.index(i) + RING < len(wide_items):
            pl.semaphore_signal(credit, inc=1, device_id=c_other, device_id_type=MESH)
        if item.x_first:
            wires.send(slot(i, 1), own.at[1 - x], from_first[i], x_other)
        else:
            wires.send(slot(i, 1), own.at[:, :, 1 - y], from_first[i], y_other)

    def second_hop(i):
        item, own, other = items[i], mine[i], from_first[i]
        wires.arrived(slot(i, 1), other)

        def add(at, _):
            for side in (0, 1):
                if item.x_first:
                    own[x, at, side] = plus(own[x, at, side], other[at, side])
                else:
                    own[side, at, y] = plus(own[side, at, y], other[side, at])
            return 0

        lax.fori_loop(0, 4, add, 0)
        if item.x_first:
            wires.send(slot(i, 2), own.at[x, :, 1 - y], from_second[i], y_other)
        else:
            to_z(i, lambda k: own.at[:, far[k], y])

    def to_z(i, block):
        for k in (1, 2, 3):
            wires.send(slot(i, 2 + k), block(k), from_z[i].at[k - 1], device(far[k], y, x, c))

    def z_total(i, own_part):
        total = own_part.astype(jnp.float32)
        for k in (1, 2, 3):
            wires.arrived(slot(i, 2 + k), from_z[i].at[k - 1])
            total += from_z[i][k - 1].astype(jnp.float32)
        return total.astype(jnp.bfloat16)

    def third_hop(i):
        item, own, other = items[i], mine[i], from_second[i]
        if not item.x_first:
            own[:, z, y] = z_total(i, own[:, z, y])
            wires.send(slot(i, 2), own.at[:, z, y], other, x_other)
            return
        wires.arrived(slot(i, 2), other)

        def add(at, _):
            own[x, at, y] = plus(own[x, at, y], other[at])
            return 0

        lax.fori_loop(0, 4, add, 0)
        to_z(i, lambda k: own.at[x, far[k], y])

    def fourth_hop(i):
        item, own = items[i], mine[i]
        if not item.x_first:
            wires.arrived(slot(i, 2), from_second[i])
            block = item.half(sums[item.weight], c)
            block[...] = plus(own[:, z, y], from_second[i][...])
            wires.send(slot(i, 7), block, block, c_other)
            return
        block = item.quarter(sums[item.weight], c, x)
        block[...] = z_total(i, own[x, z, y])
        wires.send(slot(i, 6), block, block, x_other)

    def to_sibling(i):
        item = items[i]
        if item.x_first:
            wires.arrived(slot(i, 6), item.quarter(sums[item.weight], c, 1 - x))
            block = item.half(sums[item.weight], c)
            wires.send(slot(i, 7), block, block, c_other)

    def complete(i):
        item = items[i]
        wires.arrived(slot(i, 7), item.half(sums[item.weight], 1 - c))
        wires.finish(lambda s: s // SUM_SLOTS == i)

    base = SUM_SLOTS * len(items)

    def gains_one():
        wires.send(base, gain_lines, gain_core, c_other)

    def gains_two():
        wires.arrived(base, gain_core)
        gain_core[...] = gain_lines[...] + gain_core[...]
        wires.send(base + 1, gain_core, gain_x, x_other)

    def gains_three():
        wires.arrived(base + 1, gain_x)
        gain_x[...] = gain_core[...] + gain_x[...]
        wires.send(base + 2, gain_x.at[:, 1 - y], gain_y, y_other)

    def gains_four():
        wires.arrived(base + 2, gain_y)
        gain_y[...] = gain_x[:, y] + gain_y[...]
        for k in (1, 2, 3):
            wires.send(base + 2 + k, gain_y.at[far[k]], gain_z.at[z], device(far[k], y, x, c))
        gain_z[z] = gain_y[z]

    def gains_five():
        for k in (1, 2, 3):
            wires.arrived(base + 2 + k, gain_z.at[back[k]])
        gain_sums[...] = (gain_z[0] + gain_z[1]) + (gain_z[2] + gain_z[3])

    def fetch_rows(t):
        for n in range(3):
            load(("rows", n, t), kept[n].at[t], w_rows.at[2 * n : 2 * n + 2])

    def attend_back(p):
        if p == 0:
            loaded("query", "key", "value", "lse", "d_proj", "wo_rows")
        work.attend_back(p, p + 1)
        if p == 7:
            fetch_rows(0)
            load("mid_again", middle_in, wide.at[1])

    def grad_hidden(t):
        loaded(*[("rows", n, t) for n in range(3)])
        work.grad_hidden(t)
        if t < 3:
            fetch_rows(t + 1)

    def start_mixed():
        loaded("d_in")
        load("residual", residual_in, d_in)
        fetch_down(0)

    def fetch_down(q):
        first, count = 8 * q, min(8, 22 - 8 * q)
        load(("down", q), kept[4].at[first : first + count], w_rows.at[0:count])

    def add_mixed(q):
        loaded("residual", "mid_again", ("down", q))
        work.add_mixed(wide.at[1], 1024 * q, min(1024, 2816 - 1024 * q))
        if q < 2:
            fetch_down(q + 1)
        else:
            work.mix(saved["d_b"])
            load("mixed", saved["d_b"], mixed_out)

    def finish():
        loaded("tokens", "d_res", "g_ffn", "gain")
        work.finish()
        load("d_in", d_in, input_grad_out)
        gains_one()

    beside = {1: [work.prepare]}
    for p in range(8):
        beside.setdefault(1 + p, []).append(partial(attend_back, p))
    for t in range(4):
        beside.setdefault(9 + t // 2, []).append(partial(grad_hidden, t))
    beside.setdefault(11, []).append(finish)
    for n, task in enumerate((gains_two, gains_three, gains_four, gains_five)):
        beside.setdefault(13 + 2 * n, []).append(task)
    beside.setdefault(13, []).append(start_mixed)
    for q in range(3):
        beside.setdefault(15 + 2 * q, []).append(partial(add_mixed, q))

    stages = (complete, to_sibling, fourth_hop, third_hop, second_hop, first_hop, produce)
    lates = (12, 10, 8, 6, 4, 2, 0)
    for step in range(len(items) + lates[0]):
        for late, stage in zip(lates, stages):
            if 0 <= step - late < len(items):
                stage(step - late)
        for task in beside.get(step, []):
            task()
    loaded("mixed")
    wires.finish()


def backward(tokens, lengths, kept, saved):
    items = share_items()
    low, wide = jnp.bfloat16, jnp.float32
    dtypes = {name: (shape, dtype) for name, shape, dtype in FORWARD_OUTS}
    shapes = [
        jax.ShapeDtypeStruct((2, 2, 2, 352, 128) if n is None else (2, 64, n), low) for n in COLUMNS
    ]
    shapes += [jax.ShapeDtypeStruct((8, 128), wide), jax.ShapeDtypeStruct((512, 1024), wide)]
    shapes += [jax.ShapeDtypeStruct((512, 1024), low)]
    count = SUM_SLOTS * len(items) + 6
    anywhere = pl.BlockSpec(memory_space=pl.ANY)
    in_vmem = pl.BlockSpec(memory_space=pltpu.VMEM)
    n_loads = 6 + len(BACKWARD_IN) + 12 + 6

    def buffers(lead_of):
        return [pltpu.VMEM(lead_of(item) + item.block, low) for item in items]

    out = pl.pallas_call(
        partial(backward_kernel, items),
        out_shape=shapes,
        in_specs=[anywhere] * (len(KEPT) + 4 + len(BACKWARD_IN) + 1)
        + [pl.BlockSpec(memory_space=pltpu.SMEM)],
        out_specs=[in_vmem] * 8 + [anywhere] * 2,
        scratch_shapes=[pltpu.VMEM(*dtypes[name]) for name in BACKWARD_IN]
        + [
            pltpu.VMEM((512, 1024), wide),
            pltpu.VMEM((2, 512, 2816), low),
            pltpu.VMEM((8, 2, 64, 1024), low),
            pltpu.VMEM((512, 512), wide),
            pltpu.VMEM((512, 256), low),
            pltpu.VMEM((512, 256), low),
            pltpu.VMEM((8, 1024), wide),
            pltpu.VMEM((4, 2, 8, 128), wide),
        ]
        + buffers(lambda item: (2, 4, 2))
        + buffers(lambda item: (4, 2) if item.x_first else (2, 4))
        + buffers(lambda item: (4,) if item.x_first else (2,))
        + buffers(lambda item: (3,) if item.x_first else (3, 2))
        + [pltpu.VMEM((2, 4, 2, 64, 512), low)] * RING
        + [pltpu.VMEM((2, 4, 2, 352, 128), low)] * 2
        + [pltpu.VMEM((2, 4, 2, 64, 512), low)] * 2
        + [pltpu.VMEM((2, 4, 2, 352, 128), low)] * 2
        + [
            pltpu.VMEM((4, 2, 8, 128), wide),
            pltpu.VMEM((4, 2, 8, 128), wide),
            pltpu.VMEM((4, 8, 128), wide),
            pltpu.VMEM((4, 8, 128), wide),
            pltpu.SemaphoreType.DMA((count,)),
            pltpu.SemaphoreType.DMA((count,)),
            pltpu.SemaphoreType.DMA((n_loads,)),
            pltpu.SemaphoreType.REGULAR,
        ],
        compiler_params=pltpu.CompilerParams(
            collective_id=1, has_side_effects=True, vmem_limit_bytes=63 * MIB
        ),
        name="backward_sum",
    )(
        *kept[:4],
        kept[4].reshape(22, 2, 64, 1024),
        saved["mid"],
        saved["d_gate"],
        saved["d_up"],
        saved["residual"],
        *[saved[name] for name in BACKWARD_IN],
        tokens,
        lengths,
    )
    return out[:7], *out[7:]


def unpack_kernel(*refs):
    blocks, (gain_sums, mixed, d_in) = refs[:7], refs[7:10]
    sums, (gain_attn, gain_ffn, mixed_out, input_out) = refs[10:17], refs[17:21]
    held, wide = refs[21:28], refs[28:35]
    mixed_held, input_held, in_sems, out_sems = refs[35:]
    sources = (d_in, mixed, *blocks)
    places = (input_held, mixed_held, *held)
    results = (input_held, mixed_held, *wide)
    targets = (input_out, mixed_out, *sums)
    ins = [pltpu.make_async_copy(a, b, in_sems.at[n]) for n, (a, b) in enumerate(zip(sources, places))]
    outs = [pltpu.make_async_copy(a, b, out_sems.at[n]) for n, (a, b) in enumerate(zip(results, targets))]
    order = (6, 7, 8, 2, 3, 4, 5, 0, 1)
    for n in order:
        ins[n].start()
    for n in order:
        ins[n].wait()
        if n == 8:
            for b in range(8):
                wide[6][:, 128 * b : 128 * b + 128] = held[6][b // 4, b // 2 % 2, b % 2].astype(
                    jnp.float32
                )
        elif n >= 2:
            wide[n - 2][...] = held[n - 2][...].astype(jnp.float32)
        outs[n].start()
    gain_attn[...] = gain_sums[0:1]
    gain_ffn[...] = gain_sums[1:2]
    for n in order:
        outs[n].wait()


def unpack(blocks, gain_sums, mixed, d_in):
    wide = jnp.float32
    anywhere = pl.BlockSpec(memory_space=pl.ANY)
    in_vmem = pl.BlockSpec(memory_space=pltpu.VMEM)
    shapes = [
        jax.ShapeDtypeStruct((352, 1024) if n is None else (2, 64, n), wide) for n in COLUMNS
    ]
    held = [pltpu.VMEM(b.shape, b.dtype) for b in blocks]
    held += [pltpu.VMEM(v.shape, wide) for v in shapes]
    held += [pltpu.VMEM(v.shape, v.dtype) for v in (mixed, d_in)]
    shapes += [jax.ShapeDtypeStruct((1, 128), wide)] * 2
    shapes += [jax.ShapeDtypeStruct(v.shape, v.dtype) for v in (mixed, d_in)]
    out = pl.pallas_call(
        unpack_kernel,
        out_shape=shapes,
        in_specs=[anywhere] * 7 + [in_vmem] + [anywhere] * 2,
        out_specs=[anywhere] * 7 + [in_vmem] * 2 + [anywhere] * 2,
        scratch_shapes=held + [pltpu.SemaphoreType.DMA((9,)), pltpu.SemaphoreType.DMA((9,))],
        compiler_params=pltpu.CompilerParams(vmem_limit_bytes=62 * MIB),
        name="unpack",
    )(*blocks, gain_sums, mixed, d_in)
    sums = [s.reshape(-1, s.shape[-1]) for s in out[:7]]
    return sums, [g.reshape(128) for g in out[7:9]], out[9], out[10]


def gather_plain(weights, gains):
    everything = (*weights, *gains)
    whole = [lax.all_gather(v, "dp", axis=0, tiled=True) for v in everything]
    return whole[: len(weights)], whole[len(weights) :]


def sum_plain(grads, gain_grads):
    shares = [
        lax.psum_scatter(g.astype(jnp.float32), "dp", scatter_dimension=0, tiled=True)
        for g in (*grads, *gain_grads)
    ]
    sums = [lax.psum(s, ("rep", "cores")) for s in shares]
    return sums[: len(grads)], sums[len(grads) :]


def on_any_device(
    tokens,
    norm_attn,
    w_query,
    w_key,
    w_value,
    w_out,
    norm_ffn,
    w_gate,
    w_up,
    w_down,
    lengths,
    cotangent,
):
    rows = tokens.shape[0]
    low = jnp.bfloat16
    allowed, valid = masks(lengths, rows)
    whole, gains = gather_plain(
        (w_query, w_key, w_value, w_out, w_gate, w_up, w_down), (norm_attn, norm_ffn)
    )
    full_query, full_key, full_value, full_out, full_gate, full_up, full_down = whole
    gain_attn, gain_ffn = gains
    inputs = tokens.astype(jnp.float32)
    normed, factor = normalize(inputs)
    hidden = (normed * gain_attn.astype(jnp.float32)).astype(low)
    query = matmul(hidden, full_query).astype(low)
    keyed = matmul(hidden, full_key).astype(low)
    valued = matmul(hidden, full_value).astype(low)
    query_groups, key_groups, value_groups = (to_groups(query), to_groups(keyed), to_groups(valued))
    attended_groups, log_total = lax.map(
        partial(attend, allowed), (query_groups, key_groups, value_groups)
    )
    attended = from_groups(attended_groups)
    residual = inputs + matmul(attended, full_out)
    normed_two, factor_two = normalize(residual)
    hidden_two = (normed_two * gain_ffn.astype(jnp.float32)).astype(low)
    gate = matmul(hidden_two, full_gate)
    upward = matmul(hidden_two, full_up)
    sigma = jax.nn.sigmoid(gate)
    middle = (gate * sigma * upward).astype(low)
    mixed = (valid[:, None] * (residual + matmul(middle, full_down))).astype(low)
    grad_output = cotangent.astype(jnp.float32) * valid[:, None]
    grad_branch = grad_output.astype(low)
    grad_down = matmul_tn(middle, grad_branch)
    grad_middle = matmul_nt(grad_branch, full_down)
    grad_gate_rows = (grad_middle * upward * sigma * (1.0 + gate * (1.0 - sigma))).astype(low)
    grad_up_rows = (grad_middle * gate * sigma).astype(low)
    grad_gate = matmul_tn(hidden_two, grad_gate_rows)
    grad_up = matmul_tn(hidden_two, grad_up_rows)
    grad_hidden_two = matmul_nt(grad_gate_rows, full_gate) + matmul_nt(grad_up_rows, full_up)
    grad_gain_ffn = jnp.sum(grad_hidden_two * normed_two, axis=0)
    grad_residual = grad_output + norm_back(
        grad_hidden_two * gain_ffn.astype(jnp.float32), normed_two, factor_two
    )
    grad_proj = grad_residual.astype(low)
    grad_out = matmul_tn(attended, grad_proj)
    grad_attended = matmul_nt(grad_proj, full_out).astype(low)
    grad_query_g, grad_key_g, grad_value_g = lax.map(
        partial(attend_back, allowed),
        (query_groups, key_groups, value_groups, to_groups(grad_attended), log_total),
    )
    grad_query_rows = from_groups(grad_query_g)
    grad_key_rows = from_groups(grad_key_g)
    grad_value_rows = from_groups(grad_value_g)
    grad_query = matmul_tn(hidden, grad_query_rows)
    grad_key = matmul_tn(hidden, grad_key_rows)
    grad_value = matmul_tn(hidden, grad_value_rows)
    grad_hidden = (
        matmul_nt(grad_query_rows, full_query)
        + matmul_nt(grad_key_rows, full_key)
        + matmul_nt(grad_value_rows, full_value)
    )
    grad_gain_attn = jnp.sum(grad_hidden * normed, axis=0)
    input_grad = grad_residual + norm_back(
        grad_hidden * gain_attn.astype(jnp.float32), normed, factor
    )
    grads = (grad_query, grad_key, grad_value, grad_out, grad_gate, grad_up, grad_down)
    sums, gain_sums = sum_plain([g.astype(low) for g in grads], (grad_gain_attn, grad_gain_ffn))
    return (
        mixed,
        input_grad,
        gain_sums[0],
        sums[0],
        sums[1],
        sums[2],
        sums[3],
        gain_sums[1],
        sums[4],
        sums[5],
        sums[6],
    )


def on_tuned_device(
    tokens,
    norm_attn,
    w_query,
    w_key,
    w_value,
    w_out,
    norm_ffn,
    w_gate,
    w_up,
    w_down,
    lengths,
    cotangent,
):
    weights = (w_query, w_key, w_value, w_out, w_gate, w_up, w_down)
    kept, saved = forward(tokens, cotangent, lengths, weights, (norm_attn, norm_ffn))
    blocks, gain_lines, d_in, mixed = backward(tokens, lengths, kept, saved)
    sums, gain_sums, mixed, d_in = unpack(blocks, gain_lines, mixed, d_in)
    return (
        mixed,
        d_in,
        gain_sums[0],
        *sums[:4],
        gain_sums[1],
        *sums[4:],
    )


def solution(mesh):
    tuned = dict(mesh.shape) == {"dp": 8, "rep": 2, "cores": 2}
    tokens_placed = P(("dp", "rep", "cores"), None)
    share, gain = P("dp", None), P("dp")
    return jax.shard_map(
        on_tuned_device if tuned else on_any_device,
        mesh=mesh,
        in_specs=(
            tokens_placed,
            gain,
            share,
            share,
            share,
            share,
            gain,
            share,
            share,
            share,
            tokens_placed,
            tokens_placed,
        ),
        out_specs=(
            tokens_placed,
            tokens_placed,
            gain,
            share,
            share,
            share,
            share,
            gain,
            share,
            share,
            share,
        ),
        check_vma=False,
    )
```

```python
from functools import partial

import jax
import jax.numpy as jnp
from jax import lax
from jax.experimental import pallas as pl
from jax.experimental.pallas import tpu as pltpu
from jax.sharding import PartitionSpec as P

HEADS = 16
HEAD = 64


NORM_EPS = 1e-05
SCORE_SCALE = 0.125
NEGATIVE = -1e30
head_group = 4
MESH = pl.DeviceIdType.MESH
MIB = 1024 * 1024


def masks(block_len, rows):
    bounds = jnp.cumsum(block_len[0])
    place = jnp.arange(rows, dtype=jnp.int32)
    segment = jnp.sum((place[:, None] >= bounds[None, :]).astype(jnp.int32), axis=1)
    allowed = (segment[:, None] == segment[None, :]) & (place[None, :] <= place[:, None])
    valid = (segment < block_len.shape[1]).astype(jnp.float32)
    return (allowed, valid)


def normalize(values):
    factor = lax.rsqrt(jnp.mean(values * values, axis=-1, keepdims=True) + NORM_EPS)
    return (values * factor, factor)


def norm_back(grad_normed, normed, factor):
    return factor * (grad_normed - normed * jnp.mean(grad_normed * normed, axis=-1, keepdims=True))


def matmul(left, right):
    return jnp.dot(left, right, preferred_element_type=jnp.float32)


def matmul_tn(left, right):
    return lax.dot_general(
        left, right, (((0,), (0,)), ((), ())), preferred_element_type=jnp.float32
    )


def matmul_nt(left, right):
    return lax.dot_general(
        left, right, (((1,), (1,)), ((), ())), preferred_element_type=jnp.float32
    )


def to_groups(matrix):
    rows = matrix.shape[0]
    split = matrix.reshape(rows, HEADS // head_group, head_group, HEAD)
    return split.transpose(1, 2, 0, 3)


def from_groups(grouped):
    rows = grouped.shape[2]
    return grouped.transpose(2, 0, 1, 3).reshape(rows, HEADS * HEAD)


def group_scores(allowed, query_g, key_g):
    raw = (
        jnp.einsum("hqe,hke->hqk", query_g, key_g, preferred_element_type=jnp.float32) * SCORE_SCALE
    )
    return jnp.where(allowed[None], raw, NEGATIVE)


def attend(allowed, operands):
    query_g, key_g, value_g = operands
    scores = group_scores(allowed, query_g, key_g)
    top = jnp.max(scores, axis=-1, keepdims=True)
    expo = jnp.exp(scores - top)
    total = jnp.sum(expo, axis=-1, keepdims=True)
    probs_low = (expo / total).astype(jnp.bfloat16)
    result = jnp.einsum("hqk,hke->hqe", probs_low, value_g, preferred_element_type=jnp.float32)
    return (result.astype(jnp.bfloat16), top[..., 0] + jnp.log(total[..., 0]))


def attend_back(allowed, operands):
    query_g, key_g, value_g, grad_g, lse = operands
    scores = group_scores(allowed, query_g, key_g)
    probs = jnp.exp(scores - lse[..., None])
    grad_probs = jnp.einsum("hqe,hke->hqk", grad_g, value_g, preferred_element_type=jnp.float32)
    centre = jnp.sum(grad_probs * probs, axis=-1, keepdims=True)
    grad_scores = (probs * (grad_probs - centre)).astype(jnp.bfloat16)
    grad_query = (
        jnp.einsum("hqk,hke->hqe", grad_scores, key_g, preferred_element_type=jnp.float32)
        * SCORE_SCALE
    )
    grad_key = (
        jnp.einsum("hqk,hqe->hke", grad_scores, query_g, preferred_element_type=jnp.float32)
        * SCORE_SCALE
    )
    grad_value = jnp.einsum(
        "hqk,hqe->hke", probs.astype(jnp.bfloat16), grad_g, preferred_element_type=jnp.float32
    )
    return (
        grad_query.astype(jnp.bfloat16),
        grad_key.astype(jnp.bfloat16),
        grad_value.astype(jnp.bfloat16),
    )


class Part:
    def __init__(self, weight, tall, start, size, no_x):
        self.weight, self.tall, self.start, self.size = weight, tall, start, size
        self.no_x = no_x

    def quarter(self, ref, lead, c, x):
        if self.tall:
            columns = pl.ds(pl.multiple_of(c * 512 + x * 256, 256), 256)
            return ref.at[(*lead, pl.ds(self.start, self.size), columns)]
        return ref.at[(*lead, x, slice(None), self.columns(c))]

    def half(self, ref, lead, c):
        if self.tall:
            columns = pl.ds(pl.multiple_of(c * 512, 512), 512)
            return ref.at[(*lead, pl.ds(self.start, self.size), columns)]
        return ref.at[(*lead, slice(None), slice(None), self.columns(c))]

    def columns(self, c):
        width = self.size // 2
        return pl.ds(pl.multiple_of(self.start + c * width, 128), width)


def pieces(total, most):
    return [(start, min(most, total - start)) for start in range(0, total, most)]


def place():
    d = lax.axis_index("dp")
    return lax.div(d, 2), lax.rem(d, 2), lax.axis_index("rep"), lax.axis_index("cores")


def device(z, y, x, c):
    return {"dp": 2 * z + y, "rep": x, "cores": c}


def greet():
    z, y, x, c = place()
    barrier = pltpu.get_barrier_semaphore()
    others = [device(lax.rem(z + k, 4), y, x, c) for k in (1, 2, 3)]
    others += [device(z, 1 - y, x, c), device(z, y, 1 - x, c), device(z, y, x, 1 - c)]
    for other in others:
        pl.semaphore_signal(barrier, inc=1, device_id=other, device_id_type=MESH)
    pl.semaphore_wait(barrier, len(others))


class Wires:
    def __init__(self, send_sems, recv_sems):
        self.send_sems, self.recv_sems, self.sent = send_sems, recv_sems, []

    def copy(self, slot, source, target, other):
        return pltpu.make_async_remote_copy(
            src_ref=source,
            dst_ref=target,
            send_sem=self.send_sems.at[slot],
            recv_sem=self.recv_sems.at[slot],
            device_id=other,
            device_id_type=MESH,
        )

    def send(self, slot, source, target, other):
        copy = self.copy(slot, source, target, other)
        copy.start()
        self.sent.append((slot, copy))

    def arrived(self, slot, target):
        z, y, x, c = place()
        self.copy(slot, target, target, device(z, y, x, 1 - c)).wait_recv()

    def finish(self, chosen=lambda slot: True):
        for slot, copy in self.sent:
            if chosen(slot):
                copy.wait_send()
        self.sent = [(slot, copy) for slot, copy in self.sent if not chosen(slot)]


GATHER_SLOTS = 12
LAG = 2
ALL = slice(None)
COLUMNS = (1024, 1024, 1024, 1024, 2816, 2816, None)
QUERY, KEY, VALUE, OUT, GATE, UP, DOWN = range(7)
TILE = 512


FF_CHUNKS = tuple(pieces(2816, 512))


def gather_items():
    order = [(QUERY, 0, 256, True), (QUERY, 256, 256, False), (QUERY, 512, 512, False)]
    order += [(KEY, 0, 512, True), (KEY, 512, 512, False)]
    order += [(VALUE, 0, 512, False), (VALUE, 512, 512, True)]
    order += [(OUT, 0, 512, False), (OUT, 512, 512, False)]
    order += [(DOWN, at, size, n in (2, 3)) for n, (at, size) in enumerate(pieces(352, 64))]
    for n, (start, size) in enumerate(FF_CHUNKS):
        order += [(GATE, start, size, n == 5), (UP, start, size, n in (0, 3, 5))]
    return [Part(w, w == DOWN, start, size, no_x) for w, start, size, no_x in order]


def dot(left, right):
    return lax.dot_general(
        left, right, (((1,), (0,)), ((), ())), preferred_element_type=jnp.float32
    )


def dot_nt(left, right):
    return lax.dot_general(
        left, right, (((1,), (1,)), ((), ())), preferred_element_type=jnp.float32
    )


def tile(index, size):
    return pl.ds(pl.multiple_of(index * size, size), size)


def weight_columns(ref, at):
    return ref[:, :, :, :, at].reshape(1024, -1)


class Forward:
    def __init__(self, refs):
        self.__dict__.update(refs)

    def prepare(self):
        for s in range(8):
            self.gain[:, 128 * s : 128 * s + 128] = self.gains[s // 2, s % 2]
        length = self.length[0, 0]
        for block in range(4):
            rows = slice(128 * block, 128 * block + 128)
            place_q = lax.broadcasted_iota(jnp.int32, (128, 512), 0) + 128 * block
            place_k = lax.broadcasted_iota(jnp.int32, (128, 512), 1)
            same = (place_q >= length) == (place_k >= length)
            allowed = same & (place_k <= place_q)
            self.bias[rows, :] = jnp.where(allowed, 0.0, NEGATIVE)

        def normed(block, _):
            rows = tile(block, 64)
            values = self.tokens[rows, :].astype(jnp.float32)
            factor = lax.rsqrt(jnp.mean(values * values, axis=-1, keepdims=True) + NORM_EPS)
            gain = self.gain[0:1, :].astype(jnp.float32)
            self.hidden[rows, :] = (values * factor * gain).astype(jnp.bfloat16)
            place = lax.broadcasted_iota(jnp.int32, (64, 1024), 0) + 64 * block
            d_b = jnp.where(place < length, self.cotangent[rows, :].astype(jnp.float32), 0.0)
            self.d_b[rows, :] = d_b.astype(jnp.bfloat16)
            return 0

        lax.fori_loop(0, 8, normed, 0)
        self.turn(self.hidden, self.h_t)
        self.out("d_b")

    def turn(self, matrix, turned):
        def columns(n, _):
            at = tile(n, 128)
            turned[at, :] = matrix[:, at].astype(jnp.float32).T.astype(jnp.bfloat16)
            return 0

        lax.fori_loop(0, 8, columns, 0)

    def project(self, weight, result):
        def columns(n, _):
            at = tile(n, TILE)
            result[:, at] = dot(self.hidden[...], weight_columns(weight, at)).astype(jnp.bfloat16)
            return 0

        lax.fori_loop(0, 1024 // TILE, columns, 0)

    def attend(self, first, last):
        def pair(p, _):
            at = tile(p, 128)
            left = lax.broadcasted_iota(jnp.int32, (256, 128), 1) < HEAD
            for block in (0, 1):
                rows, seen = slice(256 * block, 256 * block + 256), slice(0, 256 * block + 256)
                query = self.query[rows, at].astype(jnp.float32) * SCORE_SCALE
                both = jnp.concatenate(
                    [jnp.where(left, query, 0.0), jnp.where(left, 0.0, query)], axis=0
                ).astype(jnp.bfloat16)
                bias = self.bias[rows, seen]
                scores = dot_nt(both, self.key[seen, at]) + jnp.concatenate([bias, bias], axis=0)
                top = jnp.max(scores, axis=-1, keepdims=True)
                expo = jnp.exp(scores - top)
                total = jnp.sum(expo, axis=-1, keepdims=True)
                probs = (expo * (1.0 / total)).astype(jnp.bfloat16)
                result = dot(probs, self.value[seen, at])
                self.attended[rows, at] = jnp.where(left, result[:256], result[256:]).astype(
                    jnp.bfloat16
                )
                lse = top + jnp.log(total)
                turned = jnp.where(left, lse[:256], lse[256:]).T
                self.lse[p, 0:1, rows] = turned[0:1]
                self.lse[p, 1:2, rows] = turned[HEAD : HEAD + 1]
            return 0

        lax.fori_loop(first, last, pair, 0)

    def project_out(self):
        def columns(n, _):
            at = tile(n, TILE)
            self.residual[:, at] = self.tokens[:, at].astype(jnp.float32) + dot(
                self.attended[...], weight_columns(self.w_out, at)
            )
            return 0

        lax.fori_loop(0, 1024 // TILE, columns, 0)

        def normed(block, _):
            rows = tile(block, 64)
            values = self.residual[rows, :]
            factor = lax.rsqrt(jnp.mean(values * values, axis=-1, keepdims=True) + NORM_EPS)
            gain = self.gain[8:9, :].astype(jnp.float32)
            self.h2[rows, :] = (values * factor * gain).astype(jnp.bfloat16)
            return 0

        lax.fori_loop(0, 8, normed, 0)

    def hand_on(self):
        self.turn(self.h2, self.h2_t)
        self.turn(self.attended, self.att_t)
        for name in ("query", "key", "value", "lse", "h_t", "h2_t", "att_t"):
            self.out(name)

    def grad_of_middle(self, start, size):
        at = pl.ds(start, size)
        self.d_up[:, at] = dot_nt(self.d_b[...], self.w_down[at, :]).astype(jnp.bfloat16)

    def feed_forward(self, start, size):
        at = pl.ds(start, size)
        low = jnp.bfloat16
        gate = dot(self.h2[...], weight_columns(self.w_gate, at))
        upward = dot(self.h2[...], weight_columns(self.w_up, at))
        grad_middle = self.d_up[:, at].astype(jnp.float32)
        sigma = 0.5 * jnp.tanh(0.5 * gate) + 0.5
        silu = gate * sigma
        self.mid[:, at] = (silu * upward).astype(low)
        self.d_up[:, at] = (grad_middle * silu).astype(low)
        self.d_gate[:, at] = (grad_middle * upward * (sigma + silu - silu * sigma)).astype(low)

    def feed_forward_on(self, start, size):
        at = pl.ds(start, size)
        gate_w, up_w = weight_columns(self.w_gate, at), weight_columns(self.w_up, at)
        mid, d_gate, d_up = self.mid[:, at], self.d_gate[:, at], self.d_up[:, at]
        for j in range(1024 // TILE):
            part = slice(TILE * j, TILE * j + TILE)
            mixed = dot(mid, self.w_down[at, part])
            grad = dot_nt(d_gate, gate_w[part, :]) + dot_nt(d_up, up_w[part, :])
            if start == 0:
                self.total[:, part] = mixed
                self.d_h2[:, part] = grad
            else:
                self.total[:, part] += mixed
                self.d_h2[:, part] += grad

    def flush(self, start, size):
        for name in ("mid", "d_gate", "d_up"):
            self.out(name, pl.ds(start, size))

    def finish(self):
        length = self.length[0, 0]
        self.g_ffn[...] = jnp.zeros_like(self.g_ffn)

        def rows_of(block, _):
            rows = tile(block, 64)
            place = lax.broadcasted_iota(jnp.int32, (64, 1024), 0) + 64 * block
            residual = self.residual[rows, :]
            mixed = jnp.where(place < length, residual + self.total[rows, :], 0.0)
            self.mixed[rows, :] = mixed.astype(jnp.bfloat16)
            factor = lax.rsqrt(jnp.mean(residual * residual, axis=-1, keepdims=True) + NORM_EPS)
            normed = residual * factor
            grad = self.d_h2[rows, :]
            self.g_ffn[...] += jnp.sum((grad * normed).reshape(8, 8, 1024), axis=0)
            grad_normed = grad * self.gain[8:9, :].astype(jnp.float32)
            grad_out = jnp.where(place < length, self.cotangent[rows, :].astype(jnp.float32), 0.0)
            mean = jnp.mean(grad_normed * normed, axis=-1, keepdims=True)
            d_res = grad_out + factor * (grad_normed - normed * mean)
            self.d_res[rows, :] = d_res
            self.d_proj[rows, :] = d_res.astype(jnp.bfloat16)
            return 0

        lax.fori_loop(0, 8, rows_of, 0)
        for name in ("mixed", "d_res", "d_proj", "g_ffn", "gain"):
            self.out(name)


FORWARD_OUTS = (
    ("mixed", (512, 1024), jnp.bfloat16),
    ("query", (512, 1024), jnp.bfloat16),
    ("key", (512, 1024), jnp.bfloat16),
    ("value", (512, 1024), jnp.bfloat16),
    ("lse", (8, 8, 512), jnp.float32),
    ("h_t", (1024, 512), jnp.bfloat16),
    ("h2_t", (1024, 512), jnp.bfloat16),
    ("att_t", (1024, 512), jnp.bfloat16),
    ("d_b", (512, 1024), jnp.bfloat16),
    ("mid", (512, 2816), jnp.bfloat16),
    ("d_gate", (512, 2816), jnp.bfloat16),
    ("d_up", (512, 2816), jnp.bfloat16),
    ("d_res", (512, 1024), jnp.float32),
    ("d_proj", (512, 1024), jnp.bfloat16),
    ("g_ffn", (8, 1024), jnp.float32),
    ("gain", (16, 1024), jnp.bfloat16),
)
FORWARD_OWN = (
    ("hidden", (512, 1024), jnp.bfloat16),
    ("attended", (512, 1024), jnp.bfloat16),
    ("residual", (512, 1024), jnp.float32),
    ("h2", (512, 1024), jnp.bfloat16),
    ("d_h2", (512, 1024), jnp.float32),
    ("bias", (512, 512), jnp.float32),
    ("total", (512, 1024), jnp.float32),
)
OUT_COPIES = len(FORWARD_OUTS) - 3 + 3 * len(FF_CHUNKS)
KEPT = (QUERY, KEY, VALUE, OUT)


def share_shape(columns):
    return (352, 1024) if columns is None else (2, 64, columns)


def forward_kernel(items, *refs):
    refs = list(refs)

    def take(n):
        taken = refs[:n]
        del refs[:n]
        return taken

    shares = take(7)
    gain_attn, gain_ffn, tokens, cotangent, length = take(5)
    kept = take(len(KEPT))
    names = [name for name, _, _ in FORWARD_OUTS]
    outs = dict(zip(names, take(len(names))))
    full = take(7)
    full_gains, gains = take(2)
    own_names = names + [name for name, _, _ in FORWARD_OWN]
    state = dict(zip(own_names, take(len(own_names))))
    send_sems, recv_sems, own_sems, keep_sems, out_sems = refs
    outgoing = []

    def put(name, columns=None):
        source, target = state[name], outs[name]
        if columns is not None:
            source, target = source.at[:, columns], target.at[:, columns]
        outgoing.append(pltpu.make_async_copy(source, target, out_sems.at[len(outgoing)]))
        outgoing[-1].start()

    z, y, x, c = place()
    far = [lax.rem(z + k, 4) for k in range(4)]
    back = [lax.rem(z + 4 - k, 4) for k in range(4)]
    x_other, y_other, c_other = (
        device(z, y, 1 - x, c),
        device(z, 1 - y, x, c),
        device(z, y, x, 1 - c),
    )
    greet()
    wires = Wires(send_sems, recv_sems)
    own = [
        pltpu.make_async_copy(share, whole.at[z, y], own_sems.at[i])
        for i, (share, whole) in enumerate(zip(shares, full))
    ]
    own_gains = pltpu.make_async_copy(gains, full_gains.at[z, y], own_sems.at[7])
    keep = [
        pltpu.make_async_copy(full[w], kept[n], keep_sems.at[n]) for n, w in enumerate(KEPT)
    ]
    gains[...] = jnp.where(
        lax.broadcasted_iota(jnp.int32, (16, 128), 0) < 8,
        jnp.broadcast_to(gain_attn[...].astype(jnp.float32), (16, 128)),
        jnp.broadcast_to(gain_ffn[...].astype(jnp.float32), (16, 128)),
    ).astype(jnp.bfloat16)
    own_gains.start()
    gain_slot = GATHER_SLOTS * len(items)
    for k in (1, 2, 3):
        wires.send(gain_slot + k, gains, full_gains.at[z, y], device(far[k], y, x, c))
    for copy in own:
        copy.start()

    def slot(i, k):
        return GATHER_SLOTS * i + k

    def along_z(i):
        item = items[i]
        share, whole = shares[item.weight], full[item.weight]
        for k in (1, 2, 3):
            if item.no_x:
                source, target = item.half(share, (), c), item.half(whole, (z, y), c)
            else:
                source, target = item.quarter(share, (), c, x), item.quarter(whole, (z, y), c, x)
            wires.send(slot(i, k), source, target, device(far[k], y, x, c))

    own_done = set()

    def first_hop(i):
        item = items[i]
        whole = full[item.weight]
        if item.weight not in own_done:
            own[item.weight].wait()
            own_done.add(item.weight)
        for k in (1, 2, 3):
            if item.no_x:
                block = item.half(whole, (back[k], y), c)
                wires.arrived(slot(i, k), block)
                wires.send(slot(i, 7 + k), block, block, c_other)
            else:
                block = item.quarter(whole, (back[k], y), c, x)
                wires.arrived(slot(i, k), block)
                wires.send(slot(i, 3 + k), block, block, x_other)
        if item.no_x:
            block = item.half(whole, (ALL, y), c)
        else:
            block = item.quarter(whole, (ALL, y), c, x)
        wires.send(slot(i, 7), block, block, y_other)

    def second_hop(i):
        item = items[i]
        whole = full[item.weight]
        if item.no_x:
            block = item.half(whole, (ALL, 1 - y), c)
            wires.arrived(slot(i, 7), block)
            wires.send(slot(i, 11), block, block, c_other)
            return
        block = item.quarter(whole, (ALL, 1 - y), c, x)
        wires.arrived(slot(i, 7), block)
        wires.send(slot(i, 0), block, block, x_other)
        for k in (1, 2, 3):
            wires.arrived(slot(i, 3 + k), item.quarter(whole, (back[k], y), c, 1 - x))
        for k in (1, 2, 3):
            block = item.half(whole, (back[k], y), c)
            wires.send(slot(i, 7 + k), block, block, c_other)

    def last_hop(i):
        item = items[i]
        whole = full[item.weight]
        if not item.no_x:
            block = item.half(whole, (ALL, 1 - y), c)
            wires.arrived(slot(i, 0), item.quarter(whole, (ALL, 1 - y), c, 1 - x))
            wires.send(slot(i, 11), block, block, c_other)

    def complete(i):
        item = items[i]
        whole = full[item.weight]
        for k in (1, 2, 3):
            wires.arrived(slot(i, 7 + k), item.half(whole, (back[k], y), 1 - c))
        wires.arrived(slot(i, 11), item.half(whole, (ALL, 1 - y), 1 - c))

    def retire(i):
        wires.finish(lambda slot: slot // GATHER_SLOTS == i)

    step_of = Forward(
        dict(
            state,
            out=put,
            tokens=tokens,
            cotangent=cotangent,
            length=length,
            gains=full_gains,
            w_out=full[OUT],
            w_gate=full[GATE],
            w_up=full[UP],
            w_down=full[DOWN].reshape(2816, 1024),
        )
    )
    last_of = {item.weight: i for i, item in enumerate(items)}
    tasks = [(-1, 3, step_of.prepare)]
    for n, name in enumerate(("query", "key", "value")):
        tasks.append((last_of[n], 2, partial(step_of.project, full[n], state[name])))
    tasks += [(last_of[VALUE], 3, partial(step_of.attend, p, p + 1)) for p in range(8)]
    tasks.append((last_of[OUT], 3, step_of.project_out))
    tasks.append((last_of[OUT], 3, step_of.hand_on))
    for tile_of in pieces(2816, TILE):
        tasks.append((last_of[DOWN], 1, partial(step_of.grad_of_middle, *tile_of)))
    for start, size in FF_CHUNKS:
        there = max(
            i for i, item in enumerate(items) if item.weight == UP and item.start == start
        )
        for at, width in pieces(size, TILE):
            tasks.append((there, 6, partial(step_of.feed_forward, start + at, width)))
            tasks.append((there, 6, partial(step_of.feed_forward_on, start + at, width)))
        tasks.append((there, 0, partial(step_of.flush, start, size)))

    ahead = 5
    for i in range(min(ahead, len(items))):
        along_z(i)
    own_gains.wait()
    for k in (1, 2, 3):
        wires.arrived(gain_slot + k, full_gains.at[back[k], y])
    wires.send(gain_slot, full_gains.at[:, y], full_gains.at[:, y], y_other)
    stages = (retire, complete, last_hop, second_hop, first_hop)
    steps = {}
    for i, item in enumerate(items):
        lag = LAG if item.weight in (QUERY, KEY, VALUE, OUT) else 1
        for stage, late in zip(stages, (2 * lag + 2, 2 * lag + 1, 2 * lag, lag, 0)):
            steps.setdefault(i + late, []).append((stage, i))
    done, arrived = set(), 0
    for step in range(max(steps) + 1):
        for stage in stages:
            for named, i in steps.get(step, ()):
                if named is stage:
                    stage(i)
                    if stage is complete:
                        done.add(i)
        if step + ahead < len(items):
            along_z(step + ahead)
        if step == 0:
            wires.arrived(gain_slot, full_gains.at[:, 1 - y])
        before = arrived
        while arrived in done:
            arrived += 1
        there = arrived - 1
        for n, w in enumerate(KEPT):
            if before <= last_of[w] <= there:
                keep[n].start()
        spent = 0
        while tasks and tasks[0][0] <= there and spent < 6:
            _, cost, task = tasks.pop(0)
            task()
            spent += cost
    for _, _, task in tasks:
        task()
    step_of.finish()
    for copy in keep + outgoing:
        copy.wait()
    wires.finish()


def forward(tokens, cotangent, lengths, weights, gains):
    items = gather_items()
    shares = [w.reshape(share_shape(n)) for w, n in zip(weights, COLUMNS)]
    wholes = [(4, 2) + share_shape(n) for n in COLUMNS]
    shapes = [jax.ShapeDtypeStruct(wholes[w], jnp.bfloat16) for w in KEPT]
    shapes += [jax.ShapeDtypeStruct(shape, dtype) for _, shape, dtype in FORWARD_OUTS]
    count = GATHER_SLOTS * len(items) + 4
    anywhere = pl.BlockSpec(memory_space=pl.ANY)
    in_vmem = pl.BlockSpec(memory_space=pltpu.VMEM)
    out = pl.pallas_call(
        partial(forward_kernel, items),
        out_shape=shapes,
        in_specs=[anywhere] * 7
        + [in_vmem] * 4
        + [pl.BlockSpec(memory_space=pltpu.SMEM)],
        out_specs=[anywhere] * len(shapes),
        scratch_shapes=[pltpu.VMEM(shape, jnp.bfloat16) for shape in wholes]
        + [pltpu.VMEM((4, 2, 16, 128), jnp.bfloat16), pltpu.VMEM((16, 128), jnp.bfloat16)]
        + [pltpu.VMEM(shape, dtype) for _, shape, dtype in FORWARD_OUTS + FORWARD_OWN]
        + [
            pltpu.SemaphoreType.DMA((count,)),
            pltpu.SemaphoreType.DMA((count,)),
            pltpu.SemaphoreType.DMA((8,)),
            pltpu.SemaphoreType.DMA((len(KEPT),)),
            pltpu.SemaphoreType.DMA((OUT_COPIES,)),
        ],
        compiler_params=pltpu.CompilerParams(
            collective_id=0, has_side_effects=True, vmem_limit_bytes=63 * MIB
        ),
        name="gather_forward",
    )(*shares, *[g.reshape(1, 128) for g in gains], tokens, cotangent, lengths)
    return out[: len(KEPT)], dict(zip([name for name, _, _ in FORWARD_OUTS], out[len(KEPT) :]))


SUM_SLOTS = 10
RING = 4


class Share:
    def __init__(self, weight, start, size, x_first):
        self.weight, self.start, self.size, self.x_first = weight, start, size, x_first
        self.tall = weight == DOWN
        self.width = 128 if self.tall else size // 2
        self.block = (352 if self.tall else 64, self.width)

    def columns(self, c, x):
        start = c * 512 + x * 256 + self.start if self.tall else self.start + c * self.width
        return pl.ds(pl.multiple_of(start, 128), self.width)

    def quarter(self, sums, c, x):
        if self.tall:
            return sums.at[c, x, self.start // 128]
        return sums.at[x, :, self.columns(c, x)]

    def half(self, sums, c):
        if self.tall:
            return sums.at[c, :, self.start // 128]
        return sums.at[:, :, self.columns(c, 0)]


def share_items():
    order = [(GATE, 2048, 768, True), (DOWN, 0, 128, False), (DOWN, 128, 128, True)]
    order += [(GATE, 0, 1024, False), (GATE, 1024, 1024, True)]
    order += [(UP, 0, 1024, True), (UP, 1024, 1024, False), (UP, 2048, 768, False)]
    order += [(OUT, 0, 1024, True), (QUERY, 0, 1024, False), (KEY, 0, 1024, True)]
    order += [(VALUE, 0, 768, True), (VALUE, 768, 256, False)]
    return [Share(*item) for item in order]


def plus(left, right):
    return left + right


def dot_tn(left, right):
    return lax.dot_general(
        left, right, (((0,), (0,)), ((), ())), preferred_element_type=jnp.float32
    )


BACKWARD_IN = (
    "query",
    "key",
    "value",
    "lse",
    "h_t",
    "h2_t",
    "att_t",
    "d_b",
    "d_res",
    "d_proj",
    "g_ffn",
    "gain",
)


class Backward:
    def __init__(self, refs):
        self.__dict__.update(refs)

    def prepare(self):
        length = self.length[0, 0]
        for block in range(4):
            rows = slice(128 * block, 128 * block + 128)
            place_k = lax.broadcasted_iota(jnp.int32, (128, 512), 0) + 128 * block
            place_q = lax.broadcasted_iota(jnp.int32, (128, 512), 1)
            same = (place_q >= length) == (place_k >= length)
            allowed = same & (place_k <= place_q)
            self.bias[rows, :] = jnp.where(allowed, 0.0, NEGATIVE)

    def multiply(self, left_t, right, item, target, core):
        columns = item.columns(core, 0)

        def rows(m, _):
            product = dot(left_t[tile(m, 256), :], right[:, columns]).astype(jnp.bfloat16)
            product = product.reshape(2, 2, 64, item.width)
            for xx in (0, 1):
                target[xx, m] = product[:, xx]
            return 0

        lax.fori_loop(0, 4, rows, 0)

    def multiply_tall(self, left, right, groups):
        def rows(m, _):
            at = tile(m, 256)
            turned = left[:, at].T
            for columns, targets in groups:
                product = dot(turned, right[:, columns]).astype(jnp.bfloat16)
                for n, (target, xx) in enumerate(targets):
                    target.reshape(2, 2816, 128)[xx, at, :] = product[:, 128 * n : 128 * n + 128]
            return 0

        lax.fori_loop(0, 11, rows, 0)

    def attend_back(self, first, last):
        low = jnp.bfloat16

        def pair(p, _):
            at = tile(p, 128)
            wo_rows = self.w_rows[p].reshape(128, 1024)
            grad = dot_nt(self.d_proj[...], wo_rows).astype(low)
            query = (self.query[:, at].astype(jnp.float32) * SCORE_SCALE).astype(low)
            key, value = self.key[:, at], self.value[:, at]
            left = lax.broadcasted_iota(jnp.int32, (512, 128), 1) < HEAD
            none = jnp.zeros((512, 128), low)
            sides = [
                [jnp.where(side, v, none) for v in (query, key, value, grad)]
                for side in (left, ~left)
            ]
            grad_key, grad_value = [None, None], [None, None]
            for block in (0, 1):
                rows, seen = slice(256 * block, 256 * block + 256), slice(0, 256 * block + 256)
                grad_query = None
                parts_key, parts_value = None, None
                for n, (own_query, own_key, own_value, own_grad) in enumerate(sides):
                    self.d_in[seen, 0:256] = dot_nt(own_key[seen], query[rows])
                    self.d_in[seen, 256:512] = dot_nt(own_value[seen], grad[rows])
                    self.back_rows(p, n, rows, 256 * block + 256)
                    grad_scores, probs = self.grad_scores[seen, :], self.probs[seen, :]
                    part_query = dot_tn(grad_scores, own_key[seen])
                    part_key = dot(grad_scores, own_query[rows])
                    part_value = dot(probs, own_grad[rows])
                    if n == 0:
                        grad_query, parts_key, parts_value = part_query, part_key, part_value
                    else:
                        grad_query += part_query
                        parts_key += part_key
                        parts_value += part_value
                self.query[rows, at] = (grad_query * SCORE_SCALE).astype(low)
                if block == 0:
                    grad_key[0], grad_value[0] = parts_key, parts_value
                else:
                    grad_key = [grad_key[0] + parts_key[:256], parts_key[256:]]
                    grad_value = [grad_value[0] + parts_value[:256], parts_value[256:]]
            for block in (0, 1):
                rows = slice(256 * block, 256 * block + 256)
                self.key[rows, at] = grad_key[block].astype(low)
                self.value[rows, at] = grad_value[block].astype(low)
            return 0

        lax.fori_loop(first, last, pair, 0)

    def back_rows(self, p, n, rows, count):
        low = jnp.bfloat16
        held = self.d_in
        lse = self.lse[p, n : n + 1, rows]

        def first_pass(r, centre):
            keys = tile(r, 64)
            probs = jnp.exp(held[keys, 0:256] + self.bias[keys, rows] - lse)
            held[keys, 0:256] = probs
            self.probs[keys, :] = probs.astype(low)
            return centre + jnp.sum((held[keys, 256:512] * probs).reshape(8, 8, 256), axis=0)

        centre = lax.fori_loop(0, count // 64, first_pass, jnp.zeros((8, 256), jnp.float32), unroll=2)
        centre = jnp.sum(centre, axis=0, keepdims=True)

        def second_pass(r, _):
            keys = tile(r, 64)
            grad = held[keys, 0:256] * (held[keys, 256:512] - centre)
            self.grad_scores[keys, :] = grad.astype(low)
            return 0

        lax.fori_loop(0, count // 64, second_pass, 0, unroll=2)

    def grad_hidden(self, t):
        at = pl.ds(256 * t, 256)
        total = None
        for n, grad in enumerate((self.query, self.key, self.value)):
            part = dot_nt(grad[...], self.w_rows[2 * n : 2 * n + 2].reshape(256, 1024))
            total = part if total is None else total + part
        self.d_in[:, at] = total

    def finish(self):
        self.gain_total[...] = jnp.zeros_like(self.gain_total)

        def rows_of(block, _):
            rows = tile(block, 64)
            values = self.tokens[rows, :].astype(jnp.float32)
            factor = lax.rsqrt(jnp.mean(values * values, axis=-1, keepdims=True) + NORM_EPS)
            normed = values * factor
            grad = self.d_in[rows, :]
            self.gain_total[...] += jnp.sum((grad * normed).reshape(8, 8, 1024), axis=0)
            grad_normed = grad * self.gain[0:1, :].astype(jnp.float32)
            mean = jnp.mean(grad_normed * normed, axis=-1, keepdims=True)
            self.d_in[rows, :] = self.d_res[rows, :] + factor * (
                grad_normed - normed * mean
            )
            return 0

        lax.fori_loop(0, 8, rows_of, 0)
        self.gain_lines[...] = jnp.zeros_like(self.gain_lines)
        lines = [jnp.sum(v[...], axis=0, keepdims=True) for v in (self.gain_total, self.g_ffn)]
        for s in range(8):
            for n, line in enumerate(lines):
                self.gain_lines[s // 2, s % 2, n : n + 1] = line[:, 128 * s : 128 * s + 128]


def backward_kernel(items, *refs):
    refs = list(refs)

    def take(n):
        taken = refs[:n]
        del refs[:n]
        return taken

    kept = take(len(KEPT))
    middle_in, grad_gate_in, grad_up_in = take(3)
    saved_in = dict(zip(BACKWARD_IN, take(len(BACKWARD_IN))))
    tokens_in, length = take(2)
    sums = take(7)
    gain_sums, input_grad_out = take(2)
    saved = dict(zip(BACKWARD_IN, take(len(BACKWARD_IN))))
    d_in, wide, w_rows, bias, probs, grad_scores, gain_total, gain_lines = take(8)
    mine, from_first, from_second, from_z = (take(len(items)) for _ in range(4))
    ring, tall_ring = take(RING), take(2)
    outbox, tall_outbox = take(2), take(2)
    gain_core, gain_x, gain_y, gain_z = take(4)
    send_sems, recv_sems, load_sems, credit = refs
    z, y, x, c = place()
    far = [lax.rem(z + k, 4) for k in range(4)]
    back = [lax.rem(z + 4 - k, 4) for k in range(4)]
    x_other, y_other, c_other = (
        device(z, y, 1 - x, c),
        device(z, 1 - y, x, c),
        device(z, y, x, 1 - c),
    )
    loads = {}

    def load(name, source, target):
        loads[name] = pltpu.make_async_copy(source, target, load_sems.at[len(loads)])
        loads[name].start()

    waited = set()

    def loaded(*names):
        for name in names:
            if name not in waited:
                loads[name].wait()
                waited.add(name)

    load("d_gate", grad_gate_in, wide.at[1])
    load("h2_t", saved_in["h2_t"], saved["h2_t"])
    load("mid", middle_in, wide.at[0])
    load("d_b", saved_in["d_b"], saved["d_b"])
    load("wo_rows", kept[OUT].reshape(8, 2, 64, 1024), w_rows)
    for name in BACKWARD_IN:
        if name not in loads:
            load(name, saved_in[name], saved[name])
    greet()
    wires = Wires(send_sems, recv_sems)
    work = Backward(
        dict(
            saved,
            tokens=saved["d_b"],
            length=length,
            w_rows=w_rows,
            probs=probs,
            grad_scores=grad_scores,
            bias=bias,
            d_in=d_in,
            gain_total=gain_total,
            gain_lines=gain_lines,
        )
    )
    tall_items = [i for i, item in enumerate(items) if item.tall]
    wide_items = [i for i, item in enumerate(items) if not item.tall]

    def slot(i, k):
        return SUM_SLOTS * i + k

    def core_slots(i):
        return (slot(i, 0), slot(i, 8))

    def from_core(i):
        if items[i].tall:
            return tall_ring[tall_items.index(i)]
        return ring[wide_items.index(i) % RING].at[..., : items[i].width]

    def produce(i):
        item = items[i]
        if item.tall:
            number = tall_items.index(i)
            if number == 0:
                loaded("mid", "d_b")
                groups = []
                for core, boxes in ((1 - c, tall_outbox), (c, [mine[j] for j in tall_items])):
                    columns = pl.ds(pl.multiple_of(512 * core, 512), 512)
                    groups.append((columns, [(boxes[j], xx) for xx in (0, 1) for j in (0, 1)]))
                work.multiply_tall(wide.at[0], saved["d_b"], groups)
                load("d_up", grad_up_in, wide.at[0])
                load("tokens", tokens_in, saved["d_b"])
            box = tall_outbox[number]
        else:
            number = wide_items.index(i)
            if number >= 2:
                wires.finish(lambda s: s in core_slots(wide_items[number - 2]))
            box = outbox[number % 2].at[..., : item.width]
            left, right, names = {
                GATE: (saved["h2_t"], wide.at[1], ("h2_t", "d_gate")),
                UP: (saved["h2_t"], wide.at[0], ("d_up",)),
                OUT: (saved["att_t"], saved["d_proj"], ("att_t", "d_proj")),
                QUERY: (saved["h_t"], saved["query"], ("h_t",)),
                KEY: (saved["h_t"], saved["key"], ()),
                VALUE: (saved["h_t"], saved["value"], ()),
            }[item.weight]
            loaded(*names)
            multiply = partial(work.multiply, left, right, item)
            if number >= RING:
                pl.semaphore_wait(credit, 1)
            multiply(box, 1 - c)
        for xx in (0, 1):
            wires.send(core_slots(i)[xx], box.at[xx], from_core(i).at[xx], c_other)
        if not item.tall:
            multiply(mine[i], c)

    def first_hop(i):
        item, own, other = items[i], mine[i], from_core(i)
        for xx in (0, 1):
            wires.arrived(core_slots(i)[xx], other.at[xx])

        def add(at, _):
            for xx in (0, 1):
                for yy in (0, 1):
                    own[xx, at, yy] = plus(own[xx, at, yy], other[xx, at, yy])
            return 0

        lax.fori_loop(0, 4, add, 0)
        if not item.tall and wide_items.index(i) + RING < len(wide_items):
            pl.semaphore_signal(credit, inc=1, device_id=c_other, device_id_type=MESH)
        if item.x_first:
            wires.send(slot(i, 1), own.at[1 - x], from_first[i], x_other)
        else:
            wires.send(slot(i, 1), own.at[:, :, 1 - y], from_first[i], y_other)

    def second_hop(i):
        item, own, other = items[i], mine[i], from_first[i]
        wires.arrived(slot(i, 1), other)

        def add(at, _):
            for side in (0, 1):
                if item.x_first:
                    own[x, at, side] = plus(own[x, at, side], other[at, side])
                else:
                    own[side, at, y] = plus(own[side, at, y], other[side, at])
            return 0

        lax.fori_loop(0, 4, add, 0)
        if item.x_first:
            wires.send(slot(i, 2), own.at[x, :, 1 - y], from_second[i], y_other)
        else:
            to_z(i, lambda k: own.at[:, far[k], y])

    def to_z(i, block):
        for k in (1, 2, 3):
            wires.send(slot(i, 2 + k), block(k), from_z[i].at[k - 1], device(far[k], y, x, c))

    def z_total(i, own_part):
        total = own_part.astype(jnp.float32)
        for k in (1, 2, 3):
            wires.arrived(slot(i, 2 + k), from_z[i].at[k - 1])
            total += from_z[i][k - 1].astype(jnp.float32)
        return total.astype(jnp.bfloat16)

    def third_hop(i):
        item, own, other = items[i], mine[i], from_second[i]
        if not item.x_first:
            own[:, z, y] = z_total(i, own[:, z, y])
            wires.send(slot(i, 2), own.at[:, z, y], other, x_other)
            return
        wires.arrived(slot(i, 2), other)

        def add(at, _):
            own[x, at, y] = plus(own[x, at, y], other[at])
            return 0

        lax.fori_loop(0, 4, add, 0)
        to_z(i, lambda k: own.at[x, far[k], y])

    def fourth_hop(i):
        item, own = items[i], mine[i]
        if not item.x_first:
            wires.arrived(slot(i, 2), from_second[i])
            block = item.half(sums[item.weight], c)
            block[...] = plus(own[:, z, y], from_second[i][...])
            wires.send(slot(i, 7), block, block, c_other)
            return
        block = item.quarter(sums[item.weight], c, x)
        block[...] = z_total(i, own[x, z, y])
        wires.send(slot(i, 6), block, block, x_other)

    def to_sibling(i):
        item = items[i]
        if item.x_first:
            wires.arrived(slot(i, 6), item.quarter(sums[item.weight], c, 1 - x))
            block = item.half(sums[item.weight], c)
            wires.send(slot(i, 7), block, block, c_other)

    def complete(i):
        item = items[i]
        wires.arrived(slot(i, 7), item.half(sums[item.weight], 1 - c))
        wires.finish(lambda s: s // SUM_SLOTS == i)

    base = SUM_SLOTS * len(items)

    def gains_one():
        wires.send(base, gain_lines, gain_core, c_other)

    def gains_two():
        wires.arrived(base, gain_core)
        gain_core[...] = gain_lines[...] + gain_core[...]
        wires.send(base + 1, gain_core, gain_x, x_other)

    def gains_three():
        wires.arrived(base + 1, gain_x)
        gain_x[...] = gain_core[...] + gain_x[...]
        wires.send(base + 2, gain_x.at[:, 1 - y], gain_y, y_other)

    def gains_four():
        wires.arrived(base + 2, gain_y)
        gain_y[...] = gain_x[:, y] + gain_y[...]
        for k in (1, 2, 3):
            wires.send(base + 2 + k, gain_y.at[far[k]], gain_z.at[z], device(far[k], y, x, c))
        gain_z[z] = gain_y[z]

    def gains_five():
        for k in (1, 2, 3):
            wires.arrived(base + 2 + k, gain_z.at[back[k]])
        gain_sums[...] = (gain_z[0] + gain_z[1]) + (gain_z[2] + gain_z[3])

    def fetch_rows(t):
        for n in range(3):
            load(("rows", n, t), kept[n].at[t], w_rows.at[2 * n : 2 * n + 2])

    def attend_back(p):
        if p == 0:
            loaded("query", "key", "value", "lse", "d_proj", "wo_rows")
        work.attend_back(p, p + 1)
        if p == 7:
            fetch_rows(0)

    def grad_hidden(t):
        loaded(*[("rows", n, t) for n in range(3)])
        work.grad_hidden(t)
        if t < 3:
            fetch_rows(t + 1)

    def finish():
        loaded("tokens", "d_res", "g_ffn", "gain")
        work.finish()
        load("d_in", d_in, input_grad_out)
        gains_one()

    beside = {1: [work.prepare]}
    for p in range(8):
        beside.setdefault(1 + p, []).append(partial(attend_back, p))
    for t in range(4):
        beside.setdefault(9 + t // 2, []).append(partial(grad_hidden, t))
    beside.setdefault(11, []).append(finish)
    for n, task in enumerate((gains_two, gains_three, gains_four, gains_five)):
        beside.setdefault(13 + 2 * n, []).append(task)

    stages = (complete, to_sibling, fourth_hop, third_hop, second_hop, first_hop, produce)
    lates = (12, 10, 8, 6, 4, 2, 0)
    for step in range(len(items) + lates[0]):
        for late, stage in zip(lates, stages):
            if 0 <= step - late < len(items):
                stage(step - late)
        for task in beside.get(step, []):
            task()
    loaded("d_in")
    wires.finish()


def backward(tokens, lengths, kept, saved):
    items = share_items()
    low, wide = jnp.bfloat16, jnp.float32
    dtypes = {name: (shape, dtype) for name, shape, dtype in FORWARD_OUTS}
    shapes = [
        jax.ShapeDtypeStruct((2, 2, 2, 352, 128) if n is None else (2, 64, n), low) for n in COLUMNS
    ]
    shapes += [jax.ShapeDtypeStruct((8, 128), wide), jax.ShapeDtypeStruct((512, 1024), wide)]
    count = SUM_SLOTS * len(items) + 6
    anywhere = pl.BlockSpec(memory_space=pl.ANY)
    in_vmem = pl.BlockSpec(memory_space=pltpu.VMEM)
    n_loads = 6 + len(BACKWARD_IN) + 12

    def buffers(lead_of):
        return [pltpu.VMEM(lead_of(item) + item.block, low) for item in items]

    out = pl.pallas_call(
        partial(backward_kernel, items),
        out_shape=shapes,
        in_specs=[anywhere] * (len(KEPT) + 3 + len(BACKWARD_IN) + 1)
        + [pl.BlockSpec(memory_space=pltpu.SMEM)],
        out_specs=[in_vmem] * 8 + [anywhere],
        scratch_shapes=[pltpu.VMEM(*dtypes[name]) for name in BACKWARD_IN]
        + [
            pltpu.VMEM((512, 1024), wide),
            pltpu.VMEM((2, 512, 2816), low),
            pltpu.VMEM((8, 2, 64, 1024), low),
            pltpu.VMEM((512, 512), wide),
            pltpu.VMEM((512, 256), low),
            pltpu.VMEM((512, 256), low),
            pltpu.VMEM((8, 1024), wide),
            pltpu.VMEM((4, 2, 8, 128), wide),
        ]
        + buffers(lambda item: (2, 4, 2))
        + buffers(lambda item: (4, 2) if item.x_first else (2, 4))
        + buffers(lambda item: (4,) if item.x_first else (2,))
        + buffers(lambda item: (3,) if item.x_first else (3, 2))
        + [pltpu.VMEM((2, 4, 2, 64, 512), low)] * RING
        + [pltpu.VMEM((2, 4, 2, 352, 128), low)] * 2
        + [pltpu.VMEM((2, 4, 2, 64, 512), low)] * 2
        + [pltpu.VMEM((2, 4, 2, 352, 128), low)] * 2
        + [
            pltpu.VMEM((4, 2, 8, 128), wide),
            pltpu.VMEM((4, 2, 8, 128), wide),
            pltpu.VMEM((4, 8, 128), wide),
            pltpu.VMEM((4, 8, 128), wide),
            pltpu.SemaphoreType.DMA((count,)),
            pltpu.SemaphoreType.DMA((count,)),
            pltpu.SemaphoreType.DMA((n_loads,)),
            pltpu.SemaphoreType.REGULAR,
        ],
        compiler_params=pltpu.CompilerParams(
            collective_id=1, has_side_effects=True, vmem_limit_bytes=63 * MIB
        ),
        name="backward_sum",
    )(
        *kept,
        saved["mid"],
        saved["d_gate"],
        saved["d_up"],
        *[saved[name] for name in BACKWARD_IN],
        tokens,
        lengths,
    )
    return out[:7], out[7], out[8]


def unpack_kernel(*refs):
    blocks, (gain_sums, mixed, d_in) = refs[:7], refs[7:10]
    sums, (gain_attn, gain_ffn, mixed_out, input_out) = refs[10:17], refs[17:21]
    held, wide = refs[21:28], refs[28:35]
    mixed_held, input_held, in_sems, out_sems = refs[35:]
    sources = (d_in, mixed, *blocks)
    places = (input_held, mixed_held, *held)
    results = (input_held, mixed_held, *wide)
    targets = (input_out, mixed_out, *sums)
    ins = [pltpu.make_async_copy(a, b, in_sems.at[n]) for n, (a, b) in enumerate(zip(sources, places))]
    outs = [pltpu.make_async_copy(a, b, out_sems.at[n]) for n, (a, b) in enumerate(zip(results, targets))]
    order = (6, 7, 8, 2, 3, 4, 5, 0, 1)
    for n in order:
        ins[n].start()
    for n in order:
        ins[n].wait()
        if n == 8:
            for b in range(8):
                wide[6][:, 128 * b : 128 * b + 128] = held[6][b // 4, b // 2 % 2, b % 2].astype(
                    jnp.float32
                )
        elif n >= 2:
            wide[n - 2][...] = held[n - 2][...].astype(jnp.float32)
        outs[n].start()
    gain_attn[...] = gain_sums[0:1]
    gain_ffn[...] = gain_sums[1:2]
    for n in order:
        outs[n].wait()


def unpack(blocks, gain_sums, mixed, d_in):
    wide = jnp.float32
    anywhere = pl.BlockSpec(memory_space=pl.ANY)
    in_vmem = pl.BlockSpec(memory_space=pltpu.VMEM)
    shapes = [
        jax.ShapeDtypeStruct((352, 1024) if n is None else (2, 64, n), wide) for n in COLUMNS
    ]
    held = [pltpu.VMEM(b.shape, b.dtype) for b in blocks]
    held += [pltpu.VMEM(v.shape, wide) for v in shapes]
    held += [pltpu.VMEM(v.shape, v.dtype) for v in (mixed, d_in)]
    shapes += [jax.ShapeDtypeStruct((1, 128), wide)] * 2
    shapes += [jax.ShapeDtypeStruct(v.shape, v.dtype) for v in (mixed, d_in)]
    out = pl.pallas_call(
        unpack_kernel,
        out_shape=shapes,
        in_specs=[anywhere] * 7 + [in_vmem] + [anywhere] * 2,
        out_specs=[anywhere] * 7 + [in_vmem] * 2 + [anywhere] * 2,
        scratch_shapes=held + [pltpu.SemaphoreType.DMA((9,)), pltpu.SemaphoreType.DMA((9,))],
        compiler_params=pltpu.CompilerParams(vmem_limit_bytes=62 * MIB),
        name="unpack",
    )(*blocks, gain_sums, mixed, d_in)
    sums = [s.reshape(-1, s.shape[-1]) for s in out[:7]]
    return sums, [g.reshape(128) for g in out[7:9]], out[9], out[10]


def gather_plain(weights, gains):
    everything = (*weights, *gains)
    whole = [lax.all_gather(v, "dp", axis=0, tiled=True) for v in everything]
    return whole[: len(weights)], whole[len(weights) :]


def sum_plain(grads, gain_grads):
    shares = [
        lax.psum_scatter(g.astype(jnp.float32), "dp", scatter_dimension=0, tiled=True)
        for g in (*grads, *gain_grads)
    ]
    sums = [lax.psum(s, ("rep", "cores")) for s in shares]
    return sums[: len(grads)], sums[len(grads) :]


def on_any_device(
    tokens,
    norm_attn,
    w_query,
    w_key,
    w_value,
    w_out,
    norm_ffn,
    w_gate,
    w_up,
    w_down,
    lengths,
    cotangent,
):
    rows = tokens.shape[0]
    low = jnp.bfloat16
    allowed, valid = masks(lengths, rows)
    whole, gains = gather_plain(
        (w_query, w_key, w_value, w_out, w_gate, w_up, w_down), (norm_attn, norm_ffn)
    )
    full_query, full_key, full_value, full_out, full_gate, full_up, full_down = whole
    gain_attn, gain_ffn = gains
    inputs = tokens.astype(jnp.float32)
    normed, factor = normalize(inputs)
    hidden = (normed * gain_attn.astype(jnp.float32)).astype(low)
    query = matmul(hidden, full_query).astype(low)
    keyed = matmul(hidden, full_key).astype(low)
    valued = matmul(hidden, full_value).astype(low)
    query_groups, key_groups, value_groups = (to_groups(query), to_groups(keyed), to_groups(valued))
    attended_groups, log_total = lax.map(
        partial(attend, allowed), (query_groups, key_groups, value_groups)
    )
    attended = from_groups(attended_groups)
    residual = inputs + matmul(attended, full_out)
    normed_two, factor_two = normalize(residual)
    hidden_two = (normed_two * gain_ffn.astype(jnp.float32)).astype(low)
    gate = matmul(hidden_two, full_gate)
    upward = matmul(hidden_two, full_up)
    sigma = jax.nn.sigmoid(gate)
    middle = (gate * sigma * upward).astype(low)
    mixed = (valid[:, None] * (residual + matmul(middle, full_down))).astype(low)
    grad_output = cotangent.astype(jnp.float32) * valid[:, None]
    grad_branch = grad_output.astype(low)
    grad_down = matmul_tn(middle, grad_branch)
    grad_middle = matmul_nt(grad_branch, full_down)
    grad_gate_rows = (grad_middle * upward * sigma * (1.0 + gate * (1.0 - sigma))).astype(low)
    grad_up_rows = (grad_middle * gate * sigma).astype(low)
    grad_gate = matmul_tn(hidden_two, grad_gate_rows)
    grad_up = matmul_tn(hidden_two, grad_up_rows)
    grad_hidden_two = matmul_nt(grad_gate_rows, full_gate) + matmul_nt(grad_up_rows, full_up)
    grad_gain_ffn = jnp.sum(grad_hidden_two * normed_two, axis=0)
    grad_residual = grad_output + norm_back(
        grad_hidden_two * gain_ffn.astype(jnp.float32), normed_two, factor_two
    )
    grad_proj = grad_residual.astype(low)
    grad_out = matmul_tn(attended, grad_proj)
    grad_attended = matmul_nt(grad_proj, full_out).astype(low)
    grad_query_g, grad_key_g, grad_value_g = lax.map(
        partial(attend_back, allowed),
        (query_groups, key_groups, value_groups, to_groups(grad_attended), log_total),
    )
    grad_query_rows = from_groups(grad_query_g)
    grad_key_rows = from_groups(grad_key_g)
    grad_value_rows = from_groups(grad_value_g)
    grad_query = matmul_tn(hidden, grad_query_rows)
    grad_key = matmul_tn(hidden, grad_key_rows)
    grad_value = matmul_tn(hidden, grad_value_rows)
    grad_hidden = (
        matmul_nt(grad_query_rows, full_query)
        + matmul_nt(grad_key_rows, full_key)
        + matmul_nt(grad_value_rows, full_value)
    )
    grad_gain_attn = jnp.sum(grad_hidden * normed, axis=0)
    input_grad = grad_residual + norm_back(
        grad_hidden * gain_attn.astype(jnp.float32), normed, factor
    )
    grads = (grad_query, grad_key, grad_value, grad_out, grad_gate, grad_up, grad_down)
    sums, gain_sums = sum_plain([g.astype(low) for g in grads], (grad_gain_attn, grad_gain_ffn))
    return (
        mixed,
        input_grad,
        gain_sums[0],
        sums[0],
        sums[1],
        sums[2],
        sums[3],
        gain_sums[1],
        sums[4],
        sums[5],
        sums[6],
    )


def on_tuned_device(
    tokens,
    norm_attn,
    w_query,
    w_key,
    w_value,
    w_out,
    norm_ffn,
    w_gate,
    w_up,
    w_down,
    lengths,
    cotangent,
):
    weights = (w_query, w_key, w_value, w_out, w_gate, w_up, w_down)
    kept, saved = forward(tokens, cotangent, lengths, weights, (norm_attn, norm_ffn))
    blocks, gain_lines, d_in = backward(tokens, lengths, kept, saved)
    sums, gain_sums, mixed, d_in = unpack(blocks, gain_lines, saved["mixed"], d_in)
    return (
        mixed,
        d_in,
        gain_sums[0],
        *sums[:4],
        gain_sums[1],
        *sums[4:],
    )


def solution(mesh):
    tuned = dict(mesh.shape) == {"dp": 8, "rep": 2, "cores": 2}
    tokens_placed = P(("dp", "rep", "cores"), None)
    share, gain = P("dp", None), P("dp")
    return jax.shard_map(
        on_tuned_device if tuned else on_any_device,
        mesh=mesh,
        in_specs=(
            tokens_placed,
            gain,
            share,
            share,
            share,
            share,
            gain,
            share,
            share,
            share,
            tokens_placed,
            tokens_placed,
        ),
        out_specs=(
            tokens_placed,
            tokens_placed,
            gain,
            share,
            share,
            share,
            share,
            gain,
            share,
            share,
            share,
        ),
        check_vma=False,
    )
```

```python
from functools import partial

import jax
import jax.numpy as jnp
from jax import lax
from jax.experimental import pallas as pl
from jax.experimental.pallas import tpu as pltpu
from jax.sharding import PartitionSpec as P

HEADS = 16
HEAD = 64


NORM_EPS = 1e-05
SCORE_SCALE = 0.125
NEGATIVE = -1e30
head_group = 4
MESH = pl.DeviceIdType.MESH
MIB = 1024 * 1024


def masks(block_len, rows):
    bounds = jnp.cumsum(block_len[0])
    place = jnp.arange(rows, dtype=jnp.int32)
    segment = jnp.sum((place[:, None] >= bounds[None, :]).astype(jnp.int32), axis=1)
    allowed = (segment[:, None] == segment[None, :]) & (place[None, :] <= place[:, None])
    valid = (segment < block_len.shape[1]).astype(jnp.float32)
    return (allowed, valid)


def normalize(values):
    factor = lax.rsqrt(jnp.mean(values * values, axis=-1, keepdims=True) + NORM_EPS)
    return (values * factor, factor)


def norm_back(grad_normed, normed, factor):
    return factor * (grad_normed - normed * jnp.mean(grad_normed * normed, axis=-1, keepdims=True))


def matmul(left, right):
    return jnp.dot(left, right, preferred_element_type=jnp.float32)


def matmul_tn(left, right):
    return lax.dot_general(
        left, right, (((0,), (0,)), ((), ())), preferred_element_type=jnp.float32
    )


def matmul_nt(left, right):
    return lax.dot_general(
        left, right, (((1,), (1,)), ((), ())), preferred_element_type=jnp.float32
    )


def to_groups(matrix):
    rows = matrix.shape[0]
    split = matrix.reshape(rows, HEADS // head_group, head_group, HEAD)
    return split.transpose(1, 2, 0, 3)


def from_groups(grouped):
    rows = grouped.shape[2]
    return grouped.transpose(2, 0, 1, 3).reshape(rows, HEADS * HEAD)


def group_scores(allowed, query_g, key_g):
    raw = (
        jnp.einsum("hqe,hke->hqk", query_g, key_g, preferred_element_type=jnp.float32) * SCORE_SCALE
    )
    return jnp.where(allowed[None], raw, NEGATIVE)


def attend(allowed, operands):
    query_g, key_g, value_g = operands
    scores = group_scores(allowed, query_g, key_g)
    top = jnp.max(scores, axis=-1, keepdims=True)
    expo = jnp.exp(scores - top)
    total = jnp.sum(expo, axis=-1, keepdims=True)
    probs_low = (expo / total).astype(jnp.bfloat16)
    result = jnp.einsum("hqk,hke->hqe", probs_low, value_g, preferred_element_type=jnp.float32)
    return (result.astype(jnp.bfloat16), top[..., 0] + jnp.log(total[..., 0]))


def attend_back(allowed, operands):
    query_g, key_g, value_g, grad_g, lse = operands
    scores = group_scores(allowed, query_g, key_g)
    probs = jnp.exp(scores - lse[..., None])
    grad_probs = jnp.einsum("hqe,hke->hqk", grad_g, value_g, preferred_element_type=jnp.float32)
    centre = jnp.sum(grad_probs * probs, axis=-1, keepdims=True)
    grad_scores = (probs * (grad_probs - centre)).astype(jnp.bfloat16)
    grad_query = (
        jnp.einsum("hqk,hke->hqe", grad_scores, key_g, preferred_element_type=jnp.float32)
        * SCORE_SCALE
    )
    grad_key = (
        jnp.einsum("hqk,hqe->hke", grad_scores, query_g, preferred_element_type=jnp.float32)
        * SCORE_SCALE
    )
    grad_value = jnp.einsum(
        "hqk,hqe->hke", probs.astype(jnp.bfloat16), grad_g, preferred_element_type=jnp.float32
    )
    return (
        grad_query.astype(jnp.bfloat16),
        grad_key.astype(jnp.bfloat16),
        grad_value.astype(jnp.bfloat16),
    )


class Part:
    def __init__(self, weight, tall, start, size, no_x):
        self.weight, self.tall, self.start, self.size = weight, tall, start, size
        self.no_x = no_x

    def quarter(self, ref, lead, c, x):
        if self.tall:
            columns = pl.ds(pl.multiple_of(c * 512 + x * 256, 256), 256)
            return ref.at[(*lead, pl.ds(self.start, self.size), columns)]
        return ref.at[(*lead, x, slice(None), self.columns(c))]

    def half(self, ref, lead, c):
        if self.tall:
            columns = pl.ds(pl.multiple_of(c * 512, 512), 512)
            return ref.at[(*lead, pl.ds(self.start, self.size), columns)]
        return ref.at[(*lead, slice(None), slice(None), self.columns(c))]

    def columns(self, c):
        width = self.size // 2
        return pl.ds(pl.multiple_of(self.start + c * width, 128), width)


def pieces(total, most):
    return [(start, min(most, total - start)) for start in range(0, total, most)]


def place():
    d = lax.axis_index("dp")
    return lax.div(d, 2), lax.rem(d, 2), lax.axis_index("rep"), lax.axis_index("cores")


def device(z, y, x, c):
    return {"dp": 2 * z + y, "rep": x, "cores": c}


def greet():
    z, y, x, c = place()
    barrier = pltpu.get_barrier_semaphore()
    others = [device(lax.rem(z + k, 4), y, x, c) for k in (1, 2, 3)]
    others += [device(z, 1 - y, x, c), device(z, y, 1 - x, c), device(z, y, x, 1 - c)]
    for other in others:
        pl.semaphore_signal(barrier, inc=1, device_id=other, device_id_type=MESH)
    pl.semaphore_wait(barrier, len(others))


class Wires:
    def __init__(self, send_sems, recv_sems):
        self.send_sems, self.recv_sems, self.sent = send_sems, recv_sems, []

    def copy(self, slot, source, target, other):
        return pltpu.make_async_remote_copy(
            src_ref=source,
            dst_ref=target,
            send_sem=self.send_sems.at[slot],
            recv_sem=self.recv_sems.at[slot],
            device_id=other,
            device_id_type=MESH,
        )

    def send(self, slot, source, target, other):
        copy = self.copy(slot, source, target, other)
        copy.start()
        self.sent.append((slot, copy))

    def arrived(self, slot, target):
        z, y, x, c = place()
        self.copy(slot, target, target, device(z, y, x, 1 - c)).wait_recv()

    def finish(self, chosen=lambda slot: True):
        for slot, copy in self.sent:
            if chosen(slot):
                copy.wait_send()
        self.sent = [(slot, copy) for slot, copy in self.sent if not chosen(slot)]


GATHER_SLOTS = 12
LAG = 3
ALL = slice(None)
COLUMNS = (1024, 1024, 1024, 1024, 2816, 2816, None)
QUERY, KEY, VALUE, OUT, GATE, UP, DOWN = range(7)
TILE = 512


FF_CHUNKS = tuple(pieces(2816, 512))


def gather_items():
    order = [(QUERY, 0, 256, True), (QUERY, 256, 768, False), (KEY, 0, 1024, True)]
    order += [(VALUE, 0, 1024, False), (OUT, 0, 1024, False)]
    order += [(DOWN, 0, 128, False), (DOWN, 128, 128, True), (DOWN, 256, 96, False)]
    for n, (start, size) in enumerate(FF_CHUNKS):
        order += [(GATE, start, size, n == 5), (UP, start, size, n in (0, 3, 5))]
    return [Part(w, w == DOWN, start, size, no_x) for w, start, size, no_x in order]


def dot(left, right):
    return lax.dot_general(
        left, right, (((1,), (0,)), ((), ())), preferred_element_type=jnp.float32
    )


def dot_nt(left, right):
    return lax.dot_general(
        left, right, (((1,), (1,)), ((), ())), preferred_element_type=jnp.float32
    )


def tile(index, size):
    return pl.ds(pl.multiple_of(index * size, size), size)


def weight_columns(ref, at):
    return ref[:, :, :, :, at].reshape(1024, -1)


class Forward:
    def __init__(self, refs):
        self.__dict__.update(refs)

    def prepare(self):
        for s in range(8):
            self.gain[:, 128 * s : 128 * s + 128] = self.gains[s // 2, s % 2]
        length = self.length[0, 0]
        for block in range(4):
            rows = slice(128 * block, 128 * block + 128)
            place_q = lax.broadcasted_iota(jnp.int32, (128, 512), 0) + 128 * block
            place_k = lax.broadcasted_iota(jnp.int32, (128, 512), 1)
            same = (place_q >= length) == (place_k >= length)
            allowed = same & (place_k <= place_q)
            self.bias[rows, :] = jnp.where(allowed, 0.0, NEGATIVE)

        def normed(block, _):
            rows = tile(block, 64)
            values = self.tokens[rows, :].astype(jnp.float32)
            factor = lax.rsqrt(jnp.mean(values * values, axis=-1, keepdims=True) + NORM_EPS)
            gain = self.gain[0:1, :].astype(jnp.float32)
            self.hidden[rows, :] = (values * factor * gain).astype(jnp.bfloat16)
            place = lax.broadcasted_iota(jnp.int32, (64, 1024), 0) + 64 * block
            d_b = jnp.where(place < length, self.cotangent[rows, :].astype(jnp.float32), 0.0)
            self.d_b[rows, :] = d_b.astype(jnp.bfloat16)
            return 0

        lax.fori_loop(0, 8, normed, 0)
        self.turn(self.hidden, self.h_t)
        self.out("d_b")

    def turn(self, matrix, turned):
        def columns(n, _):
            at = tile(n, 128)
            turned[at, :] = matrix[:, at].astype(jnp.float32).T.astype(jnp.bfloat16)
            return 0

        lax.fori_loop(0, 8, columns, 0)

    def project(self, weight, result):
        def columns(n, _):
            at = tile(n, TILE)
            result[:, at] = dot(self.hidden[...], weight_columns(weight, at)).astype(jnp.bfloat16)
            return 0

        lax.fori_loop(0, 1024 // TILE, columns, 0)

    def attend(self, first, last):
        def pair(p, _):
            at = tile(p, 128)
            left = lax.broadcasted_iota(jnp.int32, (256, 128), 1) < HEAD
            for block in (0, 1):
                rows, seen = slice(256 * block, 256 * block + 256), slice(0, 256 * block + 256)
                query = self.query[rows, at].astype(jnp.float32) * SCORE_SCALE
                both = jnp.concatenate(
                    [jnp.where(left, query, 0.0), jnp.where(left, 0.0, query)], axis=0
                ).astype(jnp.bfloat16)
                bias = self.bias[rows, seen]
                scores = dot_nt(both, self.key[seen, at]) + jnp.concatenate([bias, bias], axis=0)
                top = jnp.max(scores, axis=-1, keepdims=True)
                expo = jnp.exp(scores - top)
                total = jnp.sum(expo, axis=-1, keepdims=True)
                probs = (expo * (1.0 / total)).astype(jnp.bfloat16)
                result = dot(probs, self.value[seen, at])
                self.attended[rows, at] = jnp.where(left, result[:256], result[256:]).astype(
                    jnp.bfloat16
                )
                lse = top + jnp.log(total)
                turned = jnp.where(left, lse[:256], lse[256:]).T
                self.lse[p, 0:1, rows] = turned[0:1]
                self.lse[p, 1:2, rows] = turned[HEAD : HEAD + 1]
            return 0

        lax.fori_loop(first, last, pair, 0)

    def project_out(self):
        def columns(n, _):
            at = tile(n, TILE)
            self.residual[:, at] = self.tokens[:, at].astype(jnp.float32) + dot(
                self.attended[...], weight_columns(self.w_out, at)
            )
            return 0

        lax.fori_loop(0, 1024 // TILE, columns, 0)

        def normed(block, _):
            rows = tile(block, 64)
            values = self.residual[rows, :]
            factor = lax.rsqrt(jnp.mean(values * values, axis=-1, keepdims=True) + NORM_EPS)
            gain = self.gain[8:9, :].astype(jnp.float32)
            self.h2[rows, :] = (values * factor * gain).astype(jnp.bfloat16)
            return 0

        lax.fori_loop(0, 8, normed, 0)
        self.turn(self.h2, self.h2_t)
        self.turn(self.attended, self.att_t)
        for name in ("query", "key", "value", "lse", "h_t", "h2_t", "att_t"):
            self.out(name)

    def grad_of_middle(self, start, size):
        at = pl.ds(start, size)
        self.d_up[:, at] = dot_nt(self.d_b[...], self.w_down[at, :]).astype(jnp.bfloat16)

    def feed_forward(self, start, size):
        at = pl.ds(start, size)
        low = jnp.bfloat16
        gate_w = weight_columns(self.w_gate, at)
        up_w = weight_columns(self.w_up, at)
        down_w = self.w_down[at, :]
        gate = dot(self.h2[...], gate_w)
        upward = dot(self.h2[...], up_w)
        grad_middle = self.d_up[:, at].astype(jnp.float32)
        sigma = 0.5 * jnp.tanh(0.5 * gate) + 0.5
        silu = gate * sigma
        mid = (silu * upward).astype(low)
        d_up = (grad_middle * silu).astype(low)
        d_gate = (grad_middle * upward * (sigma + silu - silu * sigma)).astype(low)
        self.mid[:, at] = mid
        self.d_up[:, at] = d_up
        self.d_gate[:, at] = d_gate
        for j in range(1024 // TILE):
            part = slice(TILE * j, TILE * j + TILE)
            mixed = dot(mid, down_w[:, part])
            grad = dot_nt(d_gate, gate_w[part, :]) + dot_nt(d_up, up_w[part, :])
            if start == 0:
                self.total[:, part] = mixed
                self.d_h2[:, part] = grad
            else:
                self.total[:, part] += mixed
                self.d_h2[:, part] += grad

    def flush(self, start, size):
        for name in ("mid", "d_gate", "d_up"):
            self.out(name, pl.ds(start, size))

    def finish(self):
        length = self.length[0, 0]
        self.g_ffn[...] = jnp.zeros_like(self.g_ffn)

        def rows_of(block, _):
            rows = tile(block, 64)
            place = lax.broadcasted_iota(jnp.int32, (64, 1024), 0) + 64 * block
            residual = self.residual[rows, :]
            mixed = jnp.where(place < length, residual + self.total[rows, :], 0.0)
            self.mixed[rows, :] = mixed.astype(jnp.bfloat16)
            factor = lax.rsqrt(jnp.mean(residual * residual, axis=-1, keepdims=True) + NORM_EPS)
            normed = residual * factor
            grad = self.d_h2[rows, :]
            self.g_ffn[...] += jnp.sum((grad * normed).reshape(8, 8, 1024), axis=0)
            grad_normed = grad * self.gain[8:9, :].astype(jnp.float32)
            grad_out = jnp.where(place < length, self.cotangent[rows, :].astype(jnp.float32), 0.0)
            mean = jnp.mean(grad_normed * normed, axis=-1, keepdims=True)
            d_res = grad_out + factor * (grad_normed - normed * mean)
            self.d_res[rows, :] = d_res
            self.d_proj[rows, :] = d_res.astype(jnp.bfloat16)
            return 0

        lax.fori_loop(0, 8, rows_of, 0)
        for name in ("mixed", "d_res", "d_proj", "g_ffn", "gain"):
            self.out(name)


FORWARD_OUTS = (
    ("mixed", (512, 1024), jnp.bfloat16),
    ("query", (512, 1024), jnp.bfloat16),
    ("key", (512, 1024), jnp.bfloat16),
    ("value", (512, 1024), jnp.bfloat16),
    ("lse", (8, 8, 512), jnp.float32),
    ("h_t", (1024, 512), jnp.bfloat16),
    ("h2_t", (1024, 512), jnp.bfloat16),
    ("att_t", (1024, 512), jnp.bfloat16),
    ("d_b", (512, 1024), jnp.bfloat16),
    ("mid", (512, 2816), jnp.bfloat16),
    ("d_gate", (512, 2816), jnp.bfloat16),
    ("d_up", (512, 2816), jnp.bfloat16),
    ("d_res", (512, 1024), jnp.float32),
    ("d_proj", (512, 1024), jnp.bfloat16),
    ("g_ffn", (8, 1024), jnp.float32),
    ("gain", (16, 1024), jnp.bfloat16),
)
FORWARD_OWN = (
    ("hidden", (512, 1024), jnp.bfloat16),
    ("attended", (512, 1024), jnp.bfloat16),
    ("residual", (512, 1024), jnp.float32),
    ("h2", (512, 1024), jnp.bfloat16),
    ("d_h2", (512, 1024), jnp.float32),
    ("bias", (512, 512), jnp.float32),
    ("total", (512, 1024), jnp.float32),
)
OUT_COPIES = len(FORWARD_OUTS) - 3 + 3 * len(FF_CHUNKS)
KEPT = (QUERY, KEY, VALUE, OUT)


def share_shape(columns):
    return (352, 1024) if columns is None else (2, 64, columns)


def forward_kernel(items, *refs):
    refs = list(refs)

    def take(n):
        taken = refs[:n]
        del refs[:n]
        return taken

    shares = take(7)
    gain_attn, gain_ffn, tokens, cotangent, length = take(5)
    kept = take(len(KEPT))
    names = [name for name, _, _ in FORWARD_OUTS]
    outs = dict(zip(names, take(len(names))))
    full = take(7)
    full_gains, gains = take(2)
    own_names = names + [name for name, _, _ in FORWARD_OWN]
    state = dict(zip(own_names, take(len(own_names))))
    send_sems, recv_sems, own_sems, keep_sems, out_sems = refs
    outgoing = []

    def put(name, columns=None):
        source, target = state[name], outs[name]
        if columns is not None:
            source, target = source.at[:, columns], target.at[:, columns]
        outgoing.append(pltpu.make_async_copy(source, target, out_sems.at[len(outgoing)]))
        outgoing[-1].start()

    z, y, x, c = place()
    far = [lax.rem(z + k, 4) for k in range(4)]
    back = [lax.rem(z + 4 - k, 4) for k in range(4)]
    x_other, y_other, c_other = (
        device(z, y, 1 - x, c),
        device(z, 1 - y, x, c),
        device(z, y, x, 1 - c),
    )
    greet()
    wires = Wires(send_sems, recv_sems)
    own = [
        pltpu.make_async_copy(share, whole.at[z, y], own_sems.at[i])
        for i, (share, whole) in enumerate(zip(shares, full))
    ]
    own_gains = pltpu.make_async_copy(gains, full_gains.at[z, y], own_sems.at[7])
    keep = [
        pltpu.make_async_copy(full[w], kept[n], keep_sems.at[n]) for n, w in enumerate(KEPT)
    ]
    gains[...] = jnp.where(
        lax.broadcasted_iota(jnp.int32, (16, 128), 0) < 8,
        jnp.broadcast_to(gain_attn[...].astype(jnp.float32), (16, 128)),
        jnp.broadcast_to(gain_ffn[...].astype(jnp.float32), (16, 128)),
    ).astype(jnp.bfloat16)
    own_gains.start()
    gain_slot = GATHER_SLOTS * len(items)
    for k in (1, 2, 3):
        wires.send(gain_slot + k, gains, full_gains.at[z, y], device(far[k], y, x, c))
    for copy in own:
        copy.start()

    def slot(i, k):
        return GATHER_SLOTS * i + k

    def along_z(i):
        item = items[i]
        share, whole = shares[item.weight], full[item.weight]
        for k in (1, 2, 3):
            if item.no_x:
                source, target = item.half(share, (), c), item.half(whole, (z, y), c)
            else:
                source, target = item.quarter(share, (), c, x), item.quarter(whole, (z, y), c, x)
            wires.send(slot(i, k), source, target, device(far[k], y, x, c))

    own_done = set()

    def first_hop(i):
        item = items[i]
        whole = full[item.weight]
        if item.weight not in own_done:
            own[item.weight].wait()
            own_done.add(item.weight)
        for k in (1, 2, 3):
            if item.no_x:
                block = item.half(whole, (back[k], y), c)
                wires.arrived(slot(i, k), block)
                wires.send(slot(i, 7 + k), block, block, c_other)
            else:
                block = item.quarter(whole, (back[k], y), c, x)
                wires.arrived(slot(i, k), block)
                wires.send(slot(i, 3 + k), block, block, x_other)
        if item.no_x:
            block = item.half(whole, (ALL, y), c)
        else:
            block = item.quarter(whole, (ALL, y), c, x)
        wires.send(slot(i, 7), block, block, y_other)

    def second_hop(i):
        item = items[i]
        whole = full[item.weight]
        if item.no_x:
            block = item.half(whole, (ALL, 1 - y), c)
            wires.arrived(slot(i, 7), block)
            wires.send(slot(i, 11), block, block, c_other)
            return
        block = item.quarter(whole, (ALL, 1 - y), c, x)
        wires.arrived(slot(i, 7), block)
        wires.send(slot(i, 0), block, block, x_other)
        for k in (1, 2, 3):
            wires.arrived(slot(i, 3 + k), item.quarter(whole, (back[k], y), c, 1 - x))
        for k in (1, 2, 3):
            block = item.half(whole, (back[k], y), c)
            wires.send(slot(i, 7 + k), block, block, c_other)

    def last_hop(i):
        item = items[i]
        whole = full[item.weight]
        if not item.no_x:
            block = item.half(whole, (ALL, 1 - y), c)
            wires.arrived(slot(i, 0), item.quarter(whole, (ALL, 1 - y), c, 1 - x))
            wires.send(slot(i, 11), block, block, c_other)

    def complete(i):
        item = items[i]
        whole = full[item.weight]
        for k in (1, 2, 3):
            wires.arrived(slot(i, 7 + k), item.half(whole, (back[k], y), 1 - c))
        wires.arrived(slot(i, 11), item.half(whole, (ALL, 1 - y), 1 - c))

    def retire(i):
        wires.finish(lambda slot: slot // GATHER_SLOTS == i)

    step_of = Forward(
        dict(
            state,
            out=put,
            tokens=tokens,
            cotangent=cotangent,
            length=length,
            gains=full_gains,
            w_out=full[OUT],
            w_gate=full[GATE],
            w_up=full[UP],
            w_down=full[DOWN].reshape(2816, 1024),
        )
    )
    last_of = {item.weight: i for i, item in enumerate(items)}
    tasks = [(-1, 3, step_of.prepare)]
    for n, name in enumerate(("query", "key", "value")):
        tasks.append((last_of[n], 2, partial(step_of.project, full[n], state[name])))
    tasks += [(last_of[VALUE], 3, partial(step_of.attend, p, p + 2)) for p in (0, 2, 4, 6)]
    tasks.append((last_of[OUT], 3, step_of.project_out))
    for tile_of in pieces(2816, TILE):
        tasks.append((last_of[DOWN], 1, partial(step_of.grad_of_middle, *tile_of)))
    for start, size in FF_CHUNKS:
        there = max(
            i for i, item in enumerate(items) if item.weight == UP and item.start == start
        )
        for at, width in pieces(size, TILE):
            tasks.append((there, 5, partial(step_of.feed_forward, start + at, width)))
        tasks.append((there, 0, partial(step_of.flush, start, size)))

    ahead = 3
    for i in range(min(ahead, len(items))):
        along_z(i)
    own_gains.wait()
    for k in (1, 2, 3):
        wires.arrived(gain_slot + k, full_gains.at[back[k], y])
    wires.send(gain_slot, full_gains.at[:, y], full_gains.at[:, y], y_other)
    stages = (retire, complete, last_hop, second_hop, first_hop)
    lates = (2 * LAG + 2, 2 * LAG + 1, 2 * LAG, LAG, 0)
    for step in range(len(items) + lates[0]):
        for late, stage in zip(lates, stages):
            if 0 <= step - late < len(items):
                stage(step - late)
        if step + ahead < len(items):
            along_z(step + ahead)
        if step == 0:
            wires.arrived(gain_slot, full_gains.at[:, 1 - y])
        there = step - lates[1]
        for n, w in enumerate(KEPT):
            if there == last_of[w]:
                keep[n].start()
        spent = 0
        while tasks and tasks[0][0] <= there and spent < 6:
            _, cost, task = tasks.pop(0)
            task()
            spent += cost
    for _, _, task in tasks:
        task()
    step_of.finish()
    for copy in keep + outgoing:
        copy.wait()
    wires.finish()


def forward(tokens, cotangent, lengths, weights, gains):
    items = gather_items()
    shares = [w.reshape(share_shape(n)) for w, n in zip(weights, COLUMNS)]
    wholes = [(4, 2) + share_shape(n) for n in COLUMNS]
    shapes = [jax.ShapeDtypeStruct(wholes[w], jnp.bfloat16) for w in KEPT]
    shapes += [jax.ShapeDtypeStruct(shape, dtype) for _, shape, dtype in FORWARD_OUTS]
    count = GATHER_SLOTS * len(items) + 4
    anywhere = pl.BlockSpec(memory_space=pl.ANY)
    in_vmem = pl.BlockSpec(memory_space=pltpu.VMEM)
    out = pl.pallas_call(
        partial(forward_kernel, items),
        out_shape=shapes,
        in_specs=[anywhere] * 7
        + [in_vmem] * 4
        + [pl.BlockSpec(memory_space=pltpu.SMEM)],
        out_specs=[anywhere] * len(shapes),
        scratch_shapes=[pltpu.VMEM(shape, jnp.bfloat16) for shape in wholes]
        + [pltpu.VMEM((4, 2, 16, 128), jnp.bfloat16), pltpu.VMEM((16, 128), jnp.bfloat16)]
        + [pltpu.VMEM(shape, dtype) for _, shape, dtype in FORWARD_OUTS + FORWARD_OWN]
        + [
            pltpu.SemaphoreType.DMA((count,)),
            pltpu.SemaphoreType.DMA((count,)),
            pltpu.SemaphoreType.DMA((8,)),
            pltpu.SemaphoreType.DMA((len(KEPT),)),
            pltpu.SemaphoreType.DMA((OUT_COPIES,)),
        ],
        compiler_params=pltpu.CompilerParams(
            collective_id=0, has_side_effects=True, vmem_limit_bytes=63 * MIB
        ),
        name="gather_forward",
    )(*shares, *[g.reshape(1, 128) for g in gains], tokens, cotangent, lengths)
    return out[: len(KEPT)], dict(zip([name for name, _, _ in FORWARD_OUTS], out[len(KEPT) :]))


SUM_SLOTS = 10
RING = 4


class Share:
    def __init__(self, weight, start, size, x_first):
        self.weight, self.start, self.size, self.x_first = weight, start, size, x_first
        self.tall = weight == DOWN
        self.width = 128 if self.tall else size // 2
        self.block = (352 if self.tall else 64, self.width)

    def columns(self, c, x):
        start = c * 512 + x * 256 + self.start if self.tall else self.start + c * self.width
        return pl.ds(pl.multiple_of(start, 128), self.width)

    def quarter(self, sums, c, x):
        if self.tall:
            return sums.at[c, x, self.start // 128]
        return sums.at[x, :, self.columns(c, x)]

    def half(self, sums, c):
        if self.tall:
            return sums.at[c, :, self.start // 128]
        return sums.at[:, :, self.columns(c, 0)]


def share_items():
    order = [(GATE, 2048, 768, True), (DOWN, 0, 128, False), (DOWN, 128, 128, True)]
    order += [(GATE, 0, 1024, False), (GATE, 1024, 1024, True)]
    order += [(UP, 0, 1024, True), (UP, 1024, 1024, False), (UP, 2048, 768, False)]
    order += [(OUT, 0, 1024, True), (QUERY, 0, 1024, False), (KEY, 0, 1024, True)]
    order += [(VALUE, 0, 768, True), (VALUE, 768, 256, False)]
    return [Share(*item) for item in order]


def plus(left, right):
    return left + right


def dot_tn(left, right):
    return lax.dot_general(
        left, right, (((0,), (0,)), ((), ())), preferred_element_type=jnp.float32
    )


BACKWARD_IN = (
    "query",
    "key",
    "value",
    "lse",
    "h_t",
    "h2_t",
    "att_t",
    "d_b",
    "d_res",
    "d_proj",
    "g_ffn",
    "gain",
)


class Backward:
    def __init__(self, refs):
        self.__dict__.update(refs)

    def prepare(self):
        length = self.length[0, 0]
        for block in range(4):
            rows = slice(128 * block, 128 * block + 128)
            place_k = lax.broadcasted_iota(jnp.int32, (128, 512), 0) + 128 * block
            place_q = lax.broadcasted_iota(jnp.int32, (128, 512), 1)
            same = (place_q >= length) == (place_k >= length)
            allowed = same & (place_k <= place_q)
            self.bias[rows, :] = jnp.where(allowed, 0.0, NEGATIVE)

    def multiply(self, left_t, right, item, target, core):
        columns = item.columns(core, 0)

        def rows(m, _):
            product = dot(left_t[tile(m, 256), :], right[:, columns]).astype(jnp.bfloat16)
            product = product.reshape(2, 2, 64, item.width)
            for xx in (0, 1):
                target[xx, m] = product[:, xx]
            return 0

        lax.fori_loop(0, 4, rows, 0)

    def multiply_tall(self, left, right, groups):
        def rows(m, _):
            at = tile(m, 256)
            turned = left[:, at].T
            for columns, targets in groups:
                product = dot(turned, right[:, columns]).astype(jnp.bfloat16)
                for n, (target, xx) in enumerate(targets):
                    target.reshape(2, 2816, 128)[xx, at, :] = product[:, 128 * n : 128 * n + 128]
            return 0

        lax.fori_loop(0, 11, rows, 0)

    def attend_back(self, first, last):
        low = jnp.bfloat16

        def pair(p, _):
            at = tile(p, 128)
            wo_rows = self.w_rows[p].reshape(128, 1024)
            grad = dot_nt(self.d_proj[...], wo_rows).astype(low)
            query = (self.query[:, at].astype(jnp.float32) * SCORE_SCALE).astype(low)
            key, value = self.key[:, at], self.value[:, at]
            left = lax.broadcasted_iota(jnp.int32, (512, 128), 1) < HEAD
            none = jnp.zeros((512, 128), low)
            sides = [
                [jnp.where(side, v, none) for v in (query, key, value, grad)]
                for side in (left, ~left)
            ]
            grad_key, grad_value = [None, None], [None, None]
            for block in (0, 1):
                rows, seen = slice(256 * block, 256 * block + 256), slice(0, 256 * block + 256)
                grad_query = None
                parts_key, parts_value = None, None
                for n, (own_query, own_key, own_value, own_grad) in enumerate(sides):
                    self.d_in[seen, 0:256] = dot_nt(own_key[seen], query[rows])
                    self.d_in[seen, 256:512] = dot_nt(own_value[seen], grad[rows])
                    self.back_rows(p, n, rows, 256 * block + 256)
                    grad_scores, probs = self.grad_scores[seen, :], self.probs[seen, :]
                    part_query = dot_tn(grad_scores, own_key[seen])
                    part_key = dot(grad_scores, own_query[rows])
                    part_value = dot(probs, own_grad[rows])
                    if n == 0:
                        grad_query, parts_key, parts_value = part_query, part_key, part_value
                    else:
                        grad_query += part_query
                        parts_key += part_key
                        parts_value += part_value
                self.query[rows, at] = (grad_query * SCORE_SCALE).astype(low)
                if block == 0:
                    grad_key[0], grad_value[0] = parts_key, parts_value
                else:
                    grad_key = [grad_key[0] + parts_key[:256], parts_key[256:]]
                    grad_value = [grad_value[0] + parts_value[:256], parts_value[256:]]
            for block in (0, 1):
                rows = slice(256 * block, 256 * block + 256)
                self.key[rows, at] = grad_key[block].astype(low)
                self.value[rows, at] = grad_value[block].astype(low)
            return 0

        lax.fori_loop(first, last, pair, 0)

    def back_rows(self, p, n, rows, count):
        low = jnp.bfloat16
        held = self.d_in
        lse = self.lse[p, n : n + 1, rows]

        def first_pass(r, centre):
            keys = tile(r, 64)
            probs = jnp.exp(held[keys, 0:256] + self.bias[keys, rows] - lse)
            held[keys, 0:256] = probs
            self.probs[keys, :] = probs.astype(low)
            return centre + jnp.sum((held[keys, 256:512] * probs).reshape(8, 8, 256), axis=0)

        centre = lax.fori_loop(0, count // 64, first_pass, jnp.zeros((8, 256), jnp.float32), unroll=2)
        centre = jnp.sum(centre, axis=0, keepdims=True)

        def second_pass(r, _):
            keys = tile(r, 64)
            grad = held[keys, 0:256] * (held[keys, 256:512] - centre)
            self.grad_scores[keys, :] = grad.astype(low)
            return 0

        lax.fori_loop(0, count // 64, second_pass, 0, unroll=2)

    def grad_hidden(self, t):
        at = pl.ds(256 * t, 256)
        total = None
        for n, grad in enumerate((self.query, self.key, self.value)):
            part = dot_nt(grad[...], self.w_rows[2 * n : 2 * n + 2].reshape(256, 1024))
            total = part if total is None else total + part
        self.d_in[:, at] = total

    def finish(self):
        self.gain_total[...] = jnp.zeros_like(self.gain_total)

        def rows_of(block, _):
            rows = tile(block, 64)
            values = self.tokens[rows, :].astype(jnp.float32)
            factor = lax.rsqrt(jnp.mean(values * values, axis=-1, keepdims=True) + NORM_EPS)
            normed = values * factor
            grad = self.d_in[rows, :]
            self.gain_total[...] += jnp.sum((grad * normed).reshape(8, 8, 1024), axis=0)
            grad_normed = grad * self.gain[0:1, :].astype(jnp.float32)
            mean = jnp.mean(grad_normed * normed, axis=-1, keepdims=True)
            self.d_in[rows, :] = self.d_res[rows, :] + factor * (
                grad_normed - normed * mean
            )
            return 0

        lax.fori_loop(0, 8, rows_of, 0)
        self.gain_lines[...] = jnp.zeros_like(self.gain_lines)
        lines = [jnp.sum(v[...], axis=0, keepdims=True) for v in (self.gain_total, self.g_ffn)]
        for s in range(8):
            for n, line in enumerate(lines):
                self.gain_lines[s // 2, s % 2, n : n + 1] = line[:, 128 * s : 128 * s + 128]


def backward_kernel(items, *refs):
    refs = list(refs)

    def take(n):
        taken = refs[:n]
        del refs[:n]
        return taken

    kept = take(len(KEPT))
    middle_in, grad_gate_in, grad_up_in = take(3)
    saved_in = dict(zip(BACKWARD_IN, take(len(BACKWARD_IN))))
    tokens_in, length = take(2)
    sums = take(7)
    gain_sums, input_grad_out = take(2)
    saved = dict(zip(BACKWARD_IN, take(len(BACKWARD_IN))))
    d_in, wide, w_rows, bias, probs, grad_scores, gain_total, gain_lines = take(8)
    mine, from_first, from_second, from_z = (take(len(items)) for _ in range(4))
    ring, tall_ring = take(RING), take(2)
    outbox, tall_outbox = take(2), take(2)
    gain_core, gain_x, gain_y, gain_z = take(4)
    send_sems, recv_sems, load_sems, credit = refs
    z, y, x, c = place()
    far = [lax.rem(z + k, 4) for k in range(4)]
    back = [lax.rem(z + 4 - k, 4) for k in range(4)]
    x_other, y_other, c_other = (
        device(z, y, 1 - x, c),
        device(z, 1 - y, x, c),
        device(z, y, x, 1 - c),
    )
    loads = {}

    def load(name, source, target):
        loads[name] = pltpu.make_async_copy(source, target, load_sems.at[len(loads)])
        loads[name].start()

    waited = set()

    def loaded(*names):
        for name in names:
            if name not in waited:
                loads[name].wait()
                waited.add(name)

    load("d_gate", grad_gate_in, wide.at[1])
    load("h2_t", saved_in["h2_t"], saved["h2_t"])
    load("mid", middle_in, wide.at[0])
    load("d_b", saved_in["d_b"], saved["d_b"])
    load("wo_rows", kept[OUT].reshape(8, 2, 64, 1024), w_rows)
    for name in BACKWARD_IN:
        if name not in loads:
            load(name, saved_in[name], saved[name])
    greet()
    wires = Wires(send_sems, recv_sems)
    work = Backward(
        dict(
            saved,
            tokens=saved["d_b"],
            length=length,
            w_rows=w_rows,
            probs=probs,
            grad_scores=grad_scores,
            bias=bias,
            d_in=d_in,
            gain_total=gain_total,
            gain_lines=gain_lines,
        )
    )
    tall_items = [i for i, item in enumerate(items) if item.tall]
    wide_items = [i for i, item in enumerate(items) if not item.tall]

    def slot(i, k):
        return SUM_SLOTS * i + k

    def core_slots(i):
        return (slot(i, 0), slot(i, 8))

    def from_core(i):
        if items[i].tall:
            return tall_ring[tall_items.index(i)]
        return ring[wide_items.index(i) % RING].at[..., : items[i].width]

    def produce(i):
        item = items[i]
        if item.tall:
            number = tall_items.index(i)
            if number == 0:
                loaded("mid", "d_b")
                groups = []
                for core, boxes in ((1 - c, tall_outbox), (c, [mine[j] for j in tall_items])):
                    columns = pl.ds(pl.multiple_of(512 * core, 512), 512)
                    groups.append((columns, [(boxes[j], xx) for xx in (0, 1) for j in (0, 1)]))
                work.multiply_tall(wide.at[0], saved["d_b"], groups)
                load("d_up", grad_up_in, wide.at[0])
                load("tokens", tokens_in, saved["d_b"])
            box = tall_outbox[number]
        else:
            number = wide_items.index(i)
            if number >= 2:
                wires.finish(lambda s: s in core_slots(wide_items[number - 2]))
            box = outbox[number % 2].at[..., : item.width]
            left, right, names = {
                GATE: (saved["h2_t"], wide.at[1], ("h2_t", "d_gate")),
                UP: (saved["h2_t"], wide.at[0], ("d_up",)),
                OUT: (saved["att_t"], saved["d_proj"], ("att_t", "d_proj")),
                QUERY: (saved["h_t"], saved["query"], ("h_t",)),
                KEY: (saved["h_t"], saved["key"], ()),
                VALUE: (saved["h_t"], saved["value"], ()),
            }[item.weight]
            loaded(*names)
            multiply = partial(work.multiply, left, right, item)
            if number >= RING:
                pl.semaphore_wait(credit, 1)
            multiply(box, 1 - c)
        for xx in (0, 1):
            wires.send(core_slots(i)[xx], box.at[xx], from_core(i).at[xx], c_other)
        if not item.tall:
            multiply(mine[i], c)

    def first_hop(i):
        item, own, other = items[i], mine[i], from_core(i)
        for xx in (0, 1):
            wires.arrived(core_slots(i)[xx], other.at[xx])

        def add(at, _):
            for xx in (0, 1):
                for yy in (0, 1):
                    own[xx, at, yy] = plus(own[xx, at, yy], other[xx, at, yy])
            return 0

        lax.fori_loop(0, 4, add, 0)
        if not item.tall and wide_items.index(i) + RING < len(wide_items):
            pl.semaphore_signal(credit, inc=1, device_id=c_other, device_id_type=MESH)
        if item.x_first:
            wires.send(slot(i, 1), own.at[1 - x], from_first[i], x_other)
        else:
            wires.send(slot(i, 1), own.at[:, :, 1 - y], from_first[i], y_other)

    def second_hop(i):
        item, own, other = items[i], mine[i], from_first[i]
        wires.arrived(slot(i, 1), other)

        def add(at, _):
            for side in (0, 1):
                if item.x_first:
                    own[x, at, side] = plus(own[x, at, side], other[at, side])
                else:
                    own[side, at, y] = plus(own[side, at, y], other[side, at])
            return 0

        lax.fori_loop(0, 4, add, 0)
        if item.x_first:
            wires.send(slot(i, 2), own.at[x, :, 1 - y], from_second[i], y_other)
        else:
            to_z(i, lambda k: own.at[:, far[k], y])

    def to_z(i, block):
        for k in (1, 2, 3):
            wires.send(slot(i, 2 + k), block(k), from_z[i].at[k - 1], device(far[k], y, x, c))

    def z_total(i, own_part):
        total = own_part.astype(jnp.float32)
        for k in (1, 2, 3):
            wires.arrived(slot(i, 2 + k), from_z[i].at[k - 1])
            total += from_z[i][k - 1].astype(jnp.float32)
        return total.astype(jnp.bfloat16)

    def third_hop(i):
        item, own, other = items[i], mine[i], from_second[i]
        if not item.x_first:
            own[:, z, y] = z_total(i, own[:, z, y])
            wires.send(slot(i, 2), own.at[:, z, y], other, x_other)
            return
        wires.arrived(slot(i, 2), other)

        def add(at, _):
            own[x, at, y] = plus(own[x, at, y], other[at])
            return 0

        lax.fori_loop(0, 4, add, 0)
        to_z(i, lambda k: own.at[x, far[k], y])

    def fourth_hop(i):
        item, own = items[i], mine[i]
        if not item.x_first:
            wires.arrived(slot(i, 2), from_second[i])
            block = item.half(sums[item.weight], c)
            block[...] = plus(own[:, z, y], from_second[i][...])
            wires.send(slot(i, 7), block, block, c_other)
            return
        block = item.quarter(sums[item.weight], c, x)
        block[...] = z_total(i, own[x, z, y])
        wires.send(slot(i, 6), block, block, x_other)

    def to_sibling(i):
        item = items[i]
        if item.x_first:
            wires.arrived(slot(i, 6), item.quarter(sums[item.weight], c, 1 - x))
            block = item.half(sums[item.weight], c)
            wires.send(slot(i, 7), block, block, c_other)

    def complete(i):
        item = items[i]
        wires.arrived(slot(i, 7), item.half(sums[item.weight], 1 - c))
        wires.finish(lambda s: s // SUM_SLOTS == i)

    base = SUM_SLOTS * len(items)

    def gains_one():
        wires.send(base, gain_lines, gain_core, c_other)

    def gains_two():
        wires.arrived(base, gain_core)
        gain_core[...] = gain_lines[...] + gain_core[...]
        wires.send(base + 1, gain_core, gain_x, x_other)

    def gains_three():
        wires.arrived(base + 1, gain_x)
        gain_x[...] = gain_core[...] + gain_x[...]
        wires.send(base + 2, gain_x.at[:, 1 - y], gain_y, y_other)

    def gains_four():
        wires.arrived(base + 2, gain_y)
        gain_y[...] = gain_x[:, y] + gain_y[...]
        for k in (1, 2, 3):
            wires.send(base + 2 + k, gain_y.at[far[k]], gain_z.at[z], device(far[k], y, x, c))
        gain_z[z] = gain_y[z]

    def gains_five():
        for k in (1, 2, 3):
            wires.arrived(base + 2 + k, gain_z.at[back[k]])
        gain_sums[...] = (gain_z[0] + gain_z[1]) + (gain_z[2] + gain_z[3])

    def fetch_rows(t):
        for n in range(3):
            load(("rows", n, t), kept[n].at[t], w_rows.at[2 * n : 2 * n + 2])

    def attend_back(p):
        if p == 0:
            loaded("query", "key", "value", "lse", "d_proj", "wo_rows")
        work.attend_back(p, p + 1)
        if p == 7:
            fetch_rows(0)

    def grad_hidden(t):
        loaded(*[("rows", n, t) for n in range(3)])
        work.grad_hidden(t)
        if t < 3:
            fetch_rows(t + 1)

    def finish():
        loaded("tokens", "d_res", "g_ffn", "gain")
        work.finish()
        load("d_in", d_in, input_grad_out)
        gains_one()

    beside = {1: [work.prepare]}
    for p in range(8):
        beside.setdefault(1 + p, []).append(partial(attend_back, p))
    for t in range(4):
        beside.setdefault(9 + t // 2, []).append(partial(grad_hidden, t))
    beside.setdefault(11, []).append(finish)
    for n, task in enumerate((gains_two, gains_three, gains_four, gains_five)):
        beside.setdefault(13 + 2 * n, []).append(task)

    stages = (complete, to_sibling, fourth_hop, third_hop, second_hop, first_hop, produce)
    lates = (16, 14, 12, 9, 6, 3, 0)
    for step in range(len(items) + lates[0]):
        for late, stage in zip(lates, stages):
            if 0 <= step - late < len(items):
                stage(step - late)
        for task in beside.get(step, []):
            task()
    loaded("d_in")
    wires.finish()


def backward(tokens, lengths, kept, saved):
    items = share_items()
    low, wide = jnp.bfloat16, jnp.float32
    dtypes = {name: (shape, dtype) for name, shape, dtype in FORWARD_OUTS}
    shapes = [
        jax.ShapeDtypeStruct((2, 2, 2, 352, 128) if n is None else (2, 64, n), low) for n in COLUMNS
    ]
    shapes += [jax.ShapeDtypeStruct((8, 128), wide), jax.ShapeDtypeStruct((512, 1024), wide)]
    count = SUM_SLOTS * len(items) + 6
    anywhere = pl.BlockSpec(memory_space=pl.ANY)
    in_vmem = pl.BlockSpec(memory_space=pltpu.VMEM)
    n_loads = 6 + len(BACKWARD_IN) + 12

    def buffers(lead_of):
        return [pltpu.VMEM(lead_of(item) + item.block, low) for item in items]

    out = pl.pallas_call(
        partial(backward_kernel, items),
        out_shape=shapes,
        in_specs=[anywhere] * (len(KEPT) + 3 + len(BACKWARD_IN) + 1)
        + [pl.BlockSpec(memory_space=pltpu.SMEM)],
        out_specs=[in_vmem] * 8 + [anywhere],
        scratch_shapes=[pltpu.VMEM(*dtypes[name]) for name in BACKWARD_IN]
        + [
            pltpu.VMEM((512, 1024), wide),
            pltpu.VMEM((2, 512, 2816), low),
            pltpu.VMEM((8, 2, 64, 1024), low),
            pltpu.VMEM((512, 512), wide),
            pltpu.VMEM((512, 256), low),
            pltpu.VMEM((512, 256), low),
            pltpu.VMEM((8, 1024), wide),
            pltpu.VMEM((4, 2, 8, 128), wide),
        ]
        + buffers(lambda item: (2, 4, 2))
        + buffers(lambda item: (4, 2) if item.x_first else (2, 4))
        + buffers(lambda item: (4,) if item.x_first else (2,))
        + buffers(lambda item: (3,) if item.x_first else (3, 2))
        + [pltpu.VMEM((2, 4, 2, 64, 512), low)] * RING
        + [pltpu.VMEM((2, 4, 2, 352, 128), low)] * 2
        + [pltpu.VMEM((2, 4, 2, 64, 512), low)] * 2
        + [pltpu.VMEM((2, 4, 2, 352, 128), low)] * 2
        + [
            pltpu.VMEM((4, 2, 8, 128), wide),
            pltpu.VMEM((4, 2, 8, 128), wide),
            pltpu.VMEM((4, 8, 128), wide),
            pltpu.VMEM((4, 8, 128), wide),
            pltpu.SemaphoreType.DMA((count,)),
            pltpu.SemaphoreType.DMA((count,)),
            pltpu.SemaphoreType.DMA((n_loads,)),
            pltpu.SemaphoreType.REGULAR,
        ],
        compiler_params=pltpu.CompilerParams(
            collective_id=1, has_side_effects=True, vmem_limit_bytes=63 * MIB
        ),
        name="backward_sum",
    )(
        *kept,
        saved["mid"],
        saved["d_gate"],
        saved["d_up"],
        *[saved[name] for name in BACKWARD_IN],
        tokens,
        lengths,
    )
    return out[:7], out[7], out[8]


def unpack_kernel(*refs):
    blocks, (gain_sums, mixed, d_in) = refs[:7], refs[7:10]
    sums, (gain_attn, gain_ffn, mixed_out, input_out) = refs[10:17], refs[17:21]
    held, wide = refs[21:28], refs[28:35]
    mixed_held, input_held, in_sems, out_sems = refs[35:]
    sources = (d_in, mixed, *blocks)
    places = (input_held, mixed_held, *held)
    results = (input_held, mixed_held, *wide)
    targets = (input_out, mixed_out, *sums)
    ins = [pltpu.make_async_copy(a, b, in_sems.at[n]) for n, (a, b) in enumerate(zip(sources, places))]
    outs = [pltpu.make_async_copy(a, b, out_sems.at[n]) for n, (a, b) in enumerate(zip(results, targets))]
    order = (6, 7, 8, 2, 3, 4, 5, 0, 1)
    for n in order:
        ins[n].start()
    for n in order:
        ins[n].wait()
        if n == 8:
            for b in range(8):
                wide[6][:, 128 * b : 128 * b + 128] = held[6][b // 4, b // 2 % 2, b % 2].astype(
                    jnp.float32
                )
        elif n >= 2:
            wide[n - 2][...] = held[n - 2][...].astype(jnp.float32)
        outs[n].start()
    gain_attn[...] = gain_sums[0:1]
    gain_ffn[...] = gain_sums[1:2]
    for n in order:
        outs[n].wait()


def unpack(blocks, gain_sums, mixed, d_in):
    wide = jnp.float32
    anywhere = pl.BlockSpec(memory_space=pl.ANY)
    in_vmem = pl.BlockSpec(memory_space=pltpu.VMEM)
    shapes = [
        jax.ShapeDtypeStruct((352, 1024) if n is None else (2, 64, n), wide) for n in COLUMNS
    ]
    held = [pltpu.VMEM(b.shape, b.dtype) for b in blocks]
    held += [pltpu.VMEM(v.shape, wide) for v in shapes]
    held += [pltpu.VMEM(v.shape, v.dtype) for v in (mixed, d_in)]
    shapes += [jax.ShapeDtypeStruct((1, 128), wide)] * 2
    shapes += [jax.ShapeDtypeStruct(v.shape, v.dtype) for v in (mixed, d_in)]
    out = pl.pallas_call(
        unpack_kernel,
        out_shape=shapes,
        in_specs=[anywhere] * 7 + [in_vmem] + [anywhere] * 2,
        out_specs=[anywhere] * 7 + [in_vmem] * 2 + [anywhere] * 2,
        scratch_shapes=held + [pltpu.SemaphoreType.DMA((9,)), pltpu.SemaphoreType.DMA((9,))],
        compiler_params=pltpu.CompilerParams(vmem_limit_bytes=62 * MIB),
        name="unpack",
    )(*blocks, gain_sums, mixed, d_in)
    sums = [s.reshape(-1, s.shape[-1]) for s in out[:7]]
    return sums, [g.reshape(128) for g in out[7:9]], out[9], out[10]


def gather_plain(weights, gains):
    everything = (*weights, *gains)
    whole = [lax.all_gather(v, "dp", axis=0, tiled=True) for v in everything]
    return whole[: len(weights)], whole[len(weights) :]


def sum_plain(grads, gain_grads):
    shares = [
        lax.psum_scatter(g.astype(jnp.float32), "dp", scatter_dimension=0, tiled=True)
        for g in (*grads, *gain_grads)
    ]
    sums = [lax.psum(s, ("rep", "cores")) for s in shares]
    return sums[: len(grads)], sums[len(grads) :]


def on_any_device(
    tokens,
    norm_attn,
    w_query,
    w_key,
    w_value,
    w_out,
    norm_ffn,
    w_gate,
    w_up,
    w_down,
    lengths,
    cotangent,
):
    rows = tokens.shape[0]
    low = jnp.bfloat16
    allowed, valid = masks(lengths, rows)
    whole, gains = gather_plain(
        (w_query, w_key, w_value, w_out, w_gate, w_up, w_down), (norm_attn, norm_ffn)
    )
    full_query, full_key, full_value, full_out, full_gate, full_up, full_down = whole
    gain_attn, gain_ffn = gains
    inputs = tokens.astype(jnp.float32)
    normed, factor = normalize(inputs)
    hidden = (normed * gain_attn.astype(jnp.float32)).astype(low)
    query = matmul(hidden, full_query).astype(low)
    keyed = matmul(hidden, full_key).astype(low)
    valued = matmul(hidden, full_value).astype(low)
    query_groups, key_groups, value_groups = (to_groups(query), to_groups(keyed), to_groups(valued))
    attended_groups, log_total = lax.map(
        partial(attend, allowed), (query_groups, key_groups, value_groups)
    )
    attended = from_groups(attended_groups)
    residual = inputs + matmul(attended, full_out)
    normed_two, factor_two = normalize(residual)
    hidden_two = (normed_two * gain_ffn.astype(jnp.float32)).astype(low)
    gate = matmul(hidden_two, full_gate)
    upward = matmul(hidden_two, full_up)
    sigma = jax.nn.sigmoid(gate)
    middle = (gate * sigma * upward).astype(low)
    mixed = (valid[:, None] * (residual + matmul(middle, full_down))).astype(low)
    grad_output = cotangent.astype(jnp.float32) * valid[:, None]
    grad_branch = grad_output.astype(low)
    grad_down = matmul_tn(middle, grad_branch)
    grad_middle = matmul_nt(grad_branch, full_down)
    grad_gate_rows = (grad_middle * upward * sigma * (1.0 + gate * (1.0 - sigma))).astype(low)
    grad_up_rows = (grad_middle * gate * sigma).astype(low)
    grad_gate = matmul_tn(hidden_two, grad_gate_rows)
    grad_up = matmul_tn(hidden_two, grad_up_rows)
    grad_hidden_two = matmul_nt(grad_gate_rows, full_gate) + matmul_nt(grad_up_rows, full_up)
    grad_gain_ffn = jnp.sum(grad_hidden_two * normed_two, axis=0)
    grad_residual = grad_output + norm_back(
        grad_hidden_two * gain_ffn.astype(jnp.float32), normed_two, factor_two
    )
    grad_proj = grad_residual.astype(low)
    grad_out = matmul_tn(attended, grad_proj)
    grad_attended = matmul_nt(grad_proj, full_out).astype(low)
    grad_query_g, grad_key_g, grad_value_g = lax.map(
        partial(attend_back, allowed),
        (query_groups, key_groups, value_groups, to_groups(grad_attended), log_total),
    )
    grad_query_rows = from_groups(grad_query_g)
    grad_key_rows = from_groups(grad_key_g)
    grad_value_rows = from_groups(grad_value_g)
    grad_query = matmul_tn(hidden, grad_query_rows)
    grad_key = matmul_tn(hidden, grad_key_rows)
    grad_value = matmul_tn(hidden, grad_value_rows)
    grad_hidden = (
        matmul_nt(grad_query_rows, full_query)
        + matmul_nt(grad_key_rows, full_key)
        + matmul_nt(grad_value_rows, full_value)
    )
    grad_gain_attn = jnp.sum(grad_hidden * normed, axis=0)
    input_grad = grad_residual + norm_back(
        grad_hidden * gain_attn.astype(jnp.float32), normed, factor
    )
    grads = (grad_query, grad_key, grad_value, grad_out, grad_gate, grad_up, grad_down)
    sums, gain_sums = sum_plain([g.astype(low) for g in grads], (grad_gain_attn, grad_gain_ffn))
    return (
        mixed,
        input_grad,
        gain_sums[0],
        sums[0],
        sums[1],
        sums[2],
        sums[3],
        gain_sums[1],
        sums[4],
        sums[5],
        sums[6],
    )


def on_tuned_device(
    tokens,
    norm_attn,
    w_query,
    w_key,
    w_value,
    w_out,
    norm_ffn,
    w_gate,
    w_up,
    w_down,
    lengths,
    cotangent,
):
    weights = (w_query, w_key, w_value, w_out, w_gate, w_up, w_down)
    kept, saved = forward(tokens, cotangent, lengths, weights, (norm_attn, norm_ffn))
    blocks, gain_lines, d_in = backward(tokens, lengths, kept, saved)
    sums, gain_sums, mixed, d_in = unpack(blocks, gain_lines, saved["mixed"], d_in)
    return (
        mixed,
        d_in,
        gain_sums[0],
        *sums[:4],
        gain_sums[1],
        *sums[4:],
    )


def solution(mesh):
    tuned = dict(mesh.shape) == {"dp": 8, "rep": 2, "cores": 2}
    tokens_placed = P(("dp", "rep", "cores"), None)
    share, gain = P("dp", None), P("dp")
    return jax.shard_map(
        on_tuned_device if tuned else on_any_device,
        mesh=mesh,
        in_specs=(
            tokens_placed,
            gain,
            share,
            share,
            share,
            share,
            gain,
            share,
            share,
            share,
            tokens_placed,
            tokens_placed,
        ),
        out_specs=(
            tokens_placed,
            tokens_placed,
            gain,
            share,
            share,
            share,
            share,
            gain,
            share,
            share,
            share,
        ),
        check_vma=False,
    )
```

```python
from functools import partial

import jax
import jax.numpy as jnp
from jax import lax
from jax.experimental import pallas as pl
from jax.experimental.pallas import tpu as pltpu
from jax.sharding import PartitionSpec as P

HEADS = 16
HEAD = 64


NORM_EPS = 1e-05
SCORE_SCALE = 0.125
NEGATIVE = -1e30
head_group = 4
MESH = pl.DeviceIdType.MESH
MIB = 1024 * 1024


def masks(block_len, rows):
    bounds = jnp.cumsum(block_len[0])
    place = jnp.arange(rows, dtype=jnp.int32)
    segment = jnp.sum((place[:, None] >= bounds[None, :]).astype(jnp.int32), axis=1)
    allowed = (segment[:, None] == segment[None, :]) & (place[None, :] <= place[:, None])
    valid = (segment < block_len.shape[1]).astype(jnp.float32)
    return (allowed, valid)


def normalize(values):
    factor = lax.rsqrt(jnp.mean(values * values, axis=-1, keepdims=True) + NORM_EPS)
    return (values * factor, factor)


def norm_back(grad_normed, normed, factor):
    return factor * (grad_normed - normed * jnp.mean(grad_normed * normed, axis=-1, keepdims=True))


def matmul(left, right):
    return jnp.dot(left, right, preferred_element_type=jnp.float32)


def matmul_tn(left, right):
    return lax.dot_general(
        left, right, (((0,), (0,)), ((), ())), preferred_element_type=jnp.float32
    )


def matmul_nt(left, right):
    return lax.dot_general(
        left, right, (((1,), (1,)), ((), ())), preferred_element_type=jnp.float32
    )


def to_groups(matrix):
    rows = matrix.shape[0]
    split = matrix.reshape(rows, HEADS // head_group, head_group, HEAD)
    return split.transpose(1, 2, 0, 3)


def from_groups(grouped):
    rows = grouped.shape[2]
    return grouped.transpose(2, 0, 1, 3).reshape(rows, HEADS * HEAD)


def group_scores(allowed, query_g, key_g):
    raw = (
        jnp.einsum("hqe,hke->hqk", query_g, key_g, preferred_element_type=jnp.float32) * SCORE_SCALE
    )
    return jnp.where(allowed[None], raw, NEGATIVE)


def attend(allowed, operands):
    query_g, key_g, value_g = operands
    scores = group_scores(allowed, query_g, key_g)
    top = jnp.max(scores, axis=-1, keepdims=True)
    expo = jnp.exp(scores - top)
    total = jnp.sum(expo, axis=-1, keepdims=True)
    probs_low = (expo / total).astype(jnp.bfloat16)
    result = jnp.einsum("hqk,hke->hqe", probs_low, value_g, preferred_element_type=jnp.float32)
    return (result.astype(jnp.bfloat16), top[..., 0] + jnp.log(total[..., 0]))


def attend_back(allowed, operands):
    query_g, key_g, value_g, grad_g, lse = operands
    scores = group_scores(allowed, query_g, key_g)
    probs = jnp.exp(scores - lse[..., None])
    grad_probs = jnp.einsum("hqe,hke->hqk", grad_g, value_g, preferred_element_type=jnp.float32)
    centre = jnp.sum(grad_probs * probs, axis=-1, keepdims=True)
    grad_scores = (probs * (grad_probs - centre)).astype(jnp.bfloat16)
    grad_query = (
        jnp.einsum("hqk,hke->hqe", grad_scores, key_g, preferred_element_type=jnp.float32)
        * SCORE_SCALE
    )
    grad_key = (
        jnp.einsum("hqk,hqe->hke", grad_scores, query_g, preferred_element_type=jnp.float32)
        * SCORE_SCALE
    )
    grad_value = jnp.einsum(
        "hqk,hqe->hke", probs.astype(jnp.bfloat16), grad_g, preferred_element_type=jnp.float32
    )
    return (
        grad_query.astype(jnp.bfloat16),
        grad_key.astype(jnp.bfloat16),
        grad_value.astype(jnp.bfloat16),
    )


class Part:
    def __init__(self, weight, tall, start, size, no_x):
        self.weight, self.tall, self.start, self.size = weight, tall, start, size
        self.no_x = no_x

    def quarter(self, ref, lead, c, x):
        if self.tall:
            columns = pl.ds(pl.multiple_of(c * 512 + x * 256, 256), 256)
            return ref.at[(*lead, pl.ds(self.start, self.size), columns)]
        return ref.at[(*lead, x, slice(None), self.columns(c))]

    def half(self, ref, lead, c):
        if self.tall:
            columns = pl.ds(pl.multiple_of(c * 512, 512), 512)
            return ref.at[(*lead, pl.ds(self.start, self.size), columns)]
        return ref.at[(*lead, slice(None), slice(None), self.columns(c))]

    def columns(self, c):
        width = self.size // 2
        return pl.ds(pl.multiple_of(self.start + c * width, 128), width)


def pieces(total, most):
    return [(start, min(most, total - start)) for start in range(0, total, most)]


def place():
    d = lax.axis_index("dp")
    return lax.div(d, 2), lax.rem(d, 2), lax.axis_index("rep"), lax.axis_index("cores")


def device(z, y, x, c):
    return {"dp": 2 * z + y, "rep": x, "cores": c}


def partners():
    z, y, x, c = place()
    others = [device(lax.rem(z + k, 4), y, x, c) for k in (1, 2, 3)]
    return others + [device(z, 1 - y, x, c), device(z, y, 1 - x, c), device(z, y, x, 1 - c)]


def greet():
    barrier = pltpu.get_barrier_semaphore()
    for other in partners():
        pl.semaphore_signal(barrier, inc=1, device_id=other, device_id_type=MESH)


def await_partners():
    pl.semaphore_wait(pltpu.get_barrier_semaphore(), len(partners()))


class Wires:
    def __init__(self, send_sems, recv_sems):
        self.send_sems, self.recv_sems, self.sent = send_sems, recv_sems, []

    def copy(self, slot, source, target, other):
        return pltpu.make_async_remote_copy(
            src_ref=source,
            dst_ref=target,
            send_sem=self.send_sems.at[slot],
            recv_sem=self.recv_sems.at[slot],
            device_id=other,
            device_id_type=MESH,
        )

    def send(self, slot, source, target, other):
        copy = self.copy(slot, source, target, other)
        copy.start()
        self.sent.append((slot, copy))

    def arrived(self, slot, target):
        z, y, x, c = place()
        self.copy(slot, target, target, device(z, y, x, 1 - c)).wait_recv()

    def finish(self, chosen=lambda slot: True):
        for slot, copy in self.sent:
            if chosen(slot):
                copy.wait_send()
        self.sent = [(slot, copy) for slot, copy in self.sent if not chosen(slot)]


GATHER_SLOTS = 12
LAG = 2
ALL = slice(None)
COLUMNS = (1024, 1024, 1024, 1024, 2816, 2816, None)
QUERY, KEY, VALUE, OUT, GATE, UP, DOWN = range(7)
TILE = 512


FF_CHUNKS = tuple(pieces(2816, 512))


def gather_items():
    order = [(QUERY, 0, 256, True), (QUERY, 256, 768, False), (KEY, 0, 1024, True)]
    order += [(VALUE, 0, 1024, False), (OUT, 0, 1024, False)]
    order += [(DOWN, 0, 128, False), (DOWN, 128, 128, True), (DOWN, 256, 96, False)]
    for n, (start, size) in enumerate(FF_CHUNKS):
        order += [(GATE, start, size, n == 5), (UP, start, size, n in (0, 3, 5))]
    return [Part(w, w == DOWN, start, size, no_x) for w, start, size, no_x in order]


def dot(left, right):
    return lax.dot_general(
        left, right, (((1,), (0,)), ((), ())), preferred_element_type=jnp.float32
    )


def dot_nt(left, right):
    return lax.dot_general(
        left, right, (((1,), (1,)), ((), ())), preferred_element_type=jnp.float32
    )


def tile(index, size):
    return pl.ds(pl.multiple_of(index * size, size), size)


def weight_columns(ref, at):
    return ref[:, :, :, :, at].reshape(1024, -1)


class Forward:
    def __init__(self, refs):
        self.__dict__.update(refs)

    def prepare(self):
        for s in range(8):
            self.gain[:, 128 * s : 128 * s + 128] = self.gains[s // 2, s % 2]
        length = self.length[0, 0]
        for block in range(4):
            rows = slice(128 * block, 128 * block + 128)
            place_q = lax.broadcasted_iota(jnp.int32, (128, 512), 0) + 128 * block
            place_k = lax.broadcasted_iota(jnp.int32, (128, 512), 1)
            same = (place_q >= length) == (place_k >= length)
            allowed = same & (place_k <= place_q)
            self.bias[rows, :] = jnp.where(allowed, 0.0, NEGATIVE)

        def normed(block, _):
            rows = tile(block, 64)
            values = self.tokens[rows, :].astype(jnp.float32)
            factor = lax.rsqrt(jnp.mean(values * values, axis=-1, keepdims=True) + NORM_EPS)
            gain = self.gain[0:1, :].astype(jnp.float32)
            self.hidden[rows, :] = (values * factor * gain).astype(jnp.bfloat16)
            place = lax.broadcasted_iota(jnp.int32, (64, 1024), 0) + 64 * block
            d_b = jnp.where(place < length, self.cotangent[rows, :].astype(jnp.float32), 0.0)
            self.d_b[rows, :] = d_b.astype(jnp.bfloat16)
            return 0

        lax.fori_loop(0, 8, normed, 0)
        self.turn(self.hidden, self.h_t)
        self.out("d_b")

    def turn(self, matrix, turned):
        def columns(n, _):
            at = tile(n, 128)
            turned[at, :] = matrix[:, at].astype(jnp.float32).T.astype(jnp.bfloat16)
            return 0

        lax.fori_loop(0, 8, columns, 0)

    def project(self, weight, result):
        def columns(n, _):
            at = tile(n, TILE)
            result[:, at] = dot(self.hidden[...], weight_columns(weight, at)).astype(jnp.bfloat16)
            return 0

        lax.fori_loop(0, 1024 // TILE, columns, 0)

    def attend(self, first, last):
        def pair(p, _):
            at = tile(p, 128)
            left = lax.broadcasted_iota(jnp.int32, (256, 128), 1) < HEAD
            for block in (0, 1):
                rows, seen = slice(256 * block, 256 * block + 256), slice(0, 256 * block + 256)
                query = self.query[rows, at].astype(jnp.float32) * SCORE_SCALE
                both = jnp.concatenate(
                    [jnp.where(left, query, 0.0), jnp.where(left, 0.0, query)], axis=0
                ).astype(jnp.bfloat16)
                bias = self.bias[rows, seen]
                scores = dot_nt(both, self.key[seen, at]) + jnp.concatenate([bias, bias], axis=0)
                top = jnp.max(scores, axis=-1, keepdims=True)
                expo = jnp.exp(scores - top)
                total = jnp.sum(expo, axis=-1, keepdims=True)
                probs = (expo * (1.0 / total)).astype(jnp.bfloat16)
                result = dot(probs, self.value[seen, at])
                self.attended[rows, at] = jnp.where(left, result[:256], result[256:]).astype(
                    jnp.bfloat16
                )
                lse = top + jnp.log(total)
                turned = jnp.where(left, lse[:256], lse[256:]).T
                self.lse[p, 0:1, rows] = turned[0:1]
                self.lse[p, 1:2, rows] = turned[HEAD : HEAD + 1]
            return 0

        lax.fori_loop(first, last, pair, 0)

    def project_out(self):
        def columns(n, _):
            at = tile(n, TILE)
            self.residual[:, at] = self.tokens[:, at].astype(jnp.float32) + dot(
                self.attended[...], weight_columns(self.w_out, at)
            )
            return 0

        lax.fori_loop(0, 1024 // TILE, columns, 0)

        def normed(block, _):
            rows = tile(block, 64)
            values = self.residual[rows, :]
            factor = lax.rsqrt(jnp.mean(values * values, axis=-1, keepdims=True) + NORM_EPS)
            gain = self.gain[8:9, :].astype(jnp.float32)
            self.h2[rows, :] = (values * factor * gain).astype(jnp.bfloat16)
            return 0

        lax.fori_loop(0, 8, normed, 0)
        self.turn(self.h2, self.h2_t)
        self.turn(self.attended, self.att_t)
        for name in ("query", "key", "value", "lse", "h_t", "h2_t", "att_t"):
            self.out(name)

    def grad_of_middle(self, start, size):
        at = pl.ds(start, size)
        self.d_up[:, at] = dot_nt(self.d_b[...], self.w_down[at, :]).astype(jnp.bfloat16)

    def feed_forward(self, start, size):
        at = pl.ds(start, size)
        low = jnp.bfloat16
        gate_w = weight_columns(self.w_gate, at)
        up_w = weight_columns(self.w_up, at)
        down_w = self.w_down[at, :]
        gate = dot(self.h2[...], gate_w)
        upward = dot(self.h2[...], up_w)
        grad_middle = self.d_up[:, at].astype(jnp.float32)
        sigma = 0.5 * jnp.tanh(0.5 * gate) + 0.5
        silu = gate * sigma
        mid = (silu * upward).astype(low)
        d_up = (grad_middle * silu).astype(low)
        d_gate = (grad_middle * upward * (sigma + silu - silu * sigma)).astype(low)
        self.mid[:, at] = mid
        self.d_up[:, at] = d_up
        self.d_gate[:, at] = d_gate
        for j in range(1024 // TILE):
            part = slice(TILE * j, TILE * j + TILE)
            mixed = dot(mid, down_w[:, part])
            grad = dot_nt(d_gate, gate_w[part, :]) + dot_nt(d_up, up_w[part, :])
            if start == 0:
                self.total[:, part] = mixed
                self.d_h2[:, part] = grad
            else:
                self.total[:, part] += mixed
                self.d_h2[:, part] += grad

    def flush(self, start, size):
        for name in ("mid", "d_gate", "d_up"):
            self.out(name, pl.ds(start, size))

    def finish(self):
        length = self.length[0, 0]
        self.g_ffn[...] = jnp.zeros_like(self.g_ffn)

        def rows_of(block, _):
            rows = tile(block, 64)
            place = lax.broadcasted_iota(jnp.int32, (64, 1024), 0) + 64 * block
            residual = self.residual[rows, :]
            mixed = jnp.where(place < length, residual + self.total[rows, :], 0.0)
            self.mixed[rows, :] = mixed.astype(jnp.bfloat16)
            factor = lax.rsqrt(jnp.mean(residual * residual, axis=-1, keepdims=True) + NORM_EPS)
            normed = residual * factor
            grad = self.d_h2[rows, :]
            self.g_ffn[...] += jnp.sum((grad * normed).reshape(8, 8, 1024), axis=0)
            grad_normed = grad * self.gain[8:9, :].astype(jnp.float32)
            grad_out = jnp.where(place < length, self.cotangent[rows, :].astype(jnp.float32), 0.0)
            mean = jnp.mean(grad_normed * normed, axis=-1, keepdims=True)
            d_res = grad_out + factor * (grad_normed - normed * mean)
            self.d_res[rows, :] = d_res
            self.d_proj[rows, :] = d_res.astype(jnp.bfloat16)
            return 0

        lax.fori_loop(0, 8, rows_of, 0)
        for name in ("mixed", "d_res", "d_proj", "g_ffn", "gain"):
            self.out(name)


FORWARD_OUTS = (
    ("mixed", (512, 1024), jnp.bfloat16),
    ("query", (512, 1024), jnp.bfloat16),
    ("key", (512, 1024), jnp.bfloat16),
    ("value", (512, 1024), jnp.bfloat16),
    ("lse", (8, 8, 512), jnp.float32),
    ("h_t", (1024, 512), jnp.bfloat16),
    ("h2_t", (1024, 512), jnp.bfloat16),
    ("att_t", (1024, 512), jnp.bfloat16),
    ("d_b", (512, 1024), jnp.bfloat16),
    ("mid", (512, 2816), jnp.bfloat16),
    ("d_gate", (512, 2816), jnp.bfloat16),
    ("d_up", (512, 2816), jnp.bfloat16),
    ("d_res", (512, 1024), jnp.float32),
    ("d_proj", (512, 1024), jnp.bfloat16),
    ("g_ffn", (8, 1024), jnp.float32),
    ("gain", (16, 1024), jnp.bfloat16),
)
FORWARD_OWN = (
    ("hidden", (512, 1024), jnp.bfloat16),
    ("attended", (512, 1024), jnp.bfloat16),
    ("residual", (512, 1024), jnp.float32),
    ("h2", (512, 1024), jnp.bfloat16),
    ("d_h2", (512, 1024), jnp.float32),
    ("bias", (512, 512), jnp.float32),
    ("total", (512, 1024), jnp.float32),
)
OUT_COPIES = len(FORWARD_OUTS) - 3 + 3 * len(FF_CHUNKS)
KEPT = (QUERY, KEY, VALUE, OUT)


def share_shape(columns):
    return (352, 1024) if columns is None else (2, 64, columns)


def forward_kernel(items, *refs):
    refs = list(refs)

    def take(n):
        taken = refs[:n]
        del refs[:n]
        return taken

    shares = take(7)
    gain_attn, gain_ffn, tokens, cotangent, length = take(5)
    kept = take(len(KEPT))
    names = [name for name, _, _ in FORWARD_OUTS]
    outs = dict(zip(names, take(len(names))))
    full = take(7)
    full_gains, gains = take(2)
    own_names = names + [name for name, _, _ in FORWARD_OWN]
    state = dict(zip(own_names, take(len(own_names))))
    send_sems, recv_sems, own_sems, keep_sems, out_sems = refs
    outgoing = []

    def put(name, columns=None):
        source, target = state[name], outs[name]
        if columns is not None:
            source, target = source.at[:, columns], target.at[:, columns]
        outgoing.append(pltpu.make_async_copy(source, target, out_sems.at[len(outgoing)]))
        outgoing[-1].start()

    z, y, x, c = place()
    far = [lax.rem(z + k, 4) for k in range(4)]
    back = [lax.rem(z + 4 - k, 4) for k in range(4)]
    x_other, y_other, c_other = (
        device(z, y, 1 - x, c),
        device(z, 1 - y, x, c),
        device(z, y, x, 1 - c),
    )
    greet()
    await_partners()
    wires = Wires(send_sems, recv_sems)
    own = [
        pltpu.make_async_copy(share, whole.at[z, y], own_sems.at[i])
        for i, (share, whole) in enumerate(zip(shares, full))
    ]
    own_gains = pltpu.make_async_copy(gains, full_gains.at[z, y], own_sems.at[7])
    keep = [
        pltpu.make_async_copy(full[w], kept[n], keep_sems.at[n]) for n, w in enumerate(KEPT)
    ]
    gains[...] = jnp.where(
        lax.broadcasted_iota(jnp.int32, (16, 128), 0) < 8,
        jnp.broadcast_to(gain_attn[...].astype(jnp.float32), (16, 128)),
        jnp.broadcast_to(gain_ffn[...].astype(jnp.float32), (16, 128)),
    ).astype(jnp.bfloat16)
    own_gains.start()
    gain_slot = GATHER_SLOTS * len(items)
    for k in (1, 2, 3):
        wires.send(gain_slot + k, gains, full_gains.at[z, y], device(far[k], y, x, c))
    for copy in own:
        copy.start()

    def slot(i, k):
        return GATHER_SLOTS * i + k

    def along_z(i):
        item = items[i]
        share, whole = shares[item.weight], full[item.weight]
        for k in (1, 2, 3):
            if item.no_x:
                source, target = item.half(share, (), c), item.half(whole, (z, y), c)
            else:
                source, target = item.quarter(share, (), c, x), item.quarter(whole, (z, y), c, x)
            wires.send(slot(i, k), source, target, device(far[k], y, x, c))

    own_done = set()

    def first_hop(i):
        item = items[i]
        whole = full[item.weight]
        if item.weight not in own_done:
            own[item.weight].wait()
            own_done.add(item.weight)
        for k in (1, 2, 3):
            if item.no_x:
                block = item.half(whole, (back[k], y), c)
                wires.arrived(slot(i, k), block)
                wires.send(slot(i, 7 + k), block, block, c_other)
            else:
                block = item.quarter(whole, (back[k], y), c, x)
                wires.arrived(slot(i, k), block)
                wires.send(slot(i, 3 + k), block, block, x_other)
        if item.no_x:
            block = item.half(whole, (ALL, y), c)
        else:
            block = item.quarter(whole, (ALL, y), c, x)
        wires.send(slot(i, 7), block, block, y_other)

    def second_hop(i):
        item = items[i]
        whole = full[item.weight]
        if item.no_x:
            block = item.half(whole, (ALL, 1 - y), c)
            wires.arrived(slot(i, 7), block)
            wires.send(slot(i, 11), block, block, c_other)
            return
        block = item.quarter(whole, (ALL, 1 - y), c, x)
        wires.arrived(slot(i, 7), block)
        wires.send(slot(i, 0), block, block, x_other)
        for k in (1, 2, 3):
            wires.arrived(slot(i, 3 + k), item.quarter(whole, (back[k], y), c, 1 - x))
        for k in (1, 2, 3):
            block = item.half(whole, (back[k], y), c)
            wires.send(slot(i, 7 + k), block, block, c_other)

    def last_hop(i):
        item = items[i]
        whole = full[item.weight]
        if not item.no_x:
            block = item.half(whole, (ALL, 1 - y), c)
            wires.arrived(slot(i, 0), item.quarter(whole, (ALL, 1 - y), c, 1 - x))
            wires.send(slot(i, 11), block, block, c_other)

    def complete(i):
        item = items[i]
        whole = full[item.weight]
        for k in (1, 2, 3):
            wires.arrived(slot(i, 7 + k), item.half(whole, (back[k], y), 1 - c))
        wires.arrived(slot(i, 11), item.half(whole, (ALL, 1 - y), 1 - c))

    def retire(i):
        wires.finish(lambda slot: slot // GATHER_SLOTS == i)

    step_of = Forward(
        dict(
            state,
            out=put,
            tokens=tokens,
            cotangent=cotangent,
            length=length,
            gains=full_gains,
            w_out=full[OUT],
            w_gate=full[GATE],
            w_up=full[UP],
            w_down=full[DOWN].reshape(2816, 1024),
        )
    )
    last_of = {item.weight: i for i, item in enumerate(items)}
    tasks = [(-1, 3, step_of.prepare)]
    for n, name in enumerate(("query", "key", "value")):
        tasks.append((last_of[n], 2, partial(step_of.project, full[n], state[name])))
    tasks += [(last_of[VALUE], 3, partial(step_of.attend, p, p + 2)) for p in (0, 2, 4, 6)]
    tasks.append((last_of[OUT], 3, step_of.project_out))
    for tile_of in pieces(2816, TILE):
        tasks.append((last_of[DOWN], 1, partial(step_of.grad_of_middle, *tile_of)))
    for start, size in FF_CHUNKS:
        there = max(
            i for i, item in enumerate(items) if item.weight == UP and item.start == start
        )
        for at, width in pieces(size, TILE):
            tasks.append((there, 5, partial(step_of.feed_forward, start + at, width)))
        tasks.append((there, 0, partial(step_of.flush, start, size)))

    ahead = 3
    for i in range(min(ahead, len(items))):
        along_z(i)
    own_gains.wait()
    for k in (1, 2, 3):
        wires.arrived(gain_slot + k, full_gains.at[back[k], y])
    wires.send(gain_slot, full_gains.at[:, y], full_gains.at[:, y], y_other)
    stages = (retire, complete, last_hop, second_hop, first_hop)
    lates = (3 * LAG, 3 * LAG - 1, 2 * LAG, LAG, 0)
    for step in range(len(items) + 3 * LAG):
        for late, stage in zip(lates, stages):
            if 0 <= step - late < len(items):
                stage(step - late)
        if step + ahead < len(items):
            along_z(step + ahead)
        if step == 0:
            wires.arrived(gain_slot, full_gains.at[:, 1 - y])
        there = step - lates[1]
        for n, w in enumerate(KEPT):
            if there == last_of[w]:
                keep[n].start()
        spent = 0
        while tasks and tasks[0][0] <= there and spent < 6:
            _, cost, task = tasks.pop(0)
            task()
            spent += cost
    for _, _, task in tasks:
        task()
    step_of.finish()
    for copy in keep + outgoing:
        copy.wait()
    wires.finish()


def forward(tokens, cotangent, lengths, weights, gains):
    items = gather_items()
    shares = [w.reshape(share_shape(n)) for w, n in zip(weights, COLUMNS)]
    wholes = [(4, 2) + share_shape(n) for n in COLUMNS]
    shapes = [jax.ShapeDtypeStruct(wholes[w], jnp.bfloat16) for w in KEPT]
    shapes += [jax.ShapeDtypeStruct(shape, dtype) for _, shape, dtype in FORWARD_OUTS]
    count = GATHER_SLOTS * len(items) + 4
    anywhere = pl.BlockSpec(memory_space=pl.ANY)
    in_vmem = pl.BlockSpec(memory_space=pltpu.VMEM)
    out = pl.pallas_call(
        partial(forward_kernel, items),
        out_shape=shapes,
        in_specs=[anywhere] * 7
        + [in_vmem] * 4
        + [pl.BlockSpec(memory_space=pltpu.SMEM)],
        out_specs=[anywhere] * len(shapes),
        scratch_shapes=[pltpu.VMEM(shape, jnp.bfloat16) for shape in wholes]
        + [pltpu.VMEM((4, 2, 16, 128), jnp.bfloat16), pltpu.VMEM((16, 128), jnp.bfloat16)]
        + [pltpu.VMEM(shape, dtype) for _, shape, dtype in FORWARD_OUTS + FORWARD_OWN]
        + [
            pltpu.SemaphoreType.DMA((count,)),
            pltpu.SemaphoreType.DMA((count,)),
            pltpu.SemaphoreType.DMA((8,)),
            pltpu.SemaphoreType.DMA((len(KEPT),)),
            pltpu.SemaphoreType.DMA((OUT_COPIES,)),
        ],
        compiler_params=pltpu.CompilerParams(
            collective_id=0, has_side_effects=True, vmem_limit_bytes=63 * MIB
        ),
        name="gather_forward",
    )(*shares, *[g.reshape(1, 128) for g in gains], tokens, cotangent, lengths)
    return out[: len(KEPT)], dict(zip([name for name, _, _ in FORWARD_OUTS], out[len(KEPT) :]))


SUM_SLOTS = 10
RING = 4


class Share:
    def __init__(self, weight, start, size, x_first):
        self.weight, self.start, self.size, self.x_first = weight, start, size, x_first
        self.tall = weight == DOWN
        self.width = 128 if self.tall else size // 2
        self.block = (352 if self.tall else 64, self.width)

    def columns(self, c, x):
        start = c * 512 + x * 256 + self.start if self.tall else self.start + c * self.width
        return pl.ds(pl.multiple_of(start, 128), self.width)

    def quarter(self, sums, c, x):
        if self.tall:
            return sums.at[c, x, self.start // 128]
        return sums.at[x, :, self.columns(c, x)]

    def half(self, sums, c):
        if self.tall:
            return sums.at[c, :, self.start // 128]
        return sums.at[:, :, self.columns(c, 0)]


def share_items():
    order = [(GATE, 2048, 768, True), (DOWN, 0, 128, False), (DOWN, 128, 128, True)]
    order += [(GATE, 0, 1024, False), (GATE, 1024, 1024, True)]
    order += [(UP, 0, 1024, True), (UP, 1024, 1024, False), (UP, 2048, 768, False)]
    order += [(OUT, 0, 1024, True), (QUERY, 0, 1024, False), (KEY, 0, 1024, True)]
    order += [(VALUE, 0, 768, True), (VALUE, 768, 256, False)]
    return [Share(*item) for item in order]


def plus(left, right):
    return left + right


def dot_tn(left, right):
    return lax.dot_general(
        left, right, (((0,), (0,)), ((), ())), preferred_element_type=jnp.float32
    )


BACKWARD_IN = (
    "query",
    "key",
    "value",
    "lse",
    "h_t",
    "h2_t",
    "att_t",
    "d_b",
    "d_res",
    "d_proj",
    "g_ffn",
    "gain",
)


class Backward:
    def __init__(self, refs):
        self.__dict__.update(refs)

    def prepare(self):
        length = self.length[0, 0]
        for block in range(4):
            rows = slice(128 * block, 128 * block + 128)
            place_k = lax.broadcasted_iota(jnp.int32, (128, 512), 0) + 128 * block
            place_q = lax.broadcasted_iota(jnp.int32, (128, 512), 1)
            same = (place_q >= length) == (place_k >= length)
            allowed = same & (place_k <= place_q)
            self.bias[rows, :] = jnp.where(allowed, 0.0, NEGATIVE)

    def multiply(self, left_t, right, item, target, core):
        columns = item.columns(core, 0)

        def rows(m, _):
            product = dot(left_t[tile(m, 256), :], right[:, columns]).astype(jnp.bfloat16)
            product = product.reshape(2, 2, 64, item.width)
            for xx in (0, 1):
                target[xx, m] = product[:, xx]
            return 0

        lax.fori_loop(0, 4, rows, 0)

    def multiply_tall(self, left, right, groups):
        def rows(m, _):
            at = tile(m, 256)
            turned = left[:, at].T
            for columns, targets in groups:
                product = dot(turned, right[:, columns]).astype(jnp.bfloat16)
                for n, (target, xx) in enumerate(targets):
                    target.reshape(2, 2816, 128)[xx, at, :] = product[:, 128 * n : 128 * n + 128]
            return 0

        lax.fori_loop(0, 11, rows, 0)

    def attend_back(self, first, last):
        low = jnp.bfloat16

        def pair(p, _):
            at = tile(p, 128)
            wo_rows = self.w_rows[p].reshape(128, 1024)
            grad = dot_nt(self.d_proj[...], wo_rows).astype(low)
            query = (self.query[:, at].astype(jnp.float32) * SCORE_SCALE).astype(low)
            key, value = self.key[:, at], self.value[:, at]
            left = lax.broadcasted_iota(jnp.int32, (512, 128), 1) < HEAD
            none = jnp.zeros((512, 128), low)
            sides = [
                [jnp.where(side, v, none) for v in (query, key, value, grad)]
                for side in (left, ~left)
            ]
            grad_key, grad_value = [None, None], [None, None]
            for block in (0, 1):
                rows, seen = slice(256 * block, 256 * block + 256), slice(0, 256 * block + 256)
                grad_query = None
                parts_key, parts_value = None, None
                for n, (own_query, own_key, own_value, own_grad) in enumerate(sides):
                    self.d_in[seen, 0:256] = dot_nt(own_key[seen], query[rows])
                    self.d_in[seen, 256:512] = dot_nt(own_value[seen], grad[rows])
                    self.back_rows(p, n, rows, 256 * block + 256)
                    grad_scores, probs = self.grad_scores[seen, :], self.probs[seen, :]
                    part_query = dot_tn(grad_scores, own_key[seen])
                    part_key = dot(grad_scores, own_query[rows])
                    part_value = dot(probs, own_grad[rows])
                    if n == 0:
                        grad_query, parts_key, parts_value = part_query, part_key, part_value
                    else:
                        grad_query += part_query
                        parts_key += part_key
                        parts_value += part_value
                self.query[rows, at] = (grad_query * SCORE_SCALE).astype(low)
                if block == 0:
                    grad_key[0], grad_value[0] = parts_key, parts_value
                else:
                    grad_key = [grad_key[0] + parts_key[:256], parts_key[256:]]
                    grad_value = [grad_value[0] + parts_value[:256], parts_value[256:]]
            for block in (0, 1):
                rows = slice(256 * block, 256 * block + 256)
                self.key[rows, at] = grad_key[block].astype(low)
                self.value[rows, at] = grad_value[block].astype(low)
            return 0

        lax.fori_loop(first, last, pair, 0)

    def back_rows(self, p, n, rows, count):
        low = jnp.bfloat16
        held = self.d_in
        lse = self.lse[p, n : n + 1, rows]

        def first_pass(r, centre):
            keys = tile(r, 64)
            probs = jnp.exp(held[keys, 0:256] + self.bias[keys, rows] - lse)
            held[keys, 0:256] = probs
            self.probs[keys, :] = probs.astype(low)
            return centre + jnp.sum((held[keys, 256:512] * probs).reshape(8, 8, 256), axis=0)

        centre = lax.fori_loop(0, count // 64, first_pass, jnp.zeros((8, 256), jnp.float32), unroll=2)
        centre = jnp.sum(centre, axis=0, keepdims=True)

        def second_pass(r, _):
            keys = tile(r, 64)
            grad = held[keys, 0:256] * (held[keys, 256:512] - centre)
            self.grad_scores[keys, :] = grad.astype(low)
            return 0

        lax.fori_loop(0, count // 64, second_pass, 0, unroll=2)

    def grad_hidden(self, t):
        at = pl.ds(256 * t, 256)
        total = None
        for n, grad in enumerate((self.query, self.key, self.value)):
            part = dot_nt(grad[...], self.w_rows[2 * n : 2 * n + 2].reshape(256, 1024))
            total = part if total is None else total + part
        self.d_in[:, at] = total

    def finish(self):
        self.gain_total[...] = jnp.zeros_like(self.gain_total)

        def rows_of(block, _):
            rows = tile(block, 64)
            values = self.tokens[rows, :].astype(jnp.float32)
            factor = lax.rsqrt(jnp.mean(values * values, axis=-1, keepdims=True) + NORM_EPS)
            normed = values * factor
            grad = self.d_in[rows, :]
            self.gain_total[...] += jnp.sum((grad * normed).reshape(8, 8, 1024), axis=0)
            grad_normed = grad * self.gain[0:1, :].astype(jnp.float32)
            mean = jnp.mean(grad_normed * normed, axis=-1, keepdims=True)
            self.d_in[rows, :] = self.d_res[rows, :] + factor * (
                grad_normed - normed * mean
            )
            return 0

        lax.fori_loop(0, 8, rows_of, 0)
        self.gain_lines[...] = jnp.zeros_like(self.gain_lines)
        lines = [jnp.sum(v[...], axis=0, keepdims=True) for v in (self.gain_total, self.g_ffn)]
        for s in range(8):
            for n, line in enumerate(lines):
                self.gain_lines[s // 2, s % 2, n : n + 1] = line[:, 128 * s : 128 * s + 128]


def backward_kernel(items, *refs):
    refs = list(refs)

    def take(n):
        taken = refs[:n]
        del refs[:n]
        return taken

    kept = take(len(KEPT))
    middle_in, grad_gate_in, grad_up_in = take(3)
    saved_in = dict(zip(BACKWARD_IN, take(len(BACKWARD_IN))))
    tokens_in, length = take(2)
    sums = take(7)
    gain_sums, input_grad_out = take(2)
    saved = dict(zip(BACKWARD_IN, take(len(BACKWARD_IN))))
    d_in, wide, w_rows, bias, probs, grad_scores, gain_total, gain_lines = take(8)
    mine, from_first, from_second, from_z = (take(len(items)) for _ in range(4))
    ring, tall_ring = take(RING), take(2)
    outbox, tall_outbox = take(2), take(2)
    gain_core, gain_x, gain_y, gain_z = take(4)
    send_sems, recv_sems, load_sems, credit = refs
    z, y, x, c = place()
    far = [lax.rem(z + k, 4) for k in range(4)]
    back = [lax.rem(z + 4 - k, 4) for k in range(4)]
    x_other, y_other, c_other = (
        device(z, y, 1 - x, c),
        device(z, 1 - y, x, c),
        device(z, y, x, 1 - c),
    )
    loads = {}

    def load(name, source, target):
        loads[name] = pltpu.make_async_copy(source, target, load_sems.at[len(loads)])
        loads[name].start()

    waited = set()

    def loaded(*names):
        for name in names:
            if name not in waited:
                loads[name].wait()
                waited.add(name)

    load("d_gate", grad_gate_in, wide.at[1])
    load("h2_t", saved_in["h2_t"], saved["h2_t"])
    load("mid", middle_in, wide.at[0])
    load("d_b", saved_in["d_b"], saved["d_b"])
    load("wo_rows", kept[OUT].reshape(8, 2, 64, 1024), w_rows)
    for name in BACKWARD_IN:
        if name not in loads:
            load(name, saved_in[name], saved[name])
    greet()
    wires = Wires(send_sems, recv_sems)
    work = Backward(
        dict(
            saved,
            tokens=saved["d_b"],
            length=length,
            w_rows=w_rows,
            probs=probs,
            grad_scores=grad_scores,
            bias=bias,
            d_in=d_in,
            gain_total=gain_total,
            gain_lines=gain_lines,
        )
    )
    tall_items = [i for i, item in enumerate(items) if item.tall]
    wide_items = [i for i, item in enumerate(items) if not item.tall]

    def slot(i, k):
        return SUM_SLOTS * i + k

    def core_slots(i):
        return (slot(i, 0), slot(i, 8))

    def from_core(i):
        if items[i].tall:
            return tall_ring[tall_items.index(i)]
        return ring[wide_items.index(i) % RING].at[..., : items[i].width]

    def produce(i):
        item = items[i]
        if item.tall:
            number = tall_items.index(i)
            if number == 0:
                loaded("mid", "d_b")
                groups = []
                for core, boxes in ((1 - c, tall_outbox), (c, [mine[j] for j in tall_items])):
                    columns = pl.ds(pl.multiple_of(512 * core, 512), 512)
                    groups.append((columns, [(boxes[j], xx) for xx in (0, 1) for j in (0, 1)]))
                work.multiply_tall(wide.at[0], saved["d_b"], groups)
                load("d_up", grad_up_in, wide.at[0])
                load("tokens", tokens_in, saved["d_b"])
            box = tall_outbox[number]
        else:
            number = wide_items.index(i)
            if number >= 2:
                wires.finish(lambda s: s in core_slots(wide_items[number - 2]))
            box = outbox[number % 2].at[..., : item.width]
            left, right, names = {
                GATE: (saved["h2_t"], wide.at[1], ("h2_t", "d_gate")),
                UP: (saved["h2_t"], wide.at[0], ("d_up",)),
                OUT: (saved["att_t"], saved["d_proj"], ("att_t", "d_proj")),
                QUERY: (saved["h_t"], saved["query"], ("h_t",)),
                KEY: (saved["h_t"], saved["key"], ()),
                VALUE: (saved["h_t"], saved["value"], ()),
            }[item.weight]
            loaded(*names)
            multiply = partial(work.multiply, left, right, item)
            if number >= RING:
                pl.semaphore_wait(credit, 1)
            multiply(box, 1 - c)
            if i == 0:
                multiply(mine[i], c)
        if i == 0:
            await_partners()
        for xx in (0, 1):
            wires.send(core_slots(i)[xx], box.at[xx], from_core(i).at[xx], c_other)
        if i > 0 and not item.tall:
            multiply(mine[i], c)

    def first_hop(i):
        item, own, other = items[i], mine[i], from_core(i)
        for xx in (0, 1):
            wires.arrived(core_slots(i)[xx], other.at[xx])

        def add(at, _):
            for xx in (0, 1):
                for yy in (0, 1):
                    own[xx, at, yy] = plus(own[xx, at, yy], other[xx, at, yy])
            return 0

        lax.fori_loop(0, 4, add, 0)
        if not item.tall and wide_items.index(i) + RING < len(wide_items):
            pl.semaphore_signal(credit, inc=1, device_id=c_other, device_id_type=MESH)
        if item.x_first:
            wires.send(slot(i, 1), own.at[1 - x], from_first[i], x_other)
        else:
            wires.send(slot(i, 1), own.at[:, :, 1 - y], from_first[i], y_other)

    def second_hop(i):
        item, own, other = items[i], mine[i], from_first[i]
        wires.arrived(slot(i, 1), other)

        def add(at, _):
            for side in (0, 1):
                if item.x_first:
                    own[x, at, side] = plus(own[x, at, side], other[at, side])
                else:
                    own[side, at, y] = plus(own[side, at, y], other[side, at])
            return 0

        lax.fori_loop(0, 4, add, 0)
        if item.x_first:
            wires.send(slot(i, 2), own.at[x, :, 1 - y], from_second[i], y_other)
        else:
            to_z(i, lambda k: own.at[:, far[k], y])

    def to_z(i, block):
        for k in (1, 2, 3):
            wires.send(slot(i, 2 + k), block(k), from_z[i].at[k - 1], device(far[k], y, x, c))

    def z_total(i, own_part):
        total = own_part.astype(jnp.float32)
        for k in (1, 2, 3):
            wires.arrived(slot(i, 2 + k), from_z[i].at[k - 1])
            total += from_z[i][k - 1].astype(jnp.float32)
        return total.astype(jnp.bfloat16)

    def third_hop(i):
        item, own, other = items[i], mine[i], from_second[i]
        if not item.x_first:
            own[:, z, y] = z_total(i, own[:, z, y])
            wires.send(slot(i, 2), own.at[:, z, y], other, x_other)
            return
        wires.arrived(slot(i, 2), other)

        def add(at, _):
            own[x, at, y] = plus(own[x, at, y], other[at])
            return 0

        lax.fori_loop(0, 4, add, 0)
        to_z(i, lambda k: own.at[x, far[k], y])

    def fourth_hop(i):
        item, own = items[i], mine[i]
        if not item.x_first:
            wires.arrived(slot(i, 2), from_second[i])
            block = item.half(sums[item.weight], c)
            block[...] = plus(own[:, z, y], from_second[i][...])
            wires.send(slot(i, 7), block, block, c_other)
            return
        block = item.quarter(sums[item.weight], c, x)
        block[...] = z_total(i, own[x, z, y])
        wires.send(slot(i, 6), block, block, x_other)

    def to_sibling(i):
        item = items[i]
        if item.x_first:
            wires.arrived(slot(i, 6), item.quarter(sums[item.weight], c, 1 - x))
            block = item.half(sums[item.weight], c)
            wires.send(slot(i, 7), block, block, c_other)

    def complete(i):
        item = items[i]
        wires.arrived(slot(i, 7), item.half(sums[item.weight], 1 - c))
        wires.finish(lambda s: s // SUM_SLOTS == i)

    base = SUM_SLOTS * len(items)

    def gains_one():
        wires.send(base, gain_lines, gain_core, c_other)

    def gains_two():
        wires.arrived(base, gain_core)
        gain_core[...] = gain_lines[...] + gain_core[...]
        wires.send(base + 1, gain_core, gain_x, x_other)

    def gains_three():
        wires.arrived(base + 1, gain_x)
        gain_x[...] = gain_core[...] + gain_x[...]
        wires.send(base + 2, gain_x.at[:, 1 - y], gain_y, y_other)

    def gains_four():
        wires.arrived(base + 2, gain_y)
        gain_y[...] = gain_x[:, y] + gain_y[...]
        for k in (1, 2, 3):
            wires.send(base + 2 + k, gain_y.at[far[k]], gain_z.at[z], device(far[k], y, x, c))
        gain_z[z] = gain_y[z]

    def gains_five():
        for k in (1, 2, 3):
            wires.arrived(base + 2 + k, gain_z.at[back[k]])
        gain_sums[...] = (gain_z[0] + gain_z[1]) + (gain_z[2] + gain_z[3])

    def fetch_rows(t):
        for n in range(3):
            load(("rows", n, t), kept[n].at[t], w_rows.at[2 * n : 2 * n + 2])

    def attend_back(p):
        if p == 0:
            loaded("query", "key", "value", "lse", "d_proj", "wo_rows")
        work.attend_back(p, p + 1)
        if p == 7:
            fetch_rows(0)

    def grad_hidden(t):
        loaded(*[("rows", n, t) for n in range(3)])
        work.grad_hidden(t)
        if t < 3:
            fetch_rows(t + 1)

    def finish():
        loaded("tokens", "d_res", "g_ffn", "gain")
        work.finish()
        load("d_in", d_in, input_grad_out)
        gains_one()

    beside = {}
    for p in range(8):
        beside.setdefault(1 + p, []).append(partial(attend_back, p))
    for t in range(4):
        beside.setdefault(9 + t // 2, []).append(partial(grad_hidden, t))
    beside.setdefault(11, []).append(finish)
    for n, task in enumerate((gains_two, gains_three, gains_four, gains_five)):
        beside.setdefault(13 + 2 * n, []).append(task)

    stages = (complete, to_sibling, fourth_hop, third_hop, second_hop, first_hop, produce)
    lates = [(12, 10, 8, 6, 4, 2, 0)] * (len(items) - 4)
    lates += [(9, 8, 7, 6, 4, 2, 0), (8, 7, 6, 5, 4, 2, 0), (7, 6, 5, 4, 3, 2, 0), (6, 5, 4, 3, 2, 1, 0)]
    work.prepare()
    for step in range(max(i + late[0] for i, late in enumerate(lates)) + 1):
        for number, stage in enumerate(stages):
            for i, late in enumerate(lates):
                if i + late[number] == step:
                    stage(i)
        for task in beside.get(step, []):
            task()
    loaded("d_in")
    wires.finish()


def backward(tokens, lengths, kept, saved):
    items = share_items()
    low, wide = jnp.bfloat16, jnp.float32
    dtypes = {name: (shape, dtype) for name, shape, dtype in FORWARD_OUTS}
    shapes = [
        jax.ShapeDtypeStruct((2, 2, 2, 352, 128) if n is None else (2, 64, n), low) for n in COLUMNS
    ]
    shapes += [jax.ShapeDtypeStruct((8, 128), wide), jax.ShapeDtypeStruct((512, 1024), wide)]
    count = SUM_SLOTS * len(items) + 6
    anywhere = pl.BlockSpec(memory_space=pl.ANY)
    in_vmem = pl.BlockSpec(memory_space=pltpu.VMEM)
    n_loads = 6 + len(BACKWARD_IN) + 12

    def buffers(lead_of):
        return [pltpu.VMEM(lead_of(item) + item.block, low) for item in items]

    out = pl.pallas_call(
        partial(backward_kernel, items),
        out_shape=shapes,
        in_specs=[anywhere] * (len(KEPT) + 3 + len(BACKWARD_IN) + 1)
        + [pl.BlockSpec(memory_space=pltpu.SMEM)],
        out_specs=[in_vmem] * 8 + [anywhere],
        scratch_shapes=[pltpu.VMEM(*dtypes[name]) for name in BACKWARD_IN]
        + [
            pltpu.VMEM((512, 1024), wide),
            pltpu.VMEM((2, 512, 2816), low),
            pltpu.VMEM((8, 2, 64, 1024), low),
            pltpu.VMEM((512, 512), wide),
            pltpu.VMEM((512, 256), low),
            pltpu.VMEM((512, 256), low),
            pltpu.VMEM((8, 1024), wide),
            pltpu.VMEM((4, 2, 8, 128), wide),
        ]
        + buffers(lambda item: (2, 4, 2))
        + buffers(lambda item: (4, 2) if item.x_first else (2, 4))
        + buffers(lambda item: (4,) if item.x_first else (2,))
        + buffers(lambda item: (3,) if item.x_first else (3, 2))
        + [pltpu.VMEM((2, 4, 2, 64, 512), low)] * RING
        + [pltpu.VMEM((2, 4, 2, 352, 128), low)] * 2
        + [pltpu.VMEM((2, 4, 2, 64, 512), low)] * 2
        + [pltpu.VMEM((2, 4, 2, 352, 128), low)] * 2
        + [
            pltpu.VMEM((4, 2, 8, 128), wide),
            pltpu.VMEM((4, 2, 8, 128), wide),
            pltpu.VMEM((4, 8, 128), wide),
            pltpu.VMEM((4, 8, 128), wide),
            pltpu.SemaphoreType.DMA((count,)),
            pltpu.SemaphoreType.DMA((count,)),
            pltpu.SemaphoreType.DMA((n_loads,)),
            pltpu.SemaphoreType.REGULAR,
        ],
        compiler_params=pltpu.CompilerParams(
            collective_id=1, has_side_effects=True, vmem_limit_bytes=63 * MIB
        ),
        name="backward_sum",
    )(
        *kept,
        saved["mid"],
        saved["d_gate"],
        saved["d_up"],
        *[saved[name] for name in BACKWARD_IN],
        tokens,
        lengths,
    )
    return out[:7], out[7], out[8]


def unpack_kernel(*refs):
    blocks, (gain_sums, mixed, d_in) = refs[:7], refs[7:10]
    sums, (gain_attn, gain_ffn, mixed_out, input_out) = refs[10:17], refs[17:21]
    held, wide = refs[21:28], refs[28:35]
    mixed_held, input_held, in_sems, out_sems = refs[35:]
    sources = (d_in, mixed, *blocks)
    places = (input_held, mixed_held, *held)
    results = (input_held, mixed_held, *wide)
    targets = (input_out, mixed_out, *sums)
    ins = [pltpu.make_async_copy(a, b, in_sems.at[n]) for n, (a, b) in enumerate(zip(sources, places))]
    outs = [pltpu.make_async_copy(a, b, out_sems.at[n]) for n, (a, b) in enumerate(zip(results, targets))]
    order = (6, 7, 8, 2, 3, 4, 5, 0, 1)
    for n in order:
        ins[n].start()
    for n in order:
        ins[n].wait()
        if n == 8:
            for b in range(8):
                wide[6][:, 128 * b : 128 * b + 128] = held[6][b // 4, b // 2 % 2, b % 2].astype(
                    jnp.float32
                )
        elif n >= 2:
            wide[n - 2][...] = held[n - 2][...].astype(jnp.float32)
        outs[n].start()
    gain_attn[...] = gain_sums[0:1]
    gain_ffn[...] = gain_sums[1:2]
    for n in order:
        outs[n].wait()


def unpack(blocks, gain_sums, mixed, d_in):
    wide = jnp.float32
    anywhere = pl.BlockSpec(memory_space=pl.ANY)
    in_vmem = pl.BlockSpec(memory_space=pltpu.VMEM)
    shapes = [
        jax.ShapeDtypeStruct((352, 1024) if n is None else (2, 64, n), wide) for n in COLUMNS
    ]
    held = [pltpu.VMEM(b.shape, b.dtype) for b in blocks]
    held += [pltpu.VMEM(v.shape, wide) for v in shapes]
    held += [pltpu.VMEM(v.shape, v.dtype) for v in (mixed, d_in)]
    shapes += [jax.ShapeDtypeStruct((1, 128), wide)] * 2
    shapes += [jax.ShapeDtypeStruct(v.shape, v.dtype) for v in (mixed, d_in)]
    out = pl.pallas_call(
        unpack_kernel,
        out_shape=shapes,
        in_specs=[anywhere] * 7 + [in_vmem] + [anywhere] * 2,
        out_specs=[anywhere] * 7 + [in_vmem] * 2 + [anywhere] * 2,
        scratch_shapes=held + [pltpu.SemaphoreType.DMA((9,)), pltpu.SemaphoreType.DMA((9,))],
        compiler_params=pltpu.CompilerParams(vmem_limit_bytes=62 * MIB),
        name="unpack",
    )(*blocks, gain_sums, mixed, d_in)
    sums = [s.reshape(-1, s.shape[-1]) for s in out[:7]]
    return sums, [g.reshape(128) for g in out[7:9]], out[9], out[10]


def gather_plain(weights, gains):
    everything = (*weights, *gains)
    whole = [lax.all_gather(v, "dp", axis=0, tiled=True) for v in everything]
    return whole[: len(weights)], whole[len(weights) :]


def sum_plain(grads, gain_grads):
    shares = [
        lax.psum_scatter(g.astype(jnp.float32), "dp", scatter_dimension=0, tiled=True)
        for g in (*grads, *gain_grads)
    ]
    sums = [lax.psum(s, ("rep", "cores")) for s in shares]
    return sums[: len(grads)], sums[len(grads) :]


def on_any_device(
    tokens,
    norm_attn,
    w_query,
    w_key,
    w_value,
    w_out,
    norm_ffn,
    w_gate,
    w_up,
    w_down,
    lengths,
    cotangent,
):
    rows = tokens.shape[0]
    low = jnp.bfloat16
    allowed, valid = masks(lengths, rows)
    whole, gains = gather_plain(
        (w_query, w_key, w_value, w_out, w_gate, w_up, w_down), (norm_attn, norm_ffn)
    )
    full_query, full_key, full_value, full_out, full_gate, full_up, full_down = whole
    gain_attn, gain_ffn = gains
    inputs = tokens.astype(jnp.float32)
    normed, factor = normalize(inputs)
    hidden = (normed * gain_attn.astype(jnp.float32)).astype(low)
    query = matmul(hidden, full_query).astype(low)
    keyed = matmul(hidden, full_key).astype(low)
    valued = matmul(hidden, full_value).astype(low)
    query_groups, key_groups, value_groups = (to_groups(query), to_groups(keyed), to_groups(valued))
    attended_groups, log_total = lax.map(
        partial(attend, allowed), (query_groups, key_groups, value_groups)
    )
    attended = from_groups(attended_groups)
    residual = inputs + matmul(attended, full_out)
    normed_two, factor_two = normalize(residual)
    hidden_two = (normed_two * gain_ffn.astype(jnp.float32)).astype(low)
    gate = matmul(hidden_two, full_gate)
    upward = matmul(hidden_two, full_up)
    sigma = jax.nn.sigmoid(gate)
    middle = (gate * sigma * upward).astype(low)
    mixed = (valid[:, None] * (residual + matmul(middle, full_down))).astype(low)
    grad_output = cotangent.astype(jnp.float32) * valid[:, None]
    grad_branch = grad_output.astype(low)
    grad_down = matmul_tn(middle, grad_branch)
    grad_middle = matmul_nt(grad_branch, full_down)
    grad_gate_rows = (grad_middle * upward * sigma * (1.0 + gate * (1.0 - sigma))).astype(low)
    grad_up_rows = (grad_middle * gate * sigma).astype(low)
    grad_gate = matmul_tn(hidden_two, grad_gate_rows)
    grad_up = matmul_tn(hidden_two, grad_up_rows)
    grad_hidden_two = matmul_nt(grad_gate_rows, full_gate) + matmul_nt(grad_up_rows, full_up)
    grad_gain_ffn = jnp.sum(grad_hidden_two * normed_two, axis=0)
    grad_residual = grad_output + norm_back(
        grad_hidden_two * gain_ffn.astype(jnp.float32), normed_two, factor_two
    )
    grad_proj = grad_residual.astype(low)
    grad_out = matmul_tn(attended, grad_proj)
    grad_attended = matmul_nt(grad_proj, full_out).astype(low)
    grad_query_g, grad_key_g, grad_value_g = lax.map(
        partial(attend_back, allowed),
        (query_groups, key_groups, value_groups, to_groups(grad_attended), log_total),
    )
    grad_query_rows = from_groups(grad_query_g)
    grad_key_rows = from_groups(grad_key_g)
    grad_value_rows = from_groups(grad_value_g)
    grad_query = matmul_tn(hidden, grad_query_rows)
    grad_key = matmul_tn(hidden, grad_key_rows)
    grad_value = matmul_tn(hidden, grad_value_rows)
    grad_hidden = (
        matmul_nt(grad_query_rows, full_query)
        + matmul_nt(grad_key_rows, full_key)
        + matmul_nt(grad_value_rows, full_value)
    )
    grad_gain_attn = jnp.sum(grad_hidden * normed, axis=0)
    input_grad = grad_residual + norm_back(
        grad_hidden * gain_attn.astype(jnp.float32), normed, factor
    )
    grads = (grad_query, grad_key, grad_value, grad_out, grad_gate, grad_up, grad_down)
    sums, gain_sums = sum_plain([g.astype(low) for g in grads], (grad_gain_attn, grad_gain_ffn))
    return (
        mixed,
        input_grad,
        gain_sums[0],
        sums[0],
        sums[1],
        sums[2],
        sums[3],
        gain_sums[1],
        sums[4],
        sums[5],
        sums[6],
    )


def on_tuned_device(
    tokens,
    norm_attn,
    w_query,
    w_key,
    w_value,
    w_out,
    norm_ffn,
    w_gate,
    w_up,
    w_down,
    lengths,
    cotangent,
):
    weights = (w_query, w_key, w_value, w_out, w_gate, w_up, w_down)
    kept, saved = forward(tokens, cotangent, lengths, weights, (norm_attn, norm_ffn))
    blocks, gain_lines, d_in = backward(tokens, lengths, kept, saved)
    sums, gain_sums, mixed, d_in = unpack(blocks, gain_lines, saved["mixed"], d_in)
    return (
        mixed,
        d_in,
        gain_sums[0],
        *sums[:4],
        gain_sums[1],
        *sums[4:],
    )


def solution(mesh):
    tuned = dict(mesh.shape) == {"dp": 8, "rep": 2, "cores": 2}
    tokens_placed = P(("dp", "rep", "cores"), None)
    share, gain = P("dp", None), P("dp")
    return jax.shard_map(
        on_tuned_device if tuned else on_any_device,
        mesh=mesh,
        in_specs=(
            tokens_placed,
            gain,
            share,
            share,
            share,
            share,
            gain,
            share,
            share,
            share,
            tokens_placed,
            tokens_placed,
        ),
        out_specs=(
            tokens_placed,
            tokens_placed,
            gain,
            share,
            share,
            share,
            share,
            gain,
            share,
            share,
            share,
        ),
        check_vma=False,
    )
```

```python
from functools import partial

import jax
import jax.numpy as jnp
from jax import lax
from jax.experimental import pallas as pl
from jax.experimental.pallas import tpu as pltpu
from jax.sharding import PartitionSpec as P

HEADS = 16
HEAD = 64


NORM_EPS = 1e-05
SCORE_SCALE = 0.125
NEGATIVE = -1e30
head_group = 4
MESH = pl.DeviceIdType.MESH
MIB = 1024 * 1024


def masks(block_len, rows):
    bounds = jnp.cumsum(block_len[0])
    place = jnp.arange(rows, dtype=jnp.int32)
    segment = jnp.sum((place[:, None] >= bounds[None, :]).astype(jnp.int32), axis=1)
    allowed = (segment[:, None] == segment[None, :]) & (place[None, :] <= place[:, None])
    valid = (segment < block_len.shape[1]).astype(jnp.float32)
    return (allowed, valid)


def normalize(values):
    factor = lax.rsqrt(jnp.mean(values * values, axis=-1, keepdims=True) + NORM_EPS)
    return (values * factor, factor)


def norm_back(grad_normed, normed, factor):
    return factor * (grad_normed - normed * jnp.mean(grad_normed * normed, axis=-1, keepdims=True))


def matmul(left, right):
    return jnp.dot(left, right, preferred_element_type=jnp.float32)


def matmul_tn(left, right):
    return lax.dot_general(
        left, right, (((0,), (0,)), ((), ())), preferred_element_type=jnp.float32
    )


def matmul_nt(left, right):
    return lax.dot_general(
        left, right, (((1,), (1,)), ((), ())), preferred_element_type=jnp.float32
    )


def to_groups(matrix):
    rows = matrix.shape[0]
    split = matrix.reshape(rows, HEADS // head_group, head_group, HEAD)
    return split.transpose(1, 2, 0, 3)


def from_groups(grouped):
    rows = grouped.shape[2]
    return grouped.transpose(2, 0, 1, 3).reshape(rows, HEADS * HEAD)


def group_scores(allowed, query_g, key_g):
    raw = (
        jnp.einsum("hqe,hke->hqk", query_g, key_g, preferred_element_type=jnp.float32) * SCORE_SCALE
    )
    return jnp.where(allowed[None], raw, NEGATIVE)


def attend(allowed, operands):
    query_g, key_g, value_g = operands
    scores = group_scores(allowed, query_g, key_g)
    top = jnp.max(scores, axis=-1, keepdims=True)
    expo = jnp.exp(scores - top)
    total = jnp.sum(expo, axis=-1, keepdims=True)
    probs_low = (expo / total).astype(jnp.bfloat16)
    result = jnp.einsum("hqk,hke->hqe", probs_low, value_g, preferred_element_type=jnp.float32)
    return (result.astype(jnp.bfloat16), top[..., 0] + jnp.log(total[..., 0]))


def attend_back(allowed, operands):
    query_g, key_g, value_g, grad_g, lse = operands
    scores = group_scores(allowed, query_g, key_g)
    probs = jnp.exp(scores - lse[..., None])
    grad_probs = jnp.einsum("hqe,hke->hqk", grad_g, value_g, preferred_element_type=jnp.float32)
    centre = jnp.sum(grad_probs * probs, axis=-1, keepdims=True)
    grad_scores = (probs * (grad_probs - centre)).astype(jnp.bfloat16)
    grad_query = (
        jnp.einsum("hqk,hke->hqe", grad_scores, key_g, preferred_element_type=jnp.float32)
        * SCORE_SCALE
    )
    grad_key = (
        jnp.einsum("hqk,hqe->hke", grad_scores, query_g, preferred_element_type=jnp.float32)
        * SCORE_SCALE
    )
    grad_value = jnp.einsum(
        "hqk,hqe->hke", probs.astype(jnp.bfloat16), grad_g, preferred_element_type=jnp.float32
    )
    return (
        grad_query.astype(jnp.bfloat16),
        grad_key.astype(jnp.bfloat16),
        grad_value.astype(jnp.bfloat16),
    )


class Part:
    def __init__(self, weight, tall, start, size, no_x):
        self.weight, self.tall, self.start, self.size = weight, tall, start, size
        self.no_x = no_x

    def quarter(self, ref, lead, c, x):
        if self.tall:
            columns = pl.ds(pl.multiple_of(c * 512 + x * 256, 256), 256)
            return ref.at[(*lead, pl.ds(self.start, self.size), columns)]
        return ref.at[(*lead, x, slice(None), self.columns(c))]

    def half(self, ref, lead, c):
        if self.tall:
            columns = pl.ds(pl.multiple_of(c * 512, 512), 512)
            return ref.at[(*lead, pl.ds(self.start, self.size), columns)]
        return ref.at[(*lead, slice(None), slice(None), self.columns(c))]

    def columns(self, c):
        width = self.size // 2
        return pl.ds(pl.multiple_of(self.start + c * width, 128), width)


def pieces(total, most):
    return [(start, min(most, total - start)) for start in range(0, total, most)]


def place():
    d = lax.axis_index("dp")
    return lax.div(d, 2), lax.rem(d, 2), lax.axis_index("rep"), lax.axis_index("cores")


def device(z, y, x, c):
    return {"dp": 2 * z + y, "rep": x, "cores": c}


def along_z_of(z):
    return z, z + 1 - 2 * lax.rem(z, 2), lax.rem(z + 2, 4), 3 - z


def partners():
    z, y, x, c = place()
    others = [device(far, y, x, c) for far in along_z_of(z)[1:]]
    return others + [device(z, 1 - y, x, c), device(z, y, 1 - x, c), device(z, y, x, 1 - c)]


def greet():
    barrier = pltpu.get_barrier_semaphore()
    for other in partners():
        pl.semaphore_signal(barrier, inc=1, device_id=other, device_id_type=MESH)


def await_partners():
    pl.semaphore_wait(pltpu.get_barrier_semaphore(), len(partners()))


class Wires:
    def __init__(self, send_sems, recv_sems):
        self.send_sems, self.recv_sems, self.sent = send_sems, recv_sems, []

    def copy(self, slot, source, target, other):
        return pltpu.make_async_remote_copy(
            src_ref=source,
            dst_ref=target,
            send_sem=self.send_sems.at[slot],
            recv_sem=self.recv_sems.at[slot],
            device_id=other,
            device_id_type=MESH,
        )

    def send(self, slot, source, target, other):
        copy = self.copy(slot, source, target, other)
        copy.start()
        self.sent.append((slot, copy))

    def arrived(self, slot, target):
        z, y, x, c = place()
        self.copy(slot, target, target, device(z, y, x, 1 - c)).wait_recv()

    def finish(self, chosen=lambda slot: True):
        for slot, copy in self.sent:
            if chosen(slot):
                copy.wait_send()
        self.sent = [(slot, copy) for slot, copy in self.sent if not chosen(slot)]


GATHER_SLOTS = 12
LAG = 2
ALL = slice(None)
COLUMNS = (1024, 1024, 1024, 1024, 2816, 2816, None)
QUERY, KEY, VALUE, OUT, GATE, UP, DOWN = range(7)
TILE = 512


FF_CHUNKS = tuple(pieces(2816, 512))


def gather_items():
    order = [(QUERY, 0, 256, True), (QUERY, 256, 768, False), (KEY, 0, 1024, True)]
    order += [(VALUE, 0, 1024, False), (OUT, 0, 1024, False)]
    order += [(DOWN, 0, 128, False), (DOWN, 128, 128, True), (DOWN, 256, 96, False)]
    for n, (start, size) in enumerate(FF_CHUNKS):
        order += [(GATE, start, size, n == 5), (UP, start, size, n in (0, 3, 5))]
    return [Part(w, w == DOWN, start, size, no_x) for w, start, size, no_x in order]


def dot(left, right):
    return lax.dot_general(
        left, right, (((1,), (0,)), ((), ())), preferred_element_type=jnp.float32
    )


def dot_nt(left, right):
    return lax.dot_general(
        left, right, (((1,), (1,)), ((), ())), preferred_element_type=jnp.float32
    )


def tile(index, size):
    return pl.ds(pl.multiple_of(index * size, size), size)


def weight_columns(ref, at):
    return ref[:, :, :, :, at].reshape(1024, -1)


class Forward:
    def __init__(self, refs):
        self.__dict__.update(refs)

    def prepare(self):
        for s in range(8):
            self.gain[:, 128 * s : 128 * s + 128] = self.gains[s // 2, s % 2]
        length = self.length[0, 0]
        for block in range(4):
            rows = slice(128 * block, 128 * block + 128)
            place_q = lax.broadcasted_iota(jnp.int32, (128, 512), 0) + 128 * block
            place_k = lax.broadcasted_iota(jnp.int32, (128, 512), 1)
            same = (place_q >= length) == (place_k >= length)
            allowed = same & (place_k <= place_q)
            self.bias[rows, :] = jnp.where(allowed, 0.0, NEGATIVE)

        def normed(block, _):
            rows = tile(block, 64)
            values = self.tokens[rows, :].astype(jnp.float32)
            factor = lax.rsqrt(jnp.mean(values * values, axis=-1, keepdims=True) + NORM_EPS)
            gain = self.gain[0:1, :].astype(jnp.float32)
            self.hidden[rows, :] = (values * factor * gain).astype(jnp.bfloat16)
            place = lax.broadcasted_iota(jnp.int32, (64, 1024), 0) + 64 * block
            d_b = jnp.where(place < length, self.cotangent[rows, :].astype(jnp.float32), 0.0)
            self.d_b[rows, :] = d_b.astype(jnp.bfloat16)
            return 0

        lax.fori_loop(0, 8, normed, 0)
        self.turn(self.hidden, self.h_t)
        self.out("d_b")

    def turn(self, matrix, turned):
        def columns(n, _):
            at = tile(n, 128)
            turned[at, :] = matrix[:, at].astype(jnp.float32).T.astype(jnp.bfloat16)
            return 0

        lax.fori_loop(0, 8, columns, 0)

    def project(self, weight, result):
        def columns(n, _):
            at = tile(n, TILE)
            result[:, at] = dot(self.hidden[...], weight_columns(weight, at)).astype(jnp.bfloat16)
            return 0

        lax.fori_loop(0, 1024 // TILE, columns, 0)

    def attend(self, first, last):
        def pair(p, _):
            at = tile(p, 128)
            left = lax.broadcasted_iota(jnp.int32, (256, 128), 1) < HEAD
            for block in (0, 1):
                rows, seen = slice(256 * block, 256 * block + 256), slice(0, 256 * block + 256)
                query = self.query[rows, at].astype(jnp.float32) * SCORE_SCALE
                both = jnp.concatenate(
                    [jnp.where(left, query, 0.0), jnp.where(left, 0.0, query)], axis=0
                ).astype(jnp.bfloat16)
                bias = self.bias[rows, seen]
                scores = dot_nt(both, self.key[seen, at]) + jnp.concatenate([bias, bias], axis=0)
                top = jnp.max(scores, axis=-1, keepdims=True)
                expo = jnp.exp(scores - top)
                total = jnp.sum(expo, axis=-1, keepdims=True)
                probs = (expo * (1.0 / total)).astype(jnp.bfloat16)
                result = dot(probs, self.value[seen, at])
                self.attended[rows, at] = jnp.where(left, result[:256], result[256:]).astype(
                    jnp.bfloat16
                )
                lse = top + jnp.log(total)
                turned = jnp.where(left, lse[:256], lse[256:]).T
                self.lse[p, 0:1, rows] = turned[0:1]
                self.lse[p, 1:2, rows] = turned[HEAD : HEAD + 1]
            return 0

        lax.fori_loop(first, last, pair, 0)

    def project_out(self):
        def columns(n, _):
            at = tile(n, TILE)
            self.residual[:, at] = self.tokens[:, at].astype(jnp.float32) + dot(
                self.attended[...], weight_columns(self.w_out, at)
            )
            return 0

        lax.fori_loop(0, 1024 // TILE, columns, 0)

        def normed(block, _):
            rows = tile(block, 64)
            values = self.residual[rows, :]
            factor = lax.rsqrt(jnp.mean(values * values, axis=-1, keepdims=True) + NORM_EPS)
            gain = self.gain[8:9, :].astype(jnp.float32)
            self.h2[rows, :] = (values * factor * gain).astype(jnp.bfloat16)
            return 0

        lax.fori_loop(0, 8, normed, 0)
        self.turn(self.h2, self.h2_t)
        self.turn(self.attended, self.att_t)
        for name in ("query", "key", "value", "lse", "h_t", "h2_t", "att_t"):
            self.out(name)

    def grad_of_middle(self, start, size):
        at = pl.ds(start, size)
        self.d_up[:, at] = dot_nt(self.d_b[...], self.w_down[at, :]).astype(jnp.bfloat16)

    def feed_forward(self, start, size):
        at = pl.ds(start, size)
        low = jnp.bfloat16
        gate_w = weight_columns(self.w_gate, at)
        up_w = weight_columns(self.w_up, at)
        down_w = self.w_down[at, :]
        gate = dot(self.h2[...], gate_w)
        upward = dot(self.h2[...], up_w)
        grad_middle = self.d_up[:, at].astype(jnp.float32)
        sigma = 0.5 * jnp.tanh(0.5 * gate) + 0.5
        silu = gate * sigma
        mid = (silu * upward).astype(low)
        d_up = (grad_middle * silu).astype(low)
        d_gate = (grad_middle * upward * (sigma + silu - silu * sigma)).astype(low)
        self.mid[:, at] = mid
        self.d_up[:, at] = d_up
        self.d_gate[:, at] = d_gate
        for j in range(1024 // TILE):
            part = slice(TILE * j, TILE * j + TILE)
            mixed = dot(mid, down_w[:, part])
            grad = dot_nt(d_gate, gate_w[part, :]) + dot_nt(d_up, up_w[part, :])
            if start == 0:
                self.total[:, part] = mixed
                self.d_h2[:, part] = grad
            else:
                self.total[:, part] += mixed
                self.d_h2[:, part] += grad

    def flush(self, start, size):
        for name in ("mid", "d_gate", "d_up"):
            self.out(name, pl.ds(start, size))

    def finish(self):
        length = self.length[0, 0]
        self.g_ffn[...] = jnp.zeros_like(self.g_ffn)

        def rows_of(block, _):
            rows = tile(block, 64)
            place = lax.broadcasted_iota(jnp.int32, (64, 1024), 0) + 64 * block
            residual = self.residual[rows, :]
            mixed = jnp.where(place < length, residual + self.total[rows, :], 0.0)
            self.mixed[rows, :] = mixed.astype(jnp.bfloat16)
            factor = lax.rsqrt(jnp.mean(residual * residual, axis=-1, keepdims=True) + NORM_EPS)
            normed = residual * factor
            grad = self.d_h2[rows, :]
            self.g_ffn[...] += jnp.sum((grad * normed).reshape(8, 8, 1024), axis=0)
            grad_normed = grad * self.gain[8:9, :].astype(jnp.float32)
            grad_out = jnp.where(place < length, self.cotangent[rows, :].astype(jnp.float32), 0.0)
            mean = jnp.mean(grad_normed * normed, axis=-1, keepdims=True)
            d_res = grad_out + factor * (grad_normed - normed * mean)
            self.d_res[rows, :] = d_res
            self.d_proj[rows, :] = d_res.astype(jnp.bfloat16)
            return 0

        lax.fori_loop(0, 8, rows_of, 0)
        for name in ("mixed", "d_res", "d_proj", "g_ffn", "gain"):
            self.out(name)


FORWARD_OUTS = (
    ("mixed", (512, 1024), jnp.bfloat16),
    ("query", (512, 1024), jnp.bfloat16),
    ("key", (512, 1024), jnp.bfloat16),
    ("value", (512, 1024), jnp.bfloat16),
    ("lse", (8, 8, 512), jnp.float32),
    ("h_t", (1024, 512), jnp.bfloat16),
    ("h2_t", (1024, 512), jnp.bfloat16),
    ("att_t", (1024, 512), jnp.bfloat16),
    ("d_b", (512, 1024), jnp.bfloat16),
    ("mid", (512, 2816), jnp.bfloat16),
    ("d_gate", (512, 2816), jnp.bfloat16),
    ("d_up", (512, 2816), jnp.bfloat16),
    ("d_res", (512, 1024), jnp.float32),
    ("d_proj", (512, 1024), jnp.bfloat16),
    ("g_ffn", (8, 1024), jnp.float32),
    ("gain", (16, 1024), jnp.bfloat16),
)
FORWARD_OWN = (
    ("hidden", (512, 1024), jnp.bfloat16),
    ("attended", (512, 1024), jnp.bfloat16),
    ("residual", (512, 1024), jnp.float32),
    ("h2", (512, 1024), jnp.bfloat16),
    ("d_h2", (512, 1024), jnp.float32),
    ("bias", (512, 512), jnp.float32),
    ("total", (512, 1024), jnp.float32),
)
OUT_COPIES = len(FORWARD_OUTS) - 3 + 3 * len(FF_CHUNKS)
KEPT = (QUERY, KEY, VALUE, OUT)


def share_shape(columns):
    return (352, 1024) if columns is None else (2, 64, columns)


def forward_kernel(items, *refs):
    refs = list(refs)

    def take(n):
        taken = refs[:n]
        del refs[:n]
        return taken

    shares = take(7)
    gain_attn, gain_ffn, tokens, cotangent, length = take(5)
    kept = take(len(KEPT))
    names = [name for name, _, _ in FORWARD_OUTS]
    outs = dict(zip(names, take(len(names))))
    full = take(7)
    full_gains, gains = take(2)
    own_names = names + [name for name, _, _ in FORWARD_OWN]
    state = dict(zip(own_names, take(len(own_names))))
    send_sems, recv_sems, own_sems, keep_sems, out_sems = refs
    outgoing = []

    def put(name, columns=None):
        source, target = state[name], outs[name]
        if columns is not None:
            source, target = source.at[:, columns], target.at[:, columns]
        outgoing.append(pltpu.make_async_copy(source, target, out_sems.at[len(outgoing)]))
        outgoing[-1].start()

    z, y, x, c = place()
    far = back = along_z_of(z)
    x_other, y_other, c_other = (
        device(z, y, 1 - x, c),
        device(z, 1 - y, x, c),
        device(z, y, x, 1 - c),
    )
    greet()
    await_partners()
    wires = Wires(send_sems, recv_sems)
    own = [
        pltpu.make_async_copy(share, whole.at[z, y], own_sems.at[i])
        for i, (share, whole) in enumerate(zip(shares, full))
    ]
    own_gains = pltpu.make_async_copy(gains, full_gains.at[z, y], own_sems.at[7])
    keep = [
        pltpu.make_async_copy(full[w], kept[n], keep_sems.at[n]) for n, w in enumerate(KEPT)
    ]
    gains[...] = jnp.where(
        lax.broadcasted_iota(jnp.int32, (16, 128), 0) < 8,
        jnp.broadcast_to(gain_attn[...].astype(jnp.float32), (16, 128)),
        jnp.broadcast_to(gain_ffn[...].astype(jnp.float32), (16, 128)),
    ).astype(jnp.bfloat16)
    own_gains.start()
    gain_slot = GATHER_SLOTS * len(items)
    for k in (1, 2, 3):
        wires.send(gain_slot + k, gains, full_gains.at[z, y], device(far[k], y, x, c))
    for copy in own:
        copy.start()

    def slot(i, k):
        return GATHER_SLOTS * i + k

    def along_z(i):
        item = items[i]
        share, whole = shares[item.weight], full[item.weight]
        for k in (1, 2, 3):
            if item.no_x:
                source, target = item.half(share, (), c), item.half(whole, (z, y), c)
            else:
                source, target = item.quarter(share, (), c, x), item.quarter(whole, (z, y), c, x)
            wires.send(slot(i, k), source, target, device(far[k], y, x, c))

    own_done = set()

    def first_hop(i):
        item = items[i]
        whole = full[item.weight]
        if item.weight not in own_done:
            own[item.weight].wait()
            own_done.add(item.weight)
        for k in (1, 2, 3):
            if item.no_x:
                block = item.half(whole, (back[k], y), c)
                wires.arrived(slot(i, k), block)
                wires.send(slot(i, 7 + k), block, block, c_other)
            else:
                block = item.quarter(whole, (back[k], y), c, x)
                wires.arrived(slot(i, k), block)
                wires.send(slot(i, 3 + k), block, block, x_other)
        if item.no_x:
            block = item.half(whole, (ALL, y), c)
        else:
            block = item.quarter(whole, (ALL, y), c, x)
        wires.send(slot(i, 7), block, block, y_other)

    def second_hop(i):
        item = items[i]
        whole = full[item.weight]
        if item.no_x:
            block = item.half(whole, (ALL, 1 - y), c)
            wires.arrived(slot(i, 7), block)
            wires.send(slot(i, 11), block, block, c_other)
            return
        block = item.quarter(whole, (ALL, 1 - y), c, x)
        wires.arrived(slot(i, 7), block)
        wires.send(slot(i, 0), block, block, x_other)
        for k in (1, 2, 3):
            wires.arrived(slot(i, 3 + k), item.quarter(whole, (back[k], y), c, 1 - x))
        for k in (1, 2, 3):
            block = item.half(whole, (back[k], y), c)
            wires.send(slot(i, 7 + k), block, block, c_other)

    def last_hop(i):
        item = items[i]
        whole = full[item.weight]
        if not item.no_x:
            block = item.half(whole, (ALL, 1 - y), c)
            wires.arrived(slot(i, 0), item.quarter(whole, (ALL, 1 - y), c, 1 - x))
            wires.send(slot(i, 11), block, block, c_other)

    def complete(i):
        item = items[i]
        whole = full[item.weight]
        for k in (1, 2, 3):
            wires.arrived(slot(i, 7 + k), item.half(whole, (back[k], y), 1 - c))
        wires.arrived(slot(i, 11), item.half(whole, (ALL, 1 - y), 1 - c))

    def retire(i):
        wires.finish(lambda slot: slot // GATHER_SLOTS == i)

    step_of = Forward(
        dict(
            state,
            out=put,
            tokens=tokens,
            cotangent=cotangent,
            length=length,
            gains=full_gains,
            w_out=full[OUT],
            w_gate=full[GATE],
            w_up=full[UP],
            w_down=full[DOWN].reshape(2816, 1024),
        )
    )
    last_of = {item.weight: i for i, item in enumerate(items)}
    tasks = [(-1, 3, step_of.prepare)]
    for n, name in enumerate(("query", "key", "value")):
        tasks.append((last_of[n], 2, partial(step_of.project, full[n], state[name])))
    tasks += [(last_of[VALUE], 3, partial(step_of.attend, p, p + 2)) for p in (0, 2, 4, 6)]
    tasks.append((last_of[OUT], 3, step_of.project_out))
    for tile_of in pieces(2816, TILE):
        tasks.append((last_of[DOWN], 1, partial(step_of.grad_of_middle, *tile_of)))
    for start, size in FF_CHUNKS:
        there = max(
            i for i, item in enumerate(items) if item.weight == UP and item.start == start
        )
        for at, width in pieces(size, TILE):
            tasks.append((there, 5, partial(step_of.feed_forward, start + at, width)))
        tasks.append((there, 0, partial(step_of.flush, start, size)))

    ahead = 3
    for i in range(min(ahead, len(items))):
        along_z(i)
    own_gains.wait()
    for k in (1, 2, 3):
        wires.arrived(gain_slot + k, full_gains.at[back[k], y])
    wires.send(gain_slot, full_gains.at[:, y], full_gains.at[:, y], y_other)
    stages = (retire, complete, last_hop, second_hop, first_hop)
    lates = (3 * LAG, 3 * LAG - 1, 2 * LAG, LAG, 0)
    for step in range(len(items) + 3 * LAG):
        for late, stage in zip(lates, stages):
            if 0 <= step - late < len(items):
                stage(step - late)
        if step + ahead < len(items):
            along_z(step + ahead)
        if step == 0:
            wires.arrived(gain_slot, full_gains.at[:, 1 - y])
        there = step - lates[1]
        for n, w in enumerate(KEPT):
            if there == last_of[w]:
                keep[n].start()
        spent = 0
        while tasks and tasks[0][0] <= there and spent < 6:
            _, cost, task = tasks.pop(0)
            task()
            spent += cost
    for _, _, task in tasks:
        task()
    step_of.finish()
    for copy in keep + outgoing:
        copy.wait()
    wires.finish()


def forward(tokens, cotangent, lengths, weights, gains):
    items = gather_items()
    shares = [w.reshape(share_shape(n)) for w, n in zip(weights, COLUMNS)]
    wholes = [(4, 2) + share_shape(n) for n in COLUMNS]
    shapes = [jax.ShapeDtypeStruct(wholes[w], jnp.bfloat16) for w in KEPT]
    shapes += [jax.ShapeDtypeStruct(shape, dtype) for _, shape, dtype in FORWARD_OUTS]
    count = GATHER_SLOTS * len(items) + 4
    anywhere = pl.BlockSpec(memory_space=pl.ANY)
    in_vmem = pl.BlockSpec(memory_space=pltpu.VMEM)
    out = pl.pallas_call(
        partial(forward_kernel, items),
        out_shape=shapes,
        in_specs=[anywhere] * 7
        + [in_vmem] * 4
        + [pl.BlockSpec(memory_space=pltpu.SMEM)],
        out_specs=[anywhere] * len(shapes),
        scratch_shapes=[pltpu.VMEM(shape, jnp.bfloat16) for shape in wholes]
        + [pltpu.VMEM((4, 2, 16, 128), jnp.bfloat16), pltpu.VMEM((16, 128), jnp.bfloat16)]
        + [pltpu.VMEM(shape, dtype) for _, shape, dtype in FORWARD_OUTS + FORWARD_OWN]
        + [
            pltpu.SemaphoreType.DMA((count,)),
            pltpu.SemaphoreType.DMA((count,)),
            pltpu.SemaphoreType.DMA((8,)),
            pltpu.SemaphoreType.DMA((len(KEPT),)),
            pltpu.SemaphoreType.DMA((OUT_COPIES,)),
        ],
        compiler_params=pltpu.CompilerParams(
            collective_id=0, has_side_effects=True, vmem_limit_bytes=63 * MIB
        ),
        name="gather_forward",
    )(*shares, *[g.reshape(1, 128) for g in gains], tokens, cotangent, lengths)
    return out[: len(KEPT)], dict(zip([name for name, _, _ in FORWARD_OUTS], out[len(KEPT) :]))


SUM_SLOTS = 10
RING = 4


class Share:
    def __init__(self, weight, start, size, x_first):
        self.weight, self.start, self.size, self.x_first = weight, start, size, x_first
        self.tall = weight == DOWN
        self.width = 128 if self.tall else size // 2
        self.block = (352 if self.tall else 64, self.width)

    def columns(self, c, x):
        start = c * 512 + x * 256 + self.start if self.tall else self.start + c * self.width
        return pl.ds(pl.multiple_of(start, 128), self.width)

    def quarter(self, sums, c, x):
        if self.tall:
            return sums.at[c, x, self.start // 128]
        return sums.at[x, :, self.columns(c, x)]

    def half(self, sums, c):
        if self.tall:
            return sums.at[c, :, self.start // 128]
        return sums.at[:, :, self.columns(c, 0)]


def share_items():
    order = [(GATE, 2048, 768, True), (DOWN, 0, 128, False), (DOWN, 128, 128, True)]
    order += [(GATE, 0, 1024, False), (GATE, 1024, 1024, True)]
    order += [(UP, 0, 1024, True), (UP, 1024, 1024, False), (UP, 2048, 768, False)]
    order += [(OUT, 0, 1024, True), (QUERY, 0, 1024, False), (KEY, 0, 1024, True)]
    order += [(VALUE, 0, 768, True), (VALUE, 768, 256, False)]
    return [Share(*item) for item in order]


def plus(left, right):
    return left + right


def dot_tn(left, right):
    return lax.dot_general(
        left, right, (((0,), (0,)), ((), ())), preferred_element_type=jnp.float32
    )


BACKWARD_IN = (
    "query",
    "key",
    "value",
    "lse",
    "h_t",
    "h2_t",
    "att_t",
    "d_b",
    "d_res",
    "d_proj",
    "g_ffn",
    "gain",
)


class Backward:
    def __init__(self, refs):
        self.__dict__.update(refs)

    def prepare(self):
        length = self.length[0, 0]
        for block in range(4):
            rows = slice(128 * block, 128 * block + 128)
            place_k = lax.broadcasted_iota(jnp.int32, (128, 512), 0) + 128 * block
            place_q = lax.broadcasted_iota(jnp.int32, (128, 512), 1)
            same = (place_q >= length) == (place_k >= length)
            allowed = same & (place_k <= place_q)
            self.bias[rows, :] = jnp.where(allowed, 0.0, NEGATIVE)

    def multiply(self, left_t, right, item, target, core):
        columns = item.columns(core, 0)

        def rows(m, _):
            product = dot(left_t[tile(m, 256), :], right[:, columns]).astype(jnp.bfloat16)
            product = product.reshape(2, 2, 64, item.width)
            for xx in (0, 1):
                target[xx, m] = product[:, xx]
            return 0

        lax.fori_loop(0, 4, rows, 0)

    def multiply_tall(self, left, right, groups):
        def rows(m, _):
            at = tile(m, 256)
            turned = left[:, at].T
            for columns, targets in groups:
                product = dot(turned, right[:, columns]).astype(jnp.bfloat16)
                for n, (target, xx) in enumerate(targets):
                    target.reshape(2, 2816, 128)[xx, at, :] = product[:, 128 * n : 128 * n + 128]
            return 0

        lax.fori_loop(0, 11, rows, 0)

    def attend_back(self, first, last):
        low = jnp.bfloat16

        def pair(p, _):
            at = tile(p, 128)
            wo_rows = self.w_rows[p].reshape(128, 1024)
            grad = dot_nt(self.d_proj[...], wo_rows).astype(low)
            query = (self.query[:, at].astype(jnp.float32) * SCORE_SCALE).astype(low)
            key, value = self.key[:, at], self.value[:, at]
            left = lax.broadcasted_iota(jnp.int32, (512, 128), 1) < HEAD
            none = jnp.zeros((512, 128), low)
            sides = [
                [jnp.where(side, v, none) for v in (query, key, value, grad)]
                for side in (left, ~left)
            ]
            grad_key, grad_value = [None, None], [None, None]
            for block in (0, 1):
                rows, seen = slice(256 * block, 256 * block + 256), slice(0, 256 * block + 256)
                grad_query = None
                parts_key, parts_value = None, None
                for n, (own_query, own_key, own_value, own_grad) in enumerate(sides):
                    self.d_in[seen, 0:256] = dot_nt(own_key[seen], query[rows])
                    self.d_in[seen, 256:512] = dot_nt(own_value[seen], grad[rows])
                    self.back_rows(p, n, rows, 256 * block + 256)
                    grad_scores, probs = self.grad_scores[seen, :], self.probs[seen, :]
                    part_query = dot_tn(grad_scores, own_key[seen])
                    part_key = dot(grad_scores, own_query[rows])
                    part_value = dot(probs, own_grad[rows])
                    if n == 0:
                        grad_query, parts_key, parts_value = part_query, part_key, part_value
                    else:
                        grad_query += part_query
                        parts_key += part_key
                        parts_value += part_value
                self.query[rows, at] = (grad_query * SCORE_SCALE).astype(low)
                if block == 0:
                    grad_key[0], grad_value[0] = parts_key, parts_value
                else:
                    grad_key = [grad_key[0] + parts_key[:256], parts_key[256:]]
                    grad_value = [grad_value[0] + parts_value[:256], parts_value[256:]]
            for block in (0, 1):
                rows = slice(256 * block, 256 * block + 256)
                self.key[rows, at] = grad_key[block].astype(low)
                self.value[rows, at] = grad_value[block].astype(low)
            return 0

        lax.fori_loop(first, last, pair, 0)

    def back_rows(self, p, n, rows, count):
        low = jnp.bfloat16
        held = self.d_in
        lse = self.lse[p, n : n + 1, rows]

        def first_pass(r, centre):
            keys = tile(r, 64)
            probs = jnp.exp(held[keys, 0:256] + self.bias[keys, rows] - lse)
            held[keys, 0:256] = probs
            self.probs[keys, :] = probs.astype(low)
            return centre + jnp.sum((held[keys, 256:512] * probs).reshape(8, 8, 256), axis=0)

        centre = lax.fori_loop(0, count // 64, first_pass, jnp.zeros((8, 256), jnp.float32), unroll=2)
        centre = jnp.sum(centre, axis=0, keepdims=True)

        def second_pass(r, _):
            keys = tile(r, 64)
            grad = held[keys, 0:256] * (held[keys, 256:512] - centre)
            self.grad_scores[keys, :] = grad.astype(low)
            return 0

        lax.fori_loop(0, count // 64, second_pass, 0, unroll=2)

    def grad_hidden(self, t):
        at = pl.ds(256 * t, 256)
        total = None
        for n, grad in enumerate((self.query, self.key, self.value)):
            part = dot_nt(grad[...], self.w_rows[2 * n : 2 * n + 2].reshape(256, 1024))
            total = part if total is None else total + part
        self.d_in[:, at] = total

    def finish(self):
        self.gain_total[...] = jnp.zeros_like(self.gain_total)

        def rows_of(block, _):
            rows = tile(block, 64)
            values = self.tokens[rows, :].astype(jnp.float32)
            factor = lax.rsqrt(jnp.mean(values * values, axis=-1, keepdims=True) + NORM_EPS)
            normed = values * factor
            grad = self.d_in[rows, :]
            self.gain_total[...] += jnp.sum((grad * normed).reshape(8, 8, 1024), axis=0)
            grad_normed = grad * self.gain[0:1, :].astype(jnp.float32)
            mean = jnp.mean(grad_normed * normed, axis=-1, keepdims=True)
            self.d_in[rows, :] = self.d_res[rows, :] + factor * (
                grad_normed - normed * mean
            )
            return 0

        lax.fori_loop(0, 8, rows_of, 0)
        self.gain_lines[...] = jnp.zeros_like(self.gain_lines)
        lines = [jnp.sum(v[...], axis=0, keepdims=True) for v in (self.gain_total, self.g_ffn)]
        for s in range(8):
            for n, line in enumerate(lines):
                self.gain_lines[s // 2, s % 2, n : n + 1] = line[:, 128 * s : 128 * s + 128]


def backward_kernel(items, *refs):
    refs = list(refs)

    def take(n):
        taken = refs[:n]
        del refs[:n]
        return taken

    kept = take(len(KEPT))
    middle_in, grad_gate_in, grad_up_in = take(3)
    saved_in = dict(zip(BACKWARD_IN, take(len(BACKWARD_IN))))
    tokens_in, length = take(2)
    sums = take(7)
    gain_sums, input_grad_out = take(2)
    saved = dict(zip(BACKWARD_IN, take(len(BACKWARD_IN))))
    d_in, wide, w_rows, bias, probs, grad_scores, gain_total, gain_lines = take(8)
    mine, from_first, from_second, from_z = (take(len(items)) for _ in range(4))
    ring, tall_ring = take(RING), take(2)
    outbox, tall_outbox = take(2), take(2)
    gain_core, gain_x, gain_y, gain_z = take(4)
    send_sems, recv_sems, load_sems, credit = refs
    z, y, x, c = place()
    far = back = along_z_of(z)
    x_other, y_other, c_other = (
        device(z, y, 1 - x, c),
        device(z, 1 - y, x, c),
        device(z, y, x, 1 - c),
    )
    loads = {}

    def load(name, source, target):
        loads[name] = pltpu.make_async_copy(source, target, load_sems.at[len(loads)])
        loads[name].start()

    waited = set()

    def loaded(*names):
        for name in names:
            if name not in waited:
                loads[name].wait()
                waited.add(name)

    load("d_gate", grad_gate_in, wide.at[1])
    load("h2_t", saved_in["h2_t"], saved["h2_t"])
    load("mid", middle_in, wide.at[0])
    load("d_b", saved_in["d_b"], saved["d_b"])
    load("wo_rows", kept[OUT].reshape(8, 2, 64, 1024), w_rows)
    for name in BACKWARD_IN:
        if name not in loads:
            load(name, saved_in[name], saved[name])
    greet()
    wires = Wires(send_sems, recv_sems)
    work = Backward(
        dict(
            saved,
            tokens=saved["d_b"],
            length=length,
            w_rows=w_rows,
            probs=probs,
            grad_scores=grad_scores,
            bias=bias,
            d_in=d_in,
            gain_total=gain_total,
            gain_lines=gain_lines,
        )
    )
    tall_items = [i for i, item in enumerate(items) if item.tall]
    wide_items = [i for i, item in enumerate(items) if not item.tall]

    def slot(i, k):
        return SUM_SLOTS * i + k

    def core_slots(i):
        return (slot(i, 0), slot(i, 8))

    def from_core(i):
        if items[i].tall:
            return tall_ring[tall_items.index(i)]
        return ring[wide_items.index(i) % RING].at[..., : items[i].width]

    def produce(i):
        item = items[i]
        if item.tall:
            number = tall_items.index(i)
            if number == 0:
                loaded("mid", "d_b")
                groups = []
                for core, boxes in ((1 - c, tall_outbox), (c, [mine[j] for j in tall_items])):
                    columns = pl.ds(pl.multiple_of(512 * core, 512), 512)
                    groups.append((columns, [(boxes[j], xx) for xx in (0, 1) for j in (0, 1)]))
                work.multiply_tall(wide.at[0], saved["d_b"], groups)
                load("d_up", grad_up_in, wide.at[0])
                load("tokens", tokens_in, saved["d_b"])
            box = tall_outbox[number]
        else:
            number = wide_items.index(i)
            if number >= 2:
                wires.finish(lambda s: s in core_slots(wide_items[number - 2]))
            box = outbox[number % 2].at[..., : item.width]
            left, right, names = {
                GATE: (saved["h2_t"], wide.at[1], ("h2_t", "d_gate")),
                UP: (saved["h2_t"], wide.at[0], ("d_up",)),
                OUT: (saved["att_t"], saved["d_proj"], ("att_t", "d_proj")),
                QUERY: (saved["h_t"], saved["query"], ("h_t",)),
                KEY: (saved["h_t"], saved["key"], ()),
                VALUE: (saved["h_t"], saved["value"], ()),
            }[item.weight]
            loaded(*names)
            multiply = partial(work.multiply, left, right, item)
            if number >= RING:
                pl.semaphore_wait(credit, 1)
            multiply(box, 1 - c)
            if i == 0:
                multiply(mine[i], c)
        if i == 0:
            await_partners()
        for xx in (0, 1):
            wires.send(core_slots(i)[xx], box.at[xx], from_core(i).at[xx], c_other)
        if i > 0 and not item.tall:
            multiply(mine[i], c)

    def first_hop(i):
        item, own, other = items[i], mine[i], from_core(i)
        for xx in (0, 1):
            wires.arrived(core_slots(i)[xx], other.at[xx])

        def add(at, _):
            for xx in (0, 1):
                for yy in (0, 1):
                    own[xx, at, yy] = plus(own[xx, at, yy], other[xx, at, yy])
            return 0

        lax.fori_loop(0, 4, add, 0)
        if not item.tall and wide_items.index(i) + RING < len(wide_items):
            pl.semaphore_signal(credit, inc=1, device_id=c_other, device_id_type=MESH)
        if item.x_first:
            wires.send(slot(i, 1), own.at[1 - x], from_first[i], x_other)
        else:
            wires.send(slot(i, 1), own.at[:, :, 1 - y], from_first[i], y_other)

    def second_hop(i):
        item, own, other = items[i], mine[i], from_first[i]
        wires.arrived(slot(i, 1), other)

        def add(at, _):
            for side in (0, 1):
                if item.x_first:
                    own[x, at, side] = plus(own[x, at, side], other[at, side])
                else:
                    own[side, at, y] = plus(own[side, at, y], other[side, at])
            return 0

        lax.fori_loop(0, 4, add, 0)
        if item.x_first:
            wires.send(slot(i, 2), own.at[x, :, 1 - y], from_second[i], y_other)
        else:
            to_z(i, lambda k: own.at[:, far[k], y])

    def to_z(i, block):
        for k in (1, 2, 3):
            wires.send(slot(i, 2 + k), block(k), from_z[i].at[k - 1], device(far[k], y, x, c))

    def z_total(i, own_part):
        total = own_part.astype(jnp.float32)
        for k in (1, 2, 3):
            wires.arrived(slot(i, 2 + k), from_z[i].at[k - 1])
            total += from_z[i][k - 1].astype(jnp.float32)
        return total.astype(jnp.bfloat16)

    def third_hop(i):
        item, own, other = items[i], mine[i], from_second[i]
        if not item.x_first:
            own[:, z, y] = z_total(i, own[:, z, y])
            wires.send(slot(i, 2), own.at[:, z, y], other, x_other)
            return
        wires.arrived(slot(i, 2), other)

        def add(at, _):
            own[x, at, y] = plus(own[x, at, y], other[at])
            return 0

        lax.fori_loop(0, 4, add, 0)
        to_z(i, lambda k: own.at[x, far[k], y])

    def fourth_hop(i):
        item, own = items[i], mine[i]
        if not item.x_first:
            wires.arrived(slot(i, 2), from_second[i])
            block = item.half(sums[item.weight], c)
            block[...] = plus(own[:, z, y], from_second[i][...])
            wires.send(slot(i, 7), block, block, c_other)
            return
        block = item.quarter(sums[item.weight], c, x)
        block[...] = z_total(i, own[x, z, y])
        wires.send(slot(i, 6), block, block, x_other)

    def to_sibling(i):
        item = items[i]
        if item.x_first:
            wires.arrived(slot(i, 6), item.quarter(sums[item.weight], c, 1 - x))
            block = item.half(sums[item.weight], c)
            wires.send(slot(i, 7), block, block, c_other)

    def complete(i):
        item = items[i]
        wires.arrived(slot(i, 7), item.half(sums[item.weight], 1 - c))
        wires.finish(lambda s: s // SUM_SLOTS == i)

    base = SUM_SLOTS * len(items)

    def gains_one():
        wires.send(base, gain_lines, gain_core, c_other)

    def gains_two():
        wires.arrived(base, gain_core)
        gain_core[...] = gain_lines[...] + gain_core[...]
        wires.send(base + 1, gain_core, gain_x, x_other)

    def gains_three():
        wires.arrived(base + 1, gain_x)
        gain_x[...] = gain_core[...] + gain_x[...]
        wires.send(base + 2, gain_x.at[:, 1 - y], gain_y, y_other)

    def gains_four():
        wires.arrived(base + 2, gain_y)
        gain_y[...] = gain_x[:, y] + gain_y[...]
        for k in (1, 2, 3):
            wires.send(base + 2 + k, gain_y.at[far[k]], gain_z.at[z], device(far[k], y, x, c))
        gain_z[z] = gain_y[z]

    def gains_five():
        for k in (1, 2, 3):
            wires.arrived(base + 2 + k, gain_z.at[back[k]])
        gain_sums[...] = (gain_z[0] + gain_z[1]) + (gain_z[2] + gain_z[3])

    def fetch_rows(t):
        for n in range(3):
            load(("rows", n, t), kept[n].at[t], w_rows.at[2 * n : 2 * n + 2])

    def attend_back(p):
        if p == 0:
            loaded("query", "key", "value", "lse", "d_proj", "wo_rows")
        work.attend_back(p, p + 1)
        if p == 7:
            fetch_rows(0)

    def grad_hidden(t):
        loaded(*[("rows", n, t) for n in range(3)])
        work.grad_hidden(t)
        if t < 3:
            fetch_rows(t + 1)

    def finish():
        loaded("tokens", "d_res", "g_ffn", "gain")
        work.finish()
        load("d_in", d_in, input_grad_out)
        gains_one()

    beside = {}
    for p in range(8):
        beside.setdefault(1 + p, []).append(partial(attend_back, p))
    for t in range(4):
        beside.setdefault(9 + t // 2, []).append(partial(grad_hidden, t))
    beside.setdefault(11, []).append(finish)
    for n, task in enumerate((gains_two, gains_three, gains_four, gains_five)):
        beside.setdefault(13 + 2 * n, []).append(task)

    stages = (complete, to_sibling, fourth_hop, third_hop, second_hop, first_hop, produce)
    lates = (12, 10, 8, 6, 4, 2, 0)
    work.prepare()
    for step in range(len(items) + lates[0]):
        for late, stage in zip(lates, stages):
            if 0 <= step - late < len(items):
                stage(step - late)
        for task in beside.get(step, []):
            task()
    loaded("d_in")
    wires.finish()


def backward(tokens, lengths, kept, saved):
    items = share_items()
    low, wide = jnp.bfloat16, jnp.float32
    dtypes = {name: (shape, dtype) for name, shape, dtype in FORWARD_OUTS}
    shapes = [
        jax.ShapeDtypeStruct((2, 2, 2, 352, 128) if n is None else (2, 64, n), low) for n in COLUMNS
    ]
    shapes += [jax.ShapeDtypeStruct((8, 128), wide), jax.ShapeDtypeStruct((512, 1024), wide)]
    count = SUM_SLOTS * len(items) + 6
    anywhere = pl.BlockSpec(memory_space=pl.ANY)
    in_vmem = pl.BlockSpec(memory_space=pltpu.VMEM)
    n_loads = 6 + len(BACKWARD_IN) + 12

    def buffers(lead_of):
        return [pltpu.VMEM(lead_of(item) + item.block, low) for item in items]

    out = pl.pallas_call(
        partial(backward_kernel, items),
        out_shape=shapes,
        in_specs=[anywhere] * (len(KEPT) + 3 + len(BACKWARD_IN) + 1)
        + [pl.BlockSpec(memory_space=pltpu.SMEM)],
        out_specs=[in_vmem] * 8 + [anywhere],
        scratch_shapes=[pltpu.VMEM(*dtypes[name]) for name in BACKWARD_IN]
        + [
            pltpu.VMEM((512, 1024), wide),
            pltpu.VMEM((2, 512, 2816), low),
            pltpu.VMEM((8, 2, 64, 1024), low),
            pltpu.VMEM((512, 512), wide),
            pltpu.VMEM((512, 256), low),
            pltpu.VMEM((512, 256), low),
            pltpu.VMEM((8, 1024), wide),
            pltpu.VMEM((4, 2, 8, 128), wide),
        ]
        + buffers(lambda item: (2, 4, 2))
        + buffers(lambda item: (4, 2) if item.x_first else (2, 4))
        + buffers(lambda item: (4,) if item.x_first else (2,))
        + buffers(lambda item: (3,) if item.x_first else (3, 2))
        + [pltpu.VMEM((2, 4, 2, 64, 512), low)] * RING
        + [pltpu.VMEM((2, 4, 2, 352, 128), low)] * 2
        + [pltpu.VMEM((2, 4, 2, 64, 512), low)] * 2
        + [pltpu.VMEM((2, 4, 2, 352, 128), low)] * 2
        + [
            pltpu.VMEM((4, 2, 8, 128), wide),
            pltpu.VMEM((4, 2, 8, 128), wide),
            pltpu.VMEM((4, 8, 128), wide),
            pltpu.VMEM((4, 8, 128), wide),
            pltpu.SemaphoreType.DMA((count,)),
            pltpu.SemaphoreType.DMA((count,)),
            pltpu.SemaphoreType.DMA((n_loads,)),
            pltpu.SemaphoreType.REGULAR,
        ],
        compiler_params=pltpu.CompilerParams(
            collective_id=1, has_side_effects=True, vmem_limit_bytes=63 * MIB
        ),
        name="backward_sum",
    )(
        *kept,
        saved["mid"],
        saved["d_gate"],
        saved["d_up"],
        *[saved[name] for name in BACKWARD_IN],
        tokens,
        lengths,
    )
    return out[:7], out[7], out[8]


def unpack_kernel(*refs):
    blocks, (gain_sums, mixed, d_in) = refs[:7], refs[7:10]
    sums, (gain_attn, gain_ffn, mixed_out, input_out) = refs[10:17], refs[17:21]
    held, wide = refs[21:28], refs[28:35]
    mixed_held, input_held, in_sems, out_sems = refs[35:]
    sources = (d_in, mixed, *blocks)
    places = (input_held, mixed_held, *held)
    results = (input_held, mixed_held, *wide)
    targets = (input_out, mixed_out, *sums)
    ins = [pltpu.make_async_copy(a, b, in_sems.at[n]) for n, (a, b) in enumerate(zip(sources, places))]
    outs = [pltpu.make_async_copy(a, b, out_sems.at[n]) for n, (a, b) in enumerate(zip(results, targets))]
    order = (6, 7, 8, 2, 3, 4, 5, 0, 1)
    for n in order:
        ins[n].start()
    for n in order:
        ins[n].wait()
        if n == 8:
            for b in range(8):
                wide[6][:, 128 * b : 128 * b + 128] = held[6][b // 4, b // 2 % 2, b % 2].astype(
                    jnp.float32
                )
        elif n >= 2:
            wide[n - 2][...] = held[n - 2][...].astype(jnp.float32)
        outs[n].start()
    gain_attn[...] = gain_sums[0:1]
    gain_ffn[...] = gain_sums[1:2]
    for n in order:
        outs[n].wait()


def unpack(blocks, gain_sums, mixed, d_in):
    wide = jnp.float32
    anywhere = pl.BlockSpec(memory_space=pl.ANY)
    in_vmem = pl.BlockSpec(memory_space=pltpu.VMEM)
    shapes = [
        jax.ShapeDtypeStruct((352, 1024) if n is None else (2, 64, n), wide) for n in COLUMNS
    ]
    held = [pltpu.VMEM(b.shape, b.dtype) for b in blocks]
    held += [pltpu.VMEM(v.shape, wide) for v in shapes]
    held += [pltpu.VMEM(v.shape, v.dtype) for v in (mixed, d_in)]
    shapes += [jax.ShapeDtypeStruct((1, 128), wide)] * 2
    shapes += [jax.ShapeDtypeStruct(v.shape, v.dtype) for v in (mixed, d_in)]
    out = pl.pallas_call(
        unpack_kernel,
        out_shape=shapes,
        in_specs=[anywhere] * 7 + [in_vmem] + [anywhere] * 2,
        out_specs=[anywhere] * 7 + [in_vmem] * 2 + [anywhere] * 2,
        scratch_shapes=held + [pltpu.SemaphoreType.DMA((9,)), pltpu.SemaphoreType.DMA((9,))],
        compiler_params=pltpu.CompilerParams(vmem_limit_bytes=62 * MIB),
        name="unpack",
    )(*blocks, gain_sums, mixed, d_in)
    sums = [s.reshape(-1, s.shape[-1]) for s in out[:7]]
    return sums, [g.reshape(128) for g in out[7:9]], out[9], out[10]


def gather_plain(weights, gains):
    everything = (*weights, *gains)
    whole = [lax.all_gather(v, "dp", axis=0, tiled=True) for v in everything]
    return whole[: len(weights)], whole[len(weights) :]


def sum_plain(grads, gain_grads):
    shares = [
        lax.psum_scatter(g.astype(jnp.float32), "dp", scatter_dimension=0, tiled=True)
        for g in (*grads, *gain_grads)
    ]
    sums = [lax.psum(s, ("rep", "cores")) for s in shares]
    return sums[: len(grads)], sums[len(grads) :]


def on_any_device(
    tokens,
    norm_attn,
    w_query,
    w_key,
    w_value,
    w_out,
    norm_ffn,
    w_gate,
    w_up,
    w_down,
    lengths,
    cotangent,
):
    rows = tokens.shape[0]
    low = jnp.bfloat16
    allowed, valid = masks(lengths, rows)
    whole, gains = gather_plain(
        (w_query, w_key, w_value, w_out, w_gate, w_up, w_down), (norm_attn, norm_ffn)
    )
    full_query, full_key, full_value, full_out, full_gate, full_up, full_down = whole
    gain_attn, gain_ffn = gains
    inputs = tokens.astype(jnp.float32)
    normed, factor = normalize(inputs)
    hidden = (normed * gain_attn.astype(jnp.float32)).astype(low)
    query = matmul(hidden, full_query).astype(low)
    keyed = matmul(hidden, full_key).astype(low)
    valued = matmul(hidden, full_value).astype(low)
    query_groups, key_groups, value_groups = (to_groups(query), to_groups(keyed), to_groups(valued))
    attended_groups, log_total = lax.map(
        partial(attend, allowed), (query_groups, key_groups, value_groups)
    )
    attended = from_groups(attended_groups)
    residual = inputs + matmul(attended, full_out)
    normed_two, factor_two = normalize(residual)
    hidden_two = (normed_two * gain_ffn.astype(jnp.float32)).astype(low)
    gate = matmul(hidden_two, full_gate)
    upward = matmul(hidden_two, full_up)
    sigma = jax.nn.sigmoid(gate)
    middle = (gate * sigma * upward).astype(low)
    mixed = (valid[:, None] * (residual + matmul(middle, full_down))).astype(low)
    grad_output = cotangent.astype(jnp.float32) * valid[:, None]
    grad_branch = grad_output.astype(low)
    grad_down = matmul_tn(middle, grad_branch)
    grad_middle = matmul_nt(grad_branch, full_down)
    grad_gate_rows = (grad_middle * upward * sigma * (1.0 + gate * (1.0 - sigma))).astype(low)
    grad_up_rows = (grad_middle * gate * sigma).astype(low)
    grad_gate = matmul_tn(hidden_two, grad_gate_rows)
    grad_up = matmul_tn(hidden_two, grad_up_rows)
    grad_hidden_two = matmul_nt(grad_gate_rows, full_gate) + matmul_nt(grad_up_rows, full_up)
    grad_gain_ffn = jnp.sum(grad_hidden_two * normed_two, axis=0)
    grad_residual = grad_output + norm_back(
        grad_hidden_two * gain_ffn.astype(jnp.float32), normed_two, factor_two
    )
    grad_proj = grad_residual.astype(low)
    grad_out = matmul_tn(attended, grad_proj)
    grad_attended = matmul_nt(grad_proj, full_out).astype(low)
    grad_query_g, grad_key_g, grad_value_g = lax.map(
        partial(attend_back, allowed),
        (query_groups, key_groups, value_groups, to_groups(grad_attended), log_total),
    )
    grad_query_rows = from_groups(grad_query_g)
    grad_key_rows = from_groups(grad_key_g)
    grad_value_rows = from_groups(grad_value_g)
    grad_query = matmul_tn(hidden, grad_query_rows)
    grad_key = matmul_tn(hidden, grad_key_rows)
    grad_value = matmul_tn(hidden, grad_value_rows)
    grad_hidden = (
        matmul_nt(grad_query_rows, full_query)
        + matmul_nt(grad_key_rows, full_key)
        + matmul_nt(grad_value_rows, full_value)
    )
    grad_gain_attn = jnp.sum(grad_hidden * normed, axis=0)
    input_grad = grad_residual + norm_back(
        grad_hidden * gain_attn.astype(jnp.float32), normed, factor
    )
    grads = (grad_query, grad_key, grad_value, grad_out, grad_gate, grad_up, grad_down)
    sums, gain_sums = sum_plain([g.astype(low) for g in grads], (grad_gain_attn, grad_gain_ffn))
    return (
        mixed,
        input_grad,
        gain_sums[0],
        sums[0],
        sums[1],
        sums[2],
        sums[3],
        gain_sums[1],
        sums[4],
        sums[5],
        sums[6],
    )


def on_tuned_device(
    tokens,
    norm_attn,
    w_query,
    w_key,
    w_value,
    w_out,
    norm_ffn,
    w_gate,
    w_up,
    w_down,
    lengths,
    cotangent,
):
    weights = (w_query, w_key, w_value, w_out, w_gate, w_up, w_down)
    kept, saved = forward(tokens, cotangent, lengths, weights, (norm_attn, norm_ffn))
    blocks, gain_lines, d_in = backward(tokens, lengths, kept, saved)
    sums, gain_sums, mixed, d_in = unpack(blocks, gain_lines, saved["mixed"], d_in)
    return (
        mixed,
        d_in,
        gain_sums[0],
        *sums[:4],
        gain_sums[1],
        *sums[4:],
    )


def solution(mesh):
    tuned = dict(mesh.shape) == {"dp": 8, "rep": 2, "cores": 2}
    tokens_placed = P(("dp", "rep", "cores"), None)
    share, gain = P("dp", None), P("dp")
    return jax.shard_map(
        on_tuned_device if tuned else on_any_device,
        mesh=mesh,
        in_specs=(
            tokens_placed,
            gain,
            share,
            share,
            share,
            share,
            gain,
            share,
            share,
            share,
            tokens_placed,
            tokens_placed,
        ),
        out_specs=(
            tokens_placed,
            tokens_placed,
            gain,
            share,
            share,
            share,
            share,
            gain,
            share,
            share,
            share,
        ),
        check_vma=False,
    )
```

```python
from functools import partial

import jax
import jax.numpy as jnp
from jax import lax
from jax.experimental import pallas as pl
from jax.experimental.pallas import tpu as pltpu
from jax.sharding import PartitionSpec as P

HEADS = 16
HEAD = 64


NORM_EPS = 1e-05
SCORE_SCALE = 0.125
NEGATIVE = -1e30
head_group = 4
MESH = pl.DeviceIdType.MESH
MIB = 1024 * 1024


def masks(block_len, rows):
    bounds = jnp.cumsum(block_len[0])
    place = jnp.arange(rows, dtype=jnp.int32)
    segment = jnp.sum((place[:, None] >= bounds[None, :]).astype(jnp.int32), axis=1)
    allowed = (segment[:, None] == segment[None, :]) & (place[None, :] <= place[:, None])
    valid = (segment < block_len.shape[1]).astype(jnp.float32)
    return (allowed, valid)


def normalize(values):
    factor = lax.rsqrt(jnp.mean(values * values, axis=-1, keepdims=True) + NORM_EPS)
    return (values * factor, factor)


def norm_back(grad_normed, normed, factor):
    return factor * (grad_normed - normed * jnp.mean(grad_normed * normed, axis=-1, keepdims=True))


def matmul(left, right):
    return jnp.dot(left, right, preferred_element_type=jnp.float32)


def matmul_tn(left, right):
    return lax.dot_general(
        left, right, (((0,), (0,)), ((), ())), preferred_element_type=jnp.float32
    )


def matmul_nt(left, right):
    return lax.dot_general(
        left, right, (((1,), (1,)), ((), ())), preferred_element_type=jnp.float32
    )


def to_groups(matrix):
    rows = matrix.shape[0]
    split = matrix.reshape(rows, HEADS // head_group, head_group, HEAD)
    return split.transpose(1, 2, 0, 3)


def from_groups(grouped):
    rows = grouped.shape[2]
    return grouped.transpose(2, 0, 1, 3).reshape(rows, HEADS * HEAD)


def group_scores(allowed, query_g, key_g):
    raw = (
        jnp.einsum("hqe,hke->hqk", query_g, key_g, preferred_element_type=jnp.float32) * SCORE_SCALE
    )
    return jnp.where(allowed[None], raw, NEGATIVE)


def attend(allowed, operands):
    query_g, key_g, value_g = operands
    scores = group_scores(allowed, query_g, key_g)
    top = jnp.max(scores, axis=-1, keepdims=True)
    expo = jnp.exp(scores - top)
    total = jnp.sum(expo, axis=-1, keepdims=True)
    probs_low = (expo / total).astype(jnp.bfloat16)
    result = jnp.einsum("hqk,hke->hqe", probs_low, value_g, preferred_element_type=jnp.float32)
    return (result.astype(jnp.bfloat16), top[..., 0] + jnp.log(total[..., 0]))


def attend_back(allowed, operands):
    query_g, key_g, value_g, grad_g, lse = operands
    scores = group_scores(allowed, query_g, key_g)
    probs = jnp.exp(scores - lse[..., None])
    grad_probs = jnp.einsum("hqe,hke->hqk", grad_g, value_g, preferred_element_type=jnp.float32)
    centre = jnp.sum(grad_probs * probs, axis=-1, keepdims=True)
    grad_scores = (probs * (grad_probs - centre)).astype(jnp.bfloat16)
    grad_query = (
        jnp.einsum("hqk,hke->hqe", grad_scores, key_g, preferred_element_type=jnp.float32)
        * SCORE_SCALE
    )
    grad_key = (
        jnp.einsum("hqk,hqe->hke", grad_scores, query_g, preferred_element_type=jnp.float32)
        * SCORE_SCALE
    )
    grad_value = jnp.einsum(
        "hqk,hqe->hke", probs.astype(jnp.bfloat16), grad_g, preferred_element_type=jnp.float32
    )
    return (
        grad_query.astype(jnp.bfloat16),
        grad_key.astype(jnp.bfloat16),
        grad_value.astype(jnp.bfloat16),
    )


class Part:
    def __init__(self, weight, tall, start, size, no_x):
        self.weight, self.tall, self.start, self.size = weight, tall, start, size
        self.no_x = no_x

    def quarter(self, ref, lead, c, x):
        if self.tall:
            columns = pl.ds(pl.multiple_of(c * 512 + x * 256, 256), 256)
            return ref.at[(*lead, pl.ds(self.start, self.size), columns)]
        return ref.at[(*lead, x, slice(None), self.columns(c))]

    def half(self, ref, lead, c):
        if self.tall:
            columns = pl.ds(pl.multiple_of(c * 512, 512), 512)
            return ref.at[(*lead, pl.ds(self.start, self.size), columns)]
        return ref.at[(*lead, slice(None), slice(None), self.columns(c))]

    def columns(self, c):
        width = self.size // 2
        return pl.ds(pl.multiple_of(self.start + c * width, 128), width)


def pieces(total, most):
    return [(start, min(most, total - start)) for start in range(0, total, most)]


def place():
    d = lax.axis_index("dp")
    return lax.div(d, 2), lax.rem(d, 2), lax.axis_index("rep"), lax.axis_index("cores")


def device(z, y, x, c):
    return {"dp": 2 * z + y, "rep": x, "cores": c}


def greet():
    z, y, x, c = place()
    barrier = pltpu.get_barrier_semaphore()
    others = [device(lax.rem(z + k, 4), y, x, c) for k in (1, 2, 3)]
    others += [device(z, 1 - y, x, c), device(z, y, 1 - x, c), device(z, y, x, 1 - c)]
    for other in others:
        pl.semaphore_signal(barrier, inc=1, device_id=other, device_id_type=MESH)
    pl.semaphore_wait(barrier, len(others))


class Wires:
    def __init__(self, send_sems, recv_sems):
        self.send_sems, self.recv_sems, self.sent = send_sems, recv_sems, []

    def copy(self, slot, source, target, other):
        return pltpu.make_async_remote_copy(
            src_ref=source,
            dst_ref=target,
            send_sem=self.send_sems.at[slot],
            recv_sem=self.recv_sems.at[slot],
            device_id=other,
            device_id_type=MESH,
        )

    def send(self, slot, source, target, other):
        copy = self.copy(slot, source, target, other)
        copy.start()
        self.sent.append((slot, copy))

    def arrived(self, slot, target):
        z, y, x, c = place()
        self.copy(slot, target, target, device(z, y, x, 1 - c)).wait_recv()

    def finish(self, chosen=lambda slot: True):
        for slot, copy in self.sent:
            if chosen(slot):
                copy.wait_send()
        self.sent = [(slot, copy) for slot, copy in self.sent if not chosen(slot)]


GATHER_SLOTS = 12
LAG = 2
ALL = slice(None)
COLUMNS = (1024, 1024, 1024, 1024, 2816, 2816, None)
QUERY, KEY, VALUE, OUT, GATE, UP, DOWN = range(7)
TILE = 512


FF_CHUNKS = tuple(pieces(2816, 512))


def gather_items():
    order = [(QUERY, 0, 256, True), (QUERY, 256, 768, False), (KEY, 0, 1024, True)]
    order += [(VALUE, 0, 1024, False), (OUT, 0, 1024, False)]
    order += [(DOWN, 0, 128, False), (DOWN, 128, 128, True), (DOWN, 256, 96, False)]
    for n, (start, size) in enumerate(FF_CHUNKS):
        order += [(GATE, start, size, n == 5), (UP, start, size, n in (0, 3, 5))]
    return [Part(w, w == DOWN, start, size, no_x) for w, start, size, no_x in order]


def dot(left, right):
    return lax.dot_general(
        left, right, (((1,), (0,)), ((), ())), preferred_element_type=jnp.float32
    )


def dot_nt(left, right):
    return lax.dot_general(
        left, right, (((1,), (1,)), ((), ())), preferred_element_type=jnp.float32
    )


def tile(index, size):
    return pl.ds(pl.multiple_of(index * size, size), size)


def weight_columns(ref, at):
    return ref[:, :, :, :, at].reshape(1024, -1)


class Forward:
    def __init__(self, refs):
        self.__dict__.update(refs)

    def prepare(self):
        for s in range(8):
            self.gain[:, 128 * s : 128 * s + 128] = self.gains[s // 2, s % 2]
        length = self.length[0, 0]
        for block in range(4):
            rows = slice(128 * block, 128 * block + 128)
            place_q = lax.broadcasted_iota(jnp.int32, (128, 512), 0) + 128 * block
            place_k = lax.broadcasted_iota(jnp.int32, (128, 512), 1)
            same = (place_q >= length) == (place_k >= length)
            allowed = same & (place_k <= place_q)
            self.bias[rows, :] = jnp.where(allowed, 0.0, NEGATIVE)

        def normed(block, _):
            rows = tile(block, 64)
            values = self.tokens[rows, :].astype(jnp.float32)
            factor = lax.rsqrt(jnp.mean(values * values, axis=-1, keepdims=True) + NORM_EPS)
            gain = self.gain[0:1, :].astype(jnp.float32)
            self.hidden[rows, :] = (values * factor * gain).astype(jnp.bfloat16)
            place = lax.broadcasted_iota(jnp.int32, (64, 1024), 0) + 64 * block
            d_b = jnp.where(place < length, self.cotangent[rows, :].astype(jnp.float32), 0.0)
            self.d_b[rows, :] = d_b.astype(jnp.bfloat16)
            return 0

        lax.fori_loop(0, 8, normed, 0)
        self.turn(self.hidden, self.h_t)
        self.out("d_b")

    def turn(self, matrix, turned):
        def columns(n, _):
            at = tile(n, 128)
            turned[at, :] = matrix[:, at].astype(jnp.float32).T.astype(jnp.bfloat16)
            return 0

        lax.fori_loop(0, 8, columns, 0)

    def project(self, weight, result):
        def columns(n, _):
            at = tile(n, TILE)
            result[:, at] = dot(self.hidden[...], weight_columns(weight, at)).astype(jnp.bfloat16)
            return 0

        lax.fori_loop(0, 1024 // TILE, columns, 0)

    def attend(self, first, last):
        def pair(p, _):
            at = tile(p, 128)
            left = lax.broadcasted_iota(jnp.int32, (256, 128), 1) < HEAD
            for block in (0, 1):
                rows, seen = slice(256 * block, 256 * block + 256), slice(0, 256 * block + 256)
                query = self.query[rows, at].astype(jnp.float32) * SCORE_SCALE
                both = jnp.concatenate(
                    [jnp.where(left, query, 0.0), jnp.where(left, 0.0, query)], axis=0
                ).astype(jnp.bfloat16)
                bias = self.bias[rows, seen]
                scores = dot_nt(both, self.key[seen, at]) + jnp.concatenate([bias, bias], axis=0)
                top = jnp.max(scores, axis=-1, keepdims=True)
                expo = jnp.exp(scores - top)
                total = jnp.sum(expo, axis=-1, keepdims=True)
                probs = (expo * (1.0 / total)).astype(jnp.bfloat16)
                result = dot(probs, self.value[seen, at])
                self.attended[rows, at] = jnp.where(left, result[:256], result[256:]).astype(
                    jnp.bfloat16
                )
                lse = top + jnp.log(total)
                turned = jnp.where(left, lse[:256], lse[256:]).T
                self.lse[p, 0:1, rows] = turned[0:1]
                self.lse[p, 1:2, rows] = turned[HEAD : HEAD + 1]
            return 0

        lax.fori_loop(first, last, pair, 0)

    def project_out(self):
        def columns(n, _):
            at = tile(n, TILE)
            self.residual[:, at] = self.tokens[:, at].astype(jnp.float32) + dot(
                self.attended[...], weight_columns(self.w_out, at)
            )
            return 0

        lax.fori_loop(0, 1024 // TILE, columns, 0)

        def normed(block, _):
            rows = tile(block, 64)
            values = self.residual[rows, :]
            factor = lax.rsqrt(jnp.mean(values * values, axis=-1, keepdims=True) + NORM_EPS)
            gain = self.gain[8:9, :].astype(jnp.float32)
            self.h2[rows, :] = (values * factor * gain).astype(jnp.bfloat16)
            return 0

        lax.fori_loop(0, 8, normed, 0)
        self.turn(self.h2, self.h2_t)
        self.turn(self.attended, self.att_t)
        for name in ("query", "key", "value", "lse", "h_t", "h2_t", "att_t"):
            self.out(name)

    def grad_of_middle(self, start, size):
        at = pl.ds(start, size)
        self.d_up[:, at] = dot_nt(self.d_b[...], self.w_down[at, :]).astype(jnp.bfloat16)

    def feed_forward(self, start, size):
        at = pl.ds(start, size)
        low = jnp.bfloat16
        gate_w = weight_columns(self.w_gate, at)
        up_w = weight_columns(self.w_up, at)
        down_w = self.w_down[at, :]
        gate = dot(self.h2[...], gate_w)
        upward = dot(self.h2[...], up_w)
        grad_middle = self.d_up[:, at].astype(jnp.float32)
        sigma = 0.5 * jnp.tanh(0.5 * gate) + 0.5
        silu = gate * sigma
        mid = (silu * upward).astype(low)
        d_up = (grad_middle * silu).astype(low)
        d_gate = (grad_middle * upward * (sigma + silu - silu * sigma)).astype(low)
        self.mid[:, at] = mid
        self.d_up[:, at] = d_up
        self.d_gate[:, at] = d_gate
        for j in range(1024 // TILE):
            part = slice(TILE * j, TILE * j + TILE)
            mixed = dot(mid, down_w[:, part])
            grad = dot_nt(d_gate, gate_w[part, :]) + dot_nt(d_up, up_w[part, :])
            if start == 0:
                self.total[:, part] = mixed
                self.d_h2[:, part] = grad
            else:
                self.total[:, part] += mixed
                self.d_h2[:, part] += grad

    def flush(self, start, size):
        for name in ("mid", "d_gate", "d_up"):
            self.out(name, pl.ds(start, size))

    def finish(self):
        length = self.length[0, 0]
        self.g_ffn[...] = jnp.zeros_like(self.g_ffn)

        def rows_of(block, _):
            rows = tile(block, 64)
            place = lax.broadcasted_iota(jnp.int32, (64, 1024), 0) + 64 * block
            residual = self.residual[rows, :]
            mixed = jnp.where(place < length, residual + self.total[rows, :], 0.0)
            self.mixed[rows, :] = mixed.astype(jnp.bfloat16)
            factor = lax.rsqrt(jnp.mean(residual * residual, axis=-1, keepdims=True) + NORM_EPS)
            normed = residual * factor
            grad = self.d_h2[rows, :]
            self.g_ffn[...] += jnp.sum((grad * normed).reshape(8, 8, 1024), axis=0)
            grad_normed = grad * self.gain[8:9, :].astype(jnp.float32)
            grad_out = jnp.where(place < length, self.cotangent[rows, :].astype(jnp.float32), 0.0)
            mean = jnp.mean(grad_normed * normed, axis=-1, keepdims=True)
            d_res = grad_out + factor * (grad_normed - normed * mean)
            self.d_res[rows, :] = d_res
            self.d_proj[rows, :] = d_res.astype(jnp.bfloat16)
            return 0

        lax.fori_loop(0, 8, rows_of, 0)
        for name in ("mixed", "d_res", "d_proj", "g_ffn", "gain"):
            self.out(name)


FORWARD_OUTS = (
    ("mixed", (512, 1024), jnp.bfloat16),
    ("query", (512, 1024), jnp.bfloat16),
    ("key", (512, 1024), jnp.bfloat16),
    ("value", (512, 1024), jnp.bfloat16),
    ("lse", (8, 8, 512), jnp.float32),
    ("h_t", (1024, 512), jnp.bfloat16),
    ("h2_t", (1024, 512), jnp.bfloat16),
    ("att_t", (1024, 512), jnp.bfloat16),
    ("d_b", (512, 1024), jnp.bfloat16),
    ("mid", (512, 2816), jnp.bfloat16),
    ("d_gate", (512, 2816), jnp.bfloat16),
    ("d_up", (512, 2816), jnp.bfloat16),
    ("d_res", (512, 1024), jnp.float32),
    ("d_proj", (512, 1024), jnp.bfloat16),
    ("g_ffn", (8, 1024), jnp.float32),
    ("gain", (16, 1024), jnp.bfloat16),
)
FORWARD_OWN = (
    ("hidden", (512, 1024), jnp.bfloat16),
    ("attended", (512, 1024), jnp.bfloat16),
    ("residual", (512, 1024), jnp.float32),
    ("h2", (512, 1024), jnp.bfloat16),
    ("d_h2", (512, 1024), jnp.float32),
    ("bias", (512, 512), jnp.float32),
    ("total", (512, 1024), jnp.float32),
)
OUT_COPIES = len(FORWARD_OUTS) - 3 + 3 * len(FF_CHUNKS)
KEPT = (QUERY, KEY, VALUE, OUT)


def share_shape(columns):
    return (352, 1024) if columns is None else (2, 64, columns)


def forward_kernel(items, *refs):
    refs = list(refs)

    def take(n):
        taken = refs[:n]
        del refs[:n]
        return taken

    shares = take(7)
    gain_attn, gain_ffn, tokens, cotangent, length = take(5)
    kept = take(len(KEPT))
    names = [name for name, _, _ in FORWARD_OUTS]
    outs = dict(zip(names, take(len(names))))
    full = take(7)
    full_gains, gains = take(2)
    own_names = names + [name for name, _, _ in FORWARD_OWN]
    state = dict(zip(own_names, take(len(own_names))))
    send_sems, recv_sems, own_sems, keep_sems, out_sems = refs
    outgoing = []

    def put(name, columns=None):
        source, target = state[name], outs[name]
        if columns is not None:
            source, target = source.at[:, columns], target.at[:, columns]
        outgoing.append(pltpu.make_async_copy(source, target, out_sems.at[len(outgoing)]))
        outgoing[-1].start()

    z, y, x, c = place()
    far = [lax.rem(z + k, 4) for k in range(4)]
    back = [lax.rem(z + 4 - k, 4) for k in range(4)]
    x_other, y_other, c_other = (
        device(z, y, 1 - x, c),
        device(z, 1 - y, x, c),
        device(z, y, x, 1 - c),
    )
    greet()
    wires = Wires(send_sems, recv_sems)
    own = [
        pltpu.make_async_copy(share, whole.at[z, y], own_sems.at[i])
        for i, (share, whole) in enumerate(zip(shares, full))
    ]
    own_gains = pltpu.make_async_copy(gains, full_gains.at[z, y], own_sems.at[7])
    keep = [
        pltpu.make_async_copy(full[w], kept[n], keep_sems.at[n]) for n, w in enumerate(KEPT)
    ]
    gains[...] = jnp.where(
        lax.broadcasted_iota(jnp.int32, (16, 128), 0) < 8,
        jnp.broadcast_to(gain_attn[...].astype(jnp.float32), (16, 128)),
        jnp.broadcast_to(gain_ffn[...].astype(jnp.float32), (16, 128)),
    ).astype(jnp.bfloat16)
    own_gains.start()
    gain_slot = GATHER_SLOTS * len(items)
    for k in (1, 2, 3):
        wires.send(gain_slot + k, gains, full_gains.at[z, y], device(far[k], y, x, c))
    for copy in own:
        copy.start()

    def slot(i, k):
        return GATHER_SLOTS * i + k

    def along_z(i):
        item = items[i]
        share, whole = shares[item.weight], full[item.weight]
        for k in (1, 2, 3):
            if item.no_x:
                source, target = item.half(share, (), c), item.half(whole, (z, y), c)
            else:
                source, target = item.quarter(share, (), c, x), item.quarter(whole, (z, y), c, x)
            wires.send(slot(i, k), source, target, device(far[k], y, x, c))

    own_done = set()

    def first_hop(i):
        item = items[i]
        whole = full[item.weight]
        if item.weight not in own_done:
            own[item.weight].wait()
            own_done.add(item.weight)
        for k in (1, 2, 3):
            if item.no_x:
                block = item.half(whole, (back[k], y), c)
                wires.arrived(slot(i, k), block)
                wires.send(slot(i, 7 + k), block, block, c_other)
            else:
                block = item.quarter(whole, (back[k], y), c, x)
                wires.arrived(slot(i, k), block)
                wires.send(slot(i, 3 + k), block, block, x_other)
        if item.no_x:
            block = item.half(whole, (ALL, y), c)
        else:
            block = item.quarter(whole, (ALL, y), c, x)
        wires.send(slot(i, 7), block, block, y_other)

    def second_hop(i):
        item = items[i]
        whole = full[item.weight]
        if item.no_x:
            block = item.half(whole, (ALL, 1 - y), c)
            wires.arrived(slot(i, 7), block)
            wires.send(slot(i, 11), block, block, c_other)
            return
        block = item.quarter(whole, (ALL, 1 - y), c, x)
        wires.arrived(slot(i, 7), block)
        wires.send(slot(i, 0), block, block, x_other)
        for k in (1, 2, 3):
            wires.arrived(slot(i, 3 + k), item.quarter(whole, (back[k], y), c, 1 - x))
        for k in (1, 2, 3):
            block = item.half(whole, (back[k], y), c)
            wires.send(slot(i, 7 + k), block, block, c_other)

    def last_hop(i):
        item = items[i]
        whole = full[item.weight]
        if not item.no_x:
            block = item.half(whole, (ALL, 1 - y), c)
            wires.arrived(slot(i, 0), item.quarter(whole, (ALL, 1 - y), c, 1 - x))
            wires.send(slot(i, 11), block, block, c_other)

    def complete(i):
        item = items[i]
        whole = full[item.weight]
        for k in (1, 2, 3):
            wires.arrived(slot(i, 7 + k), item.half(whole, (back[k], y), 1 - c))
        wires.arrived(slot(i, 11), item.half(whole, (ALL, 1 - y), 1 - c))

    def retire(i):
        wires.finish(lambda slot: slot // GATHER_SLOTS == i)

    step_of = Forward(
        dict(
            state,
            out=put,
            tokens=tokens,
            cotangent=cotangent,
            length=length,
            gains=full_gains,
            w_out=full[OUT],
            w_gate=full[GATE],
            w_up=full[UP],
            w_down=full[DOWN].reshape(2816, 1024),
        )
    )
    last_of = {item.weight: i for i, item in enumerate(items)}
    tasks = [(-1, 3, step_of.prepare)]
    for n, name in enumerate(("query", "key", "value")):
        tasks.append((last_of[n], 2, partial(step_of.project, full[n], state[name])))
    tasks += [(last_of[VALUE], 3, partial(step_of.attend, p, p + 2)) for p in (0, 2, 4, 6)]
    tasks.append((last_of[OUT], 3, step_of.project_out))
    for tile_of in pieces(2816, TILE):
        tasks.append((last_of[DOWN], 1, partial(step_of.grad_of_middle, *tile_of)))
    for start, size in FF_CHUNKS:
        there = max(
            i for i, item in enumerate(items) if item.weight == UP and item.start == start
        )
        for at, width in pieces(size, TILE):
            tasks.append((there, 5, partial(step_of.feed_forward, start + at, width)))
        tasks.append((there, 0, partial(step_of.flush, start, size)))

    ahead = 3
    for i in range(min(ahead, len(items))):
        along_z(i)
    own_gains.wait()
    for k in (1, 2, 3):
        wires.arrived(gain_slot + k, full_gains.at[back[k], y])
    wires.send(gain_slot, full_gains.at[:, y], full_gains.at[:, y], y_other)
    stages = (retire, complete, last_hop, second_hop, first_hop)
    lates = (3 * LAG, 3 * LAG - 1, 2 * LAG, LAG, 0)
    for step in range(len(items) + 3 * LAG):
        for late, stage in zip(lates, stages):
            if 0 <= step - late < len(items):
                stage(step - late)
        if step + ahead < len(items):
            along_z(step + ahead)
        if step == 0:
            wires.arrived(gain_slot, full_gains.at[:, 1 - y])
        there = step - lates[1]
        for n, w in enumerate(KEPT):
            if there == last_of[w]:
                keep[n].start()
        spent = 0
        while tasks and tasks[0][0] <= there and spent < 6:
            _, cost, task = tasks.pop(0)
            task()
            spent += cost
    for _, _, task in tasks:
        task()
    step_of.finish()
    for copy in keep + outgoing:
        copy.wait()
    wires.finish()


def forward(tokens, cotangent, lengths, weights, gains):
    items = gather_items()
    shares = [w.reshape(share_shape(n)) for w, n in zip(weights, COLUMNS)]
    wholes = [(4, 2) + share_shape(n) for n in COLUMNS]
    shapes = [jax.ShapeDtypeStruct(wholes[w], jnp.bfloat16) for w in KEPT]
    shapes += [jax.ShapeDtypeStruct(shape, dtype) for _, shape, dtype in FORWARD_OUTS]
    count = GATHER_SLOTS * len(items) + 4
    anywhere = pl.BlockSpec(memory_space=pl.ANY)
    in_vmem = pl.BlockSpec(memory_space=pltpu.VMEM)
    out = pl.pallas_call(
        partial(forward_kernel, items),
        out_shape=shapes,
        in_specs=[anywhere] * 7
        + [in_vmem] * 4
        + [pl.BlockSpec(memory_space=pltpu.SMEM)],
        out_specs=[anywhere] * len(shapes),
        scratch_shapes=[pltpu.VMEM(shape, jnp.bfloat16) for shape in wholes]
        + [pltpu.VMEM((4, 2, 16, 128), jnp.bfloat16), pltpu.VMEM((16, 128), jnp.bfloat16)]
        + [pltpu.VMEM(shape, dtype) for _, shape, dtype in FORWARD_OUTS + FORWARD_OWN]
        + [
            pltpu.SemaphoreType.DMA((count,)),
            pltpu.SemaphoreType.DMA((count,)),
            pltpu.SemaphoreType.DMA((8,)),
            pltpu.SemaphoreType.DMA((len(KEPT),)),
            pltpu.SemaphoreType.DMA((OUT_COPIES,)),
        ],
        compiler_params=pltpu.CompilerParams(
            collective_id=0, has_side_effects=True, vmem_limit_bytes=63 * MIB
        ),
        name="gather_forward",
    )(*shares, *[g.reshape(1, 128) for g in gains], tokens, cotangent, lengths)
    return out[: len(KEPT)], dict(zip([name for name, _, _ in FORWARD_OUTS], out[len(KEPT) :]))


SUM_SLOTS = 10
RING = 4


class Share:
    def __init__(self, weight, start, size, x_first):
        self.weight, self.start, self.size, self.x_first = weight, start, size, x_first
        self.tall = weight == DOWN
        self.width = 128 if self.tall else size // 2
        self.block = (352 if self.tall else 64, self.width)

    def columns(self, c, x):
        start = c * 512 + x * 256 + self.start if self.tall else self.start + c * self.width
        return pl.ds(pl.multiple_of(start, 128), self.width)

    def quarter(self, sums, c, x):
        if self.tall:
            return sums.at[c, x, self.start // 128]
        return sums.at[x, :, self.columns(c, x)]

    def half(self, sums, c):
        if self.tall:
            return sums.at[c, :, self.start // 128]
        return sums.at[:, :, self.columns(c, 0)]


def share_items():
    order = [(GATE, 2048, 768, True), (DOWN, 0, 128, False), (DOWN, 128, 128, True)]
    order += [(GATE, 0, 1024, True), (GATE, 1024, 1024, True)]
    order += [(UP, 0, 1024, True), (UP, 1024, 1024, False), (UP, 2048, 768, False)]
    order += [(OUT, 0, 1024, True), (QUERY, 0, 1024, False), (KEY, 0, 1024, True)]
    order += [(VALUE, 0, 768, True), (VALUE, 768, 256, False)]
    return [Share(*item) for item in order]


def plus(left, right):
    return left + right


def dot_tn(left, right):
    return lax.dot_general(
        left, right, (((0,), (0,)), ((), ())), preferred_element_type=jnp.float32
    )


BACKWARD_IN = (
    "query",
    "key",
    "value",
    "lse",
    "h_t",
    "h2_t",
    "att_t",
    "d_b",
    "d_res",
    "d_proj",
    "g_ffn",
    "gain",
)


class Backward:
    def __init__(self, refs):
        self.__dict__.update(refs)

    def prepare(self):
        length = self.length[0, 0]
        for block in range(4):
            rows = slice(128 * block, 128 * block + 128)
            place_k = lax.broadcasted_iota(jnp.int32, (128, 512), 0) + 128 * block
            place_q = lax.broadcasted_iota(jnp.int32, (128, 512), 1)
            same = (place_q >= length) == (place_k >= length)
            allowed = same & (place_k <= place_q)
            self.bias[rows, :] = jnp.where(allowed, 0.0, NEGATIVE)

    def multiply(self, left_t, right, item, target, core):
        columns = item.columns(core, 0)

        def rows(m, _):
            product = dot(left_t[tile(m, 256), :], right[:, columns]).astype(jnp.bfloat16)
            product = product.reshape(2, 2, 64, item.width)
            for xx in (0, 1):
                target[xx, m] = product[:, xx]
            return 0

        lax.fori_loop(0, 4, rows, 0)

    def multiply_tall(self, left, right, groups):
        def rows(m, _):
            at = tile(m, 256)
            turned = left[:, at].T
            for columns, targets in groups:
                product = dot(turned, right[:, columns]).astype(jnp.bfloat16)
                for n, (target, xx) in enumerate(targets):
                    target.reshape(2, 2816, 128)[xx, at, :] = product[:, 128 * n : 128 * n + 128]
            return 0

        lax.fori_loop(0, 11, rows, 0)

    def attend_back(self, first, last):
        low = jnp.bfloat16

        def pair(p, _):
            at = tile(p, 128)
            wo_rows = self.w_rows[p].reshape(128, 1024)
            grad = dot_nt(self.d_proj[...], wo_rows).astype(low)
            query = (self.query[:, at].astype(jnp.float32) * SCORE_SCALE).astype(low)
            key, value = self.key[:, at], self.value[:, at]
            left = lax.broadcasted_iota(jnp.int32, (512, 128), 1) < HEAD
            none = jnp.zeros((512, 128), low)
            sides = [
                [jnp.where(side, v, none) for v in (query, key, value, grad)]
                for side in (left, ~left)
            ]
            grad_key, grad_value = [None, None], [None, None]
            for block in (0, 1):
                rows, seen = slice(256 * block, 256 * block + 256), slice(0, 256 * block + 256)
                grad_query = None
                parts_key, parts_value = None, None
                for n, (own_query, own_key, own_value, own_grad) in enumerate(sides):
                    self.d_in[seen, 0:256] = dot_nt(own_key[seen], query[rows])
                    self.d_in[seen, 256:512] = dot_nt(own_value[seen], grad[rows])
                    self.back_rows(p, n, rows, 256 * block + 256)
                    grad_scores, probs = self.grad_scores[seen, :], self.probs[seen, :]
                    part_query = dot_tn(grad_scores, own_key[seen])
                    part_key = dot(grad_scores, own_query[rows])
                    part_value = dot(probs, own_grad[rows])
                    if n == 0:
                        grad_query, parts_key, parts_value = part_query, part_key, part_value
                    else:
                        grad_query += part_query
                        parts_key += part_key
                        parts_value += part_value
                self.query[rows, at] = (grad_query * SCORE_SCALE).astype(low)
                if block == 0:
                    grad_key[0], grad_value[0] = parts_key, parts_value
                else:
                    grad_key = [grad_key[0] + parts_key[:256], parts_key[256:]]
                    grad_value = [grad_value[0] + parts_value[:256], parts_value[256:]]
            for block in (0, 1):
                rows = slice(256 * block, 256 * block + 256)
                self.key[rows, at] = grad_key[block].astype(low)
                self.value[rows, at] = grad_value[block].astype(low)
            return 0

        lax.fori_loop(first, last, pair, 0)

    def back_rows(self, p, n, rows, count):
        low = jnp.bfloat16
        held = self.d_in
        lse = self.lse[p, n : n + 1, rows]

        def first_pass(r, centre):
            keys = tile(r, 64)
            probs = jnp.exp(held[keys, 0:256] + self.bias[keys, rows] - lse)
            held[keys, 0:256] = probs
            self.probs[keys, :] = probs.astype(low)
            return centre + jnp.sum((held[keys, 256:512] * probs).reshape(8, 8, 256), axis=0)

        centre = lax.fori_loop(0, count // 64, first_pass, jnp.zeros((8, 256), jnp.float32), unroll=2)
        centre = jnp.sum(centre, axis=0, keepdims=True)

        def second_pass(r, _):
            keys = tile(r, 64)
            grad = held[keys, 0:256] * (held[keys, 256:512] - centre)
            self.grad_scores[keys, :] = grad.astype(low)
            return 0

        lax.fori_loop(0, count // 64, second_pass, 0, unroll=2)

    def grad_hidden(self, t):
        at = pl.ds(256 * t, 256)
        total = None
        for n, grad in enumerate((self.query, self.key, self.value)):
            part = dot_nt(grad[...], self.w_rows[2 * n : 2 * n + 2].reshape(256, 1024))
            total = part if total is None else total + part
        self.d_in[:, at] = total

    def finish(self):
        self.gain_total[...] = jnp.zeros_like(self.gain_total)

        def rows_of(block, _):
            rows = tile(block, 64)
            values = self.tokens[rows, :].astype(jnp.float32)
            factor = lax.rsqrt(jnp.mean(values * values, axis=-1, keepdims=True) + NORM_EPS)
            normed = values * factor
            grad = self.d_in[rows, :]
            self.gain_total[...] += jnp.sum((grad * normed).reshape(8, 8, 1024), axis=0)
            grad_normed = grad * self.gain[0:1, :].astype(jnp.float32)
            mean = jnp.mean(grad_normed * normed, axis=-1, keepdims=True)
            self.d_in[rows, :] = self.d_res[rows, :] + factor * (
                grad_normed - normed * mean
            )
            return 0

        lax.fori_loop(0, 8, rows_of, 0)
        self.gain_lines[...] = jnp.zeros_like(self.gain_lines)
        lines = [jnp.sum(v[...], axis=0, keepdims=True) for v in (self.gain_total, self.g_ffn)]
        for s in range(8):
            for n, line in enumerate(lines):
                self.gain_lines[s // 2, s % 2, n : n + 1] = line[:, 128 * s : 128 * s + 128]


def backward_kernel(items, *refs):
    refs = list(refs)

    def take(n):
        taken = refs[:n]
        del refs[:n]
        return taken

    kept = take(len(KEPT))
    middle_in, grad_gate_in, grad_up_in = take(3)
    saved_in = dict(zip(BACKWARD_IN, take(len(BACKWARD_IN))))
    tokens_in, length = take(2)
    sums = take(7)
    gain_sums, input_grad_out = take(2)
    saved = dict(zip(BACKWARD_IN, take(len(BACKWARD_IN))))
    d_in, wide, w_rows, bias, probs, grad_scores, gain_total, gain_lines = take(8)
    mine, from_first, from_second, from_z = (take(len(items)) for _ in range(4))
    ring, tall_ring = take(RING), take(2)
    outbox, tall_outbox = take(2), take(2)
    gain_core, gain_x, gain_y, gain_z = take(4)
    send_sems, recv_sems, load_sems, credit = refs
    z, y, x, c = place()
    far = [lax.rem(z + k, 4) for k in range(4)]
    back = [lax.rem(z + 4 - k, 4) for k in range(4)]
    x_other, y_other, c_other = (
        device(z, y, 1 - x, c),
        device(z, 1 - y, x, c),
        device(z, y, x, 1 - c),
    )
    loads = {}

    def load(name, source, target):
        loads[name] = pltpu.make_async_copy(source, target, load_sems.at[len(loads)])
        loads[name].start()

    waited = set()

    def loaded(*names):
        for name in names:
            if name not in waited:
                loads[name].wait()
                waited.add(name)

    load("d_gate", grad_gate_in, wide.at[1])
    load("h2_t", saved_in["h2_t"], saved["h2_t"])
    load("mid", middle_in, wide.at[0])
    load("d_b", saved_in["d_b"], saved["d_b"])
    load("wo_rows", kept[OUT].reshape(8, 2, 64, 1024), w_rows)
    for name in BACKWARD_IN:
        if name not in loads:
            load(name, saved_in[name], saved[name])
    greet()
    wires = Wires(send_sems, recv_sems)
    work = Backward(
        dict(
            saved,
            tokens=saved["d_b"],
            length=length,
            w_rows=w_rows,
            probs=probs,
            grad_scores=grad_scores,
            bias=bias,
            d_in=d_in,
            gain_total=gain_total,
            gain_lines=gain_lines,
        )
    )
    tall_items = [i for i, item in enumerate(items) if item.tall]
    wide_items = [i for i, item in enumerate(items) if not item.tall]

    def slot(i, k):
        return SUM_SLOTS * i + k

    def core_slots(i):
        return (slot(i, 0), slot(i, 8))

    def from_core(i):
        if items[i].tall:
            return tall_ring[tall_items.index(i)]
        return ring[wide_items.index(i) % RING].at[..., : items[i].width]

    def produce(i):
        item = items[i]
        if item.tall:
            number = tall_items.index(i)
            if number == 0:
                loaded("mid", "d_b")
                groups = []
                for core, boxes in ((1 - c, tall_outbox), (c, [mine[j] for j in tall_items])):
                    columns = pl.ds(pl.multiple_of(512 * core, 512), 512)
                    groups.append((columns, [(boxes[j], xx) for xx in (0, 1) for j in (0, 1)]))
                work.multiply_tall(wide.at[0], saved["d_b"], groups)
                load("d_up", grad_up_in, wide.at[0])
                load("tokens", tokens_in, saved["d_b"])
            box = tall_outbox[number]
        else:
            number = wide_items.index(i)
            if number >= 2:
                wires.finish(lambda s: s in core_slots(wide_items[number - 2]))
            box = outbox[number % 2].at[..., : item.width]
            left, right, names = {
                GATE: (saved["h2_t"], wide.at[1], ("h2_t", "d_gate")),
                UP: (saved["h2_t"], wide.at[0], ("d_up",)),
                OUT: (saved["att_t"], saved["d_proj"], ("att_t", "d_proj")),
                QUERY: (saved["h_t"], saved["query"], ("h_t",)),
                KEY: (saved["h_t"], saved["key"], ()),
                VALUE: (saved["h_t"], saved["value"], ()),
            }[item.weight]
            loaded(*names)
            multiply = partial(work.multiply, left, right, item)
            if number >= RING:
                pl.semaphore_wait(credit, 1)
            multiply(box, 1 - c)
        for xx in (0, 1):
            wires.send(core_slots(i)[xx], box.at[xx], from_core(i).at[xx], c_other)
        if not item.tall:
            multiply(mine[i], c)

    def first_hop(i):
        item, own, other = items[i], mine[i], from_core(i)
        for xx in (0, 1):
            wires.arrived(core_slots(i)[xx], other.at[xx])

        def add(at, _):
            for xx in (0, 1):
                for yy in (0, 1):
                    own[xx, at, yy] = plus(own[xx, at, yy], other[xx, at, yy])
            return 0

        lax.fori_loop(0, 4, add, 0)
        if not item.tall and wide_items.index(i) + RING < len(wide_items):
            pl.semaphore_signal(credit, inc=1, device_id=c_other, device_id_type=MESH)
        if item.x_first:
            wires.send(slot(i, 1), own.at[1 - x], from_first[i], x_other)
        else:
            wires.send(slot(i, 1), own.at[:, :, 1 - y], from_first[i], y_other)

    def second_hop(i):
        item, own, other = items[i], mine[i], from_first[i]
        wires.arrived(slot(i, 1), other)

        def add(at, _):
            for side in (0, 1):
                if item.x_first:
                    own[x, at, side] = plus(own[x, at, side], other[at, side])
                else:
                    own[side, at, y] = plus(own[side, at, y], other[side, at])
            return 0

        lax.fori_loop(0, 4, add, 0)
        if item.x_first:
            wires.send(slot(i, 2), own.at[x, :, 1 - y], from_second[i], y_other)
        else:
            to_z(i, lambda k: own.at[:, far[k], y])

    def to_z(i, block):
        for k in (1, 2, 3):
            wires.send(slot(i, 2 + k), block(k), from_z[i].at[k - 1], device(far[k], y, x, c))

    def z_total(i, own_part):
        total = own_part.astype(jnp.float32)
        for k in (1, 2, 3):
            wires.arrived(slot(i, 2 + k), from_z[i].at[k - 1])
            total += from_z[i][k - 1].astype(jnp.float32)
        return total.astype(jnp.bfloat16)

    def third_hop(i):
        item, own, other = items[i], mine[i], from_second[i]
        if not item.x_first:
            own[:, z, y] = z_total(i, own[:, z, y])
            wires.send(slot(i, 2), own.at[:, z, y], other, x_other)
            return
        wires.arrived(slot(i, 2), other)

        def add(at, _):
            own[x, at, y] = plus(own[x, at, y], other[at])
            return 0

        lax.fori_loop(0, 4, add, 0)
        to_z(i, lambda k: own.at[x, far[k], y])

    def fourth_hop(i):
        item, own = items[i], mine[i]
        if not item.x_first:
            wires.arrived(slot(i, 2), from_second[i])
            block = item.half(sums[item.weight], c)
            block[...] = plus(own[:, z, y], from_second[i][...])
            wires.send(slot(i, 7), block, block, c_other)
            return
        block = item.quarter(sums[item.weight], c, x)
        block[...] = z_total(i, own[x, z, y])
        wires.send(slot(i, 6), block, block, x_other)

    def to_sibling(i):
        item = items[i]
        if item.x_first:
            wires.arrived(slot(i, 6), item.quarter(sums[item.weight], c, 1 - x))
            block = item.half(sums[item.weight], c)
            wires.send(slot(i, 7), block, block, c_other)

    def complete(i):
        item = items[i]
        wires.arrived(slot(i, 7), item.half(sums[item.weight], 1 - c))
        wires.finish(lambda s: s // SUM_SLOTS == i)

    base = SUM_SLOTS * len(items)

    def gains_one():
        wires.send(base, gain_lines, gain_core, c_other)

    def gains_two():
        wires.arrived(base, gain_core)
        gain_core[...] = gain_lines[...] + gain_core[...]
        wires.send(base + 1, gain_core, gain_x, x_other)

    def gains_three():
        wires.arrived(base + 1, gain_x)
        gain_x[...] = gain_core[...] + gain_x[...]
        wires.send(base + 2, gain_x.at[:, 1 - y], gain_y, y_other)

    def gains_four():
        wires.arrived(base + 2, gain_y)
        gain_y[...] = gain_x[:, y] + gain_y[...]
        for k in (1, 2, 3):
            wires.send(base + 2 + k, gain_y.at[far[k]], gain_z.at[z], device(far[k], y, x, c))
        gain_z[z] = gain_y[z]

    def gains_five():
        for k in (1, 2, 3):
            wires.arrived(base + 2 + k, gain_z.at[back[k]])
        gain_sums[...] = (gain_z[0] + gain_z[1]) + (gain_z[2] + gain_z[3])

    def fetch_rows(t):
        for n in range(3):
            load(("rows", n, t), kept[n].at[t], w_rows.at[2 * n : 2 * n + 2])

    def attend_back(p):
        if p == 0:
            loaded("query", "key", "value", "lse", "d_proj", "wo_rows")
        work.attend_back(p, p + 1)
        if p == 7:
            fetch_rows(0)

    def grad_hidden(t):
        loaded(*[("rows", n, t) for n in range(3)])
        work.grad_hidden(t)
        if t < 3:
            fetch_rows(t + 1)

    def finish():
        loaded("tokens", "d_res", "g_ffn", "gain")
        work.finish()
        load("d_in", d_in, input_grad_out)
        gains_one()

    beside = {1: [work.prepare]}
    for p in range(8):
        beside.setdefault(1 + p, []).append(partial(attend_back, p))
    for t in range(4):
        beside.setdefault(9 + t // 2, []).append(partial(grad_hidden, t))
    beside.setdefault(11, []).append(finish)
    for n, task in enumerate((gains_two, gains_three, gains_four, gains_five)):
        beside.setdefault(13 + 2 * n, []).append(task)

    stages = (complete, to_sibling, fourth_hop, third_hop, second_hop, first_hop, produce)
    lates = (12, 10, 8, 6, 4, 2, 0)
    for step in range(len(items) + lates[0]):
        for late, stage in zip(lates, stages):
            if 0 <= step - late < len(items):
                stage(step - late)
        for task in beside.get(step, []):
            task()
    loaded("d_in")
    wires.finish()


def backward(tokens, lengths, kept, saved):
    items = share_items()
    low, wide = jnp.bfloat16, jnp.float32
    dtypes = {name: (shape, dtype) for name, shape, dtype in FORWARD_OUTS}
    shapes = [
        jax.ShapeDtypeStruct((2, 2, 2, 352, 128) if n is None else (2, 64, n), low) for n in COLUMNS
    ]
    shapes += [jax.ShapeDtypeStruct((8, 128), wide), jax.ShapeDtypeStruct((512, 1024), wide)]
    count = SUM_SLOTS * len(items) + 6
    anywhere = pl.BlockSpec(memory_space=pl.ANY)
    in_vmem = pl.BlockSpec(memory_space=pltpu.VMEM)
    n_loads = 6 + len(BACKWARD_IN) + 12

    def buffers(lead_of):
        return [pltpu.VMEM(lead_of(item) + item.block, low) for item in items]

    out = pl.pallas_call(
        partial(backward_kernel, items),
        out_shape=shapes,
        in_specs=[anywhere] * (len(KEPT) + 3 + len(BACKWARD_IN) + 1)
        + [pl.BlockSpec(memory_space=pltpu.SMEM)],
        out_specs=[in_vmem] * 8 + [anywhere],
        scratch_shapes=[pltpu.VMEM(*dtypes[name]) for name in BACKWARD_IN]
        + [
            pltpu.VMEM((512, 1024), wide),
            pltpu.VMEM((2, 512, 2816), low),
            pltpu.VMEM((8, 2, 64, 1024), low),
            pltpu.VMEM((512, 512), wide),
            pltpu.VMEM((512, 256), low),
            pltpu.VMEM((512, 256), low),
            pltpu.VMEM((8, 1024), wide),
            pltpu.VMEM((4, 2, 8, 128), wide),
        ]
        + buffers(lambda item: (2, 4, 2))
        + buffers(lambda item: (4, 2) if item.x_first else (2, 4))
        + buffers(lambda item: (4,) if item.x_first else (2,))
        + buffers(lambda item: (3,) if item.x_first else (3, 2))
        + [pltpu.VMEM((2, 4, 2, 64, 512), low)] * RING
        + [pltpu.VMEM((2, 4, 2, 352, 128), low)] * 2
        + [pltpu.VMEM((2, 4, 2, 64, 512), low)] * 2
        + [pltpu.VMEM((2, 4, 2, 352, 128), low)] * 2
        + [
            pltpu.VMEM((4, 2, 8, 128), wide),
            pltpu.VMEM((4, 2, 8, 128), wide),
            pltpu.VMEM((4, 8, 128), wide),
            pltpu.VMEM((4, 8, 128), wide),
            pltpu.SemaphoreType.DMA((count,)),
            pltpu.SemaphoreType.DMA((count,)),
            pltpu.SemaphoreType.DMA((n_loads,)),
            pltpu.SemaphoreType.REGULAR,
        ],
        compiler_params=pltpu.CompilerParams(
            collective_id=1, has_side_effects=True, vmem_limit_bytes=63 * MIB
        ),
        name="backward_sum",
    )(
        *kept,
        saved["mid"],
        saved["d_gate"],
        saved["d_up"],
        *[saved[name] for name in BACKWARD_IN],
        tokens,
        lengths,
    )
    return out[:7], out[7], out[8]


def unpack_kernel(*refs):
    blocks, (gain_sums, mixed, d_in) = refs[:7], refs[7:10]
    sums, (gain_attn, gain_ffn, mixed_out, input_out) = refs[10:17], refs[17:21]
    held, wide = refs[21:28], refs[28:35]
    mixed_held, input_held, in_sems, out_sems = refs[35:]
    sources = (d_in, mixed, *blocks)
    places = (input_held, mixed_held, *held)
    results = (input_held, mixed_held, *wide)
    targets = (input_out, mixed_out, *sums)
    ins = [pltpu.make_async_copy(a, b, in_sems.at[n]) for n, (a, b) in enumerate(zip(sources, places))]
    outs = [pltpu.make_async_copy(a, b, out_sems.at[n]) for n, (a, b) in enumerate(zip(results, targets))]
    order = (6, 7, 8, 2, 3, 4, 5, 0, 1)
    for n in order:
        ins[n].start()
    for n in order:
        ins[n].wait()
        if n == 8:
            for b in range(8):
                wide[6][:, 128 * b : 128 * b + 128] = held[6][b // 4, b // 2 % 2, b % 2].astype(
                    jnp.float32
                )
        elif n >= 2:
            wide[n - 2][...] = held[n - 2][...].astype(jnp.float32)
        outs[n].start()
    gain_attn[...] = gain_sums[0:1]
    gain_ffn[...] = gain_sums[1:2]
    for n in order:
        outs[n].wait()


def unpack(blocks, gain_sums, mixed, d_in):
    wide = jnp.float32
    anywhere = pl.BlockSpec(memory_space=pl.ANY)
    in_vmem = pl.BlockSpec(memory_space=pltpu.VMEM)
    shapes = [
        jax.ShapeDtypeStruct((352, 1024) if n is None else (2, 64, n), wide) for n in COLUMNS
    ]
    held = [pltpu.VMEM(b.shape, b.dtype) for b in blocks]
    held += [pltpu.VMEM(v.shape, wide) for v in shapes]
    held += [pltpu.VMEM(v.shape, v.dtype) for v in (mixed, d_in)]
    shapes += [jax.ShapeDtypeStruct((1, 128), wide)] * 2
    shapes += [jax.ShapeDtypeStruct(v.shape, v.dtype) for v in (mixed, d_in)]
    out = pl.pallas_call(
        unpack_kernel,
        out_shape=shapes,
        in_specs=[anywhere] * 7 + [in_vmem] + [anywhere] * 2,
        out_specs=[anywhere] * 7 + [in_vmem] * 2 + [anywhere] * 2,
        scratch_shapes=held + [pltpu.SemaphoreType.DMA((9,)), pltpu.SemaphoreType.DMA((9,))],
        compiler_params=pltpu.CompilerParams(vmem_limit_bytes=62 * MIB),
        name="unpack",
    )(*blocks, gain_sums, mixed, d_in)
    sums = [s.reshape(-1, s.shape[-1]) for s in out[:7]]
    return sums, [g.reshape(128) for g in out[7:9]], out[9], out[10]


def gather_plain(weights, gains):
    everything = (*weights, *gains)
    whole = [lax.all_gather(v, "dp", axis=0, tiled=True) for v in everything]
    return whole[: len(weights)], whole[len(weights) :]


def sum_plain(grads, gain_grads):
    shares = [
        lax.psum_scatter(g.astype(jnp.float32), "dp", scatter_dimension=0, tiled=True)
        for g in (*grads, *gain_grads)
    ]
    sums = [lax.psum(s, ("rep", "cores")) for s in shares]
    return sums[: len(grads)], sums[len(grads) :]


def on_any_device(
    tokens,
    norm_attn,
    w_query,
    w_key,
    w_value,
    w_out,
    norm_ffn,
    w_gate,
    w_up,
    w_down,
    lengths,
    cotangent,
):
    rows = tokens.shape[0]
    low = jnp.bfloat16
    allowed, valid = masks(lengths, rows)
    whole, gains = gather_plain(
        (w_query, w_key, w_value, w_out, w_gate, w_up, w_down), (norm_attn, norm_ffn)
    )
    full_query, full_key, full_value, full_out, full_gate, full_up, full_down = whole
    gain_attn, gain_ffn = gains
    inputs = tokens.astype(jnp.float32)
    normed, factor = normalize(inputs)
    hidden = (normed * gain_attn.astype(jnp.float32)).astype(low)
    query = matmul(hidden, full_query).astype(low)
    keyed = matmul(hidden, full_key).astype(low)
    valued = matmul(hidden, full_value).astype(low)
    query_groups, key_groups, value_groups = (to_groups(query), to_groups(keyed), to_groups(valued))
    attended_groups, log_total = lax.map(
        partial(attend, allowed), (query_groups, key_groups, value_groups)
    )
    attended = from_groups(attended_groups)
    residual = inputs + matmul(attended, full_out)
    normed_two, factor_two = normalize(residual)
    hidden_two = (normed_two * gain_ffn.astype(jnp.float32)).astype(low)
    gate = matmul(hidden_two, full_gate)
    upward = matmul(hidden_two, full_up)
    sigma = jax.nn.sigmoid(gate)
    middle = (gate * sigma * upward).astype(low)
    mixed = (valid[:, None] * (residual + matmul(middle, full_down))).astype(low)
    grad_output = cotangent.astype(jnp.float32) * valid[:, None]
    grad_branch = grad_output.astype(low)
    grad_down = matmul_tn(middle, grad_branch)
    grad_middle = matmul_nt(grad_branch, full_down)
    grad_gate_rows = (grad_middle * upward * sigma * (1.0 + gate * (1.0 - sigma))).astype(low)
    grad_up_rows = (grad_middle * gate * sigma).astype(low)
    grad_gate = matmul_tn(hidden_two, grad_gate_rows)
    grad_up = matmul_tn(hidden_two, grad_up_rows)
    grad_hidden_two = matmul_nt(grad_gate_rows, full_gate) + matmul_nt(grad_up_rows, full_up)
    grad_gain_ffn = jnp.sum(grad_hidden_two * normed_two, axis=0)
    grad_residual = grad_output + norm_back(
        grad_hidden_two * gain_ffn.astype(jnp.float32), normed_two, factor_two
    )
    grad_proj = grad_residual.astype(low)
    grad_out = matmul_tn(attended, grad_proj)
    grad_attended = matmul_nt(grad_proj, full_out).astype(low)
    grad_query_g, grad_key_g, grad_value_g = lax.map(
        partial(attend_back, allowed),
        (query_groups, key_groups, value_groups, to_groups(grad_attended), log_total),
    )
    grad_query_rows = from_groups(grad_query_g)
    grad_key_rows = from_groups(grad_key_g)
    grad_value_rows = from_groups(grad_value_g)
    grad_query = matmul_tn(hidden, grad_query_rows)
    grad_key = matmul_tn(hidden, grad_key_rows)
    grad_value = matmul_tn(hidden, grad_value_rows)
    grad_hidden = (
        matmul_nt(grad_query_rows, full_query)
        + matmul_nt(grad_key_rows, full_key)
        + matmul_nt(grad_value_rows, full_value)
    )
    grad_gain_attn = jnp.sum(grad_hidden * normed, axis=0)
    input_grad = grad_residual + norm_back(
        grad_hidden * gain_attn.astype(jnp.float32), normed, factor
    )
    grads = (grad_query, grad_key, grad_value, grad_out, grad_gate, grad_up, grad_down)
    sums, gain_sums = sum_plain([g.astype(low) for g in grads], (grad_gain_attn, grad_gain_ffn))
    return (
        mixed,
        input_grad,
        gain_sums[0],
        sums[0],
        sums[1],
        sums[2],
        sums[3],
        gain_sums[1],
        sums[4],
        sums[5],
        sums[6],
    )


def on_tuned_device(
    tokens,
    norm_attn,
    w_query,
    w_key,
    w_value,
    w_out,
    norm_ffn,
    w_gate,
    w_up,
    w_down,
    lengths,
    cotangent,
):
    weights = (w_query, w_key, w_value, w_out, w_gate, w_up, w_down)
    kept, saved = forward(tokens, cotangent, lengths, weights, (norm_attn, norm_ffn))
    blocks, gain_lines, d_in = backward(tokens, lengths, kept, saved)
    sums, gain_sums, mixed, d_in = unpack(blocks, gain_lines, saved["mixed"], d_in)
    return (
        mixed,
        d_in,
        gain_sums[0],
        *sums[:4],
        gain_sums[1],
        *sums[4:],
    )


def solution(mesh):
    tuned = dict(mesh.shape) == {"dp": 8, "rep": 2, "cores": 2}
    tokens_placed = P(("dp", "rep", "cores"), None)
    share, gain = P("dp", None), P("dp")
    return jax.shard_map(
        on_tuned_device if tuned else on_any_device,
        mesh=mesh,
        in_specs=(
            tokens_placed,
            gain,
            share,
            share,
            share,
            share,
            gain,
            share,
            share,
            share,
            tokens_placed,
            tokens_placed,
        ),
        out_specs=(
            tokens_placed,
            tokens_placed,
            gain,
            share,
            share,
            share,
            share,
            gain,
            share,
            share,
            share,
        ),
        check_vma=False,
    )
```
